32 devices in a mesh: rep: 8 (over y, x, core), shard: 4 (over z).
Axes of the slice: x: 2, y: 2, z: 4, core: 2. Of those that a mesh axis runs over, the one named last changes fastest.
Arguments:
- tokens: bfloat16 [32768, 1024], P(('rep', 'shard')), may hold values from -6 to 6
- encoder: bfloat16 [4096, 1024], P(('rep', 'shard')), may hold values from -6 to 6
- cotangent: bfloat16 [32768, 1024], P(('rep', 'shard')), may hold values from -6 to 6
- lengths: int32 [32], replicated, may hold values from 1 to 1024, as said below
- encoder_lengths: int32 [32], replicated, may hold values from 32 to 128, as said below
- dealt_order: int32 [32], replicated, may hold values from 0 to 31, as said below
- attention_weights: float32 [1024, 8, 1024], P('shard')
- expand_weight: float32 [1024, 4096], P('shard'), may hold values from -0.1875 to 0.1875
- shrink_weight: float32 [4096, 1024], P('shard'), may hold values from -0.09375 to 0.09375
- small_params: float32 [17408], replicated
- attention_rows: float32 [8, 1024], P(None, 'shard'), may hold values from 32.768 to 26214.4
- attention_cols: float32 [8, 1024], replicated, may hold values from 327.68 to 3276.8
- expand_rows: float32 [1024], P('shard'), may hold values from 163.84 to 114688
- expand_cols: float32 [4096], replicated, may hold values from 1638.4 to 13107.2
- shrink_rows: float32 [4096], P('shard'), may hold values from 163.84 to 114688
- shrink_cols: float32 [1024], replicated, may hold values from 1638.4 to 13107.2
- small_moment: float32 [17408], replicated, may hold values from 6553.6 to 52428.8
Outputs:
- output: bfloat16 [32768, 1024], P(('rep', 'shard'))
- input_grad: bfloat16 [32768, 1024], P(('rep', 'shard'))
- encoder_grad: bfloat16 [4096, 1024], P(('rep', 'shard'))
- attention_grad: float32 [1024, 8, 1024], P('shard')
- expand_grad: float32 [1024, 4096], P('shard')
- shrink_grad: float32 [4096, 1024], P('shard')
- small_grad: float32 [17408], replicated
- attention_new: float32 [1024, 8, 1024], P('shard')
- expand_new: float32 [1024, 4096], P('shard')
- shrink_new: float32 [4096, 1024], P('shard')
- small_new: float32 [17408], replicated
- attention_copy: bfloat16 [1024, 8, 1024], P('shard')
- expand_copy: bfloat16 [1024, 4096], P('shard')
- shrink_copy: bfloat16 [4096, 1024], P('shard')
- attention_rows_new: float32 [8, 1024], P(None, 'shard')
- attention_cols_new: float32 [8, 1024], replicated
- expand_rows_new: float32 [1024], P('shard')
- expand_cols_new: float32 [4096], replicated
- shrink_rows_new: float32 [4096], P('shard')
- shrink_cols_new: float32 [1024], replicated
- small_moment_new: float32 [17408], replicated
- norm_stats: float32 [6], replicated
The draws below stay inside these ranges and needn't reach their ends.
Inputs may be any that keep to these rules, and one draw needn't show every extreme that they name: Sequence s has lengths[s] valid tokens at the start of its slot; at least one sequence has exactly 1024. `encoder_lengths`: valid encoder states lie at the start of a sequence's block; at least one sequence has exactly 128. `dealt_order`: A permutation of the sequence numbers.
All inputs are finite; a program needn't handle non-finite values.
Results may differ from the reference program's by a relative error of at most 0.02.
The reference program's roundings to bfloat16 on the way count: a program that leaves them out, or rounds other values in their place, can miss the bound.
Values may be sent and summed in bfloat16 or wider, within the bound.
A program may use at most 512 MiB of HBM per device.

```python
import math
import jax
import jax.numpy as jnp
from jax import lax

D = 1024
HEADS = 16
HEAD_DIM = 64
FF = 4096
LEN = 1024
ENC = 128
REPLICAS = 8
SHARDS = 4
SEQUENCES = 32


OUT_GAIN = 8.0


def shared_deal(key):
    return jax.random.permutation(key, SEQUENCES).astype(jnp.int32)


def falling_factors(key, shape, centre, span):
    count = shape[-1]
    fraction = jnp.arange(count, dtype=jnp.float32) / (count - 1)
    trend = jnp.exp(jnp.log(span) * (0.5 - fraction))
    jitter = jnp.exp(jax.random.uniform(key, shape, jnp.float32, -0.35, 0.35))
    return (centre * trend * jitter).astype(jnp.float32)


def draw_dealt_order(key, part):
    dealt = shared_deal(key)
    key = jax.random.fold_in(key, 11)
    return dealt


def draw_lengths(key, part):
    dealt = shared_deal(key)
    key = jax.random.fold_in(key, 12)
    slots = jnp.arange(SEQUENCES, dtype=jnp.int32)
    rising = LEN * (REPLICAS - 1 + slots // SHARDS) * (SHARDS - 1 + slots % SHARDS) // (4 * (REPLICAS - 1) * (SHARDS - 1))
    jitter = jax.random.randint(key, (SEQUENCES,), -(LEN // 16), LEN // 16 + 1)
    placed = jnp.clip(rising + jitter, 1, LEN).at[SEQUENCES - 1].set(LEN).astype(jnp.int32)
    return jnp.zeros((SEQUENCES,), jnp.int32).at[dealt].set(placed)


def draw_encoder_lengths(key, part):
    key = jax.random.fold_in(key, 13)
    first_key, second = jax.random.split(key)
    counts = jax.random.randint(first_key, (SEQUENCES,), ENC // 4, ENC + 1)
    chosen = jax.random.randint(second, (), 0, SEQUENCES)
    return counts.at[chosen].set(ENC).astype(jnp.int32)


def draw_attention_weights(key, part):
    key = jax.random.fold_in(key, 14)
    values = jax.random.normal(key, (D, 8, D), jnp.float32)
    boost = jnp.where(jnp.arange(8) % 4 == 3, OUT_GAIN, 1.0).astype(jnp.float32)
    return values * boost[None, :, None] * D ** (-0.5)


def draw_small_params(key, part):
    key = jax.random.fold_in(key, 15)
    offset_key, gain_key, shift_key = jax.random.split(key, 3)
    offsets = 0.3 * jax.random.normal(offset_key, (7 * D + FF,), jnp.float32)
    gains = jax.random.uniform(gain_key, (3, 1, D), jnp.float32, 0.7, 1.3)
    shifts = 0.3 * jax.random.normal(shift_key, (3, 1, D), jnp.float32)
    tail = jnp.concatenate([gains, shifts], axis=1).reshape(6 * D)
    return jnp.concatenate([offsets, tail])


def draw_attention_rows(key, part):
    key = jax.random.fold_in(key, 21)
    span = 100.0
    return falling_factors(key, (8, D), 0.0316 * SEQUENCES * LEN, span)


def draw_expand_rows(key, part):
    key = jax.random.fold_in(key, 22)
    span = 100.0
    return falling_factors(key, (D,), 0.141 * SEQUENCES * LEN, span)


def draw_shrink_rows(key, part):
    key = jax.random.fold_in(key, 23)
    span = 100.0
    return falling_factors(key, (FF,), 0.141 * SEQUENCES * LEN, span)


def levels(rng, shape, cuts, least, largest):
    loudness = 1.0
    for position, blocks in cuts:
        draws = jax.random.uniform(jax.random.fold_in(jax.random.fold_in(rng, 6), position), (blocks,), jnp.float32, least / len(cuts), largest / len(cuts))
        loudness = loudness * jnp.repeat(jnp.exp(draws), shape[position] // blocks).reshape((-1,) + (1,) * (len(shape) - 1 - position))
    return loudness


def gaussian(key, shape, scale, bound, cuts=(), held_as=jnp.bfloat16):
    array = jax.random.normal(key, shape, jnp.float32) * scale
    if len(cuts) > 0:
        array = levels(key, shape, cuts, -0.22, 0.18) * array
    return jnp.clip(array, min=-bound, max=bound).astype(held_as)


def setup_inputs(seed: int = 0) -> dict:
    splits = jax.random.split(jax.random.key(seed), 18)
    tokens = gaussian(splits[0], (SEQUENCES * LEN, D), 1.0, 6.0, ((0, 32),))
    encoder = gaussian(splits[1], (SEQUENCES * ENC, D), 1.0, 6.0, ((0, 32),))
    cotangent = gaussian(splits[2], (SEQUENCES * LEN, D), 1.0, 6.0, ((0, 32),))
    lengths = draw_lengths(jax.random.fold_in(splits[17], 71), 0)
    encoder_lengths = draw_encoder_lengths(jax.random.fold_in(splits[17], 71), 0)
    dealt_order = draw_dealt_order(jax.random.fold_in(splits[17], 71), 0)
    attention_weights = draw_attention_weights(jax.random.fold_in(splits[17], 71), 0)
    expand_weight = gaussian(splits[7], (D, FF), D ** -0.5, 0.1875, ((0, 4),), jnp.float32)
    shrink_weight = gaussian(splits[8], (FF, D), FF ** -0.5, 0.09375, ((0, 4),), jnp.float32)
    small_params = draw_small_params(jax.random.fold_in(splits[17], 71), 0)
    attention_rows = draw_attention_rows(jax.random.fold_in(splits[17], 71), 0)
    attention_cols = jnp.clip(jnp.exp(jax.random.uniform(splits[11], (8, D), jnp.float32, math.log(327.68), math.log(3276.8))), 327.68, 3276.8)
    expand_rows = draw_expand_rows(jax.random.fold_in(splits[17], 71), 0)
    expand_cols = jnp.clip(jnp.exp(jax.random.uniform(splits[13], (FF,), jnp.float32, math.log(1638.4), math.log(13107.2))), 1638.4, 13107.2)
    shrink_rows = draw_shrink_rows(jax.random.fold_in(splits[17], 71), 0)
    shrink_cols = jnp.clip(jnp.exp(jax.random.uniform(splits[15], (D,), jnp.float32, math.log(1638.4), math.log(13107.2))), 1638.4, 13107.2)
    small_moment = jnp.clip(jnp.exp(jax.random.uniform(splits[16], (13 * D + FF,), jnp.float32, math.log(6553.6), math.log(52428.8))), 6553.6, 52428.8)
    return {"tokens": tokens, "encoder": encoder, "cotangent": cotangent, "lengths": lengths, "encoder_lengths": encoder_lengths, "dealt_order": dealt_order, "attention_weights": attention_weights, "expand_weight": expand_weight, "shrink_weight": shrink_weight, "small_params": small_params, "attention_rows": attention_rows, "attention_cols": attention_cols, "expand_rows": expand_rows, "expand_cols": expand_cols, "shrink_rows": shrink_rows, "shrink_cols": shrink_cols, "small_moment": small_moment}


DECAY_RATE = 0.5
CLIP_LEVEL = 0.25
STEP_RATE = 0.1
SMALL_RATE = 0.4
OUT_GAIN = 8.0
NORM_EPS = 1e-05
FACTOR_EPS = 1e-30
MASKED = -1e+30
HIGHEST = lax.Precision.HIGHEST

@jax.custom_vjp
def low(v):
    return lax.optimization_barrier(v.astype(jnp.bfloat16)).astype(jnp.float32)

@jax.custom_vjp
def low_back(v):
    return v

def low_keep(v):
    return (low(v), None)

def low_pass(kept, grad):
    return (grad,)

def back_keep(v):
    return (v, None)

def back_low(kept, grad):
    return (low(grad),)
low.defvjp(low_keep, low_pass)
low_back.defvjp(back_keep, back_low)

def layer_norm(r, norm_gain, norm_shift):
    centred = r - lax.optimization_barrier(jnp.mean(r, axis=-1, keepdims=True))
    spread = lax.optimization_barrier(jnp.mean(centred * centred, axis=-1, keepdims=True))
    return centred * lax.rsqrt(spread + NORM_EPS) * norm_gain + norm_shift

def matmul(a, b):
    return jnp.dot(a, b, precision=HIGHEST, preferred_element_type=jnp.float32)

def unpack(small):
    extents = [D] * 6 + [FF] + [D] * 7
    pieces = []
    offset = 0
    for extent in extents:
        pieces.append(small[offset:offset + extent])
        offset = offset + extent
    return pieces

def attention(q, k, v, usable):
    heads_q = q.reshape(q.shape[0], HEADS, HEAD_DIM)
    heads_k = k.reshape(k.shape[0], HEADS, HEAD_DIM)
    heads_v = v.reshape(v.shape[0], HEADS, HEAD_DIM)
    scores = low_back(jnp.einsum('qhd,khd->hqk', heads_q, heads_k, precision=HIGHEST))
    scores = jnp.where(usable[None], scores, MASKED)
    probs_low = low(jax.nn.softmax(scores, axis=-1))
    joined = jnp.einsum('hqk,khd->qhd', probs_low, heads_v, precision=HIGHEST)
    return low_back(low(joined.reshape(q.shape[0], D)))

def forward_pass(attention_w, expand_w, shrink_w, small, x, states, valid_tokens, valid_states):
    w = low(attention_w)
    w_expand = low(expand_w)
    w_shrink = low(shrink_w)
    parts = unpack(small)
    places = jnp.arange(LEN, dtype=jnp.int32)
    self_ok = (places[None, :] <= places[:, None]) & (places[None, :] < valid_tokens)
    cross_ok = jnp.broadcast_to(jnp.arange(ENC, dtype=jnp.int32)[None, :] < valid_states, (LEN, ENC))
    q = low_back(low((matmul(x, w[:, 0, :]) + parts[0]) * 0.125))
    k = low_back(low(matmul(x, w[:, 1, :])))
    v = low_back(low(matmul(x, w[:, 2, :]) + parts[1]))
    o_self = attention(q, k, v, self_ok)
    branch_a = low_back(matmul(o_self, w[:, 3, :]) + parts[2])
    hidden_one = layer_norm(x + branch_a, parts[8], parts[9])
    hidden_low = low(hidden_one)
    cq = low_back(low((matmul(hidden_low, w[:, 4, :]) + parts[3]) * 0.125))
    ck = low_back(low(matmul(states, w[:, 5, :])))
    cv = low_back(low(matmul(states, w[:, 6, :]) + parts[4]))
    o_cross = attention(cq, ck, cv, cross_ok)
    branch_c = low_back(matmul(o_cross, w[:, 7, :]) + parts[5])
    hidden_two = layer_norm(hidden_one + branch_c, parts[10], parts[11])
    pre_act = low_back(matmul(low(hidden_two), w_expand) + parts[6])
    activated = low(jax.nn.gelu(pre_act, approximate=False))
    branch_m = low_back(matmul(activated, w_shrink) + parts[7])
    result = layer_norm(hidden_two + branch_m, parts[12], parts[13])
    usable_rows = (places < valid_tokens).astype(jnp.float32)[:, None]
    squares = jnp.stack([jnp.sum(usable_rows * t * t) for t in (x, branch_a, hidden_one, branch_c, hidden_two, branch_m)])
    return (result, squares)

def factored(w, g, rows, cols, rate):
    g_square = g * g + FACTOR_EPS
    rows_new = DECAY_RATE * rows + (1.0 - DECAY_RATE) * lax.optimization_barrier(jnp.mean(g_square, axis=1))
    cols_new = DECAY_RATE * cols + (1.0 - DECAY_RATE) * lax.optimization_barrier(jnp.mean(g_square, axis=0))
    second = rows_new[:, None] * cols_new[None, :] / jnp.mean(rows_new)
    update = g * lax.rsqrt(second)
    scale = jnp.sqrt(jnp.mean(update * update))
    return (w - rate * update / jnp.maximum(1.0, scale / CLIP_LEVEL), rows_new, cols_new)

def reference(tokens, encoder, cotangent, lengths, encoder_lengths, dealt_order, attention_weights, expand_weight, shrink_weight, small_params, attention_rows, attention_cols, expand_rows, expand_cols, shrink_rows, shrink_cols, small_moment):
    inverse = jnp.zeros((SEQUENCES,), jnp.int32).at[dealt_order].set(jnp.arange(SEQUENCES, dtype=jnp.int32))
    own_tokens = tokens.reshape(SEQUENCES, LEN, D)[inverse]
    all_states = encoder.reshape(SEQUENCES, ENC, D)
    all_cotangents = cotangent.reshape(SEQUENCES, LEN, D)

    def one_sequence(running, slices):
        seq_tokens, seq_states, seq_cot, valid_tokens, valid_states = slices

        def bound_pass(attention_w, expand_w, shrink_w, small, x, states):
            return forward_pass(attention_w, expand_w, shrink_w, small, x, states, valid_tokens, valid_states)
        result, pullback, squares = jax.vjp(bound_pass, attention_weights, expand_weight, shrink_weight, small_params, seq_tokens.astype(jnp.float32), seq_states.astype(jnp.float32), has_aux=True)
        usable_rows = (jnp.arange(LEN, dtype=jnp.int32) < valid_tokens).astype(jnp.float32)[:, None]
        grads = pullback(seq_cot.astype(jnp.float32) * usable_rows)
        running = (running[0] + grads[0], running[1] + grads[1], running[2] + grads[2], running[3] + grads[3], running[4] + squares)
        return (running, (result.astype(jnp.bfloat16), grads[4].astype(jnp.bfloat16), grads[5].astype(jnp.bfloat16)))
    start = (jnp.zeros((D, 8, D), jnp.float32), jnp.zeros((D, FF), jnp.float32), jnp.zeros((FF, D), jnp.float32), jnp.zeros((13 * D + FF,), jnp.float32), jnp.zeros((6,), jnp.float32))
    running, stacked = lax.scan(one_sequence, start, (own_tokens, all_states, all_cotangents, lengths, encoder_lengths))
    attention_grad, expand_grad, shrink_grad, small_grad, squares = running
    output = stacked[0].reshape(SEQUENCES * LEN, D)
    input_grad = stacked[1].reshape(SEQUENCES * LEN, D)
    encoder_grad = stacked[2].reshape(SEQUENCES * ENC, D)
    fresh_list, rows_list, cols_list = ([], [], [])
    for index in range(8):
        rate = STEP_RATE * (OUT_GAIN if index % 4 == 3 else 1.0)
        fresh, rows_new, cols_new = factored(attention_weights[:, index, :], attention_grad[:, index, :], attention_rows[index], attention_cols[index], rate)
        fresh_list.append(fresh)
        rows_list.append(rows_new)
        cols_list.append(cols_new)
    attention_new = jnp.stack(fresh_list, axis=1)
    attention_rows_new = jnp.stack(rows_list, axis=0)
    attention_cols_new = jnp.stack(cols_list, axis=0)
    expand_new, expand_rows_new, expand_cols_new = factored(expand_weight, expand_grad, expand_rows, expand_cols, STEP_RATE)
    shrink_new, shrink_rows_new, shrink_cols_new = factored(shrink_weight, shrink_grad, shrink_rows, shrink_cols, STEP_RATE)
    small_moment_new = DECAY_RATE * small_moment + (1.0 - DECAY_RATE) * (small_grad * small_grad + FACTOR_EPS)
    small_update = small_grad * lax.rsqrt(small_moment_new)
    small_scale = jnp.sqrt(jnp.mean(small_update * small_update))
    small_new = small_params - SMALL_RATE * small_update / jnp.maximum(1.0, small_scale / CLIP_LEVEL)
    norm_stats = jnp.sqrt(squares / (jnp.sum(lengths).astype(jnp.float32) * D))
    return (output, input_grad, encoder_grad, attention_grad, expand_grad, shrink_grad, small_grad, attention_new, expand_new, shrink_new, small_new, attention_new.astype(jnp.bfloat16), expand_new.astype(jnp.bfloat16), shrink_new.astype(jnp.bfloat16), attention_rows_new, attention_cols_new, expand_rows_new, expand_cols_new, shrink_rows_new, shrink_cols_new, small_moment_new, norm_stats)
```

```python
import jax
import jax.numpy as jnp
from jax import lax
from jax.sharding import PartitionSpec as P

D = 1024
HEADS = 16
HEAD_DIM = 64
FF = 4096


DECAY_RATE = 0.5
CLIP_LEVEL = 0.25
STEP_RATE = 0.1
SMALL_RATE = 0.4
OUT_GAIN = 8.0
NORM_EPS = 1e-05
FACTOR_EPS = 1e-30
MASKED = -1e30


def layer_norm(r, norm_gain, norm_shift):
    centred = r - jnp.mean(r, axis=-1, keepdims=True)
    spread = jnp.mean(centred * centred, axis=-1, keepdims=True)
    return centred * lax.rsqrt(spread + NORM_EPS) * norm_gain + norm_shift


def gelu_exact(values):
    return jax.nn.gelu(values, approximate=False)


def unpack(small):
    extents = [D] * 6 + [FF] + [D] * 7
    pieces = []
    offset = 0
    for extent in extents:
        pieces.append(small[offset : offset + extent])
        offset = offset + extent
    return pieces


def forward_product(source, matrix):
    return jnp.dot(source, matrix, preferred_element_type=jnp.float32)


def input_product(grad_low, matrix):
    return jnp.einsum("to,io->ti", grad_low, matrix, preferred_element_type=jnp.float32)


def weight_product(source, grad_low):
    return jnp.einsum("ti,to->io", source, grad_low, preferred_element_type=jnp.float32)


def row_sum(grad_low):
    return jnp.sum(grad_low.astype(jnp.float32), axis=0)


def masked_scores(query_part, key_heads, first_row, valid_count, causal):
    scores = jnp.einsum("qhd,khd->hqk", query_part, key_heads, preferred_element_type=jnp.float32)
    key_places = jnp.arange(key_heads.shape[0], dtype=jnp.int32)[None, :]
    usable = key_places < valid_count
    if causal:
        query_places = first_row + jnp.arange(query_part.shape[0], dtype=jnp.int32)[:, None]
        usable = usable & (key_places <= query_places)
    return jnp.where(usable[None], scores, MASKED)


def attend_forward(queries, key_heads, values, valid_count, causal):
    query_rows = queries.shape[0]
    step_rows = min(512, query_rows)
    outputs, stored = ([], [])
    for b in range(query_rows // step_rows):
        first_row = b * step_rows
        key_end = first_row + step_rows if causal else key_heads.shape[0]
        scores = masked_scores(
            queries[first_row : first_row + step_rows],
            key_heads[:key_end],
            first_row,
            valid_count,
            causal,
        )
        row_max = jnp.max(scores, axis=-1, keepdims=True)
        raised = jnp.exp(scores - row_max)
        totals = jnp.sum(raised, axis=-1, keepdims=True)
        probs_low = (raised / totals).astype(jnp.bfloat16)
        outputs.append(
            jnp.einsum(
                "hqk,khd->qhd", probs_low, values[:key_end], preferred_element_type=jnp.float32
            )
        )
        stored.append(row_max + jnp.log(totals))
    return (jnp.concatenate(outputs, axis=0), stored)


def attend_backward(queries, key_heads, values, grad_out, stored, valid_count, causal):
    query_rows = queries.shape[0]
    key_rows = key_heads.shape[0]
    step_rows = min(512, query_rows)
    grad_queries = []
    grad_keys = jnp.zeros(key_heads.shape, jnp.float32)
    grad_values = jnp.zeros(values.shape, jnp.float32)
    for b in range(query_rows // step_rows):
        first_row = b * step_rows
        key_end = first_row + step_rows if causal else key_rows
        query_part = queries[first_row : first_row + step_rows]
        grad_part = grad_out[first_row : first_row + step_rows]
        scores = masked_scores(query_part, key_heads[:key_end], first_row, valid_count, causal)
        probs = jnp.exp(scores - stored[b])
        probs_low = probs.astype(jnp.bfloat16)
        grad_probs = jnp.einsum(
            "qhd,khd->hqk", grad_part, values[:key_end], preferred_element_type=jnp.float32
        )
        value_part = jnp.einsum(
            "hqk,qhd->khd", probs_low, grad_part, preferred_element_type=jnp.float32
        )
        grad_scores = probs * (grad_probs - jnp.sum(probs * grad_probs, axis=-1, keepdims=True))
        scores_low = grad_scores.astype(jnp.bfloat16)
        grad_queries.append(
            jnp.einsum(
                "hqk,khd->qhd", scores_low, key_heads[:key_end], preferred_element_type=jnp.float32
            )
        )
        key_part = jnp.einsum(
            "hqk,qhd->khd", scores_low, query_part, preferred_element_type=jnp.float32
        )
        padding = ((0, key_rows - key_end), (0, 0), (0, 0))
        grad_keys = grad_keys + jnp.pad(key_part, padding)
        grad_values = grad_values + jnp.pad(value_part, padding)
    return (jnp.concatenate(grad_queries, axis=0), grad_keys, grad_values)


def gather_rows(piece):
    return lax.all_gather(piece, ("shard", "rep"), axis=0, tiled=True)


def own_piece(block, replicas):
    rows = block.shape[0] // replicas
    return lax.dynamic_slice_in_dim(block, lax.axis_index("rep") * rows, rows, axis=0)


def scatter_rows(grad):
    piece = lax.psum_scatter(
        grad.astype(jnp.bfloat16), ("shard", "rep"), scatter_dimension=0, tiled=True
    )
    return lax.all_gather(piece, "rep", axis=0, tiled=True)


def local_factors(grad, rows):
    square = grad * grad
    rows_new = DECAY_RATE * rows + (1.0 - DECAY_RATE) * jnp.mean(square + FACTOR_EPS, axis=-1)
    col_part = jnp.sum(square + FACTOR_EPS, axis=0)
    weighted = jnp.sum(square / rows_new[..., None], axis=0)
    return rows_new, col_part, weighted, jnp.sum(rows_new, axis=0)


def finish_factors(grad, weight, rows_new, cols, col_sum, weighted, row_total, row_count, rate):
    cols_new = DECAY_RATE * cols + (1.0 - DECAY_RATE) * col_sum / row_count
    mean_rows = row_total / row_count
    mean_square = mean_rows * jnp.sum(weighted / cols_new, axis=-1) / (row_count * cols.shape[-1])
    factor = rate / jnp.maximum(1.0, jnp.sqrt(mean_square) / CLIP_LEVEL)
    scaled = lax.rsqrt(cols_new / mean_rows[..., None]) * factor[..., None]
    fresh = weight - grad * (lax.rsqrt(rows_new)[..., None] * scaled[None])
    return fresh, cols_new


def on_device(
    tokens,
    encoder,
    cotangent,
    lengths,
    encoder_lengths,
    dealt_order,
    attention_weights,
    expand_weight,
    shrink_weight,
    small_params,
    attention_rows,
    attention_cols,
    expand_rows,
    expand_cols,
    shrink_rows,
    shrink_cols,
    small_moment,
):
    devices = lax.axis_size(("rep", "shard"))
    replicas = lax.axis_size("rep")
    shards = lax.axis_size("shard")
    slot_tokens = tokens.shape[0]
    slot_states = encoder.shape[0]
    position = lax.axis_index(("rep", "shard"))
    inverse = (
        jnp.zeros((devices,), jnp.int32).at[dealt_order].set(jnp.arange(devices, dtype=jnp.int32))
    )
    qkv_piece = own_piece(attention_weights[:, 0:3, :].reshape(-1, 3 * D), replicas)
    rest_piece = own_piece(attention_weights[:, 3:8, :].reshape(-1, 5 * D), replicas)
    qkv_full = gather_rows(qkv_piece.astype(jnp.bfloat16))
    rest_full = gather_rows(rest_piece.astype(jnp.bfloat16))
    expand_full = gather_rows(own_piece(expand_weight, replicas).astype(jnp.bfloat16))
    shrink_full = gather_rows(own_piece(shrink_weight, replicas).astype(jnp.bfloat16))
    spread = lax.all_to_all(
        tokens.reshape(devices, slot_tokens // devices, D),
        ("rep", "shard"),
        split_axis=0,
        concat_axis=0,
        tiled=True,
    )
    picked = jnp.take(spread, inverse, axis=0)
    tokens = lax.all_to_all(
        picked, ("rep", "shard"), split_axis=0, concat_axis=0, tiled=True
    ).reshape(slot_tokens, D)
    states = encoder
    incoming = cotangent
    valid_tokens = lengths[position]
    valid_states = encoder_lengths[position]
    matrices = [qkv_full[:, i * D : (i + 1) * D] for i in range(3)] + [
        rest_full[:, i * D : (i + 1) * D] for i in range(5)
    ]
    parts = unpack(small_params)
    token_heads = (slot_tokens, HEADS, HEAD_DIM)
    state_heads = (slot_states, HEADS, HEAD_DIM)
    q_self = ((forward_product(tokens, matrices[0]) + parts[0]) * 0.125).astype(
        jnp.bfloat16
    )
    k_self = forward_product(tokens, matrices[1]).astype(jnp.bfloat16)
    v_self = (forward_product(tokens, matrices[2]) + parts[1]).astype(jnp.bfloat16)
    o_self, lse_self = attend_forward(
        q_self.reshape(token_heads),
        k_self.reshape(token_heads),
        v_self.reshape(token_heads),
        valid_tokens,
        True,
    )
    o_self_low = o_self.reshape(slot_tokens, D).astype(jnp.bfloat16)
    branch_a = forward_product(o_self_low, matrices[3]) + parts[2]
    tokens_wide = tokens.astype(jnp.float32)
    hidden_one, norm_one_back = jax.vjp(layer_norm, tokens_wide + branch_a, parts[8], parts[9])
    hidden_one_low = hidden_one.astype(jnp.bfloat16)
    q_cross = (
        (forward_product(hidden_one_low, matrices[4]) + parts[3]) * 0.125
    ).astype(jnp.bfloat16)
    k_cross = forward_product(states, matrices[5]).astype(jnp.bfloat16)
    v_cross = (forward_product(states, matrices[6]) + parts[4]).astype(jnp.bfloat16)
    o_cross, lse_cross = attend_forward(
        q_cross.reshape(token_heads),
        k_cross.reshape(state_heads),
        v_cross.reshape(state_heads),
        valid_states,
        False,
    )
    o_cross_low = o_cross.reshape(slot_tokens, D).astype(jnp.bfloat16)
    branch_c = forward_product(o_cross_low, matrices[7]) + parts[5]
    hidden_two, norm_two_back = jax.vjp(layer_norm, hidden_one + branch_c, parts[10], parts[11])
    hidden_two_low = hidden_two.astype(jnp.bfloat16)
    pre_act = forward_product(hidden_two_low, expand_full) + parts[6]
    activated, gelu_back = jax.vjp(gelu_exact, pre_act)
    activated_low = activated.astype(jnp.bfloat16)
    branch_m = forward_product(activated_low, shrink_full) + parts[7]
    result, norm_three_back = jax.vjp(layer_norm, hidden_two + branch_m, parts[12], parts[13])
    usable_rows = (jnp.arange(slot_tokens, dtype=jnp.int32) < valid_tokens).astype(jnp.float32)[
        :, None
    ]
    squares = jnp.stack(
        [
            jnp.sum(usable_rows * t * t)
            for t in (tokens_wide, branch_a, hidden_one, branch_c, hidden_two, branch_m)
        ]
    )
    d_third, d_gain_three, d_shift_three = norm_three_back(
        incoming.astype(jnp.float32) * usable_rows
    )
    d_mlp = d_third.astype(jnp.bfloat16)
    grad_shrink = weight_product(activated_low, d_mlp)
    grad_shrink_offset = row_sum(d_mlp)
    d_activated = input_product(d_mlp, shrink_full)
    d_pre = gelu_back(d_activated)[0].astype(jnp.bfloat16)
    grad_expand = weight_product(hidden_two_low, d_pre)
    grad_expand_offset = row_sum(d_pre)
    d_hidden_two = d_third + input_product(d_pre, expand_full)
    d_second, d_gain_two, d_shift_two = norm_two_back(d_hidden_two)
    d_branch_c = d_second.astype(jnp.bfloat16)
    grad_cross_out = weight_product(o_cross_low, d_branch_c)
    grad_cross_out_offset = row_sum(d_branch_c)
    d_o_cross = input_product(d_branch_c, matrices[7]).astype(jnp.bfloat16)
    grad_cq, grad_ck, grad_cv = attend_backward(
        q_cross.reshape(token_heads),
        k_cross.reshape(state_heads),
        v_cross.reshape(state_heads),
        d_o_cross.reshape(token_heads),
        lse_cross,
        valid_states,
        False,
    )
    dq_cross = (grad_cq.reshape(slot_tokens, D) * 0.125).astype(jnp.bfloat16)
    dk_cross = grad_ck.reshape(slot_states, D).astype(jnp.bfloat16)
    dv_cross = grad_cv.reshape(slot_states, D).astype(jnp.bfloat16)
    grad_cross_query = weight_product(hidden_one_low, dq_cross)
    grad_cross_key = weight_product(states, dk_cross)
    grad_cross_value = weight_product(states, dv_cross)
    state_grad = input_product(dk_cross, matrices[5]) + input_product(
        dv_cross, matrices[6]
    )
    d_hidden_one = d_second + input_product(dq_cross, matrices[4])
    d_first, d_gain_one, d_shift_one = norm_one_back(d_hidden_one)
    d_branch_a = d_first.astype(jnp.bfloat16)
    grad_self_out = weight_product(o_self_low, d_branch_a)
    grad_self_out_offset = row_sum(d_branch_a)
    d_o_self = input_product(d_branch_a, matrices[3]).astype(jnp.bfloat16)
    grad_sq, grad_sk, grad_sv = attend_backward(
        q_self.reshape(token_heads),
        k_self.reshape(token_heads),
        v_self.reshape(token_heads),
        d_o_self.reshape(token_heads),
        lse_self,
        valid_tokens,
        True,
    )
    dq_self = (grad_sq.reshape(slot_tokens, D) * 0.125).astype(jnp.bfloat16)
    dk_self = grad_sk.reshape(slot_tokens, D).astype(jnp.bfloat16)
    dv_self = grad_sv.reshape(slot_tokens, D).astype(jnp.bfloat16)
    grad_self_query = weight_product(tokens, dq_self)
    grad_self_key = weight_product(tokens, dk_self)
    grad_self_value = weight_product(tokens, dv_self)
    token_grad = (
        d_first
        + input_product(dq_self, matrices[0])
        + input_product(dk_self, matrices[1])
        + input_product(dv_self, matrices[2])
    )
    small_partial = jnp.concatenate(
        [
            row_sum(dq_self),
            row_sum(dv_self),
            grad_self_out_offset,
            row_sum(dq_cross),
            row_sum(dv_cross),
            grad_cross_out_offset,
            grad_expand_offset,
            grad_shrink_offset,
            d_gain_one,
            d_shift_one,
            d_gain_two,
            d_shift_two,
            d_gain_three,
            d_shift_three,
        ]
    )
    totals = lax.psum(jnp.concatenate([small_partial, squares]), ("rep", "shard"))
    g_shrink = scatter_rows(grad_shrink)
    g_expand = scatter_rows(grad_expand)
    g_rest = scatter_rows(
        jnp.concatenate(
            [grad_self_out, grad_cross_query, grad_cross_key, grad_cross_value, grad_cross_out],
            axis=1,
        )
    )
    g_qkv = scatter_rows(
        jnp.concatenate([grad_self_query, grad_self_key, grad_self_value], axis=1)
    )
    g_attention = (
        jnp.concatenate([g_qkv, g_rest], axis=1).reshape(-1, 8, D).astype(jnp.float32)
    )
    g_expand = g_expand.astype(jnp.float32)
    g_shrink = g_shrink.astype(jnp.float32)
    attention_rows_new, *attention_parts = local_factors(g_attention, attention_rows.T)
    expand_rows_new, *expand_parts = local_factors(g_expand, expand_rows)
    shrink_rows_new, *shrink_parts = local_factors(g_shrink, shrink_rows)
    flat = attention_parts + expand_parts + shrink_parts
    summed = lax.psum(jnp.concatenate([t.reshape(-1) for t in flat]), "shard")
    sums = []
    offset = 0
    for t in flat:
        sums.append(summed[offset : offset + t.size].reshape(t.shape))
        offset = offset + t.size
    attention_rates = STEP_RATE * jnp.where(jnp.arange(8) % 4 == 3, OUT_GAIN, 1.0).astype(
        jnp.float32
    )
    attention_new, attention_cols_new = finish_factors(
        g_attention,
        attention_weights,
        attention_rows_new,
        attention_cols,
        *sums[0:3],
        D,
        attention_rates,
    )
    expand_new, expand_cols_new = finish_factors(
        g_expand, expand_weight, expand_rows_new, expand_cols, *sums[3:6], D, STEP_RATE
    )
    shrink_new, shrink_cols_new = finish_factors(
        g_shrink, shrink_weight, shrink_rows_new, shrink_cols, *sums[6:9], FF, STEP_RATE
    )
    small_grad = totals[: small_params.shape[0]]
    small_moment_new = DECAY_RATE * small_moment + (1.0 - DECAY_RATE) * (
        small_grad * small_grad + FACTOR_EPS
    )
    small_update = small_grad * lax.rsqrt(small_moment_new)
    small_scale = jnp.sqrt(jnp.mean(small_update * small_update))
    small_new = small_params - SMALL_RATE * small_update / jnp.maximum(
        1.0, small_scale / CLIP_LEVEL
    )
    norm_stats = jnp.sqrt(
        totals[small_params.shape[0] :] / (jnp.sum(lengths).astype(jnp.float32) * D)
    )
    return (
        result.astype(jnp.bfloat16),
        token_grad.astype(jnp.bfloat16),
        state_grad.astype(jnp.bfloat16),
        g_attention,
        g_expand,
        g_shrink,
        small_grad,
        attention_new,
        expand_new,
        shrink_new,
        small_new,
        attention_new.astype(jnp.bfloat16),
        expand_new.astype(jnp.bfloat16),
        shrink_new.astype(jnp.bfloat16),
        attention_rows_new.T,
        attention_cols_new,
        expand_rows_new,
        expand_cols_new,
        shrink_rows_new,
        shrink_cols_new,
        small_moment_new,
        norm_stats,
    )


def solution(mesh):
    in_specs = (
        P(("rep", "shard"), None),
        P(("rep", "shard"), None),
        P(("rep", "shard"), None),
        P(),
        P(),
        P(),
        P("shard", None, None),
        P("shard", None),
        P("shard", None),
        P(),
        P(None, "shard"),
        P(),
        P("shard"),
        P(),
        P("shard"),
        P(),
        P(),
    )
    out_specs = (
        P(("rep", "shard"), None),
        P(("rep", "shard"), None),
        P(("rep", "shard"), None),
        P("shard", None, None),
        P("shard", None),
        P("shard", None),
        P(),
        P("shard", None, None),
        P("shard", None),
        P("shard", None),
        P(),
        P("shard", None, None),
        P("shard", None),
        P("shard", None),
        P(None, "shard"),
        P(),
        P("shard"),
        P(),
        P("shard"),
        P(),
        P(),
        P(),
    )
    return jax.shard_map(
        on_device, mesh=mesh, in_specs=in_specs, out_specs=out_specs, check_vma=False
    )
```

```python
import jax
import jax.numpy as jnp
from jax import lax
from jax.experimental import pallas as pl
from jax.experimental.pallas import tpu as pltpu
from jax.sharding import PartitionSpec as P

D = 1024
HEADS = 16
HEAD_DIM = 64
FF = 4096


DECAY_RATE = 0.5
CLIP_LEVEL = 0.25
STEP_RATE = 0.1
SMALL_RATE = 0.4
OUT_GAIN = 8.0
NORM_EPS = 1e-05
FACTOR_EPS = 1e-30
MASKED = -1e30


def layer_norm(r, norm_gain, norm_shift):
    centred = r - jnp.mean(r, axis=-1, keepdims=True)
    spread = jnp.mean(centred * centred, axis=-1, keepdims=True)
    return centred * lax.rsqrt(spread + NORM_EPS) * norm_gain + norm_shift


def gelu_exact(values):
    return jax.nn.gelu(values, approximate=False)


def unpack(small):
    extents = [D] * 6 + [FF] + [D] * 7
    pieces = []
    offset = 0
    for extent in extents:
        pieces.append(small[offset : offset + extent])
        offset = offset + extent
    return pieces


def forward_product(source, matrix):
    return jnp.dot(source, matrix, preferred_element_type=jnp.float32)


def input_product(grad_low, matrix):
    return jnp.einsum("to,io->ti", grad_low, matrix, preferred_element_type=jnp.float32)


def weight_product(source, grad_low):
    return jnp.einsum("ti,to->io", source, grad_low, preferred_element_type=jnp.float32)


def row_sum(grad_low):
    return jnp.sum(grad_low.astype(jnp.float32), axis=0)


def masked_scores(query_part, key_heads, first_row, valid_count, causal):
    scores = jnp.einsum("qhd,khd->hqk", query_part, key_heads, preferred_element_type=jnp.float32)
    key_places = jnp.arange(key_heads.shape[0], dtype=jnp.int32)[None, :]
    usable = key_places < valid_count
    if causal:
        query_places = first_row + jnp.arange(query_part.shape[0], dtype=jnp.int32)[:, None]
        usable = usable & (key_places <= query_places)
    return jnp.where(usable[None], scores, MASKED)


def attend_forward(queries, key_heads, values, valid_count, causal):
    query_rows = queries.shape[0]
    step_rows = min(512, query_rows)
    outputs, stored = ([], [])
    for b in range(query_rows // step_rows):
        first_row = b * step_rows
        key_end = first_row + step_rows if causal else key_heads.shape[0]
        scores = masked_scores(
            queries[first_row : first_row + step_rows],
            key_heads[:key_end],
            first_row,
            valid_count,
            causal,
        )
        row_max = jnp.max(scores, axis=-1, keepdims=True)
        raised = jnp.exp(scores - row_max)
        totals = jnp.sum(raised, axis=-1, keepdims=True)
        probs_low = (raised / totals).astype(jnp.bfloat16)
        outputs.append(
            jnp.einsum(
                "hqk,khd->qhd", probs_low, values[:key_end], preferred_element_type=jnp.float32
            )
        )
        stored.append(row_max + jnp.log(totals))
    return (jnp.concatenate(outputs, axis=0), stored)


def attend_backward(queries, key_heads, values, grad_out, stored, valid_count, causal):
    query_rows = queries.shape[0]
    key_rows = key_heads.shape[0]
    step_rows = min(512, query_rows)
    grad_queries = []
    grad_keys = jnp.zeros(key_heads.shape, jnp.float32)
    grad_values = jnp.zeros(values.shape, jnp.float32)
    for b in range(query_rows // step_rows):
        first_row = b * step_rows
        key_end = first_row + step_rows if causal else key_rows
        query_part = queries[first_row : first_row + step_rows]
        grad_part = grad_out[first_row : first_row + step_rows]
        scores = masked_scores(query_part, key_heads[:key_end], first_row, valid_count, causal)
        probs = jnp.exp(scores - stored[b])
        probs_low = probs.astype(jnp.bfloat16)
        grad_probs = jnp.einsum(
            "qhd,khd->hqk", grad_part, values[:key_end], preferred_element_type=jnp.float32
        )
        value_part = jnp.einsum(
            "hqk,qhd->khd", probs_low, grad_part, preferred_element_type=jnp.float32
        )
        grad_scores = probs * (grad_probs - jnp.sum(probs * grad_probs, axis=-1, keepdims=True))
        scores_low = grad_scores.astype(jnp.bfloat16)
        grad_queries.append(
            jnp.einsum(
                "hqk,khd->qhd", scores_low, key_heads[:key_end], preferred_element_type=jnp.float32
            )
        )
        key_part = jnp.einsum(
            "hqk,qhd->khd", scores_low, query_part, preferred_element_type=jnp.float32
        )
        padding = ((0, key_rows - key_end), (0, 0), (0, 0))
        grad_keys = grad_keys + jnp.pad(key_part, padding)
        grad_values = grad_values + jnp.pad(value_part, padding)
    return (jnp.concatenate(grad_queries, axis=0), grad_keys, grad_values)


MESH = pl.DeviceIdType.MESH
CHUNKS = 16
MIB = 1 << 20


def neighbours():
    rep = lax.axis_index("rep")
    z = lax.axis_index("shard")
    core = rep % 2
    x = (rep // 2) % 2
    y = rep // 4
    other_core = (rep + 1 - 2 * core, z)
    other_x = (rep + 2 - 4 * x, z)
    other_y = (rep + 4 - 8 * y, z)
    others_z = [(rep, (z + d) % 4) for d in (1, 2, 3)]
    return core, x, y, z, other_core, other_x, other_y, others_z


def greet(devices):
    barrier = pltpu.get_barrier_semaphore()
    for device in devices:
        pl.semaphore_signal(barrier, inc=1, device_id=device, device_id_type=MESH)
    pl.semaphore_wait(barrier, len(devices))


def remote(src, dst, send, recv, device):
    return pltpu.make_async_remote_copy(
        src_ref=src, dst_ref=dst, send_sem=send, recv_sem=recv, device_id=device, device_id_type=MESH
    )


def add_blocks(target, first, second, planes, rows, step):
    per_plane = rows // step

    def body(i, carry):
        s = i // per_plane
        r = pl.multiple_of((i % per_plane) * step, step)
        total = first(s, r).astype(jnp.float32) + second(s, r).astype(jnp.float32)
        target(s, r, total.astype(jnp.bfloat16))
        return carry

    lax.fori_loop(0, planes * per_plane, body, 0)


def reduce_kernel(
    att_ref,
    exp_ref,
    shr_ref,
    small_ref,
    out_ref,
    small_out_ref,
    half,
    own,
    quarter,
    eighth,
    pieces,
    final,
    small_in,
    small_sum,
    small_z,
    send_sem,
    recv_sem,
    z_send_sem,
    z_recv_sem,
    own_sem,
    place_sem,
    small_send_sem,
    small_recv_sem,
):
    core, x, y, z, other_core, other_x, other_y, others_z = neighbours()
    greet([other_core, other_x, other_y] + others_z)

    def axes(c):
        odd = c % 2
        a = x + odd * (y - x)
        b = y + odd * (x - y)
        dx = other_x[0]
        dy = other_y[0]
        return a, b, (dx + odd * (dy - dx), z), (dy + odd * (dx - dy), z)

    def by_source(c, act):
        @pl.when(c < 8)
        def _():
            act(lambda part: att_ref.at[c, :, pl.ds(part, 128), :])

        @pl.when((c >= 8) & (c < 12))
        def _():
            act(
                lambda part: exp_ref.at[
                    :, pl.ds(part, 128), pl.ds(pl.multiple_of((c - 8) * D, D), D)
                ]
            )

        @pl.when(c >= 12)
        def _():
            act(lambda part: shr_ref.at[:, c - 12, pl.ds(part, 128), :])

    kept = pl.multiple_of(core * 128, 128)
    given = pl.multiple_of(128 - core * 128, 128)

    def core_copy(c, source):
        return remote(
            source(given), half.at[c], send_sem.at[0, c], recv_sem.at[0, c], other_core
        )

    def own_copy(c, source):
        return pltpu.make_async_copy(source(kept), own.at[c % 2], own_sem.at[c % 2])

    def start_core(c):
        def act(source):
            core_copy(c, source).start()
            own_copy(c, source).start()

        by_source(c, act)

    def first_copy(c):
        a, b, first_device, second_device = axes(c)
        rows = pl.multiple_of(64 - a * 64, 64)
        return remote(
            half.at[c, :, pl.ds(rows, 64), :],
            quarter.at[c],
            send_sem.at[1, c],
            recv_sem.at[1, c],
            first_device,
        )

    def second_copy(c):
        a, b, first_device, second_device = axes(c)
        rows = pl.multiple_of(32 - b * 32, 32)
        return remote(
            quarter.at[c, :, pl.ds(rows, 32), :],
            eighth.at[c],
            send_sem.at[2, c],
            recv_sem.at[2, c],
            second_device,
        )

    def z_copy(c, d):
        device = others_z[d]
        return remote(
            eighth.at[c, device[1]],
            pieces.at[c, d],
            z_send_sem.at[c, d],
            z_recv_sem.at[c, d],
            device,
        )

    def place_copy(c):
        a, b, first_device, second_device = axes(c)
        rows = pl.ds(pl.multiple_of(core * 128 + a * 64 + b * 32, 32), 32)
        return pltpu.make_async_copy(final.at[c], out_ref.at[c, rows, :], place_sem.at[c])

    def back_second(c):
        a, b, first_device, second_device = axes(c)
        rows = pl.ds(pl.multiple_of(core * 128 + a * 64 + b * 32, 32), 32)
        return remote(
            final.at[c], out_ref.at[c, rows, :], send_sem.at[3, c], recv_sem.at[3, c], second_device
        )

    def back_first(c):
        a, b, first_device, second_device = axes(c)
        rows = pl.ds(pl.multiple_of(core * 128 + a * 64, 64), 64)
        return remote(
            out_ref.at[c, rows, :],
            out_ref.at[c, rows, :],
            send_sem.at[4, c],
            recv_sem.at[4, c],
            first_device,
        )

    def back_core(c):
        rows = pl.ds(kept, 128)
        return remote(
            out_ref.at[c, rows, :],
            out_ref.at[c, rows, :],
            send_sem.at[5, c],
            recv_sem.at[5, c],
            other_core,
        )

    def add_core(c):
        def act(source):
            core_copy(c, source).wait_recv()
            own_copy(c, source).wait()

        by_source(c, act)

        def put(s, r, value):
            half[c, s, pl.ds(r, 32), :] = value

        add_blocks(
            put,
            lambda s, r: half[c, s, pl.ds(r, 32), :],
            lambda s, r: own[c % 2, s, pl.ds(r, 32), :],
            4,
            128,
            32,
        )
        first_copy(c).start()

    def add_first(c):
        a, b, first_device, second_device = axes(c)
        first_copy(c).wait_recv()

        def put(s, r, value):
            quarter[c, s, pl.ds(r, 32), :] = value

        add_blocks(
            put,
            lambda s, r: quarter[c, s, pl.ds(r, 32), :],
            lambda s, r: half[c, s, pl.ds(pl.multiple_of(a * 64 + r, 32), 32), :],
            4,
            64,
            32,
        )
        second_copy(c).start()

    def add_second(c):
        a, b, first_device, second_device = axes(c)
        second_copy(c).wait_recv()

        def put(s, r, value):
            eighth[c, s, pl.ds(r, 32), :] = value

        add_blocks(
            put,
            lambda s, r: eighth[c, s, pl.ds(r, 32), :],
            lambda s, r: quarter[c, s, pl.ds(pl.multiple_of(b * 32 + r, 32), 32), :],
            4,
            32,
            32,
        )
        for d in range(3):
            z_copy(c, d).start()

    def add_z(c):
        for d in range(3):
            z_copy(c, d).wait_recv()
        total = eighth[c, z].astype(jnp.float32)
        for d in range(3):
            total = total + pieces[c, d].astype(jnp.float32)
        final[c] = total.astype(jnp.bfloat16)
        back_second(c).start()
        place_copy(c).start()

    def pass_first(c):
        place_copy(c).wait()
        back_second(c).wait_recv()
        back_first(c).start()

    def pass_core(c):
        back_first(c).wait_recv()
        back_core(c).start()

    def finish(c):
        back_core(c).wait()
        back_first(c).wait_send()
        back_second(c).wait_send()
        for d in range(3):
            z_copy(c, d).wait_send()
        second_copy(c).wait_send()
        first_copy(c).wait_send()
        by_source(c, lambda source: core_copy(c, source).wait_send())

    def small_copy(k):
        source = small_ref if k == 0 else small_sum.at[k - 1]
        device = (other_core, other_x, other_y)[k]
        return remote(source, small_in.at[k], small_send_sem.at[k], small_recv_sem.at[k], device)

    def small_z_copy(d):
        return remote(
            small_sum.at[2],
            small_z.at[z],
            small_send_sem.at[3 + d],
            small_recv_sem.at[3 + d],
            others_z[d],
        )

    def small_step(k):
        small_copy(k).wait()
        before = small_ref[...] if k == 0 else small_sum[k - 1]
        small_sum[k] = before + small_in[k]
        if k < 2:
            small_copy(k + 1).start()
        else:
            small_z[z] = small_sum[2]
            for d in range(3):
                small_z_copy(d).start()

    def small_end():
        for d in range(3):
            small_z_copy(d).wait()
        small_out_ref[...] = (small_z[0] + small_z[1]) + (small_z[2] + small_z[3])

    stages = (start_core, add_core, add_first, add_second, add_z, pass_first, pass_core, finish)
    small_copy(0).start()

    def step(t, carry):
        for k, stage in enumerate(stages):
            c = t - k

            @pl.when((c >= 0) & (c < CHUNKS))
            def _(stage=stage, c=c):
                stage(c)

        for k in range(3):

            @pl.when(t == k + 1)
            def _(k=k):
                small_step(k)

        @pl.when(t == 4)
        def _():
            small_end()

        return carry

    lax.fori_loop(0, CHUNKS + len(stages) - 1, step, 0)


def reduce_all(att, expand, shrink, small):
    small_rows = small.shape[0]
    dma = pltpu.SemaphoreType.DMA
    return pl.pallas_call(
        reduce_kernel,
        out_shape=(
            jax.ShapeDtypeStruct((CHUNKS, 256, D), jnp.bfloat16),
            jax.ShapeDtypeStruct(small.shape, jnp.float32),
        ),
        in_specs=[pl.BlockSpec(memory_space=pl.ANY)] * 3
        + [pl.BlockSpec(memory_space=pltpu.VMEM)],
        out_specs=(
            pl.BlockSpec(memory_space=pl.ANY),
            pl.BlockSpec(memory_space=pltpu.VMEM),
        ),
        scratch_shapes=[
            pltpu.VMEM((CHUNKS, 4, 128, D), jnp.bfloat16),
            pltpu.VMEM((2, 4, 128, D), jnp.bfloat16),
            pltpu.VMEM((CHUNKS, 4, 64, D), jnp.bfloat16),
            pltpu.VMEM((CHUNKS, 4, 32, D), jnp.bfloat16),
            pltpu.VMEM((CHUNKS, 3, 32, D), jnp.bfloat16),
            pltpu.VMEM((CHUNKS, 32, D), jnp.bfloat16),
            pltpu.VMEM((3, small_rows, 128), jnp.float32),
            pltpu.VMEM((3, small_rows, 128), jnp.float32),
            pltpu.VMEM((4, small_rows, 128), jnp.float32),
            dma((6, CHUNKS)),
            dma((6, CHUNKS)),
            dma((CHUNKS, 3)),
            dma((CHUNKS, 3)),
            dma((2,)),
            dma((CHUNKS,)),
            dma((6,)),
            dma((6,)),
        ],
        compiler_params=pltpu.CompilerParams(
            collective_id=0, has_side_effects=True, vmem_limit_bytes=48 * MIB
        ),
    )(att, expand, shrink, small)


def line_kernel(part_ref, out_ref, parts, send_sem, recv_sem):
    core, x, y, z, other_core, other_x, other_y, others_z = neighbours()
    greet(others_z)
    copies = [
        remote(part_ref, parts.at[z], send_sem.at[d], recv_sem.at[d], others_z[d])
        for d in range(3)
    ]
    for copy in copies:
        copy.start()
    parts[z] = part_ref[...]
    for copy in copies:
        copy.wait()
    out_ref[...] = (parts[0] + parts[1]) + (parts[2] + parts[3])


def sum_over_line(part):
    return pl.pallas_call(
        line_kernel,
        out_shape=jax.ShapeDtypeStruct(part.shape, jnp.float32),
        in_specs=[pl.BlockSpec(memory_space=pltpu.VMEM)],
        out_specs=pl.BlockSpec(memory_space=pltpu.VMEM),
        scratch_shapes=[
            pltpu.VMEM((4,) + part.shape, jnp.float32),
            pltpu.SemaphoreType.DMA((3,)),
            pltpu.SemaphoreType.DMA((3,)),
        ],
        compiler_params=pltpu.CompilerParams(collective_id=1, has_side_effects=True),
    )(part)


def as_rows(vector):
    rows = -(-vector.shape[0] // 1024) * 8
    return jnp.pad(vector, (0, rows * 128 - vector.shape[0])).reshape(rows, 128)


def gather_rows(piece):
    return lax.all_gather(piece, ("shard", "rep"), axis=0, tiled=True)


def own_piece(block, replicas):
    rows = block.shape[0] // replicas
    return lax.dynamic_slice_in_dim(block, lax.axis_index("rep") * rows, rows, axis=0)


def scatter_rows(grad):
    piece = lax.psum_scatter(
        grad.astype(jnp.bfloat16), ("shard", "rep"), scatter_dimension=0, tiled=True
    )
    return lax.all_gather(piece, "rep", axis=0, tiled=True)


def local_factors(grad, rows):
    square = grad * grad
    rows_new = DECAY_RATE * rows + (1.0 - DECAY_RATE) * jnp.mean(square + FACTOR_EPS, axis=-1)
    col_part = jnp.sum(square + FACTOR_EPS, axis=0)
    weighted = jnp.sum(square / rows_new[..., None], axis=0)
    return rows_new, col_part, weighted, jnp.sum(rows_new, axis=0)


def finish_factors(grad, weight, rows_new, cols, col_sum, weighted, row_total, row_count, rate):
    cols_new = DECAY_RATE * cols + (1.0 - DECAY_RATE) * col_sum / row_count
    mean_rows = row_total / row_count
    mean_square = mean_rows * jnp.sum(weighted / cols_new, axis=-1) / (row_count * cols.shape[-1])
    factor = rate / jnp.maximum(1.0, jnp.sqrt(mean_square) / CLIP_LEVEL)
    scaled = lax.rsqrt(cols_new / mean_rows[..., None]) * factor[..., None]
    fresh = weight - grad * (lax.rsqrt(rows_new)[..., None] * scaled[None])
    return fresh, cols_new


def on_device(
    tokens,
    encoder,
    cotangent,
    lengths,
    encoder_lengths,
    dealt_order,
    attention_weights,
    expand_weight,
    shrink_weight,
    small_params,
    attention_rows,
    attention_cols,
    expand_rows,
    expand_cols,
    shrink_rows,
    shrink_cols,
    small_moment,
):
    devices = lax.axis_size(("rep", "shard"))
    replicas = lax.axis_size("rep")
    shards = lax.axis_size("shard")
    slot_tokens = tokens.shape[0]
    slot_states = encoder.shape[0]
    position = lax.axis_index(("rep", "shard"))
    inverse = (
        jnp.zeros((devices,), jnp.int32).at[dealt_order].set(jnp.arange(devices, dtype=jnp.int32))
    )
    qkv_piece = own_piece(attention_weights[:, 0:3, :].reshape(-1, 3 * D), replicas)
    rest_piece = own_piece(attention_weights[:, 3:8, :].reshape(-1, 5 * D), replicas)
    qkv_full = gather_rows(qkv_piece.astype(jnp.bfloat16))
    rest_full = gather_rows(rest_piece.astype(jnp.bfloat16))
    expand_full = gather_rows(own_piece(expand_weight, replicas).astype(jnp.bfloat16))
    shrink_full = gather_rows(own_piece(shrink_weight, replicas).astype(jnp.bfloat16))
    spread = lax.all_to_all(
        tokens.reshape(devices, slot_tokens // devices, D),
        ("rep", "shard"),
        split_axis=0,
        concat_axis=0,
        tiled=True,
    )
    picked = jnp.take(spread, inverse, axis=0)
    tokens = lax.all_to_all(
        picked, ("rep", "shard"), split_axis=0, concat_axis=0, tiled=True
    ).reshape(slot_tokens, D)
    states = encoder
    incoming = cotangent
    valid_tokens = lengths[position]
    valid_states = encoder_lengths[position]
    matrices = [qkv_full[:, i * D : (i + 1) * D] for i in range(3)] + [
        rest_full[:, i * D : (i + 1) * D] for i in range(5)
    ]
    parts = unpack(small_params)
    token_heads = (slot_tokens, HEADS, HEAD_DIM)
    state_heads = (slot_states, HEADS, HEAD_DIM)
    q_self = ((forward_product(tokens, matrices[0]) + parts[0]) * 0.125).astype(
        jnp.bfloat16
    )
    k_self = forward_product(tokens, matrices[1]).astype(jnp.bfloat16)
    v_self = (forward_product(tokens, matrices[2]) + parts[1]).astype(jnp.bfloat16)
    o_self, lse_self = attend_forward(
        q_self.reshape(token_heads),
        k_self.reshape(token_heads),
        v_self.reshape(token_heads),
        valid_tokens,
        True,
    )
    o_self_low = o_self.reshape(slot_tokens, D).astype(jnp.bfloat16)
    branch_a = forward_product(o_self_low, matrices[3]) + parts[2]
    tokens_wide = tokens.astype(jnp.float32)
    hidden_one, norm_one_back = jax.vjp(layer_norm, tokens_wide + branch_a, parts[8], parts[9])
    hidden_one_low = hidden_one.astype(jnp.bfloat16)
    q_cross = (
        (forward_product(hidden_one_low, matrices[4]) + parts[3]) * 0.125
    ).astype(jnp.bfloat16)
    k_cross = forward_product(states, matrices[5]).astype(jnp.bfloat16)
    v_cross = (forward_product(states, matrices[6]) + parts[4]).astype(jnp.bfloat16)
    o_cross, lse_cross = attend_forward(
        q_cross.reshape(token_heads),
        k_cross.reshape(state_heads),
        v_cross.reshape(state_heads),
        valid_states,
        False,
    )
    o_cross_low = o_cross.reshape(slot_tokens, D).astype(jnp.bfloat16)
    branch_c = forward_product(o_cross_low, matrices[7]) + parts[5]
    hidden_two, norm_two_back = jax.vjp(layer_norm, hidden_one + branch_c, parts[10], parts[11])
    hidden_two_low = hidden_two.astype(jnp.bfloat16)
    pre_act = forward_product(hidden_two_low, expand_full) + parts[6]
    activated, gelu_back = jax.vjp(gelu_exact, pre_act)
    activated_low = activated.astype(jnp.bfloat16)
    branch_m = forward_product(activated_low, shrink_full) + parts[7]
    result, norm_three_back = jax.vjp(layer_norm, hidden_two + branch_m, parts[12], parts[13])
    usable_rows = (jnp.arange(slot_tokens, dtype=jnp.int32) < valid_tokens).astype(jnp.float32)[
        :, None
    ]
    squares = jnp.stack(
        [
            jnp.sum(usable_rows * t * t)
            for t in (tokens_wide, branch_a, hidden_one, branch_c, hidden_two, branch_m)
        ]
    )
    d_third, d_gain_three, d_shift_three = norm_three_back(
        incoming.astype(jnp.float32) * usable_rows
    )
    d_mlp = d_third.astype(jnp.bfloat16)
    grad_shrink = weight_product(activated_low, d_mlp)
    grad_shrink_offset = row_sum(d_mlp)
    d_activated = input_product(d_mlp, shrink_full)
    d_pre = gelu_back(d_activated)[0].astype(jnp.bfloat16)
    grad_expand = weight_product(hidden_two_low, d_pre)
    grad_expand_offset = row_sum(d_pre)
    d_hidden_two = d_third + input_product(d_pre, expand_full)
    d_second, d_gain_two, d_shift_two = norm_two_back(d_hidden_two)
    d_branch_c = d_second.astype(jnp.bfloat16)
    grad_cross_out = weight_product(o_cross_low, d_branch_c)
    grad_cross_out_offset = row_sum(d_branch_c)
    d_o_cross = input_product(d_branch_c, matrices[7]).astype(jnp.bfloat16)
    grad_cq, grad_ck, grad_cv = attend_backward(
        q_cross.reshape(token_heads),
        k_cross.reshape(state_heads),
        v_cross.reshape(state_heads),
        d_o_cross.reshape(token_heads),
        lse_cross,
        valid_states,
        False,
    )
    dq_cross = (grad_cq.reshape(slot_tokens, D) * 0.125).astype(jnp.bfloat16)
    dk_cross = grad_ck.reshape(slot_states, D).astype(jnp.bfloat16)
    dv_cross = grad_cv.reshape(slot_states, D).astype(jnp.bfloat16)
    grad_cross_query = weight_product(hidden_one_low, dq_cross)
    grad_cross_key = weight_product(states, dk_cross)
    grad_cross_value = weight_product(states, dv_cross)
    state_grad = input_product(dk_cross, matrices[5]) + input_product(
        dv_cross, matrices[6]
    )
    d_hidden_one = d_second + input_product(dq_cross, matrices[4])
    d_first, d_gain_one, d_shift_one = norm_one_back(d_hidden_one)
    d_branch_a = d_first.astype(jnp.bfloat16)
    grad_self_out = weight_product(o_self_low, d_branch_a)
    grad_self_out_offset = row_sum(d_branch_a)
    d_o_self = input_product(d_branch_a, matrices[3]).astype(jnp.bfloat16)
    grad_sq, grad_sk, grad_sv = attend_backward(
        q_self.reshape(token_heads),
        k_self.reshape(token_heads),
        v_self.reshape(token_heads),
        d_o_self.reshape(token_heads),
        lse_self,
        valid_tokens,
        True,
    )
    dq_self = (grad_sq.reshape(slot_tokens, D) * 0.125).astype(jnp.bfloat16)
    dk_self = grad_sk.reshape(slot_tokens, D).astype(jnp.bfloat16)
    dv_self = grad_sv.reshape(slot_tokens, D).astype(jnp.bfloat16)
    grad_self_query = weight_product(tokens, dq_self)
    grad_self_key = weight_product(tokens, dk_self)
    grad_self_value = weight_product(tokens, dv_self)
    token_grad = (
        d_first
        + input_product(dq_self, matrices[0])
        + input_product(dk_self, matrices[1])
        + input_product(dv_self, matrices[2])
    )
    small_partial = jnp.concatenate(
        [
            row_sum(dq_self),
            row_sum(dv_self),
            grad_self_out_offset,
            row_sum(dq_cross),
            row_sum(dv_cross),
            grad_cross_out_offset,
            grad_expand_offset,
            grad_shrink_offset,
            d_gain_one,
            d_shift_one,
            d_gain_two,
            d_shift_two,
            d_gain_three,
            d_shift_three,
        ]
    )
    attention_grads = [
        grad_self_query,
        grad_self_key,
        grad_self_value,
        grad_self_out,
        grad_cross_query,
        grad_cross_key,
        grad_cross_value,
        grad_cross_out,
    ]
    small_all = jnp.concatenate([small_partial, squares])
    direct = replicas == 8 and shards == 4
    if direct:
        reduced, totals = reduce_all(
            jnp.stack([t.astype(jnp.bfloat16) for t in attention_grads]).reshape(8, 4, 256, D),
            grad_expand.astype(jnp.bfloat16).reshape(4, 256, FF),
            grad_shrink.astype(jnp.bfloat16).reshape(4, 4, 256, D),
            as_rows(small_all),
        )
        totals = totals.reshape(-1)[: small_all.shape[0]]
        wide = reduced.astype(jnp.float32)
        g_attention = jnp.swapaxes(wide[0:8], 0, 1)
        g_expand = jnp.swapaxes(wide[8:12], 0, 1).reshape(-1, FF)
        g_shrink = wide[12:16].reshape(-1, D)
    else:
        totals = lax.psum(small_all, ("rep", "shard"))
        g_shrink = scatter_rows(grad_shrink).astype(jnp.float32)
        g_expand = scatter_rows(grad_expand).astype(jnp.float32)
        g_attention = (
            scatter_rows(jnp.concatenate(attention_grads, axis=1))
            .reshape(-1, 8, D)
            .astype(jnp.float32)
        )
    attention_rows_new, *attention_parts = local_factors(g_attention, attention_rows.T)
    expand_rows_new, *expand_parts = local_factors(g_expand, expand_rows)
    shrink_rows_new, *shrink_parts = local_factors(g_shrink, shrink_rows)
    flat = attention_parts + expand_parts + shrink_parts
    flat_parts = jnp.concatenate([t.reshape(-1) for t in flat])
    if direct:
        summed = sum_over_line(as_rows(flat_parts)).reshape(-1)
    else:
        summed = lax.psum(flat_parts, "shard")
    sums = []
    offset = 0
    for t in flat:
        sums.append(summed[offset : offset + t.size].reshape(t.shape))
        offset = offset + t.size
    attention_rates = STEP_RATE * jnp.where(jnp.arange(8) % 4 == 3, OUT_GAIN, 1.0).astype(
        jnp.float32
    )
    attention_new, attention_cols_new = finish_factors(
        g_attention,
        attention_weights,
        attention_rows_new,
        attention_cols,
        *sums[0:3],
        D,
        attention_rates,
    )
    expand_new, expand_cols_new = finish_factors(
        g_expand, expand_weight, expand_rows_new, expand_cols, *sums[3:6], D, STEP_RATE
    )
    shrink_new, shrink_cols_new = finish_factors(
        g_shrink, shrink_weight, shrink_rows_new, shrink_cols, *sums[6:9], FF, STEP_RATE
    )
    small_grad = totals[: small_params.shape[0]]
    small_moment_new = DECAY_RATE * small_moment + (1.0 - DECAY_RATE) * (
        small_grad * small_grad + FACTOR_EPS
    )
    small_update = small_grad * lax.rsqrt(small_moment_new)
    small_scale = jnp.sqrt(jnp.mean(small_update * small_update))
    small_new = small_params - SMALL_RATE * small_update / jnp.maximum(
        1.0, small_scale / CLIP_LEVEL
    )
    norm_stats = jnp.sqrt(
        totals[small_params.shape[0] :] / (jnp.sum(lengths).astype(jnp.float32) * D)
    )
    return (
        result.astype(jnp.bfloat16),
        token_grad.astype(jnp.bfloat16),
        state_grad.astype(jnp.bfloat16),
        g_attention,
        g_expand,
        g_shrink,
        small_grad,
        attention_new,
        expand_new,
        shrink_new,
        small_new,
        attention_new.astype(jnp.bfloat16),
        expand_new.astype(jnp.bfloat16),
        shrink_new.astype(jnp.bfloat16),
        attention_rows_new.T,
        attention_cols_new,
        expand_rows_new,
        expand_cols_new,
        shrink_rows_new,
        shrink_cols_new,
        small_moment_new,
        norm_stats,
    )


def solution(mesh):
    in_specs = (
        P(("rep", "shard"), None),
        P(("rep", "shard"), None),
        P(("rep", "shard"), None),
        P(),
        P(),
        P(),
        P("shard", None, None),
        P("shard", None),
        P("shard", None),
        P(),
        P(None, "shard"),
        P(),
        P("shard"),
        P(),
        P("shard"),
        P(),
        P(),
    )
    out_specs = (
        P(("rep", "shard"), None),
        P(("rep", "shard"), None),
        P(("rep", "shard"), None),
        P("shard", None, None),
        P("shard", None),
        P("shard", None),
        P(),
        P("shard", None, None),
        P("shard", None),
        P("shard", None),
        P(),
        P("shard", None, None),
        P("shard", None),
        P("shard", None),
        P(None, "shard"),
        P(),
        P("shard"),
        P(),
        P("shard"),
        P(),
        P(),
        P(),
    )
    return jax.shard_map(
        on_device, mesh=mesh, in_specs=in_specs, out_specs=out_specs, check_vma=False
    )
```

```python
import jax
import jax.numpy as jnp
from jax import lax
from jax.experimental import pallas as pl
from jax.experimental.pallas import tpu as pltpu
from jax.sharding import PartitionSpec as P

D = 1024
FF = 4096


DECAY_RATE = 0.5
CLIP_LEVEL = 0.25
STEP_RATE = 0.1
SMALL_RATE = 0.4
OUT_GAIN = 8.0
NORM_EPS = 1e-05
FACTOR_EPS = 1e-30
MASKED = -1e30
MESH = pl.DeviceIdType.MESH
CHUNKS = 16
MIB = 1 << 20


def layer_norm(r, norm_gain, norm_shift):
    centred = r - jnp.mean(r, axis=-1, keepdims=True)
    spread = jnp.mean(centred * centred, axis=-1, keepdims=True)
    return centred * lax.rsqrt(spread + NORM_EPS) * norm_gain + norm_shift


def gelu_exact(values):
    return jax.nn.gelu(values, approximate=False)


def unpack(small):
    extents = [D] * 6 + [FF] + [D] * 7
    pieces = []
    offset = 0
    for extent in extents:
        pieces.append(small[offset : offset + extent])
        offset = offset + extent
    return pieces


def forward_product(source, matrix):
    return jnp.dot(source, matrix, preferred_element_type=jnp.float32)


def input_product(grad_low, matrix):
    return jnp.einsum("to,io->ti", grad_low, matrix, preferred_element_type=jnp.float32)


def weight_product(source, grad_low):
    return jnp.einsum("ti,to->io", source, grad_low, preferred_element_type=jnp.float32)


def row_sum(grad_low):
    return jnp.sum(grad_low.astype(jnp.float32), axis=0)


def transposed(block):
    return block.astype(jnp.float32).T.astype(jnp.bfloat16)


def half_lanes(shape, dim):
    return lax.broadcasted_iota(jnp.int32, shape, dim)


def masked_keys(keys, length, head):
    place = half_lanes(keys.shape, 0)
    lane = half_lanes(keys.shape, 1)
    blocked = jnp.where((lane == 64 - 64 * head) & (place >= length), MASKED, 0.0)
    own = (lane >= 64 * head) & (lane < 64 * head + 64)
    return jnp.where(own, keys.astype(jnp.float32), blocked).astype(jnp.bfloat16)


def own_head(rows_t, head, fill):
    place = half_lanes(rows_t.shape, 0)
    own = (place >= 64 * head) & (place < 64 * head + 64)
    other = jnp.where(place == 64 - 64 * head, fill, 0.0)
    return jnp.where(own, rows_t.astype(jnp.float32), other).astype(jnp.bfloat16)


def product(first, second):
    return jnp.dot(first, second, preferred_element_type=jnp.float32)


def causal_mask(scores, step):
    kept = scores.shape[0] - step
    last = scores[kept:]
    allowed = half_lanes(last.shape, 0) <= half_lanes(last.shape, 1)
    last = jnp.where(allowed, last, MASKED)
    return last if kept == 0 else jnp.concatenate([scores[:kept], last], axis=0)


def attend_kernel(causal, step, length_ref, q_ref, k_ref, v_ref, o_ref, lse_ref, o_t):
    length = length_ref[0]
    q_t = transposed(q_ref[...])
    v_t = transposed(v_ref[...])
    for head in range(2):
        keys = masked_keys(k_ref[...], length, head)
        queries = own_head(q_t, head, 1.0)
        rows = slice(64 * head, 64 * head + 64)
        for start in range(0, q_ref.shape[0], step):
            columns = slice(start, start + step)
            end = start + step if causal else k_ref.shape[0]
            scores = product(keys[:end], queries[:, columns])
            if causal:
                scores = causal_mask(scores, step)
            top = jnp.max(scores, axis=0, keepdims=True)
            raised = jnp.exp(scores - top)
            total = jnp.sum(raised, axis=0, keepdims=True)
            probs = (raised * (1.0 / total)).astype(jnp.bfloat16)
            o_t[rows, columns] = product(v_t[rows, :end], probs)
            lse_ref[0, head : head + 1, columns] = top + jnp.log(total)
    o_ref[...] = o_t[...].T.astype(jnp.bfloat16)


def attend_back_kernel(
    causal,
    step,
    length_ref,
    q_ref,
    k_ref,
    v_ref,
    do_ref,
    lse_ref,
    dq_ref,
    dk_ref,
    dv_ref,
    sums_ref,
    dq_t,
    dk_sum,
    dv_sum,
):
    length = length_ref[0]
    q_t = transposed(q_ref[...])
    k_t = transposed(k_ref[...])
    do_t = transposed(do_ref[...])
    values = v_ref[...]
    for head in range(2):
        keys = masked_keys(k_ref[...], length, head)
        queries = own_head(q_t, head, 1.0)
        grads = own_head(do_t, head, 0.0)
        rows = slice(64 * head, 64 * head + 64)
        count = q_ref.shape[0] // step
        for b in reversed(range(count)):
            start = b * step
            columns = slice(start, start + step)
            end = start + step if causal else k_ref.shape[0]
            scores = product(keys[:end], queries[:, columns])
            if causal:
                scores = causal_mask(scores, step)
            probs = jnp.exp(scores - lse_ref[0, head : head + 1, columns])
            weighted = probs * product(values[:end], grads[:, columns])
            delta = jnp.sum(weighted, axis=0, keepdims=True)
            d_scores = (weighted - probs * delta).astype(jnp.bfloat16)
            dv = product(probs.astype(jnp.bfloat16), do_ref[columns, :])
            dk = product(d_scores, q_ref[columns, :])
            if b == count - 1:
                dv_sum[head] = dv
                dk_sum[head] = dk
            else:
                dv_sum[head, :end] += dv
                dk_sum[head, :end] += dk
            dq_t[rows, columns] = product(k_t[rows, :end], d_scores)
    first = half_lanes(dk_ref.shape, 1) < 64
    dk_ref[...] = jnp.where(first, dk_sum[0], dk_sum[1]).astype(jnp.bfloat16)
    dv = jnp.where(first, dv_sum[0], dv_sum[1]).astype(jnp.bfloat16)
    dv_ref[...] = dv
    dq = (dq_t[...] * 0.125).T.astype(jnp.bfloat16)
    dq_ref[...] = dq
    sums_ref[0, 0:1, :] = jnp.sum(dq.astype(jnp.float32), axis=0, keepdims=True)
    sums_ref[0, 1:2, :] = jnp.sum(dv.astype(jnp.float32), axis=0, keepdims=True)


def pair_block(rows):
    return pl.BlockSpec((rows, 128), lambda i: (0, i))


def pair_rows(columns):
    return pl.BlockSpec((1, 8, columns), lambda i: (i, 0, 0))


SCALARS = pl.BlockSpec(memory_space=pltpu.SMEM)


def attend(queries, keys, values, length, causal):
    rows, key_rows = queries.shape[0], keys.shape[0]
    pairs = queries.shape[1] // 128
    return pl.pallas_call(
        lambda *refs: attend_kernel(causal, 256 if causal else 512, *refs),
        grid=(pairs,),
        out_shape=(
            jax.ShapeDtypeStruct(queries.shape, jnp.bfloat16),
            jax.ShapeDtypeStruct((pairs, 8, rows), jnp.float32),
        ),
        in_specs=[SCALARS, pair_block(rows), pair_block(key_rows), pair_block(key_rows)],
        out_specs=(pair_block(rows), pair_rows(rows)),
        scratch_shapes=[pltpu.VMEM((128, rows), jnp.float32)],
        compiler_params=pltpu.CompilerParams(vmem_limit_bytes=40 * MIB),
    )(length.reshape(1), queries, keys, values)


def attend_back(queries, keys, values, grads, lse, length, causal):
    rows, key_rows = queries.shape[0], keys.shape[0]
    pairs = queries.shape[1] // 128
    return pl.pallas_call(
        lambda *refs: attend_back_kernel(causal, 256 if causal else 512, *refs),
        grid=(pairs,),
        out_shape=(
            jax.ShapeDtypeStruct(queries.shape, jnp.bfloat16),
            jax.ShapeDtypeStruct(keys.shape, jnp.bfloat16),
            jax.ShapeDtypeStruct(keys.shape, jnp.bfloat16),
            jax.ShapeDtypeStruct((pairs, 8, 128), jnp.float32),
        ),
        in_specs=[
            SCALARS,
            pair_block(rows),
            pair_block(key_rows),
            pair_block(key_rows),
            pair_block(rows),
            pair_rows(rows),
        ],
        out_specs=(pair_block(rows), pair_block(key_rows), pair_block(key_rows), pair_rows(128)),
        scratch_shapes=[
            pltpu.VMEM((128, rows), jnp.float32),
            pltpu.VMEM((2, key_rows, 128), jnp.float32),
            pltpu.VMEM((2, key_rows, 128), jnp.float32),
        ],
        compiler_params=pltpu.CompilerParams(vmem_limit_bytes=40 * MIB),
    )(length.reshape(1), queries, keys, values, grads, lse)


def neighbours():
    rep = lax.axis_index("rep")
    z = lax.axis_index("shard")
    core = rep % 2
    x = (rep // 2) % 2
    y = rep // 4
    other_core = (rep + 1 - 2 * core, z)
    other_x = (rep + 2 - 4 * x, z)
    other_y = (rep + 4 - 8 * y, z)
    others_z = [(rep, (z + d) % 4) for d in (1, 2, 3)]
    return core, x, y, z, other_core, other_x, other_y, others_z


def greet(devices):
    barrier = pltpu.get_barrier_semaphore()
    for device in devices:
        pl.semaphore_signal(barrier, inc=1, device_id=device, device_id_type=MESH)
    pl.semaphore_wait(barrier, len(devices))


def remote(src, dst, send, recv, device):
    return pltpu.make_async_remote_copy(
        src_ref=src, dst_ref=dst, send_sem=send, recv_sem=recv, device_id=device, device_id_type=MESH
    )


def add_blocks(target, first, second, planes, rows, step):
    per_plane = rows // step

    def body(i, carry):
        s = i // per_plane
        r = pl.multiple_of((i % per_plane) * step, step)
        total = first(s, r).astype(jnp.float32) + second(s, r).astype(jnp.float32)
        target(s, r, total.astype(jnp.bfloat16))
        return carry

    lax.fori_loop(0, planes * per_plane, body, 0)


def reduce_kernel(
    att_ref,
    exp_ref,
    shr_ref,
    small_ref,
    out_ref,
    small_out_ref,
    half,
    own,
    quarter,
    eighth,
    pieces,
    final,
    small_in,
    small_sum,
    small_z,
    send_sem,
    recv_sem,
    z_send_sem,
    z_recv_sem,
    own_sem,
    place_sem,
    small_send_sem,
    small_recv_sem,
):
    core, x, y, z, other_core, other_x, other_y, others_z = neighbours()
    greet([other_core, other_x, other_y] + others_z)

    def axes(c):
        odd = c % 2
        a = x + odd * (y - x)
        b = y + odd * (x - y)
        dx = other_x[0]
        dy = other_y[0]
        return a, b, (dx + odd * (dy - dx), z), (dy + odd * (dx - dy), z)

    def by_source(c, act):
        @pl.when(c < 8)
        def _():
            act(lambda part: att_ref.at[c, :, pl.ds(part, 128), :])

        @pl.when((c >= 8) & (c < 12))
        def _():
            act(
                lambda part: exp_ref.at[
                    :, pl.ds(part, 128), pl.ds(pl.multiple_of((c - 8) * D, D), D)
                ]
            )

        @pl.when(c >= 12)
        def _():
            act(lambda part: shr_ref.at[:, c - 12, pl.ds(part, 128), :])

    kept = pl.multiple_of(core * 128, 128)
    given = pl.multiple_of(128 - core * 128, 128)

    def core_copy(c, source):
        return remote(
            source(given), half.at[c], send_sem.at[0, c], recv_sem.at[0, c], other_core
        )

    def own_copy(c, source):
        return pltpu.make_async_copy(source(kept), own.at[c % 2], own_sem.at[c % 2])

    def start_core(c):
        def act(source):
            core_copy(c, source).start()
            own_copy(c, source).start()

        by_source(c, act)

    def first_copy(c):
        a, b, first_device, second_device = axes(c)
        rows = pl.multiple_of(64 - a * 64, 64)
        return remote(
            half.at[c, :, pl.ds(rows, 64), :],
            quarter.at[c],
            send_sem.at[1, c],
            recv_sem.at[1, c],
            first_device,
        )

    def second_copy(c):
        a, b, first_device, second_device = axes(c)
        rows = pl.multiple_of(32 - b * 32, 32)
        return remote(
            quarter.at[c, :, pl.ds(rows, 32), :],
            eighth.at[c],
            send_sem.at[2, c],
            recv_sem.at[2, c],
            second_device,
        )

    def z_copy(c, d):
        device = others_z[d]
        return remote(
            eighth.at[c, device[1]],
            pieces.at[c, d],
            z_send_sem.at[c, d],
            z_recv_sem.at[c, d],
            device,
        )

    def place_copy(c):
        a, b, first_device, second_device = axes(c)
        rows = pl.ds(pl.multiple_of(core * 128 + a * 64 + b * 32, 32), 32)
        return pltpu.make_async_copy(final.at[c], out_ref.at[c, rows, :], place_sem.at[c])

    def back_second(c):
        a, b, first_device, second_device = axes(c)
        rows = pl.ds(pl.multiple_of(core * 128 + a * 64 + b * 32, 32), 32)
        return remote(
            final.at[c], out_ref.at[c, rows, :], send_sem.at[3, c], recv_sem.at[3, c], second_device
        )

    def back_first(c):
        a, b, first_device, second_device = axes(c)
        rows = pl.ds(pl.multiple_of(core * 128 + a * 64, 64), 64)
        return remote(
            out_ref.at[c, rows, :],
            out_ref.at[c, rows, :],
            send_sem.at[4, c],
            recv_sem.at[4, c],
            first_device,
        )

    def back_core(c):
        rows = pl.ds(kept, 128)
        return remote(
            out_ref.at[c, rows, :],
            out_ref.at[c, rows, :],
            send_sem.at[5, c],
            recv_sem.at[5, c],
            other_core,
        )

    def add_core(c):
        def act(source):
            core_copy(c, source).wait_recv()
            own_copy(c, source).wait()

        by_source(c, act)

        def put(s, r, value):
            half[c, s, pl.ds(r, 32), :] = value

        add_blocks(
            put,
            lambda s, r: half[c, s, pl.ds(r, 32), :],
            lambda s, r: own[c % 2, s, pl.ds(r, 32), :],
            4,
            128,
            32,
        )
        first_copy(c).start()

    def add_first(c):
        a, b, first_device, second_device = axes(c)
        first_copy(c).wait_recv()

        def put(s, r, value):
            quarter[c, s, pl.ds(r, 32), :] = value

        add_blocks(
            put,
            lambda s, r: quarter[c, s, pl.ds(r, 32), :],
            lambda s, r: half[c, s, pl.ds(pl.multiple_of(a * 64 + r, 32), 32), :],
            4,
            64,
            32,
        )
        second_copy(c).start()

    def add_second(c):
        a, b, first_device, second_device = axes(c)
        second_copy(c).wait_recv()

        def put(s, r, value):
            eighth[c, s, pl.ds(r, 32), :] = value

        add_blocks(
            put,
            lambda s, r: eighth[c, s, pl.ds(r, 32), :],
            lambda s, r: quarter[c, s, pl.ds(pl.multiple_of(b * 32 + r, 32), 32), :],
            4,
            32,
            32,
        )
        for d in range(3):
            z_copy(c, d).start()

    def add_z(c):
        for d in range(3):
            z_copy(c, d).wait_recv()
        total = eighth[c, z].astype(jnp.float32)
        for d in range(3):
            total = total + pieces[c, d].astype(jnp.float32)
        final[c] = total.astype(jnp.bfloat16)
        back_second(c).start()
        place_copy(c).start()

    def pass_first(c):
        place_copy(c).wait()
        back_second(c).wait_recv()
        back_first(c).start()

    def pass_core(c):
        back_first(c).wait_recv()
        back_core(c).start()

    def finish(c):
        back_core(c).wait()
        back_first(c).wait_send()
        back_second(c).wait_send()
        for d in range(3):
            z_copy(c, d).wait_send()
        second_copy(c).wait_send()
        first_copy(c).wait_send()
        by_source(c, lambda source: core_copy(c, source).wait_send())

    def small_copy(k):
        source = small_ref if k == 0 else small_sum.at[k - 1]
        device = (other_core, other_x, other_y)[k]
        return remote(source, small_in.at[k], small_send_sem.at[k], small_recv_sem.at[k], device)

    def small_z_copy(d):
        return remote(
            small_sum.at[2],
            small_z.at[z],
            small_send_sem.at[3 + d],
            small_recv_sem.at[3 + d],
            others_z[d],
        )

    def small_step(k):
        small_copy(k).wait()
        before = small_ref[...] if k == 0 else small_sum[k - 1]
        small_sum[k] = before + small_in[k]
        if k < 2:
            small_copy(k + 1).start()
        else:
            small_z[z] = small_sum[2]
            for d in range(3):
                small_z_copy(d).start()

    def small_end():
        for d in range(3):
            small_z_copy(d).wait()
        small_out_ref[...] = (small_z[0] + small_z[1]) + (small_z[2] + small_z[3])

    stages = (start_core, add_core, add_first, add_second, add_z, pass_first, pass_core, finish)
    small_copy(0).start()

    def step(t, carry):
        for k, stage in enumerate(stages):
            c = t - k

            @pl.when((c >= 0) & (c < CHUNKS))
            def _(stage=stage, c=c):
                stage(c)

        for k in range(3):

            @pl.when(t == k + 1)
            def _(k=k):
                small_step(k)

        @pl.when(t == 4)
        def _():
            small_end()

        return carry

    lax.fori_loop(0, CHUNKS + len(stages) - 1, step, 0)


def reduce_all(att, expand, shrink, small):
    small_rows = small.shape[0]
    dma = pltpu.SemaphoreType.DMA
    return pl.pallas_call(
        reduce_kernel,
        out_shape=(
            jax.ShapeDtypeStruct((CHUNKS, 256, D), jnp.bfloat16),
            jax.ShapeDtypeStruct(small.shape, jnp.float32),
        ),
        in_specs=[pl.BlockSpec(memory_space=pl.ANY)] * 3
        + [pl.BlockSpec(memory_space=pltpu.VMEM)],
        out_specs=(
            pl.BlockSpec(memory_space=pl.ANY),
            pl.BlockSpec(memory_space=pltpu.VMEM),
        ),
        scratch_shapes=[
            pltpu.VMEM((CHUNKS, 4, 128, D), jnp.bfloat16),
            pltpu.VMEM((2, 4, 128, D), jnp.bfloat16),
            pltpu.VMEM((CHUNKS, 4, 64, D), jnp.bfloat16),
            pltpu.VMEM((CHUNKS, 4, 32, D), jnp.bfloat16),
            pltpu.VMEM((CHUNKS, 3, 32, D), jnp.bfloat16),
            pltpu.VMEM((CHUNKS, 32, D), jnp.bfloat16),
            pltpu.VMEM((3, small_rows, 128), jnp.float32),
            pltpu.VMEM((3, small_rows, 128), jnp.float32),
            pltpu.VMEM((4, small_rows, 128), jnp.float32),
            dma((6, CHUNKS)),
            dma((6, CHUNKS)),
            dma((CHUNKS, 3)),
            dma((CHUNKS, 3)),
            dma((2,)),
            dma((CHUNKS,)),
            dma((6,)),
            dma((6,)),
        ],
        compiler_params=pltpu.CompilerParams(
            collective_id=0, has_side_effects=True, vmem_limit_bytes=48 * MIB
        ),
    )(att, expand, shrink, small)


def line_sum(part, whole, send_sem, recv_sem, z, others_z):
    copies = [
        remote(part, whole.at[z], send_sem.at[d], recv_sem.at[d], others_z[d]) for d in range(3)
    ]
    for copy in copies:
        copy.start()
    whole[z] = part[...]
    for copy in copies:
        copy.wait()
    return (whole[0] + whole[1]) + (whole[2] + whole[3])


def fold(tile):
    return tile[0:8] + tile[8:16]


def spread_scalar(value):
    return jnp.broadcast_to(value, (1, 128))


def factor_kernel(
    grad_ref,
    att_rows_ref,
    exp_rows_ref,
    shr_rows_ref,
    cols_ref,
    att_rows_out,
    exp_rows_out,
    shr_rows_out,
    cols_out,
    scale_out,
    part,
    whole,
    send_sem,
    recv_sem,
):
    core, x, y, z, other_core, other_x, other_y, others_z = neighbours()
    greet(others_z)
    part[...] = jnp.zeros_like(part)

    def tile(chunk, r):
        return grad_ref[chunk, pl.ds(r, 16), :].astype(jnp.float32)

    def add(slot, col, weighted):
        part[slot : slot + 1, :] += jnp.sum(col, axis=0, keepdims=True)
        part[16 + slot : 17 + slot, :] += jnp.sum(weighted, axis=0, keepdims=True)

    def scan_rows(chunks, slots, rows_in, rows_out, total_at):
        width = float(len(chunks) * D)

        def body(i, carry):
            cols, weights, total = carry
            r = pl.multiple_of(i * 16, 16)
            squares = [jnp.square(tile(c, r)) for c in chunks]
            row_sum = squares[0]
            for square in squares[1:]:
                row_sum = row_sum + square
            row_sum = jnp.sum(row_sum, axis=1, keepdims=True)
            rows = DECAY_RATE * rows_in[pl.ds(r, 16), :] + (1.0 - DECAY_RATE) * (
                row_sum / width + FACTOR_EPS
            )
            rows_out[pl.ds(r, 16), :] = rows
            inverse = 1.0 / rows
            cols = [c + fold(s) for c, s in zip(cols, squares)]
            weights = [w + fold(s * inverse) for w, s in zip(weights, squares)]
            return cols, weights, total + fold(rows)

        zeros = [jnp.zeros((8, D), jnp.float32) for _ in chunks]
        cols, weights, total = lax.fori_loop(
            0, 16, body, (zeros, zeros, jnp.zeros((8, 1), jnp.float32))
        )
        for slot, col, weighted in zip(slots, cols, weights):
            add(slot, col, weighted)
        row, lane = total_at
        part[row : row + 1, lane : lane + 128] += spread_scalar(jnp.sum(total))

    for i in range(8):
        scan_rows([i], [i], att_rows_ref.at[i], att_rows_out.at[i], (13, 128 * i))
    scan_rows([8, 9, 10, 11], [8, 9, 10, 11], exp_rows_ref, exp_rows_out, (14, 0))
    for i in range(4):
        scan_rows([12 + i], [12], shr_rows_ref.at[i], shr_rows_out.at[i], (14, 128))
    total = line_sum(part, whole, send_sem, recv_sem, z, others_z)
    row_counts = [D] * 12 + [FF]
    means = [total[13:14, 128 * i : 128 * i + 1] / D for i in range(8)]
    means = means + [total[14:15, 0:1] / D] * 4 + [total[14:15, 128:129] / FF]
    cols_new, quotients = [], []
    for slot in range(13):
        new = DECAY_RATE * cols_ref[slot : slot + 1, :] + (1.0 - DECAY_RATE) * (
            total[slot : slot + 1] / row_counts[slot] + FACTOR_EPS
        )
        cols_new.append(new)
        quotients.append(jnp.sum(total[16 + slot : 17 + slot] / new, axis=1, keepdims=True))
        cols_out[slot : slot + 1, :] = new
    expand_quotient = quotients[8] + quotients[9] + quotients[10] + quotients[11]
    for slot in range(13):
        if slot < 8:
            mean_square = means[slot] * quotients[slot] / (D * D)
            rate = STEP_RATE * (OUT_GAIN if slot % 4 == 3 else 1.0)
        else:
            quotient = expand_quotient if slot < 12 else quotients[12]
            mean_square = means[slot] * quotient / (D * FF)
            rate = STEP_RATE
        factor = rate / jnp.maximum(1.0, jnp.sqrt(mean_square) / CLIP_LEVEL)
        scale_out[slot : slot + 1, :] = lax.rsqrt(cols_new[slot] / means[slot]) * factor


def factors(grads, att_rows, exp_rows, shr_rows, cols):
    vmem = pl.BlockSpec(memory_space=pltpu.VMEM)
    shape = jax.ShapeDtypeStruct
    return pl.pallas_call(
        factor_kernel,
        out_shape=(
            shape((8, 256, 1), jnp.float32),
            shape((256, 1), jnp.float32),
            shape((4, 256, 1), jnp.float32),
            shape((16, D), jnp.float32),
            shape((16, D), jnp.float32),
        ),
        in_specs=[vmem] * 5,
        out_specs=(vmem,) * 5,
        scratch_shapes=[
            pltpu.VMEM((32, D), jnp.float32),
            pltpu.VMEM((4, 32, D), jnp.float32),
            pltpu.SemaphoreType.DMA((3,)),
            pltpu.SemaphoreType.DMA((3,)),
        ],
        compiler_params=pltpu.CompilerParams(
            collective_id=1, has_side_effects=True, vmem_limit_bytes=40 * MIB
        ),
    )(grads, att_rows, exp_rows, shr_rows, cols)


def update_attention_kernel(
    grad_ref, weight_ref, rows_ref, scale_ref, grad_out, new_out, copy_out, grads, change
):
    block = grad_ref.shape[1]
    for i in range(8):
        grad = grad_ref[i].astype(jnp.float32)
        scaled = grad * lax.rsqrt(rows_ref[i]) * scale_ref[i : i + 1, :]
        every = pl.ds(i, block, stride=8)
        for lane in range(8):
            columns = slice(lane * 128, lane * 128 + 128)
            grads[lane, every, :] = grad[:, columns]
            change[lane, every, :] = scaled[:, columns]
    for lane in range(8):
        columns = slice(lane * 128, lane * 128 + 128)
        grad_out[:, columns] = grads[lane]
        new = weight_ref[:, columns] - change[lane]
        new_out[:, columns] = new
        copy_out[:, columns] = new.astype(jnp.bfloat16)


def update_attention(grads, weights, rows, scale):
    block = 32
    wide = pl.BlockSpec((block * 8, D), lambda i: (i, 0))
    shape = jax.ShapeDtypeStruct
    new = pl.pallas_call(
        update_attention_kernel,
        grid=(256 // block,),
        out_shape=(
            shape((2048, D), jnp.float32),
            shape((2048, D), jnp.float32),
            shape((2048, D), jnp.bfloat16),
        ),
        in_specs=[
            pl.BlockSpec((8, block, D), lambda i: (0, i, 0)),
            wide,
            pl.BlockSpec((8, block, 1), lambda i: (0, i, 0)),
            pl.BlockSpec((16, D), lambda i: (0, 0)),
        ],
        out_specs=(wide,) * 3,
        scratch_shapes=[pltpu.VMEM((8, block * 8, 128), jnp.float32)] * 2,
        compiler_params=pltpu.CompilerParams(vmem_limit_bytes=40 * MIB),
    )(grads, weights.reshape(2048, D), rows, scale)
    return [t.reshape(256, 8, D) for t in new]


def update_kernel(first, slots, grad_ref, weight_ref, rows_ref, scale_ref, grad_out, new_out, copy_out):
    for i in range(slots):
        grad = grad_ref[i].astype(jnp.float32)
        columns = slice(i * D, i * D + D)
        grad_out[:, columns] = grad
        new = weight_ref[:, columns] - grad * (
            lax.rsqrt(rows_ref[...]) * scale_ref[first + i : first + i + 1, :]
        )
        new_out[:, columns] = new
        copy_out[:, columns] = new.astype(jnp.bfloat16)


def update_plain(grads, weights, rows, scale, first, slots, grad_map):
    count, width = weights.shape
    block = 128 // slots
    wide = pl.BlockSpec((block, width), lambda i: (i, 0))
    shape = jax.ShapeDtypeStruct
    return pl.pallas_call(
        lambda *refs: update_kernel(first, slots, *refs),
        grid=(count // block,),
        out_shape=(
            shape(weights.shape, jnp.float32),
            shape(weights.shape, jnp.float32),
            shape(weights.shape, jnp.bfloat16),
        ),
        in_specs=[
            pl.BlockSpec((slots, block, D), grad_map),
            wide,
            pl.BlockSpec((block, 1), lambda i: (i, 0)),
            pl.BlockSpec((16, D), lambda i: (0, 0)),
        ],
        out_specs=(wide,) * 3,
        compiler_params=pltpu.CompilerParams(vmem_limit_bytes=40 * MIB),
    )(grads, weights, rows, scale)


def update_direct(
    grads,
    attention_weights,
    expand_weight,
    shrink_weight,
    attention_rows,
    attention_cols,
    expand_rows,
    expand_cols,
    shrink_rows,
    shrink_cols,
):
    cols = jnp.concatenate(
        [attention_cols, expand_cols.reshape(4, D), shrink_cols.reshape(1, D), jnp.ones((3, D))]
    )
    att_rows, exp_rows, shr_rows, cols_new, scale = factors(
        grads,
        attention_rows[:, :, None],
        expand_rows[:, None],
        shrink_rows.reshape(4, 256, 1),
        cols,
    )
    shr_rows = shr_rows.reshape(-1, 1)
    attention = update_attention(grads, attention_weights, att_rows, scale)
    expand = update_plain(grads, expand_weight, exp_rows, scale, 8, 4, lambda i: (2, i, 0))
    shrink = update_plain(
        grads, shrink_weight, shr_rows, scale, 12, 1, lambda i: (12 + i // 2, i % 2, 0)
    )
    return (
        attention,
        expand,
        shrink,
        (att_rows[:, :, 0], exp_rows[:, 0], shr_rows[:, 0]),
        (cols_new[0:8], cols_new[8:12].reshape(-1), cols_new[12]),
    )


def as_rows(vector):
    rows = -(-vector.shape[0] // 1024) * 8
    return jnp.pad(vector, (0, rows * 128 - vector.shape[0])).reshape(rows, 128)


def gather_rows(piece):
    return lax.all_gather(piece, ("shard", "rep"), axis=0, tiled=True)


def own_piece(block, replicas):
    rows = block.shape[0] // replicas
    return lax.dynamic_slice_in_dim(block, lax.axis_index("rep") * rows, rows, axis=0)


def scatter_rows(grad):
    piece = lax.psum_scatter(
        grad.astype(jnp.bfloat16), ("shard", "rep"), scatter_dimension=0, tiled=True
    )
    return lax.all_gather(piece, "rep", axis=0, tiled=True)


def local_factors(grad, rows):
    square = grad * grad
    rows_new = DECAY_RATE * rows + (1.0 - DECAY_RATE) * jnp.mean(square + FACTOR_EPS, axis=-1)
    col_part = jnp.sum(square + FACTOR_EPS, axis=0)
    weighted = jnp.sum(square / rows_new[..., None], axis=0)
    return rows_new, col_part, weighted, jnp.sum(rows_new, axis=0)


def finish_factors(grad, weight, rows_new, cols, col_sum, weighted, row_total, row_count, rate):
    cols_new = DECAY_RATE * cols + (1.0 - DECAY_RATE) * col_sum / row_count
    mean_rows = row_total / row_count
    mean_square = mean_rows * jnp.sum(weighted / cols_new, axis=-1) / (row_count * cols.shape[-1])
    factor = rate / jnp.maximum(1.0, jnp.sqrt(mean_square) / CLIP_LEVEL)
    scaled = lax.rsqrt(cols_new / mean_rows[..., None]) * factor[..., None]
    fresh = weight - grad * (lax.rsqrt(rows_new)[..., None] * scaled[None])
    return fresh, cols_new


def on_device(
    tokens,
    encoder,
    cotangent,
    lengths,
    encoder_lengths,
    dealt_order,
    attention_weights,
    expand_weight,
    shrink_weight,
    small_params,
    attention_rows,
    attention_cols,
    expand_rows,
    expand_cols,
    shrink_rows,
    shrink_cols,
    small_moment,
):
    devices = lax.axis_size(("rep", "shard"))
    replicas = lax.axis_size("rep")
    shards = lax.axis_size("shard")
    slot_tokens = tokens.shape[0]
    slot_states = encoder.shape[0]
    position = lax.axis_index(("rep", "shard"))
    inverse = (
        jnp.zeros((devices,), jnp.int32).at[dealt_order].set(jnp.arange(devices, dtype=jnp.int32))
    )
    qkv_piece = own_piece(attention_weights[:, 0:3, :].reshape(-1, 3 * D), replicas)
    rest_piece = own_piece(attention_weights[:, 3:8, :].reshape(-1, 5 * D), replicas)
    qkv_full = gather_rows(qkv_piece.astype(jnp.bfloat16))
    rest_full = gather_rows(rest_piece.astype(jnp.bfloat16))
    expand_full = gather_rows(own_piece(expand_weight, replicas).astype(jnp.bfloat16))
    shrink_full = gather_rows(own_piece(shrink_weight, replicas).astype(jnp.bfloat16))
    spread = lax.all_to_all(
        tokens.reshape(devices, slot_tokens // devices, D),
        ("rep", "shard"),
        split_axis=0,
        concat_axis=0,
        tiled=True,
    )
    picked = jnp.take(spread, inverse, axis=0)
    tokens = lax.all_to_all(
        picked, ("rep", "shard"), split_axis=0, concat_axis=0, tiled=True
    ).reshape(slot_tokens, D)
    states = encoder
    incoming = cotangent
    valid_tokens = lengths[position]
    valid_states = encoder_lengths[position]
    matrices = [qkv_full[:, i * D : (i + 1) * D] for i in range(3)] + [
        rest_full[:, i * D : (i + 1) * D] for i in range(5)
    ]
    parts = unpack(small_params)
    q_self = ((forward_product(tokens, matrices[0]) + parts[0]) * 0.125).astype(
        jnp.bfloat16
    )
    k_self = forward_product(tokens, matrices[1]).astype(jnp.bfloat16)
    v_self = (forward_product(tokens, matrices[2]) + parts[1]).astype(jnp.bfloat16)
    o_self_low, lse_self = attend(q_self, k_self, v_self, valid_tokens, True)
    branch_a = forward_product(o_self_low, matrices[3]) + parts[2]
    tokens_wide = tokens.astype(jnp.float32)
    hidden_one, norm_one_back = jax.vjp(layer_norm, tokens_wide + branch_a, parts[8], parts[9])
    hidden_one_low = hidden_one.astype(jnp.bfloat16)
    q_cross = (
        (forward_product(hidden_one_low, matrices[4]) + parts[3]) * 0.125
    ).astype(jnp.bfloat16)
    k_cross = forward_product(states, matrices[5]).astype(jnp.bfloat16)
    v_cross = (forward_product(states, matrices[6]) + parts[4]).astype(jnp.bfloat16)
    o_cross_low, lse_cross = attend(q_cross, k_cross, v_cross, valid_states, False)
    branch_c = forward_product(o_cross_low, matrices[7]) + parts[5]
    hidden_two, norm_two_back = jax.vjp(layer_norm, hidden_one + branch_c, parts[10], parts[11])
    hidden_two_low = hidden_two.astype(jnp.bfloat16)
    pre_act = forward_product(hidden_two_low, expand_full) + parts[6]
    activated, gelu_back = jax.vjp(gelu_exact, pre_act)
    activated_low = activated.astype(jnp.bfloat16)
    branch_m = forward_product(activated_low, shrink_full) + parts[7]
    result, norm_three_back = jax.vjp(layer_norm, hidden_two + branch_m, parts[12], parts[13])
    usable_rows = (jnp.arange(slot_tokens, dtype=jnp.int32) < valid_tokens).astype(jnp.float32)[
        :, None
    ]
    squares = jnp.stack(
        [
            jnp.sum(usable_rows * t * t)
            for t in (tokens_wide, branch_a, hidden_one, branch_c, hidden_two, branch_m)
        ]
    )
    d_third, d_gain_three, d_shift_three = norm_three_back(
        incoming.astype(jnp.float32) * usable_rows
    )
    d_mlp = d_third.astype(jnp.bfloat16)
    grad_shrink = weight_product(activated_low, d_mlp)
    grad_shrink_offset = row_sum(d_mlp)
    d_activated = input_product(d_mlp, shrink_full)
    d_pre = gelu_back(d_activated)[0].astype(jnp.bfloat16)
    grad_expand = weight_product(hidden_two_low, d_pre)
    grad_expand_offset = row_sum(d_pre)
    d_hidden_two = d_third + input_product(d_pre, expand_full)
    d_second, d_gain_two, d_shift_two = norm_two_back(d_hidden_two)
    d_branch_c = d_second.astype(jnp.bfloat16)
    grad_cross_out = weight_product(o_cross_low, d_branch_c)
    grad_cross_out_offset = row_sum(d_branch_c)
    d_o_cross = input_product(d_branch_c, matrices[7]).astype(jnp.bfloat16)
    dq_cross, dk_cross, dv_cross, cross_sums = attend_back(
        q_cross, k_cross, v_cross, d_o_cross, lse_cross, valid_states, False
    )
    grad_cross_query = weight_product(hidden_one_low, dq_cross)
    grad_cross_key = weight_product(states, dk_cross)
    grad_cross_value = weight_product(states, dv_cross)
    state_grad = input_product(dk_cross, matrices[5]) + input_product(
        dv_cross, matrices[6]
    )
    d_hidden_one = d_second + input_product(dq_cross, matrices[4])
    d_first, d_gain_one, d_shift_one = norm_one_back(d_hidden_one)
    d_branch_a = d_first.astype(jnp.bfloat16)
    grad_self_out = weight_product(o_self_low, d_branch_a)
    grad_self_out_offset = row_sum(d_branch_a)
    d_o_self = input_product(d_branch_a, matrices[3]).astype(jnp.bfloat16)
    dq_self, dk_self, dv_self, self_sums = attend_back(
        q_self, k_self, v_self, d_o_self, lse_self, valid_tokens, True
    )
    grad_self_query = weight_product(tokens, dq_self)
    grad_self_key = weight_product(tokens, dk_self)
    grad_self_value = weight_product(tokens, dv_self)
    token_grad = (
        d_first
        + input_product(dq_self, matrices[0])
        + input_product(dk_self, matrices[1])
        + input_product(dv_self, matrices[2])
    )
    small_partial = jnp.concatenate(
        [
            self_sums[:, 0, :].reshape(-1),
            self_sums[:, 1, :].reshape(-1),
            grad_self_out_offset,
            cross_sums[:, 0, :].reshape(-1),
            cross_sums[:, 1, :].reshape(-1),
            grad_cross_out_offset,
            grad_expand_offset,
            grad_shrink_offset,
            d_gain_one,
            d_shift_one,
            d_gain_two,
            d_shift_two,
            d_gain_three,
            d_shift_three,
        ]
    )
    attention_grads = [
        grad_self_query,
        grad_self_key,
        grad_self_value,
        grad_self_out,
        grad_cross_query,
        grad_cross_key,
        grad_cross_value,
        grad_cross_out,
    ]
    small_all = jnp.concatenate([small_partial, squares])
    direct = replicas == 8 and shards == 4
    if direct:
        reduced, totals = reduce_all(
            jnp.stack([t.astype(jnp.bfloat16) for t in attention_grads]).reshape(8, 4, 256, D),
            grad_expand.astype(jnp.bfloat16).reshape(4, 256, FF),
            grad_shrink.astype(jnp.bfloat16).reshape(4, 4, 256, D),
            as_rows(small_all),
        )
        totals = totals.reshape(-1)[: small_all.shape[0]]
        (
            (g_attention, attention_new, attention_copy),
            (g_expand, expand_new, expand_copy),
            (g_shrink, shrink_new, shrink_copy),
            (attention_rows_new, expand_rows_new, shrink_rows_new),
            (attention_cols_new, expand_cols_new, shrink_cols_new),
        ) = update_direct(
            reduced,
            attention_weights,
            expand_weight,
            shrink_weight,
            attention_rows,
            attention_cols,
            expand_rows,
            expand_cols,
            shrink_rows,
            shrink_cols,
        )
    else:
        totals = lax.psum(small_all, ("rep", "shard"))
        g_shrink = scatter_rows(grad_shrink).astype(jnp.float32)
        g_expand = scatter_rows(grad_expand).astype(jnp.float32)
        g_attention = (
            scatter_rows(jnp.concatenate(attention_grads, axis=1))
            .reshape(-1, 8, D)
            .astype(jnp.float32)
        )
        attention_rows_new, *attention_parts = local_factors(g_attention, attention_rows.T)
        expand_rows_new, *expand_parts = local_factors(g_expand, expand_rows)
        shrink_rows_new, *shrink_parts = local_factors(g_shrink, shrink_rows)
        flat = attention_parts + expand_parts + shrink_parts
        flat_parts = jnp.concatenate([t.reshape(-1) for t in flat])
        summed = lax.psum(flat_parts, "shard")
        sums = []
        offset = 0
        for t in flat:
            sums.append(summed[offset : offset + t.size].reshape(t.shape))
            offset = offset + t.size
        attention_rates = STEP_RATE * jnp.where(jnp.arange(8) % 4 == 3, OUT_GAIN, 1.0).astype(
            jnp.float32
        )
        attention_new, attention_cols_new = finish_factors(
            g_attention,
            attention_weights,
            attention_rows_new,
            attention_cols,
            *sums[0:3],
            D,
            attention_rates,
        )
        expand_new, expand_cols_new = finish_factors(
            g_expand, expand_weight, expand_rows_new, expand_cols, *sums[3:6], D, STEP_RATE
        )
        shrink_new, shrink_cols_new = finish_factors(
            g_shrink, shrink_weight, shrink_rows_new, shrink_cols, *sums[6:9], FF, STEP_RATE
        )
        attention_rows_new = attention_rows_new.T
        attention_copy = attention_new.astype(jnp.bfloat16)
        expand_copy = expand_new.astype(jnp.bfloat16)
        shrink_copy = shrink_new.astype(jnp.bfloat16)
    small_grad = totals[: small_params.shape[0]]
    small_moment_new = DECAY_RATE * small_moment + (1.0 - DECAY_RATE) * (
        small_grad * small_grad + FACTOR_EPS
    )
    small_update = small_grad * lax.rsqrt(small_moment_new)
    small_scale = jnp.sqrt(jnp.mean(small_update * small_update))
    small_new = small_params - SMALL_RATE * small_update / jnp.maximum(
        1.0, small_scale / CLIP_LEVEL
    )
    norm_stats = jnp.sqrt(
        totals[small_params.shape[0] :] / (jnp.sum(lengths).astype(jnp.float32) * D)
    )
    return (
        result.astype(jnp.bfloat16),
        token_grad.astype(jnp.bfloat16),
        state_grad.astype(jnp.bfloat16),
        g_attention,
        g_expand,
        g_shrink,
        small_grad,
        attention_new,
        expand_new,
        shrink_new,
        small_new,
        attention_copy,
        expand_copy,
        shrink_copy,
        attention_rows_new,
        attention_cols_new,
        expand_rows_new,
        expand_cols_new,
        shrink_rows_new,
        shrink_cols_new,
        small_moment_new,
        norm_stats,
    )


def solution(mesh):
    in_specs = (
        P(("rep", "shard"), None),
        P(("rep", "shard"), None),
        P(("rep", "shard"), None),
        P(),
        P(),
        P(),
        P("shard", None, None),
        P("shard", None),
        P("shard", None),
        P(),
        P(None, "shard"),
        P(),
        P("shard"),
        P(),
        P("shard"),
        P(),
        P(),
    )
    out_specs = (
        P(("rep", "shard"), None),
        P(("rep", "shard"), None),
        P(("rep", "shard"), None),
        P("shard", None, None),
        P("shard", None),
        P("shard", None),
        P(),
        P("shard", None, None),
        P("shard", None),
        P("shard", None),
        P(),
        P("shard", None, None),
        P("shard", None),
        P("shard", None),
        P(None, "shard"),
        P(),
        P("shard"),
        P(),
        P("shard"),
        P(),
        P(),
        P(),
    )
    return jax.shard_map(
        on_device, mesh=mesh, in_specs=in_specs, out_specs=out_specs, check_vma=False
    )
```

```python
import jax
import jax.numpy as jnp
from jax import lax
from jax.experimental import pallas as pl
from jax.experimental.pallas import tpu as pltpu
from jax.sharding import PartitionSpec as P

D = 1024
FF = 4096


DECAY_RATE = 0.5
CLIP_LEVEL = 0.25
STEP_RATE = 0.1
SMALL_RATE = 0.4
OUT_GAIN = 8.0
NORM_EPS = 1e-05
FACTOR_EPS = 1e-30
MASKED = -1e30
MESH = pl.DeviceIdType.MESH
CHUNKS = 16
MIB = 1 << 20


def layer_norm(r, norm_gain, norm_shift):
    centred = r - jnp.mean(r, axis=-1, keepdims=True)
    spread = jnp.mean(centred * centred, axis=-1, keepdims=True)
    return centred * lax.rsqrt(spread + NORM_EPS) * norm_gain + norm_shift


def gelu_exact(values):
    return jax.nn.gelu(values, approximate=False)


def unpack(small):
    extents = [D] * 6 + [FF] + [D] * 7
    pieces = []
    offset = 0
    for extent in extents:
        pieces.append(small[offset : offset + extent])
        offset = offset + extent
    return pieces


def forward_product(source, matrix):
    return jnp.dot(source, matrix, preferred_element_type=jnp.float32)


def input_product(grad_low, matrix):
    return jnp.einsum("to,io->ti", grad_low, matrix, preferred_element_type=jnp.float32)


def weight_product(source, grad_low):
    return jnp.einsum("ti,to->io", source, grad_low, preferred_element_type=jnp.float32)


def row_sum(grad_low):
    return jnp.sum(grad_low.astype(jnp.float32), axis=0)


def transposed(block):
    return block.astype(jnp.float32).T.astype(jnp.bfloat16)


def half_lanes(shape, dim):
    return lax.broadcasted_iota(jnp.int32, shape, dim)


def masked_keys(keys, length, head):
    place = half_lanes(keys.shape, 0)
    lane = half_lanes(keys.shape, 1)
    blocked = jnp.where((lane == 64 - 64 * head) & (place >= length), MASKED, 0.0)
    own = (lane >= 64 * head) & (lane < 64 * head + 64)
    return jnp.where(own, keys.astype(jnp.float32), blocked).astype(jnp.bfloat16)


def own_head(rows_t, head, fill):
    place = half_lanes(rows_t.shape, 0)
    own = (place >= 64 * head) & (place < 64 * head + 64)
    other = jnp.where(place == 64 - 64 * head, fill, 0.0)
    return jnp.where(own, rows_t.astype(jnp.float32), other).astype(jnp.bfloat16)


def product(first, second):
    return jnp.dot(first, second, preferred_element_type=jnp.float32)


def causal_mask(scores, step):
    kept = scores.shape[0] - step
    last = scores[kept:]
    allowed = half_lanes(last.shape, 0) <= half_lanes(last.shape, 1)
    last = jnp.where(allowed, last, MASKED)
    return last if kept == 0 else jnp.concatenate([scores[:kept], last], axis=0)


def attend_kernel(causal, step, length_ref, q_ref, k_ref, v_ref, o_ref, lse_ref, o_t):
    length = length_ref[0]
    q_t = transposed(q_ref[...])
    v_t = transposed(v_ref[...])
    for head in range(2):
        keys = masked_keys(k_ref[...], length, head)
        queries = own_head(q_t, head, 1.0)
        rows = slice(64 * head, 64 * head + 64)
        for start in range(0, q_ref.shape[0], step):
            columns = slice(start, start + step)
            end = start + step if causal else k_ref.shape[0]
            scores = product(keys[:end], queries[:, columns])
            if causal:
                scores = causal_mask(scores, step)
            top = jnp.max(scores, axis=0, keepdims=True)
            raised = jnp.exp(scores - top)
            total = jnp.sum(raised, axis=0, keepdims=True)
            probs = (raised * (1.0 / total)).astype(jnp.bfloat16)
            o_t[rows, columns] = product(v_t[rows, :end], probs)
            lse_ref[0, head : head + 1, columns] = top + jnp.log(total)
    o_ref[...] = o_t[...].T.astype(jnp.bfloat16)


def attend_back_kernel(
    causal,
    step,
    length_ref,
    q_ref,
    k_ref,
    v_ref,
    do_ref,
    lse_ref,
    dq_ref,
    dk_ref,
    dv_ref,
    sums_ref,
    dq_t,
    dk_sum,
    dv_sum,
):
    length = length_ref[0]
    q_t = transposed(q_ref[...])
    k_t = transposed(k_ref[...])
    do_t = transposed(do_ref[...])
    values = v_ref[...]
    for head in range(2):
        keys = masked_keys(k_ref[...], length, head)
        queries = own_head(q_t, head, 1.0)
        grads = own_head(do_t, head, 0.0)
        rows = slice(64 * head, 64 * head + 64)
        count = q_ref.shape[0] // step
        for b in reversed(range(count)):
            start = b * step
            columns = slice(start, start + step)
            end = start + step if causal else k_ref.shape[0]
            scores = product(keys[:end], queries[:, columns])
            if causal:
                scores = causal_mask(scores, step)
            probs = jnp.exp(scores - lse_ref[0, head : head + 1, columns])
            weighted = probs * product(values[:end], grads[:, columns])
            delta = jnp.sum(weighted, axis=0, keepdims=True)
            d_scores = (weighted - probs * delta).astype(jnp.bfloat16)
            dv = product(probs.astype(jnp.bfloat16), do_ref[columns, :])
            dk = product(d_scores, q_ref[columns, :])
            if b == count - 1:
                dv_sum[head] = dv
                dk_sum[head] = dk
            else:
                dv_sum[head, :end] += dv
                dk_sum[head, :end] += dk
            dq_t[rows, columns] = product(k_t[rows, :end], d_scores)
    first = half_lanes(dk_ref.shape, 1) < 64
    dk_ref[...] = jnp.where(first, dk_sum[0], dk_sum[1]).astype(jnp.bfloat16)
    dv = jnp.where(first, dv_sum[0], dv_sum[1]).astype(jnp.bfloat16)
    dv_ref[...] = dv
    dq = (dq_t[...] * 0.125).T.astype(jnp.bfloat16)
    dq_ref[...] = dq
    sums_ref[0, 0:1, :] = jnp.sum(dq.astype(jnp.float32), axis=0, keepdims=True)
    sums_ref[0, 1:2, :] = jnp.sum(dv.astype(jnp.float32), axis=0, keepdims=True)


def pair_block(rows):
    return pl.BlockSpec((rows, 128), lambda i: (0, i))


def pair_rows(columns):
    return pl.BlockSpec((1, 8, columns), lambda i: (i, 0, 0))


SCALARS = pl.BlockSpec(memory_space=pltpu.SMEM)


def attend(queries, keys, values, length, causal):
    rows, key_rows = queries.shape[0], keys.shape[0]
    pairs = queries.shape[1] // 128
    return pl.pallas_call(
        lambda *refs: attend_kernel(causal, 256 if causal else 512, *refs),
        grid=(pairs,),
        out_shape=(
            jax.ShapeDtypeStruct(queries.shape, jnp.bfloat16),
            jax.ShapeDtypeStruct((pairs, 8, rows), jnp.float32),
        ),
        in_specs=[SCALARS, pair_block(rows), pair_block(key_rows), pair_block(key_rows)],
        out_specs=(pair_block(rows), pair_rows(rows)),
        scratch_shapes=[pltpu.VMEM((128, rows), jnp.float32)],
        compiler_params=pltpu.CompilerParams(vmem_limit_bytes=40 * MIB),
    )(length.reshape(1), queries, keys, values)


def attend_back(queries, keys, values, grads, lse, length, causal):
    rows, key_rows = queries.shape[0], keys.shape[0]
    pairs = queries.shape[1] // 128
    return pl.pallas_call(
        lambda *refs: attend_back_kernel(causal, 256 if causal else 512, *refs),
        grid=(pairs,),
        out_shape=(
            jax.ShapeDtypeStruct(queries.shape, jnp.bfloat16),
            jax.ShapeDtypeStruct(keys.shape, jnp.bfloat16),
            jax.ShapeDtypeStruct(keys.shape, jnp.bfloat16),
            jax.ShapeDtypeStruct((pairs, 8, 128), jnp.float32),
        ),
        in_specs=[
            SCALARS,
            pair_block(rows),
            pair_block(key_rows),
            pair_block(key_rows),
            pair_block(rows),
            pair_rows(rows),
        ],
        out_specs=(pair_block(rows), pair_block(key_rows), pair_block(key_rows), pair_rows(128)),
        scratch_shapes=[
            pltpu.VMEM((128, rows), jnp.float32),
            pltpu.VMEM((2, key_rows, 128), jnp.float32),
            pltpu.VMEM((2, key_rows, 128), jnp.float32),
        ],
        compiler_params=pltpu.CompilerParams(vmem_limit_bytes=40 * MIB),
    )(length.reshape(1), queries, keys, values, grads, lse)


def neighbours():
    rep = lax.axis_index("rep")
    z = lax.axis_index("shard")
    core = rep % 2
    x = (rep // 2) % 2
    y = rep // 4
    other_core = (rep + 1 - 2 * core, z)
    other_x = (rep + 2 - 4 * x, z)
    other_y = (rep + 4 - 8 * y, z)
    others_z = [(rep, (z + d) % 4) for d in (1, 2, 3)]
    return core, x, y, z, other_core, other_x, other_y, others_z


def greet(devices):
    barrier = pltpu.get_barrier_semaphore()
    for device in devices:
        pl.semaphore_signal(barrier, inc=1, device_id=device, device_id_type=MESH)
    pl.semaphore_wait(barrier, len(devices))


def remote(src, dst, send, recv, device):
    return pltpu.make_async_remote_copy(
        src_ref=src, dst_ref=dst, send_sem=send, recv_sem=recv, device_id=device, device_id_type=MESH
    )


def gather_copies(refs, c, parity, places):
    piece, full, place_sem, z_send, z_recv, send, recv = refs
    core, x, y, z, other_core, other_x, other_y, others_z = places
    a = x + parity * (y - x)
    b = y + parity * (x - y)
    first = (other_x[0] + parity * (other_y[0] - other_x[0]), z)
    second = (other_y[0] + parity * (other_x[0] - other_y[0]), z)
    own = pl.ds(pl.multiple_of(core * 128 + a * 64 + b * 32, 32), 32)
    steps = (
        (own, second),
        (pl.ds(pl.multiple_of(core * 128 + a * 64, 64), 64), first),
        (pl.ds(pl.multiple_of(core * 128, 128), 128), other_core),
    )

    def local():
        return pltpu.make_async_copy(piece.at[c], full.at[c, z, own, :], place_sem.at[c])

    def line(d):
        return remote(
            piece.at[c], full.at[c, z, own, :], z_send.at[c, d], z_recv.at[c, d], others_z[d]
        )

    def pair(k):
        block = full.at[c, :, steps[k][0], :]
        return remote(block, block, send.at[k, c], recv.at[k, c], steps[k][1])

    return local, line, pair


def gather_stage(k, refs, c, parity, places):
    local, line, pair = gather_copies(refs, c, parity, places)
    if k == 0:
        local().start()
        for d in range(3):
            line(d).start()
    if k == 1:
        local().wait()
        for d in range(3):
            line(d).wait_recv()
        pair(0).start()
    if k == 2 or k == 3:
        pair(k - 2).wait_recv()
        pair(k - 1).start()
    if k == 4:
        pair(2).wait()
        pair(1).wait_send()
        pair(0).wait_send()
        for d in range(3):
            line(d).wait_send()


def gather_sems(count):
    dma = pltpu.SemaphoreType.DMA
    return [dma((count,)), dma((count, 3)), dma((count, 3)), dma((3, count)), dma((3, count))]


def weight_pieces(weights, places):
    core, x, y = places[0:3]
    even = lax.dynamic_slice_in_dim(weights, core * 128 + x * 64 + y * 32, 32, axis=0)
    odd = lax.dynamic_slice_in_dim(weights, core * 128 + y * 64 + x * 32, 32, axis=0)
    chosen = jnp.where((jnp.arange(8) % 2 == 0)[None, :, None], even, odd)
    return jnp.swapaxes(chosen, 0, 1).astype(jnp.bfloat16)


def front_kernel(
    order_ref,
    tokens_ref,
    piece_ref,
    x_ref,
    full_ref,
    spread,
    picked,
    spread_send,
    spread_recv,
    back_send,
    back_recv,
    *gather_sem,
):
    places = neighbours()
    z = places[3]
    me = lax.axis_index("rep") * 4 + z
    refs = (piece_ref, full_ref) + gather_sem

    def device(offset):
        j = lax.rem(me + offset, 32)
        return j, (j // 4, j % 4)

    barrier = pltpu.get_barrier_semaphore()

    def greet_one(offset, carry):
        pl.semaphore_signal(barrier, inc=1, device_id=device(offset)[1], device_id_type=MESH)
        return carry

    lax.fori_loop(1, 32, greet_one, 0)
    pl.semaphore_wait(barrier, 31)

    def stage(k):
        for c in range(3):
            gather_stage(k, refs, c, c % 2, places)

    def spread_copy(offset):
        j, target = device(offset)
        return remote(
            tokens_ref.at[j],
            spread.at[me],
            spread_send.at[offset],
            spread_recv.at[offset],
            target,
        )

    def back_copy(offset):
        target = device(offset)[1]
        return remote(
            picked.at[offset], x_ref.at[me], back_send.at[offset], back_recv.at[offset], target
        )

    own_in = pltpu.make_async_copy(tokens_ref.at[me], spread.at[me], spread_recv.at[0])
    own_out = pltpu.make_async_copy(picked.at[0], x_ref.at[me], back_recv.at[0])
    stage(0)
    own_in.start()

    def start_spread(offset, carry):
        spread_copy(offset).start()
        return carry

    lax.fori_loop(1, 32, start_spread, 0)
    stage(1)
    stage(2)
    own_in.wait()

    def wait_spread(offset, carry):
        spread_copy(offset).wait()
        return carry

    lax.fori_loop(1, 32, wait_spread, 0)
    picked[0] = spread[order_ref[me]]
    own_out.start()

    def pick(offset, carry):
        picked[offset] = spread[order_ref[device(offset)[0]]]
        back_copy(offset).start()
        return carry

    lax.fori_loop(1, 32, pick, 0)
    stage(3)
    stage(4)
    own_out.wait()

    def wait_back(offset, carry):
        back_copy(offset).wait()
        return carry

    lax.fori_loop(1, 32, wait_back, 0)


def front(inverse, tokens, pieces):
    dma = pltpu.SemaphoreType.DMA
    any_space = pl.BlockSpec(memory_space=pl.ANY)
    x, full = pl.pallas_call(
        front_kernel,
        out_shape=(
            jax.ShapeDtypeStruct((32, 32, D), jnp.bfloat16),
            jax.ShapeDtypeStruct((3, 4, 256, D), jnp.bfloat16),
        ),
        in_specs=[
            pl.BlockSpec(memory_space=pltpu.SMEM),
            any_space,
            pl.BlockSpec(memory_space=pltpu.VMEM),
        ],
        out_specs=(any_space, any_space),
        scratch_shapes=[
            pltpu.VMEM((32, 32, D), jnp.bfloat16),
            pltpu.VMEM((32, 32, D), jnp.bfloat16),
            dma((32,)),
            dma((32,)),
            dma((32,)),
            dma((32,)),
        ]
        + gather_sems(3),
        compiler_params=pltpu.CompilerParams(
            collective_id=2, has_side_effects=True, vmem_limit_bytes=24 * MIB
        ),
    )(inverse, tokens.reshape(32, 32, D), pieces)
    return x.reshape(1024, D), full.reshape(3, 1024, D)


def attend_gather_kernel(
    length_ref, q_ref, k_ref, v_ref, piece_ref, o_ref, lse_ref, full_ref, o_t, *gather_sem
):
    places = neighbours()
    t = pl.program_id(0)
    refs = (piece_ref, full_ref) + gather_sem

    @pl.when(t == 0)
    def _():
        greet(list(places[4:7]) + places[7])

    for k in range(5):
        for j in range(2):
            c = 2 * (t - k) + j

            @pl.when((t >= k) & (c < 5))
            def _(k=k, j=j, c=c):
                gather_stage(k, refs, c, 1 - j, places)

    attend_kernel(True, 256, length_ref, q_ref, k_ref, v_ref, o_ref, lse_ref, o_t)


def attend_gather(queries, keys, values, length, pieces):
    rows = queries.shape[0]
    pairs = queries.shape[1] // 128
    any_space = pl.BlockSpec(memory_space=pl.ANY)
    out, lse, full = pl.pallas_call(
        attend_gather_kernel,
        grid=(pairs,),
        out_shape=(
            jax.ShapeDtypeStruct(queries.shape, jnp.bfloat16),
            jax.ShapeDtypeStruct((pairs, 8, rows), jnp.float32),
            jax.ShapeDtypeStruct((5, 4, 256, D), jnp.bfloat16),
        ),
        in_specs=[SCALARS, pair_block(rows), pair_block(rows), pair_block(rows), any_space],
        out_specs=(pair_block(rows), pair_rows(rows), any_space),
        scratch_shapes=[pltpu.VMEM((128, rows), jnp.float32)] + gather_sems(5),
        compiler_params=pltpu.CompilerParams(
            collective_id=3, has_side_effects=True, vmem_limit_bytes=40 * MIB
        ),
    )(length.reshape(1), queries, keys, values, pieces)
    return out, lse, full.reshape(5, 1024, D)


def add_blocks(target, first, second, planes, rows, step):
    per_plane = rows // step

    def body(i, carry):
        s = i // per_plane
        r = pl.multiple_of((i % per_plane) * step, step)
        total = first(s, r).astype(jnp.float32) + second(s, r).astype(jnp.float32)
        target(s, r, total.astype(jnp.bfloat16))
        return carry

    lax.fori_loop(0, planes * per_plane, body, 0)


def reduce_kernel(
    att_ref,
    exp_ref,
    shr_ref,
    small_ref,
    out_ref,
    small_out_ref,
    half,
    own,
    quarter,
    eighth,
    pieces,
    final,
    small_in,
    small_sum,
    small_z,
    send_sem,
    recv_sem,
    z_send_sem,
    z_recv_sem,
    own_sem,
    place_sem,
    small_send_sem,
    small_recv_sem,
):
    core, x, y, z, other_core, other_x, other_y, others_z = neighbours()
    greet([other_core, other_x, other_y] + others_z)

    def axes(c):
        odd = c % 2
        a = x + odd * (y - x)
        b = y + odd * (x - y)
        dx = other_x[0]
        dy = other_y[0]
        return a, b, (dx + odd * (dy - dx), z), (dy + odd * (dx - dy), z)

    def by_source(c, act):
        @pl.when(c < 8)
        def _():
            act(lambda part: att_ref.at[c, :, pl.ds(part, 128), :])

        @pl.when((c >= 8) & (c < 12))
        def _():
            act(
                lambda part: exp_ref.at[
                    :, pl.ds(part, 128), pl.ds(pl.multiple_of((c - 8) * D, D), D)
                ]
            )

        @pl.when(c >= 12)
        def _():
            act(lambda part: shr_ref.at[:, c - 12, pl.ds(part, 128), :])

    kept = pl.multiple_of(core * 128, 128)
    given = pl.multiple_of(128 - core * 128, 128)

    def core_copy(c, source):
        return remote(
            source(given), half.at[c], send_sem.at[0, c], recv_sem.at[0, c], other_core
        )

    def own_copy(c, source):
        return pltpu.make_async_copy(source(kept), own.at[c % 2], own_sem.at[c % 2])

    def start_core(c):
        def act(source):
            core_copy(c, source).start()
            own_copy(c, source).start()

        by_source(c, act)

    def first_copy(c):
        a, b, first_device, second_device = axes(c)
        rows = pl.multiple_of(64 - a * 64, 64)
        return remote(
            half.at[c, :, pl.ds(rows, 64), :],
            quarter.at[c],
            send_sem.at[1, c],
            recv_sem.at[1, c],
            first_device,
        )

    def second_copy(c):
        a, b, first_device, second_device = axes(c)
        rows = pl.multiple_of(32 - b * 32, 32)
        return remote(
            quarter.at[c, :, pl.ds(rows, 32), :],
            eighth.at[c],
            send_sem.at[2, c],
            recv_sem.at[2, c],
            second_device,
        )

    def z_copy(c, d):
        device = others_z[d]
        return remote(
            eighth.at[c, device[1]],
            pieces.at[c, d],
            z_send_sem.at[c, d],
            z_recv_sem.at[c, d],
            device,
        )

    def place_copy(c):
        a, b, first_device, second_device = axes(c)
        rows = pl.ds(pl.multiple_of(core * 128 + a * 64 + b * 32, 32), 32)
        return pltpu.make_async_copy(final.at[c], out_ref.at[c, rows, :], place_sem.at[c])

    def back_second(c):
        a, b, first_device, second_device = axes(c)
        rows = pl.ds(pl.multiple_of(core * 128 + a * 64 + b * 32, 32), 32)
        return remote(
            final.at[c], out_ref.at[c, rows, :], send_sem.at[3, c], recv_sem.at[3, c], second_device
        )

    def back_first(c):
        a, b, first_device, second_device = axes(c)
        rows = pl.ds(pl.multiple_of(core * 128 + a * 64, 64), 64)
        return remote(
            out_ref.at[c, rows, :],
            out_ref.at[c, rows, :],
            send_sem.at[4, c],
            recv_sem.at[4, c],
            first_device,
        )

    def back_core(c):
        rows = pl.ds(kept, 128)
        return remote(
            out_ref.at[c, rows, :],
            out_ref.at[c, rows, :],
            send_sem.at[5, c],
            recv_sem.at[5, c],
            other_core,
        )

    def add_core(c):
        def act(source):
            core_copy(c, source).wait_recv()
            own_copy(c, source).wait()

        by_source(c, act)

        def put(s, r, value):
            half[c, s, pl.ds(r, 32), :] = value

        add_blocks(
            put,
            lambda s, r: half[c, s, pl.ds(r, 32), :],
            lambda s, r: own[c % 2, s, pl.ds(r, 32), :],
            4,
            128,
            32,
        )
        first_copy(c).start()

    def add_first(c):
        a, b, first_device, second_device = axes(c)
        first_copy(c).wait_recv()

        def put(s, r, value):
            quarter[c, s, pl.ds(r, 32), :] = value

        add_blocks(
            put,
            lambda s, r: quarter[c, s, pl.ds(r, 32), :],
            lambda s, r: half[c, s, pl.ds(pl.multiple_of(a * 64 + r, 32), 32), :],
            4,
            64,
            32,
        )
        second_copy(c).start()

    def add_second(c):
        a, b, first_device, second_device = axes(c)
        second_copy(c).wait_recv()

        def put(s, r, value):
            eighth[c, s, pl.ds(r, 32), :] = value

        add_blocks(
            put,
            lambda s, r: eighth[c, s, pl.ds(r, 32), :],
            lambda s, r: quarter[c, s, pl.ds(pl.multiple_of(b * 32 + r, 32), 32), :],
            4,
            32,
            32,
        )
        for d in range(3):
            z_copy(c, d).start()

    def add_z(c):
        for d in range(3):
            z_copy(c, d).wait_recv()
        total = eighth[c, z].astype(jnp.float32)
        for d in range(3):
            total = total + pieces[c, d].astype(jnp.float32)
        final[c] = total.astype(jnp.bfloat16)
        back_second(c).start()
        place_copy(c).start()

    def pass_first(c):
        place_copy(c).wait()
        back_second(c).wait_recv()
        back_first(c).start()

    def pass_core(c):
        back_first(c).wait_recv()
        back_core(c).start()

    def finish(c):
        back_core(c).wait()
        back_first(c).wait_send()
        back_second(c).wait_send()
        for d in range(3):
            z_copy(c, d).wait_send()
        second_copy(c).wait_send()
        first_copy(c).wait_send()
        by_source(c, lambda source: core_copy(c, source).wait_send())

    def small_copy(k):
        source = small_ref if k == 0 else small_sum.at[k - 1]
        device = (other_core, other_x, other_y)[k]
        return remote(source, small_in.at[k], small_send_sem.at[k], small_recv_sem.at[k], device)

    def small_z_copy(d):
        return remote(
            small_sum.at[2],
            small_z.at[z],
            small_send_sem.at[3 + d],
            small_recv_sem.at[3 + d],
            others_z[d],
        )

    def small_step(k):
        small_copy(k).wait()
        before = small_ref[...] if k == 0 else small_sum[k - 1]
        small_sum[k] = before + small_in[k]
        if k < 2:
            small_copy(k + 1).start()
        else:
            small_z[z] = small_sum[2]
            for d in range(3):
                small_z_copy(d).start()

    def small_end():
        for d in range(3):
            small_z_copy(d).wait()
        small_out_ref[...] = (small_z[0] + small_z[1]) + (small_z[2] + small_z[3])

    stages = (start_core, add_core, add_first, add_second, add_z, pass_first, pass_core, finish)
    small_copy(0).start()

    def step(t, carry):
        for k, stage in enumerate(stages):
            c = t - k

            @pl.when((c >= 0) & (c < CHUNKS))
            def _(stage=stage, c=c):
                stage(c)

        for k in range(3):

            @pl.when(t == k + 1)
            def _(k=k):
                small_step(k)

        @pl.when(t == 4)
        def _():
            small_end()

        return carry

    lax.fori_loop(0, CHUNKS + len(stages) - 1, step, 0)


def reduce_all(att, expand, shrink, small):
    small_rows = small.shape[0]
    dma = pltpu.SemaphoreType.DMA
    return pl.pallas_call(
        reduce_kernel,
        out_shape=(
            jax.ShapeDtypeStruct((CHUNKS, 256, D), jnp.bfloat16),
            jax.ShapeDtypeStruct(small.shape, jnp.float32),
        ),
        in_specs=[pl.BlockSpec(memory_space=pl.ANY)] * 3
        + [pl.BlockSpec(memory_space=pltpu.VMEM)],
        out_specs=(
            pl.BlockSpec(memory_space=pl.ANY),
            pl.BlockSpec(memory_space=pltpu.VMEM),
        ),
        scratch_shapes=[
            pltpu.VMEM((CHUNKS, 4, 128, D), jnp.bfloat16),
            pltpu.VMEM((2, 4, 128, D), jnp.bfloat16),
            pltpu.VMEM((CHUNKS, 4, 64, D), jnp.bfloat16),
            pltpu.VMEM((CHUNKS, 4, 32, D), jnp.bfloat16),
            pltpu.VMEM((CHUNKS, 3, 32, D), jnp.bfloat16),
            pltpu.VMEM((CHUNKS, 32, D), jnp.bfloat16),
            pltpu.VMEM((3, small_rows, 128), jnp.float32),
            pltpu.VMEM((3, small_rows, 128), jnp.float32),
            pltpu.VMEM((4, small_rows, 128), jnp.float32),
            dma((6, CHUNKS)),
            dma((6, CHUNKS)),
            dma((CHUNKS, 3)),
            dma((CHUNKS, 3)),
            dma((2,)),
            dma((CHUNKS,)),
            dma((6,)),
            dma((6,)),
        ],
        compiler_params=pltpu.CompilerParams(
            collective_id=0, has_side_effects=True, vmem_limit_bytes=48 * MIB
        ),
    )(att, expand, shrink, small)


def line_sum(part, whole, send_sem, recv_sem, z, others_z):
    copies = [
        remote(part, whole.at[z], send_sem.at[d], recv_sem.at[d], others_z[d]) for d in range(3)
    ]
    for copy in copies:
        copy.start()
    whole[z] = part[...]
    for copy in copies:
        copy.wait()
    return (whole[0] + whole[1]) + (whole[2] + whole[3])


def fold(tile):
    return jnp.sum(tile.reshape(-1, 8, tile.shape[-1]), axis=0)


def spread_scalar(value):
    return jnp.broadcast_to(value, (1, 128))


def factor_kernel(
    grad_ref,
    att_rows_ref,
    exp_rows_ref,
    shr_rows_ref,
    cols_ref,
    att_rows_out,
    exp_rows_out,
    shr_rows_out,
    cols_out,
    scale_out,
    part,
    whole,
    send_sem,
    recv_sem,
):
    core, x, y, z, other_core, other_x, other_y, others_z = neighbours()
    greet(others_z)
    part[...] = jnp.zeros_like(part)

    def tile(chunk, r, step):
        return grad_ref[chunk, pl.ds(r, step), :].astype(jnp.float32)

    def add(slot, col, weighted):
        part[slot : slot + 1, :] += jnp.sum(col, axis=0, keepdims=True)
        part[16 + slot : 17 + slot, :] += jnp.sum(weighted, axis=0, keepdims=True)

    def scan_rows(chunks, slots, rows_in, rows_out, total_at):
        width = float(len(chunks) * D)
        step = 64 // len(chunks)

        def body(i, carry):
            cols, weights, total = carry
            r = pl.multiple_of(i * step, step)
            squares = [jnp.square(tile(c, r, step)) for c in chunks]
            row_sum = squares[0]
            for square in squares[1:]:
                row_sum = row_sum + square
            row_sum = jnp.sum(row_sum, axis=1, keepdims=True)
            rows = DECAY_RATE * rows_in[pl.ds(r, step), :] + (1.0 - DECAY_RATE) * (
                row_sum / width + FACTOR_EPS
            )
            rows_out[pl.ds(r, step), :] = rows
            inverse = 1.0 / rows
            cols = [c + fold(s) for c, s in zip(cols, squares)]
            weights = [w + fold(s * inverse) for w, s in zip(weights, squares)]
            return cols, weights, total + fold(rows)

        zeros = [jnp.zeros((8, D), jnp.float32) for _ in chunks]
        cols, weights, total = lax.fori_loop(
            0, 256 // step, body, (zeros, zeros, jnp.zeros((8, 1), jnp.float32))
        )
        for slot, col, weighted in zip(slots, cols, weights):
            add(slot, col, weighted)
        row, lane = total_at
        part[row : row + 1, lane : lane + 128] += spread_scalar(jnp.sum(total))

    for i in range(8):
        scan_rows([i], [i], att_rows_ref.at[i], att_rows_out.at[i], (13, 128 * i))
    scan_rows([8, 9, 10, 11], [8, 9, 10, 11], exp_rows_ref, exp_rows_out, (14, 0))
    for i in range(4):
        scan_rows([12 + i], [12], shr_rows_ref.at[i], shr_rows_out.at[i], (14, 128))
    total = line_sum(part, whole, send_sem, recv_sem, z, others_z)
    row_counts = [D] * 12 + [FF]
    means = [total[13:14, 128 * i : 128 * i + 1] / D for i in range(8)]
    means = means + [total[14:15, 0:1] / D] * 4 + [total[14:15, 128:129] / FF]
    cols_new, quotients = [], []
    for slot in range(13):
        new = DECAY_RATE * cols_ref[slot : slot + 1, :] + (1.0 - DECAY_RATE) * (
            total[slot : slot + 1] / row_counts[slot] + FACTOR_EPS
        )
        cols_new.append(new)
        quotients.append(jnp.sum(total[16 + slot : 17 + slot] / new, axis=1, keepdims=True))
        cols_out[slot : slot + 1, :] = new
    expand_quotient = quotients[8] + quotients[9] + quotients[10] + quotients[11]
    for slot in range(13):
        if slot < 8:
            mean_square = means[slot] * quotients[slot] / (D * D)
            rate = STEP_RATE * (OUT_GAIN if slot % 4 == 3 else 1.0)
        else:
            quotient = expand_quotient if slot < 12 else quotients[12]
            mean_square = means[slot] * quotient / (D * FF)
            rate = STEP_RATE
        factor = rate / jnp.maximum(1.0, jnp.sqrt(mean_square) / CLIP_LEVEL)
        scale_out[slot : slot + 1, :] = lax.rsqrt(cols_new[slot] / means[slot]) * factor


def factors(grads, att_rows, exp_rows, shr_rows, cols):
    vmem = pl.BlockSpec(memory_space=pltpu.VMEM)
    shape = jax.ShapeDtypeStruct
    return pl.pallas_call(
        factor_kernel,
        out_shape=(
            shape((8, 256, 1), jnp.float32),
            shape((256, 1), jnp.float32),
            shape((4, 256, 1), jnp.float32),
            shape((16, D), jnp.float32),
            shape((16, D), jnp.float32),
        ),
        in_specs=[vmem] * 5,
        out_specs=(vmem,) * 5,
        scratch_shapes=[
            pltpu.VMEM((32, D), jnp.float32),
            pltpu.VMEM((4, 32, D), jnp.float32),
            pltpu.SemaphoreType.DMA((3,)),
            pltpu.SemaphoreType.DMA((3,)),
        ],
        compiler_params=pltpu.CompilerParams(
            collective_id=1, has_side_effects=True, vmem_limit_bytes=40 * MIB
        ),
    )(grads, att_rows, exp_rows, shr_rows, cols)


def update_attention_kernel(
    grad_ref, weight_ref, rows_ref, scale_ref, grad_out, new_out, copy_out, grads, change
):
    block = grad_ref.shape[1]
    for i in range(8):
        grad = grad_ref[i].astype(jnp.float32)
        scaled = grad * lax.rsqrt(rows_ref[i]) * scale_ref[i : i + 1, :]
        every = pl.ds(i, block, stride=8)
        for lane in range(8):
            columns = slice(lane * 128, lane * 128 + 128)
            grads[lane, every, :] = grad[:, columns]
            change[lane, every, :] = scaled[:, columns]
    for lane in range(8):
        columns = slice(lane * 128, lane * 128 + 128)
        grad_out[:, columns] = grads[lane]
        new = weight_ref[:, columns] - change[lane]
        new_out[:, columns] = new
        copy_out[:, columns] = new.astype(jnp.bfloat16)


def update_attention(grads, weights, rows, scale):
    block = 32
    wide = pl.BlockSpec((block * 8, D), lambda i: (i, 0))
    shape = jax.ShapeDtypeStruct
    new = pl.pallas_call(
        update_attention_kernel,
        grid=(256 // block,),
        out_shape=(
            shape((2048, D), jnp.float32),
            shape((2048, D), jnp.float32),
            shape((2048, D), jnp.bfloat16),
        ),
        in_specs=[
            pl.BlockSpec((8, block, D), lambda i: (0, i, 0)),
            wide,
            pl.BlockSpec((8, block, 1), lambda i: (0, i, 0)),
            pl.BlockSpec((16, D), lambda i: (0, 0)),
        ],
        out_specs=(wide,) * 3,
        scratch_shapes=[pltpu.VMEM((8, block * 8, 128), jnp.float32)] * 2,
        compiler_params=pltpu.CompilerParams(vmem_limit_bytes=40 * MIB),
    )(grads, weights.reshape(2048, D), rows, scale)
    return [t.reshape(256, 8, D) for t in new]


def update_kernel(first, slots, grad_ref, weight_ref, rows_ref, scale_ref, grad_out, new_out, copy_out):
    for i in range(slots):
        grad = grad_ref[i].astype(jnp.float32)
        columns = slice(i * D, i * D + D)
        grad_out[:, columns] = grad
        new = weight_ref[:, columns] - grad * (
            lax.rsqrt(rows_ref[...]) * scale_ref[first + i : first + i + 1, :]
        )
        new_out[:, columns] = new
        copy_out[:, columns] = new.astype(jnp.bfloat16)


def update_plain(grads, weights, rows, scale, first, slots, grad_map):
    count, width = weights.shape
    block = 128 // slots
    wide = pl.BlockSpec((block, width), lambda i: (i, 0))
    shape = jax.ShapeDtypeStruct
    return pl.pallas_call(
        lambda *refs: update_kernel(first, slots, *refs),
        grid=(count // block,),
        out_shape=(
            shape(weights.shape, jnp.float32),
            shape(weights.shape, jnp.float32),
            shape(weights.shape, jnp.bfloat16),
        ),
        in_specs=[
            pl.BlockSpec((slots, block, D), grad_map),
            wide,
            pl.BlockSpec((block, 1), lambda i: (i, 0)),
            pl.BlockSpec((16, D), lambda i: (0, 0)),
        ],
        out_specs=(wide,) * 3,
        compiler_params=pltpu.CompilerParams(vmem_limit_bytes=40 * MIB),
    )(grads, weights, rows, scale)


def update_direct(
    grads,
    attention_weights,
    expand_weight,
    shrink_weight,
    attention_rows,
    attention_cols,
    expand_rows,
    expand_cols,
    shrink_rows,
    shrink_cols,
):
    cols = jnp.concatenate(
        [attention_cols, expand_cols.reshape(4, D), shrink_cols.reshape(1, D), jnp.ones((3, D))]
    )
    att_rows, exp_rows, shr_rows, cols_new, scale = factors(
        grads,
        attention_rows[:, :, None],
        expand_rows[:, None],
        shrink_rows.reshape(4, 256, 1),
        cols,
    )
    shr_rows = shr_rows.reshape(-1, 1)
    attention = update_attention(grads, attention_weights, att_rows, scale)
    expand = update_plain(grads, expand_weight, exp_rows, scale, 8, 4, lambda i: (2, i, 0))
    shrink = update_plain(
        grads, shrink_weight, shr_rows, scale, 12, 1, lambda i: (12 + i // 2, i % 2, 0)
    )
    return (
        attention,
        expand,
        shrink,
        (att_rows[:, :, 0], exp_rows[:, 0], shr_rows[:, 0]),
        (cols_new[0:8], cols_new[8:12].reshape(-1), cols_new[12]),
    )


def as_rows(vector):
    rows = -(-vector.shape[0] // 1024) * 8
    return jnp.pad(vector, (0, rows * 128 - vector.shape[0])).reshape(rows, 128)


def gather_rows(piece):
    return lax.all_gather(piece, ("shard", "rep"), axis=0, tiled=True)


def own_piece(block, replicas):
    rows = block.shape[0] // replicas
    return lax.dynamic_slice_in_dim(block, lax.axis_index("rep") * rows, rows, axis=0)


def scatter_rows(grad):
    piece = lax.psum_scatter(
        grad.astype(jnp.bfloat16), ("shard", "rep"), scatter_dimension=0, tiled=True
    )
    return lax.all_gather(piece, "rep", axis=0, tiled=True)


def local_factors(grad, rows):
    square = grad * grad
    rows_new = DECAY_RATE * rows + (1.0 - DECAY_RATE) * jnp.mean(square + FACTOR_EPS, axis=-1)
    col_part = jnp.sum(square + FACTOR_EPS, axis=0)
    weighted = jnp.sum(square / rows_new[..., None], axis=0)
    return rows_new, col_part, weighted, jnp.sum(rows_new, axis=0)


def finish_factors(grad, weight, rows_new, cols, col_sum, weighted, row_total, row_count, rate):
    cols_new = DECAY_RATE * cols + (1.0 - DECAY_RATE) * col_sum / row_count
    mean_rows = row_total / row_count
    mean_square = mean_rows * jnp.sum(weighted / cols_new, axis=-1) / (row_count * cols.shape[-1])
    factor = rate / jnp.maximum(1.0, jnp.sqrt(mean_square) / CLIP_LEVEL)
    scaled = lax.rsqrt(cols_new / mean_rows[..., None]) * factor[..., None]
    fresh = weight - grad * (lax.rsqrt(rows_new)[..., None] * scaled[None])
    return fresh, cols_new


def on_device(
    tokens,
    encoder,
    cotangent,
    lengths,
    encoder_lengths,
    dealt_order,
    attention_weights,
    expand_weight,
    shrink_weight,
    small_params,
    attention_rows,
    attention_cols,
    expand_rows,
    expand_cols,
    shrink_rows,
    shrink_cols,
    small_moment,
):
    devices = lax.axis_size(("rep", "shard"))
    replicas = lax.axis_size("rep")
    shards = lax.axis_size("shard")
    slot_tokens = tokens.shape[0]
    slot_states = encoder.shape[0]
    position = lax.axis_index(("rep", "shard"))
    inverse = (
        jnp.zeros((devices,), jnp.int32).at[dealt_order].set(jnp.arange(devices, dtype=jnp.int32))
    )
    direct = replicas == 8 and shards == 4
    if direct:
        pieces = weight_pieces(attention_weights, neighbours())
        tokens, qkv_full = front(inverse, tokens, pieces[0:3])
        matrices = [qkv_full[i] for i in range(3)]
    else:
        attention_piece = own_piece(attention_weights.reshape(-1, 8 * D), replicas)
        attention_full = gather_rows(attention_piece.astype(jnp.bfloat16))
        matrices = [attention_full[:, i * D : (i + 1) * D] for i in range(8)]
        spread = lax.all_to_all(
            tokens.reshape(devices, slot_tokens // devices, D),
            ("rep", "shard"),
            split_axis=0,
            concat_axis=0,
            tiled=True,
        )
        picked = jnp.take(spread, inverse, axis=0)
        tokens = lax.all_to_all(
            picked, ("rep", "shard"), split_axis=0, concat_axis=0, tiled=True
        ).reshape(slot_tokens, D)
    expand_full = gather_rows(own_piece(expand_weight, replicas).astype(jnp.bfloat16))
    shrink_full = gather_rows(own_piece(shrink_weight, replicas).astype(jnp.bfloat16))
    states = encoder
    incoming = cotangent
    valid_tokens = lengths[position]
    valid_states = encoder_lengths[position]
    parts = unpack(small_params)
    q_self = ((forward_product(tokens, matrices[0]) + parts[0]) * 0.125).astype(
        jnp.bfloat16
    )
    k_self = forward_product(tokens, matrices[1]).astype(jnp.bfloat16)
    v_self = (forward_product(tokens, matrices[2]) + parts[1]).astype(jnp.bfloat16)
    if direct:
        o_self_low, lse_self, rest_full = attend_gather(
            q_self, k_self, v_self, valid_tokens, pieces[3:8]
        )
        matrices = matrices + [rest_full[i] for i in range(5)]
    else:
        o_self_low, lse_self = attend(q_self, k_self, v_self, valid_tokens, True)
    branch_a = forward_product(o_self_low, matrices[3]) + parts[2]
    tokens_wide = tokens.astype(jnp.float32)
    hidden_one, norm_one_back = jax.vjp(layer_norm, tokens_wide + branch_a, parts[8], parts[9])
    hidden_one_low = hidden_one.astype(jnp.bfloat16)
    q_cross = (
        (forward_product(hidden_one_low, matrices[4]) + parts[3]) * 0.125
    ).astype(jnp.bfloat16)
    k_cross = forward_product(states, matrices[5]).astype(jnp.bfloat16)
    v_cross = (forward_product(states, matrices[6]) + parts[4]).astype(jnp.bfloat16)
    o_cross_low, lse_cross = attend(q_cross, k_cross, v_cross, valid_states, False)
    branch_c = forward_product(o_cross_low, matrices[7]) + parts[5]
    hidden_two, norm_two_back = jax.vjp(layer_norm, hidden_one + branch_c, parts[10], parts[11])
    hidden_two_low = hidden_two.astype(jnp.bfloat16)
    pre_act = forward_product(hidden_two_low, expand_full) + parts[6]
    activated, gelu_back = jax.vjp(gelu_exact, pre_act)
    activated_low = activated.astype(jnp.bfloat16)
    branch_m = forward_product(activated_low, shrink_full) + parts[7]
    result, norm_three_back = jax.vjp(layer_norm, hidden_two + branch_m, parts[12], parts[13])
    usable_rows = (jnp.arange(slot_tokens, dtype=jnp.int32) < valid_tokens).astype(jnp.float32)[
        :, None
    ]
    squares = jnp.stack(
        [
            jnp.sum(usable_rows * t * t)
            for t in (tokens_wide, branch_a, hidden_one, branch_c, hidden_two, branch_m)
        ]
    )
    d_third, d_gain_three, d_shift_three = norm_three_back(
        incoming.astype(jnp.float32) * usable_rows
    )
    d_mlp = d_third.astype(jnp.bfloat16)
    grad_shrink = weight_product(activated_low, d_mlp)
    grad_shrink_offset = row_sum(d_mlp)
    d_activated = input_product(d_mlp, shrink_full)
    d_pre = gelu_back(d_activated)[0].astype(jnp.bfloat16)
    grad_expand = weight_product(hidden_two_low, d_pre)
    grad_expand_offset = row_sum(d_pre)
    d_hidden_two = d_third + input_product(d_pre, expand_full)
    d_second, d_gain_two, d_shift_two = norm_two_back(d_hidden_two)
    d_branch_c = d_second.astype(jnp.bfloat16)
    grad_cross_out = weight_product(o_cross_low, d_branch_c)
    grad_cross_out_offset = row_sum(d_branch_c)
    d_o_cross = input_product(d_branch_c, matrices[7]).astype(jnp.bfloat16)
    dq_cross, dk_cross, dv_cross, cross_sums = attend_back(
        q_cross, k_cross, v_cross, d_o_cross, lse_cross, valid_states, False
    )
    grad_cross_query = weight_product(hidden_one_low, dq_cross)
    grad_cross_key = weight_product(states, dk_cross)
    grad_cross_value = weight_product(states, dv_cross)
    state_grad = input_product(dk_cross, matrices[5]) + input_product(
        dv_cross, matrices[6]
    )
    d_hidden_one = d_second + input_product(dq_cross, matrices[4])
    d_first, d_gain_one, d_shift_one = norm_one_back(d_hidden_one)
    d_branch_a = d_first.astype(jnp.bfloat16)
    grad_self_out = weight_product(o_self_low, d_branch_a)
    grad_self_out_offset = row_sum(d_branch_a)
    d_o_self = input_product(d_branch_a, matrices[3]).astype(jnp.bfloat16)
    dq_self, dk_self, dv_self, self_sums = attend_back(
        q_self, k_self, v_self, d_o_self, lse_self, valid_tokens, True
    )
    grad_self_query = weight_product(tokens, dq_self)
    grad_self_key = weight_product(tokens, dk_self)
    grad_self_value = weight_product(tokens, dv_self)
    token_grad = (
        d_first
        + input_product(dq_self, matrices[0])
        + input_product(dk_self, matrices[1])
        + input_product(dv_self, matrices[2])
    )
    small_partial = jnp.concatenate(
        [
            self_sums[:, 0, :].reshape(-1),
            self_sums[:, 1, :].reshape(-1),
            grad_self_out_offset,
            cross_sums[:, 0, :].reshape(-1),
            cross_sums[:, 1, :].reshape(-1),
            grad_cross_out_offset,
            grad_expand_offset,
            grad_shrink_offset,
            d_gain_one,
            d_shift_one,
            d_gain_two,
            d_shift_two,
            d_gain_three,
            d_shift_three,
        ]
    )
    attention_grads = [
        grad_self_query,
        grad_self_key,
        grad_self_value,
        grad_self_out,
        grad_cross_query,
        grad_cross_key,
        grad_cross_value,
        grad_cross_out,
    ]
    small_all = jnp.concatenate([small_partial, squares])
    if direct:
        reduced, totals = reduce_all(
            jnp.stack([t.astype(jnp.bfloat16) for t in attention_grads]).reshape(8, 4, 256, D),
            grad_expand.astype(jnp.bfloat16).reshape(4, 256, FF),
            grad_shrink.astype(jnp.bfloat16).reshape(4, 4, 256, D),
            as_rows(small_all),
        )
        totals = totals.reshape(-1)[: small_all.shape[0]]
        (
            (g_attention, attention_new, attention_copy),
            (g_expand, expand_new, expand_copy),
            (g_shrink, shrink_new, shrink_copy),
            (attention_rows_new, expand_rows_new, shrink_rows_new),
            (attention_cols_new, expand_cols_new, shrink_cols_new),
        ) = update_direct(
            reduced,
            attention_weights,
            expand_weight,
            shrink_weight,
            attention_rows,
            attention_cols,
            expand_rows,
            expand_cols,
            shrink_rows,
            shrink_cols,
        )
    else:
        totals = lax.psum(small_all, ("rep", "shard"))
        g_shrink = scatter_rows(grad_shrink).astype(jnp.float32)
        g_expand = scatter_rows(grad_expand).astype(jnp.float32)
        g_attention = (
            scatter_rows(jnp.concatenate(attention_grads, axis=1))
            .reshape(-1, 8, D)
            .astype(jnp.float32)
        )
        attention_rows_new, *attention_parts = local_factors(g_attention, attention_rows.T)
        expand_rows_new, *expand_parts = local_factors(g_expand, expand_rows)
        shrink_rows_new, *shrink_parts = local_factors(g_shrink, shrink_rows)
        flat = attention_parts + expand_parts + shrink_parts
        flat_parts = jnp.concatenate([t.reshape(-1) for t in flat])
        summed = lax.psum(flat_parts, "shard")
        sums = []
        offset = 0
        for t in flat:
            sums.append(summed[offset : offset + t.size].reshape(t.shape))
            offset = offset + t.size
        attention_rates = STEP_RATE * jnp.where(jnp.arange(8) % 4 == 3, OUT_GAIN, 1.0).astype(
            jnp.float32
        )
        attention_new, attention_cols_new = finish_factors(
            g_attention,
            attention_weights,
            attention_rows_new,
            attention_cols,
            *sums[0:3],
            D,
            attention_rates,
        )
        expand_new, expand_cols_new = finish_factors(
            g_expand, expand_weight, expand_rows_new, expand_cols, *sums[3:6], D, STEP_RATE
        )
        shrink_new, shrink_cols_new = finish_factors(
            g_shrink, shrink_weight, shrink_rows_new, shrink_cols, *sums[6:9], FF, STEP_RATE
        )
        attention_rows_new = attention_rows_new.T
        attention_copy = attention_new.astype(jnp.bfloat16)
        expand_copy = expand_new.astype(jnp.bfloat16)
        shrink_copy = shrink_new.astype(jnp.bfloat16)
    small_grad = totals[: small_params.shape[0]]
    small_moment_new = DECAY_RATE * small_moment + (1.0 - DECAY_RATE) * (
        small_grad * small_grad + FACTOR_EPS
    )
    small_update = small_grad * lax.rsqrt(small_moment_new)
    small_scale = jnp.sqrt(jnp.mean(small_update * small_update))
    small_new = small_params - SMALL_RATE * small_update / jnp.maximum(
        1.0, small_scale / CLIP_LEVEL
    )
    norm_stats = jnp.sqrt(
        totals[small_params.shape[0] :] / (jnp.sum(lengths).astype(jnp.float32) * D)
    )
    return (
        result.astype(jnp.bfloat16),
        token_grad.astype(jnp.bfloat16),
        state_grad.astype(jnp.bfloat16),
        g_attention,
        g_expand,
        g_shrink,
        small_grad,
        attention_new,
        expand_new,
        shrink_new,
        small_new,
        attention_copy,
        expand_copy,
        shrink_copy,
        attention_rows_new,
        attention_cols_new,
        expand_rows_new,
        expand_cols_new,
        shrink_rows_new,
        shrink_cols_new,
        small_moment_new,
        norm_stats,
    )


def solution(mesh):
    in_specs = (
        P(("rep", "shard"), None),
        P(("rep", "shard"), None),
        P(("rep", "shard"), None),
        P(),
        P(),
        P(),
        P("shard", None, None),
        P("shard", None),
        P("shard", None),
        P(),
        P(None, "shard"),
        P(),
        P("shard"),
        P(),
        P("shard"),
        P(),
        P(),
    )
    out_specs = (
        P(("rep", "shard"), None),
        P(("rep", "shard"), None),
        P(("rep", "shard"), None),
        P("shard", None, None),
        P("shard", None),
        P("shard", None),
        P(),
        P("shard", None, None),
        P("shard", None),
        P("shard", None),
        P(),
        P("shard", None, None),
        P("shard", None),
        P("shard", None),
        P(None, "shard"),
        P(),
        P("shard"),
        P(),
        P("shard"),
        P(),
        P(),
        P(),
    )
    return jax.shard_map(
        on_device, mesh=mesh, in_specs=in_specs, out_specs=out_specs, check_vma=False
    )
```

```python
import jax
import jax.numpy as jnp
from jax import lax
from jax.experimental import pallas as pl
from jax.experimental.pallas import tpu as pltpu
from jax.sharding import PartitionSpec as P

D = 1024
FF = 4096


DECAY_RATE = 0.5
CLIP_LEVEL = 0.25
STEP_RATE = 0.1
SMALL_RATE = 0.4
OUT_GAIN = 8.0
NORM_EPS = 1e-05
FACTOR_EPS = 1e-30
MASKED = -1e30
MESH = pl.DeviceIdType.MESH
CHUNKS = 16
MIB = 1 << 20


def layer_norm(r, norm_gain, norm_shift):
    centred = r - jnp.mean(r, axis=-1, keepdims=True)
    spread = jnp.mean(centred * centred, axis=-1, keepdims=True)
    return centred * lax.rsqrt(spread + NORM_EPS) * norm_gain + norm_shift


def gelu_exact(values):
    return jax.nn.gelu(values, approximate=False)


def unpack(small):
    extents = [D] * 6 + [FF] + [D] * 7
    pieces = []
    offset = 0
    for extent in extents:
        pieces.append(small[offset : offset + extent])
        offset = offset + extent
    return pieces


def forward_product(source, matrix):
    return jnp.dot(source, matrix, preferred_element_type=jnp.float32)


def input_product(grad_low, matrix):
    return jnp.einsum("to,io->ti", grad_low, matrix, preferred_element_type=jnp.float32)


def weight_product(source, grad_low):
    return jnp.einsum("ti,to->io", source, grad_low, preferred_element_type=jnp.float32)


def row_sum(grad_low):
    return jnp.sum(grad_low.astype(jnp.float32), axis=0)


def transposed(block):
    return block.astype(jnp.float32).T.astype(jnp.bfloat16)


def half_lanes(shape, dim):
    return lax.broadcasted_iota(jnp.int32, shape, dim)


def masked_keys(keys, length, head):
    place = half_lanes(keys.shape, 0)
    lane = half_lanes(keys.shape, 1)
    blocked = jnp.where((lane == 64 - 64 * head) & (place >= length), MASKED, 0.0)
    own = (lane >= 64 * head) & (lane < 64 * head + 64)
    return jnp.where(own, keys.astype(jnp.float32), blocked).astype(jnp.bfloat16)


def own_head(rows_t, head, fill):
    place = half_lanes(rows_t.shape, 0)
    own = (place >= 64 * head) & (place < 64 * head + 64)
    other = jnp.where(place == 64 - 64 * head, fill, 0.0)
    return jnp.where(own, rows_t.astype(jnp.float32), other).astype(jnp.bfloat16)


def product(first, second):
    return jnp.dot(first, second, preferred_element_type=jnp.float32)


def causal_mask(scores, step):
    kept = scores.shape[0] - step
    last = scores[kept:]
    allowed = half_lanes(last.shape, 0) <= half_lanes(last.shape, 1)
    last = jnp.where(allowed, last, MASKED)
    return last if kept == 0 else jnp.concatenate([scores[:kept], last], axis=0)


def attend_kernel(causal, step, length_ref, q_ref, k_ref, v_ref, o_ref, lse_ref, o_t):
    length = length_ref[0]
    q_t = transposed(q_ref[...])
    v_t = transposed(v_ref[...])
    for head in range(2):
        keys = masked_keys(k_ref[...], length, head)
        queries = own_head(q_t, head, 1.0)
        rows = slice(64 * head, 64 * head + 64)
        for start in range(0, q_ref.shape[0], step):
            columns = slice(start, start + step)
            end = start + step if causal else k_ref.shape[0]
            scores = product(keys[:end], queries[:, columns])
            if causal:
                scores = causal_mask(scores, step)
            top = jnp.max(scores, axis=0, keepdims=True)
            raised = jnp.exp(scores - top)
            total = jnp.sum(raised, axis=0, keepdims=True)
            probs = (raised * (1.0 / total)).astype(jnp.bfloat16)
            o_t[rows, columns] = product(v_t[rows, :end], probs)
            lse_ref[0, head : head + 1, columns] = top + jnp.log(total)
    o_ref[...] = o_t[...].T.astype(jnp.bfloat16)


def attend_back_kernel(
    causal,
    step,
    length_ref,
    q_ref,
    k_ref,
    v_ref,
    do_ref,
    lse_ref,
    dq_ref,
    dk_ref,
    dv_ref,
    sums_ref,
    dq_t,
    dk_sum,
    dv_sum,
):
    length = length_ref[0]
    q_t = transposed(q_ref[...])
    k_t = transposed(k_ref[...])
    do_t = transposed(do_ref[...])
    values = v_ref[...]
    for head in range(2):
        keys = masked_keys(k_ref[...], length, head)
        queries = own_head(q_t, head, 1.0)
        grads = own_head(do_t, head, 0.0)
        rows = slice(64 * head, 64 * head + 64)
        count = q_ref.shape[0] // step
        for b in reversed(range(count)):
            start = b * step
            columns = slice(start, start + step)
            end = start + step if causal else k_ref.shape[0]
            scores = product(keys[:end], queries[:, columns])
            if causal:
                scores = causal_mask(scores, step)
            probs = jnp.exp(scores - lse_ref[0, head : head + 1, columns])
            weighted = probs * product(values[:end], grads[:, columns])
            delta = jnp.sum(weighted, axis=0, keepdims=True)
            d_scores = (weighted - probs * delta).astype(jnp.bfloat16)
            dv = product(probs.astype(jnp.bfloat16), do_ref[columns, :])
            dk = product(d_scores, q_ref[columns, :])
            if b == count - 1:
                dv_sum[head] = dv
                dk_sum[head] = dk
            else:
                dv_sum[head, :end] += dv
                dk_sum[head, :end] += dk
            dq_t[rows, columns] = product(k_t[rows, :end], d_scores)
    first = half_lanes(dk_ref.shape, 1) < 64
    dk_ref[...] = jnp.where(first, dk_sum[0], dk_sum[1]).astype(jnp.bfloat16)
    dv = jnp.where(first, dv_sum[0], dv_sum[1]).astype(jnp.bfloat16)
    dv_ref[...] = dv
    dq = (dq_t[...] * 0.125).T.astype(jnp.bfloat16)
    dq_ref[...] = dq
    sums_ref[0, 0:1, :] = jnp.sum(dq.astype(jnp.float32), axis=0, keepdims=True)
    sums_ref[0, 1:2, :] = jnp.sum(dv.astype(jnp.float32), axis=0, keepdims=True)


def pair_block(rows):
    return pl.BlockSpec((rows, 128), lambda i: (0, i))


def pair_rows(columns):
    return pl.BlockSpec((1, 8, columns), lambda i: (i, 0, 0))


SCALARS = pl.BlockSpec(memory_space=pltpu.SMEM)


def attend(queries, keys, values, length, causal):
    rows, key_rows = queries.shape[0], keys.shape[0]
    pairs = queries.shape[1] // 128
    return pl.pallas_call(
        lambda *refs: attend_kernel(causal, 256 if causal else 512, *refs),
        grid=(pairs,),
        out_shape=(
            jax.ShapeDtypeStruct(queries.shape, jnp.bfloat16),
            jax.ShapeDtypeStruct((pairs, 8, rows), jnp.float32),
        ),
        in_specs=[SCALARS, pair_block(rows), pair_block(key_rows), pair_block(key_rows)],
        out_specs=(pair_block(rows), pair_rows(rows)),
        scratch_shapes=[pltpu.VMEM((128, rows), jnp.float32)],
        compiler_params=pltpu.CompilerParams(vmem_limit_bytes=40 * MIB),
    )(length.reshape(1), queries, keys, values)


def attend_back(queries, keys, values, grads, lse, length, causal):
    rows, key_rows = queries.shape[0], keys.shape[0]
    pairs = queries.shape[1] // 128
    return pl.pallas_call(
        lambda *refs: attend_back_kernel(causal, 256 if causal else 512, *refs),
        grid=(pairs,),
        out_shape=(
            jax.ShapeDtypeStruct(queries.shape, jnp.bfloat16),
            jax.ShapeDtypeStruct(keys.shape, jnp.bfloat16),
            jax.ShapeDtypeStruct(keys.shape, jnp.bfloat16),
            jax.ShapeDtypeStruct((pairs, 8, 128), jnp.float32),
        ),
        in_specs=[
            SCALARS,
            pair_block(rows),
            pair_block(key_rows),
            pair_block(key_rows),
            pair_block(rows),
            pair_rows(rows),
        ],
        out_specs=(pair_block(rows), pair_block(key_rows), pair_block(key_rows), pair_rows(128)),
        scratch_shapes=[
            pltpu.VMEM((128, rows), jnp.float32),
            pltpu.VMEM((2, key_rows, 128), jnp.float32),
            pltpu.VMEM((2, key_rows, 128), jnp.float32),
        ],
        compiler_params=pltpu.CompilerParams(vmem_limit_bytes=40 * MIB),
    )(length.reshape(1), queries, keys, values, grads, lse)


def neighbours():
    rep = lax.axis_index("rep")
    z = lax.axis_index("shard")
    core = rep % 2
    x = (rep // 2) % 2
    y = rep // 4
    other_core = (rep + 1 - 2 * core, z)
    other_x = (rep + 2 - 4 * x, z)
    other_y = (rep + 4 - 8 * y, z)
    others_z = [(rep, (z + d) % 4) for d in (1, 2, 3)]
    return core, x, y, z, other_core, other_x, other_y, others_z


def greet(devices):
    barrier = pltpu.get_barrier_semaphore()
    for device in devices:
        pl.semaphore_signal(barrier, inc=1, device_id=device, device_id_type=MESH)
    pl.semaphore_wait(barrier, len(devices))


def remote(src, dst, send, recv, device):
    return pltpu.make_async_remote_copy(
        src_ref=src, dst_ref=dst, send_sem=send, recv_sem=recv, device_id=device, device_id_type=MESH
    )


def gather_copies(refs, c, parity, places):
    piece, full, place_sem, z_send, z_recv, send, recv = refs
    core, x, y, z, other_core, other_x, other_y, others_z = places
    a = x + parity * (y - x)
    b = y + parity * (x - y)
    first = (other_x[0] + parity * (other_y[0] - other_x[0]), z)
    second = (other_y[0] + parity * (other_x[0] - other_y[0]), z)
    own = pl.ds(pl.multiple_of(core * 128 + a * 64 + b * 32, 32), 32)
    steps = (
        (own, second),
        (pl.ds(pl.multiple_of(core * 128 + a * 64, 64), 64), first),
        (pl.ds(pl.multiple_of(core * 128, 128), 128), other_core),
    )

    def local():
        return pltpu.make_async_copy(piece.at[c], full.at[c, z, own, :], place_sem.at[c])

    def line(d):
        return remote(
            piece.at[c], full.at[c, z, own, :], z_send.at[c, d], z_recv.at[c, d], others_z[d]
        )

    def pair(k):
        block = full.at[c, :, steps[k][0], :]
        return remote(block, block, send.at[k, c], recv.at[k, c], steps[k][1])

    return local, line, pair


def gather_stage(k, refs, c, parity, places):
    local, line, pair = gather_copies(refs, c, parity, places)
    if k == 0:
        local().start()
        for d in range(3):
            line(d).start()
    if k == 1:
        local().wait()
        for d in range(3):
            line(d).wait_recv()
        pair(0).start()
    if k == 2 or k == 3:
        pair(k - 2).wait_recv()
        pair(k - 1).start()
    if k == 4:
        pair(2).wait()
        pair(1).wait_send()
        pair(0).wait_send()
        for d in range(3):
            line(d).wait_send()


def gather_sems(count):
    dma = pltpu.SemaphoreType.DMA
    return [dma((count,)), dma((count, 3)), dma((count, 3)), dma((3, count)), dma((3, count))]


def own_rows(blocks, parity, places):
    core, x, y = places[0:3]
    a = x + parity * (y - x)
    b = y + parity * (x - y)
    rows = lax.dynamic_slice_in_dim(blocks, core * 128 + a * 64 + b * 32, 32, axis=-2)
    return rows.astype(jnp.bfloat16)


def hidden_blocks(values):
    split = values.reshape(values.shape[:-1] + (4, 4, 256))
    split = jnp.swapaxes(split, -3, -2)
    return split.reshape(values.shape[:-1] + (4, 1024))


def hidden_flat(blocks):
    split = blocks.reshape(blocks.shape[:-2] + (4, 4, 256))
    split = jnp.swapaxes(split, -3, -2)
    return split.reshape(blocks.shape[:-2] + (FF,))


def weight_pieces(attention, expand, shrink, places):
    attention = jnp.swapaxes(
        jnp.stack([own_rows(jnp.swapaxes(attention, 0, 1), p, places) for p in range(2)]), 0, 1
    )
    picked = [attention[i, i % 2] for i in range(3)]
    picked = picked + [attention[3 + c, c % 2] for c in range(5)]
    ff = []
    for p in range(2):
        rows = own_rows(expand, p, places)
        ff.append(jnp.swapaxes(hidden_blocks(rows), 0, 1))
    for p in range(2):
        ff.append(own_rows(shrink.reshape(4, 256, D), p, places))
    for j in range(4):
        picked.append(ff[1][j])
        picked.append(ff[2][j])
    return jnp.stack(picked[0:3]), jnp.stack(picked[3:16])


def front_kernel(
    order_ref,
    tokens_ref,
    piece_ref,
    x_ref,
    full_ref,
    spread,
    picked,
    spread_send,
    spread_recv,
    back_send,
    back_recv,
    *gather_sem,
):
    places = neighbours()
    z = places[3]
    me = lax.axis_index("rep") * 4 + z
    refs = (piece_ref, full_ref) + gather_sem

    def device(offset):
        j = lax.rem(me + offset, 32)
        return j, (j // 4, j % 4)

    barrier = pltpu.get_barrier_semaphore()

    def greet_one(offset, carry):
        pl.semaphore_signal(barrier, inc=1, device_id=device(offset)[1], device_id_type=MESH)
        return carry

    lax.fori_loop(1, 32, greet_one, 0)
    pl.semaphore_wait(barrier, 31)

    def stage(k):
        for c in range(3):
            gather_stage(k, refs, c, c % 2, places)

    def spread_copy(offset):
        j, target = device(offset)
        return remote(
            tokens_ref.at[j],
            spread.at[me],
            spread_send.at[offset],
            spread_recv.at[offset],
            target,
        )

    def back_copy(offset):
        target = device(offset)[1]
        return remote(
            picked.at[offset], x_ref.at[me], back_send.at[offset], back_recv.at[offset], target
        )

    own_in = pltpu.make_async_copy(tokens_ref.at[me], spread.at[me], spread_recv.at[0])
    own_out = pltpu.make_async_copy(picked.at[0], x_ref.at[me], back_recv.at[0])
    stage(0)
    own_in.start()

    def start_spread(offset, carry):
        spread_copy(offset).start()
        return carry

    lax.fori_loop(1, 32, start_spread, 0)
    stage(1)
    stage(2)
    own_in.wait()

    def wait_spread(offset, carry):
        spread_copy(offset).wait()
        return carry

    lax.fori_loop(1, 32, wait_spread, 0)
    picked[0] = spread[order_ref[me]]
    own_out.start()

    def pick(offset, carry):
        picked[offset] = spread[order_ref[device(offset)[0]]]
        back_copy(offset).start()
        return carry

    lax.fori_loop(1, 32, pick, 0)
    stage(3)
    stage(4)
    own_out.wait()

    def wait_back(offset, carry):
        back_copy(offset).wait()
        return carry

    lax.fori_loop(1, 32, wait_back, 0)


def front(inverse, tokens, pieces):
    dma = pltpu.SemaphoreType.DMA
    any_space = pl.BlockSpec(memory_space=pl.ANY)
    x, full = pl.pallas_call(
        front_kernel,
        out_shape=(
            jax.ShapeDtypeStruct((32, 32, D), jnp.bfloat16),
            jax.ShapeDtypeStruct((3, 4, 256, D), jnp.bfloat16),
        ),
        in_specs=[
            pl.BlockSpec(memory_space=pltpu.SMEM),
            any_space,
            pl.BlockSpec(memory_space=pltpu.VMEM),
        ],
        out_specs=(any_space, any_space),
        scratch_shapes=[
            pltpu.VMEM((32, 32, D), jnp.bfloat16),
            pltpu.VMEM((32, 32, D), jnp.bfloat16),
            dma((32,)),
            dma((32,)),
            dma((32,)),
            dma((32,)),
        ]
        + gather_sems(3),
        compiler_params=pltpu.CompilerParams(
            collective_id=2, has_side_effects=True, vmem_limit_bytes=24 * MIB
        ),
    )(inverse, tokens.reshape(32, 32, D), pieces)
    return x.reshape(1024, D), full.reshape(3, 1024, D)


GATHERED = 13


def attend_gather_kernel(
    length_ref, q_ref, k_ref, v_ref, piece_ref, o_ref, lse_ref, full_ref, o_t, *gather_sem
):
    places = neighbours()
    t = pl.program_id(0)
    refs = (piece_ref, full_ref) + gather_sem

    @pl.when(t == 0)
    def _():
        greet(list(places[4:7]) + places[7])

    for k in range(5):
        for j in range(2):
            c = 2 * (t - k) + j

            @pl.when((t >= k) & (c < GATHERED))
            def _(k=k, j=j, c=c):
                gather_stage(k, refs, c, j, places)

    @pl.when(t < 8)
    def _():
        attend_kernel(True, 256, length_ref, q_ref, k_ref, v_ref, o_ref, lse_ref, o_t)


def attend_gather(queries, keys, values, length, pieces):
    rows = queries.shape[0]
    pairs = queries.shape[1] // 128
    any_space = pl.BlockSpec(memory_space=pl.ANY)
    pair = pl.BlockSpec((rows, 128), lambda i: (0, jnp.minimum(i, pairs - 1)))
    out, lse, full = pl.pallas_call(
        attend_gather_kernel,
        grid=((GATHERED + 1) // 2 + 4,),
        out_shape=(
            jax.ShapeDtypeStruct(queries.shape, jnp.bfloat16),
            jax.ShapeDtypeStruct((pairs, 8, rows), jnp.float32),
            jax.ShapeDtypeStruct((GATHERED, 4, 256, D), jnp.bfloat16),
        ),
        in_specs=[SCALARS, pair, pair, pair, any_space],
        out_specs=(
            pair,
            pl.BlockSpec((1, 8, rows), lambda i: (jnp.minimum(i, pairs - 1), 0, 0)),
            any_space,
        ),
        scratch_shapes=[pltpu.VMEM((128, rows), jnp.float32)] + gather_sems(GATHERED),
        compiler_params=pltpu.CompilerParams(
            collective_id=3, has_side_effects=True, vmem_limit_bytes=40 * MIB
        ),
    )(length.reshape(1), queries, keys, values, pieces)
    return out, lse, full.reshape(GATHERED, 1024, D)


def add_blocks(target, first, second, planes, rows, step):
    per_plane = rows // step

    def body(i, carry):
        s = i // per_plane
        r = pl.multiple_of((i % per_plane) * step, step)
        total = first(s, r).astype(jnp.float32) + second(s, r).astype(jnp.float32)
        target(s, r, total.astype(jnp.bfloat16))
        return carry

    lax.fori_loop(0, planes * per_plane, body, 0)


def reduce_kernel(
    att_ref,
    exp_ref,
    shr_ref,
    small_ref,
    out_ref,
    small_out_ref,
    half,
    own,
    quarter,
    eighth,
    pieces,
    final,
    small_in,
    small_sum,
    small_z,
    send_sem,
    recv_sem,
    z_send_sem,
    z_recv_sem,
    own_sem,
    place_sem,
    small_send_sem,
    small_recv_sem,
):
    core, x, y, z, other_core, other_x, other_y, others_z = neighbours()
    greet([other_core, other_x, other_y] + others_z)

    def axes(c):
        odd = c % 2
        a = x + odd * (y - x)
        b = y + odd * (x - y)
        dx = other_x[0]
        dy = other_y[0]
        return a, b, (dx + odd * (dy - dx), z), (dy + odd * (dx - dy), z)

    def by_source(c, act):
        @pl.when(c < 8)
        def _():
            act(lambda part: att_ref.at[c, :, pl.ds(part, 128), :])

        @pl.when((c >= 8) & (c < 12))
        def _():
            act(lambda part: exp_ref.at[c - 8, :, pl.ds(part, 128), :])

        @pl.when(c >= 12)
        def _():
            act(lambda part: shr_ref.at[c - 12, :, pl.ds(part, 128), :])

    kept = pl.multiple_of(core * 128, 128)
    given = pl.multiple_of(128 - core * 128, 128)

    def core_copy(c, source):
        return remote(
            source(given), half.at[c], send_sem.at[0, c], recv_sem.at[0, c], other_core
        )

    def own_copy(c, source):
        return pltpu.make_async_copy(source(kept), own.at[c % 2], own_sem.at[c % 2])

    def start_core(c):
        def act(source):
            core_copy(c, source).start()
            own_copy(c, source).start()

        by_source(c, act)

    def first_copy(c):
        a, b, first_device, second_device = axes(c)
        rows = pl.multiple_of(64 - a * 64, 64)
        return remote(
            half.at[c, :, pl.ds(rows, 64), :],
            quarter.at[c],
            send_sem.at[1, c],
            recv_sem.at[1, c],
            first_device,
        )

    def second_copy(c):
        a, b, first_device, second_device = axes(c)
        rows = pl.multiple_of(32 - b * 32, 32)
        return remote(
            quarter.at[c, :, pl.ds(rows, 32), :],
            eighth.at[c],
            send_sem.at[2, c],
            recv_sem.at[2, c],
            second_device,
        )

    def z_copy(c, d):
        device = others_z[d]
        return remote(
            eighth.at[c, device[1]],
            pieces.at[c, d],
            z_send_sem.at[c, d],
            z_recv_sem.at[c, d],
            device,
        )

    def place_copy(c):
        a, b, first_device, second_device = axes(c)
        rows = pl.ds(pl.multiple_of(core * 128 + a * 64 + b * 32, 32), 32)
        return pltpu.make_async_copy(final.at[c], out_ref.at[c, rows, :], place_sem.at[c])

    def back_second(c):
        a, b, first_device, second_device = axes(c)
        rows = pl.ds(pl.multiple_of(core * 128 + a * 64 + b * 32, 32), 32)
        return remote(
            final.at[c], out_ref.at[c, rows, :], send_sem.at[3, c], recv_sem.at[3, c], second_device
        )

    def back_first(c):
        a, b, first_device, second_device = axes(c)
        rows = pl.ds(pl.multiple_of(core * 128 + a * 64, 64), 64)
        return remote(
            out_ref.at[c, rows, :],
            out_ref.at[c, rows, :],
            send_sem.at[4, c],
            recv_sem.at[4, c],
            first_device,
        )

    def back_core(c):
        rows = pl.ds(kept, 128)
        return remote(
            out_ref.at[c, rows, :],
            out_ref.at[c, rows, :],
            send_sem.at[5, c],
            recv_sem.at[5, c],
            other_core,
        )

    def add_core(c):
        def act(source):
            core_copy(c, source).wait_recv()
            own_copy(c, source).wait()

        by_source(c, act)

        def put(s, r, value):
            half[c, s, pl.ds(r, 32), :] = value

        add_blocks(
            put,
            lambda s, r: half[c, s, pl.ds(r, 32), :],
            lambda s, r: own[c % 2, s, pl.ds(r, 32), :],
            4,
            128,
            32,
        )
        first_copy(c).start()

    def add_first(c):
        a, b, first_device, second_device = axes(c)
        first_copy(c).wait_recv()

        def put(s, r, value):
            quarter[c, s, pl.ds(r, 32), :] = value

        add_blocks(
            put,
            lambda s, r: quarter[c, s, pl.ds(r, 32), :],
            lambda s, r: half[c, s, pl.ds(pl.multiple_of(a * 64 + r, 32), 32), :],
            4,
            64,
            32,
        )
        second_copy(c).start()

    def add_second(c):
        a, b, first_device, second_device = axes(c)
        second_copy(c).wait_recv()

        def put(s, r, value):
            eighth[c, s, pl.ds(r, 32), :] = value

        add_blocks(
            put,
            lambda s, r: eighth[c, s, pl.ds(r, 32), :],
            lambda s, r: quarter[c, s, pl.ds(pl.multiple_of(b * 32 + r, 32), 32), :],
            4,
            32,
            32,
        )
        for d in range(3):
            z_copy(c, d).start()

    def add_z(c):
        for d in range(3):
            z_copy(c, d).wait_recv()
        total = eighth[c, z].astype(jnp.float32)
        for d in range(3):
            total = total + pieces[c, d].astype(jnp.float32)
        final[c] = total.astype(jnp.bfloat16)
        back_second(c).start()
        place_copy(c).start()

    def pass_first(c):
        place_copy(c).wait()
        back_second(c).wait_recv()
        back_first(c).start()

    def pass_core(c):
        back_first(c).wait_recv()
        back_core(c).start()

    def finish(c):
        back_core(c).wait()
        back_first(c).wait_send()
        back_second(c).wait_send()
        for d in range(3):
            z_copy(c, d).wait_send()
        second_copy(c).wait_send()
        first_copy(c).wait_send()
        by_source(c, lambda source: core_copy(c, source).wait_send())

    def small_copy(k):
        source = small_ref if k == 0 else small_sum.at[k - 1]
        device = (other_core, other_x, other_y)[k]
        return remote(source, small_in.at[k], small_send_sem.at[k], small_recv_sem.at[k], device)

    def small_z_copy(d):
        return remote(
            small_sum.at[2],
            small_z.at[z],
            small_send_sem.at[3 + d],
            small_recv_sem.at[3 + d],
            others_z[d],
        )

    def small_step(k):
        small_copy(k).wait()
        before = small_ref[...] if k == 0 else small_sum[k - 1]
        small_sum[k] = before + small_in[k]
        if k < 2:
            small_copy(k + 1).start()
        else:
            small_z[z] = small_sum[2]
            for d in range(3):
                small_z_copy(d).start()

    def small_end():
        for d in range(3):
            small_z_copy(d).wait()
        small_out_ref[...] = (small_z[0] + small_z[1]) + (small_z[2] + small_z[3])

    stages = (start_core, add_core, add_first, add_second, add_z, pass_first, pass_core, finish)
    small_copy(0).start()

    def step(t, carry):
        for k, stage in enumerate(stages):
            c = t - k

            @pl.when((c >= 0) & (c < CHUNKS))
            def _(stage=stage, c=c):
                stage(c)

        for k in range(3):

            @pl.when(t == k + 1)
            def _(k=k):
                small_step(k)

        @pl.when(t == 4)
        def _():
            small_end()

        return carry

    lax.fori_loop(0, CHUNKS + len(stages) - 1, step, 0)


def reduce_all(att, expand, shrink, small):
    small_rows = small.shape[0]
    dma = pltpu.SemaphoreType.DMA
    return pl.pallas_call(
        reduce_kernel,
        out_shape=(
            jax.ShapeDtypeStruct((CHUNKS, 256, D), jnp.bfloat16),
            jax.ShapeDtypeStruct(small.shape, jnp.float32),
        ),
        in_specs=[pl.BlockSpec(memory_space=pl.ANY)] * 3
        + [pl.BlockSpec(memory_space=pltpu.VMEM)],
        out_specs=(
            pl.BlockSpec(memory_space=pl.ANY),
            pl.BlockSpec(memory_space=pltpu.VMEM),
        ),
        scratch_shapes=[
            pltpu.VMEM((CHUNKS, 4, 128, D), jnp.bfloat16),
            pltpu.VMEM((2, 4, 128, D), jnp.bfloat16),
            pltpu.VMEM((CHUNKS, 4, 64, D), jnp.bfloat16),
            pltpu.VMEM((CHUNKS, 4, 32, D), jnp.bfloat16),
            pltpu.VMEM((CHUNKS, 3, 32, D), jnp.bfloat16),
            pltpu.VMEM((CHUNKS, 32, D), jnp.bfloat16),
            pltpu.VMEM((3, small_rows, 128), jnp.float32),
            pltpu.VMEM((3, small_rows, 128), jnp.float32),
            pltpu.VMEM((4, small_rows, 128), jnp.float32),
            dma((6, CHUNKS)),
            dma((6, CHUNKS)),
            dma((CHUNKS, 3)),
            dma((CHUNKS, 3)),
            dma((2,)),
            dma((CHUNKS,)),
            dma((6,)),
            dma((6,)),
        ],
        compiler_params=pltpu.CompilerParams(
            collective_id=0, has_side_effects=True, vmem_limit_bytes=48 * MIB
        ),
    )(att, expand, shrink, small)


def line_sum(part, whole, send_sem, recv_sem, z, others_z):
    copies = [
        remote(part, whole.at[z], send_sem.at[d], recv_sem.at[d], others_z[d]) for d in range(3)
    ]
    for copy in copies:
        copy.start()
    whole[z] = part[...]
    for copy in copies:
        copy.wait()
    return (whole[0] + whole[1]) + (whole[2] + whole[3])


def fold(tile):
    return jnp.sum(tile.reshape(-1, 8, tile.shape[-1]), axis=0)


def spread_scalar(value):
    return jnp.broadcast_to(value, (1, 128))


def factor_kernel(
    grad_ref,
    att_rows_ref,
    exp_rows_ref,
    shr_rows_ref,
    cols_ref,
    att_rows_out,
    exp_rows_out,
    shr_rows_out,
    cols_out,
    scale_out,
    part,
    whole,
    send_sem,
    recv_sem,
):
    core, x, y, z, other_core, other_x, other_y, others_z = neighbours()
    greet(others_z)
    part[...] = jnp.zeros_like(part)

    def tile(chunk, r, step):
        return grad_ref[chunk, pl.ds(r, step), :].astype(jnp.float32)

    def add(slot, col, weighted):
        part[slot : slot + 1, :] += jnp.sum(col, axis=0, keepdims=True)
        part[16 + slot : 17 + slot, :] += jnp.sum(weighted, axis=0, keepdims=True)

    def scan_rows(chunks, slots, rows_in, rows_out, total_at):
        width = float(len(chunks) * D)
        step = 64 // len(chunks)

        def body(i, carry):
            cols, weights, total = carry
            r = pl.multiple_of(i * step, step)
            squares = [jnp.square(tile(c, r, step)) for c in chunks]
            row_sum = squares[0]
            for square in squares[1:]:
                row_sum = row_sum + square
            row_sum = jnp.sum(row_sum, axis=1, keepdims=True)
            rows = DECAY_RATE * rows_in[pl.ds(r, step), :] + (1.0 - DECAY_RATE) * (
                row_sum / width + FACTOR_EPS
            )
            rows_out[pl.ds(r, step), :] = rows
            inverse = 1.0 / rows
            cols = [c + fold(s) for c, s in zip(cols, squares)]
            weights = [w + fold(s * inverse) for w, s in zip(weights, squares)]
            return cols, weights, total + fold(rows)

        zeros = [jnp.zeros((8, D), jnp.float32) for _ in chunks]
        cols, weights, total = lax.fori_loop(
            0, 256 // step, body, (zeros, zeros, jnp.zeros((8, 1), jnp.float32))
        )
        for slot, col, weighted in zip(slots, cols, weights):
            add(slot, col, weighted)
        row, lane = total_at
        part[row : row + 1, lane : lane + 128] += spread_scalar(jnp.sum(total))

    for i in range(8):
        scan_rows([i], [i], att_rows_ref.at[i], att_rows_out.at[i], (13, 128 * i))
    scan_rows([8, 9, 10, 11], [8, 9, 10, 11], exp_rows_ref, exp_rows_out, (14, 0))
    for i in range(4):
        scan_rows([12 + i], [12], shr_rows_ref.at[i], shr_rows_out.at[i], (14, 128))
    total = line_sum(part, whole, send_sem, recv_sem, z, others_z)
    row_counts = [D] * 12 + [FF]
    means = [total[13:14, 128 * i : 128 * i + 1] / D for i in range(8)]
    means = means + [total[14:15, 0:1] / D] * 4 + [total[14:15, 128:129] / FF]
    cols_new, quotients = [], []
    for slot in range(13):
        new = DECAY_RATE * cols_ref[slot : slot + 1, :] + (1.0 - DECAY_RATE) * (
            total[slot : slot + 1] / row_counts[slot] + FACTOR_EPS
        )
        cols_new.append(new)
        quotients.append(jnp.sum(total[16 + slot : 17 + slot] / new, axis=1, keepdims=True))
        cols_out[slot : slot + 1, :] = new
    expand_quotient = quotients[8] + quotients[9] + quotients[10] + quotients[11]
    for slot in range(13):
        if slot < 8:
            mean_square = means[slot] * quotients[slot] / (D * D)
            rate = STEP_RATE * (OUT_GAIN if slot % 4 == 3 else 1.0)
        else:
            quotient = expand_quotient if slot < 12 else quotients[12]
            mean_square = means[slot] * quotient / (D * FF)
            rate = STEP_RATE
        factor = rate / jnp.maximum(1.0, jnp.sqrt(mean_square) / CLIP_LEVEL)
        scale_out[slot : slot + 1, :] = lax.rsqrt(cols_new[slot] / means[slot]) * factor


def factors(grads, att_rows, exp_rows, shr_rows, cols):
    vmem = pl.BlockSpec(memory_space=pltpu.VMEM)
    shape = jax.ShapeDtypeStruct
    return pl.pallas_call(
        factor_kernel,
        out_shape=(
            shape((8, 256, 1), jnp.float32),
            shape((256, 1), jnp.float32),
            shape((4, 256, 1), jnp.float32),
            shape((16, D), jnp.float32),
            shape((16, D), jnp.float32),
        ),
        in_specs=[vmem] * 5,
        out_specs=(vmem,) * 5,
        scratch_shapes=[
            pltpu.VMEM((32, D), jnp.float32),
            pltpu.VMEM((4, 32, D), jnp.float32),
            pltpu.SemaphoreType.DMA((3,)),
            pltpu.SemaphoreType.DMA((3,)),
        ],
        compiler_params=pltpu.CompilerParams(
            collective_id=1, has_side_effects=True, vmem_limit_bytes=40 * MIB
        ),
    )(grads, att_rows, exp_rows, shr_rows, cols)


def update_attention_kernel(
    grad_ref, weight_ref, rows_ref, scale_ref, grad_out, new_out, copy_out, grads, change
):
    block = grad_ref.shape[1]
    for i in range(8):
        grad = grad_ref[i].astype(jnp.float32)
        scaled = grad * lax.rsqrt(rows_ref[i]) * scale_ref[i : i + 1, :]
        every = pl.ds(i, block, stride=8)
        for lane in range(8):
            columns = slice(lane * 128, lane * 128 + 128)
            grads[lane, every, :] = grad[:, columns]
            change[lane, every, :] = scaled[:, columns]
    for lane in range(8):
        columns = slice(lane * 128, lane * 128 + 128)
        grad_out[:, columns] = grads[lane]
        new = weight_ref[:, columns] - change[lane]
        new_out[:, columns] = new
        copy_out[:, columns] = new.astype(jnp.bfloat16)


def update_attention(grads, weights, rows, scale):
    block = 32
    wide = pl.BlockSpec((block * 8, D), lambda i: (i, 0))
    shape = jax.ShapeDtypeStruct
    new = pl.pallas_call(
        update_attention_kernel,
        grid=(256 // block,),
        out_shape=(
            shape((2048, D), jnp.float32),
            shape((2048, D), jnp.float32),
            shape((2048, D), jnp.bfloat16),
        ),
        in_specs=[
            pl.BlockSpec((8, block, D), lambda i: (0, i, 0)),
            wide,
            pl.BlockSpec((8, block, 1), lambda i: (0, i, 0)),
            pl.BlockSpec((16, D), lambda i: (0, 0)),
        ],
        out_specs=(wide,) * 3,
        scratch_shapes=[pltpu.VMEM((8, block * 8, 128), jnp.float32)] * 2,
        compiler_params=pltpu.CompilerParams(vmem_limit_bytes=40 * MIB),
    )(grads, weights.reshape(2048, D), rows, scale)
    return [t.reshape(256, 8, D) for t in new]


def update_kernel(
    first, slots, grad_ref, weight_ref, rows_ref, scale_ref, grad_out, new_out, copy_out
):
    spans = 4 if slots == 4 else 1
    wide = D // spans
    for i in range(slots):
        grads = grad_ref[i].astype(jnp.float32)
        changes = grads * (lax.rsqrt(rows_ref[...]) * scale_ref[first + i : first + i + 1, :])
        for s in range(spans):
            start = s * D + i * wide
            columns = slice(start, start + wide)
            part = slice(s * wide, s * wide + wide)
            grad_out[:, columns] = grads[:, part]
            new = weight_ref[:, columns] - changes[:, part]
            new_out[:, columns] = new
            copy_out[:, columns] = new.astype(jnp.bfloat16)


def update_plain(grads, weights, rows, scale, first, slots, grad_map):
    count, width = weights.shape
    block = 128 // slots
    wide = pl.BlockSpec((block, width), lambda i: (i, 0))
    shape = jax.ShapeDtypeStruct
    return pl.pallas_call(
        lambda *refs: update_kernel(first, slots, *refs),
        grid=(count // block,),
        out_shape=(
            shape(weights.shape, jnp.float32),
            shape(weights.shape, jnp.float32),
            shape(weights.shape, jnp.bfloat16),
        ),
        in_specs=[
            pl.BlockSpec((slots, block, D), grad_map),
            wide,
            pl.BlockSpec((block, 1), lambda i: (i, 0)),
            pl.BlockSpec((16, D), lambda i: (0, 0)),
        ],
        out_specs=(wide,) * 3,
        compiler_params=pltpu.CompilerParams(vmem_limit_bytes=40 * MIB),
    )(grads, weights, rows, scale)


def update_direct(
    grads,
    attention_weights,
    expand_weight,
    shrink_weight,
    attention_rows,
    attention_cols,
    expand_rows,
    expand_cols,
    shrink_rows,
    shrink_cols,
):
    cols = jnp.concatenate(
        [attention_cols, hidden_blocks(expand_cols), shrink_cols.reshape(1, D), jnp.ones((3, D))]
    )
    att_rows, exp_rows, shr_rows, cols_new, scale = factors(
        grads,
        attention_rows[:, :, None],
        expand_rows[:, None],
        shrink_rows.reshape(4, 256, 1),
        cols,
    )
    shr_rows = shr_rows.reshape(-1, 1)
    attention = update_attention(grads, attention_weights, att_rows, scale)
    expand = update_plain(grads, expand_weight, exp_rows, scale, 8, 4, lambda i: (2, i, 0))
    shrink = update_plain(
        grads, shrink_weight, shr_rows, scale, 12, 1, lambda i: (12 + i // 2, i % 2, 0)
    )
    return (
        attention,
        expand,
        shrink,
        (att_rows[:, :, 0], exp_rows[:, 0], shr_rows[:, 0]),
        (cols_new[0:8], hidden_flat(cols_new[8:12]), cols_new[12]),
    )


def as_rows(vector):
    rows = -(-vector.shape[0] // 1024) * 8
    return jnp.pad(vector, (0, rows * 128 - vector.shape[0])).reshape(rows, 128)


def gather_rows(piece):
    return lax.all_gather(piece, ("shard", "rep"), axis=0, tiled=True)


def own_piece(block, replicas):
    rows = block.shape[0] // replicas
    return lax.dynamic_slice_in_dim(block, lax.axis_index("rep") * rows, rows, axis=0)


def scatter_rows(grad):
    piece = lax.psum_scatter(
        grad.astype(jnp.bfloat16), ("shard", "rep"), scatter_dimension=0, tiled=True
    )
    return lax.all_gather(piece, "rep", axis=0, tiled=True)


def local_factors(grad, rows):
    square = grad * grad
    rows_new = DECAY_RATE * rows + (1.0 - DECAY_RATE) * jnp.mean(square + FACTOR_EPS, axis=-1)
    col_part = jnp.sum(square + FACTOR_EPS, axis=0)
    weighted = jnp.sum(square / rows_new[..., None], axis=0)
    return rows_new, col_part, weighted, jnp.sum(rows_new, axis=0)


def finish_factors(grad, weight, rows_new, cols, col_sum, weighted, row_total, row_count, rate):
    cols_new = DECAY_RATE * cols + (1.0 - DECAY_RATE) * col_sum / row_count
    mean_rows = row_total / row_count
    mean_square = mean_rows * jnp.sum(weighted / cols_new, axis=-1) / (row_count * cols.shape[-1])
    factor = rate / jnp.maximum(1.0, jnp.sqrt(mean_square) / CLIP_LEVEL)
    scaled = lax.rsqrt(cols_new / mean_rows[..., None]) * factor[..., None]
    fresh = weight - grad * (lax.rsqrt(rows_new)[..., None] * scaled[None])
    return fresh, cols_new


def on_device(
    tokens,
    encoder,
    cotangent,
    lengths,
    encoder_lengths,
    dealt_order,
    attention_weights,
    expand_weight,
    shrink_weight,
    small_params,
    attention_rows,
    attention_cols,
    expand_rows,
    expand_cols,
    shrink_rows,
    shrink_cols,
    small_moment,
):
    devices = lax.axis_size(("rep", "shard"))
    replicas = lax.axis_size("rep")
    shards = lax.axis_size("shard")
    slot_tokens = tokens.shape[0]
    slot_states = encoder.shape[0]
    position = lax.axis_index(("rep", "shard"))
    inverse = (
        jnp.zeros((devices,), jnp.int32).at[dealt_order].set(jnp.arange(devices, dtype=jnp.int32))
    )
    direct = replicas == 8 and shards == 4
    if direct:
        qkv_pieces, rest_pieces = weight_pieces(
            attention_weights, expand_weight, shrink_weight, neighbours()
        )
        tokens, qkv_full = front(inverse, tokens, qkv_pieces)
        matrices = [qkv_full[i] for i in range(3)]
    else:
        attention_piece = own_piece(attention_weights.reshape(-1, 8 * D), replicas)
        attention_full = gather_rows(attention_piece.astype(jnp.bfloat16))
        matrices = [attention_full[:, i * D : (i + 1) * D] for i in range(8)]
        spread = lax.all_to_all(
            tokens.reshape(devices, slot_tokens // devices, D),
            ("rep", "shard"),
            split_axis=0,
            concat_axis=0,
            tiled=True,
        )
        picked = jnp.take(spread, inverse, axis=0)
        tokens = lax.all_to_all(
            picked, ("rep", "shard"), split_axis=0, concat_axis=0, tiled=True
        ).reshape(slot_tokens, D)
        expand_full = gather_rows(own_piece(expand_weight, replicas).astype(jnp.bfloat16))
        shrink_full = gather_rows(own_piece(shrink_weight, replicas).astype(jnp.bfloat16))
        expand_full = jnp.swapaxes(hidden_blocks(expand_full), 0, 1)
        shrink_full = jnp.swapaxes(shrink_full.reshape(4, 4, 256, D), 0, 1).reshape(4, 1024, D)
    states = encoder
    incoming = cotangent
    valid_tokens = lengths[position]
    valid_states = encoder_lengths[position]
    parts = unpack(small_params)
    q_self = ((forward_product(tokens, matrices[0]) + parts[0]) * 0.125).astype(
        jnp.bfloat16
    )
    k_self = forward_product(tokens, matrices[1]).astype(jnp.bfloat16)
    v_self = (forward_product(tokens, matrices[2]) + parts[1]).astype(jnp.bfloat16)
    if direct:
        o_self_low, lse_self, rest_full = attend_gather(
            q_self, k_self, v_self, valid_tokens, rest_pieces
        )
        matrices = matrices + [rest_full[i] for i in range(5)]
        expand_full = rest_full[5:13:2]
        shrink_full = rest_full[6:13:2]
    else:
        o_self_low, lse_self = attend(q_self, k_self, v_self, valid_tokens, True)
    branch_a = forward_product(o_self_low, matrices[3]) + parts[2]
    tokens_wide = tokens.astype(jnp.float32)
    hidden_one, norm_one_back = jax.vjp(layer_norm, tokens_wide + branch_a, parts[8], parts[9])
    hidden_one_low = hidden_one.astype(jnp.bfloat16)
    q_cross = (
        (forward_product(hidden_one_low, matrices[4]) + parts[3]) * 0.125
    ).astype(jnp.bfloat16)
    k_cross = forward_product(states, matrices[5]).astype(jnp.bfloat16)
    v_cross = (forward_product(states, matrices[6]) + parts[4]).astype(jnp.bfloat16)
    o_cross_low, lse_cross = attend(q_cross, k_cross, v_cross, valid_states, False)
    branch_c = forward_product(o_cross_low, matrices[7]) + parts[5]
    hidden_two, norm_two_back = jax.vjp(layer_norm, hidden_one + branch_c, parts[10], parts[11])
    hidden_two_low = hidden_two.astype(jnp.bfloat16)
    pre_act = (
        jnp.einsum("td,jdh->jth", hidden_two_low, expand_full, preferred_element_type=jnp.float32)
        + hidden_blocks(parts[6])[:, None, :]
    )
    activated, gelu_back = jax.vjp(gelu_exact, pre_act)
    activated_low = activated.astype(jnp.bfloat16)
    branch_m = (
        jnp.einsum("jth,jho->to", activated_low, shrink_full, preferred_element_type=jnp.float32)
        + parts[7]
    )
    result, norm_three_back = jax.vjp(layer_norm, hidden_two + branch_m, parts[12], parts[13])
    usable_rows = (jnp.arange(slot_tokens, dtype=jnp.int32) < valid_tokens).astype(jnp.float32)[
        :, None
    ]
    squares = jnp.stack(
        [
            jnp.sum(usable_rows * t * t)
            for t in (tokens_wide, branch_a, hidden_one, branch_c, hidden_two, branch_m)
        ]
    )
    d_third, d_gain_three, d_shift_three = norm_three_back(
        incoming.astype(jnp.float32) * usable_rows
    )
    d_mlp = d_third.astype(jnp.bfloat16)
    grad_shrink = jnp.einsum(
        "jth,to->jho", activated_low, d_mlp, preferred_element_type=jnp.float32
    )
    grad_shrink_offset = row_sum(d_mlp)
    d_activated = jnp.einsum(
        "to,jho->jth", d_mlp, shrink_full, preferred_element_type=jnp.float32
    )
    d_pre = gelu_back(d_activated)[0].astype(jnp.bfloat16)
    grad_expand = jnp.einsum(
        "td,jth->jdh", hidden_two_low, d_pre, preferred_element_type=jnp.float32
    )
    grad_expand_offset = hidden_flat(jnp.sum(d_pre.astype(jnp.float32), axis=1))
    d_hidden_two = d_third + jnp.einsum(
        "jth,jdh->td", d_pre, expand_full, preferred_element_type=jnp.float32
    )
    d_second, d_gain_two, d_shift_two = norm_two_back(d_hidden_two)
    d_branch_c = d_second.astype(jnp.bfloat16)
    grad_cross_out = weight_product(o_cross_low, d_branch_c)
    grad_cross_out_offset = row_sum(d_branch_c)
    d_o_cross = input_product(d_branch_c, matrices[7]).astype(jnp.bfloat16)
    dq_cross, dk_cross, dv_cross, cross_sums = attend_back(
        q_cross, k_cross, v_cross, d_o_cross, lse_cross, valid_states, False
    )
    grad_cross_query = weight_product(hidden_one_low, dq_cross)
    grad_cross_key = weight_product(states, dk_cross)
    grad_cross_value = weight_product(states, dv_cross)
    state_grad = input_product(dk_cross, matrices[5]) + input_product(
        dv_cross, matrices[6]
    )
    d_hidden_one = d_second + input_product(dq_cross, matrices[4])
    d_first, d_gain_one, d_shift_one = norm_one_back(d_hidden_one)
    d_branch_a = d_first.astype(jnp.bfloat16)
    grad_self_out = weight_product(o_self_low, d_branch_a)
    grad_self_out_offset = row_sum(d_branch_a)
    d_o_self = input_product(d_branch_a, matrices[3]).astype(jnp.bfloat16)
    dq_self, dk_self, dv_self, self_sums = attend_back(
        q_self, k_self, v_self, d_o_self, lse_self, valid_tokens, True
    )
    grad_self_query = weight_product(tokens, dq_self)
    grad_self_key = weight_product(tokens, dk_self)
    grad_self_value = weight_product(tokens, dv_self)
    token_grad = (
        d_first
        + input_product(dq_self, matrices[0])
        + input_product(dk_self, matrices[1])
        + input_product(dv_self, matrices[2])
    )
    small_partial = jnp.concatenate(
        [
            self_sums[:, 0, :].reshape(-1),
            self_sums[:, 1, :].reshape(-1),
            grad_self_out_offset,
            cross_sums[:, 0, :].reshape(-1),
            cross_sums[:, 1, :].reshape(-1),
            grad_cross_out_offset,
            grad_expand_offset,
            grad_shrink_offset,
            d_gain_one,
            d_shift_one,
            d_gain_two,
            d_shift_two,
            d_gain_three,
            d_shift_three,
        ]
    )
    attention_grads = [
        grad_self_query,
        grad_self_key,
        grad_self_value,
        grad_self_out,
        grad_cross_query,
        grad_cross_key,
        grad_cross_value,
        grad_cross_out,
    ]
    small_all = jnp.concatenate([small_partial, squares])
    if direct:
        reduced, totals = reduce_all(
            jnp.stack([t.astype(jnp.bfloat16) for t in attention_grads]).reshape(8, 4, 256, D),
            grad_expand.astype(jnp.bfloat16).reshape(4, 4, 256, D),
            grad_shrink.astype(jnp.bfloat16).reshape(4, 4, 256, D),
            as_rows(small_all),
        )
        totals = totals.reshape(-1)[: small_all.shape[0]]
        (
            (g_attention, attention_new, attention_copy),
            (g_expand, expand_new, expand_copy),
            (g_shrink, shrink_new, shrink_copy),
            (attention_rows_new, expand_rows_new, shrink_rows_new),
            (attention_cols_new, expand_cols_new, shrink_cols_new),
        ) = update_direct(
            reduced,
            attention_weights,
            expand_weight,
            shrink_weight,
            attention_rows,
            attention_cols,
            expand_rows,
            expand_cols,
            shrink_rows,
            shrink_cols,
        )
    else:
        totals = lax.psum(small_all, ("rep", "shard"))
        grad_shrink = jnp.swapaxes(grad_shrink.reshape(4, 4, 256, D), 0, 1).reshape(FF, D)
        grad_expand = hidden_flat(jnp.swapaxes(grad_expand, 0, 1))
        g_shrink = scatter_rows(grad_shrink).astype(jnp.float32)
        g_expand = scatter_rows(grad_expand).astype(jnp.float32)
        g_attention = (
            scatter_rows(jnp.concatenate(attention_grads, axis=1))
            .reshape(-1, 8, D)
            .astype(jnp.float32)
        )
        attention_rows_new, *attention_parts = local_factors(g_attention, attention_rows.T)
        expand_rows_new, *expand_parts = local_factors(g_expand, expand_rows)
        shrink_rows_new, *shrink_parts = local_factors(g_shrink, shrink_rows)
        flat = attention_parts + expand_parts + shrink_parts
        flat_parts = jnp.concatenate([t.reshape(-1) for t in flat])
        summed = lax.psum(flat_parts, "shard")
        sums = []
        offset = 0
        for t in flat:
            sums.append(summed[offset : offset + t.size].reshape(t.shape))
            offset = offset + t.size
        attention_rates = STEP_RATE * jnp.where(jnp.arange(8) % 4 == 3, OUT_GAIN, 1.0).astype(
            jnp.float32
        )
        attention_new, attention_cols_new = finish_factors(
            g_attention,
            attention_weights,
            attention_rows_new,
            attention_cols,
            *sums[0:3],
            D,
            attention_rates,
        )
        expand_new, expand_cols_new = finish_factors(
            g_expand, expand_weight, expand_rows_new, expand_cols, *sums[3:6], D, STEP_RATE
        )
        shrink_new, shrink_cols_new = finish_factors(
            g_shrink, shrink_weight, shrink_rows_new, shrink_cols, *sums[6:9], FF, STEP_RATE
        )
        attention_rows_new = attention_rows_new.T
        attention_copy = attention_new.astype(jnp.bfloat16)
        expand_copy = expand_new.astype(jnp.bfloat16)
        shrink_copy = shrink_new.astype(jnp.bfloat16)
    small_grad = totals[: small_params.shape[0]]
    small_moment_new = DECAY_RATE * small_moment + (1.0 - DECAY_RATE) * (
        small_grad * small_grad + FACTOR_EPS
    )
    small_update = small_grad * lax.rsqrt(small_moment_new)
    small_scale = jnp.sqrt(jnp.mean(small_update * small_update))
    small_new = small_params - SMALL_RATE * small_update / jnp.maximum(
        1.0, small_scale / CLIP_LEVEL
    )
    norm_stats = jnp.sqrt(
        totals[small_params.shape[0] :] / (jnp.sum(lengths).astype(jnp.float32) * D)
    )
    return (
        result.astype(jnp.bfloat16),
        token_grad.astype(jnp.bfloat16),
        state_grad.astype(jnp.bfloat16),
        g_attention,
        g_expand,
        g_shrink,
        small_grad,
        attention_new,
        expand_new,
        shrink_new,
        small_new,
        attention_copy,
        expand_copy,
        shrink_copy,
        attention_rows_new,
        attention_cols_new,
        expand_rows_new,
        expand_cols_new,
        shrink_rows_new,
        shrink_cols_new,
        small_moment_new,
        norm_stats,
    )


def solution(mesh):
    in_specs = (
        P(("rep", "shard"), None),
        P(("rep", "shard"), None),
        P(("rep", "shard"), None),
        P(),
        P(),
        P(),
        P("shard", None, None),
        P("shard", None),
        P("shard", None),
        P(),
        P(None, "shard"),
        P(),
        P("shard"),
        P(),
        P("shard"),
        P(),
        P(),
    )
    out_specs = (
        P(("rep", "shard"), None),
        P(("rep", "shard"), None),
        P(("rep", "shard"), None),
        P("shard", None, None),
        P("shard", None),
        P("shard", None),
        P(),
        P("shard", None, None),
        P("shard", None),
        P("shard", None),
        P(),
        P("shard", None, None),
        P("shard", None),
        P("shard", None),
        P(None, "shard"),
        P(),
        P("shard"),
        P(),
        P("shard"),
        P(),
        P(),
        P(),
    )
    return jax.shard_map(
        on_device, mesh=mesh, in_specs=in_specs, out_specs=out_specs, check_vma=False
    )
```

```python
import math

import jax
import jax.numpy as jnp
from jax import lax
from jax.experimental import pallas as pl
from jax.experimental.pallas import tpu as pltpu
from jax.sharding import PartitionSpec as P

D = 1024
HEADS = 16
HEAD_DIM = 64
FF = 4096


DECAY_RATE = 0.5
CLIP_LEVEL = 0.25
STEP_RATE = 0.1
SMALL_RATE = 0.4
OUT_GAIN = 8.0
NORM_EPS = 1e-05
FACTOR_EPS = 1e-30
MASKED = -1e30
MESH = pl.DeviceIdType.MESH
CHUNKS = 16
MIB = 1 << 20


def layer_norm(r, norm_gain, norm_shift):
    centred = r - jnp.mean(r, axis=-1, keepdims=True)
    spread = jnp.mean(centred * centred, axis=-1, keepdims=True)
    return centred * lax.rsqrt(spread + NORM_EPS) * norm_gain + norm_shift


def gelu_exact(values):
    return jax.nn.gelu(values, approximate=False)


def unpack(small):
    extents = [D] * 6 + [FF] + [D] * 7
    pieces = []
    offset = 0
    for extent in extents:
        pieces.append(small[offset : offset + extent])
        offset = offset + extent
    return pieces


def forward_product(source, matrix):
    return jnp.dot(source, matrix, preferred_element_type=jnp.float32)


def input_product(grad_low, matrix):
    return jnp.einsum("to,io->ti", grad_low, matrix, preferred_element_type=jnp.float32)


def weight_product(source, grad_low):
    return jnp.einsum("ti,to->io", source, grad_low, preferred_element_type=jnp.float32)


def row_sum(grad_low):
    return jnp.sum(grad_low.astype(jnp.float32), axis=0)


def transposed(block):
    return block.astype(jnp.float32).T.astype(jnp.bfloat16)


def half_lanes(shape, dim):
    return lax.broadcasted_iota(jnp.int32, shape, dim)


def masked_keys(keys, length, head):
    place = half_lanes(keys.shape, 0)
    lane = half_lanes(keys.shape, 1)
    blocked = jnp.where((lane == 64 - 64 * head) & (place >= length), MASKED, 0.0)
    own = (lane >= 64 * head) & (lane < 64 * head + 64)
    return jnp.where(own, keys.astype(jnp.float32), blocked).astype(jnp.bfloat16)


def own_head(rows_t, head, fill):
    place = half_lanes(rows_t.shape, 0)
    own = (place >= 64 * head) & (place < 64 * head + 64)
    other = jnp.where(place == 64 - 64 * head, fill, 0.0)
    return jnp.where(own, rows_t.astype(jnp.float32), other).astype(jnp.bfloat16)


def product(first, second):
    return jnp.dot(first, second, preferred_element_type=jnp.float32)


def causal_mask(scores, step):
    kept = scores.shape[0] - step
    last = scores[kept:]
    allowed = half_lanes(last.shape, 0) <= half_lanes(last.shape, 1)
    last = jnp.where(allowed, last, MASKED)
    return last if kept == 0 else jnp.concatenate([scores[:kept], last], axis=0)


def attend_pair(causal, step, length, q_ref, k_ref, v_ref, o_ref, lse_ref, o_t):
    q_t = transposed(q_ref[...])
    v_t = transposed(v_ref[...])
    for head in range(2):
        keys = masked_keys(k_ref[...], length, head)
        queries = own_head(q_t, head, 1.0)
        rows = slice(64 * head, 64 * head + 64)
        for start in range(0, q_ref.shape[0], step):
            columns = slice(start, start + step)
            end = start + step if causal else k_ref.shape[0]
            scores = product(keys[:end], queries[:, columns])
            if causal:
                scores = causal_mask(scores, step)
            top = jnp.max(scores, axis=0, keepdims=True)
            raised = jnp.exp(scores - top)
            total = jnp.sum(raised, axis=0, keepdims=True)
            probs = (raised * (1.0 / total)).astype(jnp.bfloat16)
            o_t[rows, columns] = product(v_t[rows, :end], probs)
            lse_ref[0, head : head + 1, columns] = top + jnp.log(total)
    o_ref[...] = o_t[...].T.astype(jnp.bfloat16)


def attend_back_pair(
    causal,
    step,
    length,
    q_ref,
    k_ref,
    v_ref,
    do_ref,
    lse_ref,
    dq_ref,
    dk_ref,
    dv_ref,
    put_sums,
    dq_t,
    dk_sum,
    dv_sum,
):
    key_rows = k_ref.shape[0]
    q_t = transposed(q_ref[...])
    k_t = transposed(k_ref[...])
    do_t = transposed(do_ref[...])
    values = v_ref[...]
    for head in range(2):
        keys = masked_keys(k_ref[...], length, head)
        queries = own_head(q_t, head, 1.0)
        grads = own_head(do_t, head, 0.0)
        rows = slice(64 * head, 64 * head + 64)
        count = q_ref.shape[0] // step
        for b in reversed(range(count)):
            start = b * step
            columns = slice(start, start + step)
            end = start + step if causal else key_rows
            scores = product(keys[:end], queries[:, columns])
            if causal:
                scores = causal_mask(scores, step)
            probs = jnp.exp(scores - lse_ref[0, head : head + 1, columns])
            weighted = probs * product(values[:end], grads[:, columns])
            delta = jnp.sum(weighted, axis=0, keepdims=True)
            d_scores = (weighted - probs * delta).astype(jnp.bfloat16)
            dv = product(probs.astype(jnp.bfloat16), do_ref[columns, :])
            dk = product(d_scores, q_ref[columns, :])
            if b == count - 1:
                dv_sum[head, :end] = dv
                dk_sum[head, :end] = dk
            else:
                dv_sum[head, :end] += dv
                dk_sum[head, :end] += dk
            dq_t[rows, columns] = product(k_t[rows, :end], d_scores)
    first = half_lanes((key_rows, 128), 1) < 64
    dk_ref[...] = jnp.where(first, dk_sum[0, :key_rows], dk_sum[1, :key_rows]).astype(jnp.bfloat16)
    dv = jnp.where(first, dv_sum[0, :key_rows], dv_sum[1, :key_rows]).astype(jnp.bfloat16)
    dv_ref[...] = dv
    dq = (dq_t[...] * 0.125).T.astype(jnp.bfloat16)
    dq_ref[...] = dq
    put_sums(
        jnp.sum(dq.astype(jnp.float32), axis=0, keepdims=True),
        jnp.sum(dv.astype(jnp.float32), axis=0, keepdims=True),
    )


SCALARS = pl.BlockSpec(memory_space=pltpu.SMEM)


def neighbours():
    rep = lax.axis_index("rep")
    z = lax.axis_index("shard")
    core = rep % 2
    x = (rep // 2) % 2
    y = rep // 4
    other_core = (rep + 1 - 2 * core, z)
    other_x = (rep + 2 - 4 * x, z)
    other_y = (rep + 4 - 8 * y, z)
    others_z = [(rep, (z + d) % 4) for d in (1, 2, 3)]
    return core, x, y, z, other_core, other_x, other_y, others_z


def greet(devices):
    barrier = pltpu.get_barrier_semaphore()
    for device in devices:
        pl.semaphore_signal(barrier, inc=1, device_id=device, device_id_type=MESH)
    pl.semaphore_wait(barrier, len(devices))


def remote(src, dst, send, recv, device):
    return pltpu.make_async_remote_copy(
        src_ref=src, dst_ref=dst, send_sem=send, recv_sem=recv, device_id=device, device_id_type=MESH
    )


def gather_copies(refs, c, parity, places):
    piece, full, place_sem, z_send, z_recv, send, recv = refs
    core, x, y, z, other_core, other_x, other_y, others_z = places
    a = x + parity * (y - x)
    b = y + parity * (x - y)
    first = (other_x[0] + parity * (other_y[0] - other_x[0]), z)
    second = (other_y[0] + parity * (other_x[0] - other_y[0]), z)
    own = pl.ds(pl.multiple_of(core * 128 + a * 64 + b * 32, 32), 32)
    steps = (
        (own, second),
        (pl.ds(pl.multiple_of(core * 128 + a * 64, 64), 64), first),
        (pl.ds(pl.multiple_of(core * 128, 128), 128), other_core),
    )

    def local():
        return pltpu.make_async_copy(piece.at[c], full.at[c, z, own, :], place_sem.at[c])

    def line(d):
        return remote(
            piece.at[c], full.at[c, z, own, :], z_send.at[c, d], z_recv.at[c, d], others_z[d]
        )

    def pair(k):
        block = full.at[c, :, steps[k][0], :]
        return remote(block, block, send.at[k, c], recv.at[k, c], steps[k][1])

    return local, line, pair


def gather_stage(k, refs, c, parity, places):
    local, line, pair = gather_copies(refs, c, parity, places)
    if k == 0:
        local().start()
        for d in range(3):
            line(d).start()
    if k == 1:
        local().wait()
        for d in range(3):
            line(d).wait_recv()
        pair(0).start()
    if k == 2 or k == 3:
        pair(k - 2).wait_recv()
        pair(k - 1).start()
    if k == 4:
        pair(2).wait()
        pair(1).wait_send()
        pair(0).wait_send()
        for d in range(3):
            line(d).wait_send()


def gather_sems(count):
    dma = pltpu.SemaphoreType.DMA
    return [dma((count,)), dma((count, 3)), dma((count, 3)), dma((3, count)), dma((3, count))]


def own_rows(blocks, parity, places):
    core, x, y = places[0:3]
    a = x + parity * (y - x)
    b = y + parity * (x - y)
    rows = lax.dynamic_slice_in_dim(blocks, core * 128 + a * 64 + b * 32, 32, axis=-2)
    return rows.astype(jnp.bfloat16)


def hidden_blocks(values):
    split = values.reshape(values.shape[:-1] + (4, 4, 256))
    split = jnp.swapaxes(split, -3, -2)
    return split.reshape(values.shape[:-1] + (4, 1024))


def hidden_flat(blocks):
    split = blocks.reshape(blocks.shape[:-2] + (4, 4, 256))
    split = jnp.swapaxes(split, -3, -2)
    return split.reshape(blocks.shape[:-2] + (FF,))


def weight_pieces(attention, expand, shrink, places):
    attention = jnp.swapaxes(
        jnp.stack([own_rows(jnp.swapaxes(attention, 0, 1), p, places) for p in range(2)]), 0, 1
    )
    picked = [attention[i, i % 2] for i in range(3)]
    picked = picked + [attention[3 + c, c % 2] for c in range(5)]
    ff = []
    for p in range(2):
        rows = own_rows(expand, p, places)
        ff.append(jnp.swapaxes(hidden_blocks(rows), 0, 1))
    for p in range(2):
        ff.append(own_rows(shrink.reshape(4, 256, D), p, places))
    for j in range(4):
        picked.append(ff[1][j])
        picked.append(ff[2][j])
    return jnp.stack(picked[0:3]), jnp.stack(picked[3:16])


def front_kernel(
    order_ref,
    tokens_ref,
    piece_ref,
    x_ref,
    full_ref,
    spread,
    picked,
    spread_send,
    spread_recv,
    back_send,
    back_recv,
    *gather_sem,
):
    places = neighbours()
    z = places[3]
    me = lax.axis_index("rep") * 4 + z
    refs = (piece_ref, full_ref) + gather_sem

    def device(offset):
        j = lax.rem(me + offset, 32)
        return j, (j // 4, j % 4)

    barrier = pltpu.get_barrier_semaphore()

    def greet_one(offset, carry):
        pl.semaphore_signal(barrier, inc=1, device_id=device(offset)[1], device_id_type=MESH)
        return carry

    lax.fori_loop(1, 32, greet_one, 0)
    pl.semaphore_wait(barrier, 31)

    def stage(k):
        for c in range(3):
            gather_stage(k, refs, c, c % 2, places)

    def spread_copy(offset):
        j, target = device(offset)
        return remote(
            tokens_ref.at[j],
            spread.at[me],
            spread_send.at[offset],
            spread_recv.at[offset],
            target,
        )

    def back_copy(offset):
        target = device(offset)[1]
        return remote(
            picked.at[offset], x_ref.at[me], back_send.at[offset], back_recv.at[offset], target
        )

    own_in = pltpu.make_async_copy(tokens_ref.at[me], spread.at[me], spread_recv.at[0])
    own_out = pltpu.make_async_copy(picked.at[0], x_ref.at[me], back_recv.at[0])
    stage(0)
    own_in.start()

    def start_spread(offset, carry):
        spread_copy(offset).start()
        return carry

    lax.fori_loop(1, 32, start_spread, 0)
    stage(1)
    stage(2)
    own_in.wait()

    def wait_spread(offset, carry):
        spread_copy(offset).wait()
        return carry

    lax.fori_loop(1, 32, wait_spread, 0)
    picked[0] = spread[order_ref[me]]
    own_out.start()

    def pick(offset, carry):
        picked[offset] = spread[order_ref[device(offset)[0]]]
        back_copy(offset).start()
        return carry

    lax.fori_loop(1, 32, pick, 0)
    stage(3)
    stage(4)
    own_out.wait()

    def wait_back(offset, carry):
        back_copy(offset).wait()
        return carry

    lax.fori_loop(1, 32, wait_back, 0)


def front(inverse, tokens, pieces):
    dma = pltpu.SemaphoreType.DMA
    any_space = pl.BlockSpec(memory_space=pl.ANY)
    x, full = pl.pallas_call(
        front_kernel,
        out_shape=(
            jax.ShapeDtypeStruct((32, 32, D), jnp.bfloat16),
            jax.ShapeDtypeStruct((3, 4, 256, D), jnp.bfloat16),
        ),
        in_specs=[
            pl.BlockSpec(memory_space=pltpu.SMEM),
            any_space,
            pl.BlockSpec(memory_space=pltpu.VMEM),
        ],
        out_specs=(any_space, any_space),
        scratch_shapes=[
            pltpu.VMEM((32, 32, D), jnp.bfloat16),
            pltpu.VMEM((32, 32, D), jnp.bfloat16),
            dma((32,)),
            dma((32,)),
            dma((32,)),
            dma((32,)),
        ]
        + gather_sems(3),
        compiler_params=pltpu.CompilerParams(
            collective_id=2, has_side_effects=True, vmem_limit_bytes=24 * MIB
        ),
    )(inverse, tokens.reshape(32, 32, D), pieces)
    return x.reshape(1024, D), full.reshape(3, 1024, D)


def fold(tile):
    return jnp.sum(tile.reshape(-1, 8, tile.shape[-1]), axis=0)


GATHERED = 13
GATHER_PLAN = (("z", 6.5), ("second", 6.5), ("first", 11.5), ("core", 3.0), (None, 0.0))


class GatherPlanner:
    def __init__(self, count):
        self.now = 0.0
        self.links = {"core": 0.0, "x": 0.0, "y": 0.0, "z": 0.0}
        self.stage = {c: 0 for c in range(count)}
        self.ready = {c: 0.0 for c in range(count)}

    def emit(self, c):
        stage = self.stage[c]
        link, span = GATHER_PLAN[stage]
        first, second = ("x", "y") if c % 2 == 0 else ("y", "x")
        link = {"first": first, "second": second}.get(link, link)
        self.now = max(self.now, self.ready[c]) + 0.1
        if link is not None:
            begin = max(self.now, self.links[link])
            self.links[link] = begin + span - 1.0
            self.ready[c] = begin + span
        self.stage[c] = stage + 1
        return (stage, c)

    def tick(self, spent):
        self.now += spent
        events = []
        progress = True
        while progress:
            progress = False
            for c in self.stage:
                if self.stage[c] < 5 and self.ready[c] <= self.now:
                    events.append(self.emit(c))
                    progress = True
        return events

    def until(self, c):
        events = []
        while self.stage[c] < 5:
            choices = [i for i in self.stage if self.stage[i] < 5]
            best = min(choices, key=lambda i: (self.ready[i], i))
            events.append(self.emit(best))
        return events


def gelu_parts(u):
    share = 0.5 + 0.5 * lax.erf(u * math.sqrt(0.5))
    bell = jnp.exp(-0.5 * u * u) * (1.0 / math.sqrt(2.0 * math.pi))
    return u * share, share + u * bell


def norm_parts(values):
    centred = values - jnp.mean(values, axis=1, keepdims=True)
    spread = jnp.mean(centred * centred, axis=1, keepdims=True)
    scale = lax.rsqrt(spread + NORM_EPS)
    return centred * scale, scale


def forward_kernel(
    lengths_ref,
    x_ref,
    qkv_ref,
    piece_ref,
    e_ref,
    cot_ref,
    par,
    full_ref,
    q_out,
    k_out,
    v_out,
    o_out,
    lse_out,
    cq_out,
    ck_out,
    cv_out,
    oc_out,
    lse_cross_out,
    r1_out,
    r2_out,
    h1_out,
    h2_out,
    g_out,
    gp_out,
    y_out,
    dm_out,
    d_third_out,
    small_out,
    pool,
    acc,
    held,
    o_t,
    lse_held,
    states,
    load_sem,
    store_sem,
    state_sem,
    acc_sem,
    *gather_sem,
):
    places = neighbours()
    refs = (piece_ref, full_ref) + gather_sem
    planner = GatherPlanner(GATHERED)
    length = lengths_ref[0]

    def emit_all(events):
        for stage, c in events:
            gather_stage(stage, refs, c, c % 2, places)

    def tick(spent):
        emit_all(planner.tick(spent))

    def load(slot, source):
        return pltpu.make_async_copy(source, pool.at[slot], load_sem.at[slot])

    def store(slot, target):
        return pltpu.make_async_copy(pool.at[slot], target, store_sem.at[slot])

    def product_into(left, right, put):
        def body(i, carry):
            n = pl.multiple_of(i * 256, 256)
            put(n, product(left(), pool[right, :, pl.ds(n, 256)]))
            return carry

        lax.fori_loop(0, 4, body, 0)

    def row(index, n):
        return par[index : index + 1, pl.ds(n, 256)]

    def put_low(slot, offset=None, scale=None):
        def put(n, value):
            if offset is not None:
                value = value + row(offset, n)
            if scale is not None:
                value = value * scale
            pool[slot, :, pl.ds(n, 256)] = value.astype(jnp.bfloat16)

        return put

    def put_acc(offset):
        def put(n, value):
            acc[:, pl.ds(n, 256)] = value + row(offset, n)

        return put

    def load_weight(c, slot):
        target = pool.at[slot].reshape(4, 256, D)
        return pltpu.make_async_copy(full_ref.at[c], target, load_sem.at[slot])

    def weight(c, slot):
        emit_all(planner.until(c))
        return load_weight(c, slot)

    def attend_loop(causal, step, valid, query, key, value, out, spent):
        ahead = [planner.tick(spent) for _ in range(8)]

        def body(i, carry):
            lanes = pl.ds(pl.multiple_of(i * 128, 128), 128)
            attend_pair(
                causal,
                step,
                valid,
                query.at[:, lanes],
                key.at[:, lanes],
                value.at[:, lanes],
                out.at[:, lanes],
                lse_held.at[pl.ds(i, 1)],
                o_t,
            )
            for n in range(8):
                if ahead[n]:

                    @pl.when(i == n)
                    def _(events=ahead[n]):
                        emit_all(events)

            return carry

        lax.fori_loop(0, 8, body, 0)

    TILE = 128

    def over_rows(sums, body):
        zero = jnp.zeros((8, D), jnp.float32)

        def step(i, carry):
            r = pl.multiple_of(i * TILE, TILE)
            place = half_lanes((TILE, 1), 0) + r
            usable = (place < length).astype(jnp.float32)
            terms = body(pl.ds(r, TILE), usable)
            return tuple(c + fold(t) for c, t in zip(carry, terms))

        totals = lax.fori_loop(0, D // TILE, step, (zero,) * sums)
        return [jnp.sum(t, axis=0, keepdims=True) for t in totals]

    lane = half_lanes((1, D), 1)

    def square_at(index, total):
        small_out[17:18, :] += jnp.where(lane == index, jnp.sum(total), 0.0)

    greet(list(places[4:7]) + places[7])
    load(0, x_ref).start()
    for i in range(3):
        load(1 + i, qkv_ref.at[i]).start()
    e_load = pltpu.make_async_copy(e_ref, states.at[2], state_sem.at[2])
    e_load.start()
    small_out[...] = jnp.zeros_like(small_out)
    tick(0.5)
    load(0, x_ref).wait()
    load(1, qkv_ref.at[0]).wait()
    product_into(lambda: pool[0], 1, put_low(4, 0, 0.125))
    store(4, q_out).start()
    tick(2.5)
    load(2, qkv_ref.at[1]).wait()
    product_into(lambda: pool[0], 2, put_low(5))
    store(5, k_out).start()
    tick(2.5)
    load(3, qkv_ref.at[2]).wait()
    product_into(lambda: pool[0], 3, put_low(6, 1))
    store(6, v_out).start()
    tick(2.5)

    attend_loop(True, 256, length, pool.at[4], pool.at[5], pool.at[6], pool.at[7], 4.8)
    store(7, o_out).start()
    lse_copy = pltpu.make_async_copy(lse_held, lse_out, state_sem.at[3])
    lse_copy.start()
    w_copy = weight(0, 1)
    w_copy.start()
    w_copy.wait()
    product_into(lambda: pool[7], 1, put_acc(2))
    tick(2.5)
    store(4, q_out).wait()

    def first_norm(rows, usable):
        x = pool[0, rows, :].astype(jnp.float32)
        a = acc[rows, :]
        total = x + a
        acc[rows, :] = total
        h = norm_parts(total)[0] * par[11:12, :] + par[12:13, :]
        held[rows, :] = h
        pool[4, rows, :] = h.astype(jnp.bfloat16)
        return usable * x * x, usable * a * a, usable * h * h

    for index, total in enumerate(over_rows(3, first_norm)):
        square_at(index, total)
    store(4, h1_out).start()
    r1_copy = pltpu.make_async_copy(acc, r1_out, acc_sem.at[0])
    r1_copy.start()
    tick(4.0)

    for c, slot in ((1, 2), (2, 3), (3, 1)):
        weight(c, slot).start()
    store(5, k_out).wait()
    load_weight(1, 2).wait()
    product_into(lambda: pool[4], 2, put_low(5, 3, 0.125))
    store(5, cq_out).start()
    w_copy = weight(4, 2)
    w_copy.start()
    tick(2.5)
    e_load.wait()
    load_weight(2, 3).wait()
    load_weight(3, 1).wait()

    def put_keys(n, value):
        states[0, :, pl.ds(n, 256)] = value.astype(jnp.bfloat16)

    def put_values(n, value):
        states[1, :, pl.ds(n, 256)] = (value + row(4, n)).astype(jnp.bfloat16)

    product_into(lambda: states[2], 3, put_keys)
    product_into(lambda: states[2], 1, put_values)
    state_stores = [
        pltpu.make_async_copy(states.at[0], ck_out, state_sem.at[0]),
        pltpu.make_async_copy(states.at[1], cv_out, state_sem.at[1]),
    ]
    for copy in state_stores:
        copy.start()
    tick(1.0)
    store(6, v_out).wait()
    lse_copy.wait()
    attend_loop(
        False, 512, lengths_ref[1], pool.at[5], states.at[0], states.at[1], pool.at[6], 1.6
    )
    store(6, oc_out).start()
    lse_copy = pltpu.make_async_copy(lse_held, lse_cross_out, state_sem.at[3])
    lse_copy.start()
    w_copy.wait()
    r1_copy.wait()
    product_into(lambda: pool[6], 2, put_acc(5))
    tick(2.5)
    weight(5, 0).start()
    weight(6, 2).start()
    store(7, o_out).wait()

    def second_norm(rows, usable):
        c = acc[rows, :]
        total = held[rows, :] + c
        acc[rows, :] = total
        h = norm_parts(total)[0] * par[13:14, :] + par[14:15, :]
        held[rows, :] = h
        pool[7, rows, :] = h.astype(jnp.bfloat16)
        return usable * c * c, usable * h * h

    for index, total in enumerate(over_rows(2, second_norm)):
        square_at(3 + index, total)
    store(7, h2_out).start()
    r2_copy = pltpu.make_async_copy(acc, r2_out, acc_sem.at[0])
    r2_copy.start()
    tick(4.0)

    store(4, h1_out).wait()
    store(5, cq_out).wait()
    for j in range(4):
        if j > 0:
            store(4, g_out.at[j - 1]).wait()
            store(5, gp_out.at[j - 1]).wait()
        load_weight(5 + 2 * j, j % 2).wait()

        def put_gelu(n, value, j=j):
            g, slope = gelu_parts(value + row(6 + j, n))
            pool[4, :, pl.ds(n, 256)] = g.astype(jnp.bfloat16)
            pool[5, :, pl.ds(n, 256)] = slope.astype(jnp.bfloat16)

        product_into(lambda: pool[7], j % 2, put_gelu)
        store(4, g_out.at[j]).start()
        store(5, gp_out.at[j]).start()
        tick(9.0)
        if j < 3:
            weight(7 + 2 * j, (j + 1) % 2).start()
            weight(8 + 2 * j, 2 + (j + 1) % 2).start()
        load_weight(6 + 2 * j, 2 + j % 2).wait()
        if j == 0:
            r2_copy.wait()
            product_into(lambda: pool[4], 2, put_acc(10))
        else:

            def put_more(n, value):
                acc[:, pl.ds(n, 256)] += value

            product_into(lambda: pool[4], 2 + j % 2, put_more)
        tick(2.5)
        if j == 3:
            store(6, oc_out).wait()
            load(6, cot_ref).start()

    load(6, cot_ref).wait()

    def third_norm(rows, usable):
        m = acc[rows, :]
        unit, scale = norm_parts(held[rows, :] + m)
        gain = par[15:16, :]
        pool[0, rows, :] = (unit * gain + par[16:17, :]).astype(jnp.bfloat16)
        grad = pool[6, rows, :].astype(jnp.float32) * usable
        inner = grad * gain
        first = jnp.mean(inner, axis=1, keepdims=True)
        second = jnp.mean(inner * unit, axis=1, keepdims=True)
        back = scale * (inner - first - unit * second)
        acc[rows, :] = back
        low = back.astype(jnp.bfloat16)
        pool[1, rows, :] = low
        return usable * m * m, grad * unit, grad, low.astype(jnp.float32)

    m_total, gain_sum, shift_sum, offset_sum = over_rows(4, third_norm)
    square_at(5, m_total)
    small_out[15:16, :] = gain_sum
    small_out[16:17, :] = shift_sum
    small_out[10:11, :] = offset_sum
    last = [
        store(0, y_out),
        store(1, dm_out),
        pltpu.make_async_copy(acc, d_third_out, acc_sem.at[0]),
    ]
    for copy in last:
        copy.start()
    for c in range(GATHERED):
        emit_all(planner.until(c))
    for copy in last + state_stores + [lse_copy]:
        copy.wait()
    store(7, h2_out).wait()
    store(4, g_out.at[3]).wait()
    store(5, gp_out.at[3]).wait()


def forward(lengths, x, qkv_full, pieces, states, cotangent, params):
    any_space = pl.BlockSpec(memory_space=pl.ANY)
    vmem = pl.BlockSpec(memory_space=pltpu.VMEM)
    shape = jax.ShapeDtypeStruct
    dma = pltpu.SemaphoreType.DMA
    low = jnp.bfloat16
    wide = jnp.float32
    square = shape((1024, D), low)
    square_wide = shape((1024, D), wide)
    lse = shape((8, 8, 1024), wide)
    short = shape((128, D), low)
    blocks = shape((4, 1024, D), low)
    outs = (
        shape((GATHERED, 4, 256, D), low),
        square,
        square,
        square,
        square,
        lse,
        square,
        short,
        short,
        square,
        lse,
        square_wide,
        square_wide,
        square,
        square,
        blocks,
        blocks,
        square,
        square,
        square_wide,
        shape((24, D), wide),
    )
    return pl.pallas_call(
        forward_kernel,
        out_shape=outs,
        in_specs=[SCALARS] + [any_space] * 5 + [vmem],
        out_specs=(any_space,) * 20 + (vmem,),
        scratch_shapes=[
            pltpu.VMEM((POOL, 1024, D), low),
            pltpu.VMEM((1024, D), wide),
            pltpu.VMEM((1024, D), wide),
            pltpu.VMEM((128, 1024), wide),
            pltpu.VMEM((8, 8, 1024), wide),
            pltpu.VMEM((3, 128, D), low),
            dma((POOL,)),
            dma((POOL,)),
            dma((4,)),
            dma((1,)),
        ]
        + gather_sems(GATHERED),
        compiler_params=pltpu.CompilerParams(
            collective_id=3, has_side_effects=True, vmem_limit_bytes=56 * MIB
        ),
    )(lengths, x, qkv_full, pieces, states, cotangent, params)


def add_blocks(target, first, second, planes, rows, step):
    per_plane = rows // step

    def body(i, carry):
        s = i // per_plane
        r = pl.multiple_of((i % per_plane) * step, step)
        total = first(s, r).astype(jnp.float32) + second(s, r).astype(jnp.float32)
        target(s, r, total.astype(jnp.bfloat16))
        return carry

    lax.fori_loop(0, planes * per_plane, body, 0)


POOL = 8
G_SLOTS = 3
R_SLOTS = 4
PLAN = {"core": 3.0, "load": 1.5, "a": 11.5, "b": 6.5, "z": 6.5, "bb": 2.5, "ba": 4.0, "bc": 2.0}


class Planner:
    def __init__(self):
        self.now = 0.0
        self.links = {"core": 0.0, "x": 0.0, "y": 0.0, "z": 0.0, "load": 0.0}
        self.stage = {}
        self.ready = {}

    def link_of(self, c, stage):
        first, second = ("x", "y") if c % 2 == 0 else ("y", "x")
        return {
            0: ("core", "core"),
            1: ("load", "load"),
            2: (first, "a"),
            3: (second, "b"),
            4: ("z", "z"),
            5: (second, "bb"),
            6: (first, "ba"),
            7: ("core", "bc"),
            8: (None, None),
        }[stage]

    def can(self, c):
        stage = self.stage[c]
        if stage > 8:
            return False
        if stage == 1 and c >= R_SLOTS and self.stage[c - R_SLOTS] <= 3:
            return False
        return True

    def emit(self, c):
        stage = self.stage[c]
        link, kind = self.link_of(c, stage)
        self.now = max(self.now, self.ready[c]) + {2: 1.2, 3: 0.7, 4: 0.4, 5: 0.2}.get(stage, 0.1)
        if link is not None:
            begin = max(self.now, self.links[link])
            span = PLAN[kind]
            self.links[link] = begin + span - 1.0
            self.ready[c] = begin + span
        self.stage[c] = stage + 1
        return (stage, c)

    def tick(self, spent):
        self.now += spent
        events = []
        progress = True
        while progress:
            progress = False
            for c in sorted(self.stage):
                if self.can(c) and self.ready[c] <= self.now:
                    events.append(self.emit(c))
                    progress = True
        return events

    def produce(self, c):
        self.stage[c] = 0
        self.ready[c] = self.now
        return [self.emit(c)]

    def until(self, done):
        events = []
        while not done():
            choices = [c for c in sorted(self.stage) if self.can(c)]
            c = min(choices, key=lambda i: (self.ready[i], i))
            events.append(self.emit(c))
        return events

    def free_slot(self, c):
        before = c - G_SLOTS
        if before < 0:
            return []
        return self.until(lambda: self.stage[before] > 2)

    def drain(self):
        return self.until(lambda: all(s > 8 for s in self.stage.values()))


def backward_kernel(
    lengths_ref,
    dm_ref,
    d_third_ref,
    g_ref,
    gp_ref,
    rest_ref,
    qkv_ref,
    h2_ref,
    h1_ref,
    x_in_ref,
    e_ref,
    oc_ref,
    o_ref,
    r1_ref,
    r2_ref,
    q_ref,
    k_ref,
    v_ref,
    cq_ref,
    ck_ref,
    cv_ref,
    lse_ref,
    lse_cross_ref,
    gains_ref,
    small_ref,
    token_grad_ref,
    state_grad_ref,
    out_ref,
    totals_ref,
    half,
    pool,
    acc,
    made,
    summed,
    quarter,
    eighth,
    pieces,
    stream,
    dq_t,
    dk_sum,
    dv_sum,
    lse_held,
    states,
    states_t,
    small,
    small_in,
    small_sum,
    small_z,
    load_sem,
    stream_sem,
    state_sem,
    half_sem,
    send_sem,
    recv_sem,
    z_send_sem,
    z_recv_sem,
    place_sem,
    small_send_sem,
    small_recv_sem,
):
    core, x, y, z, other_core, other_x, other_y, others_z = neighbours()
    kept = pl.multiple_of(core * 128, 128)
    given = pl.multiple_of(128 - core * 128, 128)
    planner = Planner()
    place_of = (12, 8, 13, 9, 14, 10, 15, 11, 7, 4, 5, 6, 3, 0, 1, 2)

    def axes(c):
        if c % 2 == 0:
            return x, y, other_x, other_y
        return y, x, other_y, other_x

    def core_copy(c):
        source = made.at[c % G_SLOTS, :, pl.ds(given, 128), :]
        return remote(source, half.at[c], send_sem.at[0, c], recv_sem.at[0, c], other_core)

    def half_copy(c):
        return pltpu.make_async_copy(
            half.at[c], summed.at[c % R_SLOTS], half_sem.at[c % R_SLOTS]
        )

    def first_copy(c):
        a, b, first, second = axes(c)
        rows = pl.ds(pl.multiple_of(64 - a * 64, 64), 64)
        source = summed.at[c % R_SLOTS, :, rows, :]
        return remote(source, quarter.at[c], send_sem.at[1, c], recv_sem.at[1, c], first)

    def second_copy(c):
        a, b, first, second = axes(c)
        rows = pl.ds(pl.multiple_of(32 - b * 32, 32), 32)
        source = quarter.at[c, :, rows, :]
        return remote(source, eighth.at[c], send_sem.at[2, c], recv_sem.at[2, c], second)

    def z_copy(c, d):
        device = others_z[d]
        return remote(
            eighth.at[c, device[1]],
            pieces.at[c, d],
            z_send_sem.at[c, d],
            z_recv_sem.at[c, d],
            device,
        )

    def own_rows_of(c):
        a, b, first, second = axes(c)
        return pl.ds(pl.multiple_of(core * 128 + a * 64 + b * 32, 32), 32)

    def place_copy(c):
        return pltpu.make_async_copy(
            pieces.at[c, 0], out_ref.at[place_of[c], own_rows_of(c), :], place_sem.at[c]
        )

    def back_second(c):
        device = axes(c)[3]
        target = out_ref.at[place_of[c], own_rows_of(c), :]
        return remote(pieces.at[c, 0], target, send_sem.at[3, c], recv_sem.at[3, c], device)

    def back_first(c):
        a, b, first, second = axes(c)
        block = out_ref.at[place_of[c], pl.ds(pl.multiple_of(core * 128 + a * 64, 64), 64), :]
        return remote(block, block, send_sem.at[4, c], recv_sem.at[4, c], first)

    def back_core(c):
        block = out_ref.at[place_of[c], pl.ds(kept, 128), :]
        return remote(block, block, send_sem.at[5, c], recv_sem.at[5, c], other_core)

    def emit(stage, c):
        a, b, first, second = axes(c)
        slot = c % R_SLOTS
        if stage == 0:
            core_copy(c).start()
        if stage == 1:
            if c >= R_SLOTS:
                first_copy(c - R_SLOTS).wait_send()
            core_copy(c).wait_recv()
            half_copy(c).start()
        if stage == 2:
            half_copy(c).wait()

            def put(s, r, value):
                summed[slot, s, pl.ds(r, 32), :] = value

            add_blocks(
                put,
                lambda s, r: summed[slot, s, pl.ds(r, 32), :],
                lambda s, r: made[c % G_SLOTS, s, pl.ds(pl.multiple_of(kept + r, 32), 32), :],
                4,
                128,
                32,
            )
            first_copy(c).start()
            core_copy(c).wait_send()
        if stage == 3:
            first_copy(c).wait_recv()

            def put(s, r, value):
                quarter[c, s, pl.ds(r, 32), :] = value

            add_blocks(
                put,
                lambda s, r: quarter[c, s, pl.ds(r, 32), :],
                lambda s, r: summed[slot, s, pl.ds(pl.multiple_of(a * 64 + r, 32), 32), :],
                4,
                64,
                32,
            )
            second_copy(c).start()
        if stage == 4:
            second_copy(c).wait_recv()

            def put(s, r, value):
                eighth[c, s, pl.ds(r, 32), :] = value

            add_blocks(
                put,
                lambda s, r: eighth[c, s, pl.ds(r, 32), :],
                lambda s, r: quarter[c, s, pl.ds(pl.multiple_of(b * 32 + r, 32), 32), :],
                4,
                32,
                32,
            )
            for d in range(3):
                z_copy(c, d).start()
        if stage == 5:
            for d in range(3):
                z_copy(c, d).wait_recv()
            total = eighth[c, z].astype(jnp.float32)
            for d in range(3):
                total = total + pieces[c, d].astype(jnp.float32)
            pieces[c, 0] = total.astype(jnp.bfloat16)
            back_second(c).start()
            place_copy(c).start()
        if stage == 6:
            place_copy(c).wait()
            back_second(c).wait_recv()
            back_first(c).start()
        if stage == 7:
            back_first(c).wait_recv()
            back_core(c).start()
        if stage == 8:
            back_core(c).wait()
            back_first(c).wait_send()
            back_second(c).wait_send()
            for d in range(3):
                z_copy(c, d).wait_send()
            second_copy(c).wait_send()
            if c >= CHUNKS - R_SLOTS:
                first_copy(c).wait_send()

    def emit_all(events):
        for stage, c in events:
            emit(stage, c)

    def tick(spent):
        emit_all(planner.tick(spent))

    def produced(c, spent):
        planner.now += spent
        emit_all(planner.produce(c))
        emit_all(planner.tick(0.0))

    def load(slot, source):
        return pltpu.make_async_copy(source, pool.at[slot], load_sem.at[slot])

    def state_load(index, source):
        return pltpu.make_async_copy(source, states.at[index], state_sem.at[index])

    def transpose_into(target, source):
        def body(i, carry):
            r = pl.multiple_of(i * 256, 256)
            pool[target, pl.ds(r, 256), :] = pool[source, :, pl.ds(r, 256)].T
            return carry

        lax.fori_loop(0, 4, body, 0)

    def product_nn(left, right, put):
        def body(i, carry):
            n = pl.multiple_of(i * 256, 256)
            put(n, product(left(), right(n)))
            return carry

        lax.fori_loop(0, 4, body, 0)

    def product_nt(left, right, put):
        def body(i, carry):
            n = pl.multiple_of(i * 256, 256)
            put(
                n,
                lax.dot_general(
                    left(),
                    right(n),
                    (((1,), (1,)), ((), ())),
                    preferred_element_type=jnp.float32,
                ),
            )
            return carry

        lax.fori_loop(0, 4, body, 0)

    def columns_of(slot):
        return lambda n: pool[slot, :, pl.ds(n, 256)]

    def rows_of(slot):
        return lambda n: pool[slot, pl.ds(n, 256), :]

    def weight_grad(slot_in_made, left, right):
        def put(n, value):
            low = value.astype(jnp.bfloat16).reshape(4, 256, 256)
            made[slot_in_made, :, :, pl.ds(n, 256)] = low

        product_nn(left, right, put)

    def add_to_acc(n, value):
        acc[:, pl.ds(n, 256)] += value

    def put_in(slot):
        def put(n, value):
            pool[slot, :, pl.ds(n, 256)] = value.astype(jnp.bfloat16)

        return put

    def norm_back(source, gain_row, gain_at, shift_at, offset_at, target):
        tiles = 8
        rows = 1024 // tiles

        def fetch(i):
            place = pl.ds(pl.multiple_of(i * rows, rows), rows)
            return pltpu.make_async_copy(
                source.at[place, :], stream.at[i % 2], stream_sem.at[i % 2]
            )

        fetch(0).start()

        def body(i, carry):
            gain_sum, shift_sum, offset_sum = carry

            @pl.when(i + 1 < tiles)
            def _():
                fetch(i + 1).start()

            fetch(i).wait()
            r = pl.multiple_of(i * rows, rows)
            values = stream[i % 2]
            centred = values - jnp.mean(values, axis=1, keepdims=True)
            spread = jnp.mean(centred * centred, axis=1, keepdims=True)
            scale = lax.rsqrt(spread + NORM_EPS)
            unit = centred * scale
            grad = acc[pl.ds(r, rows), :]
            inner = grad * gains_ref[gain_row : gain_row + 1, :]
            first = jnp.mean(inner, axis=1, keepdims=True)
            second = jnp.mean(inner * unit, axis=1, keepdims=True)
            back = scale * (inner - first - unit * second)
            acc[pl.ds(r, rows), :] = back
            low = back.astype(jnp.bfloat16)
            pool[target, pl.ds(r, rows), :] = low
            return (
                gain_sum + fold(grad * unit),
                shift_sum + fold(grad),
                offset_sum + fold(low.astype(jnp.float32)),
            )

        zero = jnp.zeros((8, D), jnp.float32)
        sums = lax.fori_loop(0, tiles, body, (zero, zero, zero))
        for row, value in zip((gain_at, shift_at, offset_at), sums):
            small[row : row + 1, :] = jnp.sum(value, axis=0, keepdims=True)

    greet([other_core, other_x, other_y] + others_z)
    load(0, dm_ref).start()
    load(6, h2_ref).start()
    load(2, rest_ref.at[6]).start()
    load(3, gp_ref.at[0]).start()
    load(4, g_ref.at[0]).start()
    load(5, rest_ref.at[5]).start()
    acc_load = pltpu.make_async_copy(d_third_ref, acc, place_sem.at[0])
    acc_load.start()
    small[...] = small_ref[...]
    load(6, h2_ref).wait()
    transpose_into(1, 6)
    load(0, dm_ref).wait()
    acc_load.wait()

    planner.now = 4.0
    plan = []
    for j in range(4):
        entry = []
        planner.now += 3.5
        entry.append(planner.tick(0.0) + planner.free_slot(2 * j))
        planner.now += 4.0
        entry.append(planner.produce(2 * j) + planner.tick(0.0) + planner.free_slot(2 * j + 1))
        planner.now += 2.5
        entry.append(planner.produce(2 * j + 1) + planner.tick(0.0))
        entry.append(planner.tick(2.5))
        plan.append(entry)

    def emit_planned(j, place):
        for n in range(4):
            events = plan[n][place]
            if events:

                @pl.when(j == n)
                def _(events=events):
                    emit_all(events)

    def block(j, carry):
        last = j == 3
        load(2, rest_ref.at[6]).wait()
        load(3, gp_ref.at[0]).wait()

        def put_pre(n, value):
            low = (value * pool[3, :, pl.ds(n, 256)].astype(jnp.float32)).astype(jnp.bfloat16)
            pool[7, :, pl.ds(n, 256)] = low
            small[pl.ds(6 + j, 1), pl.ds(n, 256)] = jnp.sum(
                low.astype(jnp.float32), axis=0, keepdims=True
            )

        product_nt(lambda: pool[0], rows_of(2), put_pre)

        @pl.when(jnp.logical_not(last))
        def _():
            load(2, rest_ref.at[8 + 2 * j]).start()
            load(3, gp_ref.at[j + 1]).start()

        @pl.when(last)
        def _():
            load(2, rest_ref.at[4]).start()
            load(3, cq_ref).start()

        emit_planned(j, 0)
        load(4, g_ref.at[0]).wait()
        transpose_into(6, 4)

        @pl.when(jnp.logical_not(last))
        def _():
            load(4, g_ref.at[j + 1]).start()

        @pl.when(last)
        def _():
            load(4, oc_ref).start()

        weight_grad((2 * j) % G_SLOTS, lambda: pool[6], columns_of(0))
        emit_planned(j, 1)
        weight_grad((2 * j + 1) % G_SLOTS, lambda: pool[1], columns_of(7))
        emit_planned(j, 2)
        load(5, rest_ref.at[5]).wait()
        product_nt(lambda: pool[7], rows_of(5), add_to_acc)

        @pl.when(jnp.logical_not(last))
        def _():
            load(5, rest_ref.at[7 + 2 * j]).start()

        @pl.when(last)
        def _():
            load(5, rest_ref.at[1]).start()

        emit_planned(j, 3)
        return carry

    lax.fori_loop(0, 4, block, 0)

    load(7, h1_ref).start()
    state_loads = [state_load(0, ck_ref), state_load(1, cv_ref), state_load(2, e_ref)]
    for copy in state_loads:
        copy.start()
    lse_load = pltpu.make_async_copy(lse_cross_ref, lse_held, state_sem.at[3])
    lse_load.start()
    norm_back(r2_ref, 1, 13, 14, 5, 0)
    tick(4.0)
    load(4, oc_ref).wait()
    transpose_into(6, 4)
    emit_all(planner.free_slot(8))
    weight_grad(8 % G_SLOTS, lambda: pool[6], columns_of(0))
    produced(8, 4.0)
    load(2, rest_ref.at[4]).wait()
    product_nt(lambda: pool[0], rows_of(2), put_in(4))
    load(2, rest_ref.at[0]).start()
    load(6, o_ref).start()
    tick(2.5)
    load(3, cq_ref).wait()
    for copy in state_loads:
        copy.wait()
    lse_load.wait()

    def attend_loop(causal, step, length, query, key, value, grad, rows, spent):
        ahead = [planner.tick(spent) for _ in range(8)]

        def body(i, carry):
            lanes = pl.ds(pl.multiple_of(i * 128, 128), 128)

            def sums(dq, dv):
                small[rows[0] : rows[0] + 1, lanes] = dq
                small[rows[1] : rows[1] + 1, lanes] = dv

            attend_back_pair(
                causal,
                step,
                length,
                query.at[:, lanes],
                key.at[:, lanes],
                value.at[:, lanes],
                grad.at[:, lanes],
                lse_held.at[pl.ds(i, 1)],
                query.at[:, lanes],
                key.at[:, lanes],
                value.at[:, lanes],
                sums,
                dq_t,
                dk_sum,
                dv_sum,
            )
            for n in range(8):
                if ahead[n]:

                    @pl.when(i == n)
                    def _(events=ahead[n]):
                        emit_all(events)

            return carry

        lax.fori_loop(0, 8, body, 0)

    attend_loop(
        False,
        512,
        lengths_ref[1],
        pool.at[3],
        states.at[0],
        states.at[1],
        pool.at[4],
        (3, 4),
        2.0,
    )
    lse_load = pltpu.make_async_copy(lse_ref, lse_held, state_sem.at[3])
    lse_load.start()
    load(7, h1_ref).wait()
    transpose_into(1, 7)
    load(7, rest_ref.at[2]).start()
    emit_all(planner.free_slot(9))
    weight_grad(9 % G_SLOTS, lambda: pool[1], columns_of(3))
    produced(9, 4.0)
    load(5, rest_ref.at[1]).wait()
    product_nt(lambda: pool[3], rows_of(5), add_to_acc)
    load(5, rest_ref.at[3]).start()
    load(3, q_ref).start()
    tick(2.5)
    states_t[...] = states[2].T
    for c, index in ((10, 0), (11, 1)):
        emit_all(planner.free_slot(c))
        weight_grad(
            c % G_SLOTS, lambda: states_t[...], lambda n, i=index: states[i, :, pl.ds(n, 256)]
        )
        produced(c, 1.0)
    load(7, rest_ref.at[2]).wait()
    load(5, rest_ref.at[3]).wait()

    def state_part(n):
        dims = (((1,), (1,)), ((), ()))
        return lax.dot_general(
            states[0], pool[7, pl.ds(n, 256), :], dims, preferred_element_type=jnp.float32
        ) + lax.dot_general(
            states[1], pool[5, pl.ds(n, 256), :], dims, preferred_element_type=jnp.float32
        )

    def put_state(i, carry):
        n = pl.multiple_of(i * 256, 256)
        state_grad_ref[:, pl.ds(n, 256)] = state_part(n).astype(jnp.bfloat16)
        return carry

    lax.fori_loop(0, 4, put_state, 0)
    load(5, k_ref).start()
    load(7, v_ref).start()
    tick(1.0)

    norm_back(r1_ref, 0, 11, 12, 2, 0)
    tick(4.0)
    load(6, o_ref).wait()
    transpose_into(1, 6)
    load(6, x_in_ref).start()
    emit_all(planner.free_slot(12))
    weight_grad(12 % G_SLOTS, lambda: pool[1], columns_of(0))
    produced(12, 4.0)
    load(1, qkv_ref.at[0]).start()
    load(2, rest_ref.at[0]).wait()
    product_nt(lambda: pool[0], rows_of(2), put_in(4))
    load(2, qkv_ref.at[1]).start()
    tick(2.5)
    load(6, x_in_ref).wait()
    transpose_into(0, 6)
    load(6, qkv_ref.at[2]).start()
    load(3, q_ref).wait()
    load(5, k_ref).wait()
    load(7, v_ref).wait()
    lse_load.wait()
    tick(1.5)
    attend_loop(
        True, 256, lengths_ref[0], pool.at[3], pool.at[5], pool.at[7], pool.at[4], (0, 1), 5.0
    )

    def small_copy(k):
        source = small if k == 0 else small_sum.at[k - 1]
        device = (other_core, other_x, other_y)[k]
        return remote(source, small_in.at[k], small_send_sem.at[k], small_recv_sem.at[k], device)

    def small_z_copy(d):
        return remote(
            small_sum.at[2],
            small_z.at[z],
            small_send_sem.at[3 + d],
            small_recv_sem.at[3 + d],
            others_z[d],
        )

    def small_step(k):
        small_copy(k).wait()
        before = small[...] if k == 0 else small_sum[k - 1]
        small_sum[k] = before + small_in[k]
        if k < 2:
            small_copy(k + 1).start()
        else:
            small_z[z] = small_sum[2]
            for d in range(3):
                small_z_copy(d).start()

    small_copy(0).start()
    for i, (c, slot) in enumerate(((13, 3), (14, 5), (15, 7))):
        emit_all(planner.free_slot(c))
        weight_grad(c % G_SLOTS, lambda: pool[0], columns_of(slot))
        produced(c, 2.5)
        small_step(i)
    load(1, qkv_ref.at[0]).wait()
    product_nt(lambda: pool[3], rows_of(1), add_to_acc)
    tick(2.5)
    load(2, qkv_ref.at[1]).wait()
    product_nt(lambda: pool[5], rows_of(2), add_to_acc)
    tick(2.5)
    for d in range(3):
        small_z_copy(d).wait()
    totals_ref[...] = (small_z[0] + small_z[1]) + (small_z[2] + small_z[3])
    load(6, qkv_ref.at[2]).wait()

    def put_input(n, value):
        total = acc[:, pl.ds(n, 256)] + value
        pool[4, :, pl.ds(n, 256)] = total.astype(jnp.bfloat16)

    product_nt(lambda: pool[7], rows_of(6), put_input)
    token_copy = pltpu.make_async_copy(pool.at[4], token_grad_ref, load_sem.at[4])
    token_copy.start()
    tick(2.5)
    emit_all(planner.drain())
    token_copy.wait()


def backward(lengths, held, gains, small):
    any_space = pl.BlockSpec(memory_space=pl.ANY)
    vmem = pl.BlockSpec(memory_space=pltpu.VMEM)
    shape = jax.ShapeDtypeStruct
    dma = pltpu.SemaphoreType.DMA
    low = jnp.bfloat16
    wide = jnp.float32
    rows = small.shape[0]
    return pl.pallas_call(
        backward_kernel,
        out_shape=(
            shape((1024, D), low),
            shape((128, D), low),
            shape((CHUNKS, 256, D), low),
            shape(small.shape, wide),
            shape((CHUNKS, 4, 128, D), low),
        ),
        in_specs=[SCALARS] + [any_space] * len(held) + [vmem, vmem],
        out_specs=(any_space, vmem, any_space, vmem, any_space),
        scratch_shapes=[
            pltpu.VMEM((POOL, 1024, D), low),
            pltpu.VMEM((1024, D), wide),
            pltpu.VMEM((G_SLOTS, 4, 256, D), low),
            pltpu.VMEM((R_SLOTS, 4, 128, D), low),
            pltpu.VMEM((CHUNKS, 4, 64, D), low),
            pltpu.VMEM((CHUNKS, 4, 32, D), low),
            pltpu.VMEM((CHUNKS, 3, 32, D), low),
            pltpu.VMEM((2, 128, D), wide),
            pltpu.VMEM((128, 1024), wide),
            pltpu.VMEM((2, 1024, 128), wide),
            pltpu.VMEM((2, 1024, 128), wide),
            pltpu.VMEM((8, 8, 1024), wide),
            pltpu.VMEM((3, 128, D), low),
            pltpu.VMEM((D, 128), low),
            pltpu.VMEM((rows, D), wide),
            pltpu.VMEM((3, rows, D), wide),
            pltpu.VMEM((3, rows, D), wide),
            pltpu.VMEM((4, rows, D), wide),
            dma((POOL,)),
            dma((2,)),
            dma((4,)),
            dma((R_SLOTS,)),
            dma((6, CHUNKS)),
            dma((6, CHUNKS)),
            dma((CHUNKS, 3)),
            dma((CHUNKS, 3)),
            dma((CHUNKS,)),
            dma((6,)),
            dma((6,)),
        ],
        compiler_params=pltpu.CompilerParams(
            collective_id=0, has_side_effects=True, vmem_limit_bytes=62 * MIB
        ),
    )(lengths, *held, gains, small)[0:4]


def line_sum(part, whole, send_sem, recv_sem, z, others_z):
    copies = [
        remote(part, whole.at[z], send_sem.at[d], recv_sem.at[d], others_z[d]) for d in range(3)
    ]
    for copy in copies:
        copy.start()
    whole[z] = part[...]
    for copy in copies:
        copy.wait()
    return (whole[0] + whole[1]) + (whole[2] + whole[3])


def spread_scalar(value):
    return jnp.broadcast_to(value, (1, 128))


def factor_kernel(
    grad_ref,
    att_rows_ref,
    exp_rows_ref,
    shr_rows_ref,
    cols_ref,
    att_rows_out,
    exp_rows_out,
    shr_rows_out,
    cols_out,
    scale_out,
    part,
    whole,
    send_sem,
    recv_sem,
):
    core, x, y, z, other_core, other_x, other_y, others_z = neighbours()
    greet(others_z)
    part[...] = jnp.zeros_like(part)

    def tile(chunk, r, step):
        return grad_ref[chunk, pl.ds(r, step), :].astype(jnp.float32)

    def add(slot, col, weighted):
        part[slot : slot + 1, :] += jnp.sum(col, axis=0, keepdims=True)
        part[16 + slot : 17 + slot, :] += jnp.sum(weighted, axis=0, keepdims=True)

    def scan_rows(chunks, slots, rows_in, rows_out, total_at):
        width = float(len(chunks) * D)
        step = 64 // len(chunks)

        def body(i, carry):
            cols, weights, total = carry
            r = pl.multiple_of(i * step, step)
            squares = [jnp.square(tile(c, r, step)) for c in chunks]
            row_sum = squares[0]
            for square in squares[1:]:
                row_sum = row_sum + square
            row_sum = jnp.sum(row_sum, axis=1, keepdims=True)
            rows = DECAY_RATE * rows_in[pl.ds(r, step), :] + (1.0 - DECAY_RATE) * (
                row_sum / width + FACTOR_EPS
            )
            rows_out[pl.ds(r, step), :] = rows
            inverse = 1.0 / rows
            cols = [c + fold(s) for c, s in zip(cols, squares)]
            weights = [w + fold(s * inverse) for w, s in zip(weights, squares)]
            return cols, weights, total + fold(rows)

        zeros = [jnp.zeros((8, D), jnp.float32) for _ in chunks]
        cols, weights, total = lax.fori_loop(
            0, 256 // step, body, (zeros, zeros, jnp.zeros((8, 1), jnp.float32))
        )
        for slot, col, weighted in zip(slots, cols, weights):
            add(slot, col, weighted)
        row, lane = total_at
        part[row : row + 1, lane : lane + 128] += spread_scalar(jnp.sum(total))

    for i in range(8):
        scan_rows([i], [i], att_rows_ref.at[i], att_rows_out.at[i], (13, 128 * i))
    scan_rows([8, 9, 10, 11], [8, 9, 10, 11], exp_rows_ref, exp_rows_out, (14, 0))
    for i in range(4):
        scan_rows([12 + i], [12], shr_rows_ref.at[i], shr_rows_out.at[i], (14, 128))
    total = line_sum(part, whole, send_sem, recv_sem, z, others_z)
    row_counts = [D] * 12 + [FF]
    means = [total[13:14, 128 * i : 128 * i + 1] / D for i in range(8)]
    means = means + [total[14:15, 0:1] / D] * 4 + [total[14:15, 128:129] / FF]
    cols_new, quotients = [], []
    for slot in range(13):
        new = DECAY_RATE * cols_ref[slot : slot + 1, :] + (1.0 - DECAY_RATE) * (
            total[slot : slot + 1] / row_counts[slot] + FACTOR_EPS
        )
        cols_new.append(new)
        quotients.append(jnp.sum(total[16 + slot : 17 + slot] / new, axis=1, keepdims=True))
        cols_out[slot : slot + 1, :] = new
    expand_quotient = quotients[8] + quotients[9] + quotients[10] + quotients[11]
    for slot in range(13):
        if slot < 8:
            mean_square = means[slot] * quotients[slot] / (D * D)
            rate = STEP_RATE * (OUT_GAIN if slot % 4 == 3 else 1.0)
        else:
            quotient = expand_quotient if slot < 12 else quotients[12]
            mean_square = means[slot] * quotient / (D * FF)
            rate = STEP_RATE
        factor = rate / jnp.maximum(1.0, jnp.sqrt(mean_square) / CLIP_LEVEL)
        scale_out[slot : slot + 1, :] = lax.rsqrt(cols_new[slot] / means[slot]) * factor


def factors(grads, att_rows, exp_rows, shr_rows, cols):
    vmem = pl.BlockSpec(memory_space=pltpu.VMEM)
    shape = jax.ShapeDtypeStruct
    return pl.pallas_call(
        factor_kernel,
        out_shape=(
            shape((8, 256, 1), jnp.float32),
            shape((256, 1), jnp.float32),
            shape((4, 256, 1), jnp.float32),
            shape((16, D), jnp.float32),
            shape((16, D), jnp.float32),
        ),
        in_specs=[vmem] * 5,
        out_specs=(vmem,) * 5,
        scratch_shapes=[
            pltpu.VMEM((32, D), jnp.float32),
            pltpu.VMEM((4, 32, D), jnp.float32),
            pltpu.SemaphoreType.DMA((3,)),
            pltpu.SemaphoreType.DMA((3,)),
        ],
        compiler_params=pltpu.CompilerParams(
            collective_id=1, has_side_effects=True, vmem_limit_bytes=40 * MIB
        ),
    )(grads, att_rows, exp_rows, shr_rows, cols)


def update_attention_kernel(
    grad_ref, weight_ref, rows_ref, scale_ref, grad_out, new_out, copy_out, grads, change
):
    block = grad_ref.shape[1]
    for i in range(8):
        grad = grad_ref[i].astype(jnp.float32)
        scaled = grad * lax.rsqrt(rows_ref[i]) * scale_ref[i : i + 1, :]
        every = pl.ds(i, block, stride=8)
        for lane in range(8):
            columns = slice(lane * 128, lane * 128 + 128)
            grads[lane, every, :] = grad[:, columns]
            change[lane, every, :] = scaled[:, columns]
    for lane in range(8):
        columns = slice(lane * 128, lane * 128 + 128)
        grad_out[:, columns] = grads[lane]
        new = weight_ref[:, columns] - change[lane]
        new_out[:, columns] = new
        copy_out[:, columns] = new.astype(jnp.bfloat16)


def update_attention(grads, weights, rows, scale):
    block = 32
    wide = pl.BlockSpec((block * 8, D), lambda i: (i, 0))
    shape = jax.ShapeDtypeStruct
    new = pl.pallas_call(
        update_attention_kernel,
        grid=(256 // block,),
        out_shape=(
            shape((2048, D), jnp.float32),
            shape((2048, D), jnp.float32),
            shape((2048, D), jnp.bfloat16),
        ),
        in_specs=[
            pl.BlockSpec((8, block, D), lambda i: (0, i, 0)),
            wide,
            pl.BlockSpec((8, block, 1), lambda i: (0, i, 0)),
            pl.BlockSpec((16, D), lambda i: (0, 0)),
        ],
        out_specs=(wide,) * 3,
        scratch_shapes=[pltpu.VMEM((8, block * 8, 128), jnp.float32)] * 2,
        compiler_params=pltpu.CompilerParams(vmem_limit_bytes=40 * MIB),
    )(grads, weights.reshape(2048, D), rows, scale)
    return [t.reshape(256, 8, D) for t in new]


def update_kernel(
    first, slots, grad_ref, weight_ref, rows_ref, scale_ref, grad_out, new_out, copy_out
):
    spans = 4 if slots == 4 else 1
    wide = D // spans
    for i in range(slots):
        grads = grad_ref[i].astype(jnp.float32)
        changes = grads * (lax.rsqrt(rows_ref[...]) * scale_ref[first + i : first + i + 1, :])
        for s in range(spans):
            start = s * D + i * wide
            columns = slice(start, start + wide)
            part = slice(s * wide, s * wide + wide)
            grad_out[:, columns] = grads[:, part]
            new = weight_ref[:, columns] - changes[:, part]
            new_out[:, columns] = new
            copy_out[:, columns] = new.astype(jnp.bfloat16)


def update_plain(grads, weights, rows, scale, first, slots, grad_map):
    count, width = weights.shape
    block = 128 // slots
    wide = pl.BlockSpec((block, width), lambda i: (i, 0))
    shape = jax.ShapeDtypeStruct
    return pl.pallas_call(
        lambda *refs: update_kernel(first, slots, *refs),
        grid=(count // block,),
        out_shape=(
            shape(weights.shape, jnp.float32),
            shape(weights.shape, jnp.float32),
            shape(weights.shape, jnp.bfloat16),
        ),
        in_specs=[
            pl.BlockSpec((slots, block, D), grad_map),
            wide,
            pl.BlockSpec((block, 1), lambda i: (i, 0)),
            pl.BlockSpec((16, D), lambda i: (0, 0)),
        ],
        out_specs=(wide,) * 3,
        compiler_params=pltpu.CompilerParams(vmem_limit_bytes=40 * MIB),
    )(grads, weights, rows, scale)


def update_direct(
    grads,
    attention_weights,
    expand_weight,
    shrink_weight,
    attention_rows,
    attention_cols,
    expand_rows,
    expand_cols,
    shrink_rows,
    shrink_cols,
):
    cols = jnp.concatenate(
        [attention_cols, hidden_blocks(expand_cols), shrink_cols.reshape(1, D), jnp.ones((3, D))]
    )
    att_rows, exp_rows, shr_rows, cols_new, scale = factors(
        grads,
        attention_rows[:, :, None],
        expand_rows[:, None],
        shrink_rows.reshape(4, 256, 1),
        cols,
    )
    shr_rows = shr_rows.reshape(-1, 1)
    attention = update_attention(grads, attention_weights, att_rows, scale)
    expand = update_plain(grads, expand_weight, exp_rows, scale, 8, 4, lambda i: (2, i, 0))
    shrink = update_plain(
        grads, shrink_weight, shr_rows, scale, 12, 1, lambda i: (12 + i // 2, i % 2, 0)
    )
    return (
        attention,
        expand,
        shrink,
        (att_rows[:, :, 0], exp_rows[:, 0], shr_rows[:, 0]),
        (cols_new[0:8], hidden_flat(cols_new[8:12]), cols_new[12]),
    )


def as_rows(vector):
    rows = -(-vector.shape[0] // 1024) * 8
    return jnp.pad(vector, (0, rows * 128 - vector.shape[0])).reshape(rows, 128)


def masked_scores(query_part, key_heads, first_row, valid_count, causal):
    scores = jnp.einsum("qhd,khd->hqk", query_part, key_heads, preferred_element_type=jnp.float32)
    key_places = jnp.arange(key_heads.shape[0], dtype=jnp.int32)[None, :]
    usable = key_places < valid_count
    if causal:
        query_places = first_row + jnp.arange(query_part.shape[0], dtype=jnp.int32)[:, None]
        usable = usable & (key_places <= query_places)
    return jnp.where(usable[None], scores, MASKED)


def attend_forward(queries, key_heads, values, valid_count, causal):
    query_rows = queries.shape[0]
    step_rows = min(512, query_rows)
    outputs, stored = ([], [])
    for b in range(query_rows // step_rows):
        first_row = b * step_rows
        key_end = first_row + step_rows if causal else key_heads.shape[0]
        scores = masked_scores(
            queries[first_row : first_row + step_rows],
            key_heads[:key_end],
            first_row,
            valid_count,
            causal,
        )
        row_max = jnp.max(scores, axis=-1, keepdims=True)
        raised = jnp.exp(scores - row_max)
        totals = jnp.sum(raised, axis=-1, keepdims=True)
        probs_low = (raised / totals).astype(jnp.bfloat16)
        outputs.append(
            jnp.einsum(
                "hqk,khd->qhd", probs_low, values[:key_end], preferred_element_type=jnp.float32
            )
        )
        stored.append(row_max + jnp.log(totals))
    return (jnp.concatenate(outputs, axis=0), stored)


def attend_backward(queries, key_heads, values, grad_out, stored, valid_count, causal):
    query_rows = queries.shape[0]
    key_rows = key_heads.shape[0]
    step_rows = min(512, query_rows)
    grad_queries = []
    grad_keys = jnp.zeros(key_heads.shape, jnp.float32)
    grad_values = jnp.zeros(values.shape, jnp.float32)
    for b in range(query_rows // step_rows):
        first_row = b * step_rows
        key_end = first_row + step_rows if causal else key_rows
        query_part = queries[first_row : first_row + step_rows]
        grad_part = grad_out[first_row : first_row + step_rows]
        scores = masked_scores(query_part, key_heads[:key_end], first_row, valid_count, causal)
        probs = jnp.exp(scores - stored[b])
        probs_low = probs.astype(jnp.bfloat16)
        grad_probs = jnp.einsum(
            "qhd,khd->hqk", grad_part, values[:key_end], preferred_element_type=jnp.float32
        )
        value_part = jnp.einsum(
            "hqk,qhd->khd", probs_low, grad_part, preferred_element_type=jnp.float32
        )
        grad_scores = probs * (grad_probs - jnp.sum(probs * grad_probs, axis=-1, keepdims=True))
        scores_low = grad_scores.astype(jnp.bfloat16)
        grad_queries.append(
            jnp.einsum(
                "hqk,khd->qhd", scores_low, key_heads[:key_end], preferred_element_type=jnp.float32
            )
        )
        key_part = jnp.einsum(
            "hqk,qhd->khd", scores_low, query_part, preferred_element_type=jnp.float32
        )
        padding = ((0, key_rows - key_end), (0, 0), (0, 0))
        grad_keys = grad_keys + jnp.pad(key_part, padding)
        grad_values = grad_values + jnp.pad(value_part, padding)
    return (jnp.concatenate(grad_queries, axis=0), grad_keys, grad_values)


def gather_rows(piece):
    return lax.all_gather(piece, ("shard", "rep"), axis=0, tiled=True)


def own_piece(block, replicas):
    rows = block.shape[0] // replicas
    return lax.dynamic_slice_in_dim(block, lax.axis_index("rep") * rows, rows, axis=0)


def scatter_rows(grad):
    piece = lax.psum_scatter(
        grad.astype(jnp.bfloat16), ("shard", "rep"), scatter_dimension=0, tiled=True
    )
    return lax.all_gather(piece, "rep", axis=0, tiled=True)


def local_factors(grad, rows):
    square = grad * grad
    rows_new = DECAY_RATE * rows + (1.0 - DECAY_RATE) * jnp.mean(square + FACTOR_EPS, axis=-1)
    col_part = jnp.sum(square + FACTOR_EPS, axis=0)
    weighted = jnp.sum(square / rows_new[..., None], axis=0)
    return rows_new, col_part, weighted, jnp.sum(rows_new, axis=0)


def finish_factors(grad, weight, rows_new, cols, col_sum, weighted, row_total, row_count, rate):
    cols_new = DECAY_RATE * cols + (1.0 - DECAY_RATE) * col_sum / row_count
    mean_rows = row_total / row_count
    mean_square = mean_rows * jnp.sum(weighted / cols_new, axis=-1) / (row_count * cols.shape[-1])
    factor = rate / jnp.maximum(1.0, jnp.sqrt(mean_square) / CLIP_LEVEL)
    scaled = lax.rsqrt(cols_new / mean_rows[..., None]) * factor[..., None]
    fresh = weight - grad * (lax.rsqrt(rows_new)[..., None] * scaled[None])
    return fresh, cols_new


def plain_device(
    tokens,
    encoder,
    cotangent,
    lengths,
    encoder_lengths,
    dealt_order,
    attention_weights,
    expand_weight,
    shrink_weight,
    small_params,
    attention_rows,
    attention_cols,
    expand_rows,
    expand_cols,
    shrink_rows,
    shrink_cols,
    small_moment,
):
    devices = lax.axis_size(("rep", "shard"))
    replicas = lax.axis_size("rep")
    shards = lax.axis_size("shard")
    slot_tokens = tokens.shape[0]
    slot_states = encoder.shape[0]
    position = lax.axis_index(("rep", "shard"))
    inverse = (
        jnp.zeros((devices,), jnp.int32).at[dealt_order].set(jnp.arange(devices, dtype=jnp.int32))
    )
    qkv_piece = own_piece(attention_weights[:, 0:3, :].reshape(-1, 3 * D), replicas)
    rest_piece = own_piece(attention_weights[:, 3:8, :].reshape(-1, 5 * D), replicas)
    qkv_full = gather_rows(qkv_piece.astype(jnp.bfloat16))
    rest_full = gather_rows(rest_piece.astype(jnp.bfloat16))
    expand_full = gather_rows(own_piece(expand_weight, replicas).astype(jnp.bfloat16))
    shrink_full = gather_rows(own_piece(shrink_weight, replicas).astype(jnp.bfloat16))
    spread = lax.all_to_all(
        tokens.reshape(devices, slot_tokens // devices, D),
        ("rep", "shard"),
        split_axis=0,
        concat_axis=0,
        tiled=True,
    )
    picked = jnp.take(spread, inverse, axis=0)
    tokens = lax.all_to_all(
        picked, ("rep", "shard"), split_axis=0, concat_axis=0, tiled=True
    ).reshape(slot_tokens, D)
    states = encoder
    incoming = cotangent
    valid_tokens = lengths[position]
    valid_states = encoder_lengths[position]
    matrices = [qkv_full[:, i * D : (i + 1) * D] for i in range(3)] + [
        rest_full[:, i * D : (i + 1) * D] for i in range(5)
    ]
    parts = unpack(small_params)
    token_heads = (slot_tokens, HEADS, HEAD_DIM)
    state_heads = (slot_states, HEADS, HEAD_DIM)
    q_self = ((forward_product(tokens, matrices[0]) + parts[0]) * 0.125).astype(
        jnp.bfloat16
    )
    k_self = forward_product(tokens, matrices[1]).astype(jnp.bfloat16)
    v_self = (forward_product(tokens, matrices[2]) + parts[1]).astype(jnp.bfloat16)
    o_self, lse_self = attend_forward(
        q_self.reshape(token_heads),
        k_self.reshape(token_heads),
        v_self.reshape(token_heads),
        valid_tokens,
        True,
    )
    o_self_low = o_self.reshape(slot_tokens, D).astype(jnp.bfloat16)
    branch_a = forward_product(o_self_low, matrices[3]) + parts[2]
    tokens_wide = tokens.astype(jnp.float32)
    hidden_one, norm_one_back = jax.vjp(layer_norm, tokens_wide + branch_a, parts[8], parts[9])
    hidden_one_low = hidden_one.astype(jnp.bfloat16)
    q_cross = (
        (forward_product(hidden_one_low, matrices[4]) + parts[3]) * 0.125
    ).astype(jnp.bfloat16)
    k_cross = forward_product(states, matrices[5]).astype(jnp.bfloat16)
    v_cross = (forward_product(states, matrices[6]) + parts[4]).astype(jnp.bfloat16)
    o_cross, lse_cross = attend_forward(
        q_cross.reshape(token_heads),
        k_cross.reshape(state_heads),
        v_cross.reshape(state_heads),
        valid_states,
        False,
    )
    o_cross_low = o_cross.reshape(slot_tokens, D).astype(jnp.bfloat16)
    branch_c = forward_product(o_cross_low, matrices[7]) + parts[5]
    hidden_two, norm_two_back = jax.vjp(layer_norm, hidden_one + branch_c, parts[10], parts[11])
    hidden_two_low = hidden_two.astype(jnp.bfloat16)
    pre_act = forward_product(hidden_two_low, expand_full) + parts[6]
    activated, gelu_back = jax.vjp(gelu_exact, pre_act)
    activated_low = activated.astype(jnp.bfloat16)
    branch_m = forward_product(activated_low, shrink_full) + parts[7]
    result, norm_three_back = jax.vjp(layer_norm, hidden_two + branch_m, parts[12], parts[13])
    usable_rows = (jnp.arange(slot_tokens, dtype=jnp.int32) < valid_tokens).astype(jnp.float32)[
        :, None
    ]
    squares = jnp.stack(
        [
            jnp.sum(usable_rows * t * t)
            for t in (tokens_wide, branch_a, hidden_one, branch_c, hidden_two, branch_m)
        ]
    )
    d_third, d_gain_three, d_shift_three = norm_three_back(
        incoming.astype(jnp.float32) * usable_rows
    )
    d_mlp = d_third.astype(jnp.bfloat16)
    grad_shrink = weight_product(activated_low, d_mlp)
    grad_shrink_offset = row_sum(d_mlp)
    d_activated = input_product(d_mlp, shrink_full)
    d_pre = gelu_back(d_activated)[0].astype(jnp.bfloat16)
    grad_expand = weight_product(hidden_two_low, d_pre)
    grad_expand_offset = row_sum(d_pre)
    d_hidden_two = d_third + input_product(d_pre, expand_full)
    d_second, d_gain_two, d_shift_two = norm_two_back(d_hidden_two)
    d_branch_c = d_second.astype(jnp.bfloat16)
    grad_cross_out = weight_product(o_cross_low, d_branch_c)
    grad_cross_out_offset = row_sum(d_branch_c)
    d_o_cross = input_product(d_branch_c, matrices[7]).astype(jnp.bfloat16)
    grad_cq, grad_ck, grad_cv = attend_backward(
        q_cross.reshape(token_heads),
        k_cross.reshape(state_heads),
        v_cross.reshape(state_heads),
        d_o_cross.reshape(token_heads),
        lse_cross,
        valid_states,
        False,
    )
    dq_cross = (grad_cq.reshape(slot_tokens, D) * 0.125).astype(jnp.bfloat16)
    dk_cross = grad_ck.reshape(slot_states, D).astype(jnp.bfloat16)
    dv_cross = grad_cv.reshape(slot_states, D).astype(jnp.bfloat16)
    grad_cross_query = weight_product(hidden_one_low, dq_cross)
    grad_cross_key = weight_product(states, dk_cross)
    grad_cross_value = weight_product(states, dv_cross)
    state_grad = input_product(dk_cross, matrices[5]) + input_product(
        dv_cross, matrices[6]
    )
    d_hidden_one = d_second + input_product(dq_cross, matrices[4])
    d_first, d_gain_one, d_shift_one = norm_one_back(d_hidden_one)
    d_branch_a = d_first.astype(jnp.bfloat16)
    grad_self_out = weight_product(o_self_low, d_branch_a)
    grad_self_out_offset = row_sum(d_branch_a)
    d_o_self = input_product(d_branch_a, matrices[3]).astype(jnp.bfloat16)
    grad_sq, grad_sk, grad_sv = attend_backward(
        q_self.reshape(token_heads),
        k_self.reshape(token_heads),
        v_self.reshape(token_heads),
        d_o_self.reshape(token_heads),
        lse_self,
        valid_tokens,
        True,
    )
    dq_self = (grad_sq.reshape(slot_tokens, D) * 0.125).astype(jnp.bfloat16)
    dk_self = grad_sk.reshape(slot_tokens, D).astype(jnp.bfloat16)
    dv_self = grad_sv.reshape(slot_tokens, D).astype(jnp.bfloat16)
    grad_self_query = weight_product(tokens, dq_self)
    grad_self_key = weight_product(tokens, dk_self)
    grad_self_value = weight_product(tokens, dv_self)
    token_grad = (
        d_first
        + input_product(dq_self, matrices[0])
        + input_product(dk_self, matrices[1])
        + input_product(dv_self, matrices[2])
    )
    small_partial = jnp.concatenate(
        [
            row_sum(dq_self),
            row_sum(dv_self),
            grad_self_out_offset,
            row_sum(dq_cross),
            row_sum(dv_cross),
            grad_cross_out_offset,
            grad_expand_offset,
            grad_shrink_offset,
            d_gain_one,
            d_shift_one,
            d_gain_two,
            d_shift_two,
            d_gain_three,
            d_shift_three,
        ]
    )
    totals = lax.psum(jnp.concatenate([small_partial, squares]), ("rep", "shard"))
    g_shrink = scatter_rows(grad_shrink)
    g_expand = scatter_rows(grad_expand)
    g_rest = scatter_rows(
        jnp.concatenate(
            [grad_self_out, grad_cross_query, grad_cross_key, grad_cross_value, grad_cross_out],
            axis=1,
        )
    )
    g_qkv = scatter_rows(
        jnp.concatenate([grad_self_query, grad_self_key, grad_self_value], axis=1)
    )
    g_attention = (
        jnp.concatenate([g_qkv, g_rest], axis=1).reshape(-1, 8, D).astype(jnp.float32)
    )
    g_expand = g_expand.astype(jnp.float32)
    g_shrink = g_shrink.astype(jnp.float32)
    attention_rows_new, *attention_parts = local_factors(g_attention, attention_rows.T)
    expand_rows_new, *expand_parts = local_factors(g_expand, expand_rows)
    shrink_rows_new, *shrink_parts = local_factors(g_shrink, shrink_rows)
    flat = attention_parts + expand_parts + shrink_parts
    summed = lax.psum(jnp.concatenate([t.reshape(-1) for t in flat]), "shard")
    sums = []
    offset = 0
    for t in flat:
        sums.append(summed[offset : offset + t.size].reshape(t.shape))
        offset = offset + t.size
    attention_rates = STEP_RATE * jnp.where(jnp.arange(8) % 4 == 3, OUT_GAIN, 1.0).astype(
        jnp.float32
    )
    attention_new, attention_cols_new = finish_factors(
        g_attention,
        attention_weights,
        attention_rows_new,
        attention_cols,
        *sums[0:3],
        D,
        attention_rates,
    )
    expand_new, expand_cols_new = finish_factors(
        g_expand, expand_weight, expand_rows_new, expand_cols, *sums[3:6], D, STEP_RATE
    )
    shrink_new, shrink_cols_new = finish_factors(
        g_shrink, shrink_weight, shrink_rows_new, shrink_cols, *sums[6:9], FF, STEP_RATE
    )
    small_grad = totals[: small_params.shape[0]]
    small_moment_new = DECAY_RATE * small_moment + (1.0 - DECAY_RATE) * (
        small_grad * small_grad + FACTOR_EPS
    )
    small_update = small_grad * lax.rsqrt(small_moment_new)
    small_scale = jnp.sqrt(jnp.mean(small_update * small_update))
    small_new = small_params - SMALL_RATE * small_update / jnp.maximum(
        1.0, small_scale / CLIP_LEVEL
    )
    norm_stats = jnp.sqrt(
        totals[small_params.shape[0] :] / (jnp.sum(lengths).astype(jnp.float32) * D)
    )
    return (
        result.astype(jnp.bfloat16),
        token_grad.astype(jnp.bfloat16),
        state_grad.astype(jnp.bfloat16),
        g_attention,
        g_expand,
        g_shrink,
        small_grad,
        attention_new,
        expand_new,
        shrink_new,
        small_new,
        attention_new.astype(jnp.bfloat16),
        expand_new.astype(jnp.bfloat16),
        shrink_new.astype(jnp.bfloat16),
        attention_rows_new.T,
        attention_cols_new,
        expand_rows_new,
        expand_cols_new,
        shrink_rows_new,
        shrink_cols_new,
        small_moment_new,
        norm_stats,
    )


def direct_device(
    tokens,
    encoder,
    cotangent,
    lengths,
    encoder_lengths,
    dealt_order,
    attention_weights,
    expand_weight,
    shrink_weight,
    small_params,
    attention_rows,
    attention_cols,
    expand_rows,
    expand_cols,
    shrink_rows,
    shrink_cols,
    small_moment,
):
    position = lax.axis_index(("rep", "shard"))
    inverse = jnp.zeros((32,), jnp.int32).at[dealt_order].set(jnp.arange(32, dtype=jnp.int32))
    valid = jnp.stack([lengths[position], encoder_lengths[position]])
    parts = unpack(small_params)
    blank = jnp.zeros((D,), jnp.float32)
    params = jnp.concatenate(
        [
            small_params[0 : 6 * D].reshape(6, D),
            hidden_blocks(parts[6]),
            small_params[6 * D + FF :].reshape(7, D),
            jnp.zeros((7, D), jnp.float32),
        ]
    )
    gains = jnp.stack([parts[8], parts[10]] + [blank] * 6)
    qkv_pieces, rest_pieces = weight_pieces(
        attention_weights, expand_weight, shrink_weight, neighbours()
    )
    tokens, qkv_full = front(inverse, tokens, qkv_pieces)
    (
        rest_full,
        q_self,
        k_self,
        v_self,
        o_self,
        lse_self,
        q_cross,
        k_cross,
        v_cross,
        o_cross,
        lse_cross,
        summed_one,
        summed_two,
        hidden_one,
        hidden_two,
        activated,
        slope,
        output,
        d_mlp,
        d_third,
        small_first,
    ) = forward(valid, tokens, qkv_full, rest_pieces, encoder, cotangent, params)
    token_grad, state_grad, reduced, totals = backward(
        valid,
        (
            d_mlp,
            d_third,
            activated,
            slope,
            rest_full.reshape(GATHERED, 1024, D),
            qkv_full,
            hidden_two,
            hidden_one,
            tokens,
            encoder,
            o_cross,
            o_self,
            summed_one,
            summed_two,
            q_self,
            k_self,
            v_self,
            q_cross,
            k_cross,
            v_cross,
            lse_self,
            lse_cross,
        ),
        gains,
        small_first,
    )
    attention, expand, shrink, rows_new, cols_new = update_direct(
        reduced,
        attention_weights,
        expand_weight,
        shrink_weight,
        attention_rows,
        attention_cols,
        expand_rows,
        expand_cols,
        shrink_rows,
        shrink_cols,
    )
    small_grad = jnp.concatenate(
        [totals[0:6].reshape(-1), hidden_flat(totals[6:10]), totals[10:17].reshape(-1)]
    )
    small_moment_new = DECAY_RATE * small_moment + (1.0 - DECAY_RATE) * (
        small_grad * small_grad + FACTOR_EPS
    )
    small_update = small_grad * lax.rsqrt(small_moment_new)
    small_scale = jnp.sqrt(jnp.mean(small_update * small_update))
    small_new = small_params - SMALL_RATE * small_update / jnp.maximum(
        1.0, small_scale / CLIP_LEVEL
    )
    norm_stats = jnp.sqrt(totals[17, 0:6] / (jnp.sum(lengths).astype(jnp.float32) * D))
    return (
        output,
        token_grad,
        state_grad,
        attention[0],
        expand[0],
        shrink[0],
        small_grad,
        attention[1],
        expand[1],
        shrink[1],
        small_new,
        attention[2],
        expand[2],
        shrink[2],
        rows_new[0],
        cols_new[0],
        rows_new[1],
        cols_new[1],
        rows_new[2],
        cols_new[2],
        small_moment_new,
        norm_stats,
    )


def on_device(*args):
    if lax.axis_size("rep") == 8 and lax.axis_size("shard") == 4:
        return direct_device(*args)
    return plain_device(*args)


def solution(mesh):
    in_specs = (
        P(("rep", "shard"), None),
        P(("rep", "shard"), None),
        P(("rep", "shard"), None),
        P(),
        P(),
        P(),
        P("shard", None, None),
        P("shard", None),
        P("shard", None),
        P(),
        P(None, "shard"),
        P(),
        P("shard"),
        P(),
        P("shard"),
        P(),
        P(),
    )
    out_specs = (
        P(("rep", "shard"), None),
        P(("rep", "shard"), None),
        P(("rep", "shard"), None),
        P("shard", None, None),
        P("shard", None),
        P("shard", None),
        P(),
        P("shard", None, None),
        P("shard", None),
        P("shard", None),
        P(),
        P("shard", None, None),
        P("shard", None),
        P("shard", None),
        P(None, "shard"),
        P(),
        P("shard"),
        P(),
        P("shard"),
        P(),
        P(),
        P(),
    )
    return jax.shard_map(
        on_device, mesh=mesh, in_specs=in_specs, out_specs=out_specs, check_vma=False
    )
```

```python
import math

import jax
import jax.numpy as jnp
from jax import lax
from jax.experimental import pallas as pl
from jax.experimental.pallas import tpu as pltpu
from jax.sharding import PartitionSpec as P

D = 1024
HEADS = 16
HEAD_DIM = 64
FF = 4096


DECAY_RATE = 0.5
CLIP_LEVEL = 0.25
STEP_RATE = 0.1
SMALL_RATE = 0.4
OUT_GAIN = 8.0
NORM_EPS = 1e-05
FACTOR_EPS = 1e-30
MASKED = -1e30
MESH = pl.DeviceIdType.MESH
CHUNKS = 16
MIB = 1 << 20


def layer_norm(r, norm_gain, norm_shift):
    centred = r - jnp.mean(r, axis=-1, keepdims=True)
    spread = jnp.mean(centred * centred, axis=-1, keepdims=True)
    return centred * lax.rsqrt(spread + NORM_EPS) * norm_gain + norm_shift


def gelu_exact(values):
    return jax.nn.gelu(values, approximate=False)


def unpack(small):
    extents = [D] * 6 + [FF] + [D] * 7
    pieces = []
    offset = 0
    for extent in extents:
        pieces.append(small[offset : offset + extent])
        offset = offset + extent
    return pieces


def forward_product(source, matrix):
    return jnp.dot(source, matrix, preferred_element_type=jnp.float32)


def input_product(grad_low, matrix):
    return jnp.einsum("to,io->ti", grad_low, matrix, preferred_element_type=jnp.float32)


def weight_product(source, grad_low):
    return jnp.einsum("ti,to->io", source, grad_low, preferred_element_type=jnp.float32)


def row_sum(grad_low):
    return jnp.sum(grad_low.astype(jnp.float32), axis=0)


def transposed(block):
    return block.astype(jnp.float32).T.astype(jnp.bfloat16)


def half_lanes(shape, dim):
    return lax.broadcasted_iota(jnp.int32, shape, dim)


def masked_keys(keys, length, head):
    place = half_lanes(keys.shape, 0)
    lane = half_lanes(keys.shape, 1)
    blocked = jnp.where((lane == 64 - 64 * head) & (place >= length), MASKED, 0.0)
    own = (lane >= 64 * head) & (lane < 64 * head + 64)
    return jnp.where(own, keys.astype(jnp.float32), blocked).astype(jnp.bfloat16)


def own_head(rows_t, head, fill):
    place = half_lanes(rows_t.shape, 0)
    own = (place >= 64 * head) & (place < 64 * head + 64)
    other = jnp.where(place == 64 - 64 * head, fill, 0.0)
    return jnp.where(own, rows_t.astype(jnp.float32), other).astype(jnp.bfloat16)


def product(first, second):
    return jnp.dot(first, second, preferred_element_type=jnp.float32)


def causal_mask(scores, step):
    kept = scores.shape[0] - step
    last = scores[kept:]
    allowed = half_lanes(last.shape, 0) <= half_lanes(last.shape, 1)
    last = jnp.where(allowed, last, MASKED)
    return last if kept == 0 else jnp.concatenate([scores[:kept], last], axis=0)


def attend_pair(causal, step, length, q_ref, k_ref, v_ref, o_ref, lse_ref, o_t):
    q_t = transposed(q_ref[...])
    v_t = transposed(v_ref[...])
    keys = [masked_keys(k_ref[...], length, head) for head in range(2)]
    queries = [own_head(q_t, head, 1.0) for head in range(2)]
    units = [(head, start) for start in range(0, q_ref.shape[0], step) for head in range(2)]

    def scores_of(head, start):
        end = start + step if causal else k_ref.shape[0]
        return product(keys[head][:end], queries[head][:, start : start + step])

    ahead = scores_of(*units[0])
    for index, (head, start) in enumerate(units):
        scores = ahead
        if index + 1 < len(units):
            ahead = scores_of(*units[index + 1])
        rows = slice(64 * head, 64 * head + 64)
        columns = slice(start, start + step)
        if causal:
            scores = causal_mask(scores, step)
        top = jnp.max(scores, axis=0, keepdims=True)
        raised = jnp.exp(scores - top)
        total = jnp.sum(raised, axis=0, keepdims=True)
        probs = (raised * (1.0 / total)).astype(jnp.bfloat16)
        o_t[rows, columns] = product(v_t[rows, : scores.shape[0]], probs)
        lse_ref[0, head : head + 1, columns] = top + jnp.log(total)
    o_ref[...] = o_t[...].T.astype(jnp.bfloat16)


def attend_back_pair(
    causal,
    step,
    length,
    q_ref,
    k_ref,
    v_ref,
    do_ref,
    lse_ref,
    dq_ref,
    dk_ref,
    dv_ref,
    put_sums,
    dq_t,
    dk_sum,
    dv_sum,
):
    key_rows = k_ref.shape[0]
    q_t = transposed(q_ref[...])
    k_t = transposed(k_ref[...])
    do_t = transposed(do_ref[...])
    values = v_ref[...]
    keys = [masked_keys(k_ref[...], length, head) for head in range(2)]
    queries = [own_head(q_t, head, 1.0) for head in range(2)]
    grads = [own_head(do_t, head, 0.0) for head in range(2)]
    count = q_ref.shape[0] // step
    units = [(head, b) for b in reversed(range(count)) for head in range(2)]

    def products_of(head, b):
        columns = slice(b * step, b * step + step)
        end = b * step + step if causal else key_rows
        scores = product(keys[head][:end], queries[head][:, columns])
        return scores, product(values[:end], grads[head][:, columns])

    ahead = products_of(*units[0])
    for index, (head, b) in enumerate(units):
        scores, d_probs = ahead
        if index + 1 < len(units):
            ahead = products_of(*units[index + 1])
        rows = slice(64 * head, 64 * head + 64)
        columns = slice(b * step, b * step + step)
        end = scores.shape[0]
        if causal:
            scores = causal_mask(scores, step)
        probs = jnp.exp(scores - lse_ref[0, head : head + 1, columns])
        weighted = probs * d_probs
        delta = jnp.sum(weighted, axis=0, keepdims=True)
        d_scores = (weighted - probs * delta).astype(jnp.bfloat16)
        dv = product(probs.astype(jnp.bfloat16), do_ref[columns, :])
        dk = product(d_scores, q_ref[columns, :])
        if b == count - 1:
            dv_sum[head, :end] = dv
            dk_sum[head, :end] = dk
        else:
            dv_sum[head, :end] += dv
            dk_sum[head, :end] += dk
        dq_t[rows, columns] = product(k_t[rows, :end], d_scores)
    first = half_lanes((key_rows, 128), 1) < 64
    dk_ref[...] = jnp.where(first, dk_sum[0, :key_rows], dk_sum[1, :key_rows]).astype(jnp.bfloat16)
    dv = jnp.where(first, dv_sum[0, :key_rows], dv_sum[1, :key_rows]).astype(jnp.bfloat16)
    dv_ref[...] = dv
    dq = (dq_t[...] * 0.125).T.astype(jnp.bfloat16)
    dq_ref[...] = dq
    put_sums(
        jnp.sum(dq.astype(jnp.float32), axis=0, keepdims=True),
        jnp.sum(dv.astype(jnp.float32), axis=0, keepdims=True),
    )


SCALARS = pl.BlockSpec(memory_space=pltpu.SMEM)


def neighbours():
    rep = lax.axis_index("rep")
    z = lax.axis_index("shard")
    core = rep % 2
    x = (rep // 2) % 2
    y = rep // 4
    other_core = (rep + 1 - 2 * core, z)
    other_x = (rep + 2 - 4 * x, z)
    other_y = (rep + 4 - 8 * y, z)
    others_z = [(rep, (z + d) % 4) for d in (1, 2, 3)]
    return core, x, y, z, other_core, other_x, other_y, others_z


def greet(devices):
    barrier = pltpu.get_barrier_semaphore()
    for device in devices:
        pl.semaphore_signal(barrier, inc=1, device_id=device, device_id_type=MESH)
    pl.semaphore_wait(barrier, len(devices))


def remote(src, dst, send, recv, device):
    return pltpu.make_async_remote_copy(
        src_ref=src, dst_ref=dst, send_sem=send, recv_sem=recv, device_id=device, device_id_type=MESH
    )


def gather_copies(refs, c, parity, places):
    piece, full, place_sem, z_send, z_recv, send, recv = refs
    core, x, y, z, other_core, other_x, other_y, others_z = places
    a = x + parity * (y - x)
    b = y + parity * (x - y)
    first = (other_x[0] + parity * (other_y[0] - other_x[0]), z)
    second = (other_y[0] + parity * (other_x[0] - other_y[0]), z)
    own = pl.ds(pl.multiple_of(core * 128 + a * 64 + b * 32, 32), 32)
    steps = (
        (own, second),
        (pl.ds(pl.multiple_of(core * 128 + a * 64, 64), 64), first),
        (pl.ds(pl.multiple_of(core * 128, 128), 128), other_core),
    )

    def local():
        return pltpu.make_async_copy(piece.at[c], full.at[c, z, own, :], place_sem.at[c])

    def line(d):
        return remote(
            piece.at[c], full.at[c, z, own, :], z_send.at[c, d], z_recv.at[c, d], others_z[d]
        )

    def pair(k):
        block = full.at[c, :, steps[k][0], :]
        return remote(block, block, send.at[k, c], recv.at[k, c], steps[k][1])

    return local, line, pair


def gather_stage(k, refs, c, parity, places):
    local, line, pair = gather_copies(refs, c, parity, places)
    if k == 0:
        local().start()
        for d in range(3):
            line(d).start()
    if k == 1:
        local().wait()
        for d in range(3):
            line(d).wait_recv()
        pair(0).start()
    if k == 2 or k == 3:
        pair(k - 2).wait_recv()
        pair(k - 1).start()
    if k == 4:
        pair(2).wait()
        pair(1).wait_send()
        pair(0).wait_send()
        for d in range(3):
            line(d).wait_send()


def gather_sems(count):
    dma = pltpu.SemaphoreType.DMA
    return [dma((count,)), dma((count, 3)), dma((count, 3)), dma((3, count)), dma((3, count))]


def own_rows(blocks, parity, places):
    core, x, y = places[0:3]
    a = x + parity * (y - x)
    b = y + parity * (x - y)
    rows = lax.dynamic_slice_in_dim(blocks, core * 128 + a * 64 + b * 32, 32, axis=-2)
    return rows.astype(jnp.bfloat16)


def hidden_blocks(values):
    split = values.reshape(values.shape[:-1] + (4, 4, 256))
    split = jnp.swapaxes(split, -3, -2)
    return split.reshape(values.shape[:-1] + (4, 1024))


def hidden_flat(blocks):
    split = blocks.reshape(blocks.shape[:-2] + (4, 4, 256))
    split = jnp.swapaxes(split, -3, -2)
    return split.reshape(blocks.shape[:-2] + (FF,))


def weight_pieces(attention, expand, shrink, places):
    attention = jnp.swapaxes(
        jnp.stack([own_rows(jnp.swapaxes(attention, 0, 1), p, places) for p in range(2)]), 0, 1
    )
    picked = [attention[i, i % 2] for i in range(3)]
    picked = picked + [attention[3 + c, c % 2] for c in range(5)]
    ff = []
    for p in range(2):
        rows = own_rows(expand, p, places)
        ff.append(jnp.swapaxes(hidden_blocks(rows), 0, 1))
    for p in range(2):
        ff.append(own_rows(shrink.reshape(4, 256, D), p, places))
    for j in range(4):
        picked.append(ff[1][j])
        picked.append(ff[2][j])
    return jnp.stack(picked[0:3]), jnp.stack(picked[3:16])


def front_kernel(
    order_ref,
    tokens_ref,
    piece_ref,
    x_ref,
    full_ref,
    spread,
    picked,
    spread_send,
    spread_recv,
    back_send,
    back_recv,
    *gather_sem,
):
    places = neighbours()
    z = places[3]
    me = lax.axis_index("rep") * 4 + z
    refs = (piece_ref, full_ref) + gather_sem

    def device(offset):
        j = lax.rem(me + offset, 32)
        return j, (j // 4, j % 4)

    barrier = pltpu.get_barrier_semaphore()

    def greet_one(offset, carry):
        pl.semaphore_signal(barrier, inc=1, device_id=device(offset)[1], device_id_type=MESH)
        return carry

    lax.fori_loop(1, 32, greet_one, 0)
    pl.semaphore_wait(barrier, 31)

    def stage(k):
        for c in range(3):
            gather_stage(k, refs, c, c % 2, places)

    def spread_copy(offset):
        j, target = device(offset)
        return remote(
            tokens_ref.at[j],
            spread.at[me],
            spread_send.at[offset],
            spread_recv.at[offset],
            target,
        )

    def back_copy(offset):
        target = device(offset)[1]
        return remote(
            picked.at[offset], x_ref.at[me], back_send.at[offset], back_recv.at[offset], target
        )

    own_in = pltpu.make_async_copy(tokens_ref.at[me], spread.at[me], spread_recv.at[0])
    own_out = pltpu.make_async_copy(picked.at[0], x_ref.at[me], back_recv.at[0])
    stage(0)
    own_in.start()

    def start_spread(offset, carry):
        spread_copy(offset).start()
        return carry

    lax.fori_loop(1, 32, start_spread, 0)
    stage(1)
    stage(2)
    own_in.wait()

    def wait_spread(offset, carry):
        spread_copy(offset).wait()
        return carry

    lax.fori_loop(1, 32, wait_spread, 0)
    picked[0] = spread[order_ref[me]]
    own_out.start()

    def pick(offset, carry):
        picked[offset] = spread[order_ref[device(offset)[0]]]
        back_copy(offset).start()
        return carry

    lax.fori_loop(1, 32, pick, 0)
    stage(3)
    stage(4)
    own_out.wait()

    def wait_back(offset, carry):
        back_copy(offset).wait()
        return carry

    lax.fori_loop(1, 32, wait_back, 0)


def front(inverse, tokens, pieces):
    dma = pltpu.SemaphoreType.DMA
    any_space = pl.BlockSpec(memory_space=pl.ANY)
    x, full = pl.pallas_call(
        front_kernel,
        out_shape=(
            jax.ShapeDtypeStruct((32, 32, D), jnp.bfloat16),
            jax.ShapeDtypeStruct((3, 4, 256, D), jnp.bfloat16),
        ),
        in_specs=[
            pl.BlockSpec(memory_space=pltpu.SMEM),
            any_space,
            pl.BlockSpec(memory_space=pltpu.VMEM),
        ],
        out_specs=(any_space, any_space),
        scratch_shapes=[
            pltpu.VMEM((32, 32, D), jnp.bfloat16),
            pltpu.VMEM((32, 32, D), jnp.bfloat16),
            dma((32,)),
            dma((32,)),
            dma((32,)),
            dma((32,)),
        ]
        + gather_sems(3),
        compiler_params=pltpu.CompilerParams(
            collective_id=2, has_side_effects=True, vmem_limit_bytes=24 * MIB
        ),
    )(inverse, tokens.reshape(32, 32, D), pieces)
    return x.reshape(1024, D), full.reshape(3, 1024, D)


def fold(tile):
    return jnp.sum(tile.reshape(-1, 8, tile.shape[-1]), axis=0)


GATHERED = 13
GATHER_PLAN = (("z", 6.5), ("second", 6.5), ("first", 11.5), ("core", 3.0), (None, 0.0))


class GatherPlanner:
    def __init__(self, count):
        self.now = 0.0
        self.links = {"core": 0.0, "x": 0.0, "y": 0.0, "z": 0.0}
        self.stage = {c: 0 for c in range(count)}
        self.ready = {c: 0.0 for c in range(count)}

    def emit(self, c):
        stage = self.stage[c]
        link, span = GATHER_PLAN[stage]
        first, second = ("x", "y") if c % 2 == 0 else ("y", "x")
        link = {"first": first, "second": second}.get(link, link)
        self.now = max(self.now, self.ready[c]) + 0.1
        if link is not None:
            begin = max(self.now, self.links[link])
            self.links[link] = begin + span - 1.0
            self.ready[c] = begin + span
        self.stage[c] = stage + 1
        return (stage, c)

    def tick(self, spent):
        self.now += spent
        events = []
        progress = True
        while progress:
            progress = False
            for c in self.stage:
                if self.stage[c] < 5 and self.ready[c] <= self.now:
                    events.append(self.emit(c))
                    progress = True
        return events

    def until(self, c):
        events = []
        while self.stage[c] < 5:
            choices = [i for i in self.stage if self.stage[i] < 5]
            best = min(choices, key=lambda i: (self.ready[i], i))
            events.append(self.emit(best))
        return events


def gelu_parts(u):
    share = 0.5 + 0.5 * lax.erf(u * math.sqrt(0.5))
    bell = jnp.exp(-0.5 * u * u) * (1.0 / math.sqrt(2.0 * math.pi))
    return u * share, share + u * bell


def norm_parts(values):
    centred = values - jnp.mean(values, axis=1, keepdims=True)
    spread = jnp.mean(centred * centred, axis=1, keepdims=True)
    scale = lax.rsqrt(spread + NORM_EPS)
    return centred * scale, scale


def forward_kernel(
    lengths_ref,
    x_ref,
    qkv_ref,
    piece_ref,
    e_ref,
    cot_ref,
    par,
    full_ref,
    q_out,
    k_out,
    v_out,
    o_out,
    lse_out,
    cq_out,
    ck_out,
    cv_out,
    oc_out,
    lse_cross_out,
    r1_out,
    r2_out,
    h1_out,
    h2_out,
    g_out,
    gp_out,
    y_out,
    dm_out,
    d_third_out,
    small_out,
    pool,
    acc,
    held,
    o_t,
    lse_held,
    states,
    load_sem,
    store_sem,
    state_sem,
    acc_sem,
    *gather_sem,
):
    places = neighbours()
    refs = (piece_ref, full_ref) + gather_sem
    planner = GatherPlanner(GATHERED)
    length = lengths_ref[0]

    def emit_all(events):
        for stage, c in events:
            gather_stage(stage, refs, c, c % 2, places)

    def tick(spent):
        emit_all(planner.tick(spent))

    def load(slot, source):
        return pltpu.make_async_copy(source, pool.at[slot], load_sem.at[slot])

    def store(slot, target):
        return pltpu.make_async_copy(pool.at[slot], target, store_sem.at[slot])

    def product_into(left, right, put):
        def body(i, carry):
            n = pl.multiple_of(i * 256, 256)
            put(n, product(left(), pool[right, :, pl.ds(n, 256)]))
            return carry

        lax.fori_loop(0, 4, body, 0)

    def row(index, n):
        return par[index : index + 1, pl.ds(n, 256)]

    def put_low(slot, offset=None, scale=None):
        def put(n, value):
            if offset is not None:
                value = value + row(offset, n)
            if scale is not None:
                value = value * scale
            pool[slot, :, pl.ds(n, 256)] = value.astype(jnp.bfloat16)

        return put

    def put_acc(offset):
        def put(n, value):
            acc[:, pl.ds(n, 256)] = value + row(offset, n)

        return put

    def load_weight(c, slot):
        target = pool.at[slot].reshape(4, 256, D)
        return pltpu.make_async_copy(full_ref.at[c], target, load_sem.at[slot])

    def weight(c, slot):
        emit_all(planner.until(c))
        return load_weight(c, slot)

    def attend_loop(causal, step, valid, query, key, value, out, spent):
        ahead = [planner.tick(spent) for _ in range(8)]

        def body(i, carry):
            lanes = pl.ds(pl.multiple_of(i * 128, 128), 128)
            attend_pair(
                causal,
                step,
                valid,
                query.at[:, lanes],
                key.at[:, lanes],
                value.at[:, lanes],
                out.at[:, lanes],
                lse_held.at[pl.ds(i, 1)],
                o_t,
            )
            for n in range(8):
                if ahead[n]:

                    @pl.when(i == n)
                    def _(events=ahead[n]):
                        emit_all(events)

            return carry

        lax.fori_loop(0, 8, body, 0)

    TILE = 128

    def over_rows(sums, body):
        zero = jnp.zeros((8, D), jnp.float32)

        def step(i, carry):
            r = pl.multiple_of(i * TILE, TILE)
            place = half_lanes((TILE, 1), 0) + r
            usable = (place < length).astype(jnp.float32)
            terms = body(pl.ds(r, TILE), usable)
            return tuple(c + fold(t) for c, t in zip(carry, terms))

        totals = lax.fori_loop(0, D // TILE, step, (zero,) * sums)
        return [jnp.sum(t, axis=0, keepdims=True) for t in totals]

    lane = half_lanes((1, D), 1)

    def square_at(index, total):
        small_out[17:18, :] += jnp.where(lane == index, jnp.sum(total), 0.0)

    greet(list(places[4:7]) + places[7])
    load(0, x_ref).start()
    for i in range(3):
        load(1 + i, qkv_ref.at[i]).start()
    load(9, cot_ref).start()
    e_load = pltpu.make_async_copy(e_ref, states.at[2], state_sem.at[2])
    e_load.start()
    small_out[...] = jnp.zeros_like(small_out)
    tick(0.5)
    load(0, x_ref).wait()
    load(1, qkv_ref.at[0]).wait()
    product_into(lambda: pool[0], 1, put_low(4, 0, 0.125))
    store(4, q_out).start()
    tick(2.5)
    load(2, qkv_ref.at[1]).wait()
    product_into(lambda: pool[0], 2, put_low(5))
    store(5, k_out).start()
    tick(2.5)
    load(3, qkv_ref.at[2]).wait()
    product_into(lambda: pool[0], 3, put_low(6, 1))
    store(6, v_out).start()
    tick(2.5)

    attend_loop(True, 256, length, pool.at[4], pool.at[5], pool.at[6], pool.at[7], 4.8)
    store(7, o_out).start()
    lse_copy = pltpu.make_async_copy(lse_held, lse_out, state_sem.at[3])
    lse_copy.start()
    w_copy = weight(0, 1)
    w_copy.start()
    w_copy.wait()
    product_into(lambda: pool[7], 1, put_acc(2))
    tick(2.5)
    store(4, q_out).wait()

    def first_norm(rows, usable):
        x = pool[0, rows, :].astype(jnp.float32)
        a = acc[rows, :]
        total = x + a
        acc[rows, :] = total
        h = norm_parts(total)[0] * par[11:12, :] + par[12:13, :]
        held[rows, :] = h
        pool[4, rows, :] = h.astype(jnp.bfloat16)
        return usable * x * x, usable * a * a, usable * h * h

    for index, total in enumerate(over_rows(3, first_norm)):
        square_at(index, total)
    store(4, h1_out).start()
    r1_copy = pltpu.make_async_copy(acc, r1_out, acc_sem.at[0])
    r1_copy.start()
    tick(4.0)

    for c, slot in ((1, 2), (2, 3), (3, 1)):
        weight(c, slot).start()
    store(5, k_out).wait()
    load_weight(1, 2).wait()
    product_into(lambda: pool[4], 2, put_low(5, 3, 0.125))
    store(5, cq_out).start()
    w_copy = weight(4, 2)
    w_copy.start()
    tick(2.5)
    e_load.wait()
    load_weight(2, 3).wait()
    load_weight(3, 1).wait()

    def put_keys(n, value):
        states[0, :, pl.ds(n, 256)] = value.astype(jnp.bfloat16)

    def put_values(n, value):
        states[1, :, pl.ds(n, 256)] = (value + row(4, n)).astype(jnp.bfloat16)

    product_into(lambda: states[2], 3, put_keys)
    product_into(lambda: states[2], 1, put_values)
    state_stores = [
        pltpu.make_async_copy(states.at[0], ck_out, state_sem.at[0]),
        pltpu.make_async_copy(states.at[1], cv_out, state_sem.at[1]),
    ]
    for copy in state_stores:
        copy.start()
    tick(1.0)
    store(6, v_out).wait()
    lse_copy.wait()
    attend_loop(
        False, 512, lengths_ref[1], pool.at[5], states.at[0], states.at[1], pool.at[6], 1.6
    )
    store(6, oc_out).start()
    lse_copy = pltpu.make_async_copy(lse_held, lse_cross_out, state_sem.at[3])
    lse_copy.start()
    w_copy.wait()
    r1_copy.wait()
    product_into(lambda: pool[6], 2, put_acc(5))
    tick(2.5)
    weight(5, 0).start()
    weight(6, 2).start()
    store(7, o_out).wait()

    def second_norm(rows, usable):
        c = acc[rows, :]
        total = held[rows, :] + c
        acc[rows, :] = total
        h = norm_parts(total)[0] * par[13:14, :] + par[14:15, :]
        held[rows, :] = h
        pool[7, rows, :] = h.astype(jnp.bfloat16)
        return usable * c * c, usable * h * h

    for index, total in enumerate(over_rows(2, second_norm)):
        square_at(3 + index, total)
    store(7, h2_out).start()
    r2_copy = pltpu.make_async_copy(acc, r2_out, acc_sem.at[0])
    r2_copy.start()
    tick(4.0)

    store(4, h1_out).wait()
    store(5, cq_out).wait()
    g_slots, slope_slots = (4, 6), (5, 8)
    r2_copy.wait()
    store(6, oc_out).wait()
    for j in range(5):
        if j > 1:
            store(g_slots[j % 2], g_out.at[j - 2]).wait()
            store(slope_slots[j % 2], gp_out.at[j - 2]).wait()
        if j < 4:
            load_weight(5 + 2 * j, j % 2).wait()
        if j > 0:
            load_weight(4 + 2 * j, 2 + (j - 1) % 2).wait()

        def body(i, carry, j=j):
            n = pl.multiple_of(i * 256, 256)
            here = pl.ds(n, 256)
            if j < 4:
                u = product(pool[7], pool[j % 2, :, here]) + row(6 + j, n)
            if j > 0:
                more = product(pool[g_slots[(j - 1) % 2]], pool[2 + (j - 1) % 2, :, here])
                if j == 1:
                    acc[:, here] = more + row(10, n)
                else:
                    acc[:, here] += more
            if j < 4:
                g, slope = gelu_parts(u)
                pool[g_slots[j % 2], :, here] = g.astype(jnp.bfloat16)
                pool[slope_slots[j % 2], :, here] = slope.astype(jnp.bfloat16)
            return carry

        lax.fori_loop(0, 4, body, 0)
        if j < 4:
            store(g_slots[j % 2], g_out.at[j]).start()
            store(slope_slots[j % 2], gp_out.at[j]).start()
        tick(9.0 if j < 4 else 2.5)
        if j < 3:
            weight(7 + 2 * j, (j + 1) % 2).start()
            weight(8 + 2 * j, 2 + (j + 1) % 2).start()

    load(9, cot_ref).wait()

    def third_norm(rows, usable):
        m = acc[rows, :]
        unit, scale = norm_parts(held[rows, :] + m)
        gain = par[15:16, :]
        pool[0, rows, :] = (unit * gain + par[16:17, :]).astype(jnp.bfloat16)
        grad = pool[9, rows, :].astype(jnp.float32) * usable
        inner = grad * gain
        first = jnp.mean(inner, axis=1, keepdims=True)
        second = jnp.mean(inner * unit, axis=1, keepdims=True)
        back = scale * (inner - first - unit * second)
        acc[rows, :] = back
        low = back.astype(jnp.bfloat16)
        pool[1, rows, :] = low
        return usable * m * m, grad * unit, grad, low.astype(jnp.float32)

    m_total, gain_sum, shift_sum, offset_sum = over_rows(4, third_norm)
    square_at(5, m_total)
    small_out[15:16, :] = gain_sum
    small_out[16:17, :] = shift_sum
    small_out[10:11, :] = offset_sum
    last = [
        store(0, y_out),
        store(1, dm_out),
        pltpu.make_async_copy(acc, d_third_out, acc_sem.at[0]),
    ]
    for copy in last:
        copy.start()
    for c in range(GATHERED):
        emit_all(planner.until(c))
    for copy in last + state_stores + [lse_copy]:
        copy.wait()
    store(7, h2_out).wait()
    store(6, g_out.at[3]).wait()
    store(8, gp_out.at[3]).wait()


def forward(lengths, x, qkv_full, pieces, states, cotangent, params):
    any_space = pl.BlockSpec(memory_space=pl.ANY)
    vmem = pl.BlockSpec(memory_space=pltpu.VMEM)
    shape = jax.ShapeDtypeStruct
    dma = pltpu.SemaphoreType.DMA
    low = jnp.bfloat16
    wide = jnp.float32
    square = shape((1024, D), low)
    square_wide = shape((1024, D), wide)
    lse = shape((8, 8, 1024), wide)
    short = shape((128, D), low)
    blocks = shape((4, 1024, D), low)
    outs = (
        shape((GATHERED, 4, 256, D), low),
        square,
        square,
        square,
        square,
        lse,
        square,
        short,
        short,
        square,
        lse,
        square_wide,
        square_wide,
        square,
        square,
        blocks,
        blocks,
        square,
        square,
        square_wide,
        shape((24, D), wide),
    )
    return pl.pallas_call(
        forward_kernel,
        out_shape=outs,
        in_specs=[SCALARS] + [any_space] * 5 + [vmem],
        out_specs=(any_space,) * 20 + (vmem,),
        scratch_shapes=[
            pltpu.VMEM((10, 1024, D), low),
            pltpu.VMEM((1024, D), wide),
            pltpu.VMEM((1024, D), wide),
            pltpu.VMEM((128, 1024), wide),
            pltpu.VMEM((8, 8, 1024), wide),
            pltpu.VMEM((3, 128, D), low),
            dma((10,)),
            dma((10,)),
            dma((4,)),
            dma((1,)),
        ]
        + gather_sems(GATHERED),
        compiler_params=pltpu.CompilerParams(
            collective_id=3, has_side_effects=True, vmem_limit_bytes=56 * MIB
        ),
    )(lengths, x, qkv_full, pieces, states, cotangent, params)


def add_blocks(target, first, second, planes, rows, step):
    per_plane = rows // step

    def body(i, carry):
        s = i // per_plane
        r = pl.multiple_of((i % per_plane) * step, step)
        target(s, r, first(s, r) + second(s, r))
        return carry

    lax.fori_loop(0, planes * per_plane, body, 0)


POOL = 8
G_SLOTS = 3
R_SLOTS = 4
PLAN = {"core": 3.0, "load": 1.5, "a": 11.5, "b": 6.5, "z": 6.5, "bb": 2.5, "ba": 4.0, "bc": 2.0}


class Planner:
    def __init__(self):
        self.now = 0.0
        self.links = {"core": 0.0, "x": 0.0, "y": 0.0, "z": 0.0, "load": 0.0}
        self.stage = {}
        self.ready = {}

    def link_of(self, c, stage):
        first, second = ("x", "y") if c % 2 == 0 else ("y", "x")
        return {
            0: ("core", "core"),
            1: ("load", "load"),
            2: (first, "a"),
            3: (second, "b"),
            4: ("z", "z"),
            5: (second, "bb"),
            6: (first, "ba"),
            7: ("core", "bc"),
            8: (None, None),
        }[stage]

    def can(self, c):
        stage = self.stage[c]
        if stage > 8:
            return False
        if stage == 1 and c >= R_SLOTS and self.stage[c - R_SLOTS] <= 3:
            return False
        return True

    def emit(self, c):
        stage = self.stage[c]
        link, kind = self.link_of(c, stage)
        self.now = max(self.now, self.ready[c]) + {2: 0.8, 3: 0.5, 4: 0.3, 5: 0.2}.get(stage, 0.1)
        if link is not None:
            begin = max(self.now, self.links[link])
            span = PLAN[kind]
            self.links[link] = begin + span - 1.0
            self.ready[c] = begin + span
        self.stage[c] = stage + 1
        return (stage, c)

    def tick(self, spent):
        self.now += spent
        events = []
        progress = True
        while progress:
            progress = False
            for c in sorted(self.stage):
                if self.can(c) and self.ready[c] <= self.now:
                    events.append(self.emit(c))
                    progress = True
        return events

    def produce(self, c):
        self.stage[c] = 0
        self.ready[c] = self.now
        return [self.emit(c)]

    def until(self, done):
        events = []
        while not done():
            choices = [c for c in sorted(self.stage) if self.can(c)]
            c = min(choices, key=lambda i: (self.ready[i], i))
            events.append(self.emit(c))
        return events

    def free_slot(self, c):
        before = c - G_SLOTS
        if before < 0:
            return []
        return self.until(lambda: self.stage[before] > 2)

    def drain(self):
        return self.until(lambda: all(s > 8 for s in self.stage.values()))


def backward_kernel(
    lengths_ref,
    dm_ref,
    d_third_ref,
    g_ref,
    gp_ref,
    rest_ref,
    qkv_ref,
    h2_ref,
    h1_ref,
    x_in_ref,
    e_ref,
    oc_ref,
    o_ref,
    r1_ref,
    r2_ref,
    q_ref,
    k_ref,
    v_ref,
    cq_ref,
    ck_ref,
    cv_ref,
    lse_ref,
    lse_cross_ref,
    gains_ref,
    small_ref,
    token_grad_ref,
    state_grad_ref,
    out_ref,
    totals_ref,
    half,
    pool,
    acc,
    made,
    summed,
    quarter,
    eighth,
    pieces,
    stream,
    dq_t,
    dk_sum,
    dv_sum,
    lse_held,
    states,
    states_t,
    small,
    small_in,
    small_sum,
    small_z,
    load_sem,
    stream_sem,
    state_sem,
    half_sem,
    send_sem,
    recv_sem,
    z_send_sem,
    z_recv_sem,
    place_sem,
    small_send_sem,
    small_recv_sem,
):
    core, x, y, z, other_core, other_x, other_y, others_z = neighbours()
    kept = pl.multiple_of(core * 128, 128)
    given = pl.multiple_of(128 - core * 128, 128)
    planner = Planner()
    place_of = (12, 8, 13, 9, 14, 10, 15, 11, 7, 4, 5, 6, 3, 0, 1, 2)

    def axes(c):
        if c % 2 == 0:
            return x, y, other_x, other_y
        return y, x, other_y, other_x

    def core_copy(c):
        source = made.at[c % G_SLOTS, :, pl.ds(given, 128), :]
        return remote(source, half.at[c], send_sem.at[0, c], recv_sem.at[0, c], other_core)

    def half_copy(c):
        return pltpu.make_async_copy(
            half.at[c], summed.at[c % R_SLOTS], half_sem.at[c % R_SLOTS]
        )

    def first_copy(c):
        a, b, first, second = axes(c)
        rows = pl.ds(pl.multiple_of(64 - a * 64, 64), 64)
        source = summed.at[c % R_SLOTS, :, rows, :]
        return remote(source, quarter.at[c], send_sem.at[1, c], recv_sem.at[1, c], first)

    def second_copy(c):
        a, b, first, second = axes(c)
        rows = pl.ds(pl.multiple_of(32 - b * 32, 32), 32)
        source = quarter.at[c, :, rows, :]
        return remote(source, eighth.at[c], send_sem.at[2, c], recv_sem.at[2, c], second)

    def z_copy(c, d):
        device = others_z[d]
        return remote(
            eighth.at[c, device[1]],
            pieces.at[c, d],
            z_send_sem.at[c, d],
            z_recv_sem.at[c, d],
            device,
        )

    def own_rows_of(c):
        a, b, first, second = axes(c)
        return pl.ds(pl.multiple_of(core * 128 + a * 64 + b * 32, 32), 32)

    def place_copy(c):
        return pltpu.make_async_copy(
            pieces.at[c, 0], out_ref.at[place_of[c], own_rows_of(c), :], place_sem.at[c]
        )

    def back_second(c):
        device = axes(c)[3]
        target = out_ref.at[place_of[c], own_rows_of(c), :]
        return remote(pieces.at[c, 0], target, send_sem.at[3, c], recv_sem.at[3, c], device)

    def back_first(c):
        a, b, first, second = axes(c)
        block = out_ref.at[place_of[c], pl.ds(pl.multiple_of(core * 128 + a * 64, 64), 64), :]
        return remote(block, block, send_sem.at[4, c], recv_sem.at[4, c], first)

    def back_core(c):
        block = out_ref.at[place_of[c], pl.ds(kept, 128), :]
        return remote(block, block, send_sem.at[5, c], recv_sem.at[5, c], other_core)

    def emit(stage, c):
        a, b, first, second = axes(c)
        slot = c % R_SLOTS
        if stage == 0:
            core_copy(c).start()
        if stage == 1:
            if c >= R_SLOTS:
                first_copy(c - R_SLOTS).wait_send()
            core_copy(c).wait_recv()
            half_copy(c).start()
        if stage == 2:
            half_copy(c).wait()

            def put(s, r, value):
                summed[slot, s, pl.ds(r, 32), :] = value

            add_blocks(
                put,
                lambda s, r: summed[slot, s, pl.ds(r, 32), :],
                lambda s, r: made[c % G_SLOTS, s, pl.ds(pl.multiple_of(kept + r, 32), 32), :],
                4,
                128,
                32,
            )
            first_copy(c).start()
            core_copy(c).wait_send()
        if stage == 3:
            first_copy(c).wait_recv()

            def put(s, r, value):
                quarter[c, s, pl.ds(r, 32), :] = value

            add_blocks(
                put,
                lambda s, r: quarter[c, s, pl.ds(r, 32), :],
                lambda s, r: summed[slot, s, pl.ds(pl.multiple_of(a * 64 + r, 32), 32), :],
                4,
                64,
                32,
            )
            second_copy(c).start()
        if stage == 4:
            second_copy(c).wait_recv()

            def put(s, r, value):
                eighth[c, s, pl.ds(r, 32), :] = value

            add_blocks(
                put,
                lambda s, r: eighth[c, s, pl.ds(r, 32), :],
                lambda s, r: quarter[c, s, pl.ds(pl.multiple_of(b * 32 + r, 32), 32), :],
                4,
                32,
                32,
            )
            for d in range(3):
                z_copy(c, d).start()
        if stage == 5:
            for d in range(3):
                z_copy(c, d).wait_recv()
            total = eighth[c, z].astype(jnp.float32)
            for d in range(3):
                total = total + pieces[c, d].astype(jnp.float32)
            pieces[c, 0] = total.astype(jnp.bfloat16)
            back_second(c).start()
            place_copy(c).start()
        if stage == 6:
            place_copy(c).wait()
            back_second(c).wait_recv()
            back_first(c).start()
        if stage == 7:
            back_first(c).wait_recv()
            back_core(c).start()
        if stage == 8:
            back_core(c).wait()
            back_first(c).wait_send()
            back_second(c).wait_send()
            for d in range(3):
                z_copy(c, d).wait_send()
            second_copy(c).wait_send()
            if c >= CHUNKS - R_SLOTS:
                first_copy(c).wait_send()

    def emit_all(events):
        for stage, c in events:
            emit(stage, c)

    def tick(spent):
        emit_all(planner.tick(spent))

    def produced(c, spent):
        planner.now += spent
        emit_all(planner.produce(c))
        emit_all(planner.tick(0.0))

    def load(slot, source):
        return pltpu.make_async_copy(source, pool.at[slot], load_sem.at[slot])

    def state_load(index, source):
        return pltpu.make_async_copy(source, states.at[index], state_sem.at[index])

    def turn_tile(target, source):
        def turn(n):
            pool[target, pl.ds(n, 256), :] = pool[source, :, pl.ds(n, 256)].T

        return turn

    def transpose_into(target, source):
        turn = turn_tile(target, source)

        def body(i, carry):
            turn(pl.multiple_of(i * 256, 256))
            return carry

        lax.fori_loop(0, 4, body, 0)

    def product_nn(left, right, put, beside=None):
        def body(i, carry):
            n = pl.multiple_of(i * 256, 256)
            if beside is not None:
                beside(n)
            put(n, product(left(), right(n)))
            return carry

        lax.fori_loop(0, 4, body, 0)

    def product_nt(left, right, put, beside=None):
        def body(i, carry):
            n = pl.multiple_of(i * 256, 256)
            if beside is not None:
                beside(n)
            put(
                n,
                lax.dot_general(
                    left(),
                    right(n),
                    (((1,), (1,)), ((), ())),
                    preferred_element_type=jnp.float32,
                ),
            )
            return carry

        lax.fori_loop(0, 4, body, 0)

    def columns_of(slot):
        return lambda n: pool[slot, :, pl.ds(n, 256)]

    def rows_of(slot):
        return lambda n: pool[slot, pl.ds(n, 256), :]

    def weight_grad(slot_in_made, left, right, beside=None):
        def put(n, value):
            low = value.astype(jnp.bfloat16).reshape(4, 256, 256)
            made[slot_in_made, :, :, pl.ds(n, 256)] = low

        product_nn(left, right, put, beside)

    def add_to_acc(n, value):
        acc[:, pl.ds(n, 256)] += value

    def put_in(slot):
        def put(n, value):
            pool[slot, :, pl.ds(n, 256)] = value.astype(jnp.bfloat16)

        return put

    def norm_back(source, gain_row, gain_at, shift_at, offset_at, target):
        tiles = 8
        rows = 1024 // tiles

        def fetch(i):
            place = pl.ds(pl.multiple_of(i * rows, rows), rows)
            return pltpu.make_async_copy(
                source.at[place, :], stream.at[i % 2], stream_sem.at[i % 2]
            )

        fetch(0).start()

        def body(i, carry):
            gain_sum, shift_sum, offset_sum = carry

            @pl.when(i + 1 < tiles)
            def _():
                fetch(i + 1).start()

            fetch(i).wait()
            r = pl.multiple_of(i * rows, rows)
            values = stream[i % 2]
            centred = values - jnp.mean(values, axis=1, keepdims=True)
            spread = jnp.mean(centred * centred, axis=1, keepdims=True)
            scale = lax.rsqrt(spread + NORM_EPS)
            unit = centred * scale
            grad = acc[pl.ds(r, rows), :]
            inner = grad * gains_ref[gain_row : gain_row + 1, :]
            first = jnp.mean(inner, axis=1, keepdims=True)
            second = jnp.mean(inner * unit, axis=1, keepdims=True)
            back = scale * (inner - first - unit * second)
            acc[pl.ds(r, rows), :] = back
            low = back.astype(jnp.bfloat16)
            pool[target, pl.ds(r, rows), :] = low
            return (
                gain_sum + fold(grad * unit),
                shift_sum + fold(grad),
                offset_sum + fold(low.astype(jnp.float32)),
            )

        zero = jnp.zeros((8, D), jnp.float32)
        sums = lax.fori_loop(0, tiles, body, (zero, zero, zero))
        for row, value in zip((gain_at, shift_at, offset_at), sums):
            small[row : row + 1, :] = jnp.sum(value, axis=0, keepdims=True)

    greet([other_core, other_x, other_y] + others_z)
    load(0, dm_ref).start()
    load(6, h2_ref).start()
    load(2, rest_ref.at[6]).start()
    load(3, gp_ref.at[0]).start()
    load(4, g_ref.at[0]).start()
    load(5, rest_ref.at[5]).start()
    acc_load = pltpu.make_async_copy(d_third_ref, acc, place_sem.at[0])
    acc_load.start()
    small[...] = small_ref[...]
    load(6, h2_ref).wait()
    transpose_into(1, 6)
    load(0, dm_ref).wait()
    acc_load.wait()

    planner.now = 4.0
    plan = []
    for j in range(4):
        entry = []
        planner.now += 3.5
        entry.append(planner.tick(0.0) + planner.free_slot(2 * j))
        planner.now += 2.5
        entry.append(planner.produce(2 * j) + planner.tick(0.0) + planner.free_slot(2 * j + 1))
        planner.now += 2.5
        entry.append(planner.produce(2 * j + 1) + planner.tick(0.0))
        entry.append(planner.tick(2.5))
        plan.append(entry)

    def emit_planned(j, place):
        for n in range(4):
            events = plan[n][place]
            if events:

                @pl.when(j == n)
                def _(events=events):
                    emit_all(events)

    def block(j, carry):
        last = j == 3
        load(2, rest_ref.at[6]).wait()
        load(3, gp_ref.at[0]).wait()

        def put_pre(n, value):
            low = (value * pool[3, :, pl.ds(n, 256)].astype(jnp.float32)).astype(jnp.bfloat16)
            pool[7, :, pl.ds(n, 256)] = low
            small[pl.ds(6 + j, 1), pl.ds(n, 256)] = jnp.sum(
                low.astype(jnp.float32), axis=0, keepdims=True
            )

        load(4, g_ref.at[0]).wait()
        product_nt(lambda: pool[0], rows_of(2), put_pre, turn_tile(6, 4))

        @pl.when(jnp.logical_not(last))
        def _():
            load(2, rest_ref.at[8 + 2 * j]).start()
            load(3, gp_ref.at[j + 1]).start()

        @pl.when(last)
        def _():
            load(2, rest_ref.at[4]).start()
            load(3, cq_ref).start()

        emit_planned(j, 0)

        @pl.when(jnp.logical_not(last))
        def _():
            load(4, g_ref.at[j + 1]).start()

        @pl.when(last)
        def _():
            load(4, oc_ref).start()

        weight_grad((2 * j) % G_SLOTS, lambda: pool[6], columns_of(0))
        emit_planned(j, 1)
        weight_grad((2 * j + 1) % G_SLOTS, lambda: pool[1], columns_of(7))
        emit_planned(j, 2)
        load(5, rest_ref.at[5]).wait()
        product_nt(lambda: pool[7], rows_of(5), add_to_acc)

        @pl.when(jnp.logical_not(last))
        def _():
            load(5, rest_ref.at[7 + 2 * j]).start()

        @pl.when(last)
        def _():
            load(5, rest_ref.at[1]).start()

        emit_planned(j, 3)
        return carry

    lax.fori_loop(0, 4, block, 0)

    load(7, h1_ref).start()
    state_loads = [state_load(0, ck_ref), state_load(1, cv_ref), state_load(2, e_ref)]
    for copy in state_loads:
        copy.start()
    lse_load = pltpu.make_async_copy(lse_cross_ref, lse_held, state_sem.at[3])
    lse_load.start()
    norm_back(r2_ref, 1, 13, 14, 5, 0)
    tick(4.0)
    load(4, oc_ref).wait()
    load(2, rest_ref.at[4]).wait()
    product_nt(lambda: pool[0], rows_of(2), put_in(4), turn_tile(6, 4))
    load(2, rest_ref.at[0]).start()
    tick(2.5)
    emit_all(planner.free_slot(8))
    load(7, h1_ref).wait()
    weight_grad(8 % G_SLOTS, lambda: pool[6], columns_of(0), turn_tile(1, 7))
    load(6, o_ref).start()
    load(7, rest_ref.at[2]).start()
    produced(8, 2.5)
    load(3, cq_ref).wait()
    for copy in state_loads:
        copy.wait()
    lse_load.wait()

    def attend_loop(causal, step, length, query, key, value, grad, rows, spent):
        ahead = [planner.tick(spent) for _ in range(8)]

        def body(i, carry):
            lanes = pl.ds(pl.multiple_of(i * 128, 128), 128)

            def sums(dq, dv):
                small[rows[0] : rows[0] + 1, lanes] = dq
                small[rows[1] : rows[1] + 1, lanes] = dv

            attend_back_pair(
                causal,
                step,
                length,
                query.at[:, lanes],
                key.at[:, lanes],
                value.at[:, lanes],
                grad.at[:, lanes],
                lse_held.at[pl.ds(i, 1)],
                query.at[:, lanes],
                key.at[:, lanes],
                value.at[:, lanes],
                sums,
                dq_t,
                dk_sum,
                dv_sum,
            )
            for n in range(8):
                if ahead[n]:

                    @pl.when(i == n)
                    def _(events=ahead[n]):
                        emit_all(events)

            return carry

        lax.fori_loop(0, 8, body, 0)

    attend_loop(
        False,
        512,
        lengths_ref[1],
        pool.at[3],
        states.at[0],
        states.at[1],
        pool.at[4],
        (3, 4),
        2.0,
    )
    lse_load = pltpu.make_async_copy(lse_ref, lse_held, state_sem.at[3])
    lse_load.start()
    emit_all(planner.free_slot(9))
    weight_grad(9 % G_SLOTS, lambda: pool[1], columns_of(3))
    produced(9, 2.5)
    load(5, rest_ref.at[1]).wait()
    load(6, o_ref).wait()
    product_nt(lambda: pool[3], rows_of(5), add_to_acc, turn_tile(1, 6))
    load(6, x_in_ref).start()
    load(5, rest_ref.at[3]).start()
    load(3, q_ref).start()
    tick(2.5)
    states_t[...] = states[2].T
    for c, index in ((10, 0), (11, 1)):
        emit_all(planner.free_slot(c))
        weight_grad(
            c % G_SLOTS, lambda: states_t[...], lambda n, i=index: states[i, :, pl.ds(n, 256)]
        )
        produced(c, 1.0)
    load(7, rest_ref.at[2]).wait()
    load(5, rest_ref.at[3]).wait()

    def state_part(n):
        dims = (((1,), (1,)), ((), ()))
        return lax.dot_general(
            states[0], pool[7, pl.ds(n, 256), :], dims, preferred_element_type=jnp.float32
        ) + lax.dot_general(
            states[1], pool[5, pl.ds(n, 256), :], dims, preferred_element_type=jnp.float32
        )

    def put_state(i, carry):
        n = pl.multiple_of(i * 256, 256)
        state_grad_ref[:, pl.ds(n, 256)] = state_part(n).astype(jnp.bfloat16)
        return carry

    lax.fori_loop(0, 4, put_state, 0)
    load(5, k_ref).start()
    load(7, v_ref).start()
    tick(1.0)

    norm_back(r1_ref, 0, 11, 12, 2, 0)
    tick(4.0)
    emit_all(planner.free_slot(12))
    weight_grad(12 % G_SLOTS, lambda: pool[1], columns_of(0))
    produced(12, 2.5)
    load(2, rest_ref.at[0]).wait()
    load(6, x_in_ref).wait()
    product_nt(lambda: pool[0], rows_of(2), put_in(4), turn_tile(1, 6))
    load(0, qkv_ref.at[0]).start()
    load(2, qkv_ref.at[1]).start()
    load(6, qkv_ref.at[2]).start()
    tick(2.5)
    load(3, q_ref).wait()
    load(5, k_ref).wait()
    load(7, v_ref).wait()
    lse_load.wait()
    attend_loop(
        True, 256, lengths_ref[0], pool.at[3], pool.at[5], pool.at[7], pool.at[4], (0, 1), 5.0
    )

    def small_copy(k):
        source = small if k == 0 else small_sum.at[k - 1]
        device = (other_core, other_x, other_y)[k]
        return remote(source, small_in.at[k], small_send_sem.at[k], small_recv_sem.at[k], device)

    def small_z_copy(d):
        return remote(
            small_sum.at[2],
            small_z.at[z],
            small_send_sem.at[3 + d],
            small_recv_sem.at[3 + d],
            others_z[d],
        )

    def small_step(k):
        small_copy(k).wait()
        before = small[...] if k == 0 else small_sum[k - 1]
        small_sum[k] = before + small_in[k]
        if k < 2:
            small_copy(k + 1).start()
        else:
            small_z[z] = small_sum[2]
            for d in range(3):
                small_z_copy(d).start()

    small_copy(0).start()
    for i, (c, slot) in enumerate(((13, 3), (14, 5), (15, 7))):
        emit_all(planner.free_slot(c))
        weight_grad(c % G_SLOTS, lambda: pool[1], columns_of(slot))
        produced(c, 2.5)
        small_step(i)
    load(0, qkv_ref.at[0]).wait()
    product_nt(lambda: pool[3], rows_of(0), add_to_acc)
    tick(2.5)
    load(2, qkv_ref.at[1]).wait()
    product_nt(lambda: pool[5], rows_of(2), add_to_acc)
    tick(2.5)
    for d in range(3):
        small_z_copy(d).wait()
    totals_ref[...] = (small_z[0] + small_z[1]) + (small_z[2] + small_z[3])
    load(6, qkv_ref.at[2]).wait()

    def put_input(n, value):
        total = acc[:, pl.ds(n, 256)] + value
        pool[4, :, pl.ds(n, 256)] = total.astype(jnp.bfloat16)

    product_nt(lambda: pool[7], rows_of(6), put_input)
    token_copy = pltpu.make_async_copy(pool.at[4], token_grad_ref, load_sem.at[4])
    token_copy.start()
    tick(2.5)
    emit_all(planner.drain())
    token_copy.wait()


def backward(lengths, held, gains, small):
    any_space = pl.BlockSpec(memory_space=pl.ANY)
    vmem = pl.BlockSpec(memory_space=pltpu.VMEM)
    shape = jax.ShapeDtypeStruct
    dma = pltpu.SemaphoreType.DMA
    low = jnp.bfloat16
    wide = jnp.float32
    rows = small.shape[0]
    return pl.pallas_call(
        backward_kernel,
        out_shape=(
            shape((1024, D), low),
            shape((128, D), low),
            shape((CHUNKS, 256, D), low),
            shape(small.shape, wide),
            shape((CHUNKS, 4, 128, D), low),
        ),
        in_specs=[SCALARS] + [any_space] * len(held) + [vmem, vmem],
        out_specs=(any_space, vmem, any_space, vmem, any_space),
        scratch_shapes=[
            pltpu.VMEM((POOL, 1024, D), low),
            pltpu.VMEM((1024, D), wide),
            pltpu.VMEM((G_SLOTS, 4, 256, D), low),
            pltpu.VMEM((R_SLOTS, 4, 128, D), low),
            pltpu.VMEM((CHUNKS, 4, 64, D), low),
            pltpu.VMEM((CHUNKS, 4, 32, D), low),
            pltpu.VMEM((CHUNKS, 3, 32, D), low),
            pltpu.VMEM((2, 128, D), wide),
            pltpu.VMEM((128, 1024), wide),
            pltpu.VMEM((2, 1024, 128), wide),
            pltpu.VMEM((2, 1024, 128), wide),
            pltpu.VMEM((8, 8, 1024), wide),
            pltpu.VMEM((3, 128, D), low),
            pltpu.VMEM((D, 128), low),
            pltpu.VMEM((rows, D), wide),
            pltpu.VMEM((3, rows, D), wide),
            pltpu.VMEM((3, rows, D), wide),
            pltpu.VMEM((4, rows, D), wide),
            dma((POOL,)),
            dma((2,)),
            dma((4,)),
            dma((R_SLOTS,)),
            dma((6, CHUNKS)),
            dma((6, CHUNKS)),
            dma((CHUNKS, 3)),
            dma((CHUNKS, 3)),
            dma((CHUNKS,)),
            dma((6,)),
            dma((6,)),
        ],
        compiler_params=pltpu.CompilerParams(
            collective_id=0, has_side_effects=True, vmem_limit_bytes=62 * MIB
        ),
    )(lengths, *held, gains, small)[0:4]


def line_sum(part, whole, send_sem, recv_sem, z, others_z):
    copies = [
        remote(part, whole.at[z], send_sem.at[d], recv_sem.at[d], others_z[d]) for d in range(3)
    ]
    for copy in copies:
        copy.start()
    whole[z] = part[...]
    for copy in copies:
        copy.wait()
    return (whole[0] + whole[1]) + (whole[2] + whole[3])


def spread_scalar(value):
    return jnp.broadcast_to(value, (1, 128))


def factor_kernel(
    grad_ref,
    att_rows_ref,
    exp_rows_ref,
    shr_rows_ref,
    cols_ref,
    att_rows_out,
    exp_rows_out,
    shr_rows_out,
    cols_out,
    scale_out,
    part,
    whole,
    send_sem,
    recv_sem,
):
    core, x, y, z, other_core, other_x, other_y, others_z = neighbours()
    greet(others_z)
    part[...] = jnp.zeros_like(part)

    def tile(chunk, r, step):
        return grad_ref[chunk, pl.ds(r, step), :].astype(jnp.float32)

    def add(slot, col, weighted):
        part[slot : slot + 1, :] += jnp.sum(col, axis=0, keepdims=True)
        part[16 + slot : 17 + slot, :] += jnp.sum(weighted, axis=0, keepdims=True)

    def scan_rows(chunks, slots, rows_in, rows_out, total_at):
        width = float(len(chunks) * D)
        step = 64 // len(chunks)

        def body(i, carry):
            cols, weights, total = carry
            r = pl.multiple_of(i * step, step)
            squares = [jnp.square(tile(c, r, step)) for c in chunks]
            row_sum = squares[0]
            for square in squares[1:]:
                row_sum = row_sum + square
            row_sum = jnp.sum(row_sum, axis=1, keepdims=True)
            rows = DECAY_RATE * rows_in[pl.ds(r, step), :] + (1.0 - DECAY_RATE) * (
                row_sum / width + FACTOR_EPS
            )
            rows_out[pl.ds(r, step), :] = rows
            inverse = 1.0 / rows
            cols = [c + fold(s) for c, s in zip(cols, squares)]
            weights = [w + fold(s * inverse) for w, s in zip(weights, squares)]
            return cols, weights, total + fold(rows)

        zeros = [jnp.zeros((8, D), jnp.float32) for _ in chunks]
        cols, weights, total = lax.fori_loop(
            0, 256 // step, body, (zeros, zeros, jnp.zeros((8, 1), jnp.float32))
        )
        for slot, col, weighted in zip(slots, cols, weights):
            add(slot, col, weighted)
        row, lane = total_at
        part[row : row + 1, lane : lane + 128] += spread_scalar(jnp.sum(total))

    for i in range(8):
        scan_rows([i], [i], att_rows_ref.at[i], att_rows_out.at[i], (13, 128 * i))
    scan_rows([8, 9, 10, 11], [8, 9, 10, 11], exp_rows_ref, exp_rows_out, (14, 0))
    for i in range(4):
        scan_rows([12 + i], [12], shr_rows_ref.at[i], shr_rows_out.at[i], (14, 128))
    total = line_sum(part, whole, send_sem, recv_sem, z, others_z)
    row_counts = [D] * 12 + [FF]
    means = [total[13:14, 128 * i : 128 * i + 1] / D for i in range(8)]
    means = means + [total[14:15, 0:1] / D] * 4 + [total[14:15, 128:129] / FF]
    cols_new, quotients = [], []
    for slot in range(13):
        new = DECAY_RATE * cols_ref[slot : slot + 1, :] + (1.0 - DECAY_RATE) * (
            total[slot : slot + 1] / row_counts[slot] + FACTOR_EPS
        )
        cols_new.append(new)
        quotients.append(jnp.sum(total[16 + slot : 17 + slot] / new, axis=1, keepdims=True))
        cols_out[slot : slot + 1, :] = new
    expand_quotient = quotients[8] + quotients[9] + quotients[10] + quotients[11]
    for slot in range(13):
        if slot < 8:
            mean_square = means[slot] * quotients[slot] / (D * D)
            rate = STEP_RATE * (OUT_GAIN if slot % 4 == 3 else 1.0)
        else:
            quotient = expand_quotient if slot < 12 else quotients[12]
            mean_square = means[slot] * quotient / (D * FF)
            rate = STEP_RATE
        factor = rate / jnp.maximum(1.0, jnp.sqrt(mean_square) / CLIP_LEVEL)
        scale_out[slot : slot + 1, :] = lax.rsqrt(cols_new[slot] / means[slot]) * factor


def factors(grads, att_rows, exp_rows, shr_rows, cols):
    vmem = pl.BlockSpec(memory_space=pltpu.VMEM)
    shape = jax.ShapeDtypeStruct
    return pl.pallas_call(
        factor_kernel,
        out_shape=(
            shape((8, 256, 1), jnp.float32),
            shape((256, 1), jnp.float32),
            shape((4, 256, 1), jnp.float32),
            shape((16, D), jnp.float32),
            shape((16, D), jnp.float32),
        ),
        in_specs=[vmem] * 5,
        out_specs=(vmem,) * 5,
        scratch_shapes=[
            pltpu.VMEM((32, D), jnp.float32),
            pltpu.VMEM((4, 32, D), jnp.float32),
            pltpu.SemaphoreType.DMA((3,)),
            pltpu.SemaphoreType.DMA((3,)),
        ],
        compiler_params=pltpu.CompilerParams(
            collective_id=1, has_side_effects=True, vmem_limit_bytes=40 * MIB
        ),
    )(grads, att_rows, exp_rows, shr_rows, cols)


def update_attention_kernel(
    grad_ref, weight_ref, rows_ref, scale_ref, grad_out, new_out, copy_out, grads, change
):
    block = grad_ref.shape[1]
    for i in range(8):
        grad = grad_ref[i].astype(jnp.float32)
        scaled = grad * lax.rsqrt(rows_ref[i]) * scale_ref[i : i + 1, :]
        every = pl.ds(i, block, stride=8)
        for lane in range(8):
            columns = slice(lane * 128, lane * 128 + 128)
            grads[lane, every, :] = grad[:, columns]
            change[lane, every, :] = scaled[:, columns]
    for lane in range(8):
        columns = slice(lane * 128, lane * 128 + 128)
        grad_out[:, columns] = grads[lane]
        new = weight_ref[:, columns] - change[lane]
        new_out[:, columns] = new
        copy_out[:, columns] = new.astype(jnp.bfloat16)


def update_attention(grads, weights, rows, scale):
    block = 32
    wide = pl.BlockSpec((block * 8, D), lambda i: (i, 0))
    shape = jax.ShapeDtypeStruct
    new = pl.pallas_call(
        update_attention_kernel,
        grid=(256 // block,),
        out_shape=(
            shape((2048, D), jnp.float32),
            shape((2048, D), jnp.float32),
            shape((2048, D), jnp.bfloat16),
        ),
        in_specs=[
            pl.BlockSpec((8, block, D), lambda i: (0, i, 0)),
            wide,
            pl.BlockSpec((8, block, 1), lambda i: (0, i, 0)),
            pl.BlockSpec((16, D), lambda i: (0, 0)),
        ],
        out_specs=(wide,) * 3,
        scratch_shapes=[pltpu.VMEM((8, block * 8, 128), jnp.float32)] * 2,
        compiler_params=pltpu.CompilerParams(vmem_limit_bytes=40 * MIB),
    )(grads, weights.reshape(2048, D), rows, scale)
    return [t.reshape(256, 8, D) for t in new]


def update_kernel(
    first, slots, grad_ref, weight_ref, rows_ref, scale_ref, grad_out, new_out, copy_out
):
    spans = 4 if slots == 4 else 1
    wide = D // spans
    for i in range(slots):
        grads = grad_ref[i].astype(jnp.float32)
        changes = grads * (lax.rsqrt(rows_ref[...]) * scale_ref[first + i : first + i + 1, :])
        for s in range(spans):
            start = s * D + i * wide
            columns = slice(start, start + wide)
            part = slice(s * wide, s * wide + wide)
            grad_out[:, columns] = grads[:, part]
            new = weight_ref[:, columns] - changes[:, part]
            new_out[:, columns] = new
            copy_out[:, columns] = new.astype(jnp.bfloat16)


def update_plain(grads, weights, rows, scale, first, slots, grad_map):
    count, width = weights.shape
    block = 128 // slots
    wide = pl.BlockSpec((block, width), lambda i: (i, 0))
    shape = jax.ShapeDtypeStruct
    return pl.pallas_call(
        lambda *refs: update_kernel(first, slots, *refs),
        grid=(count // block,),
        out_shape=(
            shape(weights.shape, jnp.float32),
            shape(weights.shape, jnp.float32),
            shape(weights.shape, jnp.bfloat16),
        ),
        in_specs=[
            pl.BlockSpec((slots, block, D), grad_map),
            wide,
            pl.BlockSpec((block, 1), lambda i: (i, 0)),
            pl.BlockSpec((16, D), lambda i: (0, 0)),
        ],
        out_specs=(wide,) * 3,
        compiler_params=pltpu.CompilerParams(vmem_limit_bytes=40 * MIB),
    )(grads, weights, rows, scale)


def update_direct(
    grads,
    attention_weights,
    expand_weight,
    shrink_weight,
    attention_rows,
    attention_cols,
    expand_rows,
    expand_cols,
    shrink_rows,
    shrink_cols,
):
    cols = jnp.concatenate(
        [attention_cols, hidden_blocks(expand_cols), shrink_cols.reshape(1, D), jnp.ones((3, D))]
    )
    att_rows, exp_rows, shr_rows, cols_new, scale = factors(
        grads,
        attention_rows[:, :, None],
        expand_rows[:, None],
        shrink_rows.reshape(4, 256, 1),
        cols,
    )
    shr_rows = shr_rows.reshape(-1, 1)
    attention = update_attention(grads, attention_weights, att_rows, scale)
    expand = update_plain(grads, expand_weight, exp_rows, scale, 8, 4, lambda i: (2, i, 0))
    shrink = update_plain(
        grads, shrink_weight, shr_rows, scale, 12, 1, lambda i: (12 + i // 2, i % 2, 0)
    )
    return (
        attention,
        expand,
        shrink,
        (att_rows[:, :, 0], exp_rows[:, 0], shr_rows[:, 0]),
        (cols_new[0:8], hidden_flat(cols_new[8:12]), cols_new[12]),
    )


def as_rows(vector):
    rows = -(-vector.shape[0] // 1024) * 8
    return jnp.pad(vector, (0, rows * 128 - vector.shape[0])).reshape(rows, 128)


def masked_scores(query_part, key_heads, first_row, valid_count, causal):
    scores = jnp.einsum("qhd,khd->hqk", query_part, key_heads, preferred_element_type=jnp.float32)
    key_places = jnp.arange(key_heads.shape[0], dtype=jnp.int32)[None, :]
    usable = key_places < valid_count
    if causal:
        query_places = first_row + jnp.arange(query_part.shape[0], dtype=jnp.int32)[:, None]
        usable = usable & (key_places <= query_places)
    return jnp.where(usable[None], scores, MASKED)


def attend_forward(queries, key_heads, values, valid_count, causal):
    query_rows = queries.shape[0]
    step_rows = min(512, query_rows)
    outputs, stored = ([], [])
    for b in range(query_rows // step_rows):
        first_row = b * step_rows
        key_end = first_row + step_rows if causal else key_heads.shape[0]
        scores = masked_scores(
            queries[first_row : first_row + step_rows],
            key_heads[:key_end],
            first_row,
            valid_count,
            causal,
        )
        row_max = jnp.max(scores, axis=-1, keepdims=True)
        raised = jnp.exp(scores - row_max)
        totals = jnp.sum(raised, axis=-1, keepdims=True)
        probs_low = (raised / totals).astype(jnp.bfloat16)
        outputs.append(
            jnp.einsum(
                "hqk,khd->qhd", probs_low, values[:key_end], preferred_element_type=jnp.float32
            )
        )
        stored.append(row_max + jnp.log(totals))
    return (jnp.concatenate(outputs, axis=0), stored)


def attend_backward(queries, key_heads, values, grad_out, stored, valid_count, causal):
    query_rows = queries.shape[0]
    key_rows = key_heads.shape[0]
    step_rows = min(512, query_rows)
    grad_queries = []
    grad_keys = jnp.zeros(key_heads.shape, jnp.float32)
    grad_values = jnp.zeros(values.shape, jnp.float32)
    for b in range(query_rows // step_rows):
        first_row = b * step_rows
        key_end = first_row + step_rows if causal else key_rows
        query_part = queries[first_row : first_row + step_rows]
        grad_part = grad_out[first_row : first_row + step_rows]
        scores = masked_scores(query_part, key_heads[:key_end], first_row, valid_count, causal)
        probs = jnp.exp(scores - stored[b])
        probs_low = probs.astype(jnp.bfloat16)
        grad_probs = jnp.einsum(
            "qhd,khd->hqk", grad_part, values[:key_end], preferred_element_type=jnp.float32
        )
        value_part = jnp.einsum(
            "hqk,qhd->khd", probs_low, grad_part, preferred_element_type=jnp.float32
        )
        grad_scores = probs * (grad_probs - jnp.sum(probs * grad_probs, axis=-1, keepdims=True))
        scores_low = grad_scores.astype(jnp.bfloat16)
        grad_queries.append(
            jnp.einsum(
                "hqk,khd->qhd", scores_low, key_heads[:key_end], preferred_element_type=jnp.float32
            )
        )
        key_part = jnp.einsum(
            "hqk,qhd->khd", scores_low, query_part, preferred_element_type=jnp.float32
        )
        padding = ((0, key_rows - key_end), (0, 0), (0, 0))
        grad_keys = grad_keys + jnp.pad(key_part, padding)
        grad_values = grad_values + jnp.pad(value_part, padding)
    return (jnp.concatenate(grad_queries, axis=0), grad_keys, grad_values)


def gather_rows(piece):
    return lax.all_gather(piece, ("shard", "rep"), axis=0, tiled=True)


def own_piece(block, replicas):
    rows = block.shape[0] // replicas
    return lax.dynamic_slice_in_dim(block, lax.axis_index("rep") * rows, rows, axis=0)


def scatter_rows(grad):
    piece = lax.psum_scatter(
        grad.astype(jnp.bfloat16), ("shard", "rep"), scatter_dimension=0, tiled=True
    )
    return lax.all_gather(piece, "rep", axis=0, tiled=True)


def local_factors(grad, rows):
    square = grad * grad
    rows_new = DECAY_RATE * rows + (1.0 - DECAY_RATE) * jnp.mean(square + FACTOR_EPS, axis=-1)
    col_part = jnp.sum(square + FACTOR_EPS, axis=0)
    weighted = jnp.sum(square / rows_new[..., None], axis=0)
    return rows_new, col_part, weighted, jnp.sum(rows_new, axis=0)


def finish_factors(grad, weight, rows_new, cols, col_sum, weighted, row_total, row_count, rate):
    cols_new = DECAY_RATE * cols + (1.0 - DECAY_RATE) * col_sum / row_count
    mean_rows = row_total / row_count
    mean_square = mean_rows * jnp.sum(weighted / cols_new, axis=-1) / (row_count * cols.shape[-1])
    factor = rate / jnp.maximum(1.0, jnp.sqrt(mean_square) / CLIP_LEVEL)
    scaled = lax.rsqrt(cols_new / mean_rows[..., None]) * factor[..., None]
    fresh = weight - grad * (lax.rsqrt(rows_new)[..., None] * scaled[None])
    return fresh, cols_new


def plain_device(
    tokens,
    encoder,
    cotangent,
    lengths,
    encoder_lengths,
    dealt_order,
    attention_weights,
    expand_weight,
    shrink_weight,
    small_params,
    attention_rows,
    attention_cols,
    expand_rows,
    expand_cols,
    shrink_rows,
    shrink_cols,
    small_moment,
):
    devices = lax.axis_size(("rep", "shard"))
    replicas = lax.axis_size("rep")
    shards = lax.axis_size("shard")
    slot_tokens = tokens.shape[0]
    slot_states = encoder.shape[0]
    position = lax.axis_index(("rep", "shard"))
    inverse = (
        jnp.zeros((devices,), jnp.int32).at[dealt_order].set(jnp.arange(devices, dtype=jnp.int32))
    )
    qkv_piece = own_piece(attention_weights[:, 0:3, :].reshape(-1, 3 * D), replicas)
    rest_piece = own_piece(attention_weights[:, 3:8, :].reshape(-1, 5 * D), replicas)
    qkv_full = gather_rows(qkv_piece.astype(jnp.bfloat16))
    rest_full = gather_rows(rest_piece.astype(jnp.bfloat16))
    expand_full = gather_rows(own_piece(expand_weight, replicas).astype(jnp.bfloat16))
    shrink_full = gather_rows(own_piece(shrink_weight, replicas).astype(jnp.bfloat16))
    spread = lax.all_to_all(
        tokens.reshape(devices, slot_tokens // devices, D),
        ("rep", "shard"),
        split_axis=0,
        concat_axis=0,
        tiled=True,
    )
    picked = jnp.take(spread, inverse, axis=0)
    tokens = lax.all_to_all(
        picked, ("rep", "shard"), split_axis=0, concat_axis=0, tiled=True
    ).reshape(slot_tokens, D)
    states = encoder
    incoming = cotangent
    valid_tokens = lengths[position]
    valid_states = encoder_lengths[position]
    matrices = [qkv_full[:, i * D : (i + 1) * D] for i in range(3)] + [
        rest_full[:, i * D : (i + 1) * D] for i in range(5)
    ]
    parts = unpack(small_params)
    token_heads = (slot_tokens, HEADS, HEAD_DIM)
    state_heads = (slot_states, HEADS, HEAD_DIM)
    q_self = ((forward_product(tokens, matrices[0]) + parts[0]) * 0.125).astype(
        jnp.bfloat16
    )
    k_self = forward_product(tokens, matrices[1]).astype(jnp.bfloat16)
    v_self = (forward_product(tokens, matrices[2]) + parts[1]).astype(jnp.bfloat16)
    o_self, lse_self = attend_forward(
        q_self.reshape(token_heads),
        k_self.reshape(token_heads),
        v_self.reshape(token_heads),
        valid_tokens,
        True,
    )
    o_self_low = o_self.reshape(slot_tokens, D).astype(jnp.bfloat16)
    branch_a = forward_product(o_self_low, matrices[3]) + parts[2]
    tokens_wide = tokens.astype(jnp.float32)
    hidden_one, norm_one_back = jax.vjp(layer_norm, tokens_wide + branch_a, parts[8], parts[9])
    hidden_one_low = hidden_one.astype(jnp.bfloat16)
    q_cross = (
        (forward_product(hidden_one_low, matrices[4]) + parts[3]) * 0.125
    ).astype(jnp.bfloat16)
    k_cross = forward_product(states, matrices[5]).astype(jnp.bfloat16)
    v_cross = (forward_product(states, matrices[6]) + parts[4]).astype(jnp.bfloat16)
    o_cross, lse_cross = attend_forward(
        q_cross.reshape(token_heads),
        k_cross.reshape(state_heads),
        v_cross.reshape(state_heads),
        valid_states,
        False,
    )
    o_cross_low = o_cross.reshape(slot_tokens, D).astype(jnp.bfloat16)
    branch_c = forward_product(o_cross_low, matrices[7]) + parts[5]
    hidden_two, norm_two_back = jax.vjp(layer_norm, hidden_one + branch_c, parts[10], parts[11])
    hidden_two_low = hidden_two.astype(jnp.bfloat16)
    pre_act = forward_product(hidden_two_low, expand_full) + parts[6]
    activated, gelu_back = jax.vjp(gelu_exact, pre_act)
    activated_low = activated.astype(jnp.bfloat16)
    branch_m = forward_product(activated_low, shrink_full) + parts[7]
    result, norm_three_back = jax.vjp(layer_norm, hidden_two + branch_m, parts[12], parts[13])
    usable_rows = (jnp.arange(slot_tokens, dtype=jnp.int32) < valid_tokens).astype(jnp.float32)[
        :, None
    ]
    squares = jnp.stack(
        [
            jnp.sum(usable_rows * t * t)
            for t in (tokens_wide, branch_a, hidden_one, branch_c, hidden_two, branch_m)
        ]
    )
    d_third, d_gain_three, d_shift_three = norm_three_back(
        incoming.astype(jnp.float32) * usable_rows
    )
    d_mlp = d_third.astype(jnp.bfloat16)
    grad_shrink = weight_product(activated_low, d_mlp)
    grad_shrink_offset = row_sum(d_mlp)
    d_activated = input_product(d_mlp, shrink_full)
    d_pre = gelu_back(d_activated)[0].astype(jnp.bfloat16)
    grad_expand = weight_product(hidden_two_low, d_pre)
    grad_expand_offset = row_sum(d_pre)
    d_hidden_two = d_third + input_product(d_pre, expand_full)
    d_second, d_gain_two, d_shift_two = norm_two_back(d_hidden_two)
    d_branch_c = d_second.astype(jnp.bfloat16)
    grad_cross_out = weight_product(o_cross_low, d_branch_c)
    grad_cross_out_offset = row_sum(d_branch_c)
    d_o_cross = input_product(d_branch_c, matrices[7]).astype(jnp.bfloat16)
    grad_cq, grad_ck, grad_cv = attend_backward(
        q_cross.reshape(token_heads),
        k_cross.reshape(state_heads),
        v_cross.reshape(state_heads),
        d_o_cross.reshape(token_heads),
        lse_cross,
        valid_states,
        False,
    )
    dq_cross = (grad_cq.reshape(slot_tokens, D) * 0.125).astype(jnp.bfloat16)
    dk_cross = grad_ck.reshape(slot_states, D).astype(jnp.bfloat16)
    dv_cross = grad_cv.reshape(slot_states, D).astype(jnp.bfloat16)
    grad_cross_query = weight_product(hidden_one_low, dq_cross)
    grad_cross_key = weight_product(states, dk_cross)
    grad_cross_value = weight_product(states, dv_cross)
    state_grad = input_product(dk_cross, matrices[5]) + input_product(
        dv_cross, matrices[6]
    )
    d_hidden_one = d_second + input_product(dq_cross, matrices[4])
    d_first, d_gain_one, d_shift_one = norm_one_back(d_hidden_one)
    d_branch_a = d_first.astype(jnp.bfloat16)
    grad_self_out = weight_product(o_self_low, d_branch_a)
    grad_self_out_offset = row_sum(d_branch_a)
    d_o_self = input_product(d_branch_a, matrices[3]).astype(jnp.bfloat16)
    grad_sq, grad_sk, grad_sv = attend_backward(
        q_self.reshape(token_heads),
        k_self.reshape(token_heads),
        v_self.reshape(token_heads),
        d_o_self.reshape(token_heads),
        lse_self,
        valid_tokens,
        True,
    )
    dq_self = (grad_sq.reshape(slot_tokens, D) * 0.125).astype(jnp.bfloat16)
    dk_self = grad_sk.reshape(slot_tokens, D).astype(jnp.bfloat16)
    dv_self = grad_sv.reshape(slot_tokens, D).astype(jnp.bfloat16)
    grad_self_query = weight_product(tokens, dq_self)
    grad_self_key = weight_product(tokens, dk_self)
    grad_self_value = weight_product(tokens, dv_self)
    token_grad = (
        d_first
        + input_product(dq_self, matrices[0])
        + input_product(dk_self, matrices[1])
        + input_product(dv_self, matrices[2])
    )
    small_partial = jnp.concatenate(
        [
            row_sum(dq_self),
            row_sum(dv_self),
            grad_self_out_offset,
            row_sum(dq_cross),
            row_sum(dv_cross),
            grad_cross_out_offset,
            grad_expand_offset,
            grad_shrink_offset,
            d_gain_one,
            d_shift_one,
            d_gain_two,
            d_shift_two,
            d_gain_three,
            d_shift_three,
        ]
    )
    totals = lax.psum(jnp.concatenate([small_partial, squares]), ("rep", "shard"))
    g_shrink = scatter_rows(grad_shrink)
    g_expand = scatter_rows(grad_expand)
    g_rest = scatter_rows(
        jnp.concatenate(
            [grad_self_out, grad_cross_query, grad_cross_key, grad_cross_value, grad_cross_out],
            axis=1,
        )
    )
    g_qkv = scatter_rows(
        jnp.concatenate([grad_self_query, grad_self_key, grad_self_value], axis=1)
    )
    g_attention = (
        jnp.concatenate([g_qkv, g_rest], axis=1).reshape(-1, 8, D).astype(jnp.float32)
    )
    g_expand = g_expand.astype(jnp.float32)
    g_shrink = g_shrink.astype(jnp.float32)
    attention_rows_new, *attention_parts = local_factors(g_attention, attention_rows.T)
    expand_rows_new, *expand_parts = local_factors(g_expand, expand_rows)
    shrink_rows_new, *shrink_parts = local_factors(g_shrink, shrink_rows)
    flat = attention_parts + expand_parts + shrink_parts
    summed = lax.psum(jnp.concatenate([t.reshape(-1) for t in flat]), "shard")
    sums = []
    offset = 0
    for t in flat:
        sums.append(summed[offset : offset + t.size].reshape(t.shape))
        offset = offset + t.size
    attention_rates = STEP_RATE * jnp.where(jnp.arange(8) % 4 == 3, OUT_GAIN, 1.0).astype(
        jnp.float32
    )
    attention_new, attention_cols_new = finish_factors(
        g_attention,
        attention_weights,
        attention_rows_new,
        attention_cols,
        *sums[0:3],
        D,
        attention_rates,
    )
    expand_new, expand_cols_new = finish_factors(
        g_expand, expand_weight, expand_rows_new, expand_cols, *sums[3:6], D, STEP_RATE
    )
    shrink_new, shrink_cols_new = finish_factors(
        g_shrink, shrink_weight, shrink_rows_new, shrink_cols, *sums[6:9], FF, STEP_RATE
    )
    small_grad = totals[: small_params.shape[0]]
    small_moment_new = DECAY_RATE * small_moment + (1.0 - DECAY_RATE) * (
        small_grad * small_grad + FACTOR_EPS
    )
    small_update = small_grad * lax.rsqrt(small_moment_new)
    small_scale = jnp.sqrt(jnp.mean(small_update * small_update))
    small_new = small_params - SMALL_RATE * small_update / jnp.maximum(
        1.0, small_scale / CLIP_LEVEL
    )
    norm_stats = jnp.sqrt(
        totals[small_params.shape[0] :] / (jnp.sum(lengths).astype(jnp.float32) * D)
    )
    return (
        result.astype(jnp.bfloat16),
        token_grad.astype(jnp.bfloat16),
        state_grad.astype(jnp.bfloat16),
        g_attention,
        g_expand,
        g_shrink,
        small_grad,
        attention_new,
        expand_new,
        shrink_new,
        small_new,
        attention_new.astype(jnp.bfloat16),
        expand_new.astype(jnp.bfloat16),
        shrink_new.astype(jnp.bfloat16),
        attention_rows_new.T,
        attention_cols_new,
        expand_rows_new,
        expand_cols_new,
        shrink_rows_new,
        shrink_cols_new,
        small_moment_new,
        norm_stats,
    )


def direct_device(
    tokens,
    encoder,
    cotangent,
    lengths,
    encoder_lengths,
    dealt_order,
    attention_weights,
    expand_weight,
    shrink_weight,
    small_params,
    attention_rows,
    attention_cols,
    expand_rows,
    expand_cols,
    shrink_rows,
    shrink_cols,
    small_moment,
):
    position = lax.axis_index(("rep", "shard"))
    inverse = jnp.zeros((32,), jnp.int32).at[dealt_order].set(jnp.arange(32, dtype=jnp.int32))
    valid = jnp.stack([lengths[position], encoder_lengths[position]])
    parts = unpack(small_params)
    blank = jnp.zeros((D,), jnp.float32)
    params = jnp.concatenate(
        [
            small_params[0 : 6 * D].reshape(6, D),
            hidden_blocks(parts[6]),
            small_params[6 * D + FF :].reshape(7, D),
            jnp.zeros((7, D), jnp.float32),
        ]
    )
    gains = jnp.stack([parts[8], parts[10]] + [blank] * 6)
    qkv_pieces, rest_pieces = weight_pieces(
        attention_weights, expand_weight, shrink_weight, neighbours()
    )
    tokens, qkv_full = front(inverse, tokens, qkv_pieces)
    (
        rest_full,
        q_self,
        k_self,
        v_self,
        o_self,
        lse_self,
        q_cross,
        k_cross,
        v_cross,
        o_cross,
        lse_cross,
        summed_one,
        summed_two,
        hidden_one,
        hidden_two,
        activated,
        slope,
        output,
        d_mlp,
        d_third,
        small_first,
    ) = forward(valid, tokens, qkv_full, rest_pieces, encoder, cotangent, params)
    token_grad, state_grad, reduced, totals = backward(
        valid,
        (
            d_mlp,
            d_third,
            activated,
            slope,
            rest_full.reshape(GATHERED, 1024, D),
            qkv_full,
            hidden_two,
            hidden_one,
            tokens,
            encoder,
            o_cross,
            o_self,
            summed_one,
            summed_two,
            q_self,
            k_self,
            v_self,
            q_cross,
            k_cross,
            v_cross,
            lse_self,
            lse_cross,
        ),
        gains,
        small_first,
    )
    attention, expand, shrink, rows_new, cols_new = update_direct(
        reduced,
        attention_weights,
        expand_weight,
        shrink_weight,
        attention_rows,
        attention_cols,
        expand_rows,
        expand_cols,
        shrink_rows,
        shrink_cols,
    )
    small_grad = jnp.concatenate(
        [totals[0:6].reshape(-1), hidden_flat(totals[6:10]), totals[10:17].reshape(-1)]
    )
    small_moment_new = DECAY_RATE * small_moment + (1.0 - DECAY_RATE) * (
        small_grad * small_grad + FACTOR_EPS
    )
    small_update = small_grad * lax.rsqrt(small_moment_new)
    small_scale = jnp.sqrt(jnp.mean(small_update * small_update))
    small_new = small_params - SMALL_RATE * small_update / jnp.maximum(
        1.0, small_scale / CLIP_LEVEL
    )
    norm_stats = jnp.sqrt(totals[17, 0:6] / (jnp.sum(lengths).astype(jnp.float32) * D))
    return (
        output,
        token_grad,
        state_grad,
        attention[0],
        expand[0],
        shrink[0],
        small_grad,
        attention[1],
        expand[1],
        shrink[1],
        small_new,
        attention[2],
        expand[2],
        shrink[2],
        rows_new[0],
        cols_new[0],
        rows_new[1],
        cols_new[1],
        rows_new[2],
        cols_new[2],
        small_moment_new,
        norm_stats,
    )


def on_device(*args):
    if lax.axis_size("rep") == 8 and lax.axis_size("shard") == 4:
        return direct_device(*args)
    return plain_device(*args)


def solution(mesh):
    in_specs = (
        P(("rep", "shard"), None),
        P(("rep", "shard"), None),
        P(("rep", "shard"), None),
        P(),
        P(),
        P(),
        P("shard", None, None),
        P("shard", None),
        P("shard", None),
        P(),
        P(None, "shard"),
        P(),
        P("shard"),
        P(),
        P("shard"),
        P(),
        P(),
    )
    out_specs = (
        P(("rep", "shard"), None),
        P(("rep", "shard"), None),
        P(("rep", "shard"), None),
        P("shard", None, None),
        P("shard", None),
        P("shard", None),
        P(),
        P("shard", None, None),
        P("shard", None),
        P("shard", None),
        P(),
        P("shard", None, None),
        P("shard", None),
        P("shard", None),
        P(None, "shard"),
        P(),
        P("shard"),
        P(),
        P("shard"),
        P(),
        P(),
        P(),
    )
    return jax.shard_map(
        on_device, mesh=mesh, in_specs=in_specs, out_specs=out_specs, check_vma=False
    )
```

```python
import math

import jax
import jax.numpy as jnp
from jax import lax
from jax.experimental import pallas as pl
from jax.experimental.pallas import tpu as pltpu
from jax.sharding import PartitionSpec as P

D = 1024
HEADS = 16
HEAD_DIM = 64
FF = 4096


DECAY_RATE = 0.5
CLIP_LEVEL = 0.25
STEP_RATE = 0.1
SMALL_RATE = 0.4
OUT_GAIN = 8.0
NORM_EPS = 1e-05
FACTOR_EPS = 1e-30
MASKED = -1e30
MESH = pl.DeviceIdType.MESH
CHUNKS = 16
MIB = 1 << 20


def layer_norm(r, norm_gain, norm_shift):
    centred = r - jnp.mean(r, axis=-1, keepdims=True)
    spread = jnp.mean(centred * centred, axis=-1, keepdims=True)
    return centred * lax.rsqrt(spread + NORM_EPS) * norm_gain + norm_shift


def gelu_exact(values):
    return jax.nn.gelu(values, approximate=False)


def unpack(small):
    extents = [D] * 6 + [FF] + [D] * 7
    pieces = []
    offset = 0
    for extent in extents:
        pieces.append(small[offset : offset + extent])
        offset = offset + extent
    return pieces


def forward_product(source, matrix):
    return jnp.dot(source, matrix, preferred_element_type=jnp.float32)


def input_product(grad_low, matrix):
    return jnp.einsum("to,io->ti", grad_low, matrix, preferred_element_type=jnp.float32)


def weight_product(source, grad_low):
    return jnp.einsum("ti,to->io", source, grad_low, preferred_element_type=jnp.float32)


def row_sum(grad_low):
    return jnp.sum(grad_low.astype(jnp.float32), axis=0)


def transposed(block):
    return block.astype(jnp.float32).T.astype(jnp.bfloat16)


def half_lanes(shape, dim):
    return lax.broadcasted_iota(jnp.int32, shape, dim)


def masked_keys(keys, length, head):
    place = half_lanes(keys.shape, 0)
    lane = half_lanes(keys.shape, 1)
    blocked = jnp.where((lane == 64 - 64 * head) & (place >= length), MASKED, 0.0)
    own = (lane >= 64 * head) & (lane < 64 * head + 64)
    return jnp.where(own, keys.astype(jnp.float32), blocked).astype(jnp.bfloat16)


def own_head(rows_t, head, fill):
    place = half_lanes(rows_t.shape, 0)
    own = (place >= 64 * head) & (place < 64 * head + 64)
    other = jnp.where(place == 64 - 64 * head, fill, 0.0)
    return jnp.where(own, rows_t.astype(jnp.float32), other).astype(jnp.bfloat16)


def product(first, second):
    return jnp.dot(first, second, preferred_element_type=jnp.float32)


def causal_mask(scores, step):
    kept = scores.shape[0] - step
    last = scores[kept:]
    allowed = half_lanes(last.shape, 0) <= half_lanes(last.shape, 1)
    last = jnp.where(allowed, last, MASKED)
    return last if kept == 0 else jnp.concatenate([scores[:kept], last], axis=0)


def attend_pair(causal, step, length, q_ref, k_ref, v_ref, o_ref, lse_ref, o_t):
    q_t = transposed(q_ref[...])
    v_t = transposed(v_ref[...])
    keys = [masked_keys(k_ref[...], length, head) for head in range(2)]
    queries = [own_head(q_t, head, 1.0) for head in range(2)]
    units = [(head, start) for start in range(0, q_ref.shape[0], step) for head in range(2)]

    def scores_of(head, start):
        end = start + step if causal else k_ref.shape[0]
        return product(keys[head][:end], queries[head][:, start : start + step])

    ahead = scores_of(*units[0])
    for index, (head, start) in enumerate(units):
        scores = ahead
        if index + 1 < len(units):
            ahead = scores_of(*units[index + 1])
        rows = slice(64 * head, 64 * head + 64)
        columns = slice(start, start + step)
        if causal:
            scores = causal_mask(scores, step)
        top = jnp.max(scores, axis=0, keepdims=True)
        raised = jnp.exp(scores - top)
        total = jnp.sum(raised, axis=0, keepdims=True)
        probs = (raised * (1.0 / total)).astype(jnp.bfloat16)
        o_t[rows, columns] = product(v_t[rows, : scores.shape[0]], probs)
        lse_ref[0, head : head + 1, columns] = top + jnp.log(total)
    o_ref[...] = o_t[...].T.astype(jnp.bfloat16)


def attend_back_pair(
    causal,
    step,
    length,
    q_ref,
    k_ref,
    v_ref,
    do_ref,
    lse_ref,
    dq_ref,
    dk_ref,
    dv_ref,
    put_sums,
    dq_t,
    dk_sum,
    dv_sum,
):
    key_rows = k_ref.shape[0]
    q_t = transposed(q_ref[...])
    k_t = transposed(k_ref[...])
    do_t = transposed(do_ref[...])
    values = v_ref[...]
    keys = [masked_keys(k_ref[...], length, head) for head in range(2)]
    queries = [own_head(q_t, head, 1.0) for head in range(2)]
    grads = [own_head(do_t, head, 0.0) for head in range(2)]
    count = q_ref.shape[0] // step
    units = [(head, b) for b in reversed(range(count)) for head in range(2)]

    def products_of(head, b):
        columns = slice(b * step, b * step + step)
        end = b * step + step if causal else key_rows
        scores = product(keys[head][:end], queries[head][:, columns])
        return scores, product(values[:end], grads[head][:, columns])

    ahead = products_of(*units[0])
    for index, (head, b) in enumerate(units):
        scores, d_probs = ahead
        if index + 1 < len(units):
            ahead = products_of(*units[index + 1])
        rows = slice(64 * head, 64 * head + 64)
        columns = slice(b * step, b * step + step)
        end = scores.shape[0]
        if causal:
            scores = causal_mask(scores, step)
        probs = jnp.exp(scores - lse_ref[0, head : head + 1, columns])
        weighted = probs * d_probs
        delta = jnp.sum(weighted, axis=0, keepdims=True)
        d_scores = (weighted - probs * delta).astype(jnp.bfloat16)
        dv = product(probs.astype(jnp.bfloat16), do_ref[columns, :])
        dk = product(d_scores, q_ref[columns, :])
        if b == count - 1:
            dv_sum[head, :end] = dv
            dk_sum[head, :end] = dk
        else:
            dv_sum[head, :end] += dv
            dk_sum[head, :end] += dk
        dq_t[rows, columns] = product(k_t[rows, :end], d_scores)
    first = half_lanes((key_rows, 128), 1) < 64
    dk_ref[...] = jnp.where(first, dk_sum[0, :key_rows], dk_sum[1, :key_rows]).astype(jnp.bfloat16)
    dv = jnp.where(first, dv_sum[0, :key_rows], dv_sum[1, :key_rows]).astype(jnp.bfloat16)
    dv_ref[...] = dv
    dq = (dq_t[...] * 0.125).T.astype(jnp.bfloat16)
    dq_ref[...] = dq
    put_sums(
        jnp.sum(dq.astype(jnp.float32), axis=0, keepdims=True),
        jnp.sum(dv.astype(jnp.float32), axis=0, keepdims=True),
    )


SCALARS = pl.BlockSpec(memory_space=pltpu.SMEM)


def neighbours():
    rep = lax.axis_index("rep")
    z = lax.axis_index("shard")
    core = rep % 2
    x = (rep // 2) % 2
    y = rep // 4
    other_core = (rep + 1 - 2 * core, z)
    other_x = (rep + 2 - 4 * x, z)
    other_y = (rep + 4 - 8 * y, z)
    others_z = [(rep, (z + d) % 4) for d in (1, 2, 3)]
    return core, x, y, z, other_core, other_x, other_y, others_z


def greet(devices):
    barrier = pltpu.get_barrier_semaphore()
    for device in devices:
        pl.semaphore_signal(barrier, inc=1, device_id=device, device_id_type=MESH)
    pl.semaphore_wait(barrier, len(devices))


def remote(src, dst, send, recv, device):
    return pltpu.make_async_remote_copy(
        src_ref=src, dst_ref=dst, send_sem=send, recv_sem=recv, device_id=device, device_id_type=MESH
    )


def gather_copies(refs, c, parity, places):
    piece, full, place_sem, z_send, z_recv, send, recv = refs
    core, x, y, z, other_core, other_x, other_y, others_z = places
    a = x + parity * (y - x)
    b = y + parity * (x - y)
    first = (other_x[0] + parity * (other_y[0] - other_x[0]), z)
    second = (other_y[0] + parity * (other_x[0] - other_y[0]), z)
    own = pl.ds(pl.multiple_of(core * 128 + a * 64 + b * 32, 32), 32)
    steps = (
        (own, second),
        (pl.ds(pl.multiple_of(core * 128 + a * 64, 64), 64), first),
        (pl.ds(pl.multiple_of(core * 128, 128), 128), other_core),
    )

    def local():
        return pltpu.make_async_copy(piece.at[c], full.at[c, z, own, :], place_sem.at[c])

    def line(d):
        return remote(
            piece.at[c], full.at[c, z, own, :], z_send.at[c, d], z_recv.at[c, d], others_z[d]
        )

    def pair(k):
        block = full.at[c, :, steps[k][0], :]
        return remote(block, block, send.at[k, c], recv.at[k, c], steps[k][1])

    return local, line, pair


def gather_stage(k, refs, c, parity, places):
    local, line, pair = gather_copies(refs, c, parity, places)
    if k == 0:
        local().start()
        for d in range(3):
            line(d).start()
    if k == 1:
        local().wait()
        for d in range(3):
            line(d).wait_recv()
        pair(0).start()
    if k == 2 or k == 3:
        pair(k - 2).wait_recv()
        pair(k - 1).start()
    if k == 4:
        pair(2).wait()
        pair(1).wait_send()
        pair(0).wait_send()
        for d in range(3):
            line(d).wait_send()


def gather_sems(count):
    dma = pltpu.SemaphoreType.DMA
    return [dma((count,)), dma((count, 3)), dma((count, 3)), dma((3, count)), dma((3, count))]


def own_rows(blocks, parity, places):
    core, x, y = places[0:3]
    a = x + parity * (y - x)
    b = y + parity * (x - y)
    rows = lax.dynamic_slice_in_dim(blocks, core * 128 + a * 64 + b * 32, 32, axis=-2)
    return rows.astype(jnp.bfloat16)


def hidden_blocks(values):
    split = values.reshape(values.shape[:-1] + (4, 4, 256))
    split = jnp.swapaxes(split, -3, -2)
    return split.reshape(values.shape[:-1] + (4, 1024))


def hidden_flat(blocks):
    split = blocks.reshape(blocks.shape[:-2] + (4, 4, 256))
    split = jnp.swapaxes(split, -3, -2)
    return split.reshape(blocks.shape[:-2] + (FF,))


def weight_pieces(attention, expand, shrink, places):
    attention = jnp.swapaxes(
        jnp.stack([own_rows(jnp.swapaxes(attention, 0, 1), p, places) for p in range(2)]), 0, 1
    )
    picked = [attention[i, i % 2] for i in range(3)]
    picked = picked + [attention[3 + c, c % 2] for c in range(5)]
    ff = []
    for p in range(2):
        rows = own_rows(expand, p, places)
        ff.append(jnp.swapaxes(hidden_blocks(rows), 0, 1))
    for p in range(2):
        ff.append(own_rows(shrink.reshape(4, 256, D), p, places))
    for j in range(4):
        picked.append(ff[1][j])
        picked.append(ff[2][j])
    return jnp.stack(picked[0:3]), jnp.stack(picked[3:16])


def front_kernel(
    order_ref,
    tokens_ref,
    piece_ref,
    x_ref,
    full_ref,
    spread,
    picked,
    spread_send,
    spread_recv,
    back_send,
    back_recv,
    *gather_sem,
):
    places = neighbours()
    z = places[3]
    me = lax.axis_index("rep") * 4 + z
    refs = (piece_ref, full_ref) + gather_sem

    def device(offset):
        j = lax.rem(me + offset, 32)
        return j, (j // 4, j % 4)

    barrier = pltpu.get_barrier_semaphore()

    def greet_one(offset, carry):
        pl.semaphore_signal(barrier, inc=1, device_id=device(offset)[1], device_id_type=MESH)
        return carry

    lax.fori_loop(1, 32, greet_one, 0)
    pl.semaphore_wait(barrier, 31)

    def stage(k):
        for c in range(3):
            gather_stage(k, refs, c, c % 2, places)

    def spread_copy(offset):
        j, target = device(offset)
        return remote(
            tokens_ref.at[j],
            spread.at[me],
            spread_send.at[offset],
            spread_recv.at[offset],
            target,
        )

    def back_copy(offset):
        target = device(offset)[1]
        return remote(
            picked.at[offset], x_ref.at[me], back_send.at[offset], back_recv.at[offset], target
        )

    own_in = pltpu.make_async_copy(tokens_ref.at[me], spread.at[me], spread_recv.at[0])
    own_out = pltpu.make_async_copy(picked.at[0], x_ref.at[me], back_recv.at[0])
    stage(0)
    own_in.start()

    def start_spread(offset, carry):
        spread_copy(offset).start()
        return carry

    lax.fori_loop(1, 32, start_spread, 0)
    stage(1)
    stage(2)
    own_in.wait()

    def wait_spread(offset, carry):
        spread_copy(offset).wait()
        return carry

    lax.fori_loop(1, 32, wait_spread, 0)
    picked[0] = spread[order_ref[me]]
    own_out.start()

    def pick(offset, carry):
        picked[offset] = spread[order_ref[device(offset)[0]]]
        back_copy(offset).start()
        return carry

    lax.fori_loop(1, 32, pick, 0)
    stage(3)
    stage(4)
    own_out.wait()

    def wait_back(offset, carry):
        back_copy(offset).wait()
        return carry

    lax.fori_loop(1, 32, wait_back, 0)


def front(inverse, tokens, pieces):
    dma = pltpu.SemaphoreType.DMA
    any_space = pl.BlockSpec(memory_space=pl.ANY)
    x, full = pl.pallas_call(
        front_kernel,
        out_shape=(
            jax.ShapeDtypeStruct((32, 32, D), jnp.bfloat16),
            jax.ShapeDtypeStruct((3, 4, 256, D), jnp.bfloat16),
        ),
        in_specs=[
            pl.BlockSpec(memory_space=pltpu.SMEM),
            any_space,
            pl.BlockSpec(memory_space=pltpu.VMEM),
        ],
        out_specs=(any_space, any_space),
        scratch_shapes=[
            pltpu.VMEM((32, 32, D), jnp.bfloat16),
            pltpu.VMEM((32, 32, D), jnp.bfloat16),
            dma((32,)),
            dma((32,)),
            dma((32,)),
            dma((32,)),
        ]
        + gather_sems(3),
        compiler_params=pltpu.CompilerParams(
            collective_id=2, has_side_effects=True, vmem_limit_bytes=24 * MIB
        ),
    )(inverse, tokens.reshape(32, 32, D), pieces)
    return x.reshape(1024, D), full.reshape(3, 1024, D)


def fold(tile):
    return jnp.sum(tile.reshape(-1, 8, tile.shape[-1]), axis=0)


GATHERED = 13
GATHER_PLAN = (("z", 6.5), ("second", 6.5), ("first", 11.5), ("core", 3.0), (None, 0.0))


class GatherPlanner:
    def __init__(self, count):
        self.now = 0.0
        self.links = {"core": 0.0, "x": 0.0, "y": 0.0, "z": 0.0}
        self.stage = {c: 0 for c in range(count)}
        self.ready = {c: 0.0 for c in range(count)}

    def emit(self, c):
        stage = self.stage[c]
        link, span = GATHER_PLAN[stage]
        first, second = ("x", "y") if c % 2 == 0 else ("y", "x")
        link = {"first": first, "second": second}.get(link, link)
        self.now = max(self.now, self.ready[c]) + 0.1
        if link is not None:
            begin = max(self.now, self.links[link])
            self.links[link] = begin + span - 1.0
            self.ready[c] = begin + span
        self.stage[c] = stage + 1
        return (stage, c)

    def tick(self, spent):
        self.now += spent
        events = []
        progress = True
        while progress:
            progress = False
            for c in self.stage:
                if self.stage[c] < 5 and self.ready[c] <= self.now:
                    events.append(self.emit(c))
                    progress = True
        return events

    def until(self, c):
        events = []
        while self.stage[c] < 5:
            choices = [i for i in self.stage if self.stage[i] < 5]
            best = min(choices, key=lambda i: (self.ready[i], i))
            events.append(self.emit(best))
        return events


def gelu_parts(u):
    share = 0.5 + 0.5 * lax.erf(u * math.sqrt(0.5))
    bell = jnp.exp(-0.5 * u * u) * (1.0 / math.sqrt(2.0 * math.pi))
    return u * share, share + u * bell


def norm_parts(values):
    centred = values - jnp.mean(values, axis=1, keepdims=True)
    spread = jnp.mean(centred * centred, axis=1, keepdims=True)
    scale = lax.rsqrt(spread + NORM_EPS)
    return centred * scale, scale


def forward_kernel(
    lengths_ref,
    x_ref,
    qkv_ref,
    piece_ref,
    e_ref,
    cot_ref,
    par,
    full_ref,
    q_out,
    k_out,
    v_out,
    o_out,
    lse_out,
    cq_out,
    ck_out,
    cv_out,
    oc_out,
    lse_cross_out,
    r1_out,
    r2_out,
    h1_out,
    h2_out,
    g_out,
    gp_out,
    y_out,
    dm_out,
    d_third_out,
    small_out,
    pool,
    acc,
    held,
    o_t,
    lse_held,
    states,
    load_sem,
    store_sem,
    state_sem,
    acc_sem,
    *gather_sem,
):
    places = neighbours()
    refs = (piece_ref, full_ref) + gather_sem
    planner = GatherPlanner(GATHERED)
    length = lengths_ref[0]

    def emit_all(events):
        for stage, c in events:
            gather_stage(stage, refs, c, c % 2, places)

    def tick(spent):
        emit_all(planner.tick(spent))

    def load(slot, source):
        return pltpu.make_async_copy(source, pool.at[slot], load_sem.at[slot])

    def store(slot, target):
        return pltpu.make_async_copy(pool.at[slot], target, store_sem.at[slot])

    def product_into(left, right, put):
        def body(i, carry):
            n = pl.multiple_of(i * 256, 256)
            put(n, product(left(), pool[right, :, pl.ds(n, 256)]))
            return carry

        lax.fori_loop(0, 4, body, 0)

    def row(index, n):
        return par[index : index + 1, pl.ds(n, 256)]

    def put_low(slot, offset=None, scale=None):
        def put(n, value):
            if offset is not None:
                value = value + row(offset, n)
            if scale is not None:
                value = value * scale
            pool[slot, :, pl.ds(n, 256)] = value.astype(jnp.bfloat16)

        return put

    def put_acc(offset):
        def put(n, value):
            acc[:, pl.ds(n, 256)] = value + row(offset, n)

        return put

    def load_weight(c, slot):
        target = pool.at[slot].reshape(4, 256, D)
        return pltpu.make_async_copy(full_ref.at[c], target, load_sem.at[slot])

    def weight(c, slot):
        emit_all(planner.until(c))
        return load_weight(c, slot)

    def attend_loop(causal, step, valid, query, key, value, out, spent):
        ahead = [planner.tick(spent) for _ in range(8)]

        def body(i, carry):
            lanes = pl.ds(pl.multiple_of(i * 128, 128), 128)
            attend_pair(
                causal,
                step,
                valid,
                query.at[:, lanes],
                key.at[:, lanes],
                value.at[:, lanes],
                out.at[:, lanes],
                lse_held.at[pl.ds(i, 1)],
                o_t,
            )
            for n in range(8):
                if ahead[n]:

                    @pl.when(i == n)
                    def _(events=ahead[n]):
                        emit_all(events)

            return carry

        lax.fori_loop(0, 8, body, 0)

    TILE = 128

    def over_rows(sums, body):
        zero = jnp.zeros((8, D), jnp.float32)

        def step(i, carry):
            r = pl.multiple_of(i * TILE, TILE)
            place = half_lanes((TILE, 1), 0) + r
            usable = (place < length).astype(jnp.float32)
            terms = body(pl.ds(r, TILE), usable)
            return tuple(c + fold(t) for c, t in zip(carry, terms))

        totals = lax.fori_loop(0, D // TILE, step, (zero,) * sums)
        return [jnp.sum(t, axis=0, keepdims=True) for t in totals]

    lane = half_lanes((1, D), 1)

    def square_at(index, total):
        small_out[17:18, :] += jnp.where(lane == index, jnp.sum(total), 0.0)

    greet(list(places[4:7]) + places[7])
    load(0, x_ref).start()
    for i in range(3):
        load(1 + i, qkv_ref.at[i]).start()
    load(9, cot_ref).start()
    e_load = pltpu.make_async_copy(e_ref, states.at[2], state_sem.at[2])
    e_load.start()
    small_out[...] = jnp.zeros_like(small_out)
    tick(0.5)
    load(0, x_ref).wait()
    load(1, qkv_ref.at[0]).wait()
    product_into(lambda: pool[0], 1, put_low(4, 0, 0.125))
    store(4, q_out).start()
    tick(2.5)
    load(2, qkv_ref.at[1]).wait()
    product_into(lambda: pool[0], 2, put_low(5))
    store(5, k_out).start()
    tick(2.5)
    load(3, qkv_ref.at[2]).wait()
    product_into(lambda: pool[0], 3, put_low(6, 1))
    store(6, v_out).start()
    tick(2.5)

    attend_loop(True, 256, length, pool.at[4], pool.at[5], pool.at[6], pool.at[7], 4.8)
    store(7, o_out).start()
    lse_copy = pltpu.make_async_copy(lse_held, lse_out, state_sem.at[3])
    lse_copy.start()
    w_copy = weight(0, 1)
    w_copy.start()
    w_copy.wait()
    product_into(lambda: pool[7], 1, put_acc(2))
    tick(2.5)
    store(4, q_out).wait()

    def first_norm(rows, usable):
        x = pool[0, rows, :].astype(jnp.float32)
        a = acc[rows, :]
        total = x + a
        acc[rows, :] = total
        h = norm_parts(total)[0] * par[11:12, :] + par[12:13, :]
        held[rows, :] = h
        pool[4, rows, :] = h.astype(jnp.bfloat16)
        return usable * x * x, usable * a * a, usable * h * h

    for index, total in enumerate(over_rows(3, first_norm)):
        square_at(index, total)
    store(4, h1_out).start()
    r1_copy = pltpu.make_async_copy(acc, r1_out, acc_sem.at[0])
    r1_copy.start()
    tick(4.0)

    for c, slot in ((1, 2), (2, 3), (3, 1)):
        weight(c, slot).start()
    store(5, k_out).wait()
    load_weight(1, 2).wait()
    product_into(lambda: pool[4], 2, put_low(5, 3, 0.125))
    store(5, cq_out).start()
    w_copy = weight(4, 2)
    w_copy.start()
    tick(2.5)
    e_load.wait()
    load_weight(2, 3).wait()
    load_weight(3, 1).wait()

    def put_keys(n, value):
        states[0, :, pl.ds(n, 256)] = value.astype(jnp.bfloat16)

    def put_values(n, value):
        states[1, :, pl.ds(n, 256)] = (value + row(4, n)).astype(jnp.bfloat16)

    product_into(lambda: states[2], 3, put_keys)
    product_into(lambda: states[2], 1, put_values)
    state_stores = [
        pltpu.make_async_copy(states.at[0], ck_out, state_sem.at[0]),
        pltpu.make_async_copy(states.at[1], cv_out, state_sem.at[1]),
    ]
    for copy in state_stores:
        copy.start()
    tick(1.0)
    store(6, v_out).wait()
    lse_copy.wait()
    attend_loop(
        False, 512, lengths_ref[1], pool.at[5], states.at[0], states.at[1], pool.at[6], 1.6
    )
    store(6, oc_out).start()
    lse_copy = pltpu.make_async_copy(lse_held, lse_cross_out, state_sem.at[3])
    lse_copy.start()
    w_copy.wait()
    r1_copy.wait()
    product_into(lambda: pool[6], 2, put_acc(5))
    tick(2.5)
    weight(5, 0).start()
    weight(6, 2).start()
    store(7, o_out).wait()

    def second_norm(rows, usable):
        c = acc[rows, :]
        total = held[rows, :] + c
        acc[rows, :] = total
        h = norm_parts(total)[0] * par[13:14, :] + par[14:15, :]
        held[rows, :] = h
        pool[7, rows, :] = h.astype(jnp.bfloat16)
        return usable * c * c, usable * h * h

    for index, total in enumerate(over_rows(2, second_norm)):
        square_at(3 + index, total)
    store(7, h2_out).start()
    r2_copy = pltpu.make_async_copy(acc, r2_out, acc_sem.at[0])
    r2_copy.start()
    tick(4.0)

    store(4, h1_out).wait()
    store(5, cq_out).wait()
    g_slots, slope_slots = (4, 6), (5, 8)
    r2_copy.wait()
    store(6, oc_out).wait()
    for j in range(5):
        if j > 1:
            store(g_slots[j % 2], g_out.at[j - 2]).wait()
            store(slope_slots[j % 2], gp_out.at[j - 2]).wait()
        if j < 4:
            load_weight(5 + 2 * j, j % 2).wait()
        if j > 0:
            load_weight(4 + 2 * j, 2 + (j - 1) % 2).wait()

        def body(i, carry, j=j):
            n = pl.multiple_of(i * 256, 256)
            here = pl.ds(n, 256)
            if j < 4:
                u = product(pool[7], pool[j % 2, :, here]) + row(6 + j, n)
            if j > 0:
                more = product(pool[g_slots[(j - 1) % 2]], pool[2 + (j - 1) % 2, :, here])
                if j == 1:
                    acc[:, here] = more + row(10, n)
                else:
                    acc[:, here] += more
            if j < 4:
                g, slope = gelu_parts(u)
                pool[g_slots[j % 2], :, here] = g.astype(jnp.bfloat16)
                pool[slope_slots[j % 2], :, here] = slope.astype(jnp.bfloat16)
            return carry

        lax.fori_loop(0, 4, body, 0)
        if j < 4:
            store(g_slots[j % 2], g_out.at[j]).start()
            store(slope_slots[j % 2], gp_out.at[j]).start()
        tick(9.0 if j < 4 else 2.5)
        if j < 3:
            weight(7 + 2 * j, (j + 1) % 2).start()
            weight(8 + 2 * j, 2 + (j + 1) % 2).start()

    load(9, cot_ref).wait()

    def third_norm(rows, usable):
        m = acc[rows, :]
        unit, scale = norm_parts(held[rows, :] + m)
        gain = par[15:16, :]
        pool[0, rows, :] = (unit * gain + par[16:17, :]).astype(jnp.bfloat16)
        grad = pool[9, rows, :].astype(jnp.float32) * usable
        inner = grad * gain
        first = jnp.mean(inner, axis=1, keepdims=True)
        second = jnp.mean(inner * unit, axis=1, keepdims=True)
        back = scale * (inner - first - unit * second)
        acc[rows, :] = back
        low = back.astype(jnp.bfloat16)
        pool[1, rows, :] = low
        return usable * m * m, grad * unit, grad, low.astype(jnp.float32)

    m_total, gain_sum, shift_sum, offset_sum = over_rows(4, third_norm)
    square_at(5, m_total)
    small_out[15:16, :] = gain_sum
    small_out[16:17, :] = shift_sum
    small_out[10:11, :] = offset_sum
    last = [
        store(0, y_out),
        store(1, dm_out),
        pltpu.make_async_copy(acc, d_third_out, acc_sem.at[0]),
    ]
    for copy in last:
        copy.start()
    for c in range(GATHERED):
        emit_all(planner.until(c))
    for copy in last + state_stores + [lse_copy]:
        copy.wait()
    store(7, h2_out).wait()
    store(6, g_out.at[3]).wait()
    store(8, gp_out.at[3]).wait()


def forward(lengths, x, qkv_full, pieces, states, cotangent, params):
    any_space = pl.BlockSpec(memory_space=pl.ANY)
    vmem = pl.BlockSpec(memory_space=pltpu.VMEM)
    shape = jax.ShapeDtypeStruct
    dma = pltpu.SemaphoreType.DMA
    low = jnp.bfloat16
    wide = jnp.float32
    square = shape((1024, D), low)
    square_wide = shape((1024, D), wide)
    lse = shape((8, 8, 1024), wide)
    short = shape((128, D), low)
    blocks = shape((4, 1024, D), low)
    outs = (
        shape((GATHERED, 4, 256, D), low),
        square,
        square,
        square,
        square,
        lse,
        square,
        short,
        short,
        square,
        lse,
        square_wide,
        square_wide,
        square,
        square,
        blocks,
        blocks,
        square,
        square,
        square_wide,
        shape((24, D), wide),
    )
    return pl.pallas_call(
        forward_kernel,
        out_shape=outs,
        in_specs=[SCALARS] + [any_space] * 5 + [vmem],
        out_specs=(any_space,) * 20 + (vmem,),
        scratch_shapes=[
            pltpu.VMEM((10, 1024, D), low),
            pltpu.VMEM((1024, D), wide),
            pltpu.VMEM((1024, D), wide),
            pltpu.VMEM((128, 1024), wide),
            pltpu.VMEM((8, 8, 1024), wide),
            pltpu.VMEM((3, 128, D), low),
            dma((10,)),
            dma((10,)),
            dma((4,)),
            dma((1,)),
        ]
        + gather_sems(GATHERED),
        compiler_params=pltpu.CompilerParams(
            collective_id=3, has_side_effects=True, vmem_limit_bytes=56 * MIB
        ),
    )(lengths, x, qkv_full, pieces, states, cotangent, params)


def add_blocks(target, first, second, planes, rows, step):
    per_plane = rows // step

    def body(i, carry):
        s = i // per_plane
        r = pl.multiple_of((i % per_plane) * step, step)
        target(s, r, first(s, r) + second(s, r))
        return carry

    lax.fori_loop(0, planes * per_plane, body, 0)


POOL = 8
G_SLOTS = 3
R_SLOTS = 4
PLAN = {"core": 3.0, "load": 1.5, "a": 11.5, "b": 6.5, "z": 6.5, "bb": 2.5, "ba": 4.0, "bc": 2.0}


class Planner:
    def __init__(self):
        self.now = 0.0
        self.links = {"core": 0.0, "x": 0.0, "y": 0.0, "z": 0.0, "load": 0.0}
        self.stage = {}
        self.ready = {}

    def link_of(self, c, stage):
        first, second = ("x", "y") if c % 2 == 0 else ("y", "x")
        return {
            0: ("core", "core"),
            1: ("load", "load"),
            2: (first, "a"),
            3: (second, "b"),
            4: ("z", "z"),
            5: (second, "bb"),
            6: (first, "ba"),
            7: ("core", "bc"),
            8: (None, None),
        }[stage]

    def can(self, c):
        stage = self.stage[c]
        if stage > 8:
            return False
        if stage == 1 and c >= R_SLOTS and self.stage[c - R_SLOTS] <= 3:
            return False
        return True

    def emit(self, c):
        stage = self.stage[c]
        link, kind = self.link_of(c, stage)
        self.now = max(self.now, self.ready[c]) + {2: 0.8, 3: 0.5, 4: 0.3, 5: 0.2}.get(stage, 0.1)
        if link is not None:
            begin = max(self.now, self.links[link])
            span = PLAN[kind]
            self.links[link] = begin + span - 1.0
            self.ready[c] = begin + span
        self.stage[c] = stage + 1
        return (stage, c)

    def tick(self, spent):
        self.now += spent
        events = []
        progress = True
        while progress:
            progress = False
            for c in sorted(self.stage):
                if self.can(c) and self.ready[c] <= self.now:
                    events.append(self.emit(c))
                    progress = True
        return events

    def produce(self, c):
        self.stage[c] = 0
        self.ready[c] = self.now
        return [self.emit(c)]

    def until(self, done):
        events = []
        while not done():
            choices = [c for c in sorted(self.stage) if self.can(c)]
            c = min(choices, key=lambda i: (self.ready[i], i))
            events.append(self.emit(c))
        return events

    def free_slot(self, c):
        before = c - G_SLOTS
        if before < 0:
            return []
        return self.until(lambda: self.stage[before] > 2)

    def drain(self, tasks, spent):
        events = []
        waiting = list(tasks)
        while waiting or any(s <= 8 for s in self.stage.values()):
            choices = [c for c in sorted(self.stage) if self.can(c)]
            best = min(choices, key=lambda i: (self.ready[i], i)) if choices else None
            open_tasks = [t for t in waiting if all(self.stage[c] > 8 for c in t[0])]
            if open_tasks and (best is None or self.ready[best] > self.now):
                task = open_tasks[0]
                waiting.remove(task)
                self.now += spent
                events.append(("task", task[1]))
            else:
                events.append(self.emit(best))
        return events


def backward_kernel(
    lengths_ref,
    dm_ref,
    d_third_ref,
    g_ref,
    gp_ref,
    rest_ref,
    qkv_ref,
    h2_ref,
    h1_ref,
    x_in_ref,
    e_ref,
    oc_ref,
    o_ref,
    r1_ref,
    r2_ref,
    q_ref,
    k_ref,
    v_ref,
    cq_ref,
    ck_ref,
    cv_ref,
    lse_ref,
    lse_cross_ref,
    gains_ref,
    small_ref,
    rows_ref,
    cols_ref,
    token_grad_ref,
    state_grad_ref,
    out_ref,
    totals_ref,
    rows_out,
    cols_out,
    scale_out,
    half,
    pool,
    acc,
    made,
    summed,
    quarter,
    eighth,
    pieces,
    stream,
    dq_t,
    dk_sum,
    dv_sum,
    lse_held,
    states,
    states_t,
    small,
    small_in,
    small_sum,
    small_z,
    part,
    whole,
    load_sem,
    stream_sem,
    state_sem,
    half_sem,
    scan_sem,
    line_send_sem,
    line_recv_sem,
    send_sem,
    recv_sem,
    z_send_sem,
    z_recv_sem,
    place_sem,
    small_send_sem,
    small_recv_sem,
):
    core, x, y, z, other_core, other_x, other_y, others_z = neighbours()
    kept = pl.multiple_of(core * 128, 128)
    given = pl.multiple_of(128 - core * 128, 128)
    planner = Planner()
    place_of = (12, 8, 13, 9, 14, 10, 15, 11, 7, 4, 5, 6, 3, 0, 1, 2)

    def axes(c):
        if c % 2 == 0:
            return x, y, other_x, other_y
        return y, x, other_y, other_x

    def core_copy(c):
        source = made.at[c % G_SLOTS, :, pl.ds(given, 128), :]
        return remote(source, half.at[c], send_sem.at[0, c], recv_sem.at[0, c], other_core)

    def half_copy(c):
        return pltpu.make_async_copy(
            half.at[c], summed.at[c % R_SLOTS], half_sem.at[c % R_SLOTS]
        )

    def first_copy(c):
        a, b, first, second = axes(c)
        rows = pl.ds(pl.multiple_of(64 - a * 64, 64), 64)
        source = summed.at[c % R_SLOTS, :, rows, :]
        return remote(source, quarter.at[c], send_sem.at[1, c], recv_sem.at[1, c], first)

    def second_copy(c):
        a, b, first, second = axes(c)
        rows = pl.ds(pl.multiple_of(32 - b * 32, 32), 32)
        source = quarter.at[c, :, rows, :]
        return remote(source, eighth.at[c], send_sem.at[2, c], recv_sem.at[2, c], second)

    def z_copy(c, d):
        device = others_z[d]
        return remote(
            eighth.at[c, device[1]],
            pieces.at[c, d],
            z_send_sem.at[c, d],
            z_recv_sem.at[c, d],
            device,
        )

    def own_rows_of(c):
        a, b, first, second = axes(c)
        return pl.ds(pl.multiple_of(core * 128 + a * 64 + b * 32, 32), 32)

    def place_copy(c):
        return pltpu.make_async_copy(
            pieces.at[c, 0], out_ref.at[place_of[c], own_rows_of(c), :], place_sem.at[c]
        )

    def back_second(c):
        device = axes(c)[3]
        target = out_ref.at[place_of[c], own_rows_of(c), :]
        return remote(pieces.at[c, 0], target, send_sem.at[3, c], recv_sem.at[3, c], device)

    def back_first(c):
        a, b, first, second = axes(c)
        block = out_ref.at[place_of[c], pl.ds(pl.multiple_of(core * 128 + a * 64, 64), 64), :]
        return remote(block, block, send_sem.at[4, c], recv_sem.at[4, c], first)

    def back_core(c):
        block = out_ref.at[place_of[c], pl.ds(kept, 128), :]
        return remote(block, block, send_sem.at[5, c], recv_sem.at[5, c], other_core)

    def emit(stage, c):
        a, b, first, second = axes(c)
        slot = c % R_SLOTS
        if stage == 0:
            core_copy(c).start()
        if stage == 1:
            if c >= R_SLOTS:
                first_copy(c - R_SLOTS).wait_send()
            core_copy(c).wait_recv()
            half_copy(c).start()
        if stage == 2:
            half_copy(c).wait()

            def put(s, r, value):
                summed[slot, s, pl.ds(r, 32), :] = value

            add_blocks(
                put,
                lambda s, r: summed[slot, s, pl.ds(r, 32), :],
                lambda s, r: made[c % G_SLOTS, s, pl.ds(pl.multiple_of(kept + r, 32), 32), :],
                4,
                128,
                32,
            )
            first_copy(c).start()
            core_copy(c).wait_send()
        if stage == 3:
            first_copy(c).wait_recv()

            def put(s, r, value):
                quarter[c, s, pl.ds(r, 32), :] = value

            add_blocks(
                put,
                lambda s, r: quarter[c, s, pl.ds(r, 32), :],
                lambda s, r: summed[slot, s, pl.ds(pl.multiple_of(a * 64 + r, 32), 32), :],
                4,
                64,
                32,
            )
            second_copy(c).start()
        if stage == 4:
            second_copy(c).wait_recv()

            def put(s, r, value):
                eighth[c, s, pl.ds(r, 32), :] = value

            add_blocks(
                put,
                lambda s, r: eighth[c, s, pl.ds(r, 32), :],
                lambda s, r: quarter[c, s, pl.ds(pl.multiple_of(b * 32 + r, 32), 32), :],
                4,
                32,
                32,
            )
            for d in range(3):
                z_copy(c, d).start()
        if stage == 5:
            for d in range(3):
                z_copy(c, d).wait_recv()
            total = eighth[c, z].astype(jnp.float32)
            for d in range(3):
                total = total + pieces[c, d].astype(jnp.float32)
            pieces[c, 0] = total.astype(jnp.bfloat16)
            back_second(c).start()
            place_copy(c).start()
        if stage == 6:
            place_copy(c).wait()
            back_second(c).wait_recv()
            back_first(c).start()
        if stage == 7:
            back_first(c).wait_recv()
            back_core(c).start()
        if stage == 8:
            back_core(c).wait()
            back_first(c).wait_send()
            back_second(c).wait_send()
            for d in range(3):
                z_copy(c, d).wait_send()
            second_copy(c).wait_send()
            if c >= CHUNKS - R_SLOTS:
                first_copy(c).wait_send()

    def emit_all(events):
        for stage, c in events:
            emit(stage, c)

    def tick(spent):
        emit_all(planner.tick(spent))

    def produced(c, spent):
        planner.now += spent
        emit_all(planner.produce(c))
        emit_all(planner.tick(0.0))

    def load(slot, source):
        return pltpu.make_async_copy(source, pool.at[slot], load_sem.at[slot])

    def state_load(index, source):
        return pltpu.make_async_copy(source, states.at[index], state_sem.at[index])

    def turn_tile(target, source):
        def turn(n):
            pool[target, pl.ds(n, 256), :] = pool[source, :, pl.ds(n, 256)].T

        return turn

    def transpose_into(target, source):
        turn = turn_tile(target, source)

        def body(i, carry):
            turn(pl.multiple_of(i * 256, 256))
            return carry

        lax.fori_loop(0, 4, body, 0)

    def product_nn(left, right, put, beside=None):
        def body(i, carry):
            n = pl.multiple_of(i * 256, 256)
            if beside is not None:
                beside(n)
            put(n, product(left(), right(n)))
            return carry

        lax.fori_loop(0, 4, body, 0)

    def product_nt(left, right, put, beside=None):
        def body(i, carry):
            n = pl.multiple_of(i * 256, 256)
            if beside is not None:
                beside(n)
            put(
                n,
                lax.dot_general(
                    left(),
                    right(n),
                    (((1,), (1,)), ((), ())),
                    preferred_element_type=jnp.float32,
                ),
            )
            return carry

        lax.fori_loop(0, 4, body, 0)

    def columns_of(slot):
        return lambda n: pool[slot, :, pl.ds(n, 256)]

    def rows_of(slot):
        return lambda n: pool[slot, pl.ds(n, 256), :]

    def weight_grad(slot_in_made, left, right, beside=None):
        def put(n, value):
            low = value.astype(jnp.bfloat16).reshape(4, 256, 256)
            made[slot_in_made, :, :, pl.ds(n, 256)] = low

        product_nn(left, right, put, beside)

    def add_to_acc(n, value):
        acc[:, pl.ds(n, 256)] += value

    def put_in(slot):
        def put(n, value):
            pool[slot, :, pl.ds(n, 256)] = value.astype(jnp.bfloat16)

        return put

    def norm_back(source, gain_row, gain_at, shift_at, offset_at, target):
        tiles = 8
        rows = 1024 // tiles

        def fetch(i):
            place = pl.ds(pl.multiple_of(i * rows, rows), rows)
            return pltpu.make_async_copy(
                source.at[place, :], stream.at[i % 2], stream_sem.at[i % 2]
            )

        fetch(0).start()

        def body(i, carry):
            gain_sum, shift_sum, offset_sum = carry

            @pl.when(i + 1 < tiles)
            def _():
                fetch(i + 1).start()

            fetch(i).wait()
            r = pl.multiple_of(i * rows, rows)
            values = stream[i % 2]
            centred = values - jnp.mean(values, axis=1, keepdims=True)
            spread = jnp.mean(centred * centred, axis=1, keepdims=True)
            scale = lax.rsqrt(spread + NORM_EPS)
            unit = centred * scale
            grad = acc[pl.ds(r, rows), :]
            inner = grad * gains_ref[gain_row : gain_row + 1, :]
            first = jnp.mean(inner, axis=1, keepdims=True)
            second = jnp.mean(inner * unit, axis=1, keepdims=True)
            back = scale * (inner - first - unit * second)
            acc[pl.ds(r, rows), :] = back
            low = back.astype(jnp.bfloat16)
            pool[target, pl.ds(r, rows), :] = low
            return (
                gain_sum + fold(grad * unit),
                shift_sum + fold(grad),
                offset_sum + fold(low.astype(jnp.float32)),
            )

        zero = jnp.zeros((8, D), jnp.float32)
        sums = lax.fori_loop(0, tiles, body, (zero, zero, zero))
        for row, value in zip((gain_at, shift_at, offset_at), sums):
            small[row : row + 1, :] = jnp.sum(value, axis=0, keepdims=True)

    greet([other_core, other_x, other_y] + others_z)
    load(0, dm_ref).start()
    load(6, h2_ref).start()
    load(2, rest_ref.at[6]).start()
    load(3, gp_ref.at[0]).start()
    load(4, g_ref.at[0]).start()
    load(5, rest_ref.at[5]).start()
    acc_load = pltpu.make_async_copy(d_third_ref, acc, place_sem.at[0])
    acc_load.start()
    small[...] = small_ref[...]
    load(6, h2_ref).wait()
    transpose_into(1, 6)
    load(0, dm_ref).wait()
    acc_load.wait()

    planner.now = 4.0
    plan = []
    for j in range(4):
        entry = []
        planner.now += 3.5
        entry.append(planner.tick(0.0) + planner.free_slot(2 * j))
        planner.now += 2.5
        entry.append(planner.produce(2 * j) + planner.tick(0.0) + planner.free_slot(2 * j + 1))
        planner.now += 2.5
        entry.append(planner.produce(2 * j + 1) + planner.tick(0.0))
        entry.append(planner.tick(2.5))
        plan.append(entry)

    def emit_planned(j, place):
        for n in range(4):
            events = plan[n][place]
            if events:

                @pl.when(j == n)
                def _(events=events):
                    emit_all(events)

    def block(j, carry):
        last = j == 3
        load(2, rest_ref.at[6]).wait()
        load(3, gp_ref.at[0]).wait()

        def put_pre(n, value):
            low = (value * pool[3, :, pl.ds(n, 256)].astype(jnp.float32)).astype(jnp.bfloat16)
            pool[7, :, pl.ds(n, 256)] = low
            small[pl.ds(6 + j, 1), pl.ds(n, 256)] = jnp.sum(
                low.astype(jnp.float32), axis=0, keepdims=True
            )

        load(4, g_ref.at[0]).wait()
        product_nt(lambda: pool[0], rows_of(2), put_pre, turn_tile(6, 4))

        @pl.when(jnp.logical_not(last))
        def _():
            load(2, rest_ref.at[8 + 2 * j]).start()
            load(3, gp_ref.at[j + 1]).start()

        @pl.when(last)
        def _():
            load(2, rest_ref.at[4]).start()
            load(3, cq_ref).start()

        emit_planned(j, 0)

        @pl.when(jnp.logical_not(last))
        def _():
            load(4, g_ref.at[j + 1]).start()

        @pl.when(last)
        def _():
            load(4, oc_ref).start()

        weight_grad((2 * j) % G_SLOTS, lambda: pool[6], columns_of(0))
        emit_planned(j, 1)
        weight_grad((2 * j + 1) % G_SLOTS, lambda: pool[1], columns_of(7))
        emit_planned(j, 2)
        load(5, rest_ref.at[5]).wait()
        product_nt(lambda: pool[7], rows_of(5), add_to_acc)

        @pl.when(jnp.logical_not(last))
        def _():
            load(5, rest_ref.at[7 + 2 * j]).start()

        @pl.when(last)
        def _():
            load(5, rest_ref.at[1]).start()

        emit_planned(j, 3)
        return carry

    lax.fori_loop(0, 4, block, 0)

    load(7, h1_ref).start()
    state_loads = [state_load(0, ck_ref), state_load(1, cv_ref), state_load(2, e_ref)]
    for copy in state_loads:
        copy.start()
    lse_load = pltpu.make_async_copy(lse_cross_ref, lse_held, state_sem.at[3])
    lse_load.start()
    norm_back(r2_ref, 1, 13, 14, 5, 0)
    tick(4.0)
    load(4, oc_ref).wait()
    load(2, rest_ref.at[4]).wait()
    product_nt(lambda: pool[0], rows_of(2), put_in(4), turn_tile(6, 4))
    load(2, rest_ref.at[0]).start()
    tick(2.5)
    emit_all(planner.free_slot(8))
    load(7, h1_ref).wait()
    weight_grad(8 % G_SLOTS, lambda: pool[6], columns_of(0), turn_tile(1, 7))
    load(6, o_ref).start()
    load(7, rest_ref.at[2]).start()
    produced(8, 2.5)
    load(3, cq_ref).wait()
    for copy in state_loads:
        copy.wait()
    lse_load.wait()

    def attend_loop(causal, step, length, query, key, value, grad, rows, spent, span=(0, 8)):
        ahead = {n: planner.tick(spent) for n in range(*span)}

        def body(i, carry):
            lanes = pl.ds(pl.multiple_of(i * 128, 128), 128)

            def sums(dq, dv):
                small[rows[0] : rows[0] + 1, lanes] = dq
                small[rows[1] : rows[1] + 1, lanes] = dv

            attend_back_pair(
                causal,
                step,
                length,
                query.at[:, lanes],
                key.at[:, lanes],
                value.at[:, lanes],
                grad.at[:, lanes],
                lse_held.at[pl.ds(i, 1)],
                query.at[:, lanes],
                key.at[:, lanes],
                value.at[:, lanes],
                sums,
                dq_t,
                dk_sum,
                dv_sum,
            )
            for n in range(*span):
                if ahead[n]:

                    @pl.when(i == n)
                    def _(events=ahead[n]):
                        emit_all(events)

            return carry

        lax.fori_loop(*span, body, 0)

    attend_loop(
        False,
        512,
        lengths_ref[1],
        pool.at[3],
        states.at[0],
        states.at[1],
        pool.at[4],
        (3, 4),
        2.0,
    )
    lse_load = pltpu.make_async_copy(lse_ref, lse_held, state_sem.at[3])
    lse_load.start()
    emit_all(planner.free_slot(9))
    weight_grad(9 % G_SLOTS, lambda: pool[1], columns_of(3))
    produced(9, 2.5)
    load(5, rest_ref.at[1]).wait()
    load(6, o_ref).wait()
    product_nt(lambda: pool[3], rows_of(5), add_to_acc, turn_tile(1, 6))
    load(6, x_in_ref).start()
    load(5, rest_ref.at[3]).start()
    load(3, q_ref).start()
    tick(2.5)
    states_t[...] = states[2].T
    for c, index in ((10, 0), (11, 1)):
        emit_all(planner.free_slot(c))
        weight_grad(
            c % G_SLOTS, lambda: states_t[...], lambda n, i=index: states[i, :, pl.ds(n, 256)]
        )
        produced(c, 1.0)
    load(7, rest_ref.at[2]).wait()
    load(5, rest_ref.at[3]).wait()

    def state_part(n):
        dims = (((1,), (1,)), ((), ()))
        return lax.dot_general(
            states[0], pool[7, pl.ds(n, 256), :], dims, preferred_element_type=jnp.float32
        ) + lax.dot_general(
            states[1], pool[5, pl.ds(n, 256), :], dims, preferred_element_type=jnp.float32
        )

    def put_state(i, carry):
        n = pl.multiple_of(i * 256, 256)
        state_grad_ref[:, pl.ds(n, 256)] = state_part(n).astype(jnp.bfloat16)
        return carry

    lax.fori_loop(0, 4, put_state, 0)
    load(5, k_ref).start()
    load(7, v_ref).start()
    tick(1.0)

    norm_back(r1_ref, 0, 11, 12, 2, 0)
    tick(4.0)
    emit_all(planner.free_slot(12))
    weight_grad(12 % G_SLOTS, lambda: pool[1], columns_of(0))
    produced(12, 2.5)
    load(2, rest_ref.at[0]).wait()
    load(6, x_in_ref).wait()
    product_nt(lambda: pool[0], rows_of(2), put_in(4), turn_tile(1, 6))
    load(0, qkv_ref.at[0]).start()
    load(2, qkv_ref.at[1]).start()
    load(6, qkv_ref.at[2]).start()
    tick(2.5)
    load(3, q_ref).wait()
    load(5, k_ref).wait()
    load(7, v_ref).wait()
    lse_load.wait()
    def self_heads(span):
        refs = [pool.at[slot] for slot in (3, 5, 7, 4)]
        attend_loop(True, 256, lengths_ref[0], *refs, (0, 1), 5.0, span)

    def query_key_grad(c, half_of):
        def put(i, carry):
            n = pl.multiple_of((i % 2) * 256 + 512 * half_of, 256)
            value = product(pool[1], pool[3 + 2 * (i // 2), :, pl.ds(n, 256)])
            low = value.astype(jnp.bfloat16).reshape(4, 256, 256)
            made[c % G_SLOTS, :, :, pl.ds(pl.multiple_of(i * 256, 256), 256)] = low
            return carry

        emit_all(planner.free_slot(c))
        lax.fori_loop(0, 4, put, 0)
        produced(c, 2.5)

    self_heads((0, 4))
    query_key_grad(13, 0)
    self_heads((4, 8))

    def small_copy(k):
        source = small if k == 0 else small_sum.at[k - 1]
        device = (other_core, other_x, other_y)[k]
        return remote(source, small_in.at[k], small_send_sem.at[k], small_recv_sem.at[k], device)

    def small_z_copy(d):
        return remote(
            small_sum.at[2],
            small_z.at[z],
            small_send_sem.at[3 + d],
            small_recv_sem.at[3 + d],
            others_z[d],
        )

    def small_step(k):
        small_copy(k).wait()
        before = small[...] if k == 0 else small_sum[k - 1]
        small_sum[k] = before + small_in[k]
        if k < 2:
            small_copy(k + 1).start()
        else:
            small_z[z] = small_sum[2]
            for d in range(3):
                small_z_copy(d).start()

    small_copy(0).start()
    emit_all(planner.free_slot(14))
    weight_grad(14 % G_SLOTS, lambda: pool[1], columns_of(7))
    produced(14, 2.5)
    small_step(0)
    query_key_grad(15, 1)
    small_step(1)
    load(0, qkv_ref.at[0]).wait()
    product_nt(lambda: pool[3], rows_of(0), add_to_acc)
    tick(2.5)
    small_step(2)
    load(2, qkv_ref.at[1]).wait()
    product_nt(lambda: pool[5], rows_of(2), add_to_acc)
    tick(2.5)
    for d in range(3):
        small_z_copy(d).wait()
    totals_ref[...] = (small_z[0] + small_z[1]) + (small_z[2] + small_z[3])
    load(6, qkv_ref.at[2]).wait()

    def put_input(n, value):
        total = acc[:, pl.ds(n, 256)] + value
        pool[4, :, pl.ds(n, 256)] = total.astype(jnp.bfloat16)

    product_nt(lambda: pool[7], rows_of(6), put_input)
    token_copy = pltpu.make_async_copy(pool.at[4], token_grad_ref, load_sem.at[4])
    token_copy.start()
    tick(2.5)

    part[...] = jnp.zeros_like(part)

    def spot(place):
        return (0, 1, 2, 6)[place // 4], (place % 4) * 256

    def scan_load(place):
        slot, row = spot(place)
        return pltpu.make_async_copy(
            out_ref.at[place], pool.at[slot, pl.ds(row, 256), :], scan_sem.at[place]
        )

    scans = {}
    for i in range(2):
        scans[i] = ([(0, 512 * i, 512, i, 0), (2, 512 * i, 512, i, 512)], i, (13, 128 * i))
    for i in range(2, 8):
        scans[i] = ([(1 if i == 2 else i, 0, D, i, 0)], i, (13, 128 * i))
    scans[8] = ([(8 + i, 0, D, 8 + i, 0) for i in range(4)], 8, (14, 0))
    for i in range(4):
        scans[9 + i] = ([(12 + i, 0, D, 12, 0)], 9 + i, (14, 128))

    def scan(name):
        sources, row_lane, (total_row, total_lane) = scans[name]
        width = float(sum(source[2] for source in sources))
        step = 16 if name == 8 else 64

        def body(i, carry):
            cols, weights, total = carry
            r = pl.multiple_of(i * step, step)
            squares = []
            for place, lane, lanes, _, _ in sources:
                slot, row = spot(place)
                tile = pool[slot, pl.ds(row + r, step), lane : lane + lanes]
                squares.append(jnp.square(tile.astype(jnp.float32)))
            row_sum = sum(jnp.sum(square, axis=1, keepdims=True) for square in squares)
            rows = DECAY_RATE * rows_ref[pl.ds(r, step), row_lane : row_lane + 1] + (
                1.0 - DECAY_RATE
            ) * (row_sum / width + FACTOR_EPS)
            rows_out[pl.ds(r, step), row_lane : row_lane + 1] = rows
            inverse = 1.0 / rows
            cols = [c + fold(s) for c, s in zip(cols, squares)]
            weights = [w + fold(s * inverse) for w, s in zip(weights, squares)]
            return cols, weights, total + fold(rows)

        zeros = [jnp.zeros((8, source[2]), jnp.float32) for source in sources]
        cols, weights, total = lax.fori_loop(
            0, 256 // step, body, (zeros, zeros, jnp.zeros((8, 1), jnp.float32))
        )
        for (_, _, lanes, slot, lane), col, weighted in zip(sources, cols, weights):
            here = slice(lane, lane + lanes)
            part[slot : slot + 1, here] += jnp.sum(col, axis=0, keepdims=True)
            part[16 + slot : 17 + slot, here] += jnp.sum(weighted, axis=0, keepdims=True)
        part[total_row : total_row + 1, total_lane : total_lane + 128] += jnp.broadcast_to(
            jnp.sum(total), (1, 128)
        )

    chunk_at = {place: c for c, place in enumerate(place_of)}
    tasks = [
        ([chunk_at[source[0]] for source in scans[name][0]], name)
        for name in (9, 10, 11, 12, 8, 7, 4, 5, 6, 3, 2, 0, 1)
    ]
    loaded = set()
    for c in range(CHUNKS):
        if planner.stage[c] > 8:
            scan_load(place_of[c]).start()
    for first, second in planner.drain(tasks, 1.5):
        if first != "task":
            emit(first, second)
            if first == 8:
                scan_load(place_of[second]).start()
            continue
        for source in scans[second][0]:
            if source[0] not in loaded:
                loaded.add(source[0])
                scan_load(source[0]).wait()
        scan(second)
    total = line_sum(part, whole, line_send_sem, line_recv_sem, z, others_z)
    row_counts = [D] * 12 + [FF]
    means = [total[13:14, 128 * i : 128 * i + 1] / D for i in range(8)]
    means = means + [total[14:15, 0:1] / D] * 4 + [total[14:15, 128:129] / FF]
    cols_new, quotients = [], []
    for slot in range(13):
        new = DECAY_RATE * cols_ref[slot : slot + 1, :] + (1.0 - DECAY_RATE) * (
            total[slot : slot + 1] / row_counts[slot] + FACTOR_EPS
        )
        cols_new.append(new)
        quotients.append(jnp.sum(total[16 + slot : 17 + slot] / new, axis=1, keepdims=True))
        cols_out[slot : slot + 1, :] = new
    expand_quotient = quotients[8] + quotients[9] + quotients[10] + quotients[11]
    for slot in range(13):
        if slot < 8:
            mean_square = means[slot] * quotients[slot] / (D * D)
            rate = STEP_RATE * (OUT_GAIN if slot % 4 == 3 else 1.0)
        else:
            quotient = expand_quotient if slot < 12 else quotients[12]
            mean_square = means[slot] * quotient / (D * FF)
            rate = STEP_RATE
        factor = rate / jnp.maximum(1.0, jnp.sqrt(mean_square) / CLIP_LEVEL)
        scale_out[slot : slot + 1, :] = lax.rsqrt(cols_new[slot] / means[slot]) * factor
    token_copy.wait()


def backward(lengths, held, gains, small, factor_rows, factor_cols):
    any_space = pl.BlockSpec(memory_space=pl.ANY)
    vmem = pl.BlockSpec(memory_space=pltpu.VMEM)
    shape = jax.ShapeDtypeStruct
    dma = pltpu.SemaphoreType.DMA
    low = jnp.bfloat16
    wide = jnp.float32
    rows = small.shape[0]
    return pl.pallas_call(
        backward_kernel,
        out_shape=(
            shape((1024, D), low),
            shape((128, D), low),
            shape((CHUNKS, 256, D), low),
            shape(small.shape, wide),
            shape((256, 128), wide),
            shape((16, D), wide),
            shape((16, D), wide),
            shape((CHUNKS, 4, 128, D), low),
        ),
        in_specs=[SCALARS] + [any_space] * len(held) + [vmem] * 4,
        out_specs=(any_space, vmem, any_space, vmem, vmem, vmem, vmem, any_space),
        scratch_shapes=[
            pltpu.VMEM((POOL, 1024, D), low),
            pltpu.VMEM((1024, D), wide),
            pltpu.VMEM((G_SLOTS, 4, 256, D), low),
            pltpu.VMEM((R_SLOTS, 4, 128, D), low),
            pltpu.VMEM((CHUNKS, 4, 64, D), low),
            pltpu.VMEM((CHUNKS, 4, 32, D), low),
            pltpu.VMEM((CHUNKS, 3, 32, D), low),
            pltpu.VMEM((2, 128, D), wide),
            pltpu.VMEM((128, 1024), wide),
            pltpu.VMEM((2, 1024, 128), wide),
            pltpu.VMEM((2, 1024, 128), wide),
            pltpu.VMEM((8, 8, 1024), wide),
            pltpu.VMEM((3, 128, D), low),
            pltpu.VMEM((D, 128), low),
            pltpu.VMEM((rows, D), wide),
            pltpu.VMEM((3, rows, D), wide),
            pltpu.VMEM((3, rows, D), wide),
            pltpu.VMEM((4, rows, D), wide),
            pltpu.VMEM((32, D), wide),
            pltpu.VMEM((4, 32, D), wide),
            dma((POOL,)),
            dma((2,)),
            dma((4,)),
            dma((R_SLOTS,)),
            dma((CHUNKS,)),
            dma((3,)),
            dma((3,)),
            dma((6, CHUNKS)),
            dma((6, CHUNKS)),
            dma((CHUNKS, 3)),
            dma((CHUNKS, 3)),
            dma((CHUNKS,)),
            dma((6,)),
            dma((6,)),
        ],
        compiler_params=pltpu.CompilerParams(
            collective_id=0, has_side_effects=True, vmem_limit_bytes=62 * MIB
        ),
    )(lengths, *held, gains, small, factor_rows, factor_cols)[0:7]


def line_sum(part, whole, send_sem, recv_sem, z, others_z):
    copies = [
        remote(part, whole.at[z], send_sem.at[d], recv_sem.at[d], others_z[d]) for d in range(3)
    ]
    for copy in copies:
        copy.start()
    whole[z] = part[...]
    for copy in copies:
        copy.wait()
    return (whole[0] + whole[1]) + (whole[2] + whole[3])


def update_attention_kernel(
    grad_ref, weight_ref, rows_ref, scale_ref, grad_out, new_out, copy_out, grads, change
):
    block = grad_ref.shape[1]
    for i in range(8):
        rows = lax.rsqrt(rows_ref[:, i : i + 1])
        every = pl.ds(i, block, stride=8)
        for lane in range(8):
            columns = slice(lane * 128, lane * 128 + 128)
            if i < 2:
                start = 512 * i + 128 * (lane % 4)
                grad = grad_ref[2 * (lane // 4), :, start : start + 128]
            else:
                grad = grad_ref[1 if i == 2 else i, :, columns]
            grad = grad.astype(jnp.float32)
            grads[lane, every, :] = grad
            change[lane, every, :] = grad * rows * scale_ref[i : i + 1, columns]
    for lane in range(8):
        columns = slice(lane * 128, lane * 128 + 128)
        grad_out[:, columns] = grads[lane]
        new = weight_ref[:, columns] - change[lane]
        new_out[:, columns] = new
        copy_out[:, columns] = new.astype(jnp.bfloat16)


def update_attention(grads, weights, rows, scale):
    block = 32
    wide = pl.BlockSpec((block * 8, D), lambda i: (i, 0))
    shape = jax.ShapeDtypeStruct
    new = pl.pallas_call(
        update_attention_kernel,
        grid=(256 // block,),
        out_shape=(
            shape((2048, D), jnp.float32),
            shape((2048, D), jnp.float32),
            shape((2048, D), jnp.bfloat16),
        ),
        in_specs=[
            pl.BlockSpec((8, block, D), lambda i: (0, i, 0)),
            wide,
            pl.BlockSpec((block, 128), lambda i: (i, 0)),
            pl.BlockSpec((16, D), lambda i: (0, 0)),
        ],
        out_specs=(wide,) * 3,
        scratch_shapes=[pltpu.VMEM((8, block * 8, 128), jnp.float32)] * 2,
        compiler_params=pltpu.CompilerParams(vmem_limit_bytes=40 * MIB),
    )(grads, weights.reshape(2048, D), rows, scale)
    return [t.reshape(256, 8, D) for t in new]


def update_kernel(
    first, slots, grad_ref, weight_ref, rows_ref, scale_ref, grad_out, new_out, copy_out
):
    spans = 4 if slots == 4 else 1
    wide = D // spans
    for i in range(slots):
        grads = grad_ref[i].astype(jnp.float32)
        changes = grads * (lax.rsqrt(rows_ref[...]) * scale_ref[first + i : first + i + 1, :])
        for s in range(spans):
            start = s * D + i * wide
            columns = slice(start, start + wide)
            part = slice(s * wide, s * wide + wide)
            grad_out[:, columns] = grads[:, part]
            new = weight_ref[:, columns] - changes[:, part]
            new_out[:, columns] = new
            copy_out[:, columns] = new.astype(jnp.bfloat16)


def update_plain(grads, weights, rows, scale, first, slots, grad_map):
    count, width = weights.shape
    block = 128 // slots
    wide = pl.BlockSpec((block, width), lambda i: (i, 0))
    shape = jax.ShapeDtypeStruct
    return pl.pallas_call(
        lambda *refs: update_kernel(first, slots, *refs),
        grid=(count // block,),
        out_shape=(
            shape(weights.shape, jnp.float32),
            shape(weights.shape, jnp.float32),
            shape(weights.shape, jnp.bfloat16),
        ),
        in_specs=[
            pl.BlockSpec((slots, block, D), grad_map),
            wide,
            pl.BlockSpec((block, 1), lambda i: (i, 0)),
            pl.BlockSpec((16, D), lambda i: (0, 0)),
        ],
        out_specs=(wide,) * 3,
        compiler_params=pltpu.CompilerParams(vmem_limit_bytes=40 * MIB),
    )(grads, weights, rows, scale)


def update_direct(grads, rows, scale, attention_weights, expand_weight, shrink_weight):
    shr_rows = rows[:, 9:13].T.reshape(-1, 1)
    attention = update_attention(grads, attention_weights, rows, scale)
    expand = update_plain(grads, expand_weight, rows[:, 8:9], scale, 8, 4, lambda i: (2, i, 0))
    shrink = update_plain(
        grads, shrink_weight, shr_rows, scale, 12, 1, lambda i: (12 + i // 2, i % 2, 0)
    )
    return attention, expand, shrink, (rows[:, 0:8].T, rows[:, 8], shr_rows[:, 0])


def as_rows(vector):
    rows = -(-vector.shape[0] // 1024) * 8
    return jnp.pad(vector, (0, rows * 128 - vector.shape[0])).reshape(rows, 128)


def masked_scores(query_part, key_heads, first_row, valid_count, causal):
    scores = jnp.einsum("qhd,khd->hqk", query_part, key_heads, preferred_element_type=jnp.float32)
    key_places = jnp.arange(key_heads.shape[0], dtype=jnp.int32)[None, :]
    usable = key_places < valid_count
    if causal:
        query_places = first_row + jnp.arange(query_part.shape[0], dtype=jnp.int32)[:, None]
        usable = usable & (key_places <= query_places)
    return jnp.where(usable[None], scores, MASKED)


def attend_forward(queries, key_heads, values, valid_count, causal):
    query_rows = queries.shape[0]
    step_rows = min(512, query_rows)
    outputs, stored = ([], [])
    for b in range(query_rows // step_rows):
        first_row = b * step_rows
        key_end = first_row + step_rows if causal else key_heads.shape[0]
        scores = masked_scores(
            queries[first_row : first_row + step_rows],
            key_heads[:key_end],
            first_row,
            valid_count,
            causal,
        )
        row_max = jnp.max(scores, axis=-1, keepdims=True)
        raised = jnp.exp(scores - row_max)
        totals = jnp.sum(raised, axis=-1, keepdims=True)
        probs_low = (raised / totals).astype(jnp.bfloat16)
        outputs.append(
            jnp.einsum(
                "hqk,khd->qhd", probs_low, values[:key_end], preferred_element_type=jnp.float32
            )
        )
        stored.append(row_max + jnp.log(totals))
    return (jnp.concatenate(outputs, axis=0), stored)


def attend_backward(queries, key_heads, values, grad_out, stored, valid_count, causal):
    query_rows = queries.shape[0]
    key_rows = key_heads.shape[0]
    step_rows = min(512, query_rows)
    grad_queries = []
    grad_keys = jnp.zeros(key_heads.shape, jnp.float32)
    grad_values = jnp.zeros(values.shape, jnp.float32)
    for b in range(query_rows // step_rows):
        first_row = b * step_rows
        key_end = first_row + step_rows if causal else key_rows
        query_part = queries[first_row : first_row + step_rows]
        grad_part = grad_out[first_row : first_row + step_rows]
        scores = masked_scores(query_part, key_heads[:key_end], first_row, valid_count, causal)
        probs = jnp.exp(scores - stored[b])
        probs_low = probs.astype(jnp.bfloat16)
        grad_probs = jnp.einsum(
            "qhd,khd->hqk", grad_part, values[:key_end], preferred_element_type=jnp.float32
        )
        value_part = jnp.einsum(
            "hqk,qhd->khd", probs_low, grad_part, preferred_element_type=jnp.float32
        )
        grad_scores = probs * (grad_probs - jnp.sum(probs * grad_probs, axis=-1, keepdims=True))
        scores_low = grad_scores.astype(jnp.bfloat16)
        grad_queries.append(
            jnp.einsum(
                "hqk,khd->qhd", scores_low, key_heads[:key_end], preferred_element_type=jnp.float32
            )
        )
        key_part = jnp.einsum(
            "hqk,qhd->khd", scores_low, query_part, preferred_element_type=jnp.float32
        )
        padding = ((0, key_rows - key_end), (0, 0), (0, 0))
        grad_keys = grad_keys + jnp.pad(key_part, padding)
        grad_values = grad_values + jnp.pad(value_part, padding)
    return (jnp.concatenate(grad_queries, axis=0), grad_keys, grad_values)


def gather_rows(piece):
    return lax.all_gather(piece, ("shard", "rep"), axis=0, tiled=True)


def own_piece(block, replicas):
    rows = block.shape[0] // replicas
    return lax.dynamic_slice_in_dim(block, lax.axis_index("rep") * rows, rows, axis=0)


def scatter_rows(grad):
    piece = lax.psum_scatter(
        grad.astype(jnp.bfloat16), ("shard", "rep"), scatter_dimension=0, tiled=True
    )
    return lax.all_gather(piece, "rep", axis=0, tiled=True)


def local_factors(grad, rows):
    square = grad * grad
    rows_new = DECAY_RATE * rows + (1.0 - DECAY_RATE) * jnp.mean(square + FACTOR_EPS, axis=-1)
    col_part = jnp.sum(square + FACTOR_EPS, axis=0)
    weighted = jnp.sum(square / rows_new[..., None], axis=0)
    return rows_new, col_part, weighted, jnp.sum(rows_new, axis=0)


def finish_factors(grad, weight, rows_new, cols, col_sum, weighted, row_total, row_count, rate):
    cols_new = DECAY_RATE * cols + (1.0 - DECAY_RATE) * col_sum / row_count
    mean_rows = row_total / row_count
    mean_square = mean_rows * jnp.sum(weighted / cols_new, axis=-1) / (row_count * cols.shape[-1])
    factor = rate / jnp.maximum(1.0, jnp.sqrt(mean_square) / CLIP_LEVEL)
    scaled = lax.rsqrt(cols_new / mean_rows[..., None]) * factor[..., None]
    fresh = weight - grad * (lax.rsqrt(rows_new)[..., None] * scaled[None])
    return fresh, cols_new


def plain_device(
    tokens,
    encoder,
    cotangent,
    lengths,
    encoder_lengths,
    dealt_order,
    attention_weights,
    expand_weight,
    shrink_weight,
    small_params,
    attention_rows,
    attention_cols,
    expand_rows,
    expand_cols,
    shrink_rows,
    shrink_cols,
    small_moment,
):
    devices = lax.axis_size(("rep", "shard"))
    replicas = lax.axis_size("rep")
    shards = lax.axis_size("shard")
    slot_tokens = tokens.shape[0]
    slot_states = encoder.shape[0]
    position = lax.axis_index(("rep", "shard"))
    inverse = (
        jnp.zeros((devices,), jnp.int32).at[dealt_order].set(jnp.arange(devices, dtype=jnp.int32))
    )
    qkv_piece = own_piece(attention_weights[:, 0:3, :].reshape(-1, 3 * D), replicas)
    rest_piece = own_piece(attention_weights[:, 3:8, :].reshape(-1, 5 * D), replicas)
    qkv_full = gather_rows(qkv_piece.astype(jnp.bfloat16))
    rest_full = gather_rows(rest_piece.astype(jnp.bfloat16))
    expand_full = gather_rows(own_piece(expand_weight, replicas).astype(jnp.bfloat16))
    shrink_full = gather_rows(own_piece(shrink_weight, replicas).astype(jnp.bfloat16))
    spread = lax.all_to_all(
        tokens.reshape(devices, slot_tokens // devices, D),
        ("rep", "shard"),
        split_axis=0,
        concat_axis=0,
        tiled=True,
    )
    picked = jnp.take(spread, inverse, axis=0)
    tokens = lax.all_to_all(
        picked, ("rep", "shard"), split_axis=0, concat_axis=0, tiled=True
    ).reshape(slot_tokens, D)
    states = encoder
    incoming = cotangent
    valid_tokens = lengths[position]
    valid_states = encoder_lengths[position]
    matrices = [qkv_full[:, i * D : (i + 1) * D] for i in range(3)] + [
        rest_full[:, i * D : (i + 1) * D] for i in range(5)
    ]
    parts = unpack(small_params)
    token_heads = (slot_tokens, HEADS, HEAD_DIM)
    state_heads = (slot_states, HEADS, HEAD_DIM)
    q_self = ((forward_product(tokens, matrices[0]) + parts[0]) * 0.125).astype(
        jnp.bfloat16
    )
    k_self = forward_product(tokens, matrices[1]).astype(jnp.bfloat16)
    v_self = (forward_product(tokens, matrices[2]) + parts[1]).astype(jnp.bfloat16)
    o_self, lse_self = attend_forward(
        q_self.reshape(token_heads),
        k_self.reshape(token_heads),
        v_self.reshape(token_heads),
        valid_tokens,
        True,
    )
    o_self_low = o_self.reshape(slot_tokens, D).astype(jnp.bfloat16)
    branch_a = forward_product(o_self_low, matrices[3]) + parts[2]
    tokens_wide = tokens.astype(jnp.float32)
    hidden_one, norm_one_back = jax.vjp(layer_norm, tokens_wide + branch_a, parts[8], parts[9])
    hidden_one_low = hidden_one.astype(jnp.bfloat16)
    q_cross = (
        (forward_product(hidden_one_low, matrices[4]) + parts[3]) * 0.125
    ).astype(jnp.bfloat16)
    k_cross = forward_product(states, matrices[5]).astype(jnp.bfloat16)
    v_cross = (forward_product(states, matrices[6]) + parts[4]).astype(jnp.bfloat16)
    o_cross, lse_cross = attend_forward(
        q_cross.reshape(token_heads),
        k_cross.reshape(state_heads),
        v_cross.reshape(state_heads),
        valid_states,
        False,
    )
    o_cross_low = o_cross.reshape(slot_tokens, D).astype(jnp.bfloat16)
    branch_c = forward_product(o_cross_low, matrices[7]) + parts[5]
    hidden_two, norm_two_back = jax.vjp(layer_norm, hidden_one + branch_c, parts[10], parts[11])
    hidden_two_low = hidden_two.astype(jnp.bfloat16)
    pre_act = forward_product(hidden_two_low, expand_full) + parts[6]
    activated, gelu_back = jax.vjp(gelu_exact, pre_act)
    activated_low = activated.astype(jnp.bfloat16)
    branch_m = forward_product(activated_low, shrink_full) + parts[7]
    result, norm_three_back = jax.vjp(layer_norm, hidden_two + branch_m, parts[12], parts[13])
    usable_rows = (jnp.arange(slot_tokens, dtype=jnp.int32) < valid_tokens).astype(jnp.float32)[
        :, None
    ]
    squares = jnp.stack(
        [
            jnp.sum(usable_rows * t * t)
            for t in (tokens_wide, branch_a, hidden_one, branch_c, hidden_two, branch_m)
        ]
    )
    d_third, d_gain_three, d_shift_three = norm_three_back(
        incoming.astype(jnp.float32) * usable_rows
    )
    d_mlp = d_third.astype(jnp.bfloat16)
    grad_shrink = weight_product(activated_low, d_mlp)
    grad_shrink_offset = row_sum(d_mlp)
    d_activated = input_product(d_mlp, shrink_full)
    d_pre = gelu_back(d_activated)[0].astype(jnp.bfloat16)
    grad_expand = weight_product(hidden_two_low, d_pre)
    grad_expand_offset = row_sum(d_pre)
    d_hidden_two = d_third + input_product(d_pre, expand_full)
    d_second, d_gain_two, d_shift_two = norm_two_back(d_hidden_two)
    d_branch_c = d_second.astype(jnp.bfloat16)
    grad_cross_out = weight_product(o_cross_low, d_branch_c)
    grad_cross_out_offset = row_sum(d_branch_c)
    d_o_cross = input_product(d_branch_c, matrices[7]).astype(jnp.bfloat16)
    grad_cq, grad_ck, grad_cv = attend_backward(
        q_cross.reshape(token_heads),
        k_cross.reshape(state_heads),
        v_cross.reshape(state_heads),
        d_o_cross.reshape(token_heads),
        lse_cross,
        valid_states,
        False,
    )
    dq_cross = (grad_cq.reshape(slot_tokens, D) * 0.125).astype(jnp.bfloat16)
    dk_cross = grad_ck.reshape(slot_states, D).astype(jnp.bfloat16)
    dv_cross = grad_cv.reshape(slot_states, D).astype(jnp.bfloat16)
    grad_cross_query = weight_product(hidden_one_low, dq_cross)
    grad_cross_key = weight_product(states, dk_cross)
    grad_cross_value = weight_product(states, dv_cross)
    state_grad = input_product(dk_cross, matrices[5]) + input_product(
        dv_cross, matrices[6]
    )
    d_hidden_one = d_second + input_product(dq_cross, matrices[4])
    d_first, d_gain_one, d_shift_one = norm_one_back(d_hidden_one)
    d_branch_a = d_first.astype(jnp.bfloat16)
    grad_self_out = weight_product(o_self_low, d_branch_a)
    grad_self_out_offset = row_sum(d_branch_a)
    d_o_self = input_product(d_branch_a, matrices[3]).astype(jnp.bfloat16)
    grad_sq, grad_sk, grad_sv = attend_backward(
        q_self.reshape(token_heads),
        k_self.reshape(token_heads),
        v_self.reshape(token_heads),
        d_o_self.reshape(token_heads),
        lse_self,
        valid_tokens,
        True,
    )
    dq_self = (grad_sq.reshape(slot_tokens, D) * 0.125).astype(jnp.bfloat16)
    dk_self = grad_sk.reshape(slot_tokens, D).astype(jnp.bfloat16)
    dv_self = grad_sv.reshape(slot_tokens, D).astype(jnp.bfloat16)
    grad_self_query = weight_product(tokens, dq_self)
    grad_self_key = weight_product(tokens, dk_self)
    grad_self_value = weight_product(tokens, dv_self)
    token_grad = (
        d_first
        + input_product(dq_self, matrices[0])
        + input_product(dk_self, matrices[1])
        + input_product(dv_self, matrices[2])
    )
    small_partial = jnp.concatenate(
        [
            row_sum(dq_self),
            row_sum(dv_self),
            grad_self_out_offset,
            row_sum(dq_cross),
            row_sum(dv_cross),
            grad_cross_out_offset,
            grad_expand_offset,
            grad_shrink_offset,
            d_gain_one,
            d_shift_one,
            d_gain_two,
            d_shift_two,
            d_gain_three,
            d_shift_three,
        ]
    )
    totals = lax.psum(jnp.concatenate([small_partial, squares]), ("rep", "shard"))
    g_shrink = scatter_rows(grad_shrink)
    g_expand = scatter_rows(grad_expand)
    g_rest = scatter_rows(
        jnp.concatenate(
            [grad_self_out, grad_cross_query, grad_cross_key, grad_cross_value, grad_cross_out],
            axis=1,
        )
    )
    g_qkv = scatter_rows(
        jnp.concatenate([grad_self_query, grad_self_key, grad_self_value], axis=1)
    )
    g_attention = (
        jnp.concatenate([g_qkv, g_rest], axis=1).reshape(-1, 8, D).astype(jnp.float32)
    )
    g_expand = g_expand.astype(jnp.float32)
    g_shrink = g_shrink.astype(jnp.float32)
    attention_rows_new, *attention_parts = local_factors(g_attention, attention_rows.T)
    expand_rows_new, *expand_parts = local_factors(g_expand, expand_rows)
    shrink_rows_new, *shrink_parts = local_factors(g_shrink, shrink_rows)
    flat = attention_parts + expand_parts + shrink_parts
    summed = lax.psum(jnp.concatenate([t.reshape(-1) for t in flat]), "shard")
    sums = []
    offset = 0
    for t in flat:
        sums.append(summed[offset : offset + t.size].reshape(t.shape))
        offset = offset + t.size
    attention_rates = STEP_RATE * jnp.where(jnp.arange(8) % 4 == 3, OUT_GAIN, 1.0).astype(
        jnp.float32
    )
    attention_new, attention_cols_new = finish_factors(
        g_attention,
        attention_weights,
        attention_rows_new,
        attention_cols,
        *sums[0:3],
        D,
        attention_rates,
    )
    expand_new, expand_cols_new = finish_factors(
        g_expand, expand_weight, expand_rows_new, expand_cols, *sums[3:6], D, STEP_RATE
    )
    shrink_new, shrink_cols_new = finish_factors(
        g_shrink, shrink_weight, shrink_rows_new, shrink_cols, *sums[6:9], FF, STEP_RATE
    )
    small_grad = totals[: small_params.shape[0]]
    small_moment_new = DECAY_RATE * small_moment + (1.0 - DECAY_RATE) * (
        small_grad * small_grad + FACTOR_EPS
    )
    small_update = small_grad * lax.rsqrt(small_moment_new)
    small_scale = jnp.sqrt(jnp.mean(small_update * small_update))
    small_new = small_params - SMALL_RATE * small_update / jnp.maximum(
        1.0, small_scale / CLIP_LEVEL
    )
    norm_stats = jnp.sqrt(
        totals[small_params.shape[0] :] / (jnp.sum(lengths).astype(jnp.float32) * D)
    )
    return (
        result.astype(jnp.bfloat16),
        token_grad.astype(jnp.bfloat16),
        state_grad.astype(jnp.bfloat16),
        g_attention,
        g_expand,
        g_shrink,
        small_grad,
        attention_new,
        expand_new,
        shrink_new,
        small_new,
        attention_new.astype(jnp.bfloat16),
        expand_new.astype(jnp.bfloat16),
        shrink_new.astype(jnp.bfloat16),
        attention_rows_new.T,
        attention_cols_new,
        expand_rows_new,
        expand_cols_new,
        shrink_rows_new,
        shrink_cols_new,
        small_moment_new,
        norm_stats,
    )


def direct_device(
    tokens,
    encoder,
    cotangent,
    lengths,
    encoder_lengths,
    dealt_order,
    attention_weights,
    expand_weight,
    shrink_weight,
    small_params,
    attention_rows,
    attention_cols,
    expand_rows,
    expand_cols,
    shrink_rows,
    shrink_cols,
    small_moment,
):
    position = lax.axis_index(("rep", "shard"))
    inverse = jnp.zeros((32,), jnp.int32).at[dealt_order].set(jnp.arange(32, dtype=jnp.int32))
    valid = jnp.stack([lengths[position], encoder_lengths[position]])
    parts = unpack(small_params)
    blank = jnp.zeros((D,), jnp.float32)
    params = jnp.concatenate(
        [
            small_params[0 : 6 * D].reshape(6, D),
            hidden_blocks(parts[6]),
            small_params[6 * D + FF :].reshape(7, D),
            jnp.zeros((7, D), jnp.float32),
        ]
    )
    gains = jnp.stack([parts[8], parts[10]] + [blank] * 6)
    qkv_pieces, rest_pieces = weight_pieces(
        attention_weights, expand_weight, shrink_weight, neighbours()
    )
    tokens, qkv_full = front(inverse, tokens, qkv_pieces)
    (
        rest_full,
        q_self,
        k_self,
        v_self,
        o_self,
        lse_self,
        q_cross,
        k_cross,
        v_cross,
        o_cross,
        lse_cross,
        summed_one,
        summed_two,
        hidden_one,
        hidden_two,
        activated,
        slope,
        output,
        d_mlp,
        d_third,
        small_first,
    ) = forward(valid, tokens, qkv_full, rest_pieces, encoder, cotangent, params)
    factor_rows = jnp.concatenate(
        [attention_rows, expand_rows.reshape(1, 256), shrink_rows.reshape(4, 256)]
    )
    factor_rows = jnp.pad(factor_rows.T, ((0, 0), (0, 115)))
    factor_cols = jnp.concatenate(
        [attention_cols, hidden_blocks(expand_cols), shrink_cols.reshape(1, D), jnp.ones((3, D))]
    )
    token_grad, state_grad, reduced, totals, factor_rows, factor_cols, scale = backward(
        valid,
        (
            d_mlp,
            d_third,
            activated,
            slope,
            rest_full.reshape(GATHERED, 1024, D),
            qkv_full,
            hidden_two,
            hidden_one,
            tokens,
            encoder,
            o_cross,
            o_self,
            summed_one,
            summed_two,
            q_self,
            k_self,
            v_self,
            q_cross,
            k_cross,
            v_cross,
            lse_self,
            lse_cross,
        ),
        gains,
        small_first,
        factor_rows,
        factor_cols,
    )
    attention, expand, shrink, rows_new = update_direct(
        reduced, factor_rows, scale, attention_weights, expand_weight, shrink_weight
    )
    cols_new = (factor_cols[0:8], hidden_flat(factor_cols[8:12]), factor_cols[12])
    small_grad = jnp.concatenate(
        [totals[0:6].reshape(-1), hidden_flat(totals[6:10]), totals[10:17].reshape(-1)]
    )
    small_moment_new = DECAY_RATE * small_moment + (1.0 - DECAY_RATE) * (
        small_grad * small_grad + FACTOR_EPS
    )
    small_update = small_grad * lax.rsqrt(small_moment_new)
    small_scale = jnp.sqrt(jnp.mean(small_update * small_update))
    small_new = small_params - SMALL_RATE * small_update / jnp.maximum(
        1.0, small_scale / CLIP_LEVEL
    )
    norm_stats = jnp.sqrt(totals[17, 0:6] / (jnp.sum(lengths).astype(jnp.float32) * D))
    return (
        output,
        token_grad,
        state_grad,
        attention[0],
        expand[0],
        shrink[0],
        small_grad,
        attention[1],
        expand[1],
        shrink[1],
        small_new,
        attention[2],
        expand[2],
        shrink[2],
        rows_new[0],
        cols_new[0],
        rows_new[1],
        cols_new[1],
        rows_new[2],
        cols_new[2],
        small_moment_new,
        norm_stats,
    )


def on_device(*args):
    if lax.axis_size("rep") == 8 and lax.axis_size("shard") == 4:
        return direct_device(*args)
    return plain_device(*args)


def solution(mesh):
    in_specs = (
        P(("rep", "shard"), None),
        P(("rep", "shard"), None),
        P(("rep", "shard"), None),
        P(),
        P(),
        P(),
        P("shard", None, None),
        P("shard", None),
        P("shard", None),
        P(),
        P(None, "shard"),
        P(),
        P("shard"),
        P(),
        P("shard"),
        P(),
        P(),
    )
    out_specs = (
        P(("rep", "shard"), None),
        P(("rep", "shard"), None),
        P(("rep", "shard"), None),
        P("shard", None, None),
        P("shard", None),
        P("shard", None),
        P(),
        P("shard", None, None),
        P("shard", None),
        P("shard", None),
        P(),
        P("shard", None, None),
        P("shard", None),
        P("shard", None),
        P(None, "shard"),
        P(),
        P("shard"),
        P(),
        P("shard"),
        P(),
        P(),
        P(),
    )
    return jax.shard_map(
        on_device, mesh=mesh, in_specs=in_specs, out_specs=out_specs, check_vma=False
    )
```

```python
import math

import jax
import jax.numpy as jnp
from jax import lax
from jax.experimental import pallas as pl
from jax.experimental.pallas import tpu as pltpu
from jax.sharding import PartitionSpec as P

D = 1024
HEADS = 16
HEAD_DIM = 64
FF = 4096


DECAY_RATE = 0.5
CLIP_LEVEL = 0.25
STEP_RATE = 0.1
SMALL_RATE = 0.4
OUT_GAIN = 8.0
NORM_EPS = 1e-05
FACTOR_EPS = 1e-30
MASKED = -1e30
MESH = pl.DeviceIdType.MESH
CHUNKS = 16
GATHERED = 16
EXPAND_AT = (8, 9, 11, 13)
SHRINK_AT = (10, 12, 14, 15)
MIB = 1 << 20


def layer_norm(r, norm_gain, norm_shift):
    centred = r - jnp.mean(r, axis=-1, keepdims=True)
    spread = jnp.mean(centred * centred, axis=-1, keepdims=True)
    return centred * lax.rsqrt(spread + NORM_EPS) * norm_gain + norm_shift


def gelu_exact(values):
    return jax.nn.gelu(values, approximate=False)


def unpack(small):
    extents = [D] * 6 + [FF] + [D] * 7
    pieces = []
    offset = 0
    for extent in extents:
        pieces.append(small[offset : offset + extent])
        offset = offset + extent
    return pieces


def forward_product(source, matrix):
    return jnp.dot(source, matrix, preferred_element_type=jnp.float32)


def input_product(grad_low, matrix):
    return jnp.einsum("to,io->ti", grad_low, matrix, preferred_element_type=jnp.float32)


def weight_product(source, grad_low):
    return jnp.einsum("ti,to->io", source, grad_low, preferred_element_type=jnp.float32)


def row_sum(grad_low):
    return jnp.sum(grad_low.astype(jnp.float32), axis=0)


def transposed(block):
    return block.astype(jnp.float32).T.astype(jnp.bfloat16)


def half_lanes(shape, dim):
    return lax.broadcasted_iota(jnp.int32, shape, dim)


def masked_keys(keys, length, head):
    place = half_lanes(keys.shape, 0)
    lane = half_lanes(keys.shape, 1)
    blocked = jnp.where((lane == 64 - 64 * head) & (place >= length), MASKED, 0.0)
    own = (lane >= 64 * head) & (lane < 64 * head + 64)
    return jnp.where(own, keys.astype(jnp.float32), blocked).astype(jnp.bfloat16)


def own_head(rows_t, head, fill):
    place = half_lanes(rows_t.shape, 0)
    own = (place >= 64 * head) & (place < 64 * head + 64)
    other = jnp.where(place == 64 - 64 * head, fill, 0.0)
    return jnp.where(own, rows_t.astype(jnp.float32), other).astype(jnp.bfloat16)


def product(first, second):
    return jnp.dot(first, second, preferred_element_type=jnp.float32)


def causal_mask(scores, step):
    kept = scores.shape[0] - step
    last = scores[kept:]
    allowed = half_lanes(last.shape, 0) <= half_lanes(last.shape, 1)
    last = jnp.where(allowed, last, MASKED)
    return last if kept == 0 else jnp.concatenate([scores[:kept], last], axis=0)


def attend_pair(
    causal, step, length, q_ref, k_ref, v_ref, o_ref, lse_ref, o_t, first_row=0
):
    count = q_ref.shape[0]
    q_t = transposed(q_ref[...])
    v_t = transposed(v_ref[...])
    keys = [masked_keys(k_ref[...], length, head) for head in range(2)]
    queries = [own_head(q_t, head, 1.0) for head in range(2)]
    units = [(head, start) for start in range(0, count, step) for head in range(2)]

    def scores_of(head, start):
        end = first_row + start + step if causal else k_ref.shape[0]
        return product(keys[head][:end], queries[head][:, start : start + step])

    ahead = scores_of(*units[0])
    for index, (head, start) in enumerate(units):
        scores = ahead
        if index + 1 < len(units):
            ahead = scores_of(*units[index + 1])
        rows = slice(64 * head, 64 * head + 64)
        columns = slice(start, start + step)
        if causal:
            scores = causal_mask(scores, step)
        top = jnp.max(scores, axis=0, keepdims=True)
        raised = jnp.exp(scores - top)
        total = jnp.sum(raised, axis=0, keepdims=True)
        probs = (raised * (1.0 / total)).astype(jnp.bfloat16)
        o_t[rows, columns] = product(v_t[rows, : scores.shape[0]], probs)
        place = slice(first_row + start, first_row + start + step)
        lse_ref[0, head : head + 1, place] = top + jnp.log(total)
    o_ref[...] = o_t[:, :count].T.astype(jnp.bfloat16)


def attend_back_pair(
    causal,
    step,
    length,
    q_ref,
    k_ref,
    v_ref,
    do_ref,
    lse_ref,
    dq_ref,
    dk_ref,
    dv_ref,
    put_sums,
    dq_t,
    dk_sum,
    dv_sum,
):
    key_rows = k_ref.shape[0]
    q_t = transposed(q_ref[...])
    k_t = transposed(k_ref[...])
    do_t = transposed(do_ref[...])
    values = v_ref[...]
    keys = [masked_keys(k_ref[...], length, head) for head in range(2)]
    queries = [own_head(q_t, head, 1.0) for head in range(2)]
    grads = [own_head(do_t, head, 0.0) for head in range(2)]
    count = q_ref.shape[0] // step
    units = [(head, b) for b in reversed(range(count)) for head in range(2)]

    def products_of(head, b):
        columns = slice(b * step, b * step + step)
        end = b * step + step if causal else key_rows
        scores = product(keys[head][:end], queries[head][:, columns])
        return scores, product(values[:end], grads[head][:, columns])

    ahead = products_of(*units[0])
    for index, (head, b) in enumerate(units):
        scores, d_probs = ahead
        if index + 1 < len(units):
            ahead = products_of(*units[index + 1])
        rows = slice(64 * head, 64 * head + 64)
        columns = slice(b * step, b * step + step)
        end = scores.shape[0]
        if causal:
            scores = causal_mask(scores, step)
        probs = jnp.exp(scores - lse_ref[0, head : head + 1, columns])
        weighted = probs * d_probs
        delta = jnp.sum(weighted, axis=0, keepdims=True)
        d_scores = (weighted - probs * delta).astype(jnp.bfloat16)
        dv = product(probs.astype(jnp.bfloat16), do_ref[columns, :])
        dk = product(d_scores, q_ref[columns, :])
        if b == count - 1:
            dv_sum[head, :end] = dv
            dk_sum[head, :end] = dk
        else:
            dv_sum[head, :end] += dv
            dk_sum[head, :end] += dk
        dq_t[rows, columns] = product(k_t[rows, :end], d_scores)
    first = half_lanes((key_rows, 128), 1) < 64
    dk_ref[...] = jnp.where(first, dk_sum[0, :key_rows], dk_sum[1, :key_rows]).astype(jnp.bfloat16)
    dv = jnp.where(first, dv_sum[0, :key_rows], dv_sum[1, :key_rows]).astype(jnp.bfloat16)
    dv_ref[...] = dv
    dq = (dq_t[...] * 0.125).T.astype(jnp.bfloat16)
    dq_ref[...] = dq
    put_sums(
        jnp.sum(dq.astype(jnp.float32), axis=0, keepdims=True),
        jnp.sum(dv.astype(jnp.float32), axis=0, keepdims=True),
    )


SCALARS = pl.BlockSpec(memory_space=pltpu.SMEM)


def neighbours():
    rep = lax.axis_index("rep")
    z = lax.axis_index("shard")
    core = rep % 2
    x = (rep // 2) % 2
    y = rep // 4
    other_core = (rep + 1 - 2 * core, z)
    other_x = (rep + 2 - 4 * x, z)
    other_y = (rep + 4 - 8 * y, z)
    others_z = [(rep, (z + d) % 4) for d in (1, 2, 3)]
    return core, x, y, z, other_core, other_x, other_y, others_z


def greet(devices):
    barrier = pltpu.get_barrier_semaphore()
    for device in devices:
        pl.semaphore_signal(barrier, inc=1, device_id=device, device_id_type=MESH)
    pl.semaphore_wait(barrier, len(devices))


def remote(src, dst, send, recv, device):
    return pltpu.make_async_remote_copy(
        src_ref=src, dst_ref=dst, send_sem=send, recv_sem=recv, device_id=device, device_id_type=MESH
    )


def gather_copies(refs, c, parity, places):
    piece, full, place_sem, z_send, z_recv, send, recv = refs
    core, x, y, z, other_core, other_x, other_y, others_z = places
    a = x + parity * (y - x)
    b = y + parity * (x - y)
    first = (other_x[0] + parity * (other_y[0] - other_x[0]), z)
    second = (other_y[0] + parity * (other_x[0] - other_y[0]), z)
    own = pl.ds(pl.multiple_of(core * 128 + a * 64 + b * 32, 32), 32)
    steps = (
        (own, second),
        (pl.ds(pl.multiple_of(core * 128 + a * 64, 64), 64), first),
        (pl.ds(pl.multiple_of(core * 128, 128), 128), other_core),
    )

    def local():
        return pltpu.make_async_copy(piece.at[c], full.at[c, z, own, :], place_sem.at[c])

    def line(d):
        return remote(
            piece.at[c], full.at[c, z, own, :], z_send.at[c, d], z_recv.at[c, d], others_z[d]
        )

    def pair(k):
        block = full.at[c, :, steps[k][0], :]
        return remote(block, block, send.at[k, c], recv.at[k, c], steps[k][1])

    return local, line, pair


def gather_stage(k, refs, c, parity, places):
    local, line, pair = gather_copies(refs, c, parity, places)
    if k == 0:
        local().start()
        for d in range(3):
            line(d).start()
    if k == 1:
        local().wait()
        for d in range(3):
            line(d).wait_recv()
        pair(0).start()
    if k == 2 or k == 3:
        pair(k - 2).wait_recv()
        pair(k - 1).start()
    if k == 4:
        pair(2).wait()
        pair(1).wait_send()
        pair(0).wait_send()
        for d in range(3):
            line(d).wait_send()


def gather_sems(count):
    dma = pltpu.SemaphoreType.DMA
    return [dma((count,)), dma((count, 3)), dma((count, 3)), dma((3, count)), dma((3, count))]


def own_rows(blocks, parity, places):
    core, x, y = places[0:3]
    a = x + parity * (y - x)
    b = y + parity * (x - y)
    rows = lax.dynamic_slice_in_dim(blocks, core * 128 + a * 64 + b * 32, 32, axis=-2)
    return rows.astype(jnp.bfloat16)


def hidden_blocks(values):
    split = values.reshape(values.shape[:-1] + (4, 4, 256))
    split = jnp.swapaxes(split, -3, -2)
    return split.reshape(values.shape[:-1] + (4, 1024))


def hidden_flat(blocks):
    split = blocks.reshape(blocks.shape[:-2] + (4, 4, 256))
    split = jnp.swapaxes(split, -3, -2)
    return split.reshape(blocks.shape[:-2] + (FF,))


def weight_pieces(attention, expand, shrink, places):
    attention = [own_rows(jnp.swapaxes(attention, 0, 1), p, places) for p in range(2)]
    expand = [jnp.swapaxes(hidden_blocks(own_rows(expand, p, places)), 0, 1) for p in range(2)]
    shrink = [own_rows(shrink.reshape(4, 256, D), p, places) for p in range(2)]
    picked = [attention[c % 2][c] for c in range(8)]
    for c in range(8, GATHERED):
        if c in EXPAND_AT:
            picked.append(expand[c % 2][EXPAND_AT.index(c)])
        else:
            picked.append(shrink[c % 2][SHRINK_AT.index(c)])
    return jnp.stack(picked)


def fold(tile):
    return jnp.sum(tile.reshape(-1, 8, tile.shape[-1]), axis=0)


GATHER_PLAN = (("z", 6.5), ("second", 6.5), ("first", 11.5), ("core", 3.0), (None, 0.0))


class GatherPlanner:
    def __init__(self, count):
        self.now = 0.0
        self.links = {"core": 0.0, "x": 0.0, "y": 0.0, "z": 0.0}
        self.stage = {c: 0 for c in range(count)}
        self.ready = {c: 0.0 for c in range(count)}
        self.opened = count

    def spend(self, now, **busy):
        self.now = max(self.now, now)
        for link, span in busy.items():
            self.links[link] = max(self.links[link], self.now) + span

    def emit(self, c):
        stage = self.stage[c]
        link, span = GATHER_PLAN[stage]
        first, second = ("x", "y") if c % 2 == 0 else ("y", "x")
        link = {"first": first, "second": second}.get(link, link)
        self.now = max(self.now, self.ready[c]) + 0.1
        if link is not None:
            begin = max(self.now, self.links[link])
            self.links[link] = begin + span - 1.0
            self.ready[c] = begin + span
        self.stage[c] = stage + 1
        return (stage, c)

    def tick(self, spent):
        self.now += spent
        events = []
        progress = True
        while progress:
            progress = False
            for c in range(self.opened):
                if self.stage[c] < 5 and self.ready[c] <= self.now:
                    events.append(self.emit(c))
                    progress = True
        return events

    def until(self, c):
        events = []
        while self.stage[c] < 5:
            choices = [i for i in range(self.opened) if self.stage[i] < 5]
            best = min(choices, key=lambda i: (self.ready[i], i))
            events.append(self.emit(best))
        return events


def gelu_parts(u):
    share = 0.5 + 0.5 * lax.erf(u * math.sqrt(0.5))
    bell = jnp.exp(-0.5 * u * u) * (1.0 / math.sqrt(2.0 * math.pi))
    return u * share, share + u * bell


def norm_parts(values):
    centred = values - jnp.mean(values, axis=1, keepdims=True)
    spread = jnp.mean(centred * centred, axis=1, keepdims=True)
    scale = lax.rsqrt(spread + NORM_EPS)
    return centred * scale, scale


def forward_kernel(
    order_ref,
    lengths_ref,
    tokens_ref,
    piece_ref,
    e_ref,
    cot_ref,
    par,
    x_out,
    full_ref,
    q_out,
    k_out,
    v_out,
    o_out,
    lse_out,
    cq_out,
    ck_out,
    cv_out,
    oc_out,
    lse_cross_out,
    r1_out,
    r2_out,
    h1_out,
    h2_out,
    g_out,
    gp_out,
    y_out,
    dm_out,
    d_third_out,
    small_out,
    pool,
    acc,
    held,
    o_t,
    lse_held,
    states,
    x_held,
    spread_first,
    spread_second,
    picked,
    load_sem,
    store_sem,
    state_sem,
    acc_sem,
    spread_send,
    spread_recv,
    back_send,
    back_recv,
    *gather_sem,
):
    places = neighbours()
    refs = (piece_ref, full_ref) + gather_sem
    planner = GatherPlanner(GATHERED)
    length = lengths_ref[0]
    me = lax.axis_index("rep") * 4 + places[3]
    spread = (spread_first, spread_second)

    def device(offset):
        j = lax.rem(me + offset, 32)
        return j, (j // 4, j % 4)

    def spread_copy(p, offset):
        j, target = device(offset)
        return remote(
            tokens_ref.at[32 * p + j],
            spread[p].at[me],
            spread_send.at[p, offset],
            spread_recv.at[p, offset],
            target,
        )

    def back_copy(p, offset):
        return remote(
            picked.at[32 * p + offset],
            x_held.at[32 * p + me],
            back_send.at[p, offset],
            back_recv.at[p, offset],
            device(offset)[1],
        )

    def own_spread(p):
        return pltpu.make_async_copy(
            tokens_ref.at[32 * p + me], spread[p].at[me], spread_recv.at[p, 0]
        )

    def own_back(p):
        return pltpu.make_async_copy(
            picked.at[32 * p], x_held.at[32 * p + me], back_recv.at[p, 0]
        )

    def each_other(act):
        def body(offset, carry):
            act(offset)
            return carry

        lax.fori_loop(1, 32, body, 0)

    def start_spread(p):
        own_spread(p).start()
        each_other(lambda offset: spread_copy(p, offset).start())

    def turn_back(p):
        own_spread(p).wait()
        each_other(lambda offset: spread_copy(p, offset).wait())
        picked[32 * p] = spread[p][order_ref[me]]
        own_back(p).start()

        def pick(offset):
            picked[32 * p + offset] = spread[p][order_ref[device(offset)[0]]]
            back_copy(p, offset).start()

        each_other(pick)

    def arrive(p):
        own_back(p).wait()
        each_other(lambda offset: back_copy(p, offset).wait())

    def emit_all(events):
        for stage, c in events:
            gather_stage(stage, refs, c, c % 2, places)

    def tick(spent):
        emit_all(planner.tick(spent))

    def load(slot, source):
        return pltpu.make_async_copy(source, pool.at[slot], load_sem.at[slot])

    def store(slot, target):
        return pltpu.make_async_copy(pool.at[slot], target, store_sem.at[slot])

    def product_into(left, right, put):
        def body(i, carry):
            n = pl.multiple_of(i * 256, 256)
            put(n, product(left(), pool[right, :, pl.ds(n, 256)]))
            return carry

        lax.fori_loop(0, 4, body, 0)

    def row(index, n):
        return par[index : index + 1, pl.ds(n, 256)]

    def put_low(slot, offset=None, scale=None):
        def put(n, value):
            if offset is not None:
                value = value + row(offset, n)
            if scale is not None:
                value = value * scale
            pool[slot, :, pl.ds(n, 256)] = value.astype(jnp.bfloat16)

        return put

    def put_acc(offset):
        def put(n, value):
            acc[:, pl.ds(n, 256)] = value + row(offset, n)

        return put

    def load_weight(c, slot):
        target = pool.at[slot].reshape(4, 256, D)
        return pltpu.make_async_copy(full_ref.at[c], target, load_sem.at[slot])

    def weight(c, slot):
        emit_all(planner.until(c))
        return load_weight(c, slot)

    def attend_loop(causal, step, valid, query, key, value, out, spent, rows, key_rows):
        ahead = [planner.tick(spent) for _ in range(8)]
        first_row, count = rows

        def body(i, carry):
            lanes = pl.ds(pl.multiple_of(i * 128, 128), 128)
            attend_pair(
                causal,
                step,
                valid,
                query.at[pl.ds(first_row, count), lanes],
                key.at[pl.ds(0, key_rows), lanes],
                value.at[pl.ds(0, key_rows), lanes],
                out.at[pl.ds(first_row, count), lanes],
                lse_held.at[pl.ds(i, 1)],
                o_t,
                first_row,
            )
            for n in range(8):
                if ahead[n]:

                    @pl.when(i == n)
                    def _(events=ahead[n]):
                        emit_all(events)

            return carry

        lax.fori_loop(0, 8, body, 0)

    TILE = 128

    def over_rows(sums, body):
        zero = jnp.zeros((8, D), jnp.float32)

        def step(i, carry):
            r = pl.multiple_of(i * TILE, TILE)
            place = half_lanes((TILE, 1), 0) + r
            usable = (place < length).astype(jnp.float32)
            terms = body(pl.ds(r, TILE), usable)
            return tuple(c + fold(t) for c, t in zip(carry, terms))

        totals = lax.fori_loop(0, D // TILE, step, (zero,) * sums)
        return [jnp.sum(t, axis=0, keepdims=True) for t in totals]

    lane = half_lanes((1, D), 1)

    def square_at(index, total):
        small_out[17:18, :] += jnp.where(lane == index, jnp.sum(total), 0.0)

    barrier = pltpu.get_barrier_semaphore()

    def greet_one(offset):
        pl.semaphore_signal(barrier, inc=1, device_id=device(offset)[1], device_id_type=MESH)

    each_other(greet_one)
    pl.semaphore_wait(barrier, 31)
    planner.opened = 3
    tick(0.5)
    start_spread(0)
    start_spread(1)
    planner.spend(3.0, z=42.0, x=21.0, y=21.0)
    e_load = pltpu.make_async_copy(e_ref, states.at[2], state_sem.at[2])
    e_load.start()
    load(9, cot_ref).start()
    small_out[...] = jnp.zeros_like(small_out)
    tick(35.0)
    turn_back(0)
    planner.spend(42.0, z=21.0, x=10.0, y=10.0)
    tick(18.0)
    turn_back(1)
    planner.spend(62.0, z=21.0, x=10.0, y=10.0)
    for i in range(3):
        weight(i, 1 + i).start()
    planner.opened = GATHERED
    tick(1.0)
    emit_all(planner.tick(14.0))
    arrive(0)
    planner.spend(82.0)

    for p in range(2):
        if p == 1:
            arrive(1)
            planner.spend(103.0)
            x_store = pltpu.make_async_copy(x_held, x_out, acc_sem.at[1])
            x_store.start()
        rows = slice(512 * p, 512 * p + 512)
        for i, (slot, offset, scale) in enumerate(((4, 0, 0.125), (5, None, None), (6, 1, None))):
            if p == 0:
                load_weight(i, 1 + i).wait()

            def put_rows(n, value, slot=slot, offset=offset, scale=scale, rows=rows):
                if offset is not None:
                    value = value + row(offset, n)
                if scale is not None:
                    value = value * scale
                pool[slot, rows, pl.ds(n, 256)] = value.astype(jnp.bfloat16)

            product_into(
                lambda p=p: x_held[32 * p : 32 * p + 32].reshape(512, D), 1 + i, put_rows
            )
        if p == 1:
            store(4, q_out).start()
            store(5, k_out).start()
            store(6, v_out).start()
        tick(4.0)
        attend_loop(
            True,
            256,
            length,
            pool.at[4],
            pool.at[5],
            pool.at[6],
            pool.at[7],
            (1.6, 3.4)[p],
            (512 * p, 512),
            512 * p + 512,
        )
    store(7, o_out).start()
    lse_copy = pltpu.make_async_copy(lse_held, lse_out, state_sem.at[3])
    lse_copy.start()
    w_copy = weight(3, 1)
    w_copy.start()
    w_copy.wait()
    product_into(lambda: pool[7], 1, put_acc(2))
    tick(2.5)
    store(4, q_out).wait()

    def first_norm(rows, usable):
        held_rows = pl.ds(pl.multiple_of(rows.start // 16, TILE // 16), TILE // 16)
        x = x_held[held_rows].reshape(TILE, D).astype(jnp.float32)
        a = acc[rows, :]
        total = x + a
        acc[rows, :] = total
        h = norm_parts(total)[0] * par[11:12, :] + par[12:13, :]
        held[rows, :] = h
        pool[4, rows, :] = h.astype(jnp.bfloat16)
        return usable * x * x, usable * a * a, usable * h * h

    for index, total in enumerate(over_rows(3, first_norm)):
        square_at(index, total)
    store(4, h1_out).start()
    r1_copy = pltpu.make_async_copy(acc, r1_out, acc_sem.at[0])
    r1_copy.start()
    tick(4.0)

    for c, slot in ((4, 2), (5, 3), (6, 1)):
        weight(c, slot).start()
    store(5, k_out).wait()
    load_weight(4, 2).wait()
    product_into(lambda: pool[4], 2, put_low(5, 3, 0.125))
    store(5, cq_out).start()
    w_copy = weight(7, 2)
    w_copy.start()
    tick(2.5)
    e_load.wait()
    load_weight(5, 3).wait()
    load_weight(6, 1).wait()

    def put_keys(n, value):
        states[0, :, pl.ds(n, 256)] = value.astype(jnp.bfloat16)

    def put_values(n, value):
        states[1, :, pl.ds(n, 256)] = (value + row(4, n)).astype(jnp.bfloat16)

    product_into(lambda: states[2], 3, put_keys)
    product_into(lambda: states[2], 1, put_values)
    state_stores = [
        pltpu.make_async_copy(states.at[0], ck_out, state_sem.at[0]),
        pltpu.make_async_copy(states.at[1], cv_out, state_sem.at[1]),
    ]
    for copy in state_stores:
        copy.start()
    tick(1.0)
    store(6, v_out).wait()
    lse_copy.wait()
    attend_loop(
        False,
        512,
        lengths_ref[1],
        pool.at[5],
        states.at[0],
        states.at[1],
        pool.at[6],
        1.6,
        (0, 1024),
        128,
    )
    store(6, oc_out).start()
    lse_copy = pltpu.make_async_copy(lse_held, lse_cross_out, state_sem.at[3])
    lse_copy.start()
    w_copy.wait()
    r1_copy.wait()
    product_into(lambda: pool[6], 2, put_acc(5))
    tick(2.5)
    weight(EXPAND_AT[0], 0).start()
    weight(SHRINK_AT[0], 2).start()
    store(7, o_out).wait()

    def second_norm(rows, usable):
        c = acc[rows, :]
        total = held[rows, :] + c
        acc[rows, :] = total
        h = norm_parts(total)[0] * par[13:14, :] + par[14:15, :]
        held[rows, :] = h
        pool[7, rows, :] = h.astype(jnp.bfloat16)
        return usable * c * c, usable * h * h

    for index, total in enumerate(over_rows(2, second_norm)):
        square_at(3 + index, total)
    store(7, h2_out).start()
    r2_copy = pltpu.make_async_copy(acc, r2_out, acc_sem.at[0])
    r2_copy.start()
    tick(4.0)

    store(4, h1_out).wait()
    store(5, cq_out).wait()
    g_slots, slope_slots = (4, 6), (5, 8)
    r2_copy.wait()
    store(6, oc_out).wait()
    for j in range(5):
        if j > 1:
            store(g_slots[j % 2], g_out.at[j - 2]).wait()
            store(slope_slots[j % 2], gp_out.at[j - 2]).wait()
        if j < 4:
            load_weight(EXPAND_AT[j], j % 2).wait()
        if j > 0:
            load_weight(SHRINK_AT[j - 1], 2 + (j - 1) % 2).wait()

        def body(i, carry, j=j):
            n = pl.multiple_of(i * 256, 256)
            here = pl.ds(n, 256)
            if j < 4:
                u = product(pool[7], pool[j % 2, :, here]) + row(6 + j, n)
            if j > 0:
                more = product(pool[g_slots[(j - 1) % 2]], pool[2 + (j - 1) % 2, :, here])
                if j == 1:
                    acc[:, here] = more + row(10, n)
                else:
                    acc[:, here] += more
            if j < 4:
                g, slope = gelu_parts(u)
                pool[g_slots[j % 2], :, here] = g.astype(jnp.bfloat16)
                pool[slope_slots[j % 2], :, here] = slope.astype(jnp.bfloat16)
            return carry

        lax.fori_loop(0, 4, body, 0)
        if j < 4:
            store(g_slots[j % 2], g_out.at[j]).start()
            store(slope_slots[j % 2], gp_out.at[j]).start()
        tick(9.0 if j < 4 else 2.5)
        if j < 3:
            weight(EXPAND_AT[j + 1], (j + 1) % 2).start()
            weight(SHRINK_AT[j + 1], 2 + (j + 1) % 2).start()

    load(9, cot_ref).wait()

    def third_norm(rows, usable):
        m = acc[rows, :]
        unit, scale = norm_parts(held[rows, :] + m)
        gain = par[15:16, :]
        pool[0, rows, :] = (unit * gain + par[16:17, :]).astype(jnp.bfloat16)
        grad = pool[9, rows, :].astype(jnp.float32) * usable
        inner = grad * gain
        first = jnp.mean(inner, axis=1, keepdims=True)
        second = jnp.mean(inner * unit, axis=1, keepdims=True)
        back = scale * (inner - first - unit * second)
        acc[rows, :] = back
        low = back.astype(jnp.bfloat16)
        pool[1, rows, :] = low
        return usable * m * m, grad * unit, grad, low.astype(jnp.float32)

    m_total, gain_sum, shift_sum, offset_sum = over_rows(4, third_norm)
    square_at(5, m_total)
    small_out[15:16, :] = gain_sum
    small_out[16:17, :] = shift_sum
    small_out[10:11, :] = offset_sum
    last = [
        store(0, y_out),
        store(1, dm_out),
        pltpu.make_async_copy(acc, d_third_out, acc_sem.at[0]),
    ]
    for copy in last:
        copy.start()
    for c in range(GATHERED):
        emit_all(planner.until(c))
    for copy in last + state_stores + [lse_copy, x_store]:
        copy.wait()
    store(7, h2_out).wait()
    store(6, g_out.at[3]).wait()
    store(8, gp_out.at[3]).wait()


def forward(order, lengths, tokens, pieces, states, cotangent, params):
    any_space = pl.BlockSpec(memory_space=pl.ANY)
    vmem = pl.BlockSpec(memory_space=pltpu.VMEM)
    shape = jax.ShapeDtypeStruct
    dma = pltpu.SemaphoreType.DMA
    low = jnp.bfloat16
    wide = jnp.float32
    square = shape((1024, D), low)
    square_wide = shape((1024, D), wide)
    lse = shape((8, 8, 1024), wide)
    short = shape((128, D), low)
    blocks = shape((4, 1024, D), low)
    outs = (
        shape((64, 16, D), low),
        shape((GATHERED, 4, 256, D), low),
        square,
        square,
        square,
        square,
        lse,
        square,
        short,
        short,
        square,
        lse,
        square_wide,
        square_wide,
        square,
        square,
        blocks,
        blocks,
        square,
        square,
        square_wide,
        shape((24, D), wide),
    )
    return pl.pallas_call(
        forward_kernel,
        out_shape=outs,
        in_specs=[SCALARS] * 2 + [any_space] * 4 + [vmem],
        out_specs=(any_space,) * 21 + (vmem,),
        scratch_shapes=[
            pltpu.VMEM((10, 1024, D), low),
            pltpu.VMEM((1024, D), wide),
            pltpu.VMEM((1024, D), wide),
            pltpu.VMEM((128, 1024), wide),
            pltpu.VMEM((8, 8, 1024), wide),
            pltpu.VMEM((3, 128, D), low),
            pltpu.VMEM((64, 16, D), low),
            pltpu.VMEM((32, 16, D), low),
            pltpu.VMEM((32, 16, D), low),
            pltpu.VMEM((64, 16, D), low),
            dma((10,)),
            dma((10,)),
            dma((4,)),
            dma((2,)),
            dma((2, 32)),
            dma((2, 32)),
            dma((2, 32)),
            dma((2, 32)),
        ]
        + gather_sems(GATHERED),
        compiler_params=pltpu.CompilerParams(
            collective_id=3, has_side_effects=True, vmem_limit_bytes=62 * MIB
        ),
    )(order, lengths, tokens.reshape(64, 16, D), pieces, states, cotangent, params)


def add_blocks(target, first, second, planes, rows, step):
    per_plane = rows // step

    def body(i, carry):
        s = i // per_plane
        r = pl.multiple_of((i % per_plane) * step, step)
        target(s, r, first(s, r) + second(s, r))
        return carry

    lax.fori_loop(0, planes * per_plane, body, 0)


POOL = 8
G_SLOTS = 3
R_SLOTS = 4
PLAN = {"core": 3.0, "load": 1.5, "a": 11.5, "b": 6.5, "z": 6.5, "bb": 2.5, "ba": 4.0, "bc": 2.0}


class Planner:
    def __init__(self):
        self.now = 0.0
        self.links = {"core": 0.0, "x": 0.0, "y": 0.0, "z": 0.0, "load": 0.0}
        self.stage = {}
        self.ready = {}

    def link_of(self, c, stage):
        first, second = ("x", "y") if c % 2 == 0 else ("y", "x")
        return {
            0: ("core", "core"),
            1: ("load", "load"),
            2: (first, "a"),
            3: (second, "b"),
            4: ("z", "z"),
            5: (second, "bb"),
            6: (first, "ba"),
            7: ("core", "bc"),
            8: (None, None),
        }[stage]

    def can(self, c):
        stage = self.stage[c]
        if stage > 8:
            return False
        if stage == 1 and c >= R_SLOTS and self.stage[c - R_SLOTS] <= 3:
            return False
        return True

    def emit(self, c):
        stage = self.stage[c]
        link, kind = self.link_of(c, stage)
        self.now = max(self.now, self.ready[c]) + {2: 0.8, 3: 0.5, 4: 0.3, 5: 0.2}.get(stage, 0.1)
        if link is not None:
            begin = max(self.now, self.links[link])
            span = PLAN[kind]
            self.links[link] = begin + span - 1.0
            self.ready[c] = begin + span
        self.stage[c] = stage + 1
        return (stage, c)

    def tick(self, spent):
        self.now += spent
        events = []
        progress = True
        while progress:
            progress = False
            for c in sorted(self.stage):
                if self.can(c) and self.ready[c] <= self.now:
                    events.append(self.emit(c))
                    progress = True
        return events

    def produce(self, c):
        self.stage[c] = 0
        self.ready[c] = self.now
        return [self.emit(c)]

    def until(self, done):
        events = []
        while not done():
            choices = [c for c in sorted(self.stage) if self.can(c)]
            c = min(choices, key=lambda i: (self.ready[i], i))
            events.append(self.emit(c))
        return events

    def free_slot(self, c):
        before = c - G_SLOTS
        if before < 0:
            return []
        return self.until(lambda: self.stage[before] > 2)

    def drain(self, tasks, spent):
        events = []
        waiting = list(tasks)
        while waiting or any(s <= 8 for s in self.stage.values()):
            choices = [c for c in sorted(self.stage) if self.can(c)]
            best = min(choices, key=lambda i: (self.ready[i], i)) if choices else None
            open_tasks = [t for t in waiting if all(self.stage[c] > 8 for c in t[0])]
            if open_tasks and (best is None or self.ready[best] > self.now):
                task = open_tasks[0]
                waiting.remove(task)
                self.now += spent
                events.append(("task", task[1]))
            else:
                events.append(self.emit(best))
        return events


def backward_kernel(
    lengths_ref,
    dm_ref,
    d_third_ref,
    g_ref,
    gp_ref,
    full_ref,
    h2_ref,
    h1_ref,
    x_in_ref,
    e_ref,
    oc_ref,
    o_ref,
    r1_ref,
    r2_ref,
    q_ref,
    k_ref,
    v_ref,
    cq_ref,
    ck_ref,
    cv_ref,
    lse_ref,
    lse_cross_ref,
    gains_ref,
    small_ref,
    rows_ref,
    cols_ref,
    token_grad_ref,
    state_grad_ref,
    out_ref,
    totals_ref,
    rows_out,
    cols_out,
    scale_out,
    half,
    pool,
    acc,
    made,
    summed,
    quarter,
    eighth,
    pieces,
    stream,
    dq_t,
    dk_sum,
    dv_sum,
    lse_held,
    states,
    states_t,
    small,
    small_in,
    small_sum,
    small_z,
    part,
    whole,
    load_sem,
    stream_sem,
    state_sem,
    half_sem,
    scan_sem,
    line_send_sem,
    line_recv_sem,
    send_sem,
    recv_sem,
    z_send_sem,
    z_recv_sem,
    place_sem,
    small_send_sem,
    small_recv_sem,
):
    core, x, y, z, other_core, other_x, other_y, others_z = neighbours()
    kept = pl.multiple_of(core * 128, 128)
    given = pl.multiple_of(128 - core * 128, 128)
    planner = Planner()
    place_of = (12, 8, 13, 9, 14, 10, 15, 11, 7, 4, 5, 6, 3, 0, 1, 2)

    def axes(c):
        if c % 2 == 0:
            return x, y, other_x, other_y
        return y, x, other_y, other_x

    def core_copy(c):
        source = made.at[c % G_SLOTS, :, pl.ds(given, 128), :]
        return remote(source, half.at[c], send_sem.at[0, c], recv_sem.at[0, c], other_core)

    def half_copy(c):
        return pltpu.make_async_copy(
            half.at[c], summed.at[c % R_SLOTS], half_sem.at[c % R_SLOTS]
        )

    def first_copy(c):
        a, b, first, second = axes(c)
        rows = pl.ds(pl.multiple_of(64 - a * 64, 64), 64)
        source = summed.at[c % R_SLOTS, :, rows, :]
        return remote(source, quarter.at[c], send_sem.at[1, c], recv_sem.at[1, c], first)

    def second_copy(c):
        a, b, first, second = axes(c)
        rows = pl.ds(pl.multiple_of(32 - b * 32, 32), 32)
        source = quarter.at[c, :, rows, :]
        return remote(source, eighth.at[c], send_sem.at[2, c], recv_sem.at[2, c], second)

    def z_copy(c, d):
        device = others_z[d]
        return remote(
            eighth.at[c, device[1]],
            pieces.at[c, d],
            z_send_sem.at[c, d],
            z_recv_sem.at[c, d],
            device,
        )

    def own_rows_of(c):
        a, b, first, second = axes(c)
        return pl.ds(pl.multiple_of(core * 128 + a * 64 + b * 32, 32), 32)

    def place_copy(c):
        return pltpu.make_async_copy(
            pieces.at[c, 0], out_ref.at[place_of[c], own_rows_of(c), :], place_sem.at[c]
        )

    def back_second(c):
        device = axes(c)[3]
        target = out_ref.at[place_of[c], own_rows_of(c), :]
        return remote(pieces.at[c, 0], target, send_sem.at[3, c], recv_sem.at[3, c], device)

    def back_first(c):
        a, b, first, second = axes(c)
        block = out_ref.at[place_of[c], pl.ds(pl.multiple_of(core * 128 + a * 64, 64), 64), :]
        return remote(block, block, send_sem.at[4, c], recv_sem.at[4, c], first)

    def back_core(c):
        block = out_ref.at[place_of[c], pl.ds(kept, 128), :]
        return remote(block, block, send_sem.at[5, c], recv_sem.at[5, c], other_core)

    def emit(stage, c):
        a, b, first, second = axes(c)
        slot = c % R_SLOTS
        if stage == 0:
            core_copy(c).start()
        if stage == 1:
            if c >= R_SLOTS:
                first_copy(c - R_SLOTS).wait_send()
            core_copy(c).wait_recv()
            half_copy(c).start()
        if stage == 2:
            half_copy(c).wait()

            def put(s, r, value):
                summed[slot, s, pl.ds(r, 32), :] = value

            add_blocks(
                put,
                lambda s, r: summed[slot, s, pl.ds(r, 32), :],
                lambda s, r: made[c % G_SLOTS, s, pl.ds(pl.multiple_of(kept + r, 32), 32), :],
                4,
                128,
                32,
            )
            first_copy(c).start()
            core_copy(c).wait_send()
        if stage == 3:
            first_copy(c).wait_recv()

            def put(s, r, value):
                quarter[c, s, pl.ds(r, 32), :] = value

            add_blocks(
                put,
                lambda s, r: quarter[c, s, pl.ds(r, 32), :],
                lambda s, r: summed[slot, s, pl.ds(pl.multiple_of(a * 64 + r, 32), 32), :],
                4,
                64,
                32,
            )
            second_copy(c).start()
        if stage == 4:
            second_copy(c).wait_recv()

            def put(s, r, value):
                eighth[c, s, pl.ds(r, 32), :] = value

            add_blocks(
                put,
                lambda s, r: eighth[c, s, pl.ds(r, 32), :],
                lambda s, r: quarter[c, s, pl.ds(pl.multiple_of(b * 32 + r, 32), 32), :],
                4,
                32,
                32,
            )
            for d in range(3):
                z_copy(c, d).start()
        if stage == 5:
            for d in range(3):
                z_copy(c, d).wait_recv()
            total = eighth[c, z].astype(jnp.float32)
            for d in range(3):
                total = total + pieces[c, d].astype(jnp.float32)
            pieces[c, 0] = total.astype(jnp.bfloat16)
            back_second(c).start()
            place_copy(c).start()
        if stage == 6:
            place_copy(c).wait()
            back_second(c).wait_recv()
            back_first(c).start()
        if stage == 7:
            back_first(c).wait_recv()
            back_core(c).start()
        if stage == 8:
            back_core(c).wait()
            back_first(c).wait_send()
            back_second(c).wait_send()
            for d in range(3):
                z_copy(c, d).wait_send()
            second_copy(c).wait_send()
            if c >= CHUNKS - R_SLOTS:
                first_copy(c).wait_send()

    def emit_all(events):
        for stage, c in events:
            emit(stage, c)

    def tick(spent):
        emit_all(planner.tick(spent))

    def produced(c, spent):
        planner.now += spent
        emit_all(planner.produce(c))
        emit_all(planner.tick(0.0))

    def load(slot, source):
        return pltpu.make_async_copy(source, pool.at[slot], load_sem.at[slot])

    def state_load(index, source):
        return pltpu.make_async_copy(source, states.at[index], state_sem.at[index])

    def turn_tile(target, source):
        def turn(n):
            pool[target, pl.ds(n, 256), :] = pool[source, :, pl.ds(n, 256)].T

        return turn

    def transpose_into(target, source):
        turn = turn_tile(target, source)

        def body(i, carry):
            turn(pl.multiple_of(i * 256, 256))
            return carry

        lax.fori_loop(0, 4, body, 0)

    def product_nn(left, right, put, beside=None):
        def body(i, carry):
            n = pl.multiple_of(i * 256, 256)
            if beside is not None:
                beside(n)
            put(n, product(left(), right(n)))
            return carry

        lax.fori_loop(0, 4, body, 0)

    def product_nt(left, right, put, beside=None):
        def body(i, carry):
            n = pl.multiple_of(i * 256, 256)
            if beside is not None:
                beside(n)
            put(
                n,
                lax.dot_general(
                    left(),
                    right(n),
                    (((1,), (1,)), ((), ())),
                    preferred_element_type=jnp.float32,
                ),
            )
            return carry

        lax.fori_loop(0, 4, body, 0)

    def columns_of(slot):
        return lambda n: pool[slot, :, pl.ds(n, 256)]

    def rows_of(slot):
        return lambda n: pool[slot, pl.ds(n, 256), :]

    def weight_grad(slot_in_made, left, right, beside=None):
        def put(n, value):
            low = value.astype(jnp.bfloat16).reshape(4, 256, 256)
            made[slot_in_made, :, :, pl.ds(n, 256)] = low

        product_nn(left, right, put, beside)

    def add_to_acc(n, value):
        acc[:, pl.ds(n, 256)] += value

    def put_in(slot):
        def put(n, value):
            pool[slot, :, pl.ds(n, 256)] = value.astype(jnp.bfloat16)

        return put

    def norm_back(source, gain_row, gain_at, shift_at, offset_at, target):
        tiles = 8
        rows = 1024 // tiles

        def fetch(i):
            place = pl.ds(pl.multiple_of(i * rows, rows), rows)
            return pltpu.make_async_copy(
                source.at[place, :], stream.at[i % 2], stream_sem.at[i % 2]
            )

        fetch(0).start()

        def body(i, carry):
            gain_sum, shift_sum, offset_sum = carry

            @pl.when(i + 1 < tiles)
            def _():
                fetch(i + 1).start()

            fetch(i).wait()
            r = pl.multiple_of(i * rows, rows)
            values = stream[i % 2]
            centred = values - jnp.mean(values, axis=1, keepdims=True)
            spread = jnp.mean(centred * centred, axis=1, keepdims=True)
            scale = lax.rsqrt(spread + NORM_EPS)
            unit = centred * scale
            grad = acc[pl.ds(r, rows), :]
            inner = grad * gains_ref[gain_row : gain_row + 1, :]
            first = jnp.mean(inner, axis=1, keepdims=True)
            second = jnp.mean(inner * unit, axis=1, keepdims=True)
            back = scale * (inner - first - unit * second)
            acc[pl.ds(r, rows), :] = back
            low = back.astype(jnp.bfloat16)
            pool[target, pl.ds(r, rows), :] = low
            return (
                gain_sum + fold(grad * unit),
                shift_sum + fold(grad),
                offset_sum + fold(low.astype(jnp.float32)),
            )

        zero = jnp.zeros((8, D), jnp.float32)
        sums = lax.fori_loop(0, tiles, body, (zero, zero, zero))
        for row, value in zip((gain_at, shift_at, offset_at), sums):
            small[row : row + 1, :] = jnp.sum(value, axis=0, keepdims=True)

    greet([other_core, other_x, other_y] + others_z)
    load(0, dm_ref).start()
    load(6, h2_ref).start()
    load(2, full_ref.at[SHRINK_AT[0]]).start()
    load(3, gp_ref.at[0]).start()
    load(4, g_ref.at[0]).start()
    load(5, full_ref.at[EXPAND_AT[0]]).start()
    acc_load = pltpu.make_async_copy(d_third_ref, acc, place_sem.at[0])
    acc_load.start()
    small[...] = small_ref[...]
    load(6, h2_ref).wait()
    transpose_into(1, 6)
    load(0, dm_ref).wait()
    acc_load.wait()

    planner.now = 4.0
    plan = []
    for j in range(4):
        entry = []
        planner.now += 3.5
        entry.append(planner.tick(0.0) + planner.free_slot(2 * j))
        planner.now += 2.5
        entry.append(planner.produce(2 * j) + planner.tick(0.0) + planner.free_slot(2 * j + 1))
        planner.now += 2.5
        entry.append(planner.produce(2 * j + 1) + planner.tick(0.0))
        entry.append(planner.tick(2.5))
        plan.append(entry)

    def emit_planned(j, place):
        for n in range(4):
            events = plan[n][place]
            if events:

                @pl.when(j == n)
                def _(events=events):
                    emit_all(events)

    def block(j, carry):
        last = j == 3
        load(2, full_ref.at[SHRINK_AT[0]]).wait()
        load(3, gp_ref.at[0]).wait()

        def put_pre(n, value):
            low = (value * pool[3, :, pl.ds(n, 256)].astype(jnp.float32)).astype(jnp.bfloat16)
            pool[7, :, pl.ds(n, 256)] = low
            small[pl.ds(6 + j, 1), pl.ds(n, 256)] = jnp.sum(
                low.astype(jnp.float32), axis=0, keepdims=True
            )

        load(4, g_ref.at[0]).wait()
        product_nt(lambda: pool[0], rows_of(2), put_pre, turn_tile(6, 4))

        @pl.when(jnp.logical_not(last))
        def _():
            load(2, full_ref.at[SHRINK_AT[0] + 2 * (j + 1) - (j + 1) // 3]).start()
            load(3, gp_ref.at[j + 1]).start()

        @pl.when(last)
        def _():
            load(2, full_ref.at[7]).start()
            load(3, cq_ref).start()

        emit_planned(j, 0)

        @pl.when(jnp.logical_not(last))
        def _():
            load(4, g_ref.at[j + 1]).start()

        @pl.when(last)
        def _():
            load(4, oc_ref).start()

        weight_grad((2 * j) % G_SLOTS, lambda: pool[6], columns_of(0))
        emit_planned(j, 1)
        weight_grad((2 * j + 1) % G_SLOTS, lambda: pool[1], columns_of(7))
        emit_planned(j, 2)
        load(5, full_ref.at[EXPAND_AT[0]]).wait()
        product_nt(lambda: pool[7], rows_of(5), add_to_acc)

        @pl.when(jnp.logical_not(last))
        def _():
            load(5, full_ref.at[EXPAND_AT[1] + 2 * j]).start()

        @pl.when(last)
        def _():
            load(5, full_ref.at[4]).start()

        emit_planned(j, 3)
        return carry

    lax.fori_loop(0, 4, block, 0)

    load(7, h1_ref).start()
    state_loads = [state_load(0, ck_ref), state_load(1, cv_ref), state_load(2, e_ref)]
    for copy in state_loads:
        copy.start()
    lse_load = pltpu.make_async_copy(lse_cross_ref, lse_held, state_sem.at[3])
    lse_load.start()
    norm_back(r2_ref, 1, 13, 14, 5, 0)
    tick(4.0)
    load(4, oc_ref).wait()
    load(2, full_ref.at[7]).wait()
    product_nt(lambda: pool[0], rows_of(2), put_in(4), turn_tile(6, 4))
    load(2, full_ref.at[3]).start()
    tick(2.5)
    emit_all(planner.free_slot(8))
    load(7, h1_ref).wait()
    weight_grad(8 % G_SLOTS, lambda: pool[6], columns_of(0), turn_tile(1, 7))
    load(6, o_ref).start()
    load(7, full_ref.at[5]).start()
    produced(8, 2.5)
    load(3, cq_ref).wait()
    for copy in state_loads:
        copy.wait()
    lse_load.wait()

    def attend_loop(causal, step, length, query, key, value, grad, rows, spent, span=(0, 8)):
        ahead = {n: planner.tick(spent) for n in range(*span)}

        def body(i, carry):
            lanes = pl.ds(pl.multiple_of(i * 128, 128), 128)

            def sums(dq, dv):
                small[rows[0] : rows[0] + 1, lanes] = dq
                small[rows[1] : rows[1] + 1, lanes] = dv

            attend_back_pair(
                causal,
                step,
                length,
                query.at[:, lanes],
                key.at[:, lanes],
                value.at[:, lanes],
                grad.at[:, lanes],
                lse_held.at[pl.ds(i, 1)],
                query.at[:, lanes],
                key.at[:, lanes],
                value.at[:, lanes],
                sums,
                dq_t,
                dk_sum,
                dv_sum,
            )
            for n in range(*span):
                if ahead[n]:

                    @pl.when(i == n)
                    def _(events=ahead[n]):
                        emit_all(events)

            return carry

        lax.fori_loop(*span, body, 0)

    attend_loop(
        False,
        512,
        lengths_ref[1],
        pool.at[3],
        states.at[0],
        states.at[1],
        pool.at[4],
        (3, 4),
        2.0,
    )
    lse_load = pltpu.make_async_copy(lse_ref, lse_held, state_sem.at[3])
    lse_load.start()
    emit_all(planner.free_slot(9))
    weight_grad(9 % G_SLOTS, lambda: pool[1], columns_of(3))
    produced(9, 2.5)
    load(5, full_ref.at[4]).wait()
    load(6, o_ref).wait()
    product_nt(lambda: pool[3], rows_of(5), add_to_acc, turn_tile(1, 6))
    load(6, x_in_ref).start()
    load(5, full_ref.at[6]).start()
    load(3, q_ref).start()
    tick(2.5)
    states_t[...] = states[2].T
    for c, index in ((10, 0), (11, 1)):
        emit_all(planner.free_slot(c))
        weight_grad(
            c % G_SLOTS, lambda: states_t[...], lambda n, i=index: states[i, :, pl.ds(n, 256)]
        )
        produced(c, 1.0)
    load(7, full_ref.at[5]).wait()
    load(5, full_ref.at[6]).wait()

    def state_part(n):
        dims = (((1,), (1,)), ((), ()))
        return lax.dot_general(
            states[0], pool[7, pl.ds(n, 256), :], dims, preferred_element_type=jnp.float32
        ) + lax.dot_general(
            states[1], pool[5, pl.ds(n, 256), :], dims, preferred_element_type=jnp.float32
        )

    def put_state(i, carry):
        n = pl.multiple_of(i * 256, 256)
        state_grad_ref[:, pl.ds(n, 256)] = state_part(n).astype(jnp.bfloat16)
        return carry

    lax.fori_loop(0, 4, put_state, 0)
    load(5, k_ref).start()
    load(7, v_ref).start()
    tick(1.0)

    norm_back(r1_ref, 0, 11, 12, 2, 0)
    tick(4.0)
    emit_all(planner.free_slot(12))
    weight_grad(12 % G_SLOTS, lambda: pool[1], columns_of(0))
    produced(12, 2.5)
    load(2, full_ref.at[3]).wait()
    load(6, x_in_ref).wait()
    product_nt(lambda: pool[0], rows_of(2), put_in(4), turn_tile(1, 6))
    load(0, full_ref.at[0]).start()
    load(2, full_ref.at[1]).start()
    load(6, full_ref.at[2]).start()
    tick(2.5)
    load(3, q_ref).wait()
    load(5, k_ref).wait()
    load(7, v_ref).wait()
    lse_load.wait()
    def self_heads(span):
        refs = [pool.at[slot] for slot in (3, 5, 7, 4)]
        attend_loop(True, 256, lengths_ref[0], *refs, (0, 1), 5.0, span)

    def query_key_grad(c, half_of):
        def put(i, carry):
            n = pl.multiple_of((i % 2) * 256 + 512 * half_of, 256)
            value = product(pool[1], pool[3 + 2 * (i // 2), :, pl.ds(n, 256)])
            low = value.astype(jnp.bfloat16).reshape(4, 256, 256)
            made[c % G_SLOTS, :, :, pl.ds(pl.multiple_of(i * 256, 256), 256)] = low
            return carry

        emit_all(planner.free_slot(c))
        lax.fori_loop(0, 4, put, 0)
        produced(c, 2.5)

    self_heads((0, 4))
    query_key_grad(13, 0)
    self_heads((4, 8))

    def small_copy(k):
        source = small if k == 0 else small_sum.at[k - 1]
        device = (other_core, other_x, other_y)[k]
        return remote(source, small_in.at[k], small_send_sem.at[k], small_recv_sem.at[k], device)

    def small_z_copy(d):
        return remote(
            small_sum.at[2],
            small_z.at[z],
            small_send_sem.at[3 + d],
            small_recv_sem.at[3 + d],
            others_z[d],
        )

    def small_step(k):
        small_copy(k).wait()
        before = small[...] if k == 0 else small_sum[k - 1]
        small_sum[k] = before + small_in[k]
        if k < 2:
            small_copy(k + 1).start()
        else:
            small_z[z] = small_sum[2]
            for d in range(3):
                small_z_copy(d).start()

    small_copy(0).start()
    emit_all(planner.free_slot(14))
    weight_grad(14 % G_SLOTS, lambda: pool[1], columns_of(7))
    produced(14, 2.5)
    small_step(0)
    query_key_grad(15, 1)
    small_step(1)
    load(0, full_ref.at[0]).wait()
    product_nt(lambda: pool[3], rows_of(0), add_to_acc)
    tick(2.5)
    small_step(2)
    load(2, full_ref.at[1]).wait()
    product_nt(lambda: pool[5], rows_of(2), add_to_acc)
    tick(2.5)
    for d in range(3):
        small_z_copy(d).wait()
    totals_ref[...] = (small_z[0] + small_z[1]) + (small_z[2] + small_z[3])
    load(6, full_ref.at[2]).wait()

    def put_input(n, value):
        total = acc[:, pl.ds(n, 256)] + value
        pool[4, :, pl.ds(n, 256)] = total.astype(jnp.bfloat16)

    product_nt(lambda: pool[7], rows_of(6), put_input)
    token_copy = pltpu.make_async_copy(pool.at[4], token_grad_ref, load_sem.at[4])
    token_copy.start()
    tick(2.5)

    part[...] = jnp.zeros_like(part)

    def spot(place):
        return (0, 1, 2, 6)[place // 4], (place % 4) * 256

    def scan_load(place):
        slot, row = spot(place)
        return pltpu.make_async_copy(
            out_ref.at[place], pool.at[slot, pl.ds(row, 256), :], scan_sem.at[place]
        )

    scans = {}
    for i in range(2):
        scans[i] = ([(0, 512 * i, 512, i, 0), (2, 512 * i, 512, i, 512)], i, (13, 128 * i))
    for i in range(2, 8):
        scans[i] = ([(1 if i == 2 else i, 0, D, i, 0)], i, (13, 128 * i))
    scans[8] = ([(8 + i, 0, D, 8 + i, 0) for i in range(4)], 8, (14, 0))
    for i in range(4):
        scans[9 + i] = ([(12 + i, 0, D, 12, 0)], 9 + i, (14, 128))

    def scan(name):
        sources, row_lane, (total_row, total_lane) = scans[name]
        width = float(sum(source[2] for source in sources))
        step = 64 if name == 8 else 256

        def body(i, carry):
            cols, weights, total = carry
            r = pl.multiple_of(i * step, step)
            squares = []
            for place, lane, lanes, _, _ in sources:
                slot, row = spot(place)
                tile = pool[slot, pl.ds(row + r, step), lane : lane + lanes]
                squares.append(jnp.square(tile.astype(jnp.float32)))
            row_sum = sum(jnp.sum(square, axis=1, keepdims=True) for square in squares)
            rows = DECAY_RATE * rows_ref[pl.ds(r, step), row_lane : row_lane + 1] + (
                1.0 - DECAY_RATE
            ) * (row_sum / width + FACTOR_EPS)
            rows_out[pl.ds(r, step), row_lane : row_lane + 1] = rows
            inverse = 1.0 / rows
            cols = [c + fold(s) for c, s in zip(cols, squares)]
            weights = [w + fold(s * inverse) for w, s in zip(weights, squares)]
            return cols, weights, total + fold(rows)

        zeros = [jnp.zeros((8, source[2]), jnp.float32) for source in sources]
        cols, weights, total = lax.fori_loop(
            0, 256 // step, body, (zeros, zeros, jnp.zeros((8, 1), jnp.float32))
        )
        for (_, _, lanes, slot, lane), col, weighted in zip(sources, cols, weights):
            here = slice(lane, lane + lanes)
            part[slot : slot + 1, here] += jnp.sum(col, axis=0, keepdims=True)
            part[16 + slot : 17 + slot, here] += jnp.sum(weighted, axis=0, keepdims=True)
        part[total_row : total_row + 1, total_lane : total_lane + 128] += jnp.broadcast_to(
            jnp.sum(total), (1, 128)
        )

    chunk_at = {place: c for c, place in enumerate(place_of)}
    tasks = [
        ([chunk_at[source[0]] for source in scans[name][0]], name)
        for name in (9, 10, 11, 12, 8, 7, 4, 5, 6, 3, 2, 0, 1)
    ]
    loaded = set()
    for c in range(CHUNKS):
        if planner.stage[c] > 8:
            scan_load(place_of[c]).start()
    for first, second in planner.drain(tasks, 1.5):
        if first != "task":
            emit(first, second)
            if first == 8:
                scan_load(place_of[second]).start()
            continue
        for source in scans[second][0]:
            if source[0] not in loaded:
                loaded.add(source[0])
                scan_load(source[0]).wait()
        scan(second)
    total = line_sum(part, whole, line_send_sem, line_recv_sem, z, others_z)
    row_counts = [D] * 12 + [FF]
    means = [total[13:14, 128 * i : 128 * i + 1] / D for i in range(8)]
    means = means + [total[14:15, 0:1] / D] * 4 + [total[14:15, 128:129] / FF]
    cols_new, quotients = [], []
    for slot in range(13):
        new = DECAY_RATE * cols_ref[slot : slot + 1, :] + (1.0 - DECAY_RATE) * (
            total[slot : slot + 1] / row_counts[slot] + FACTOR_EPS
        )
        cols_new.append(new)
        quotients.append(jnp.sum(total[16 + slot : 17 + slot] / new, axis=1, keepdims=True))
        cols_out[slot : slot + 1, :] = new
    expand_quotient = quotients[8] + quotients[9] + quotients[10] + quotients[11]
    for slot in range(13):
        if slot < 8:
            mean_square = means[slot] * quotients[slot] / (D * D)
            rate = STEP_RATE * (OUT_GAIN if slot % 4 == 3 else 1.0)
        else:
            quotient = expand_quotient if slot < 12 else quotients[12]
            mean_square = means[slot] * quotient / (D * FF)
            rate = STEP_RATE
        factor = rate / jnp.maximum(1.0, jnp.sqrt(mean_square) / CLIP_LEVEL)
        scale_out[slot : slot + 1, :] = lax.rsqrt(cols_new[slot] / means[slot]) * factor
    token_copy.wait()


def backward(lengths, held, gains, small, factor_rows, factor_cols):
    any_space = pl.BlockSpec(memory_space=pl.ANY)
    vmem = pl.BlockSpec(memory_space=pltpu.VMEM)
    shape = jax.ShapeDtypeStruct
    dma = pltpu.SemaphoreType.DMA
    low = jnp.bfloat16
    wide = jnp.float32
    rows = small.shape[0]
    return pl.pallas_call(
        backward_kernel,
        out_shape=(
            shape((1024, D), low),
            shape((128, D), low),
            shape((CHUNKS, 256, D), low),
            shape(small.shape, wide),
            shape((256, 128), wide),
            shape((16, D), wide),
            shape((16, D), wide),
            shape((CHUNKS, 4, 128, D), low),
        ),
        in_specs=[SCALARS] + [any_space] * len(held) + [vmem] * 4,
        out_specs=(any_space, vmem, any_space, vmem, vmem, vmem, vmem, any_space),
        scratch_shapes=[
            pltpu.VMEM((POOL, 1024, D), low),
            pltpu.VMEM((1024, D), wide),
            pltpu.VMEM((G_SLOTS, 4, 256, D), low),
            pltpu.VMEM((R_SLOTS, 4, 128, D), low),
            pltpu.VMEM((CHUNKS, 4, 64, D), low),
            pltpu.VMEM((CHUNKS, 4, 32, D), low),
            pltpu.VMEM((CHUNKS, 3, 32, D), low),
            pltpu.VMEM((2, 128, D), wide),
            pltpu.VMEM((128, 1024), wide),
            pltpu.VMEM((2, 1024, 128), wide),
            pltpu.VMEM((2, 1024, 128), wide),
            pltpu.VMEM((8, 8, 1024), wide),
            pltpu.VMEM((3, 128, D), low),
            pltpu.VMEM((D, 128), low),
            pltpu.VMEM((rows, D), wide),
            pltpu.VMEM((3, rows, D), wide),
            pltpu.VMEM((3, rows, D), wide),
            pltpu.VMEM((4, rows, D), wide),
            pltpu.VMEM((32, D), wide),
            pltpu.VMEM((4, 32, D), wide),
            dma((POOL,)),
            dma((2,)),
            dma((4,)),
            dma((R_SLOTS,)),
            dma((CHUNKS,)),
            dma((3,)),
            dma((3,)),
            dma((6, CHUNKS)),
            dma((6, CHUNKS)),
            dma((CHUNKS, 3)),
            dma((CHUNKS, 3)),
            dma((CHUNKS,)),
            dma((6,)),
            dma((6,)),
        ],
        compiler_params=pltpu.CompilerParams(
            collective_id=0, has_side_effects=True, vmem_limit_bytes=62 * MIB
        ),
    )(lengths, *held, gains, small, factor_rows, factor_cols)[0:7]


def line_sum(part, whole, send_sem, recv_sem, z, others_z):
    copies = [
        remote(part, whole.at[z], send_sem.at[d], recv_sem.at[d], others_z[d]) for d in range(3)
    ]
    for copy in copies:
        copy.start()
    whole[z] = part[...]
    for copy in copies:
        copy.wait()
    return (whole[0] + whole[1]) + (whole[2] + whole[3])


def update_attention_kernel(
    grad_ref, weight_ref, rows_ref, scale_ref, grad_out, new_out, copy_out, grads, change
):
    block = grad_ref.shape[1]
    for i in range(8):
        rows = lax.rsqrt(rows_ref[:, i : i + 1])
        every = pl.ds(i, block, stride=8)
        for lane in range(8):
            columns = slice(lane * 128, lane * 128 + 128)
            if i < 2:
                start = 512 * i + 128 * (lane % 4)
                grad = grad_ref[2 * (lane // 4), :, start : start + 128]
            else:
                grad = grad_ref[1 if i == 2 else i, :, columns]
            grad = grad.astype(jnp.float32)
            grads[lane, every, :] = grad
            change[lane, every, :] = grad * rows * scale_ref[i : i + 1, columns]
    for lane in range(8):
        columns = slice(lane * 128, lane * 128 + 128)
        grad_out[:, columns] = grads[lane]
        new = weight_ref[:, columns] - change[lane]
        new_out[:, columns] = new
        copy_out[:, columns] = new.astype(jnp.bfloat16)


def update_attention(grads, weights, rows, scale):
    block = 32
    wide = pl.BlockSpec((block * 8, D), lambda i: (i, 0))
    shape = jax.ShapeDtypeStruct
    new = pl.pallas_call(
        update_attention_kernel,
        grid=(256 // block,),
        out_shape=(
            shape((2048, D), jnp.float32),
            shape((2048, D), jnp.float32),
            shape((2048, D), jnp.bfloat16),
        ),
        in_specs=[
            pl.BlockSpec((8, block, D), lambda i: (0, i, 0)),
            wide,
            pl.BlockSpec((block, 128), lambda i: (i, 0)),
            pl.BlockSpec((16, D), lambda i: (0, 0)),
        ],
        out_specs=(wide,) * 3,
        scratch_shapes=[pltpu.VMEM((8, block * 8, 128), jnp.float32)] * 2,
        compiler_params=pltpu.CompilerParams(vmem_limit_bytes=62 * MIB),
    )(grads, weights.reshape(2048, D), rows, scale)
    return [t.reshape(256, 8, D) for t in new]


def update_kernel(
    first, slots, grad_ref, weight_ref, rows_ref, scale_ref, grad_out, new_out, copy_out
):
    spans = 4 if slots == 4 else 1
    wide = D // spans
    for i in range(slots):
        grads = grad_ref[i].astype(jnp.float32)
        changes = grads * (lax.rsqrt(rows_ref[...]) * scale_ref[first + i : first + i + 1, :])
        for s in range(spans):
            start = s * D + i * wide
            columns = slice(start, start + wide)
            part = slice(s * wide, s * wide + wide)
            grad_out[:, columns] = grads[:, part]
            new = weight_ref[:, columns] - changes[:, part]
            new_out[:, columns] = new
            copy_out[:, columns] = new.astype(jnp.bfloat16)


def update_plain(grads, weights, rows, scale, first, slots, grad_map):
    count, width = weights.shape
    block = 128 // slots
    wide = pl.BlockSpec((block, width), lambda i: (i, 0))
    shape = jax.ShapeDtypeStruct
    return pl.pallas_call(
        lambda *refs: update_kernel(first, slots, *refs),
        grid=(count // block,),
        out_shape=(
            shape(weights.shape, jnp.float32),
            shape(weights.shape, jnp.float32),
            shape(weights.shape, jnp.bfloat16),
        ),
        in_specs=[
            pl.BlockSpec((slots, block, D), grad_map),
            wide,
            pl.BlockSpec((block, 1), lambda i: (i, 0)),
            pl.BlockSpec((16, D), lambda i: (0, 0)),
        ],
        out_specs=(wide,) * 3,
        compiler_params=pltpu.CompilerParams(vmem_limit_bytes=62 * MIB),
    )(grads, weights, rows, scale)


def update_direct(grads, rows, scale, attention_weights, expand_weight, shrink_weight):
    shr_rows = rows[:, 9:13].T.reshape(-1, 1)
    attention = update_attention(grads, attention_weights, rows, scale)
    expand = update_plain(grads, expand_weight, rows[:, 8:9], scale, 8, 4, lambda i: (2, i, 0))
    shrink = update_plain(
        grads, shrink_weight, shr_rows, scale, 12, 1, lambda i: (12 + i // 2, i % 2, 0)
    )
    return attention, expand, shrink, (rows[:, 0:8].T, rows[:, 8], shr_rows[:, 0])


def as_rows(vector):
    rows = -(-vector.shape[0] // 1024) * 8
    return jnp.pad(vector, (0, rows * 128 - vector.shape[0])).reshape(rows, 128)


def masked_scores(query_part, key_heads, first_row, valid_count, causal):
    scores = jnp.einsum("qhd,khd->hqk", query_part, key_heads, preferred_element_type=jnp.float32)
    key_places = jnp.arange(key_heads.shape[0], dtype=jnp.int32)[None, :]
    usable = key_places < valid_count
    if causal:
        query_places = first_row + jnp.arange(query_part.shape[0], dtype=jnp.int32)[:, None]
        usable = usable & (key_places <= query_places)
    return jnp.where(usable[None], scores, MASKED)


def attend_forward(queries, key_heads, values, valid_count, causal):
    query_rows = queries.shape[0]
    step_rows = min(512, query_rows)
    outputs, stored = ([], [])
    for b in range(query_rows // step_rows):
        first_row = b * step_rows
        key_end = first_row + step_rows if causal else key_heads.shape[0]
        scores = masked_scores(
            queries[first_row : first_row + step_rows],
            key_heads[:key_end],
            first_row,
            valid_count,
            causal,
        )
        row_max = jnp.max(scores, axis=-1, keepdims=True)
        raised = jnp.exp(scores - row_max)
        totals = jnp.sum(raised, axis=-1, keepdims=True)
        probs_low = (raised / totals).astype(jnp.bfloat16)
        outputs.append(
            jnp.einsum(
                "hqk,khd->qhd", probs_low, values[:key_end], preferred_element_type=jnp.float32
            )
        )
        stored.append(row_max + jnp.log(totals))
    return (jnp.concatenate(outputs, axis=0), stored)


def attend_backward(queries, key_heads, values, grad_out, stored, valid_count, causal):
    query_rows = queries.shape[0]
    key_rows = key_heads.shape[0]
    step_rows = min(512, query_rows)
    grad_queries = []
    grad_keys = jnp.zeros(key_heads.shape, jnp.float32)
    grad_values = jnp.zeros(values.shape, jnp.float32)
    for b in range(query_rows // step_rows):
        first_row = b * step_rows
        key_end = first_row + step_rows if causal else key_rows
        query_part = queries[first_row : first_row + step_rows]
        grad_part = grad_out[first_row : first_row + step_rows]
        scores = masked_scores(query_part, key_heads[:key_end], first_row, valid_count, causal)
        probs = jnp.exp(scores - stored[b])
        probs_low = probs.astype(jnp.bfloat16)
        grad_probs = jnp.einsum(
            "qhd,khd->hqk", grad_part, values[:key_end], preferred_element_type=jnp.float32
        )
        value_part = jnp.einsum(
            "hqk,qhd->khd", probs_low, grad_part, preferred_element_type=jnp.float32
        )
        grad_scores = probs * (grad_probs - jnp.sum(probs * grad_probs, axis=-1, keepdims=True))
        scores_low = grad_scores.astype(jnp.bfloat16)
        grad_queries.append(
            jnp.einsum(
                "hqk,khd->qhd", scores_low, key_heads[:key_end], preferred_element_type=jnp.float32
            )
        )
        key_part = jnp.einsum(
            "hqk,qhd->khd", scores_low, query_part, preferred_element_type=jnp.float32
        )
        padding = ((0, key_rows - key_end), (0, 0), (0, 0))
        grad_keys = grad_keys + jnp.pad(key_part, padding)
        grad_values = grad_values + jnp.pad(value_part, padding)
    return (jnp.concatenate(grad_queries, axis=0), grad_keys, grad_values)


def gather_rows(piece):
    return lax.all_gather(piece, ("shard", "rep"), axis=0, tiled=True)


def own_piece(block, replicas):
    rows = block.shape[0] // replicas
    return lax.dynamic_slice_in_dim(block, lax.axis_index("rep") * rows, rows, axis=0)


def scatter_rows(grad):
    piece = lax.psum_scatter(
        grad.astype(jnp.bfloat16), ("shard", "rep"), scatter_dimension=0, tiled=True
    )
    return lax.all_gather(piece, "rep", axis=0, tiled=True)


def local_factors(grad, rows):
    square = grad * grad
    rows_new = DECAY_RATE * rows + (1.0 - DECAY_RATE) * jnp.mean(square + FACTOR_EPS, axis=-1)
    col_part = jnp.sum(square + FACTOR_EPS, axis=0)
    weighted = jnp.sum(square / rows_new[..., None], axis=0)
    return rows_new, col_part, weighted, jnp.sum(rows_new, axis=0)


def finish_factors(grad, weight, rows_new, cols, col_sum, weighted, row_total, row_count, rate):
    cols_new = DECAY_RATE * cols + (1.0 - DECAY_RATE) * col_sum / row_count
    mean_rows = row_total / row_count
    mean_square = mean_rows * jnp.sum(weighted / cols_new, axis=-1) / (row_count * cols.shape[-1])
    factor = rate / jnp.maximum(1.0, jnp.sqrt(mean_square) / CLIP_LEVEL)
    scaled = lax.rsqrt(cols_new / mean_rows[..., None]) * factor[..., None]
    fresh = weight - grad * (lax.rsqrt(rows_new)[..., None] * scaled[None])
    return fresh, cols_new


def plain_device(
    tokens,
    encoder,
    cotangent,
    lengths,
    encoder_lengths,
    dealt_order,
    attention_weights,
    expand_weight,
    shrink_weight,
    small_params,
    attention_rows,
    attention_cols,
    expand_rows,
    expand_cols,
    shrink_rows,
    shrink_cols,
    small_moment,
):
    devices = lax.axis_size(("rep", "shard"))
    replicas = lax.axis_size("rep")
    shards = lax.axis_size("shard")
    slot_tokens = tokens.shape[0]
    slot_states = encoder.shape[0]
    position = lax.axis_index(("rep", "shard"))
    inverse = (
        jnp.zeros((devices,), jnp.int32).at[dealt_order].set(jnp.arange(devices, dtype=jnp.int32))
    )
    qkv_piece = own_piece(attention_weights[:, 0:3, :].reshape(-1, 3 * D), replicas)
    rest_piece = own_piece(attention_weights[:, 3:8, :].reshape(-1, 5 * D), replicas)
    qkv_full = gather_rows(qkv_piece.astype(jnp.bfloat16))
    rest_full = gather_rows(rest_piece.astype(jnp.bfloat16))
    expand_full = gather_rows(own_piece(expand_weight, replicas).astype(jnp.bfloat16))
    shrink_full = gather_rows(own_piece(shrink_weight, replicas).astype(jnp.bfloat16))
    spread = lax.all_to_all(
        tokens.reshape(devices, slot_tokens // devices, D),
        ("rep", "shard"),
        split_axis=0,
        concat_axis=0,
        tiled=True,
    )
    picked = jnp.take(spread, inverse, axis=0)
    tokens = lax.all_to_all(
        picked, ("rep", "shard"), split_axis=0, concat_axis=0, tiled=True
    ).reshape(slot_tokens, D)
    states = encoder
    incoming = cotangent
    valid_tokens = lengths[position]
    valid_states = encoder_lengths[position]
    matrices = [qkv_full[:, i * D : (i + 1) * D] for i in range(3)] + [
        rest_full[:, i * D : (i + 1) * D] for i in range(5)
    ]
    parts = unpack(small_params)
    token_heads = (slot_tokens, HEADS, HEAD_DIM)
    state_heads = (slot_states, HEADS, HEAD_DIM)
    q_self = ((forward_product(tokens, matrices[0]) + parts[0]) * 0.125).astype(
        jnp.bfloat16
    )
    k_self = forward_product(tokens, matrices[1]).astype(jnp.bfloat16)
    v_self = (forward_product(tokens, matrices[2]) + parts[1]).astype(jnp.bfloat16)
    o_self, lse_self = attend_forward(
        q_self.reshape(token_heads),
        k_self.reshape(token_heads),
        v_self.reshape(token_heads),
        valid_tokens,
        True,
    )
    o_self_low = o_self.reshape(slot_tokens, D).astype(jnp.bfloat16)
    branch_a = forward_product(o_self_low, matrices[3]) + parts[2]
    tokens_wide = tokens.astype(jnp.float32)
    hidden_one, norm_one_back = jax.vjp(layer_norm, tokens_wide + branch_a, parts[8], parts[9])
    hidden_one_low = hidden_one.astype(jnp.bfloat16)
    q_cross = (
        (forward_product(hidden_one_low, matrices[4]) + parts[3]) * 0.125
    ).astype(jnp.bfloat16)
    k_cross = forward_product(states, matrices[5]).astype(jnp.bfloat16)
    v_cross = (forward_product(states, matrices[6]) + parts[4]).astype(jnp.bfloat16)
    o_cross, lse_cross = attend_forward(
        q_cross.reshape(token_heads),
        k_cross.reshape(state_heads),
        v_cross.reshape(state_heads),
        valid_states,
        False,
    )
    o_cross_low = o_cross.reshape(slot_tokens, D).astype(jnp.bfloat16)
    branch_c = forward_product(o_cross_low, matrices[7]) + parts[5]
    hidden_two, norm_two_back = jax.vjp(layer_norm, hidden_one + branch_c, parts[10], parts[11])
    hidden_two_low = hidden_two.astype(jnp.bfloat16)
    pre_act = forward_product(hidden_two_low, expand_full) + parts[6]
    activated, gelu_back = jax.vjp(gelu_exact, pre_act)
    activated_low = activated.astype(jnp.bfloat16)
    branch_m = forward_product(activated_low, shrink_full) + parts[7]
    result, norm_three_back = jax.vjp(layer_norm, hidden_two + branch_m, parts[12], parts[13])
    usable_rows = (jnp.arange(slot_tokens, dtype=jnp.int32) < valid_tokens).astype(jnp.float32)[
        :, None
    ]
    squares = jnp.stack(
        [
            jnp.sum(usable_rows * t * t)
            for t in (tokens_wide, branch_a, hidden_one, branch_c, hidden_two, branch_m)
        ]
    )
    d_third, d_gain_three, d_shift_three = norm_three_back(
        incoming.astype(jnp.float32) * usable_rows
    )
    d_mlp = d_third.astype(jnp.bfloat16)
    grad_shrink = weight_product(activated_low, d_mlp)
    grad_shrink_offset = row_sum(d_mlp)
    d_activated = input_product(d_mlp, shrink_full)
    d_pre = gelu_back(d_activated)[0].astype(jnp.bfloat16)
    grad_expand = weight_product(hidden_two_low, d_pre)
    grad_expand_offset = row_sum(d_pre)
    d_hidden_two = d_third + input_product(d_pre, expand_full)
    d_second, d_gain_two, d_shift_two = norm_two_back(d_hidden_two)
    d_branch_c = d_second.astype(jnp.bfloat16)
    grad_cross_out = weight_product(o_cross_low, d_branch_c)
    grad_cross_out_offset = row_sum(d_branch_c)
    d_o_cross = input_product(d_branch_c, matrices[7]).astype(jnp.bfloat16)
    grad_cq, grad_ck, grad_cv = attend_backward(
        q_cross.reshape(token_heads),
        k_cross.reshape(state_heads),
        v_cross.reshape(state_heads),
        d_o_cross.reshape(token_heads),
        lse_cross,
        valid_states,
        False,
    )
    dq_cross = (grad_cq.reshape(slot_tokens, D) * 0.125).astype(jnp.bfloat16)
    dk_cross = grad_ck.reshape(slot_states, D).astype(jnp.bfloat16)
    dv_cross = grad_cv.reshape(slot_states, D).astype(jnp.bfloat16)
    grad_cross_query = weight_product(hidden_one_low, dq_cross)
    grad_cross_key = weight_product(states, dk_cross)
    grad_cross_value = weight_product(states, dv_cross)
    state_grad = input_product(dk_cross, matrices[5]) + input_product(
        dv_cross, matrices[6]
    )
    d_hidden_one = d_second + input_product(dq_cross, matrices[4])
    d_first, d_gain_one, d_shift_one = norm_one_back(d_hidden_one)
    d_branch_a = d_first.astype(jnp.bfloat16)
    grad_self_out = weight_product(o_self_low, d_branch_a)
    grad_self_out_offset = row_sum(d_branch_a)
    d_o_self = input_product(d_branch_a, matrices[3]).astype(jnp.bfloat16)
    grad_sq, grad_sk, grad_sv = attend_backward(
        q_self.reshape(token_heads),
        k_self.reshape(token_heads),
        v_self.reshape(token_heads),
        d_o_self.reshape(token_heads),
        lse_self,
        valid_tokens,
        True,
    )
    dq_self = (grad_sq.reshape(slot_tokens, D) * 0.125).astype(jnp.bfloat16)
    dk_self = grad_sk.reshape(slot_tokens, D).astype(jnp.bfloat16)
    dv_self = grad_sv.reshape(slot_tokens, D).astype(jnp.bfloat16)
    grad_self_query = weight_product(tokens, dq_self)
    grad_self_key = weight_product(tokens, dk_self)
    grad_self_value = weight_product(tokens, dv_self)
    token_grad = (
        d_first
        + input_product(dq_self, matrices[0])
        + input_product(dk_self, matrices[1])
        + input_product(dv_self, matrices[2])
    )
    small_partial = jnp.concatenate(
        [
            row_sum(dq_self),
            row_sum(dv_self),
            grad_self_out_offset,
            row_sum(dq_cross),
            row_sum(dv_cross),
            grad_cross_out_offset,
            grad_expand_offset,
            grad_shrink_offset,
            d_gain_one,
            d_shift_one,
            d_gain_two,
            d_shift_two,
            d_gain_three,
            d_shift_three,
        ]
    )
    totals = lax.psum(jnp.concatenate([small_partial, squares]), ("rep", "shard"))
    g_shrink = scatter_rows(grad_shrink)
    g_expand = scatter_rows(grad_expand)
    g_rest = scatter_rows(
        jnp.concatenate(
            [grad_self_out, grad_cross_query, grad_cross_key, grad_cross_value, grad_cross_out],
            axis=1,
        )
    )
    g_qkv = scatter_rows(
        jnp.concatenate([grad_self_query, grad_self_key, grad_self_value], axis=1)
    )
    g_attention = (
        jnp.concatenate([g_qkv, g_rest], axis=1).reshape(-1, 8, D).astype(jnp.float32)
    )
    g_expand = g_expand.astype(jnp.float32)
    g_shrink = g_shrink.astype(jnp.float32)
    attention_rows_new, *attention_parts = local_factors(g_attention, attention_rows.T)
    expand_rows_new, *expand_parts = local_factors(g_expand, expand_rows)
    shrink_rows_new, *shrink_parts = local_factors(g_shrink, shrink_rows)
    flat = attention_parts + expand_parts + shrink_parts
    summed = lax.psum(jnp.concatenate([t.reshape(-1) for t in flat]), "shard")
    sums = []
    offset = 0
    for t in flat:
        sums.append(summed[offset : offset + t.size].reshape(t.shape))
        offset = offset + t.size
    attention_rates = STEP_RATE * jnp.where(jnp.arange(8) % 4 == 3, OUT_GAIN, 1.0).astype(
        jnp.float32
    )
    attention_new, attention_cols_new = finish_factors(
        g_attention,
        attention_weights,
        attention_rows_new,
        attention_cols,
        *sums[0:3],
        D,
        attention_rates,
    )
    expand_new, expand_cols_new = finish_factors(
        g_expand, expand_weight, expand_rows_new, expand_cols, *sums[3:6], D, STEP_RATE
    )
    shrink_new, shrink_cols_new = finish_factors(
        g_shrink, shrink_weight, shrink_rows_new, shrink_cols, *sums[6:9], FF, STEP_RATE
    )
    small_grad = totals[: small_params.shape[0]]
    small_moment_new = DECAY_RATE * small_moment + (1.0 - DECAY_RATE) * (
        small_grad * small_grad + FACTOR_EPS
    )
    small_update = small_grad * lax.rsqrt(small_moment_new)
    small_scale = jnp.sqrt(jnp.mean(small_update * small_update))
    small_new = small_params - SMALL_RATE * small_update / jnp.maximum(
        1.0, small_scale / CLIP_LEVEL
    )
    norm_stats = jnp.sqrt(
        totals[small_params.shape[0] :] / (jnp.sum(lengths).astype(jnp.float32) * D)
    )
    return (
        result.astype(jnp.bfloat16),
        token_grad.astype(jnp.bfloat16),
        state_grad.astype(jnp.bfloat16),
        g_attention,
        g_expand,
        g_shrink,
        small_grad,
        attention_new,
        expand_new,
        shrink_new,
        small_new,
        attention_new.astype(jnp.bfloat16),
        expand_new.astype(jnp.bfloat16),
        shrink_new.astype(jnp.bfloat16),
        attention_rows_new.T,
        attention_cols_new,
        expand_rows_new,
        expand_cols_new,
        shrink_rows_new,
        shrink_cols_new,
        small_moment_new,
        norm_stats,
    )


def direct_device(
    tokens,
    encoder,
    cotangent,
    lengths,
    encoder_lengths,
    dealt_order,
    attention_weights,
    expand_weight,
    shrink_weight,
    small_params,
    attention_rows,
    attention_cols,
    expand_rows,
    expand_cols,
    shrink_rows,
    shrink_cols,
    small_moment,
):
    position = lax.axis_index(("rep", "shard"))
    inverse = jnp.zeros((32,), jnp.int32).at[dealt_order].set(jnp.arange(32, dtype=jnp.int32))
    valid = jnp.stack([lengths[position], encoder_lengths[position]])
    parts = unpack(small_params)
    blank = jnp.zeros((D,), jnp.float32)
    params = jnp.concatenate(
        [
            small_params[0 : 6 * D].reshape(6, D),
            hidden_blocks(parts[6]),
            small_params[6 * D + FF :].reshape(7, D),
            jnp.zeros((7, D), jnp.float32),
        ]
    )
    gains = jnp.stack([parts[8], parts[10]] + [blank] * 6)
    pieces = weight_pieces(attention_weights, expand_weight, shrink_weight, neighbours())
    (
        tokens,
        full,
        q_self,
        k_self,
        v_self,
        o_self,
        lse_self,
        q_cross,
        k_cross,
        v_cross,
        o_cross,
        lse_cross,
        summed_one,
        summed_two,
        hidden_one,
        hidden_two,
        activated,
        slope,
        output,
        d_mlp,
        d_third,
        small_first,
    ) = forward(inverse, valid, tokens, pieces, encoder, cotangent, params)
    factor_rows = jnp.concatenate(
        [attention_rows, expand_rows.reshape(1, 256), shrink_rows.reshape(4, 256)]
    )
    factor_rows = jnp.pad(factor_rows.T, ((0, 0), (0, 115)))
    factor_cols = jnp.concatenate(
        [attention_cols, hidden_blocks(expand_cols), shrink_cols.reshape(1, D), jnp.ones((3, D))]
    )
    token_grad, state_grad, reduced, totals, factor_rows, factor_cols, scale = backward(
        valid,
        (
            d_mlp,
            d_third,
            activated,
            slope,
            full.reshape(GATHERED, 1024, D),
            hidden_two,
            hidden_one,
            tokens.reshape(1024, D),
            encoder,
            o_cross,
            o_self,
            summed_one,
            summed_two,
            q_self,
            k_self,
            v_self,
            q_cross,
            k_cross,
            v_cross,
            lse_self,
            lse_cross,
        ),
        gains,
        small_first,
        factor_rows,
        factor_cols,
    )
    attention, expand, shrink, rows_new = update_direct(
        reduced, factor_rows, scale, attention_weights, expand_weight, shrink_weight
    )
    cols_new = (factor_cols[0:8], hidden_flat(factor_cols[8:12]), factor_cols[12])
    small_grad = jnp.concatenate(
        [totals[0:6].reshape(-1), hidden_flat(totals[6:10]), totals[10:17].reshape(-1)]
    )
    small_moment_new = DECAY_RATE * small_moment + (1.0 - DECAY_RATE) * (
        small_grad * small_grad + FACTOR_EPS
    )
    small_update = small_grad * lax.rsqrt(small_moment_new)
    small_scale = jnp.sqrt(jnp.mean(small_update * small_update))
    small_new = small_params - SMALL_RATE * small_update / jnp.maximum(
        1.0, small_scale / CLIP_LEVEL
    )
    norm_stats = jnp.sqrt(totals[17, 0:6] / (jnp.sum(lengths).astype(jnp.float32) * D))
    return (
        output,
        token_grad,
        state_grad,
        attention[0],
        expand[0],
        shrink[0],
        small_grad,
        attention[1],
        expand[1],
        shrink[1],
        small_new,
        attention[2],
        expand[2],
        shrink[2],
        rows_new[0],
        cols_new[0],
        rows_new[1],
        cols_new[1],
        rows_new[2],
        cols_new[2],
        small_moment_new,
        norm_stats,
    )


def on_device(*args):
    if lax.axis_size("rep") == 8 and lax.axis_size("shard") == 4:
        return direct_device(*args)
    return plain_device(*args)


def solution(mesh):
    in_specs = (
        P(("rep", "shard"), None),
        P(("rep", "shard"), None),
        P(("rep", "shard"), None),
        P(),
        P(),
        P(),
        P("shard", None, None),
        P("shard", None),
        P("shard", None),
        P(),
        P(None, "shard"),
        P(),
        P("shard"),
        P(),
        P("shard"),
        P(),
        P(),
    )
    out_specs = (
        P(("rep", "shard"), None),
        P(("rep", "shard"), None),
        P(("rep", "shard"), None),
        P("shard", None, None),
        P("shard", None),
        P("shard", None),
        P(),
        P("shard", None, None),
        P("shard", None),
        P("shard", None),
        P(),
        P("shard", None, None),
        P("shard", None),
        P("shard", None),
        P(None, "shard"),
        P(),
        P("shard"),
        P(),
        P("shard"),
        P(),
        P(),
        P(),
    )
    return jax.shard_map(
        on_device, mesh=mesh, in_specs=in_specs, out_specs=out_specs, check_vma=False
    )
```

```python
import math

import jax
import jax.numpy as jnp
from jax import lax
from jax.experimental import pallas as pl
from jax.experimental.pallas import tpu as pltpu
from jax.sharding import PartitionSpec as P

D = 1024
HEADS = 16
HEAD_DIM = 64
FF = 4096


DECAY_RATE = 0.5
CLIP_LEVEL = 0.25
STEP_RATE = 0.1
SMALL_RATE = 0.4
OUT_GAIN = 8.0
NORM_EPS = 1e-05
FACTOR_EPS = 1e-30
MASKED = -1e30
MESH = pl.DeviceIdType.MESH
CHUNKS = 16
GATHERED = 16
EXPAND_AT = (8, 9, 11, 13)
SHRINK_AT = (10, 12, 14, 15)
MIB = 1 << 20


def layer_norm(r, norm_gain, norm_shift):
    centred = r - jnp.mean(r, axis=-1, keepdims=True)
    spread = jnp.mean(centred * centred, axis=-1, keepdims=True)
    return centred * lax.rsqrt(spread + NORM_EPS) * norm_gain + norm_shift


def gelu_exact(values):
    return jax.nn.gelu(values, approximate=False)


def unpack(small):
    extents = [D] * 6 + [FF] + [D] * 7
    pieces = []
    offset = 0
    for extent in extents:
        pieces.append(small[offset : offset + extent])
        offset = offset + extent
    return pieces


def forward_product(source, matrix):
    return jnp.dot(source, matrix, preferred_element_type=jnp.float32)


def input_product(grad_low, matrix):
    return jnp.einsum("to,io->ti", grad_low, matrix, preferred_element_type=jnp.float32)


def weight_product(source, grad_low):
    return jnp.einsum("ti,to->io", source, grad_low, preferred_element_type=jnp.float32)


def row_sum(grad_low):
    return jnp.sum(grad_low.astype(jnp.float32), axis=0)


def transposed(block):
    return block.astype(jnp.float32).T.astype(jnp.bfloat16)


def half_lanes(shape, dim):
    return lax.broadcasted_iota(jnp.int32, shape, dim)


def masked_keys(keys, length, head):
    place = half_lanes(keys.shape, 0)
    lane = half_lanes(keys.shape, 1)
    blocked = jnp.where((lane == 64 - 64 * head) & (place >= length), MASKED, 0.0)
    own = (lane >= 64 * head) & (lane < 64 * head + 64)
    return jnp.where(own, keys.astype(jnp.float32), blocked).astype(jnp.bfloat16)


def own_head(rows_t, head, fill):
    place = half_lanes(rows_t.shape, 0)
    own = (place >= 64 * head) & (place < 64 * head + 64)
    other = jnp.where(place == 64 - 64 * head, fill, 0.0)
    return jnp.where(own, rows_t.astype(jnp.float32), other).astype(jnp.bfloat16)


def product(first, second):
    return jnp.dot(first, second, preferred_element_type=jnp.float32)


def causal_mask(scores, step):
    kept = scores.shape[0] - step
    last = scores[kept:]
    allowed = half_lanes(last.shape, 0) <= half_lanes(last.shape, 1)
    last = jnp.where(allowed, last, MASKED)
    return last if kept == 0 else jnp.concatenate([scores[:kept], last], axis=0)


def attend_pair(
    causal, step, length, q_ref, k_ref, v_ref, o_ref, lse_ref, o_t, first_row=0
):
    count = q_ref.shape[0]
    q_t = transposed(q_ref[...])
    v_t = transposed(v_ref[...])
    keys = [masked_keys(k_ref[...], length, head) for head in range(2)]
    queries = [own_head(q_t, head, 1.0) for head in range(2)]
    units = [(head, start) for start in range(0, count, step) for head in range(2)]

    def scores_of(head, start):
        end = first_row + start + step if causal else k_ref.shape[0]
        return product(keys[head][:end], queries[head][:, start : start + step])

    ahead = scores_of(*units[0])
    for index, (head, start) in enumerate(units):
        scores = ahead
        if index + 1 < len(units):
            ahead = scores_of(*units[index + 1])
        rows = slice(64 * head, 64 * head + 64)
        columns = slice(start, start + step)
        if causal:
            scores = causal_mask(scores, step)
        top = jnp.max(scores, axis=0, keepdims=True)
        raised = jnp.exp(scores - top)
        total = jnp.sum(raised, axis=0, keepdims=True)
        probs = (raised * (1.0 / total)).astype(jnp.bfloat16)
        o_t[rows, columns] = product(v_t[rows, : scores.shape[0]], probs)
        place = slice(first_row + start, first_row + start + step)
        lse_ref[0, head : head + 1, place] = top + jnp.log(total)
    o_ref[...] = o_t[:, :count].T.astype(jnp.bfloat16)


def attend_back_pair(
    causal,
    step,
    length,
    q_ref,
    k_ref,
    v_ref,
    do_ref,
    lse_ref,
    dq_ref,
    dk_ref,
    dv_ref,
    put_sums,
    dq_t,
    dk_sum,
    dv_sum,
):
    key_rows = k_ref.shape[0]
    q_t = transposed(q_ref[...])
    k_t = transposed(k_ref[...])
    do_t = transposed(do_ref[...])
    values = v_ref[...]
    keys = [masked_keys(k_ref[...], length, head) for head in range(2)]
    queries = [own_head(q_t, head, 1.0) for head in range(2)]
    grads = [own_head(do_t, head, 0.0) for head in range(2)]
    count = q_ref.shape[0] // step
    units = [(head, b) for b in reversed(range(count)) for head in range(2)]

    def products_of(head, b):
        columns = slice(b * step, b * step + step)
        end = b * step + step if causal else key_rows
        scores = product(keys[head][:end], queries[head][:, columns])
        return scores, product(values[:end], grads[head][:, columns])

    ahead = products_of(*units[0])
    for index, (head, b) in enumerate(units):
        scores, d_probs = ahead
        if index + 1 < len(units):
            ahead = products_of(*units[index + 1])
        rows = slice(64 * head, 64 * head + 64)
        columns = slice(b * step, b * step + step)
        end = scores.shape[0]
        if causal:
            scores = causal_mask(scores, step)
        probs = jnp.exp(scores - lse_ref[0, head : head + 1, columns])
        weighted = probs * d_probs
        delta = jnp.sum(weighted, axis=0, keepdims=True)
        d_scores = (weighted - probs * delta).astype(jnp.bfloat16)
        dv = product(probs.astype(jnp.bfloat16), do_ref[columns, :])
        dk = product(d_scores, q_ref[columns, :])
        if b == count - 1:
            dv_sum[head, :end] = dv
            dk_sum[head, :end] = dk
        else:
            dv_sum[head, :end] += dv
            dk_sum[head, :end] += dk
        dq_t[rows, columns] = product(k_t[rows, :end], d_scores)
    first = half_lanes((key_rows, 128), 1) < 64
    dk_ref[...] = jnp.where(first, dk_sum[0, :key_rows], dk_sum[1, :key_rows]).astype(jnp.bfloat16)
    dv = jnp.where(first, dv_sum[0, :key_rows], dv_sum[1, :key_rows]).astype(jnp.bfloat16)
    dv_ref[...] = dv
    dq = (dq_t[...] * 0.125).T.astype(jnp.bfloat16)
    dq_ref[...] = dq
    put_sums(
        jnp.sum(dq.astype(jnp.float32), axis=0, keepdims=True),
        jnp.sum(dv.astype(jnp.float32), axis=0, keepdims=True),
    )


SCALARS = pl.BlockSpec(memory_space=pltpu.SMEM)


def neighbours():
    rep = lax.axis_index("rep")
    z = lax.axis_index("shard")
    core = rep % 2
    x = (rep // 2) % 2
    y = rep // 4
    other_core = (rep + 1 - 2 * core, z)
    other_x = (rep + 2 - 4 * x, z)
    other_y = (rep + 4 - 8 * y, z)
    others_z = [(rep, (z + d) % 4) for d in (1, 2, 3)]
    return core, x, y, z, other_core, other_x, other_y, others_z


def greet(devices):
    barrier = pltpu.get_barrier_semaphore()
    for device in devices:
        pl.semaphore_signal(barrier, inc=1, device_id=device, device_id_type=MESH)
    pl.semaphore_wait(barrier, len(devices))


def remote(src, dst, send, recv, device):
    return pltpu.make_async_remote_copy(
        src_ref=src, dst_ref=dst, send_sem=send, recv_sem=recv, device_id=device, device_id_type=MESH
    )


def gather_copies(refs, c, parity, places):
    piece, full, place_sem, z_send, z_recv, send, recv = refs
    core, x, y, z, other_core, other_x, other_y, others_z = places
    a = x + parity * (y - x)
    b = y + parity * (x - y)
    first = (other_x[0] + parity * (other_y[0] - other_x[0]), z)
    second = (other_y[0] + parity * (other_x[0] - other_y[0]), z)
    own = pl.ds(pl.multiple_of(core * 128 + a * 64 + b * 32, 32), 32)
    steps = (
        (own, second),
        (pl.ds(pl.multiple_of(core * 128 + a * 64, 64), 64), first),
        (pl.ds(pl.multiple_of(core * 128, 128), 128), other_core),
    )

    def local():
        return pltpu.make_async_copy(piece.at[c], full.at[c, z, own, :], place_sem.at[c])

    def line(d):
        return remote(
            piece.at[c], full.at[c, z, own, :], z_send.at[c, d], z_recv.at[c, d], others_z[d]
        )

    def pair(k):
        block = full.at[c, :, steps[k][0], :]
        return remote(block, block, send.at[k, c], recv.at[k, c], steps[k][1])

    return local, line, pair


def gather_stage(k, refs, c, parity, places):
    local, line, pair = gather_copies(refs, c, parity, places)
    if k == 0:
        local().start()
        for d in range(3):
            line(d).start()
    if k == 1:
        local().wait()
        for d in range(3):
            line(d).wait_recv()
        pair(0).start()
    if k == 2 or k == 3:
        pair(k - 2).wait_recv()
        pair(k - 1).start()
    if k == 4:
        pair(2).wait()
        pair(1).wait_send()
        pair(0).wait_send()
        for d in range(3):
            line(d).wait_send()


def gather_sems(count):
    dma = pltpu.SemaphoreType.DMA
    return [dma((count,)), dma((count, 3)), dma((count, 3)), dma((3, count)), dma((3, count))]


def own_rows(blocks, parity, places):
    core, x, y = places[0:3]
    a = x + parity * (y - x)
    b = y + parity * (x - y)
    rows = lax.dynamic_slice_in_dim(blocks, core * 128 + a * 64 + b * 32, 32, axis=-2)
    return rows.astype(jnp.bfloat16)


def hidden_blocks(values):
    split = values.reshape(values.shape[:-1] + (4, 4, 256))
    split = jnp.swapaxes(split, -3, -2)
    return split.reshape(values.shape[:-1] + (4, 1024))


def hidden_flat(blocks):
    split = blocks.reshape(blocks.shape[:-2] + (4, 4, 256))
    split = jnp.swapaxes(split, -3, -2)
    return split.reshape(blocks.shape[:-2] + (FF,))


def weight_pieces(attention, expand, shrink, places):
    attention = [own_rows(jnp.swapaxes(attention, 0, 1), p, places) for p in range(2)]
    expand = [jnp.swapaxes(hidden_blocks(own_rows(expand, p, places)), 0, 1) for p in range(2)]
    shrink = [own_rows(shrink.reshape(4, 256, D), p, places) for p in range(2)]
    picked = [attention[c % 2][c] for c in range(8)]
    for c in range(8, GATHERED):
        if c in EXPAND_AT:
            picked.append(expand[c % 2][EXPAND_AT.index(c)])
        else:
            picked.append(shrink[c % 2][SHRINK_AT.index(c)])
    return jnp.stack(picked)


def fold(tile):
    return jnp.sum(tile.reshape(-1, 8, tile.shape[-1]), axis=0)


GATHER_PLAN = (("z", 6.5), ("second", 6.5), ("first", 11.5), ("core", 3.0), (None, 0.0))


class GatherPlanner:
    def __init__(self, count):
        self.now = 0.0
        self.links = {"core": 0.0, "x": 0.0, "y": 0.0, "z": 0.0}
        self.stage = {c: 0 for c in range(count)}
        self.ready = {c: 0.0 for c in range(count)}
        self.opened = count

    def can(self, c):
        if self.stage[c] == 0 and c >= 2 and self.stage[c - 2] < 2:
            return False
        return self.stage[c] < 5

    def spend(self, now, **busy):
        self.now = max(self.now, now)
        for link, span in busy.items():
            self.links[link] = max(self.links[link], self.now) + span

    def emit(self, c):
        stage = self.stage[c]
        link, span = GATHER_PLAN[stage]
        first, second = ("x", "y") if c % 2 == 0 else ("y", "x")
        link = {"first": first, "second": second}.get(link, link)
        self.now = max(self.now, self.ready[c]) + 0.1
        if link is not None:
            begin = max(self.now, self.links[link])
            self.links[link] = begin + span - 1.0
            self.ready[c] = begin + span
        self.stage[c] = stage + 1
        return (stage, c)

    def tick(self, spent):
        self.now += spent
        events = []
        progress = True
        while progress:
            progress = False
            for c in range(self.opened):
                if self.can(c) and self.ready[c] <= self.now:
                    events.append(self.emit(c))
                    progress = True
        return events

    def until(self, c):
        events = []
        while self.stage[c] < 5:
            choices = [i for i in range(self.opened) if self.can(i)]
            best = min(choices, key=lambda i: (self.ready[i], i))
            events.append(self.emit(best))
        return events


def gelu_parts(u):
    share = 0.5 + 0.5 * lax.erf(u * math.sqrt(0.5))
    bell = jnp.exp(-0.5 * u * u) * (1.0 / math.sqrt(2.0 * math.pi))
    return u * share, share + u * bell


def norm_parts(values):
    centred = values - jnp.mean(values, axis=1, keepdims=True)
    spread = jnp.mean(centred * centred, axis=1, keepdims=True)
    scale = lax.rsqrt(spread + NORM_EPS)
    return centred * scale, scale


def forward_kernel(
    order_ref,
    lengths_ref,
    tokens_ref,
    piece_ref,
    e_ref,
    cot_ref,
    par,
    x_out,
    full_ref,
    q_out,
    k_out,
    v_out,
    o_out,
    lse_out,
    cq_out,
    ck_out,
    cv_out,
    oc_out,
    lse_cross_out,
    r1_out,
    r2_out,
    h1_out,
    h2_out,
    g_out,
    gp_out,
    y_out,
    dm_out,
    d_third_out,
    small_out,
    pool,
    acc,
    held,
    o_t,
    lse_held,
    states,
    x_held,
    spread_first,
    spread_second,
    picked,
    load_sem,
    store_sem,
    state_sem,
    acc_sem,
    spread_send,
    spread_recv,
    back_send,
    back_recv,
    *gather_sem,
):
    places = neighbours()
    refs = (piece_ref, full_ref) + gather_sem
    planner = GatherPlanner(GATHERED)
    length = lengths_ref[0]
    me = lax.axis_index("rep") * 4 + places[3]
    spread = (spread_first, spread_second)

    def device(offset):
        j = lax.rem(me + offset, 32)
        return j, (j // 4, j % 4)

    def spread_copy(p, offset):
        j, target = device(offset)
        return remote(
            tokens_ref.at[32 * p + j],
            spread[p].at[me],
            spread_send.at[p, offset],
            spread_recv.at[p, offset],
            target,
        )

    def back_copy(p, offset):
        return remote(
            picked.at[32 * p + offset],
            x_held.at[32 * p + me],
            back_send.at[p, offset],
            back_recv.at[p, offset],
            device(offset)[1],
        )

    def own_spread(p):
        return pltpu.make_async_copy(
            tokens_ref.at[32 * p + me], spread[p].at[me], spread_recv.at[p, 0]
        )

    def own_back(p):
        return pltpu.make_async_copy(
            picked.at[32 * p], x_held.at[32 * p + me], back_recv.at[p, 0]
        )

    def each_other(act):
        def body(offset, carry):
            act(offset)
            return carry

        lax.fori_loop(1, 32, body, 0)

    def start_spread(p):
        own_spread(p).start()
        each_other(lambda offset: spread_copy(p, offset).start())

    def turn_back(p):
        own_spread(p).wait()
        each_other(lambda offset: spread_copy(p, offset).wait())
        picked[32 * p] = spread[p][order_ref[me]]
        own_back(p).start()

        def pick(offset):
            picked[32 * p + offset] = spread[p][order_ref[device(offset)[0]]]
            back_copy(p, offset).start()

        each_other(pick)

    def arrive(p):
        own_back(p).wait()
        each_other(lambda offset: back_copy(p, offset).wait())

    def emit_all(events):
        for stage, c in events:
            gather_stage(stage, refs, c, c % 2, places)

    def tick(spent):
        emit_all(planner.tick(spent))

    def load(slot, source):
        return pltpu.make_async_copy(source, pool.at[slot], load_sem.at[slot])

    def store(slot, target):
        return pltpu.make_async_copy(pool.at[slot], target, store_sem.at[slot])

    def product_into(left, right, put):
        def body(i, carry):
            n = pl.multiple_of(i * 256, 256)
            put(n, product(left(), pool[right, :, pl.ds(n, 256)]))
            return carry

        lax.fori_loop(0, 4, body, 0)

    def row(index, n):
        return par[index : index + 1, pl.ds(n, 256)]

    def put_low(slot, offset=None, scale=None):
        def put(n, value):
            if offset is not None:
                value = value + row(offset, n)
            if scale is not None:
                value = value * scale
            pool[slot, :, pl.ds(n, 256)] = value.astype(jnp.bfloat16)

        return put

    def put_acc(offset):
        def put(n, value):
            acc[:, pl.ds(n, 256)] = value + row(offset, n)

        return put

    def load_weight(c, slot):
        target = pool.at[slot].reshape(4, 256, D)
        return pltpu.make_async_copy(full_ref.at[c], target, load_sem.at[slot])

    def weight(c, slot):
        emit_all(planner.until(c))
        return load_weight(c, slot)

    def attend_loop(causal, step, valid, query, key, value, out, spent, rows, key_rows):
        ahead = [planner.tick(spent) for _ in range(8)]
        first_row, count = rows

        def body(i, carry):
            lanes = pl.ds(pl.multiple_of(i * 128, 128), 128)
            attend_pair(
                causal,
                step,
                valid,
                query.at[pl.ds(first_row, count), lanes],
                key.at[pl.ds(0, key_rows), lanes],
                value.at[pl.ds(0, key_rows), lanes],
                out.at[pl.ds(first_row, count), lanes],
                lse_held.at[pl.ds(i, 1)],
                o_t,
                first_row,
            )
            for n in range(8):
                if ahead[n]:

                    @pl.when(i == n)
                    def _(events=ahead[n]):
                        emit_all(events)

            return carry

        lax.fori_loop(0, 8, body, 0)

    TILE = 128

    def over_rows(sums, body):
        zero = jnp.zeros((8, D), jnp.float32)

        def step(i, carry):
            r = pl.multiple_of(i * TILE, TILE)
            place = half_lanes((TILE, 1), 0) + r
            usable = (place < length).astype(jnp.float32)
            terms = body(pl.ds(r, TILE), usable)
            return tuple(c + fold(t) for c, t in zip(carry, terms))

        totals = lax.fori_loop(0, D // TILE, step, (zero,) * sums)
        return [jnp.sum(t, axis=0, keepdims=True) for t in totals]

    lane = half_lanes((1, D), 1)

    def square_at(index, total):
        small_out[17:18, :] += jnp.where(lane == index, jnp.sum(total), 0.0)

    barrier = pltpu.get_barrier_semaphore()

    def greet_one(offset):
        pl.semaphore_signal(barrier, inc=1, device_id=device(offset)[1], device_id_type=MESH)

    each_other(greet_one)
    pl.semaphore_wait(barrier, 31)
    planner.opened = 3
    tick(0.5)
    start_spread(0)
    planner.spend(2.0, z=21.0, x=10.0, y=10.0)
    e_load = pltpu.make_async_copy(e_ref, states.at[2], state_sem.at[2])
    e_load.start()
    load(9, cot_ref).start()
    small_out[...] = jnp.zeros_like(small_out)
    tick(10.0)
    emit_all(planner.tick(12.0))
    turn_back(0)
    start_spread(1)
    planner.spend(34.0, z=42.0, x=20.0, y=20.0)
    tick(10.0)
    emit_all(planner.tick(15.0))
    for i in range(3):
        weight(i, 1 + i).start()
    turn_back(1)
    planner.spend(80.0, z=21.0, x=10.0, y=10.0)
    planner.opened = GATHERED
    tick(1.0)
    arrive(0)
    planner.spend(82.0)

    for p in range(2):
        if p == 1:
            arrive(1)
            planner.spend(106.0)
            x_store = pltpu.make_async_copy(x_held, x_out, acc_sem.at[1])
            x_store.start()
        rows = slice(512 * p, 512 * p + 512)
        for i, (slot, offset, scale) in enumerate(((4, 0, 0.125), (5, None, None), (6, 1, None))):
            if p == 0:
                load_weight(i, 1 + i).wait()

            def put_rows(n, value, slot=slot, offset=offset, scale=scale, rows=rows):
                if offset is not None:
                    value = value + row(offset, n)
                if scale is not None:
                    value = value * scale
                pool[slot, rows, pl.ds(n, 256)] = value.astype(jnp.bfloat16)

            product_into(
                lambda p=p: x_held[32 * p : 32 * p + 32].reshape(512, D), 1 + i, put_rows
            )
        if p == 1:
            store(4, q_out).start()
            store(5, k_out).start()
            store(6, v_out).start()
        tick(4.0)
        attend_loop(
            True,
            256,
            length,
            pool.at[4],
            pool.at[5],
            pool.at[6],
            pool.at[7],
            (1.6, 3.4)[p],
            (512 * p, 512),
            512 * p + 512,
        )
    store(7, o_out).start()
    lse_copy = pltpu.make_async_copy(lse_held, lse_out, state_sem.at[3])
    lse_copy.start()
    w_copy = weight(3, 1)
    w_copy.start()
    w_copy.wait()
    product_into(lambda: pool[7], 1, put_acc(2))
    tick(2.5)
    store(4, q_out).wait()

    def first_norm(rows, usable):
        held_rows = pl.ds(pl.multiple_of(rows.start // 16, TILE // 16), TILE // 16)
        x = x_held[held_rows].reshape(TILE, D).astype(jnp.float32)
        a = acc[rows, :]
        total = x + a
        acc[rows, :] = total
        h = norm_parts(total)[0] * par[11:12, :] + par[12:13, :]
        held[rows, :] = h
        pool[4, rows, :] = h.astype(jnp.bfloat16)
        return usable * x * x, usable * a * a, usable * h * h

    for index, total in enumerate(over_rows(3, first_norm)):
        square_at(index, total)
    store(4, h1_out).start()
    r1_copy = pltpu.make_async_copy(acc, r1_out, acc_sem.at[0])
    r1_copy.start()
    tick(4.0)

    for c, slot in ((4, 2), (5, 3), (6, 1)):
        weight(c, slot).start()
    store(5, k_out).wait()
    load_weight(4, 2).wait()
    product_into(lambda: pool[4], 2, put_low(5, 3, 0.125))
    store(5, cq_out).start()
    w_copy = weight(7, 2)
    w_copy.start()
    tick(2.5)
    e_load.wait()
    load_weight(5, 3).wait()
    load_weight(6, 1).wait()

    def put_keys(n, value):
        states[0, :, pl.ds(n, 256)] = value.astype(jnp.bfloat16)

    def put_values(n, value):
        states[1, :, pl.ds(n, 256)] = (value + row(4, n)).astype(jnp.bfloat16)

    product_into(lambda: states[2], 3, put_keys)
    product_into(lambda: states[2], 1, put_values)
    state_stores = [
        pltpu.make_async_copy(states.at[0], ck_out, state_sem.at[0]),
        pltpu.make_async_copy(states.at[1], cv_out, state_sem.at[1]),
    ]
    for copy in state_stores:
        copy.start()
    tick(1.0)
    store(6, v_out).wait()
    lse_copy.wait()
    attend_loop(
        False,
        512,
        lengths_ref[1],
        pool.at[5],
        states.at[0],
        states.at[1],
        pool.at[6],
        1.6,
        (0, 1024),
        128,
    )
    store(6, oc_out).start()
    lse_copy = pltpu.make_async_copy(lse_held, lse_cross_out, state_sem.at[3])
    lse_copy.start()
    w_copy.wait()
    r1_copy.wait()
    product_into(lambda: pool[6], 2, put_acc(5))
    tick(2.5)
    weight(EXPAND_AT[0], 0).start()
    weight(SHRINK_AT[0], 2).start()
    store(7, o_out).wait()

    def second_norm(rows, usable):
        c = acc[rows, :]
        total = held[rows, :] + c
        acc[rows, :] = total
        h = norm_parts(total)[0] * par[13:14, :] + par[14:15, :]
        held[rows, :] = h
        pool[7, rows, :] = h.astype(jnp.bfloat16)
        return usable * c * c, usable * h * h

    for index, total in enumerate(over_rows(2, second_norm)):
        square_at(3 + index, total)
    store(7, h2_out).start()
    r2_copy = pltpu.make_async_copy(acc, r2_out, acc_sem.at[0])
    r2_copy.start()
    tick(4.0)

    store(4, h1_out).wait()
    store(5, cq_out).wait()
    g_slots, slope_slots = (4, 6), (5, 8)
    r2_copy.wait()
    store(6, oc_out).wait()
    for j in range(5):
        if j > 1:
            store(g_slots[j % 2], g_out.at[j - 2]).wait()
            store(slope_slots[j % 2], gp_out.at[j - 2]).wait()
        if j < 4:
            load_weight(EXPAND_AT[j], j % 2).wait()
        if j > 0:
            load_weight(SHRINK_AT[j - 1], 2 + (j - 1) % 2).wait()

        def body(i, carry, j=j):
            n = pl.multiple_of(i * 256, 256)
            here = pl.ds(n, 256)
            if j < 4:
                u = product(pool[7], pool[j % 2, :, here]) + row(6 + j, n)
            if j > 0:
                more = product(pool[g_slots[(j - 1) % 2]], pool[2 + (j - 1) % 2, :, here])
                if j == 1:
                    acc[:, here] = more + row(10, n)
                else:
                    acc[:, here] += more
            if j < 4:
                g, slope = gelu_parts(u)
                pool[g_slots[j % 2], :, here] = g.astype(jnp.bfloat16)
                pool[slope_slots[j % 2], :, here] = slope.astype(jnp.bfloat16)
            return carry

        lax.fori_loop(0, 4, body, 0)
        if j < 4:
            store(g_slots[j % 2], g_out.at[j]).start()
            store(slope_slots[j % 2], gp_out.at[j]).start()
        tick(9.0 if j < 4 else 2.5)
        if j < 3:
            weight(EXPAND_AT[j + 1], (j + 1) % 2).start()
            weight(SHRINK_AT[j + 1], 2 + (j + 1) % 2).start()

    load(9, cot_ref).wait()

    def third_norm(rows, usable):
        m = acc[rows, :]
        unit, scale = norm_parts(held[rows, :] + m)
        gain = par[15:16, :]
        pool[0, rows, :] = (unit * gain + par[16:17, :]).astype(jnp.bfloat16)
        grad = pool[9, rows, :].astype(jnp.float32) * usable
        inner = grad * gain
        first = jnp.mean(inner, axis=1, keepdims=True)
        second = jnp.mean(inner * unit, axis=1, keepdims=True)
        back = scale * (inner - first - unit * second)
        acc[rows, :] = back
        low = back.astype(jnp.bfloat16)
        pool[1, rows, :] = low
        return usable * m * m, grad * unit, grad, low.astype(jnp.float32)

    m_total, gain_sum, shift_sum, offset_sum = over_rows(4, third_norm)
    square_at(5, m_total)
    small_out[15:16, :] = gain_sum
    small_out[16:17, :] = shift_sum
    small_out[10:11, :] = offset_sum
    last = [
        store(0, y_out),
        store(1, dm_out),
        pltpu.make_async_copy(acc, d_third_out, acc_sem.at[0]),
    ]
    for copy in last:
        copy.start()
    for c in range(GATHERED):
        emit_all(planner.until(c))
    for copy in last + state_stores + [lse_copy, x_store]:
        copy.wait()
    store(7, h2_out).wait()
    store(6, g_out.at[3]).wait()
    store(8, gp_out.at[3]).wait()


def forward(order, lengths, tokens, pieces, states, cotangent, params):
    any_space = pl.BlockSpec(memory_space=pl.ANY)
    vmem = pl.BlockSpec(memory_space=pltpu.VMEM)
    shape = jax.ShapeDtypeStruct
    dma = pltpu.SemaphoreType.DMA
    low = jnp.bfloat16
    wide = jnp.float32
    square = shape((1024, D), low)
    square_wide = shape((1024, D), wide)
    lse = shape((8, 8, 1024), wide)
    short = shape((128, D), low)
    blocks = shape((4, 1024, D), low)
    outs = (
        shape((64, 16, D), low),
        shape((GATHERED, 4, 256, D), low),
        square,
        square,
        square,
        square,
        lse,
        square,
        short,
        short,
        square,
        lse,
        square_wide,
        square_wide,
        square,
        square,
        blocks,
        blocks,
        square,
        square,
        square_wide,
        shape((24, D), wide),
    )
    return pl.pallas_call(
        forward_kernel,
        out_shape=outs,
        in_specs=[SCALARS] * 2 + [any_space] * 4 + [vmem],
        out_specs=(any_space,) * 21 + (vmem,),
        scratch_shapes=[
            pltpu.VMEM((10, 1024, D), low),
            pltpu.VMEM((1024, D), wide),
            pltpu.VMEM((1024, D), wide),
            pltpu.VMEM((128, 1024), wide),
            pltpu.VMEM((8, 8, 1024), wide),
            pltpu.VMEM((3, 128, D), low),
            pltpu.VMEM((64, 16, D), low),
            pltpu.VMEM((32, 16, D), low),
            pltpu.VMEM((32, 16, D), low),
            pltpu.VMEM((64, 16, D), low),
            dma((10,)),
            dma((10,)),
            dma((4,)),
            dma((2,)),
            dma((2, 32)),
            dma((2, 32)),
            dma((2, 32)),
            dma((2, 32)),
        ]
        + gather_sems(GATHERED),
        compiler_params=pltpu.CompilerParams(
            collective_id=3, has_side_effects=True, vmem_limit_bytes=62 * MIB
        ),
    )(order, lengths, tokens.reshape(64, 16, D), pieces, states, cotangent, params)


def add_blocks(target, first, second, planes, rows, step):
    per_plane = rows // step

    def body(i, carry):
        s = i // per_plane
        r = pl.multiple_of((i % per_plane) * step, step)
        target(s, r, first(s, r) + second(s, r))
        return carry

    lax.fori_loop(0, planes * per_plane, body, 0)


POOL = 8
G_SLOTS = 3
R_SLOTS = 4
PLAN = {"core": 3.0, "load": 1.5, "a": 11.5, "b": 6.5, "z": 6.5, "bb": 2.5, "ba": 4.0, "bc": 2.0}


class Planner:
    def __init__(self):
        self.now = 0.0
        self.links = {"core": 0.0, "x": 0.0, "y": 0.0, "z": 0.0, "load": 0.0}
        self.stage = {}
        self.ready = {}

    def link_of(self, c, stage):
        first, second = ("x", "y") if c % 2 == 0 else ("y", "x")
        return {
            0: ("core", "core"),
            1: ("load", "load"),
            2: (first, "a"),
            3: (second, "b"),
            4: ("z", "z"),
            5: (second, "bb"),
            6: (first, "ba"),
            7: ("core", "bc"),
            8: (None, None),
        }[stage]

    def can(self, c):
        stage = self.stage[c]
        if stage > 8:
            return False
        if stage == 1 and c >= R_SLOTS and self.stage[c - R_SLOTS] <= 3:
            return False
        return True

    def emit(self, c):
        stage = self.stage[c]
        link, kind = self.link_of(c, stage)
        self.now = max(self.now, self.ready[c]) + {2: 0.8, 3: 0.5, 4: 0.3, 5: 0.2}.get(stage, 0.1)
        if link is not None:
            begin = max(self.now, self.links[link])
            span = PLAN[kind]
            self.links[link] = begin + span - 1.0
            self.ready[c] = begin + span
        self.stage[c] = stage + 1
        return (stage, c)

    def tick(self, spent):
        self.now += spent
        events = []
        progress = True
        while progress:
            progress = False
            for c in sorted(self.stage):
                if self.can(c) and self.ready[c] <= self.now:
                    events.append(self.emit(c))
                    progress = True
        return events

    def produce(self, c):
        self.stage[c] = 0
        self.ready[c] = self.now
        return [self.emit(c)]

    def until(self, done):
        events = []
        while not done():
            choices = [c for c in sorted(self.stage) if self.can(c)]
            c = min(choices, key=lambda i: (self.ready[i], i))
            events.append(self.emit(c))
        return events

    def free_slot(self, c):
        before = c - G_SLOTS
        if before < 0:
            return []
        return self.until(lambda: self.stage[before] > 2)

    def drain(self, tasks, spent):
        events = []
        waiting = list(tasks)
        while waiting or any(s <= 8 for s in self.stage.values()):
            choices = [c for c in sorted(self.stage) if self.can(c)]
            best = min(choices, key=lambda i: (self.ready[i], i)) if choices else None
            open_tasks = [t for t in waiting if all(self.stage[c] > 8 for c in t[0])]
            if open_tasks and (best is None or self.ready[best] > self.now):
                task = open_tasks[0]
                waiting.remove(task)
                self.now += spent
                events.append(("task", task[1]))
            else:
                events.append(self.emit(best))
        return events


def backward_kernel(
    lengths_ref,
    dm_ref,
    d_third_ref,
    g_ref,
    gp_ref,
    full_ref,
    h2_ref,
    h1_ref,
    x_in_ref,
    e_ref,
    oc_ref,
    o_ref,
    r1_ref,
    r2_ref,
    q_ref,
    k_ref,
    v_ref,
    cq_ref,
    ck_ref,
    cv_ref,
    lse_ref,
    lse_cross_ref,
    gains_ref,
    small_ref,
    rows_ref,
    cols_ref,
    token_grad_ref,
    state_grad_ref,
    out_ref,
    totals_ref,
    rows_out,
    cols_out,
    scale_out,
    half,
    pool,
    acc,
    made,
    summed,
    quarter,
    eighth,
    pieces,
    stream,
    dq_t,
    dk_sum,
    dv_sum,
    lse_held,
    states,
    states_t,
    small,
    small_in,
    small_sum,
    small_z,
    part,
    whole,
    load_sem,
    stream_sem,
    state_sem,
    half_sem,
    scan_sem,
    line_send_sem,
    line_recv_sem,
    send_sem,
    recv_sem,
    z_send_sem,
    z_recv_sem,
    place_sem,
    small_send_sem,
    small_recv_sem,
):
    core, x, y, z, other_core, other_x, other_y, others_z = neighbours()
    kept = pl.multiple_of(core * 128, 128)
    given = pl.multiple_of(128 - core * 128, 128)
    planner = Planner()
    place_of = (12, 8, 13, 9, 14, 10, 15, 11, 7, 4, 5, 6, 3, 0, 1, 2)

    def axes(c):
        if c % 2 == 0:
            return x, y, other_x, other_y
        return y, x, other_y, other_x

    def core_copy(c):
        source = made.at[c % G_SLOTS, :, pl.ds(given, 128), :]
        return remote(source, half.at[c], send_sem.at[0, c], recv_sem.at[0, c], other_core)

    def half_copy(c):
        return pltpu.make_async_copy(
            half.at[c], summed.at[c % R_SLOTS], half_sem.at[c % R_SLOTS]
        )

    def first_copy(c):
        a, b, first, second = axes(c)
        rows = pl.ds(pl.multiple_of(64 - a * 64, 64), 64)
        source = summed.at[c % R_SLOTS, :, rows, :]
        return remote(source, quarter.at[c], send_sem.at[1, c], recv_sem.at[1, c], first)

    def second_copy(c):
        a, b, first, second = axes(c)
        rows = pl.ds(pl.multiple_of(32 - b * 32, 32), 32)
        source = quarter.at[c, :, rows, :]
        return remote(source, eighth.at[c], send_sem.at[2, c], recv_sem.at[2, c], second)

    def z_copy(c, d):
        device = others_z[d]
        return remote(
            eighth.at[c, device[1]],
            pieces.at[c, d],
            z_send_sem.at[c, d],
            z_recv_sem.at[c, d],
            device,
        )

    def own_rows_of(c):
        a, b, first, second = axes(c)
        return pl.ds(pl.multiple_of(core * 128 + a * 64 + b * 32, 32), 32)

    def place_copy(c):
        return pltpu.make_async_copy(
            pieces.at[c, 0], out_ref.at[place_of[c], own_rows_of(c), :], place_sem.at[c]
        )

    def back_second(c):
        device = axes(c)[3]
        target = out_ref.at[place_of[c], own_rows_of(c), :]
        return remote(pieces.at[c, 0], target, send_sem.at[3, c], recv_sem.at[3, c], device)

    def back_first(c):
        a, b, first, second = axes(c)
        block = out_ref.at[place_of[c], pl.ds(pl.multiple_of(core * 128 + a * 64, 64), 64), :]
        return remote(block, block, send_sem.at[4, c], recv_sem.at[4, c], first)

    def back_core(c):
        block = out_ref.at[place_of[c], pl.ds(kept, 128), :]
        return remote(block, block, send_sem.at[5, c], recv_sem.at[5, c], other_core)

    def emit(stage, c):
        a, b, first, second = axes(c)
        slot = c % R_SLOTS
        if stage == 0:
            core_copy(c).start()
        if stage == 1:
            if c >= R_SLOTS:
                first_copy(c - R_SLOTS).wait_send()
            core_copy(c).wait_recv()
            half_copy(c).start()
        if stage == 2:
            half_copy(c).wait()

            def put(s, r, value):
                summed[slot, s, pl.ds(r, 32), :] = value

            add_blocks(
                put,
                lambda s, r: summed[slot, s, pl.ds(r, 32), :],
                lambda s, r: made[c % G_SLOTS, s, pl.ds(pl.multiple_of(kept + r, 32), 32), :],
                4,
                128,
                32,
            )
            first_copy(c).start()
            core_copy(c).wait_send()
        if stage == 3:
            first_copy(c).wait_recv()

            def put(s, r, value):
                quarter[c, s, pl.ds(r, 32), :] = value

            add_blocks(
                put,
                lambda s, r: quarter[c, s, pl.ds(r, 32), :],
                lambda s, r: summed[slot, s, pl.ds(pl.multiple_of(a * 64 + r, 32), 32), :],
                4,
                64,
                32,
            )
            second_copy(c).start()
        if stage == 4:
            second_copy(c).wait_recv()

            def put(s, r, value):
                eighth[c, s, pl.ds(r, 32), :] = value

            add_blocks(
                put,
                lambda s, r: eighth[c, s, pl.ds(r, 32), :],
                lambda s, r: quarter[c, s, pl.ds(pl.multiple_of(b * 32 + r, 32), 32), :],
                4,
                32,
                32,
            )
            for d in range(3):
                z_copy(c, d).start()
        if stage == 5:
            for d in range(3):
                z_copy(c, d).wait_recv()
            total = eighth[c, z].astype(jnp.float32)
            for d in range(3):
                total = total + pieces[c, d].astype(jnp.float32)
            pieces[c, 0] = total.astype(jnp.bfloat16)
            back_second(c).start()
            place_copy(c).start()
        if stage == 6:
            place_copy(c).wait()
            back_second(c).wait_recv()
            back_first(c).start()
        if stage == 7:
            back_first(c).wait_recv()
            back_core(c).start()
        if stage == 8:
            back_core(c).wait()
            back_first(c).wait_send()
            back_second(c).wait_send()
            for d in range(3):
                z_copy(c, d).wait_send()
            second_copy(c).wait_send()
            if c >= CHUNKS - R_SLOTS:
                first_copy(c).wait_send()

    def emit_all(events):
        for stage, c in events:
            emit(stage, c)

    def tick(spent):
        emit_all(planner.tick(spent))

    def produced(c, spent):
        planner.now += spent
        emit_all(planner.produce(c))
        emit_all(planner.tick(0.0))

    def load(slot, source):
        return pltpu.make_async_copy(source, pool.at[slot], load_sem.at[slot])

    def state_load(index, source):
        return pltpu.make_async_copy(source, states.at[index], state_sem.at[index])

    def turn_tile(target, source):
        def turn(n):
            pool[target, pl.ds(n, 256), :] = pool[source, :, pl.ds(n, 256)].T

        return turn

    def transpose_into(target, source):
        turn = turn_tile(target, source)

        def body(i, carry):
            turn(pl.multiple_of(i * 256, 256))
            return carry

        lax.fori_loop(0, 4, body, 0)

    def product_nn(left, right, put, beside=None):
        def body(i, carry):
            n = pl.multiple_of(i * 256, 256)
            if beside is not None:
                beside(n)
            put(n, product(left(), right(n)))
            return carry

        lax.fori_loop(0, 4, body, 0)

    def product_nt(left, right, put, beside=None):
        def body(i, carry):
            n = pl.multiple_of(i * 256, 256)
            if beside is not None:
                beside(n)
            put(
                n,
                lax.dot_general(
                    left(),
                    right(n),
                    (((1,), (1,)), ((), ())),
                    preferred_element_type=jnp.float32,
                ),
            )
            return carry

        lax.fori_loop(0, 4, body, 0)

    def columns_of(slot):
        return lambda n: pool[slot, :, pl.ds(n, 256)]

    def rows_of(slot):
        return lambda n: pool[slot, pl.ds(n, 256), :]

    def weight_grad(slot_in_made, left, right, beside=None):
        def put(n, value):
            low = value.astype(jnp.bfloat16).reshape(4, 256, 256)
            made[slot_in_made, :, :, pl.ds(n, 256)] = low

        product_nn(left, right, put, beside)

    def add_to_acc(n, value):
        acc[:, pl.ds(n, 256)] += value

    def put_in(slot):
        def put(n, value):
            pool[slot, :, pl.ds(n, 256)] = value.astype(jnp.bfloat16)

        return put

    def norm_back(source, gain_row, gain_at, shift_at, offset_at, target):
        tiles = 8
        rows = 1024 // tiles

        def fetch(i):
            place = pl.ds(pl.multiple_of(i * rows, rows), rows)
            return pltpu.make_async_copy(
                source.at[place, :], stream.at[i % 2], stream_sem.at[i % 2]
            )

        fetch(0).start()

        def body(i, carry):
            gain_sum, shift_sum, offset_sum = carry

            @pl.when(i + 1 < tiles)
            def _():
                fetch(i + 1).start()

            fetch(i).wait()
            r = pl.multiple_of(i * rows, rows)
            values = stream[i % 2]
            centred = values - jnp.mean(values, axis=1, keepdims=True)
            spread = jnp.mean(centred * centred, axis=1, keepdims=True)
            scale = lax.rsqrt(spread + NORM_EPS)
            unit = centred * scale
            grad = acc[pl.ds(r, rows), :]
            inner = grad * gains_ref[gain_row : gain_row + 1, :]
            first = jnp.mean(inner, axis=1, keepdims=True)
            second = jnp.mean(inner * unit, axis=1, keepdims=True)
            back = scale * (inner - first - unit * second)
            acc[pl.ds(r, rows), :] = back
            low = back.astype(jnp.bfloat16)
            pool[target, pl.ds(r, rows), :] = low
            return (
                gain_sum + fold(grad * unit),
                shift_sum + fold(grad),
                offset_sum + fold(low.astype(jnp.float32)),
            )

        zero = jnp.zeros((8, D), jnp.float32)
        sums = lax.fori_loop(0, tiles, body, (zero, zero, zero))
        for row, value in zip((gain_at, shift_at, offset_at), sums):
            small[row : row + 1, :] = jnp.sum(value, axis=0, keepdims=True)

    greet([other_core, other_x, other_y] + others_z)
    load(0, dm_ref).start()
    load(6, h2_ref).start()
    load(2, full_ref.at[SHRINK_AT[0]]).start()
    load(3, gp_ref.at[0]).start()
    load(4, g_ref.at[0]).start()
    load(5, full_ref.at[EXPAND_AT[0]]).start()
    acc_load = pltpu.make_async_copy(d_third_ref, acc, place_sem.at[0])
    acc_load.start()
    small[...] = small_ref[...]
    load(6, h2_ref).wait()
    transpose_into(1, 6)
    load(0, dm_ref).wait()
    acc_load.wait()

    planner.now = 4.0
    plan = []
    for j in range(4):
        entry = []
        planner.now += 3.5
        entry.append(planner.tick(0.0) + planner.free_slot(2 * j))
        planner.now += 2.5
        entry.append(planner.produce(2 * j) + planner.tick(0.0) + planner.free_slot(2 * j + 1))
        planner.now += 2.5
        entry.append(planner.produce(2 * j + 1) + planner.tick(0.0))
        entry.append(planner.tick(2.5))
        plan.append(entry)

    def emit_planned(j, place):
        for n in range(4):
            events = plan[n][place]
            if events:

                @pl.when(j == n)
                def _(events=events):
                    emit_all(events)

    def block(j, carry):
        last = j == 3
        load(2, full_ref.at[SHRINK_AT[0]]).wait()
        load(3, gp_ref.at[0]).wait()

        def put_pre(n, value):
            low = (value * pool[3, :, pl.ds(n, 256)].astype(jnp.float32)).astype(jnp.bfloat16)
            pool[7, :, pl.ds(n, 256)] = low
            small[pl.ds(6 + j, 1), pl.ds(n, 256)] = jnp.sum(
                low.astype(jnp.float32), axis=0, keepdims=True
            )

        load(4, g_ref.at[0]).wait()
        product_nt(lambda: pool[0], rows_of(2), put_pre, turn_tile(6, 4))

        @pl.when(jnp.logical_not(last))
        def _():
            load(2, full_ref.at[SHRINK_AT[0] + 2 * (j + 1) - (j + 1) // 3]).start()
            load(3, gp_ref.at[j + 1]).start()

        @pl.when(last)
        def _():
            load(2, full_ref.at[7]).start()
            load(3, cq_ref).start()

        emit_planned(j, 0)

        @pl.when(jnp.logical_not(last))
        def _():
            load(4, g_ref.at[j + 1]).start()

        @pl.when(last)
        def _():
            load(4, oc_ref).start()

        weight_grad((2 * j) % G_SLOTS, lambda: pool[6], columns_of(0))
        emit_planned(j, 1)
        weight_grad((2 * j + 1) % G_SLOTS, lambda: pool[1], columns_of(7))
        emit_planned(j, 2)
        load(5, full_ref.at[EXPAND_AT[0]]).wait()
        product_nt(lambda: pool[7], rows_of(5), add_to_acc)

        @pl.when(jnp.logical_not(last))
        def _():
            load(5, full_ref.at[EXPAND_AT[1] + 2 * j]).start()

        @pl.when(last)
        def _():
            load(5, full_ref.at[4]).start()

        emit_planned(j, 3)
        return carry

    lax.fori_loop(0, 4, block, 0)

    load(7, h1_ref).start()
    state_loads = [state_load(0, ck_ref), state_load(1, cv_ref), state_load(2, e_ref)]
    for copy in state_loads:
        copy.start()
    lse_load = pltpu.make_async_copy(lse_cross_ref, lse_held, state_sem.at[3])
    lse_load.start()
    norm_back(r2_ref, 1, 13, 14, 5, 0)
    tick(4.0)
    load(4, oc_ref).wait()
    load(2, full_ref.at[7]).wait()
    product_nt(lambda: pool[0], rows_of(2), put_in(4), turn_tile(6, 4))
    load(2, full_ref.at[3]).start()
    tick(2.5)
    emit_all(planner.free_slot(8))
    load(7, h1_ref).wait()
    weight_grad(8 % G_SLOTS, lambda: pool[6], columns_of(0), turn_tile(1, 7))
    load(6, o_ref).start()
    load(7, full_ref.at[5]).start()
    produced(8, 2.5)
    load(3, cq_ref).wait()
    for copy in state_loads:
        copy.wait()
    lse_load.wait()

    def attend_loop(causal, step, length, query, key, value, grad, rows, spent, span=(0, 8)):
        ahead = {n: planner.tick(spent) for n in range(*span)}

        def body(i, carry):
            lanes = pl.ds(pl.multiple_of(i * 128, 128), 128)

            def sums(dq, dv):
                small[rows[0] : rows[0] + 1, lanes] = dq
                small[rows[1] : rows[1] + 1, lanes] = dv

            attend_back_pair(
                causal,
                step,
                length,
                query.at[:, lanes],
                key.at[:, lanes],
                value.at[:, lanes],
                grad.at[:, lanes],
                lse_held.at[pl.ds(i, 1)],
                query.at[:, lanes],
                key.at[:, lanes],
                value.at[:, lanes],
                sums,
                dq_t,
                dk_sum,
                dv_sum,
            )
            for n in range(*span):
                if ahead[n]:

                    @pl.when(i == n)
                    def _(events=ahead[n]):
                        emit_all(events)

            return carry

        lax.fori_loop(*span, body, 0)

    attend_loop(
        False,
        512,
        lengths_ref[1],
        pool.at[3],
        states.at[0],
        states.at[1],
        pool.at[4],
        (3, 4),
        2.0,
    )
    lse_load = pltpu.make_async_copy(lse_ref, lse_held, state_sem.at[3])
    lse_load.start()
    emit_all(planner.free_slot(9))
    weight_grad(9 % G_SLOTS, lambda: pool[1], columns_of(3))
    produced(9, 2.5)
    load(5, full_ref.at[4]).wait()
    load(6, o_ref).wait()
    product_nt(lambda: pool[3], rows_of(5), add_to_acc, turn_tile(1, 6))
    load(6, x_in_ref).start()
    load(5, full_ref.at[6]).start()
    load(3, q_ref).start()
    tick(2.5)
    states_t[...] = states[2].T
    for c, index in ((10, 0), (11, 1)):
        emit_all(planner.free_slot(c))
        weight_grad(
            c % G_SLOTS, lambda: states_t[...], lambda n, i=index: states[i, :, pl.ds(n, 256)]
        )
        produced(c, 1.0)
    load(7, full_ref.at[5]).wait()
    load(5, full_ref.at[6]).wait()

    def state_part(n):
        dims = (((1,), (1,)), ((), ()))
        return lax.dot_general(
            states[0], pool[7, pl.ds(n, 256), :], dims, preferred_element_type=jnp.float32
        ) + lax.dot_general(
            states[1], pool[5, pl.ds(n, 256), :], dims, preferred_element_type=jnp.float32
        )

    def put_state(i, carry):
        n = pl.multiple_of(i * 256, 256)
        state_grad_ref[:, pl.ds(n, 256)] = state_part(n).astype(jnp.bfloat16)
        return carry

    lax.fori_loop(0, 4, put_state, 0)
    load(5, k_ref).start()
    load(7, v_ref).start()
    tick(1.0)

    norm_back(r1_ref, 0, 11, 12, 2, 0)
    tick(4.0)
    emit_all(planner.free_slot(12))
    weight_grad(12 % G_SLOTS, lambda: pool[1], columns_of(0))
    produced(12, 2.5)
    load(2, full_ref.at[3]).wait()
    load(6, x_in_ref).wait()
    product_nt(lambda: pool[0], rows_of(2), put_in(4), turn_tile(1, 6))
    load(0, full_ref.at[0]).start()
    load(2, full_ref.at[1]).start()
    load(6, full_ref.at[2]).start()
    tick(2.5)
    load(3, q_ref).wait()
    load(5, k_ref).wait()
    load(7, v_ref).wait()
    lse_load.wait()
    def self_heads(span):
        refs = [pool.at[slot] for slot in (3, 5, 7, 4)]
        attend_loop(True, 256, lengths_ref[0], *refs, (0, 1), 5.0, span)

    def query_key_grad(c, half_of):
        def put(i, carry):
            n = pl.multiple_of((i % 2) * 256 + 512 * half_of, 256)
            value = product(pool[1], pool[3 + 2 * (i // 2), :, pl.ds(n, 256)])
            low = value.astype(jnp.bfloat16).reshape(4, 256, 256)
            made[c % G_SLOTS, :, :, pl.ds(pl.multiple_of(i * 256, 256), 256)] = low
            return carry

        emit_all(planner.free_slot(c))
        lax.fori_loop(0, 4, put, 0)
        produced(c, 2.5)

    self_heads((0, 4))
    query_key_grad(13, 0)
    self_heads((4, 8))

    def small_copy(k):
        source = small if k == 0 else small_sum.at[k - 1]
        device = (other_core, other_x, other_y)[k]
        return remote(source, small_in.at[k], small_send_sem.at[k], small_recv_sem.at[k], device)

    def small_z_copy(d):
        return remote(
            small_sum.at[2],
            small_z.at[z],
            small_send_sem.at[3 + d],
            small_recv_sem.at[3 + d],
            others_z[d],
        )

    def small_step(k):
        small_copy(k).wait()
        before = small[...] if k == 0 else small_sum[k - 1]
        small_sum[k] = before + small_in[k]
        if k < 2:
            small_copy(k + 1).start()
        else:
            small_z[z] = small_sum[2]
            for d in range(3):
                small_z_copy(d).start()

    small_copy(0).start()
    emit_all(planner.free_slot(14))
    weight_grad(14 % G_SLOTS, lambda: pool[1], columns_of(7))
    produced(14, 2.5)
    small_step(0)
    query_key_grad(15, 1)
    small_step(1)
    load(0, full_ref.at[0]).wait()
    product_nt(lambda: pool[3], rows_of(0), add_to_acc)
    tick(2.5)
    small_step(2)
    load(2, full_ref.at[1]).wait()
    product_nt(lambda: pool[5], rows_of(2), add_to_acc)
    tick(2.5)
    for d in range(3):
        small_z_copy(d).wait()
    totals_ref[...] = (small_z[0] + small_z[1]) + (small_z[2] + small_z[3])
    load(6, full_ref.at[2]).wait()

    def put_input(n, value):
        total = acc[:, pl.ds(n, 256)] + value
        pool[4, :, pl.ds(n, 256)] = total.astype(jnp.bfloat16)

    product_nt(lambda: pool[7], rows_of(6), put_input)
    token_copy = pltpu.make_async_copy(pool.at[4], token_grad_ref, load_sem.at[4])
    token_copy.start()
    tick(2.5)

    part[...] = jnp.zeros_like(part)

    def spot(place):
        return (0, 1, 2, 6)[place // 4], (place % 4) * 256

    def scan_load(place):
        slot, row = spot(place)
        return pltpu.make_async_copy(
            out_ref.at[place], pool.at[slot, pl.ds(row, 256), :], scan_sem.at[place]
        )

    scans = {}
    for i in range(2):
        scans[i] = ([(0, 512 * i, 512, i, 0), (2, 512 * i, 512, i, 512)], i, (13, 128 * i))
    for i in range(2, 8):
        scans[i] = ([(1 if i == 2 else i, 0, D, i, 0)], i, (13, 128 * i))
    scans[8] = ([(8 + i, 0, D, 8 + i, 0) for i in range(4)], 8, (14, 0))
    for i in range(4):
        scans[9 + i] = ([(12 + i, 0, D, 12, 0)], 9 + i, (14, 128))

    def scan(name):
        sources, row_lane, (total_row, total_lane) = scans[name]
        width = float(sum(source[2] for source in sources))
        step = 64 if name == 8 else 256

        def body(i, carry):
            cols, weights, total = carry
            r = pl.multiple_of(i * step, step)
            squares = []
            for place, lane, lanes, _, _ in sources:
                slot, row = spot(place)
                tile = pool[slot, pl.ds(row + r, step), lane : lane + lanes]
                squares.append(jnp.square(tile.astype(jnp.float32)))
            row_sum = sum(jnp.sum(square, axis=1, keepdims=True) for square in squares)
            rows = DECAY_RATE * rows_ref[pl.ds(r, step), row_lane : row_lane + 1] + (
                1.0 - DECAY_RATE
            ) * (row_sum / width + FACTOR_EPS)
            rows_out[pl.ds(r, step), row_lane : row_lane + 1] = rows
            inverse = 1.0 / rows
            cols = [c + fold(s) for c, s in zip(cols, squares)]
            weights = [w + fold(s * inverse) for w, s in zip(weights, squares)]
            return cols, weights, total + fold(rows)

        zeros = [jnp.zeros((8, source[2]), jnp.float32) for source in sources]
        cols, weights, total = lax.fori_loop(
            0, 256 // step, body, (zeros, zeros, jnp.zeros((8, 1), jnp.float32))
        )
        for (_, _, lanes, slot, lane), col, weighted in zip(sources, cols, weights):
            here = slice(lane, lane + lanes)
            part[slot : slot + 1, here] += jnp.sum(col, axis=0, keepdims=True)
            part[16 + slot : 17 + slot, here] += jnp.sum(weighted, axis=0, keepdims=True)
        part[total_row : total_row + 1, total_lane : total_lane + 128] += jnp.broadcast_to(
            jnp.sum(total), (1, 128)
        )

    chunk_at = {place: c for c, place in enumerate(place_of)}
    tasks = [
        ([chunk_at[source[0]] for source in scans[name][0]], name)
        for name in (9, 10, 11, 12, 8, 7, 4, 5, 6, 3, 2, 0, 1)
    ]
    loaded = set()
    for c in range(CHUNKS):
        if planner.stage[c] > 8:
            scan_load(place_of[c]).start()
    for first, second in planner.drain(tasks, 1.5):
        if first != "task":
            emit(first, second)
            if first == 8:
                scan_load(place_of[second]).start()
            continue
        for source in scans[second][0]:
            if source[0] not in loaded:
                loaded.add(source[0])
                scan_load(source[0]).wait()
        scan(second)
    total = line_sum(part, whole, line_send_sem, line_recv_sem, z, others_z)
    row_counts = [D] * 12 + [FF]
    means = [total[13:14, 128 * i : 128 * i + 1] / D for i in range(8)]
    means = means + [total[14:15, 0:1] / D] * 4 + [total[14:15, 128:129] / FF]
    cols_new, quotients = [], []
    for slot in range(13):
        new = DECAY_RATE * cols_ref[slot : slot + 1, :] + (1.0 - DECAY_RATE) * (
            total[slot : slot + 1] / row_counts[slot] + FACTOR_EPS
        )
        cols_new.append(new)
        quotients.append(jnp.sum(total[16 + slot : 17 + slot] / new, axis=1, keepdims=True))
        cols_out[slot : slot + 1, :] = new
    expand_quotient = quotients[8] + quotients[9] + quotients[10] + quotients[11]
    for slot in range(13):
        if slot < 8:
            mean_square = means[slot] * quotients[slot] / (D * D)
            rate = STEP_RATE * (OUT_GAIN if slot % 4 == 3 else 1.0)
        else:
            quotient = expand_quotient if slot < 12 else quotients[12]
            mean_square = means[slot] * quotient / (D * FF)
            rate = STEP_RATE
        factor = rate / jnp.maximum(1.0, jnp.sqrt(mean_square) / CLIP_LEVEL)
        scale_out[slot : slot + 1, :] = lax.rsqrt(cols_new[slot] / means[slot]) * factor
    token_copy.wait()


def backward(lengths, held, gains, small, factor_rows, factor_cols):
    any_space = pl.BlockSpec(memory_space=pl.ANY)
    vmem = pl.BlockSpec(memory_space=pltpu.VMEM)
    shape = jax.ShapeDtypeStruct
    dma = pltpu.SemaphoreType.DMA
    low = jnp.bfloat16
    wide = jnp.float32
    rows = small.shape[0]
    return pl.pallas_call(
        backward_kernel,
        out_shape=(
            shape((1024, D), low),
            shape((128, D), low),
            shape((CHUNKS, 256, D), low),
            shape(small.shape, wide),
            shape((256, 128), wide),
            shape((16, D), wide),
            shape((16, D), wide),
            shape((CHUNKS, 4, 128, D), low),
        ),
        in_specs=[SCALARS] + [any_space] * len(held) + [vmem] * 4,
        out_specs=(any_space, vmem, any_space, vmem, vmem, vmem, vmem, any_space),
        scratch_shapes=[
            pltpu.VMEM((POOL, 1024, D), low),
            pltpu.VMEM((1024, D), wide),
            pltpu.VMEM((G_SLOTS, 4, 256, D), low),
            pltpu.VMEM((R_SLOTS, 4, 128, D), low),
            pltpu.VMEM((CHUNKS, 4, 64, D), low),
            pltpu.VMEM((CHUNKS, 4, 32, D), low),
            pltpu.VMEM((CHUNKS, 3, 32, D), low),
            pltpu.VMEM((2, 128, D), wide),
            pltpu.VMEM((128, 1024), wide),
            pltpu.VMEM((2, 1024, 128), wide),
            pltpu.VMEM((2, 1024, 128), wide),
            pltpu.VMEM((8, 8, 1024), wide),
            pltpu.VMEM((3, 128, D), low),
            pltpu.VMEM((D, 128), low),
            pltpu.VMEM((rows, D), wide),
            pltpu.VMEM((3, rows, D), wide),
            pltpu.VMEM((3, rows, D), wide),
            pltpu.VMEM((4, rows, D), wide),
            pltpu.VMEM((32, D), wide),
            pltpu.VMEM((4, 32, D), wide),
            dma((POOL,)),
            dma((2,)),
            dma((4,)),
            dma((R_SLOTS,)),
            dma((CHUNKS,)),
            dma((3,)),
            dma((3,)),
            dma((6, CHUNKS)),
            dma((6, CHUNKS)),
            dma((CHUNKS, 3)),
            dma((CHUNKS, 3)),
            dma((CHUNKS,)),
            dma((6,)),
            dma((6,)),
        ],
        compiler_params=pltpu.CompilerParams(
            collective_id=0, has_side_effects=True, vmem_limit_bytes=62 * MIB
        ),
    )(lengths, *held, gains, small, factor_rows, factor_cols)[0:7]


def line_sum(part, whole, send_sem, recv_sem, z, others_z):
    copies = [
        remote(part, whole.at[z], send_sem.at[d], recv_sem.at[d], others_z[d]) for d in range(3)
    ]
    for copy in copies:
        copy.start()
    whole[z] = part[...]
    for copy in copies:
        copy.wait()
    return (whole[0] + whole[1]) + (whole[2] + whole[3])


def update_attention_kernel(
    grad_ref, weight_ref, rows_ref, scale_ref, grad_out, new_out, copy_out, grads, change
):
    block = grad_ref.shape[1]
    for i in range(8):
        rows = lax.rsqrt(rows_ref[:, i : i + 1])
        every = pl.ds(i, block, stride=8)
        for lane in range(8):
            columns = slice(lane * 128, lane * 128 + 128)
            if i < 2:
                start = 512 * i + 128 * (lane % 4)
                grad = grad_ref[2 * (lane // 4), :, start : start + 128]
            else:
                grad = grad_ref[1 if i == 2 else i, :, columns]
            grad = grad.astype(jnp.float32)
            grads[lane, every, :] = grad
            change[lane, every, :] = grad * rows * scale_ref[i : i + 1, columns]
    for lane in range(8):
        columns = slice(lane * 128, lane * 128 + 128)
        grad_out[:, columns] = grads[lane]
        new = weight_ref[:, columns] - change[lane]
        new_out[:, columns] = new
        copy_out[:, columns] = new.astype(jnp.bfloat16)


def update_attention(grads, weights, rows, scale):
    block = 32
    wide = pl.BlockSpec((block * 8, D), lambda i: (i, 0))
    shape = jax.ShapeDtypeStruct
    new = pl.pallas_call(
        update_attention_kernel,
        grid=(256 // block,),
        out_shape=(
            shape((2048, D), jnp.float32),
            shape((2048, D), jnp.float32),
            shape((2048, D), jnp.bfloat16),
        ),
        in_specs=[
            pl.BlockSpec((8, block, D), lambda i: (0, i, 0)),
            wide,
            pl.BlockSpec((block, 128), lambda i: (i, 0)),
            pl.BlockSpec((16, D), lambda i: (0, 0)),
        ],
        out_specs=(wide,) * 3,
        scratch_shapes=[pltpu.VMEM((8, block * 8, 128), jnp.float32)] * 2,
        compiler_params=pltpu.CompilerParams(vmem_limit_bytes=62 * MIB),
    )(grads, weights.reshape(2048, D), rows, scale)
    return [t.reshape(256, 8, D) for t in new]


def update_kernel(
    first, slots, grad_ref, weight_ref, rows_ref, scale_ref, grad_out, new_out, copy_out
):
    spans = 4 if slots == 4 else 1
    wide = D // spans
    for i in range(slots):
        grads = grad_ref[i].astype(jnp.float32)
        changes = grads * (lax.rsqrt(rows_ref[...]) * scale_ref[first + i : first + i + 1, :])
        for s in range(spans):
            start = s * D + i * wide
            columns = slice(start, start + wide)
            part = slice(s * wide, s * wide + wide)
            grad_out[:, columns] = grads[:, part]
            new = weight_ref[:, columns] - changes[:, part]
            new_out[:, columns] = new
            copy_out[:, columns] = new.astype(jnp.bfloat16)


def update_plain(grads, weights, rows, scale, first, slots, grad_map):
    count, width = weights.shape
    block = 128 // slots
    wide = pl.BlockSpec((block, width), lambda i: (i, 0))
    shape = jax.ShapeDtypeStruct
    return pl.pallas_call(
        lambda *refs: update_kernel(first, slots, *refs),
        grid=(count // block,),
        out_shape=(
            shape(weights.shape, jnp.float32),
            shape(weights.shape, jnp.float32),
            shape(weights.shape, jnp.bfloat16),
        ),
        in_specs=[
            pl.BlockSpec((slots, block, D), grad_map),
            wide,
            pl.BlockSpec((block, 1), lambda i: (i, 0)),
            pl.BlockSpec((16, D), lambda i: (0, 0)),
        ],
        out_specs=(wide,) * 3,
        compiler_params=pltpu.CompilerParams(vmem_limit_bytes=62 * MIB),
    )(grads, weights, rows, scale)


def update_direct(grads, rows, scale, attention_weights, expand_weight, shrink_weight):
    shr_rows = rows[:, 9:13].T.reshape(-1, 1)
    attention = update_attention(grads, attention_weights, rows, scale)
    expand = update_plain(grads, expand_weight, rows[:, 8:9], scale, 8, 4, lambda i: (2, i, 0))
    shrink = update_plain(
        grads, shrink_weight, shr_rows, scale, 12, 1, lambda i: (12 + i // 2, i % 2, 0)
    )
    return attention, expand, shrink, (rows[:, 0:8].T, rows[:, 8], shr_rows[:, 0])


def as_rows(vector):
    rows = -(-vector.shape[0] // 1024) * 8
    return jnp.pad(vector, (0, rows * 128 - vector.shape[0])).reshape(rows, 128)


def masked_scores(query_part, key_heads, first_row, valid_count, causal):
    scores = jnp.einsum("qhd,khd->hqk", query_part, key_heads, preferred_element_type=jnp.float32)
    key_places = jnp.arange(key_heads.shape[0], dtype=jnp.int32)[None, :]
    usable = key_places < valid_count
    if causal:
        query_places = first_row + jnp.arange(query_part.shape[0], dtype=jnp.int32)[:, None]
        usable = usable & (key_places <= query_places)
    return jnp.where(usable[None], scores, MASKED)


def attend_forward(queries, key_heads, values, valid_count, causal):
    query_rows = queries.shape[0]
    step_rows = min(512, query_rows)
    outputs, stored = ([], [])
    for b in range(query_rows // step_rows):
        first_row = b * step_rows
        key_end = first_row + step_rows if causal else key_heads.shape[0]
        scores = masked_scores(
            queries[first_row : first_row + step_rows],
            key_heads[:key_end],
            first_row,
            valid_count,
            causal,
        )
        row_max = jnp.max(scores, axis=-1, keepdims=True)
        raised = jnp.exp(scores - row_max)
        totals = jnp.sum(raised, axis=-1, keepdims=True)
        probs_low = (raised / totals).astype(jnp.bfloat16)
        outputs.append(
            jnp.einsum(
                "hqk,khd->qhd", probs_low, values[:key_end], preferred_element_type=jnp.float32
            )
        )
        stored.append(row_max + jnp.log(totals))
    return (jnp.concatenate(outputs, axis=0), stored)


def attend_backward(queries, key_heads, values, grad_out, stored, valid_count, causal):
    query_rows = queries.shape[0]
    key_rows = key_heads.shape[0]
    step_rows = min(512, query_rows)
    grad_queries = []
    grad_keys = jnp.zeros(key_heads.shape, jnp.float32)
    grad_values = jnp.zeros(values.shape, jnp.float32)
    for b in range(query_rows // step_rows):
        first_row = b * step_rows
        key_end = first_row + step_rows if causal else key_rows
        query_part = queries[first_row : first_row + step_rows]
        grad_part = grad_out[first_row : first_row + step_rows]
        scores = masked_scores(query_part, key_heads[:key_end], first_row, valid_count, causal)
        probs = jnp.exp(scores - stored[b])
        probs_low = probs.astype(jnp.bfloat16)
        grad_probs = jnp.einsum(
            "qhd,khd->hqk", grad_part, values[:key_end], preferred_element_type=jnp.float32
        )
        value_part = jnp.einsum(
            "hqk,qhd->khd", probs_low, grad_part, preferred_element_type=jnp.float32
        )
        grad_scores = probs * (grad_probs - jnp.sum(probs * grad_probs, axis=-1, keepdims=True))
        scores_low = grad_scores.astype(jnp.bfloat16)
        grad_queries.append(
            jnp.einsum(
                "hqk,khd->qhd", scores_low, key_heads[:key_end], preferred_element_type=jnp.float32
            )
        )
        key_part = jnp.einsum(
            "hqk,qhd->khd", scores_low, query_part, preferred_element_type=jnp.float32
        )
        padding = ((0, key_rows - key_end), (0, 0), (0, 0))
        grad_keys = grad_keys + jnp.pad(key_part, padding)
        grad_values = grad_values + jnp.pad(value_part, padding)
    return (jnp.concatenate(grad_queries, axis=0), grad_keys, grad_values)


def gather_rows(piece):
    return lax.all_gather(piece, ("shard", "rep"), axis=0, tiled=True)


def own_piece(block, replicas):
    rows = block.shape[0] // replicas
    return lax.dynamic_slice_in_dim(block, lax.axis_index("rep") * rows, rows, axis=0)


def scatter_rows(grad):
    piece = lax.psum_scatter(
        grad.astype(jnp.bfloat16), ("shard", "rep"), scatter_dimension=0, tiled=True
    )
    return lax.all_gather(piece, "rep", axis=0, tiled=True)


def local_factors(grad, rows):
    square = grad * grad
    rows_new = DECAY_RATE * rows + (1.0 - DECAY_RATE) * jnp.mean(square + FACTOR_EPS, axis=-1)
    col_part = jnp.sum(square + FACTOR_EPS, axis=0)
    weighted = jnp.sum(square / rows_new[..., None], axis=0)
    return rows_new, col_part, weighted, jnp.sum(rows_new, axis=0)


def finish_factors(grad, weight, rows_new, cols, col_sum, weighted, row_total, row_count, rate):
    cols_new = DECAY_RATE * cols + (1.0 - DECAY_RATE) * col_sum / row_count
    mean_rows = row_total / row_count
    mean_square = mean_rows * jnp.sum(weighted / cols_new, axis=-1) / (row_count * cols.shape[-1])
    factor = rate / jnp.maximum(1.0, jnp.sqrt(mean_square) / CLIP_LEVEL)
    scaled = lax.rsqrt(cols_new / mean_rows[..., None]) * factor[..., None]
    fresh = weight - grad * (lax.rsqrt(rows_new)[..., None] * scaled[None])
    return fresh, cols_new


def plain_device(
    tokens,
    encoder,
    cotangent,
    lengths,
    encoder_lengths,
    dealt_order,
    attention_weights,
    expand_weight,
    shrink_weight,
    small_params,
    attention_rows,
    attention_cols,
    expand_rows,
    expand_cols,
    shrink_rows,
    shrink_cols,
    small_moment,
):
    devices = lax.axis_size(("rep", "shard"))
    replicas = lax.axis_size("rep")
    shards = lax.axis_size("shard")
    slot_tokens = tokens.shape[0]
    slot_states = encoder.shape[0]
    position = lax.axis_index(("rep", "shard"))
    inverse = (
        jnp.zeros((devices,), jnp.int32).at[dealt_order].set(jnp.arange(devices, dtype=jnp.int32))
    )
    qkv_piece = own_piece(attention_weights[:, 0:3, :].reshape(-1, 3 * D), replicas)
    rest_piece = own_piece(attention_weights[:, 3:8, :].reshape(-1, 5 * D), replicas)
    qkv_full = gather_rows(qkv_piece.astype(jnp.bfloat16))
    rest_full = gather_rows(rest_piece.astype(jnp.bfloat16))
    expand_full = gather_rows(own_piece(expand_weight, replicas).astype(jnp.bfloat16))
    shrink_full = gather_rows(own_piece(shrink_weight, replicas).astype(jnp.bfloat16))
    spread = lax.all_to_all(
        tokens.reshape(devices, slot_tokens // devices, D),
        ("rep", "shard"),
        split_axis=0,
        concat_axis=0,
        tiled=True,
    )
    picked = jnp.take(spread, inverse, axis=0)
    tokens = lax.all_to_all(
        picked, ("rep", "shard"), split_axis=0, concat_axis=0, tiled=True
    ).reshape(slot_tokens, D)
    states = encoder
    incoming = cotangent
    valid_tokens = lengths[position]
    valid_states = encoder_lengths[position]
    matrices = [qkv_full[:, i * D : (i + 1) * D] for i in range(3)] + [
        rest_full[:, i * D : (i + 1) * D] for i in range(5)
    ]
    parts = unpack(small_params)
    token_heads = (slot_tokens, HEADS, HEAD_DIM)
    state_heads = (slot_states, HEADS, HEAD_DIM)
    q_self = ((forward_product(tokens, matrices[0]) + parts[0]) * 0.125).astype(
        jnp.bfloat16
    )
    k_self = forward_product(tokens, matrices[1]).astype(jnp.bfloat16)
    v_self = (forward_product(tokens, matrices[2]) + parts[1]).astype(jnp.bfloat16)
    o_self, lse_self = attend_forward(
        q_self.reshape(token_heads),
        k_self.reshape(token_heads),
        v_self.reshape(token_heads),
        valid_tokens,
        True,
    )
    o_self_low = o_self.reshape(slot_tokens, D).astype(jnp.bfloat16)
    branch_a = forward_product(o_self_low, matrices[3]) + parts[2]
    tokens_wide = tokens.astype(jnp.float32)
    hidden_one, norm_one_back = jax.vjp(layer_norm, tokens_wide + branch_a, parts[8], parts[9])
    hidden_one_low = hidden_one.astype(jnp.bfloat16)
    q_cross = (
        (forward_product(hidden_one_low, matrices[4]) + parts[3]) * 0.125
    ).astype(jnp.bfloat16)
    k_cross = forward_product(states, matrices[5]).astype(jnp.bfloat16)
    v_cross = (forward_product(states, matrices[6]) + parts[4]).astype(jnp.bfloat16)
    o_cross, lse_cross = attend_forward(
        q_cross.reshape(token_heads),
        k_cross.reshape(state_heads),
        v_cross.reshape(state_heads),
        valid_states,
        False,
    )
    o_cross_low = o_cross.reshape(slot_tokens, D).astype(jnp.bfloat16)
    branch_c = forward_product(o_cross_low, matrices[7]) + parts[5]
    hidden_two, norm_two_back = jax.vjp(layer_norm, hidden_one + branch_c, parts[10], parts[11])
    hidden_two_low = hidden_two.astype(jnp.bfloat16)
    pre_act = forward_product(hidden_two_low, expand_full) + parts[6]
    activated, gelu_back = jax.vjp(gelu_exact, pre_act)
    activated_low = activated.astype(jnp.bfloat16)
    branch_m = forward_product(activated_low, shrink_full) + parts[7]
    result, norm_three_back = jax.vjp(layer_norm, hidden_two + branch_m, parts[12], parts[13])
    usable_rows = (jnp.arange(slot_tokens, dtype=jnp.int32) < valid_tokens).astype(jnp.float32)[
        :, None
    ]
    squares = jnp.stack(
        [
            jnp.sum(usable_rows * t * t)
            for t in (tokens_wide, branch_a, hidden_one, branch_c, hidden_two, branch_m)
        ]
    )
    d_third, d_gain_three, d_shift_three = norm_three_back(
        incoming.astype(jnp.float32) * usable_rows
    )
    d_mlp = d_third.astype(jnp.bfloat16)
    grad_shrink = weight_product(activated_low, d_mlp)
    grad_shrink_offset = row_sum(d_mlp)
    d_activated = input_product(d_mlp, shrink_full)
    d_pre = gelu_back(d_activated)[0].astype(jnp.bfloat16)
    grad_expand = weight_product(hidden_two_low, d_pre)
    grad_expand_offset = row_sum(d_pre)
    d_hidden_two = d_third + input_product(d_pre, expand_full)
    d_second, d_gain_two, d_shift_two = norm_two_back(d_hidden_two)
    d_branch_c = d_second.astype(jnp.bfloat16)
    grad_cross_out = weight_product(o_cross_low, d_branch_c)
    grad_cross_out_offset = row_sum(d_branch_c)
    d_o_cross = input_product(d_branch_c, matrices[7]).astype(jnp.bfloat16)
    grad_cq, grad_ck, grad_cv = attend_backward(
        q_cross.reshape(token_heads),
        k_cross.reshape(state_heads),
        v_cross.reshape(state_heads),
        d_o_cross.reshape(token_heads),
        lse_cross,
        valid_states,
        False,
    )
    dq_cross = (grad_cq.reshape(slot_tokens, D) * 0.125).astype(jnp.bfloat16)
    dk_cross = grad_ck.reshape(slot_states, D).astype(jnp.bfloat16)
    dv_cross = grad_cv.reshape(slot_states, D).astype(jnp.bfloat16)
    grad_cross_query = weight_product(hidden_one_low, dq_cross)
    grad_cross_key = weight_product(states, dk_cross)
    grad_cross_value = weight_product(states, dv_cross)
    state_grad = input_product(dk_cross, matrices[5]) + input_product(
        dv_cross, matrices[6]
    )
    d_hidden_one = d_second + input_product(dq_cross, matrices[4])
    d_first, d_gain_one, d_shift_one = norm_one_back(d_hidden_one)
    d_branch_a = d_first.astype(jnp.bfloat16)
    grad_self_out = weight_product(o_self_low, d_branch_a)
    grad_self_out_offset = row_sum(d_branch_a)
    d_o_self = input_product(d_branch_a, matrices[3]).astype(jnp.bfloat16)
    grad_sq, grad_sk, grad_sv = attend_backward(
        q_self.reshape(token_heads),
        k_self.reshape(token_heads),
        v_self.reshape(token_heads),
        d_o_self.reshape(token_heads),
        lse_self,
        valid_tokens,
        True,
    )
    dq_self = (grad_sq.reshape(slot_tokens, D) * 0.125).astype(jnp.bfloat16)
    dk_self = grad_sk.reshape(slot_tokens, D).astype(jnp.bfloat16)
    dv_self = grad_sv.reshape(slot_tokens, D).astype(jnp.bfloat16)
    grad_self_query = weight_product(tokens, dq_self)
    grad_self_key = weight_product(tokens, dk_self)
    grad_self_value = weight_product(tokens, dv_self)
    token_grad = (
        d_first
        + input_product(dq_self, matrices[0])
        + input_product(dk_self, matrices[1])
        + input_product(dv_self, matrices[2])
    )
    small_partial = jnp.concatenate(
        [
            row_sum(dq_self),
            row_sum(dv_self),
            grad_self_out_offset,
            row_sum(dq_cross),
            row_sum(dv_cross),
            grad_cross_out_offset,
            grad_expand_offset,
            grad_shrink_offset,
            d_gain_one,
            d_shift_one,
            d_gain_two,
            d_shift_two,
            d_gain_three,
            d_shift_three,
        ]
    )
    totals = lax.psum(jnp.concatenate([small_partial, squares]), ("rep", "shard"))
    g_shrink = scatter_rows(grad_shrink)
    g_expand = scatter_rows(grad_expand)
    g_rest = scatter_rows(
        jnp.concatenate(
            [grad_self_out, grad_cross_query, grad_cross_key, grad_cross_value, grad_cross_out],
            axis=1,
        )
    )
    g_qkv = scatter_rows(
        jnp.concatenate([grad_self_query, grad_self_key, grad_self_value], axis=1)
    )
    g_attention = (
        jnp.concatenate([g_qkv, g_rest], axis=1).reshape(-1, 8, D).astype(jnp.float32)
    )
    g_expand = g_expand.astype(jnp.float32)
    g_shrink = g_shrink.astype(jnp.float32)
    attention_rows_new, *attention_parts = local_factors(g_attention, attention_rows.T)
    expand_rows_new, *expand_parts = local_factors(g_expand, expand_rows)
    shrink_rows_new, *shrink_parts = local_factors(g_shrink, shrink_rows)
    flat = attention_parts + expand_parts + shrink_parts
    summed = lax.psum(jnp.concatenate([t.reshape(-1) for t in flat]), "shard")
    sums = []
    offset = 0
    for t in flat:
        sums.append(summed[offset : offset + t.size].reshape(t.shape))
        offset = offset + t.size
    attention_rates = STEP_RATE * jnp.where(jnp.arange(8) % 4 == 3, OUT_GAIN, 1.0).astype(
        jnp.float32
    )
    attention_new, attention_cols_new = finish_factors(
        g_attention,
        attention_weights,
        attention_rows_new,
        attention_cols,
        *sums[0:3],
        D,
        attention_rates,
    )
    expand_new, expand_cols_new = finish_factors(
        g_expand, expand_weight, expand_rows_new, expand_cols, *sums[3:6], D, STEP_RATE
    )
    shrink_new, shrink_cols_new = finish_factors(
        g_shrink, shrink_weight, shrink_rows_new, shrink_cols, *sums[6:9], FF, STEP_RATE
    )
    small_grad = totals[: small_params.shape[0]]
    small_moment_new = DECAY_RATE * small_moment + (1.0 - DECAY_RATE) * (
        small_grad * small_grad + FACTOR_EPS
    )
    small_update = small_grad * lax.rsqrt(small_moment_new)
    small_scale = jnp.sqrt(jnp.mean(small_update * small_update))
    small_new = small_params - SMALL_RATE * small_update / jnp.maximum(
        1.0, small_scale / CLIP_LEVEL
    )
    norm_stats = jnp.sqrt(
        totals[small_params.shape[0] :] / (jnp.sum(lengths).astype(jnp.float32) * D)
    )
    return (
        result.astype(jnp.bfloat16),
        token_grad.astype(jnp.bfloat16),
        state_grad.astype(jnp.bfloat16),
        g_attention,
        g_expand,
        g_shrink,
        small_grad,
        attention_new,
        expand_new,
        shrink_new,
        small_new,
        attention_new.astype(jnp.bfloat16),
        expand_new.astype(jnp.bfloat16),
        shrink_new.astype(jnp.bfloat16),
        attention_rows_new.T,
        attention_cols_new,
        expand_rows_new,
        expand_cols_new,
        shrink_rows_new,
        shrink_cols_new,
        small_moment_new,
        norm_stats,
    )


def direct_device(
    tokens,
    encoder,
    cotangent,
    lengths,
    encoder_lengths,
    dealt_order,
    attention_weights,
    expand_weight,
    shrink_weight,
    small_params,
    attention_rows,
    attention_cols,
    expand_rows,
    expand_cols,
    shrink_rows,
    shrink_cols,
    small_moment,
):
    position = lax.axis_index(("rep", "shard"))
    inverse = jnp.zeros((32,), jnp.int32).at[dealt_order].set(jnp.arange(32, dtype=jnp.int32))
    valid = jnp.stack([lengths[position], encoder_lengths[position]])
    parts = unpack(small_params)
    blank = jnp.zeros((D,), jnp.float32)
    params = jnp.concatenate(
        [
            small_params[0 : 6 * D].reshape(6, D),
            hidden_blocks(parts[6]),
            small_params[6 * D + FF :].reshape(7, D),
            jnp.zeros((7, D), jnp.float32),
        ]
    )
    gains = jnp.stack([parts[8], parts[10]] + [blank] * 6)
    pieces = weight_pieces(attention_weights, expand_weight, shrink_weight, neighbours())
    (
        tokens,
        full,
        q_self,
        k_self,
        v_self,
        o_self,
        lse_self,
        q_cross,
        k_cross,
        v_cross,
        o_cross,
        lse_cross,
        summed_one,
        summed_two,
        hidden_one,
        hidden_two,
        activated,
        slope,
        output,
        d_mlp,
        d_third,
        small_first,
    ) = forward(inverse, valid, tokens, pieces, encoder, cotangent, params)
    factor_rows = jnp.concatenate(
        [attention_rows, expand_rows.reshape(1, 256), shrink_rows.reshape(4, 256)]
    )
    factor_rows = jnp.pad(factor_rows.T, ((0, 0), (0, 115)))
    factor_cols = jnp.concatenate(
        [attention_cols, hidden_blocks(expand_cols), shrink_cols.reshape(1, D), jnp.ones((3, D))]
    )
    token_grad, state_grad, reduced, totals, factor_rows, factor_cols, scale = backward(
        valid,
        (
            d_mlp,
            d_third,
            activated,
            slope,
            full.reshape(GATHERED, 1024, D),
            hidden_two,
            hidden_one,
            tokens.reshape(1024, D),
            encoder,
            o_cross,
            o_self,
            summed_one,
            summed_two,
            q_self,
            k_self,
            v_self,
            q_cross,
            k_cross,
            v_cross,
            lse_self,
            lse_cross,
        ),
        gains,
        small_first,
        factor_rows,
        factor_cols,
    )
    attention, expand, shrink, rows_new = update_direct(
        reduced, factor_rows, scale, attention_weights, expand_weight, shrink_weight
    )
    cols_new = (factor_cols[0:8], hidden_flat(factor_cols[8:12]), factor_cols[12])
    small_grad = jnp.concatenate(
        [totals[0:6].reshape(-1), hidden_flat(totals[6:10]), totals[10:17].reshape(-1)]
    )
    small_moment_new = DECAY_RATE * small_moment + (1.0 - DECAY_RATE) * (
        small_grad * small_grad + FACTOR_EPS
    )
    small_update = small_grad * lax.rsqrt(small_moment_new)
    small_scale = jnp.sqrt(jnp.mean(small_update * small_update))
    small_new = small_params - SMALL_RATE * small_update / jnp.maximum(
        1.0, small_scale / CLIP_LEVEL
    )
    norm_stats = jnp.sqrt(totals[17, 0:6] / (jnp.sum(lengths).astype(jnp.float32) * D))
    return (
        output,
        token_grad,
        state_grad,
        attention[0],
        expand[0],
        shrink[0],
        small_grad,
        attention[1],
        expand[1],
        shrink[1],
        small_new,
        attention[2],
        expand[2],
        shrink[2],
        rows_new[0],
        cols_new[0],
        rows_new[1],
        cols_new[1],
        rows_new[2],
        cols_new[2],
        small_moment_new,
        norm_stats,
    )


def on_device(*args):
    if lax.axis_size("rep") == 8 and lax.axis_size("shard") == 4:
        return direct_device(*args)
    return plain_device(*args)


def solution(mesh):
    in_specs = (
        P(("rep", "shard"), None),
        P(("rep", "shard"), None),
        P(("rep", "shard"), None),
        P(),
        P(),
        P(),
        P("shard", None, None),
        P("shard", None),
        P("shard", None),
        P(),
        P(None, "shard"),
        P(),
        P("shard"),
        P(),
        P("shard"),
        P(),
        P(),
    )
    out_specs = (
        P(("rep", "shard"), None),
        P(("rep", "shard"), None),
        P(("rep", "shard"), None),
        P("shard", None, None),
        P("shard", None),
        P("shard", None),
        P(),
        P("shard", None, None),
        P("shard", None),
        P("shard", None),
        P(),
        P("shard", None, None),
        P("shard", None),
        P("shard", None),
        P(None, "shard"),
        P(),
        P("shard"),
        P(),
        P("shard"),
        P(),
        P(),
        P(),
    )
    return jax.shard_map(
        on_device, mesh=mesh, in_specs=in_specs, out_specs=out_specs, check_vma=False
    )
```

```python
import math

import jax
import jax.numpy as jnp
from jax import lax
from jax.experimental import pallas as pl
from jax.experimental.pallas import tpu as pltpu
from jax.sharding import PartitionSpec as P

D = 1024
HEADS = 16
HEAD_DIM = 64
FF = 4096


DECAY_RATE = 0.5
CLIP_LEVEL = 0.25
STEP_RATE = 0.1
SMALL_RATE = 0.4
OUT_GAIN = 8.0
NORM_EPS = 1e-05
FACTOR_EPS = 1e-30
MASKED = -1e30
MESH = pl.DeviceIdType.MESH
CHUNKS = 16
GATHERED = 16
EXPAND_AT = (8, 9, 11, 13)
SHRINK_AT = (10, 12, 14, 15)
EARLY = 2
MIB = 1 << 20


def layer_norm(r, norm_gain, norm_shift):
    centred = r - jnp.mean(r, axis=-1, keepdims=True)
    spread = jnp.mean(centred * centred, axis=-1, keepdims=True)
    return centred * lax.rsqrt(spread + NORM_EPS) * norm_gain + norm_shift


def gelu_exact(values):
    return jax.nn.gelu(values, approximate=False)


def unpack(small):
    extents = [D] * 6 + [FF] + [D] * 7
    pieces = []
    offset = 0
    for extent in extents:
        pieces.append(small[offset : offset + extent])
        offset = offset + extent
    return pieces


def forward_product(source, matrix):
    return jnp.dot(source, matrix, preferred_element_type=jnp.float32)


def input_product(grad_low, matrix):
    return jnp.einsum("to,io->ti", grad_low, matrix, preferred_element_type=jnp.float32)


def weight_product(source, grad_low):
    return jnp.einsum("ti,to->io", source, grad_low, preferred_element_type=jnp.float32)


def row_sum(grad_low):
    return jnp.sum(grad_low.astype(jnp.float32), axis=0)


def transposed(block):
    return block.astype(jnp.float32).T.astype(jnp.bfloat16)


def half_lanes(shape, dim):
    return lax.broadcasted_iota(jnp.int32, shape, dim)


def masked_keys(keys, length, head):
    place = half_lanes(keys.shape, 0)
    lane = half_lanes(keys.shape, 1)
    blocked = jnp.where((lane == 64 - 64 * head) & (place >= length), MASKED, 0.0)
    own = (lane >= 64 * head) & (lane < 64 * head + 64)
    return jnp.where(own, keys.astype(jnp.float32), blocked).astype(jnp.bfloat16)


def own_head(rows_t, head, fill):
    place = half_lanes(rows_t.shape, 0)
    own = (place >= 64 * head) & (place < 64 * head + 64)
    other = jnp.where(place == 64 - 64 * head, fill, 0.0)
    return jnp.where(own, rows_t.astype(jnp.float32), other).astype(jnp.bfloat16)


def product(first, second):
    return jnp.dot(first, second, preferred_element_type=jnp.float32)


def causal_mask(scores, step):
    kept = scores.shape[0] - step
    last = scores[kept:]
    allowed = half_lanes(last.shape, 0) <= half_lanes(last.shape, 1)
    last = jnp.where(allowed, last, MASKED)
    return last if kept == 0 else jnp.concatenate([scores[:kept], last], axis=0)


def attend_pair(
    causal, step, length, q_ref, k_ref, v_ref, o_ref, lse_ref, o_t, first_row=0
):
    count = q_ref.shape[0]
    q_t = transposed(q_ref[...])
    v_t = transposed(v_ref[...])
    keys = [masked_keys(k_ref[...], length, head) for head in range(2)]
    queries = [own_head(q_t, head, 1.0) for head in range(2)]
    units = [(head, start) for start in range(0, count, step) for head in range(2)]

    def scores_of(head, start):
        end = first_row + start + step if causal else k_ref.shape[0]
        return product(keys[head][:end], queries[head][:, start : start + step])

    ahead = scores_of(*units[0])
    for index, (head, start) in enumerate(units):
        scores = ahead
        if index + 1 < len(units):
            ahead = scores_of(*units[index + 1])
        rows = slice(64 * head, 64 * head + 64)
        columns = slice(start, start + step)
        if causal:
            scores = causal_mask(scores, step)
        top = jnp.max(scores, axis=0, keepdims=True)
        raised = jnp.exp(scores - top)
        total = jnp.sum(raised, axis=0, keepdims=True)
        probs = (raised * (1.0 / total)).astype(jnp.bfloat16)
        o_t[rows, columns] = product(v_t[rows, : scores.shape[0]], probs)
        place = slice(first_row + start, first_row + start + step)
        lse_ref[0, head : head + 1, place] = top + jnp.log(total)
    o_ref[...] = o_t[:, :count].T.astype(jnp.bfloat16)


def attend_back_pair(
    causal,
    step,
    length,
    q_ref,
    k_ref,
    v_ref,
    do_ref,
    lse_ref,
    dq_ref,
    dk_ref,
    dv_ref,
    put_sums,
    dq_t,
    dk_sum,
    dv_sum,
):
    key_rows = k_ref.shape[0]
    q_t = transposed(q_ref[...])
    k_t = transposed(k_ref[...])
    do_t = transposed(do_ref[...])
    values = v_ref[...]
    keys = [masked_keys(k_ref[...], length, head) for head in range(2)]
    queries = [own_head(q_t, head, 1.0) for head in range(2)]
    grads = [own_head(do_t, head, 0.0) for head in range(2)]
    count = q_ref.shape[0] // step
    units = [(head, b) for b in reversed(range(count)) for head in range(2)]

    def products_of(head, b):
        columns = slice(b * step, b * step + step)
        end = b * step + step if causal else key_rows
        scores = product(keys[head][:end], queries[head][:, columns])
        return scores, product(values[:end], grads[head][:, columns])

    ahead = products_of(*units[0])
    for index, (head, b) in enumerate(units):
        scores, d_probs = ahead
        if index + 1 < len(units):
            ahead = products_of(*units[index + 1])
        rows = slice(64 * head, 64 * head + 64)
        columns = slice(b * step, b * step + step)
        end = scores.shape[0]
        if causal:
            scores = causal_mask(scores, step)
        probs = jnp.exp(scores - lse_ref[0, head : head + 1, columns])
        weighted = probs * d_probs
        delta = jnp.sum(weighted, axis=0, keepdims=True)
        d_scores = (weighted - probs * delta).astype(jnp.bfloat16)
        dv = product(probs.astype(jnp.bfloat16), do_ref[columns, :])
        dk = product(d_scores, q_ref[columns, :])
        if b == count - 1:
            dv_sum[head, :end] = dv
            dk_sum[head, :end] = dk
        else:
            dv_sum[head, :end] += dv
            dk_sum[head, :end] += dk
        dq_t[rows, columns] = product(k_t[rows, :end], d_scores)
    first = half_lanes((key_rows, 128), 1) < 64
    dk_ref[...] = jnp.where(first, dk_sum[0, :key_rows], dk_sum[1, :key_rows]).astype(jnp.bfloat16)
    dv = jnp.where(first, dv_sum[0, :key_rows], dv_sum[1, :key_rows]).astype(jnp.bfloat16)
    dv_ref[...] = dv
    dq = (dq_t[...] * 0.125).T.astype(jnp.bfloat16)
    dq_ref[...] = dq
    put_sums(
        jnp.sum(dq.astype(jnp.float32), axis=0, keepdims=True),
        jnp.sum(dv.astype(jnp.float32), axis=0, keepdims=True),
    )


SCALARS = pl.BlockSpec(memory_space=pltpu.SMEM)


def neighbours():
    rep = lax.axis_index("rep")
    z = lax.axis_index("shard")
    core = rep % 2
    x = (rep // 2) % 2
    y = rep // 4
    other_core = (rep + 1 - 2 * core, z)
    other_x = (rep + 2 - 4 * x, z)
    other_y = (rep + 4 - 8 * y, z)
    others_z = [(rep, (z + d) % 4) for d in (1, 2, 3)]
    return core, x, y, z, other_core, other_x, other_y, others_z


def greet(devices):
    barrier = pltpu.get_barrier_semaphore()
    for device in devices:
        pl.semaphore_signal(barrier, inc=1, device_id=device, device_id_type=MESH)
    pl.semaphore_wait(barrier, len(devices))


def remote(src, dst, send, recv, device):
    return pltpu.make_async_remote_copy(
        src_ref=src, dst_ref=dst, send_sem=send, recv_sem=recv, device_id=device, device_id_type=MESH
    )


def gather_copies(refs, c, parity, places):
    piece, full, place_sem, z_send, z_recv, send, recv = refs
    core, x, y, z, other_core, other_x, other_y, others_z = places
    a = x + parity * (y - x)
    b = y + parity * (x - y)
    first = (other_x[0] + parity * (other_y[0] - other_x[0]), z)
    second = (other_y[0] + parity * (other_x[0] - other_y[0]), z)
    own = pl.ds(pl.multiple_of(core * 128 + a * 64 + b * 32, 32), 32)
    steps = (
        (own, second),
        (pl.ds(pl.multiple_of(core * 128 + a * 64, 64), 64), first),
        (pl.ds(pl.multiple_of(core * 128, 128), 128), other_core),
    )

    def local():
        return pltpu.make_async_copy(piece.at[c], full.at[c, z, own, :], place_sem.at[c])

    def line(d):
        return remote(
            piece.at[c], full.at[c, z, own, :], z_send.at[c, d], z_recv.at[c, d], others_z[d]
        )

    def pair(k):
        block = full.at[c, :, steps[k][0], :]
        return remote(block, block, send.at[k, c], recv.at[k, c], steps[k][1])

    return local, line, pair


def gather_stage(k, refs, c, parity, places):
    local, line, pair = gather_copies(refs, c, parity, places)
    if k == 0:
        local().start()
        for d in range(3):
            line(d).start()
    if k == 1:
        local().wait()
        for d in range(3):
            line(d).wait_recv()
        pair(0).start()
    if k == 2 or k == 3:
        pair(k - 2).wait_recv()
        pair(k - 1).start()
    if k == 4:
        pair(2).wait()
        pair(1).wait_send()
        pair(0).wait_send()
        for d in range(3):
            line(d).wait_send()


def gather_sems(count):
    dma = pltpu.SemaphoreType.DMA
    return [dma((count,)), dma((count, 3)), dma((count, 3)), dma((3, count)), dma((3, count))]


def hidden_blocks(values):
    split = values.reshape(values.shape[:-1] + (4, 4, 256))
    split = jnp.swapaxes(split, -3, -2)
    return split.reshape(values.shape[:-1] + (4, 1024))


def hidden_flat(blocks):
    split = blocks.reshape(blocks.shape[:-2] + (4, 4, 256))
    split = jnp.swapaxes(split, -3, -2)
    return split.reshape(blocks.shape[:-2] + (FF,))


def fold(tile):
    return jnp.sum(tile.reshape(-1, 8, tile.shape[-1]), axis=0)


GATHER_PLAN = (("z", 6.5), ("second", 6.5), ("first", 11.5), ("core", 3.0), (None, 0.0))


class GatherPlanner:
    def __init__(self, count):
        self.now = 0.0
        self.links = {"core": 0.0, "x": 0.0, "y": 0.0, "z": 0.0}
        self.stage = {c: 0 for c in range(count)}
        self.ready = {c: 0.0 for c in range(count)}
        self.opened = count

    def can(self, c):
        if self.stage[c] == 0 and c >= 3 and self.stage[c - 3] < 2:
            return False
        return self.stage[c] < 5

    def spend(self, now, **busy):
        self.now = max(self.now, now)
        for link, span in busy.items():
            self.links[link] = max(self.links[link], self.now) + span

    def emit(self, c):
        stage = self.stage[c]
        link, span = GATHER_PLAN[stage]
        first, second = ("x", "y") if c % 2 == 0 else ("y", "x")
        link = {"first": first, "second": second}.get(link, link)
        self.now = max(self.now, self.ready[c]) + 0.1
        if link is not None:
            begin = max(self.now, self.links[link])
            self.links[link] = begin + span - 1.0
            self.ready[c] = begin + span
        self.stage[c] = stage + 1
        return (stage, c)

    def tick(self, spent):
        self.now += spent
        events = []
        progress = True
        while progress:
            progress = False
            for c in range(self.opened):
                if self.can(c) and self.ready[c] <= self.now:
                    events.append(self.emit(c))
                    progress = True
        return events

    def until(self, c):
        events = []
        while self.stage[c] < 5:
            choices = [i for i in range(self.opened) if self.can(i)]
            best = min(choices, key=lambda i: (self.ready[i], i))
            events.append(self.emit(best))
        return events


def gelu_parts(u):
    share = 0.5 + 0.5 * lax.erf(u * math.sqrt(0.5))
    bell = jnp.exp(-0.5 * u * u) * (1.0 / math.sqrt(2.0 * math.pi))
    return u * share, share + u * bell


def norm_parts(values):
    centred = values - jnp.mean(values, axis=1, keepdims=True)
    spread = jnp.mean(centred * centred, axis=1, keepdims=True)
    scale = lax.rsqrt(spread + NORM_EPS)
    return centred * scale, scale


def forward_kernel(
    order_ref,
    lengths_ref,
    state_lengths_ref,
    tokens_ref,
    att_ref,
    exp_ref,
    shr_ref,
    e_ref,
    cot_ref,
    par,
    x_out,
    full_ref,
    q_out,
    k_out,
    v_out,
    o_out,
    lse_out,
    cq_out,
    ck_out,
    cv_out,
    oc_out,
    lse_cross_out,
    r1_out,
    r2_out,
    h1_out,
    h2_out,
    g_out,
    gp_out,
    y_out,
    dm_out,
    d_third_out,
    small_out,
    pool,
    acc,
    held,
    o_t,
    lse_held,
    states,
    x_held,
    spread,
    picked,
    piece_ref,
    att_in,
    exp_in,
    shr_in,
    prepare_sem,
    load_sem,
    store_sem,
    state_sem,
    acc_sem,
    spread_send,
    spread_recv,
    back_send,
    back_recv,
    *gather_sem,
):
    places = neighbours()
    refs = (piece_ref, full_ref) + gather_sem
    planner = GatherPlanner(GATHERED)
    me = lax.axis_index("rep") * 4 + places[3]
    length = lengths_ref[me]

    core, x, y = places[0:3]

    def own_row(parity):
        a = x + parity * (y - x)
        b = y + parity * (x - y)
        return core * 128 + a * 64 + b * 32

    prepare = []
    for p in range(2):
        for lane in range(8):
            rows = pl.ds(pl.multiple_of(own_row(p) * 8, 256), 256)
            prepare.append((att_ref.at[rows, pl.ds(lane * 128, 128)], att_in.at[p, lane]))
        rows = pl.ds(pl.multiple_of(own_row(p), 32), 32)
        prepare.append((exp_ref.at[rows, :], exp_in.at[p]))
    for j in range(4):
        rows = pl.ds(pl.multiple_of(j * 256 + own_row(SHRINK_AT[j] % 2), 32), 32)
        prepare.append((shr_ref.at[rows, :], shr_in.at[j]))
    prepare = [
        pltpu.make_async_copy(source, target, prepare_sem.at[i])
        for i, (source, target) in enumerate(prepare)
    ]

    def make_pieces():
        for copy in prepare:
            copy.wait()
        for c in range(8):
            for lane in range(8):
                tile = att_in[c % 2, lane, pl.ds(c, 32, stride=8), :]
                piece_ref[c, :, lane * 128 : lane * 128 + 128] = tile.astype(jnp.bfloat16)
        for j in range(4):
            c = EXPAND_AT[j]
            for s in range(4):
                start = s * 1024 + j * 256
                tile = exp_in[c % 2, :, start : start + 256]
                piece_ref[c, :, s * 256 : s * 256 + 256] = tile.astype(jnp.bfloat16)
            piece_ref[SHRINK_AT[j]] = shr_in[j].astype(jnp.bfloat16)

    def device(offset):
        j = lax.rem(me + offset, 32)
        return j, (j // 4, j % 4)

    def spread_copy(offset):
        j, target = device(offset)
        return remote(
            tokens_ref.at[j],
            spread.at[me],
            spread_send.at[offset],
            spread_recv.at[offset],
            target,
        )

    def back_copy(offset):
        return remote(
            picked.at[offset],
            x_held.at[me],
            back_send.at[offset],
            back_recv.at[offset],
            device(offset)[1],
        )

    def own_spread():
        return pltpu.make_async_copy(tokens_ref.at[me], spread.at[me], spread_recv.at[0])

    def own_back():
        return pltpu.make_async_copy(picked.at[0], x_held.at[me], back_recv.at[0])

    def each_other(act):
        def body(offset, carry):
            act(offset)
            return carry

        lax.fori_loop(1, 32, body, 0)

    def turn_back():
        own_spread().wait()
        each_other(lambda offset: spread_copy(offset).wait())
        picked[0] = spread[order_ref[me]]
        own_back().start()

        def pick(offset):
            picked[offset] = spread[order_ref[device(offset)[0]]]
            back_copy(offset).start()

        each_other(pick)

    def emit_all(events):
        for stage, c in events:
            gather_stage(stage, refs, c, c % 2, places)

    def tick(spent):
        emit_all(planner.tick(spent))

    def load(slot, source):
        return pltpu.make_async_copy(source, pool.at[slot], load_sem.at[slot])

    def store(slot, target):
        return pltpu.make_async_copy(pool.at[slot], target, store_sem.at[slot])

    def product_into(left, right, put):
        def body(i, carry):
            n = pl.multiple_of(i * 256, 256)
            put(n, product(left(), pool[right, :, pl.ds(n, 256)]))
            return carry

        lax.fori_loop(0, 4, body, 0)

    def row(index, n):
        return par[index : index + 1, pl.ds(n, 256)]

    def put_low(slot, offset=None, scale=None):
        def put(n, value):
            if offset is not None:
                value = value + row(offset, n)
            if scale is not None:
                value = value * scale
            pool[slot, :, pl.ds(n, 256)] = value.astype(jnp.bfloat16)

        return put

    def put_acc(offset):
        def put(n, value):
            acc[:, pl.ds(n, 256)] = value + row(offset, n)

        return put

    def load_weight(c, slot):
        target = pool.at[slot].reshape(4, 256, D)
        return pltpu.make_async_copy(full_ref.at[c], target, load_sem.at[slot])

    def weight(c, slot):
        emit_all(planner.until(c))
        return load_weight(c, slot)

    def attend_loop(causal, step, valid, query, key, value, out, spent, rows, key_rows):
        ahead = [planner.tick(spent) for _ in range(8)]
        first_row, count = rows

        def body(i, carry):
            lanes = pl.ds(pl.multiple_of(i * 128, 128), 128)
            attend_pair(
                causal,
                step,
                valid,
                query.at[pl.ds(first_row, count), lanes],
                key.at[pl.ds(0, key_rows), lanes],
                value.at[pl.ds(0, key_rows), lanes],
                out.at[pl.ds(first_row, count), lanes],
                lse_held.at[pl.ds(i, 1)],
                o_t,
                first_row,
            )
            for n in range(8):
                if ahead[n]:

                    @pl.when(i == n)
                    def _(events=ahead[n]):
                        emit_all(events)

            return carry

        lax.fori_loop(0, 8, body, 0)

    TILE = 128

    def over_rows(sums, body):
        zero = jnp.zeros((8, D), jnp.float32)

        def step(i, carry):
            r = pl.multiple_of(i * TILE, TILE)
            place = half_lanes((TILE, 1), 0) + r
            usable = (place < length).astype(jnp.float32)
            terms = body(pl.ds(r, TILE), usable)
            return tuple(c + fold(t) for c, t in zip(carry, terms))

        totals = lax.fori_loop(0, D // TILE, step, (zero,) * sums)
        return [jnp.sum(t, axis=0, keepdims=True) for t in totals]

    lane = half_lanes((1, D), 1)

    def square_at(index, total):
        small_out[17:18, :] += jnp.where(lane == index, jnp.sum(total), 0.0)

    for copy in prepare:
        copy.start()
    barrier = pltpu.get_barrier_semaphore()

    def greet_one(offset):
        pl.semaphore_signal(barrier, inc=1, device_id=device(offset)[1], device_id_type=MESH)

    each_other(greet_one)
    pl.semaphore_wait(barrier, 31)
    own_spread().start()
    each_other(lambda offset: spread_copy(offset).start())
    make_pieces()
    planner.opened = 3 + EARLY
    tick(0.5)
    planner.spend(3.0, z=42.0, x=21.0, y=21.0)
    late = 5.5 * EARLY
    e_load = pltpu.make_async_copy(e_ref, states.at[2], state_sem.at[2])
    e_load.start()
    load(9, cot_ref).start()
    small_out[...] = jnp.zeros_like(small_out)
    for _ in range(4):
        tick(12.0 + 0.25 * late)
    turn_back()
    planner.spend(58.0 + late, z=42.0, x=21.0, y=21.0)
    for _ in range(3):
        tick(10.0)
    for i in range(3):
        weight(i, 1 + i).start()
    planner.opened = GATHERED
    tick(4.0)
    own_back().wait()
    each_other(lambda offset: back_copy(offset).wait())
    planner.spend(115.0 + late)
    x_store = pltpu.make_async_copy(x_held, x_out, acc_sem.at[1])
    x_store.start()

    for i, (slot, offset, scale) in enumerate(((4, 0, 0.125), (5, None, None), (6, 1, None))):
        load_weight(i, 1 + i).wait()
        product_into(lambda: x_held[...].reshape(1024, D), 1 + i, put_low(slot, offset, scale))
        store(slot, (q_out, k_out, v_out)[i]).start()
        tick(2.5)
    refs_held = [pool.at[slot] for slot in (4, 5, 6, 7)]
    attend_loop(True, 256, length, *refs_held, 4.5, (0, 1024), 1024)
    store(7, o_out).start()
    lse_copy = pltpu.make_async_copy(lse_held, lse_out, state_sem.at[3])
    lse_copy.start()
    w_copy = weight(3, 1)
    w_copy.start()
    w_copy.wait()
    product_into(lambda: pool[7], 1, put_acc(2))
    tick(2.5)
    store(4, q_out).wait()

    def first_norm(rows, usable):
        held_rows = pl.ds(pl.multiple_of(rows.start // 32, TILE // 32), TILE // 32)
        x = x_held[held_rows].reshape(TILE, D).astype(jnp.float32)
        a = acc[rows, :]
        total = x + a
        acc[rows, :] = total
        h = norm_parts(total)[0] * par[11:12, :] + par[12:13, :]
        held[rows, :] = h
        pool[4, rows, :] = h.astype(jnp.bfloat16)
        return usable * x * x, usable * a * a, usable * h * h

    for index, total in enumerate(over_rows(3, first_norm)):
        square_at(index, total)
    store(4, h1_out).start()
    r1_copy = pltpu.make_async_copy(acc, r1_out, acc_sem.at[0])
    r1_copy.start()
    tick(4.0)

    for c, slot in ((4, 2), (5, 3), (6, 1)):
        weight(c, slot).start()
    store(5, k_out).wait()
    load_weight(4, 2).wait()
    product_into(lambda: pool[4], 2, put_low(5, 3, 0.125))
    store(5, cq_out).start()
    w_copy = weight(7, 2)
    w_copy.start()
    tick(2.5)
    e_load.wait()
    load_weight(5, 3).wait()
    load_weight(6, 1).wait()

    def put_keys(n, value):
        states[0, :, pl.ds(n, 256)] = value.astype(jnp.bfloat16)

    def put_values(n, value):
        states[1, :, pl.ds(n, 256)] = (value + row(4, n)).astype(jnp.bfloat16)

    product_into(lambda: states[2], 3, put_keys)
    product_into(lambda: states[2], 1, put_values)
    state_stores = [
        pltpu.make_async_copy(states.at[0], ck_out, state_sem.at[0]),
        pltpu.make_async_copy(states.at[1], cv_out, state_sem.at[1]),
    ]
    for copy in state_stores:
        copy.start()
    tick(1.0)
    store(6, v_out).wait()
    lse_copy.wait()
    attend_loop(
        False,
        512,
        state_lengths_ref[me],
        pool.at[5],
        states.at[0],
        states.at[1],
        pool.at[6],
        1.6,
        (0, 1024),
        128,
    )
    store(6, oc_out).start()
    lse_copy = pltpu.make_async_copy(lse_held, lse_cross_out, state_sem.at[3])
    lse_copy.start()
    w_copy.wait()
    r1_copy.wait()
    product_into(lambda: pool[6], 2, put_acc(5))
    tick(2.5)
    weight(EXPAND_AT[0], 0).start()
    weight(SHRINK_AT[0], 2).start()
    store(7, o_out).wait()

    def second_norm(rows, usable):
        c = acc[rows, :]
        total = held[rows, :] + c
        acc[rows, :] = total
        h = norm_parts(total)[0] * par[13:14, :] + par[14:15, :]
        held[rows, :] = h
        pool[7, rows, :] = h.astype(jnp.bfloat16)
        return usable * c * c, usable * h * h

    for index, total in enumerate(over_rows(2, second_norm)):
        square_at(3 + index, total)
    store(7, h2_out).start()
    r2_copy = pltpu.make_async_copy(acc, r2_out, acc_sem.at[0])
    r2_copy.start()
    tick(4.0)

    store(4, h1_out).wait()
    store(5, cq_out).wait()
    g_slots, slope_slots = (4, 6), (5, 8)
    r2_copy.wait()
    store(6, oc_out).wait()
    for j in range(5):
        if j > 1:
            store(g_slots[j % 2], g_out.at[j - 2]).wait()
            store(slope_slots[j % 2], gp_out.at[j - 2]).wait()
        if j < 4:
            load_weight(EXPAND_AT[j], j % 2).wait()
        if j > 0:
            load_weight(SHRINK_AT[j - 1], 2 + (j - 1) % 2).wait()

        def body(i, carry, j=j):
            n = pl.multiple_of(i * 256, 256)
            here = pl.ds(n, 256)
            if j < 4:
                offset = par[pl.ds(6 + i, 1), j * 256 : j * 256 + 256]
                u = product(pool[7], pool[j % 2, :, here]) + offset
            if j > 0:
                more = product(pool[g_slots[(j - 1) % 2]], pool[2 + (j - 1) % 2, :, here])
                if j == 1:
                    acc[:, here] = more + row(10, n)
                else:
                    acc[:, here] += more
            if j < 4:
                g, slope = gelu_parts(u)
                pool[g_slots[j % 2], :, here] = g.astype(jnp.bfloat16)
                pool[slope_slots[j % 2], :, here] = slope.astype(jnp.bfloat16)
            return carry

        lax.fori_loop(0, 4, body, 0)
        if j < 4:
            store(g_slots[j % 2], g_out.at[j]).start()
            store(slope_slots[j % 2], gp_out.at[j]).start()
        tick(9.0 if j < 4 else 2.5)
        if j < 3:
            weight(EXPAND_AT[j + 1], (j + 1) % 2).start()
            weight(SHRINK_AT[j + 1], 2 + (j + 1) % 2).start()

    load(9, cot_ref).wait()

    def third_norm(rows, usable):
        m = acc[rows, :]
        unit, scale = norm_parts(held[rows, :] + m)
        gain = par[15:16, :]
        pool[0, rows, :] = (unit * gain + par[16:17, :]).astype(jnp.bfloat16)
        grad = pool[9, rows, :].astype(jnp.float32) * usable
        inner = grad * gain
        first = jnp.mean(inner, axis=1, keepdims=True)
        second = jnp.mean(inner * unit, axis=1, keepdims=True)
        back = scale * (inner - first - unit * second)
        acc[rows, :] = back
        low = back.astype(jnp.bfloat16)
        pool[1, rows, :] = low
        return usable * m * m, grad * unit, grad, low.astype(jnp.float32)

    m_total, gain_sum, shift_sum, offset_sum = over_rows(4, third_norm)
    square_at(5, m_total)
    small_out[15:16, :] = gain_sum
    small_out[16:17, :] = shift_sum
    small_out[10:11, :] = offset_sum
    last = [
        store(0, y_out),
        store(1, dm_out),
        pltpu.make_async_copy(acc, d_third_out, acc_sem.at[0]),
    ]
    for copy in last:
        copy.start()
    for c in range(GATHERED):
        emit_all(planner.until(c))
    for copy in last + state_stores + [lse_copy, x_store]:
        copy.wait()
    store(7, h2_out).wait()
    store(6, g_out.at[3]).wait()
    store(8, gp_out.at[3]).wait()


def forward(scalars, tokens, weights, states, cotangent, params):
    any_space = pl.BlockSpec(memory_space=pl.ANY)
    vmem = pl.BlockSpec(memory_space=pltpu.VMEM)
    shape = jax.ShapeDtypeStruct
    dma = pltpu.SemaphoreType.DMA
    low = jnp.bfloat16
    wide = jnp.float32
    square = shape((1024, D), low)
    square_wide = shape((1024, D), wide)
    lse = shape((8, 8, 1024), wide)
    short = shape((128, D), low)
    blocks = shape((4, 1024, D), low)
    outs = (
        shape((32, 32, D), low),
        shape((GATHERED, 4, 256, D), low),
        square,
        square,
        square,
        square,
        lse,
        square,
        short,
        short,
        square,
        lse,
        square_wide,
        square_wide,
        square,
        square,
        blocks,
        blocks,
        square,
        square,
        square_wide,
        shape((24, D), wide),
    )
    return pl.pallas_call(
        forward_kernel,
        out_shape=outs,
        in_specs=[SCALARS] * 3 + [any_space] * 6 + [vmem],
        out_specs=(any_space,) * 21 + (vmem,),
        scratch_shapes=[
            pltpu.VMEM((10, 1024, D), low),
            pltpu.VMEM((1024, D), wide),
            pltpu.VMEM((1024, D), wide),
            pltpu.VMEM((128, 1024), wide),
            pltpu.VMEM((8, 8, 1024), wide),
            pltpu.VMEM((3, 128, D), low),
            pltpu.VMEM((32, 32, D), low),
            pltpu.VMEM((32, 32, D), low),
            pltpu.VMEM((32, 32, D), low),
            pltpu.VMEM((GATHERED, 32, D), low),
            pltpu.VMEM((2, 8, 256, 128), wide),
            pltpu.VMEM((2, 32, FF), wide),
            pltpu.VMEM((4, 32, D), wide),
            dma((22,)),
            dma((10,)),
            dma((10,)),
            dma((4,)),
            dma((2,)),
            dma((32,)),
            dma((32,)),
            dma((32,)),
            dma((32,)),
        ]
        + gather_sems(GATHERED),
        compiler_params=pltpu.CompilerParams(
            collective_id=3, has_side_effects=True, vmem_limit_bytes=62 * MIB
        ),
    )(*scalars, tokens.reshape(32, 32, D), *weights, states, cotangent, params)


def add_blocks(target, first, second, planes, rows, step):
    per_plane = rows // step

    def body(i, carry):
        s = i // per_plane
        r = pl.multiple_of((i % per_plane) * step, step)
        target(s, r, first(s, r) + second(s, r))
        return carry

    lax.fori_loop(0, planes * per_plane, body, 0)


POOL = 8
G_SLOTS = 3
R_SLOTS = 4
PLAN = {"core": 3.0, "load": 1.5, "a": 11.5, "b": 6.5, "z": 6.5, "bb": 2.5, "ba": 4.0, "bc": 2.0}


class Planner:
    def __init__(self):
        self.now = 0.0
        self.links = {"core": 0.0, "x": 0.0, "y": 0.0, "z": 0.0, "load": 0.0}
        self.stage = {}
        self.ready = {}

    def link_of(self, c, stage):
        first, second = ("x", "y") if c % 2 == 0 else ("y", "x")
        return {
            0: ("core", "core"),
            1: ("load", "load"),
            2: (first, "a"),
            3: (second, "b"),
            4: ("z", "z"),
            5: (second, "bb"),
            6: (first, "ba"),
            7: ("core", "bc"),
            8: (None, None),
        }[stage]

    def can(self, c):
        stage = self.stage[c]
        if stage > 8:
            return False
        if stage == 1 and c >= R_SLOTS and self.stage[c - R_SLOTS] <= 3:
            return False
        return True

    def emit(self, c):
        stage = self.stage[c]
        link, kind = self.link_of(c, stage)
        self.now = max(self.now, self.ready[c]) + {2: 0.8, 3: 0.5, 4: 0.3, 5: 0.2}.get(stage, 0.1)
        if link is not None:
            begin = max(self.now, self.links[link])
            span = PLAN[kind]
            self.links[link] = begin + span - 1.0
            self.ready[c] = begin + span
        self.stage[c] = stage + 1
        return (stage, c)

    def tick(self, spent):
        self.now += spent
        events = []
        progress = True
        while progress:
            progress = False
            for c in sorted(self.stage):
                if self.can(c) and self.ready[c] <= self.now:
                    events.append(self.emit(c))
                    progress = True
        return events

    def produce(self, c):
        self.stage[c] = 0
        self.ready[c] = self.now
        return [self.emit(c)]

    def until(self, done):
        events = []
        while not done():
            choices = [c for c in sorted(self.stage) if self.can(c)]
            c = min(choices, key=lambda i: (self.ready[i], i))
            events.append(self.emit(c))
        return events

    def free_slot(self, c):
        before = c - G_SLOTS
        if before < 0:
            return []
        return self.until(lambda: self.stage[before] > 2)

    def drain(self, tasks, spent):
        events = []
        waiting = list(tasks)
        while waiting or any(s <= 8 for s in self.stage.values()):
            choices = [c for c in sorted(self.stage) if self.can(c)]
            best = min(choices, key=lambda i: (self.ready[i], i)) if choices else None
            open_tasks = [t for t in waiting if all(self.stage[c] > 8 for c in t[0])]
            if open_tasks and (best is None or self.ready[best] > self.now):
                task = open_tasks[0]
                waiting.remove(task)
                self.now += spent
                events.append(("task", task[1]))
            else:
                events.append(self.emit(best))
        return events


def backward_kernel(
    lengths_ref,
    state_lengths_ref,
    dm_ref,
    d_third_ref,
    g_ref,
    gp_ref,
    full_ref,
    h2_ref,
    h1_ref,
    x_in_ref,
    e_ref,
    oc_ref,
    o_ref,
    r1_ref,
    r2_ref,
    q_ref,
    k_ref,
    v_ref,
    cq_ref,
    ck_ref,
    cv_ref,
    lse_ref,
    lse_cross_ref,
    gains_ref,
    small_ref,
    rows_ref,
    cols_ref,
    token_grad_ref,
    state_grad_ref,
    out_ref,
    totals_ref,
    rows_out,
    cols_out,
    scale_out,
    half,
    pool,
    acc,
    made,
    summed,
    quarter,
    eighth,
    pieces,
    stream,
    dq_t,
    dk_sum,
    dv_sum,
    lse_held,
    states,
    states_t,
    small,
    small_in,
    small_sum,
    small_z,
    part,
    whole,
    load_sem,
    stream_sem,
    state_sem,
    half_sem,
    scan_sem,
    line_send_sem,
    line_recv_sem,
    send_sem,
    recv_sem,
    z_send_sem,
    z_recv_sem,
    place_sem,
    small_send_sem,
    small_recv_sem,
):
    core, x, y, z, other_core, other_x, other_y, others_z = neighbours()
    me = lax.axis_index("rep") * 4 + z
    kept = pl.multiple_of(core * 128, 128)
    given = pl.multiple_of(128 - core * 128, 128)
    planner = Planner()
    place_of = (12, 8, 13, 9, 14, 10, 15, 11, 7, 4, 5, 6, 3, 0, 1, 2)

    def axes(c):
        if c % 2 == 0:
            return x, y, other_x, other_y
        return y, x, other_y, other_x

    def core_copy(c):
        source = made.at[c % G_SLOTS, :, pl.ds(given, 128), :]
        return remote(source, half.at[c], send_sem.at[0, c], recv_sem.at[0, c], other_core)

    def half_copy(c):
        return pltpu.make_async_copy(
            half.at[c], summed.at[c % R_SLOTS], half_sem.at[c % R_SLOTS]
        )

    def first_copy(c):
        a, b, first, second = axes(c)
        rows = pl.ds(pl.multiple_of(64 - a * 64, 64), 64)
        source = summed.at[c % R_SLOTS, :, rows, :]
        return remote(source, quarter.at[c], send_sem.at[1, c], recv_sem.at[1, c], first)

    def second_copy(c):
        a, b, first, second = axes(c)
        rows = pl.ds(pl.multiple_of(32 - b * 32, 32), 32)
        source = quarter.at[c, :, rows, :]
        return remote(source, eighth.at[c], send_sem.at[2, c], recv_sem.at[2, c], second)

    def z_copy(c, d):
        device = others_z[d]
        return remote(
            eighth.at[c, device[1]],
            pieces.at[c, d],
            z_send_sem.at[c, d],
            z_recv_sem.at[c, d],
            device,
        )

    def own_rows_of(c):
        a, b, first, second = axes(c)
        return pl.ds(pl.multiple_of(core * 128 + a * 64 + b * 32, 32), 32)

    def place_copy(c):
        return pltpu.make_async_copy(
            pieces.at[c, 0], out_ref.at[place_of[c], own_rows_of(c), :], place_sem.at[c]
        )

    def back_second(c):
        device = axes(c)[3]
        target = out_ref.at[place_of[c], own_rows_of(c), :]
        return remote(pieces.at[c, 0], target, send_sem.at[3, c], recv_sem.at[3, c], device)

    def back_first(c):
        a, b, first, second = axes(c)
        block = out_ref.at[place_of[c], pl.ds(pl.multiple_of(core * 128 + a * 64, 64), 64), :]
        return remote(block, block, send_sem.at[4, c], recv_sem.at[4, c], first)

    def back_core(c):
        block = out_ref.at[place_of[c], pl.ds(kept, 128), :]
        return remote(block, block, send_sem.at[5, c], recv_sem.at[5, c], other_core)

    def emit(stage, c):
        a, b, first, second = axes(c)
        slot = c % R_SLOTS
        if stage == 0:
            core_copy(c).start()
        if stage == 1:
            if c >= R_SLOTS:
                first_copy(c - R_SLOTS).wait_send()
            core_copy(c).wait_recv()
            half_copy(c).start()
        if stage == 2:
            half_copy(c).wait()

            def put(s, r, value):
                summed[slot, s, pl.ds(r, 32), :] = value

            add_blocks(
                put,
                lambda s, r: summed[slot, s, pl.ds(r, 32), :],
                lambda s, r: made[c % G_SLOTS, s, pl.ds(pl.multiple_of(kept + r, 32), 32), :],
                4,
                128,
                32,
            )
            first_copy(c).start()
            core_copy(c).wait_send()
        if stage == 3:
            first_copy(c).wait_recv()

            def put(s, r, value):
                quarter[c, s, pl.ds(r, 32), :] = value

            add_blocks(
                put,
                lambda s, r: quarter[c, s, pl.ds(r, 32), :],
                lambda s, r: summed[slot, s, pl.ds(pl.multiple_of(a * 64 + r, 32), 32), :],
                4,
                64,
                32,
            )
            second_copy(c).start()
        if stage == 4:
            second_copy(c).wait_recv()

            def put(s, r, value):
                eighth[c, s, pl.ds(r, 32), :] = value

            add_blocks(
                put,
                lambda s, r: eighth[c, s, pl.ds(r, 32), :],
                lambda s, r: quarter[c, s, pl.ds(pl.multiple_of(b * 32 + r, 32), 32), :],
                4,
                32,
                32,
            )
            for d in range(3):
                z_copy(c, d).start()
        if stage == 5:
            for d in range(3):
                z_copy(c, d).wait_recv()
            total = eighth[c, z].astype(jnp.float32)
            for d in range(3):
                total = total + pieces[c, d].astype(jnp.float32)
            pieces[c, 0] = total.astype(jnp.bfloat16)
            back_second(c).start()
            place_copy(c).start()
        if stage == 6:
            place_copy(c).wait()
            back_second(c).wait_recv()
            back_first(c).start()
        if stage == 7:
            back_first(c).wait_recv()
            back_core(c).start()
        if stage == 8:
            back_core(c).wait()
            back_first(c).wait_send()
            back_second(c).wait_send()
            for d in range(3):
                z_copy(c, d).wait_send()
            second_copy(c).wait_send()
            if c >= CHUNKS - R_SLOTS:
                first_copy(c).wait_send()

    def emit_all(events):
        for stage, c in events:
            emit(stage, c)

    def tick(spent):
        emit_all(planner.tick(spent))

    def produced(c, spent):
        planner.now += spent
        emit_all(planner.produce(c))
        emit_all(planner.tick(0.0))

    def load(slot, source):
        return pltpu.make_async_copy(source, pool.at[slot], load_sem.at[slot])

    def state_load(index, source):
        return pltpu.make_async_copy(source, states.at[index], state_sem.at[index])

    def turn_tile(target, source):
        def turn(n):
            pool[target, pl.ds(n, 256), :] = pool[source, :, pl.ds(n, 256)].T

        return turn

    def transpose_into(target, source):
        turn = turn_tile(target, source)

        def body(i, carry):
            turn(pl.multiple_of(i * 256, 256))
            return carry

        lax.fori_loop(0, 4, body, 0)

    def product_nn(left, right, put, beside=None):
        def body(i, carry):
            n = pl.multiple_of(i * 256, 256)
            if beside is not None:
                beside(n)
            put(n, product(left(), right(n)))
            return carry

        lax.fori_loop(0, 4, body, 0)

    def product_nt(left, right, put, beside=None):
        def body(i, carry):
            n = pl.multiple_of(i * 256, 256)
            if beside is not None:
                beside(n)
            put(
                n,
                lax.dot_general(
                    left(),
                    right(n),
                    (((1,), (1,)), ((), ())),
                    preferred_element_type=jnp.float32,
                ),
            )
            return carry

        lax.fori_loop(0, 4, body, 0)

    def columns_of(slot):
        return lambda n: pool[slot, :, pl.ds(n, 256)]

    def rows_of(slot):
        return lambda n: pool[slot, pl.ds(n, 256), :]

    def weight_grad(slot_in_made, left, right, beside=None):
        def put(n, value):
            low = value.astype(jnp.bfloat16).reshape(4, 256, 256)
            made[slot_in_made, :, :, pl.ds(n, 256)] = low

        product_nn(left, right, put, beside)

    def add_to_acc(n, value):
        acc[:, pl.ds(n, 256)] += value

    def put_in(slot):
        def put(n, value):
            pool[slot, :, pl.ds(n, 256)] = value.astype(jnp.bfloat16)

        return put

    def norm_back(source, gain_row, gain_at, shift_at, offset_at, target):
        tiles = 8
        rows = 1024 // tiles

        def fetch(i):
            place = pl.ds(pl.multiple_of(i * rows, rows), rows)
            return pltpu.make_async_copy(
                source.at[place, :], stream.at[i % 2], stream_sem.at[i % 2]
            )

        fetch(0).start()

        def body(i, carry):
            gain_sum, shift_sum, offset_sum = carry

            @pl.when(i + 1 < tiles)
            def _():
                fetch(i + 1).start()

            fetch(i).wait()
            r = pl.multiple_of(i * rows, rows)
            values = stream[i % 2]
            centred = values - jnp.mean(values, axis=1, keepdims=True)
            spread = jnp.mean(centred * centred, axis=1, keepdims=True)
            scale = lax.rsqrt(spread + NORM_EPS)
            unit = centred * scale
            grad = acc[pl.ds(r, rows), :]
            inner = grad * gains_ref[gain_row : gain_row + 1, :]
            first = jnp.mean(inner, axis=1, keepdims=True)
            second = jnp.mean(inner * unit, axis=1, keepdims=True)
            back = scale * (inner - first - unit * second)
            acc[pl.ds(r, rows), :] = back
            low = back.astype(jnp.bfloat16)
            pool[target, pl.ds(r, rows), :] = low
            return (
                gain_sum + fold(grad * unit),
                shift_sum + fold(grad),
                offset_sum + fold(low.astype(jnp.float32)),
            )

        zero = jnp.zeros((8, D), jnp.float32)
        sums = lax.fori_loop(0, tiles, body, (zero, zero, zero))
        for row, value in zip((gain_at, shift_at, offset_at), sums):
            small[row : row + 1, :] = jnp.sum(value, axis=0, keepdims=True)

    greet([other_core, other_x, other_y] + others_z)
    load(0, dm_ref).start()
    load(6, h2_ref).start()
    load(2, full_ref.at[SHRINK_AT[0]]).start()
    load(3, gp_ref.at[0]).start()
    load(4, g_ref.at[0]).start()
    load(5, full_ref.at[EXPAND_AT[0]]).start()
    acc_load = pltpu.make_async_copy(d_third_ref, acc, place_sem.at[0])
    acc_load.start()
    small[...] = small_ref[...]
    load(6, h2_ref).wait()
    transpose_into(1, 6)
    load(0, dm_ref).wait()
    acc_load.wait()

    planner.now = 4.0
    plan = []
    for j in range(4):
        entry = []
        planner.now += 3.5
        entry.append(planner.tick(0.0) + planner.free_slot(2 * j))
        planner.now += 2.5
        entry.append(planner.produce(2 * j) + planner.tick(0.0) + planner.free_slot(2 * j + 1))
        planner.now += 2.5
        entry.append(planner.produce(2 * j + 1) + planner.tick(0.0))
        entry.append(planner.tick(2.5))
        plan.append(entry)

    def emit_planned(j, place):
        for n in range(4):
            events = plan[n][place]
            if events:

                @pl.when(j == n)
                def _(events=events):
                    emit_all(events)

    def block(j, carry):
        last = j == 3
        load(2, full_ref.at[SHRINK_AT[0]]).wait()
        load(3, gp_ref.at[0]).wait()

        def put_pre(n, value):
            low = (value * pool[3, :, pl.ds(n, 256)].astype(jnp.float32)).astype(jnp.bfloat16)
            pool[7, :, pl.ds(n, 256)] = low
            small[pl.ds(6 + n // 256, 1), pl.ds(pl.multiple_of(j * 256, 256), 256)] = jnp.sum(
                low.astype(jnp.float32), axis=0, keepdims=True
            )

        load(4, g_ref.at[0]).wait()
        product_nt(lambda: pool[0], rows_of(2), put_pre, turn_tile(6, 4))

        @pl.when(jnp.logical_not(last))
        def _():
            load(2, full_ref.at[SHRINK_AT[0] + 2 * (j + 1) - (j + 1) // 3]).start()
            load(3, gp_ref.at[j + 1]).start()

        @pl.when(last)
        def _():
            load(2, full_ref.at[7]).start()
            load(3, cq_ref).start()

        emit_planned(j, 0)

        @pl.when(jnp.logical_not(last))
        def _():
            load(4, g_ref.at[j + 1]).start()

        @pl.when(last)
        def _():
            load(4, oc_ref).start()

        weight_grad((2 * j) % G_SLOTS, lambda: pool[6], columns_of(0))
        emit_planned(j, 1)
        weight_grad((2 * j + 1) % G_SLOTS, lambda: pool[1], columns_of(7))
        emit_planned(j, 2)
        load(5, full_ref.at[EXPAND_AT[0]]).wait()
        product_nt(lambda: pool[7], rows_of(5), add_to_acc)

        @pl.when(jnp.logical_not(last))
        def _():
            load(5, full_ref.at[EXPAND_AT[1] + 2 * j]).start()

        @pl.when(last)
        def _():
            load(5, full_ref.at[4]).start()

        emit_planned(j, 3)
        return carry

    lax.fori_loop(0, 4, block, 0)

    load(7, h1_ref).start()
    state_loads = [state_load(0, ck_ref), state_load(1, cv_ref), state_load(2, e_ref)]
    for copy in state_loads:
        copy.start()
    lse_load = pltpu.make_async_copy(lse_cross_ref, lse_held, state_sem.at[3])
    lse_load.start()
    norm_back(r2_ref, 13, 13, 14, 5, 0)
    tick(4.0)
    load(4, oc_ref).wait()
    load(2, full_ref.at[7]).wait()
    product_nt(lambda: pool[0], rows_of(2), put_in(4), turn_tile(6, 4))
    load(2, full_ref.at[3]).start()
    tick(2.5)
    emit_all(planner.free_slot(8))
    load(7, h1_ref).wait()
    weight_grad(8 % G_SLOTS, lambda: pool[6], columns_of(0), turn_tile(1, 7))
    load(6, o_ref).start()
    load(7, full_ref.at[5]).start()
    produced(8, 2.5)
    load(3, cq_ref).wait()
    for copy in state_loads:
        copy.wait()
    lse_load.wait()

    def attend_loop(causal, step, length, query, key, value, grad, rows, spent, span=(0, 8)):
        ahead = {n: planner.tick(spent) for n in range(*span)}

        def body(i, carry):
            lanes = pl.ds(pl.multiple_of(i * 128, 128), 128)

            def sums(dq, dv):
                small[rows[0] : rows[0] + 1, lanes] = dq
                small[rows[1] : rows[1] + 1, lanes] = dv

            attend_back_pair(
                causal,
                step,
                length,
                query.at[:, lanes],
                key.at[:, lanes],
                value.at[:, lanes],
                grad.at[:, lanes],
                lse_held.at[pl.ds(i, 1)],
                query.at[:, lanes],
                key.at[:, lanes],
                value.at[:, lanes],
                sums,
                dq_t,
                dk_sum,
                dv_sum,
            )
            for n in range(*span):
                if ahead[n]:

                    @pl.when(i == n)
                    def _(events=ahead[n]):
                        emit_all(events)

            return carry

        lax.fori_loop(*span, body, 0)

    attend_loop(
        False,
        512,
        state_lengths_ref[me],
        pool.at[3],
        states.at[0],
        states.at[1],
        pool.at[4],
        (3, 4),
        2.0,
    )
    lse_load = pltpu.make_async_copy(lse_ref, lse_held, state_sem.at[3])
    lse_load.start()
    emit_all(planner.free_slot(9))
    weight_grad(9 % G_SLOTS, lambda: pool[1], columns_of(3))
    produced(9, 2.5)
    load(5, full_ref.at[4]).wait()
    load(6, o_ref).wait()
    product_nt(lambda: pool[3], rows_of(5), add_to_acc, turn_tile(1, 6))
    load(6, x_in_ref).start()
    load(5, full_ref.at[6]).start()
    load(3, q_ref).start()
    tick(2.5)
    states_t[...] = states[2].T
    for c, index in ((10, 0), (11, 1)):
        emit_all(planner.free_slot(c))
        weight_grad(
            c % G_SLOTS, lambda: states_t[...], lambda n, i=index: states[i, :, pl.ds(n, 256)]
        )
        produced(c, 1.0)
    load(7, full_ref.at[5]).wait()
    load(5, full_ref.at[6]).wait()

    def state_part(n):
        dims = (((1,), (1,)), ((), ()))
        return lax.dot_general(
            states[0], pool[7, pl.ds(n, 256), :], dims, preferred_element_type=jnp.float32
        ) + lax.dot_general(
            states[1], pool[5, pl.ds(n, 256), :], dims, preferred_element_type=jnp.float32
        )

    def put_state(i, carry):
        n = pl.multiple_of(i * 256, 256)
        state_grad_ref[:, pl.ds(n, 256)] = state_part(n).astype(jnp.bfloat16)
        return carry

    lax.fori_loop(0, 4, put_state, 0)
    load(5, k_ref).start()
    load(7, v_ref).start()
    tick(1.0)

    norm_back(r1_ref, 11, 11, 12, 2, 0)
    tick(4.0)
    emit_all(planner.free_slot(12))
    weight_grad(12 % G_SLOTS, lambda: pool[1], columns_of(0))
    produced(12, 2.5)
    load(2, full_ref.at[3]).wait()
    load(6, x_in_ref).wait()
    product_nt(lambda: pool[0], rows_of(2), put_in(4), turn_tile(1, 6))
    load(0, full_ref.at[0]).start()
    load(2, full_ref.at[1]).start()
    load(6, full_ref.at[2]).start()
    tick(2.5)
    load(3, q_ref).wait()
    load(5, k_ref).wait()
    load(7, v_ref).wait()
    lse_load.wait()
    def self_heads(span):
        refs = [pool.at[slot] for slot in (3, 5, 7, 4)]
        attend_loop(True, 256, lengths_ref[me], *refs, (0, 1), 5.0, span)

    def query_key_grad(c, half_of):
        def put(i, carry):
            n = pl.multiple_of((i % 2) * 256 + 512 * half_of, 256)
            value = product(pool[1], pool[3 + 2 * (i // 2), :, pl.ds(n, 256)])
            low = value.astype(jnp.bfloat16).reshape(4, 256, 256)
            made[c % G_SLOTS, :, :, pl.ds(pl.multiple_of(i * 256, 256), 256)] = low
            return carry

        emit_all(planner.free_slot(c))
        lax.fori_loop(0, 4, put, 0)
        produced(c, 2.5)

    self_heads((0, 4))
    query_key_grad(13, 0)
    self_heads((4, 8))

    def small_copy(k):
        source = small if k == 0 else small_sum.at[k - 1]
        device = (other_core, other_x, other_y)[k]
        return remote(source, small_in.at[k], small_send_sem.at[k], small_recv_sem.at[k], device)

    def small_z_copy(d):
        return remote(
            small_sum.at[2],
            small_z.at[z],
            small_send_sem.at[3 + d],
            small_recv_sem.at[3 + d],
            others_z[d],
        )

    def small_step(k):
        small_copy(k).wait()
        before = small[...] if k == 0 else small_sum[k - 1]
        small_sum[k] = before + small_in[k]
        if k < 2:
            small_copy(k + 1).start()
        else:
            small_z[z] = small_sum[2]
            for d in range(3):
                small_z_copy(d).start()

    small_copy(0).start()
    emit_all(planner.free_slot(14))
    weight_grad(14 % G_SLOTS, lambda: pool[1], columns_of(7))
    produced(14, 2.5)
    small_step(0)
    query_key_grad(15, 1)
    small_step(1)
    load(0, full_ref.at[0]).wait()
    product_nt(lambda: pool[3], rows_of(0), add_to_acc)
    tick(2.5)
    small_step(2)
    load(2, full_ref.at[1]).wait()
    product_nt(lambda: pool[5], rows_of(2), add_to_acc)
    tick(2.5)
    for d in range(3):
        small_z_copy(d).wait()
    totals_ref[...] = (small_z[0] + small_z[1]) + (small_z[2] + small_z[3])
    load(6, full_ref.at[2]).wait()

    def put_input(n, value):
        total = acc[:, pl.ds(n, 256)] + value
        pool[4, :, pl.ds(n, 256)] = total.astype(jnp.bfloat16)

    product_nt(lambda: pool[7], rows_of(6), put_input)
    token_copy = pltpu.make_async_copy(pool.at[4], token_grad_ref, load_sem.at[4])
    token_copy.start()
    tick(2.5)

    part[...] = jnp.zeros_like(part)

    def spot(place):
        return (0, 1, 2, 6)[place // 4], (place % 4) * 256

    def scan_load(place):
        slot, row = spot(place)
        return pltpu.make_async_copy(
            out_ref.at[place], pool.at[slot, pl.ds(row, 256), :], scan_sem.at[place]
        )

    scans = {}
    for i in range(2):
        scans[i] = ([(0, 512 * i, 512, i, 0), (2, 512 * i, 512, i, 512)], i, (13, 128 * i))
    for i in range(2, 8):
        scans[i] = ([(1 if i == 2 else i, 0, D, i, 0)], i, (13, 128 * i))
    scans[8] = ([(8 + i, 0, D, 8 + i, 0) for i in range(4)], 8, (14, 0))
    for i in range(4):
        scans[9 + i] = ([(12 + i, 0, D, 12, 0)], 9 + i, (14, 128))

    def scan(name):
        sources, row_lane, (total_row, total_lane) = scans[name]
        width = float(sum(source[2] for source in sources))
        step = 64 if name == 8 else 256

        def body(i, carry):
            cols, weights, total = carry
            r = pl.multiple_of(i * step, step)
            squares = []
            for place, lane, lanes, _, _ in sources:
                slot, row = spot(place)
                tile = pool[slot, pl.ds(row + r, step), lane : lane + lanes]
                squares.append(jnp.square(tile.astype(jnp.float32)))
            row_sum = sum(jnp.sum(square, axis=1, keepdims=True) for square in squares)
            rows = DECAY_RATE * rows_ref[pl.ds(r, step), row_lane : row_lane + 1] + (
                1.0 - DECAY_RATE
            ) * (row_sum / width + FACTOR_EPS)
            rows_out[pl.ds(r, step), row_lane : row_lane + 1] = rows
            inverse = 1.0 / rows
            cols = [c + fold(s) for c, s in zip(cols, squares)]
            weights = [w + fold(s * inverse) for w, s in zip(weights, squares)]
            return cols, weights, total + fold(rows)

        zeros = [jnp.zeros((8, source[2]), jnp.float32) for source in sources]
        cols, weights, total = lax.fori_loop(
            0, 256 // step, body, (zeros, zeros, jnp.zeros((8, 1), jnp.float32))
        )
        for (_, _, lanes, slot, lane), col, weighted in zip(sources, cols, weights):
            here = slice(lane, lane + lanes)
            part[slot : slot + 1, here] += jnp.sum(col, axis=0, keepdims=True)
            part[16 + slot : 17 + slot, here] += jnp.sum(weighted, axis=0, keepdims=True)
        part[total_row : total_row + 1, total_lane : total_lane + 128] += jnp.broadcast_to(
            jnp.sum(total), (1, 128)
        )

    chunk_at = {place: c for c, place in enumerate(place_of)}
    tasks = [
        ([chunk_at[source[0]] for source in scans[name][0]], name)
        for name in (9, 10, 11, 12, 8, 7, 4, 5, 6, 3, 2, 0, 1)
    ]
    loaded = set()
    for c in range(CHUNKS):
        if planner.stage[c] > 8:
            scan_load(place_of[c]).start()
    for first, second in planner.drain(tasks, 1.5):
        if first != "task":
            emit(first, second)
            if first == 8:
                scan_load(place_of[second]).start()
            continue
        for source in scans[second][0]:
            if source[0] not in loaded:
                loaded.add(source[0])
                scan_load(source[0]).wait()
        scan(second)
    total = line_sum(part, whole, line_send_sem, line_recv_sem, z, others_z)
    row_counts = [D] * 12 + [FF]
    means = [total[13:14, 128 * i : 128 * i + 1] / D for i in range(8)]
    means = means + [total[14:15, 0:1] / D] * 4 + [total[14:15, 128:129] / FF]
    cols_new, quotients = [], []
    for slot in range(13):
        new = DECAY_RATE * cols_ref[slot : slot + 1, :] + (1.0 - DECAY_RATE) * (
            total[slot : slot + 1] / row_counts[slot] + FACTOR_EPS
        )
        cols_new.append(new)
        quotients.append(jnp.sum(total[16 + slot : 17 + slot] / new, axis=1, keepdims=True))
        cols_out[slot : slot + 1, :] = new
    expand_quotient = quotients[8] + quotients[9] + quotients[10] + quotients[11]
    for slot in range(13):
        if slot < 8:
            mean_square = means[slot] * quotients[slot] / (D * D)
            rate = STEP_RATE * (OUT_GAIN if slot % 4 == 3 else 1.0)
        else:
            quotient = expand_quotient if slot < 12 else quotients[12]
            mean_square = means[slot] * quotient / (D * FF)
            rate = STEP_RATE
        factor = rate / jnp.maximum(1.0, jnp.sqrt(mean_square) / CLIP_LEVEL)
        scale_out[slot : slot + 1, :] = lax.rsqrt(cols_new[slot] / means[slot]) * factor
    token_copy.wait()


def backward(scalars, held, gains, small, factor_rows, factor_cols):
    any_space = pl.BlockSpec(memory_space=pl.ANY)
    vmem = pl.BlockSpec(memory_space=pltpu.VMEM)
    shape = jax.ShapeDtypeStruct
    dma = pltpu.SemaphoreType.DMA
    low = jnp.bfloat16
    wide = jnp.float32
    rows = small.shape[0]
    return pl.pallas_call(
        backward_kernel,
        out_shape=(
            shape((1024, D), low),
            shape((128, D), low),
            shape((CHUNKS, 256, D), low),
            shape(small.shape, wide),
            shape((256, 128), wide),
            shape((16, D), wide),
            shape((16, D), wide),
            shape((CHUNKS, 4, 128, D), low),
        ),
        in_specs=[SCALARS] * 2 + [any_space] * len(held) + [vmem] * 4,
        out_specs=(any_space, vmem, any_space, vmem, vmem, vmem, vmem, any_space),
        scratch_shapes=[
            pltpu.VMEM((POOL, 1024, D), low),
            pltpu.VMEM((1024, D), wide),
            pltpu.VMEM((G_SLOTS, 4, 256, D), low),
            pltpu.VMEM((R_SLOTS, 4, 128, D), low),
            pltpu.VMEM((CHUNKS, 4, 64, D), low),
            pltpu.VMEM((CHUNKS, 4, 32, D), low),
            pltpu.VMEM((CHUNKS, 3, 32, D), low),
            pltpu.VMEM((2, 128, D), wide),
            pltpu.VMEM((128, 1024), wide),
            pltpu.VMEM((2, 1024, 128), wide),
            pltpu.VMEM((2, 1024, 128), wide),
            pltpu.VMEM((8, 8, 1024), wide),
            pltpu.VMEM((3, 128, D), low),
            pltpu.VMEM((D, 128), low),
            pltpu.VMEM((rows, D), wide),
            pltpu.VMEM((3, rows, D), wide),
            pltpu.VMEM((3, rows, D), wide),
            pltpu.VMEM((4, rows, D), wide),
            pltpu.VMEM((32, D), wide),
            pltpu.VMEM((4, 32, D), wide),
            dma((POOL,)),
            dma((2,)),
            dma((4,)),
            dma((R_SLOTS,)),
            dma((CHUNKS,)),
            dma((3,)),
            dma((3,)),
            dma((6, CHUNKS)),
            dma((6, CHUNKS)),
            dma((CHUNKS, 3)),
            dma((CHUNKS, 3)),
            dma((CHUNKS,)),
            dma((6,)),
            dma((6,)),
        ],
        compiler_params=pltpu.CompilerParams(
            collective_id=0, has_side_effects=True, vmem_limit_bytes=62 * MIB
        ),
    )(*scalars, *held, gains, small, factor_rows, factor_cols)[0:7]


def line_sum(part, whole, send_sem, recv_sem, z, others_z):
    copies = [
        remote(part, whole.at[z], send_sem.at[d], recv_sem.at[d], others_z[d]) for d in range(3)
    ]
    for copy in copies:
        copy.start()
    whole[z] = part[...]
    for copy in copies:
        copy.wait()
    return (whole[0] + whole[1]) + (whole[2] + whole[3])


def update_attention_kernel(
    grad_ref, weight_ref, rows_ref, scale_ref, grad_out, new_out, copy_out, grads, change
):
    block = grad_ref.shape[1]
    for i in range(8):
        rows = lax.rsqrt(rows_ref[:, i : i + 1])
        every = pl.ds(i, block, stride=8)
        for lane in range(8):
            columns = slice(lane * 128, lane * 128 + 128)
            if i < 2:
                start = 512 * i + 128 * (lane % 4)
                grad = grad_ref[2 * (lane // 4), :, start : start + 128]
            else:
                grad = grad_ref[1 if i == 2 else i, :, columns]
            grad = grad.astype(jnp.float32)
            grads[lane, every, :] = grad
            change[lane, every, :] = grad * rows * scale_ref[i : i + 1, columns]
    for lane in range(8):
        columns = slice(lane * 128, lane * 128 + 128)
        grad_out[:, columns] = grads[lane]
        new = weight_ref[:, columns] - change[lane]
        new_out[:, columns] = new
        copy_out[:, columns] = new.astype(jnp.bfloat16)


def update_attention(grads, weights, rows, scale):
    block = 32
    wide = pl.BlockSpec((block * 8, D), lambda i: (i, 0))
    shape = jax.ShapeDtypeStruct
    new = pl.pallas_call(
        update_attention_kernel,
        grid=(256 // block,),
        out_shape=(
            shape((2048, D), jnp.float32),
            shape((2048, D), jnp.float32),
            shape((2048, D), jnp.bfloat16),
        ),
        in_specs=[
            pl.BlockSpec((8, block, D), lambda i: (0, i, 0)),
            wide,
            pl.BlockSpec((block, 128), lambda i: (i, 0)),
            pl.BlockSpec((16, D), lambda i: (0, 0)),
        ],
        out_specs=(wide,) * 3,
        scratch_shapes=[pltpu.VMEM((8, block * 8, 128), jnp.float32)] * 2,
        compiler_params=pltpu.CompilerParams(vmem_limit_bytes=62 * MIB),
    )(grads, weights.reshape(2048, D), rows, scale)
    return [t.reshape(256, 8, D) for t in new]


def update_kernel(
    first, slots, grad_ref, weight_ref, rows_ref, scale_ref, grad_out, new_out, copy_out
):
    spans = 4 if slots == 4 else 1
    wide = D // spans
    for i in range(slots):
        grads = grad_ref[i].astype(jnp.float32)
        changes = grads * (lax.rsqrt(rows_ref[...]) * scale_ref[first + i : first + i + 1, :])
        for s in range(spans):
            start = s * D + i * wide
            columns = slice(start, start + wide)
            part = slice(s * wide, s * wide + wide)
            grad_out[:, columns] = grads[:, part]
            new = weight_ref[:, columns] - changes[:, part]
            new_out[:, columns] = new
            copy_out[:, columns] = new.astype(jnp.bfloat16)


def update_plain(grads, weights, rows, scale, first, slots, grad_map):
    count, width = weights.shape
    block = 128 // slots
    wide = pl.BlockSpec((block, width), lambda i: (i, 0))
    shape = jax.ShapeDtypeStruct
    return pl.pallas_call(
        lambda *refs: update_kernel(first, slots, *refs),
        grid=(count // block,),
        out_shape=(
            shape(weights.shape, jnp.float32),
            shape(weights.shape, jnp.float32),
            shape(weights.shape, jnp.bfloat16),
        ),
        in_specs=[
            pl.BlockSpec((slots, block, D), grad_map),
            wide,
            pl.BlockSpec((block, 1), lambda i: (i, 0)),
            pl.BlockSpec((16, D), lambda i: (0, 0)),
        ],
        out_specs=(wide,) * 3,
        compiler_params=pltpu.CompilerParams(vmem_limit_bytes=62 * MIB),
    )(grads, weights, rows, scale)


def update_direct(grads, rows, scale, attention_weights, expand_weight, shrink_weight):
    shr_rows = rows[:, 9:13].T.reshape(-1, 1)
    attention = update_attention(grads, attention_weights, rows, scale)
    expand = update_plain(grads, expand_weight, rows[:, 8:9], scale, 8, 4, lambda i: (2, i, 0))
    shrink = update_plain(
        grads, shrink_weight, shr_rows, scale, 12, 1, lambda i: (12 + i // 2, i % 2, 0)
    )
    return attention, expand, shrink, (rows[:, 0:8].T, rows[:, 8], shr_rows[:, 0])


def as_rows(vector):
    rows = -(-vector.shape[0] // 1024) * 8
    return jnp.pad(vector, (0, rows * 128 - vector.shape[0])).reshape(rows, 128)


def masked_scores(query_part, key_heads, first_row, valid_count, causal):
    scores = jnp.einsum("qhd,khd->hqk", query_part, key_heads, preferred_element_type=jnp.float32)
    key_places = jnp.arange(key_heads.shape[0], dtype=jnp.int32)[None, :]
    usable = key_places < valid_count
    if causal:
        query_places = first_row + jnp.arange(query_part.shape[0], dtype=jnp.int32)[:, None]
        usable = usable & (key_places <= query_places)
    return jnp.where(usable[None], scores, MASKED)


def attend_forward(queries, key_heads, values, valid_count, causal):
    query_rows = queries.shape[0]
    step_rows = min(512, query_rows)
    outputs, stored = ([], [])
    for b in range(query_rows // step_rows):
        first_row = b * step_rows
        key_end = first_row + step_rows if causal else key_heads.shape[0]
        scores = masked_scores(
            queries[first_row : first_row + step_rows],
            key_heads[:key_end],
            first_row,
            valid_count,
            causal,
        )
        row_max = jnp.max(scores, axis=-1, keepdims=True)
        raised = jnp.exp(scores - row_max)
        totals = jnp.sum(raised, axis=-1, keepdims=True)
        probs_low = (raised / totals).astype(jnp.bfloat16)
        outputs.append(
            jnp.einsum(
                "hqk,khd->qhd", probs_low, values[:key_end], preferred_element_type=jnp.float32
            )
        )
        stored.append(row_max + jnp.log(totals))
    return (jnp.concatenate(outputs, axis=0), stored)


def attend_backward(queries, key_heads, values, grad_out, stored, valid_count, causal):
    query_rows = queries.shape[0]
    key_rows = key_heads.shape[0]
    step_rows = min(512, query_rows)
    grad_queries = []
    grad_keys = jnp.zeros(key_heads.shape, jnp.float32)
    grad_values = jnp.zeros(values.shape, jnp.float32)
    for b in range(query_rows // step_rows):
        first_row = b * step_rows
        key_end = first_row + step_rows if causal else key_rows
        query_part = queries[first_row : first_row + step_rows]
        grad_part = grad_out[first_row : first_row + step_rows]
        scores = masked_scores(query_part, key_heads[:key_end], first_row, valid_count, causal)
        probs = jnp.exp(scores - stored[b])
        probs_low = probs.astype(jnp.bfloat16)
        grad_probs = jnp.einsum(
            "qhd,khd->hqk", grad_part, values[:key_end], preferred_element_type=jnp.float32
        )
        value_part = jnp.einsum(
            "hqk,qhd->khd", probs_low, grad_part, preferred_element_type=jnp.float32
        )
        grad_scores = probs * (grad_probs - jnp.sum(probs * grad_probs, axis=-1, keepdims=True))
        scores_low = grad_scores.astype(jnp.bfloat16)
        grad_queries.append(
            jnp.einsum(
                "hqk,khd->qhd", scores_low, key_heads[:key_end], preferred_element_type=jnp.float32
            )
        )
        key_part = jnp.einsum(
            "hqk,qhd->khd", scores_low, query_part, preferred_element_type=jnp.float32
        )
        padding = ((0, key_rows - key_end), (0, 0), (0, 0))
        grad_keys = grad_keys + jnp.pad(key_part, padding)
        grad_values = grad_values + jnp.pad(value_part, padding)
    return (jnp.concatenate(grad_queries, axis=0), grad_keys, grad_values)


def gather_rows(piece):
    return lax.all_gather(piece, ("shard", "rep"), axis=0, tiled=True)


def own_piece(block, replicas):
    rows = block.shape[0] // replicas
    return lax.dynamic_slice_in_dim(block, lax.axis_index("rep") * rows, rows, axis=0)


def scatter_rows(grad):
    piece = lax.psum_scatter(
        grad.astype(jnp.bfloat16), ("shard", "rep"), scatter_dimension=0, tiled=True
    )
    return lax.all_gather(piece, "rep", axis=0, tiled=True)


def local_factors(grad, rows):
    square = grad * grad
    rows_new = DECAY_RATE * rows + (1.0 - DECAY_RATE) * jnp.mean(square + FACTOR_EPS, axis=-1)
    col_part = jnp.sum(square + FACTOR_EPS, axis=0)
    weighted = jnp.sum(square / rows_new[..., None], axis=0)
    return rows_new, col_part, weighted, jnp.sum(rows_new, axis=0)


def finish_factors(grad, weight, rows_new, cols, col_sum, weighted, row_total, row_count, rate):
    cols_new = DECAY_RATE * cols + (1.0 - DECAY_RATE) * col_sum / row_count
    mean_rows = row_total / row_count
    mean_square = mean_rows * jnp.sum(weighted / cols_new, axis=-1) / (row_count * cols.shape[-1])
    factor = rate / jnp.maximum(1.0, jnp.sqrt(mean_square) / CLIP_LEVEL)
    scaled = lax.rsqrt(cols_new / mean_rows[..., None]) * factor[..., None]
    fresh = weight - grad * (lax.rsqrt(rows_new)[..., None] * scaled[None])
    return fresh, cols_new


def plain_device(
    tokens,
    encoder,
    cotangent,
    lengths,
    encoder_lengths,
    dealt_order,
    attention_weights,
    expand_weight,
    shrink_weight,
    small_params,
    attention_rows,
    attention_cols,
    expand_rows,
    expand_cols,
    shrink_rows,
    shrink_cols,
    small_moment,
):
    devices = lax.axis_size(("rep", "shard"))
    replicas = lax.axis_size("rep")
    shards = lax.axis_size("shard")
    slot_tokens = tokens.shape[0]
    slot_states = encoder.shape[0]
    position = lax.axis_index(("rep", "shard"))
    inverse = (
        jnp.zeros((devices,), jnp.int32).at[dealt_order].set(jnp.arange(devices, dtype=jnp.int32))
    )
    qkv_piece = own_piece(attention_weights[:, 0:3, :].reshape(-1, 3 * D), replicas)
    rest_piece = own_piece(attention_weights[:, 3:8, :].reshape(-1, 5 * D), replicas)
    qkv_full = gather_rows(qkv_piece.astype(jnp.bfloat16))
    rest_full = gather_rows(rest_piece.astype(jnp.bfloat16))
    expand_full = gather_rows(own_piece(expand_weight, replicas).astype(jnp.bfloat16))
    shrink_full = gather_rows(own_piece(shrink_weight, replicas).astype(jnp.bfloat16))
    spread = lax.all_to_all(
        tokens.reshape(devices, slot_tokens // devices, D),
        ("rep", "shard"),
        split_axis=0,
        concat_axis=0,
        tiled=True,
    )
    picked = jnp.take(spread, inverse, axis=0)
    tokens = lax.all_to_all(
        picked, ("rep", "shard"), split_axis=0, concat_axis=0, tiled=True
    ).reshape(slot_tokens, D)
    states = encoder
    incoming = cotangent
    valid_tokens = lengths[position]
    valid_states = encoder_lengths[position]
    matrices = [qkv_full[:, i * D : (i + 1) * D] for i in range(3)] + [
        rest_full[:, i * D : (i + 1) * D] for i in range(5)
    ]
    parts = unpack(small_params)
    token_heads = (slot_tokens, HEADS, HEAD_DIM)
    state_heads = (slot_states, HEADS, HEAD_DIM)
    q_self = ((forward_product(tokens, matrices[0]) + parts[0]) * 0.125).astype(
        jnp.bfloat16
    )
    k_self = forward_product(tokens, matrices[1]).astype(jnp.bfloat16)
    v_self = (forward_product(tokens, matrices[2]) + parts[1]).astype(jnp.bfloat16)
    o_self, lse_self = attend_forward(
        q_self.reshape(token_heads),
        k_self.reshape(token_heads),
        v_self.reshape(token_heads),
        valid_tokens,
        True,
    )
    o_self_low = o_self.reshape(slot_tokens, D).astype(jnp.bfloat16)
    branch_a = forward_product(o_self_low, matrices[3]) + parts[2]
    tokens_wide = tokens.astype(jnp.float32)
    hidden_one, norm_one_back = jax.vjp(layer_norm, tokens_wide + branch_a, parts[8], parts[9])
    hidden_one_low = hidden_one.astype(jnp.bfloat16)
    q_cross = (
        (forward_product(hidden_one_low, matrices[4]) + parts[3]) * 0.125
    ).astype(jnp.bfloat16)
    k_cross = forward_product(states, matrices[5]).astype(jnp.bfloat16)
    v_cross = (forward_product(states, matrices[6]) + parts[4]).astype(jnp.bfloat16)
    o_cross, lse_cross = attend_forward(
        q_cross.reshape(token_heads),
        k_cross.reshape(state_heads),
        v_cross.reshape(state_heads),
        valid_states,
        False,
    )
    o_cross_low = o_cross.reshape(slot_tokens, D).astype(jnp.bfloat16)
    branch_c = forward_product(o_cross_low, matrices[7]) + parts[5]
    hidden_two, norm_two_back = jax.vjp(layer_norm, hidden_one + branch_c, parts[10], parts[11])
    hidden_two_low = hidden_two.astype(jnp.bfloat16)
    pre_act = forward_product(hidden_two_low, expand_full) + parts[6]
    activated, gelu_back = jax.vjp(gelu_exact, pre_act)
    activated_low = activated.astype(jnp.bfloat16)
    branch_m = forward_product(activated_low, shrink_full) + parts[7]
    result, norm_three_back = jax.vjp(layer_norm, hidden_two + branch_m, parts[12], parts[13])
    usable_rows = (jnp.arange(slot_tokens, dtype=jnp.int32) < valid_tokens).astype(jnp.float32)[
        :, None
    ]
    squares = jnp.stack(
        [
            jnp.sum(usable_rows * t * t)
            for t in (tokens_wide, branch_a, hidden_one, branch_c, hidden_two, branch_m)
        ]
    )
    d_third, d_gain_three, d_shift_three = norm_three_back(
        incoming.astype(jnp.float32) * usable_rows
    )
    d_mlp = d_third.astype(jnp.bfloat16)
    grad_shrink = weight_product(activated_low, d_mlp)
    grad_shrink_offset = row_sum(d_mlp)
    d_activated = input_product(d_mlp, shrink_full)
    d_pre = gelu_back(d_activated)[0].astype(jnp.bfloat16)
    grad_expand = weight_product(hidden_two_low, d_pre)
    grad_expand_offset = row_sum(d_pre)
    d_hidden_two = d_third + input_product(d_pre, expand_full)
    d_second, d_gain_two, d_shift_two = norm_two_back(d_hidden_two)
    d_branch_c = d_second.astype(jnp.bfloat16)
    grad_cross_out = weight_product(o_cross_low, d_branch_c)
    grad_cross_out_offset = row_sum(d_branch_c)
    d_o_cross = input_product(d_branch_c, matrices[7]).astype(jnp.bfloat16)
    grad_cq, grad_ck, grad_cv = attend_backward(
        q_cross.reshape(token_heads),
        k_cross.reshape(state_heads),
        v_cross.reshape(state_heads),
        d_o_cross.reshape(token_heads),
        lse_cross,
        valid_states,
        False,
    )
    dq_cross = (grad_cq.reshape(slot_tokens, D) * 0.125).astype(jnp.bfloat16)
    dk_cross = grad_ck.reshape(slot_states, D).astype(jnp.bfloat16)
    dv_cross = grad_cv.reshape(slot_states, D).astype(jnp.bfloat16)
    grad_cross_query = weight_product(hidden_one_low, dq_cross)
    grad_cross_key = weight_product(states, dk_cross)
    grad_cross_value = weight_product(states, dv_cross)
    state_grad = input_product(dk_cross, matrices[5]) + input_product(
        dv_cross, matrices[6]
    )
    d_hidden_one = d_second + input_product(dq_cross, matrices[4])
    d_first, d_gain_one, d_shift_one = norm_one_back(d_hidden_one)
    d_branch_a = d_first.astype(jnp.bfloat16)
    grad_self_out = weight_product(o_self_low, d_branch_a)
    grad_self_out_offset = row_sum(d_branch_a)
    d_o_self = input_product(d_branch_a, matrices[3]).astype(jnp.bfloat16)
    grad_sq, grad_sk, grad_sv = attend_backward(
        q_self.reshape(token_heads),
        k_self.reshape(token_heads),
        v_self.reshape(token_heads),
        d_o_self.reshape(token_heads),
        lse_self,
        valid_tokens,
        True,
    )
    dq_self = (grad_sq.reshape(slot_tokens, D) * 0.125).astype(jnp.bfloat16)
    dk_self = grad_sk.reshape(slot_tokens, D).astype(jnp.bfloat16)
    dv_self = grad_sv.reshape(slot_tokens, D).astype(jnp.bfloat16)
    grad_self_query = weight_product(tokens, dq_self)
    grad_self_key = weight_product(tokens, dk_self)
    grad_self_value = weight_product(tokens, dv_self)
    token_grad = (
        d_first
        + input_product(dq_self, matrices[0])
        + input_product(dk_self, matrices[1])
        + input_product(dv_self, matrices[2])
    )
    small_partial = jnp.concatenate(
        [
            row_sum(dq_self),
            row_sum(dv_self),
            grad_self_out_offset,
            row_sum(dq_cross),
            row_sum(dv_cross),
            grad_cross_out_offset,
            grad_expand_offset,
            grad_shrink_offset,
            d_gain_one,
            d_shift_one,
            d_gain_two,
            d_shift_two,
            d_gain_three,
            d_shift_three,
        ]
    )
    totals = lax.psum(jnp.concatenate([small_partial, squares]), ("rep", "shard"))
    g_shrink = scatter_rows(grad_shrink)
    g_expand = scatter_rows(grad_expand)
    g_rest = scatter_rows(
        jnp.concatenate(
            [grad_self_out, grad_cross_query, grad_cross_key, grad_cross_value, grad_cross_out],
            axis=1,
        )
    )
    g_qkv = scatter_rows(
        jnp.concatenate([grad_self_query, grad_self_key, grad_self_value], axis=1)
    )
    g_attention = (
        jnp.concatenate([g_qkv, g_rest], axis=1).reshape(-1, 8, D).astype(jnp.float32)
    )
    g_expand = g_expand.astype(jnp.float32)
    g_shrink = g_shrink.astype(jnp.float32)
    attention_rows_new, *attention_parts = local_factors(g_attention, attention_rows.T)
    expand_rows_new, *expand_parts = local_factors(g_expand, expand_rows)
    shrink_rows_new, *shrink_parts = local_factors(g_shrink, shrink_rows)
    flat = attention_parts + expand_parts + shrink_parts
    summed = lax.psum(jnp.concatenate([t.reshape(-1) for t in flat]), "shard")
    sums = []
    offset = 0
    for t in flat:
        sums.append(summed[offset : offset + t.size].reshape(t.shape))
        offset = offset + t.size
    attention_rates = STEP_RATE * jnp.where(jnp.arange(8) % 4 == 3, OUT_GAIN, 1.0).astype(
        jnp.float32
    )
    attention_new, attention_cols_new = finish_factors(
        g_attention,
        attention_weights,
        attention_rows_new,
        attention_cols,
        *sums[0:3],
        D,
        attention_rates,
    )
    expand_new, expand_cols_new = finish_factors(
        g_expand, expand_weight, expand_rows_new, expand_cols, *sums[3:6], D, STEP_RATE
    )
    shrink_new, shrink_cols_new = finish_factors(
        g_shrink, shrink_weight, shrink_rows_new, shrink_cols, *sums[6:9], FF, STEP_RATE
    )
    small_grad = totals[: small_params.shape[0]]
    small_moment_new = DECAY_RATE * small_moment + (1.0 - DECAY_RATE) * (
        small_grad * small_grad + FACTOR_EPS
    )
    small_update = small_grad * lax.rsqrt(small_moment_new)
    small_scale = jnp.sqrt(jnp.mean(small_update * small_update))
    small_new = small_params - SMALL_RATE * small_update / jnp.maximum(
        1.0, small_scale / CLIP_LEVEL
    )
    norm_stats = jnp.sqrt(
        totals[small_params.shape[0] :] / (jnp.sum(lengths).astype(jnp.float32) * D)
    )
    return (
        result.astype(jnp.bfloat16),
        token_grad.astype(jnp.bfloat16),
        state_grad.astype(jnp.bfloat16),
        g_attention,
        g_expand,
        g_shrink,
        small_grad,
        attention_new,
        expand_new,
        shrink_new,
        small_new,
        attention_new.astype(jnp.bfloat16),
        expand_new.astype(jnp.bfloat16),
        shrink_new.astype(jnp.bfloat16),
        attention_rows_new.T,
        attention_cols_new,
        expand_rows_new,
        expand_cols_new,
        shrink_rows_new,
        shrink_cols_new,
        small_moment_new,
        norm_stats,
    )


def direct_device(
    tokens,
    encoder,
    cotangent,
    lengths,
    encoder_lengths,
    dealt_order,
    attention_weights,
    expand_weight,
    shrink_weight,
    small_params,
    attention_rows,
    attention_cols,
    expand_rows,
    expand_cols,
    shrink_rows,
    shrink_cols,
    small_moment,
):
    inverse = jnp.zeros((32,), jnp.int32).at[dealt_order].set(jnp.arange(32, dtype=jnp.int32))
    params = small_params.reshape(17, D)
    weights = (attention_weights.reshape(2048, D), expand_weight, shrink_weight)
    (
        tokens,
        full,
        q_self,
        k_self,
        v_self,
        o_self,
        lse_self,
        q_cross,
        k_cross,
        v_cross,
        o_cross,
        lse_cross,
        summed_one,
        summed_two,
        hidden_one,
        hidden_two,
        activated,
        slope,
        output,
        d_mlp,
        d_third,
        small_first,
    ) = forward(
        (inverse, lengths, encoder_lengths), tokens, weights, encoder, cotangent, params
    )
    factor_rows = jnp.concatenate(
        [attention_rows, expand_rows.reshape(1, 256), shrink_rows.reshape(4, 256)]
    )
    factor_rows = jnp.pad(factor_rows.T, ((0, 0), (0, 115)))
    factor_cols = jnp.concatenate(
        [attention_cols, hidden_blocks(expand_cols), shrink_cols.reshape(1, D), jnp.ones((3, D))]
    )
    token_grad, state_grad, reduced, totals, factor_rows, factor_cols, scale = backward(
        (lengths, encoder_lengths),
        (
            d_mlp,
            d_third,
            activated,
            slope,
            full.reshape(GATHERED, 1024, D),
            hidden_two,
            hidden_one,
            tokens.reshape(1024, D),
            encoder,
            o_cross,
            o_self,
            summed_one,
            summed_two,
            q_self,
            k_self,
            v_self,
            q_cross,
            k_cross,
            v_cross,
            lse_self,
            lse_cross,
        ),
        params,
        small_first,
        factor_rows,
        factor_cols,
    )
    attention, expand, shrink, rows_new = update_direct(
        reduced, factor_rows, scale, attention_weights, expand_weight, shrink_weight
    )
    cols_new = (factor_cols[0:8], hidden_flat(factor_cols[8:12]), factor_cols[12])
    small_grad = totals[0:17].reshape(-1)
    small_moment_new = DECAY_RATE * small_moment + (1.0 - DECAY_RATE) * (
        small_grad * small_grad + FACTOR_EPS
    )
    small_update = small_grad * lax.rsqrt(small_moment_new)
    small_scale = jnp.sqrt(jnp.mean(small_update * small_update))
    small_new = small_params - SMALL_RATE * small_update / jnp.maximum(
        1.0, small_scale / CLIP_LEVEL
    )
    norm_stats = jnp.sqrt(totals[17, 0:6] / (jnp.sum(lengths).astype(jnp.float32) * D))
    return (
        output,
        token_grad,
        state_grad,
        attention[0],
        expand[0],
        shrink[0],
        small_grad,
        attention[1],
        expand[1],
        shrink[1],
        small_new,
        attention[2],
        expand[2],
        shrink[2],
        rows_new[0],
        cols_new[0],
        rows_new[1],
        cols_new[1],
        rows_new[2],
        cols_new[2],
        small_moment_new,
        norm_stats,
    )


def on_device(*args):
    if lax.axis_size("rep") == 8 and lax.axis_size("shard") == 4:
        return direct_device(*args)
    return plain_device(*args)


def solution(mesh):
    in_specs = (
        P(("rep", "shard"), None),
        P(("rep", "shard"), None),
        P(("rep", "shard"), None),
        P(),
        P(),
        P(),
        P("shard", None, None),
        P("shard", None),
        P("shard", None),
        P(),
        P(None, "shard"),
        P(),
        P("shard"),
        P(),
        P("shard"),
        P(),
        P(),
    )
    out_specs = (
        P(("rep", "shard"), None),
        P(("rep", "shard"), None),
        P(("rep", "shard"), None),
        P("shard", None, None),
        P("shard", None),
        P("shard", None),
        P(),
        P("shard", None, None),
        P("shard", None),
        P("shard", None),
        P(),
        P("shard", None, None),
        P("shard", None),
        P("shard", None),
        P(None, "shard"),
        P(),
        P("shard"),
        P(),
        P("shard"),
        P(),
        P(),
        P(),
    )
    return jax.shard_map(
        on_device, mesh=mesh, in_specs=in_specs, out_specs=out_specs, check_vma=False
    )
```

```python
import math

import jax
import jax.numpy as jnp
from jax import lax
from jax.experimental import pallas as pl
from jax.experimental.pallas import tpu as pltpu
from jax.sharding import PartitionSpec as P

D = 1024
HEADS = 16
HEAD_DIM = 64
FF = 4096


DECAY_RATE = 0.5
CLIP_LEVEL = 0.25
STEP_RATE = 0.1
SMALL_RATE = 0.4
OUT_GAIN = 8.0
NORM_EPS = 1e-05
FACTOR_EPS = 1e-30
MASKED = -1e30
MESH = pl.DeviceIdType.MESH
CHUNKS = 16
GATHERED = 16
EXPAND_AT = (8, 9, 11, 13)
SHRINK_AT = (10, 12, 14, 15)
MIB = 1 << 20


def layer_norm(r, norm_gain, norm_shift):
    centred = r - jnp.mean(r, axis=-1, keepdims=True)
    spread = jnp.mean(centred * centred, axis=-1, keepdims=True)
    return centred * lax.rsqrt(spread + NORM_EPS) * norm_gain + norm_shift


def gelu_exact(values):
    return jax.nn.gelu(values, approximate=False)


def unpack(small):
    extents = [D] * 6 + [FF] + [D] * 7
    pieces = []
    offset = 0
    for extent in extents:
        pieces.append(small[offset : offset + extent])
        offset = offset + extent
    return pieces


def forward_product(source, matrix):
    return jnp.dot(source, matrix, preferred_element_type=jnp.float32)


def input_product(grad_low, matrix):
    return jnp.einsum("to,io->ti", grad_low, matrix, preferred_element_type=jnp.float32)


def weight_product(source, grad_low):
    return jnp.einsum("ti,to->io", source, grad_low, preferred_element_type=jnp.float32)


def row_sum(grad_low):
    return jnp.sum(grad_low.astype(jnp.float32), axis=0)


def transposed(block):
    return block.astype(jnp.float32).T.astype(jnp.bfloat16)


def half_lanes(shape, dim):
    return lax.broadcasted_iota(jnp.int32, shape, dim)


def masked_keys(keys, length, head):
    place = half_lanes(keys.shape, 0)
    lane = half_lanes(keys.shape, 1)
    blocked = jnp.where((lane == 64 - 64 * head) & (place >= length), MASKED, 0.0)
    own = (lane >= 64 * head) & (lane < 64 * head + 64)
    return jnp.where(own, keys.astype(jnp.float32), blocked).astype(jnp.bfloat16)


def own_head(rows_t, head, fill):
    place = half_lanes(rows_t.shape, 0)
    own = (place >= 64 * head) & (place < 64 * head + 64)
    other = jnp.where(place == 64 - 64 * head, fill, 0.0)
    return jnp.where(own, rows_t.astype(jnp.float32), other).astype(jnp.bfloat16)


def product(first, second):
    return jnp.dot(first, second, preferred_element_type=jnp.float32)


def causal_mask(scores, step):
    kept = scores.shape[0] - step
    last = scores[kept:]
    allowed = half_lanes(last.shape, 0) <= half_lanes(last.shape, 1)
    last = jnp.where(allowed, last, MASKED)
    return last if kept == 0 else jnp.concatenate([scores[:kept], last], axis=0)


def attend_pair(
    causal, step, length, q_ref, k_ref, v_ref, o_ref, lse_ref, o_t, first_row=0
):
    count = q_ref.shape[0]
    q_t = transposed(q_ref[...])
    v_t = transposed(v_ref[...])
    keys = [masked_keys(k_ref[...], length, head) for head in range(2)]
    queries = [own_head(q_t, head, 1.0) for head in range(2)]
    units = [(head, start) for start in range(0, count, step) for head in range(2)]

    def scores_of(head, start):
        end = first_row + start + step if causal else k_ref.shape[0]
        return product(keys[head][:end], queries[head][:, start : start + step])

    ahead = scores_of(*units[0])
    for index, (head, start) in enumerate(units):
        scores = ahead
        if index + 1 < len(units):
            ahead = scores_of(*units[index + 1])
        rows = slice(64 * head, 64 * head + 64)
        columns = slice(start, start + step)
        if causal:
            scores = causal_mask(scores, step)
        top = jnp.max(scores, axis=0, keepdims=True)
        raised = jnp.exp(scores - top)
        total = jnp.sum(raised, axis=0, keepdims=True)
        probs = (raised * (1.0 / total)).astype(jnp.bfloat16)
        o_t[rows, columns] = product(v_t[rows, : scores.shape[0]], probs)
        place = slice(first_row + start, first_row + start + step)
        lse_ref[0, head : head + 1, place] = top + jnp.log(total)
    o_ref[...] = o_t[:, :count].T.astype(jnp.bfloat16)


def attend_back_pair(
    causal,
    step,
    length,
    q_ref,
    k_ref,
    v_ref,
    do_ref,
    lse_ref,
    dq_ref,
    dk_ref,
    dv_ref,
    put_sums,
    dq_t,
    dk_sum,
    dv_sum,
):
    key_rows = k_ref.shape[0]
    q_t = transposed(q_ref[...])
    k_t = transposed(k_ref[...])
    do_t = transposed(do_ref[...])
    values = v_ref[...]
    keys = [masked_keys(k_ref[...], length, head) for head in range(2)]
    queries = [own_head(q_t, head, 1.0) for head in range(2)]
    grads = [own_head(do_t, head, 0.0) for head in range(2)]
    count = q_ref.shape[0] // step
    units = [(head, b) for b in reversed(range(count)) for head in range(2)]

    def products_of(head, b):
        columns = slice(b * step, b * step + step)
        end = b * step + step if causal else key_rows
        scores = product(keys[head][:end], queries[head][:, columns])
        return scores, product(values[:end], grads[head][:, columns])

    ahead = products_of(*units[0])
    for index, (head, b) in enumerate(units):
        scores, d_probs = ahead
        if index + 1 < len(units):
            ahead = products_of(*units[index + 1])
        rows = slice(64 * head, 64 * head + 64)
        columns = slice(b * step, b * step + step)
        end = scores.shape[0]
        if causal:
            scores = causal_mask(scores, step)
        probs = jnp.exp(scores - lse_ref[0, head : head + 1, columns])
        weighted = probs * d_probs
        delta = jnp.sum(weighted, axis=0, keepdims=True)
        d_scores = (weighted - probs * delta).astype(jnp.bfloat16)
        dv = product(probs.astype(jnp.bfloat16), do_ref[columns, :])
        dk = product(d_scores, q_ref[columns, :])
        if b == count - 1:
            dv_sum[head, :end] = dv
            dk_sum[head, :end] = dk
        else:
            dv_sum[head, :end] += dv
            dk_sum[head, :end] += dk
        dq_t[rows, columns] = product(k_t[rows, :end], d_scores)
    first = half_lanes((key_rows, 128), 1) < 64
    dk_ref[...] = jnp.where(first, dk_sum[0, :key_rows], dk_sum[1, :key_rows]).astype(jnp.bfloat16)
    dv = jnp.where(first, dv_sum[0, :key_rows], dv_sum[1, :key_rows]).astype(jnp.bfloat16)
    dv_ref[...] = dv
    dq = (dq_t[...] * 0.125).T.astype(jnp.bfloat16)
    dq_ref[...] = dq
    put_sums(
        jnp.sum(dq.astype(jnp.float32), axis=0, keepdims=True),
        jnp.sum(dv.astype(jnp.float32), axis=0, keepdims=True),
    )


SCALARS = pl.BlockSpec(memory_space=pltpu.SMEM)


def neighbours():
    rep = lax.axis_index("rep")
    z = lax.axis_index("shard")
    core = rep % 2
    x = (rep // 2) % 2
    y = rep // 4
    other_core = (rep + 1 - 2 * core, z)
    other_x = (rep + 2 - 4 * x, z)
    other_y = (rep + 4 - 8 * y, z)
    others_z = [(rep, (z + d) % 4) for d in (1, 2, 3)]
    return core, x, y, z, other_core, other_x, other_y, others_z


def greet(devices):
    barrier = pltpu.get_barrier_semaphore()
    for device in devices:
        pl.semaphore_signal(barrier, inc=1, device_id=device, device_id_type=MESH)
    pl.semaphore_wait(barrier, len(devices))


def remote(src, dst, send, recv, device):
    return pltpu.make_async_remote_copy(
        src_ref=src, dst_ref=dst, send_sem=send, recv_sem=recv, device_id=device, device_id_type=MESH
    )


def gather_copies(refs, c, parity, places):
    piece, full, place_sem, z_send, z_recv, send, recv = refs
    core, x, y, z, other_core, other_x, other_y, others_z = places
    a = x + parity * (y - x)
    b = y + parity * (x - y)
    first = (other_x[0] + parity * (other_y[0] - other_x[0]), z)
    second = (other_y[0] + parity * (other_x[0] - other_y[0]), z)
    own = pl.ds(pl.multiple_of(core * 128 + a * 64 + b * 32, 32), 32)
    steps = (
        (own, second),
        (pl.ds(pl.multiple_of(core * 128 + a * 64, 64), 64), first),
        (pl.ds(pl.multiple_of(core * 128, 128), 128), other_core),
    )

    def local():
        return pltpu.make_async_copy(piece.at[c], full.at[c, z, own, :], place_sem.at[c])

    def line(d):
        return remote(
            piece.at[c], full.at[c, z, own, :], z_send.at[c, d], z_recv.at[c, d], others_z[d]
        )

    def pair(k):
        block = full.at[c, :, steps[k][0], :]
        return remote(block, block, send.at[k, c], recv.at[k, c], steps[k][1])

    return local, line, pair


def gather_stage(k, refs, c, parity, places):
    local, line, pair = gather_copies(refs, c, parity, places)
    if k == 0:
        local().start()
        for d in range(3):
            line(d).start()
    if k == 1:
        local().wait()
        for d in range(3):
            line(d).wait_recv()
        pair(0).start()
    if k == 2 or k == 3:
        pair(k - 2).wait_recv()
        pair(k - 1).start()
    if k == 4:
        pair(2).wait()
        pair(1).wait_send()
        pair(0).wait_send()
        for d in range(3):
            line(d).wait_send()


def gather_sems(count):
    dma = pltpu.SemaphoreType.DMA
    return [dma((count,)), dma((count, 3)), dma((count, 3)), dma((3, count)), dma((3, count))]


def hidden_blocks(values):
    split = values.reshape(values.shape[:-1] + (4, 4, 256))
    split = jnp.swapaxes(split, -3, -2)
    return split.reshape(values.shape[:-1] + (4, 1024))


def hidden_flat(blocks):
    split = blocks.reshape(blocks.shape[:-2] + (4, 4, 256))
    split = jnp.swapaxes(split, -3, -2)
    return split.reshape(blocks.shape[:-2] + (FF,))


def fold(tile):
    return jnp.sum(tile.reshape(-1, 8, tile.shape[-1]), axis=0)


GATHER_PLAN = (("z", 6.5), ("second", 6.5), ("first", 11.5), ("core", 3.0), (None, 0.0))


class GatherPlanner:
    def __init__(self, count):
        self.now = 0.0
        self.links = {"core": 0.0, "x": 0.0, "y": 0.0, "z": 0.0}
        self.stage = {c: 0 for c in range(count)}
        self.ready = {c: 0.0 for c in range(count)}
        self.opened = count

    def can(self, c):
        if self.stage[c] == 0 and c >= 3 and self.stage[c - 3] < 2:
            return False
        return self.stage[c] < 5

    def spend(self, now, **busy):
        self.now = max(self.now, now)
        for link, span in busy.items():
            self.links[link] = max(self.links[link], self.now) + span

    def emit(self, c):
        stage = self.stage[c]
        link, span = GATHER_PLAN[stage]
        first, second = ("x", "y") if c % 2 == 0 else ("y", "x")
        link = {"first": first, "second": second}.get(link, link)
        self.now = max(self.now, self.ready[c]) + 0.1
        if link is not None:
            begin = max(self.now, self.links[link])
            self.links[link] = begin + span - 1.0
            self.ready[c] = begin + span
        self.stage[c] = stage + 1
        return (stage, c)

    def tick(self, spent):
        self.now += spent
        events = []
        progress = True
        while progress:
            progress = False
            for c in range(self.opened):
                if self.can(c) and self.ready[c] <= self.now:
                    events.append(self.emit(c))
                    progress = True
        return events

    def until(self, c):
        events = []
        while self.stage[c] < 5:
            choices = [i for i in range(self.opened) if self.can(i)]
            best = min(choices, key=lambda i: (self.ready[i], i))
            events.append(self.emit(best))
        return events


ERFC_SERIES = (
    0.08459648489952087,
    0.085321806371212,
    0.0743890032172203,
    0.10671534389257431,
    -0.04577348381280899,
    0.27184805274009705,
    -0.2545455992221832,
    0.24207571148872375,
    -0.06462734192609787,
)


def gelu_parts(u):
    bell = jnp.exp(-0.5 * u * u)
    t = 1.0 / (1.0 + (0.3 * math.sqrt(0.5)) * jnp.abs(u))
    series = ERFC_SERIES[8]
    for coefficient in ERFC_SERIES[7::-1]:
        series = series * t + coefficient
    tail = series * t * bell
    share = jnp.where(u < 0.0, tail, 1.0 - tail)
    return u * share, share + u * (bell * (1.0 / math.sqrt(2.0 * math.pi)))


def norm_parts(values):
    centred = values - jnp.mean(values, axis=1, keepdims=True)
    spread = jnp.mean(centred * centred, axis=1, keepdims=True)
    scale = lax.rsqrt(spread + NORM_EPS)
    return centred * scale, scale


def forward_kernel(
    order_ref,
    lengths_ref,
    state_lengths_ref,
    tokens_ref,
    att_ref,
    exp_ref,
    shr_ref,
    e_ref,
    cot_ref,
    par,
    x_out,
    full_ref,
    q_out,
    k_out,
    v_out,
    o_out,
    lse_out,
    cq_out,
    ck_out,
    cv_out,
    oc_out,
    lse_cross_out,
    r1_out,
    r2_out,
    h1_out,
    h2_out,
    g_out,
    gp_out,
    y_out,
    dm_out,
    d_third_out,
    small_out,
    pool,
    acc,
    held,
    o_t,
    lse_held,
    states,
    x_held,
    spread,
    picked,
    piece_ref,
    att_in,
    exp_in,
    shr_in,
    prepare_sem,
    load_sem,
    store_sem,
    state_sem,
    acc_sem,
    spread_send,
    spread_recv,
    back_send,
    back_recv,
    *gather_sem,
):
    places = neighbours()
    refs = (piece_ref, full_ref) + gather_sem
    planner = GatherPlanner(GATHERED)
    me = lax.axis_index("rep") * 4 + places[3]
    length = lengths_ref[me]

    core, x, y = places[0:3]

    def own_row(parity):
        a = x + parity * (y - x)
        b = y + parity * (x - y)
        return core * 128 + a * 64 + b * 32

    prepare = []
    for p in range(2):
        for lane in range(8):
            rows = pl.ds(pl.multiple_of(own_row(p) * 8, 256), 256)
            prepare.append((att_ref.at[rows, pl.ds(lane * 128, 128)], att_in.at[p, lane]))
        rows = pl.ds(pl.multiple_of(own_row(p), 32), 32)
        prepare.append((exp_ref.at[rows, :], exp_in.at[p]))
    for j in range(4):
        rows = pl.ds(pl.multiple_of(j * 256 + own_row(SHRINK_AT[j] % 2), 32), 32)
        prepare.append((shr_ref.at[rows, :], shr_in.at[j]))
    prepare = [
        pltpu.make_async_copy(source, target, prepare_sem.at[i])
        for i, (source, target) in enumerate(prepare)
    ]

    def make_pieces():
        for copy in prepare:
            copy.wait()
        for c in range(8):
            for lane in range(8):
                tile = att_in[c % 2, lane, pl.ds(c, 32, stride=8), :]
                piece_ref[c, :, lane * 128 : lane * 128 + 128] = tile.astype(jnp.bfloat16)
        for j in range(4):
            c = EXPAND_AT[j]
            for s in range(4):
                start = s * 1024 + j * 256
                tile = exp_in[c % 2, :, start : start + 256]
                piece_ref[c, :, s * 256 : s * 256 + 256] = tile.astype(jnp.bfloat16)
            piece_ref[SHRINK_AT[j]] = shr_in[j].astype(jnp.bfloat16)

    def device(offset):
        j = lax.rem(me + offset, 32)
        return j, (j // 4, j % 4)

    def spread_copy(offset):
        j, target = device(offset)
        return remote(
            tokens_ref.at[j],
            spread.at[me],
            spread_send.at[offset],
            spread_recv.at[offset],
            target,
        )

    def back_copy(offset):
        return remote(
            picked.at[offset],
            x_held.at[me],
            back_send.at[offset],
            back_recv.at[offset],
            device(offset)[1],
        )

    def own_spread():
        return pltpu.make_async_copy(tokens_ref.at[me], spread.at[me], spread_recv.at[0])

    def own_back():
        return pltpu.make_async_copy(picked.at[0], x_held.at[me], back_recv.at[0])

    def each_other(act):
        def body(offset, carry):
            act(offset)
            return carry

        lax.fori_loop(1, 32, body, 0)

    def turn_back():
        own_spread().wait()
        each_other(lambda offset: spread_copy(offset).wait())
        picked[0] = spread[order_ref[me]]
        own_back().start()

        def pick(offset):
            picked[offset] = spread[order_ref[device(offset)[0]]]
            back_copy(offset).start()

        each_other(pick)

    def emit_all(events):
        for stage, c in events:
            gather_stage(stage, refs, c, c % 2, places)

    def tick(spent):
        emit_all(planner.tick(spent))

    def load(slot, source):
        return pltpu.make_async_copy(source, pool.at[slot], load_sem.at[slot])

    def store(slot, target):
        return pltpu.make_async_copy(pool.at[slot], target, store_sem.at[slot])

    def product_into(left, right, put):
        def body(i, carry):
            n = pl.multiple_of(i * 256, 256)
            put(n, product(left(), pool[right, :, pl.ds(n, 256)]))
            return carry

        lax.fori_loop(0, 4, body, 0)

    def row(index, n):
        return par[index : index + 1, pl.ds(n, 256)]

    def put_low(slot, offset=None, scale=None):
        def put(n, value):
            if offset is not None:
                value = value + row(offset, n)
            if scale is not None:
                value = value * scale
            pool[slot, :, pl.ds(n, 256)] = value.astype(jnp.bfloat16)

        return put

    def put_acc(offset):
        def put(n, value):
            acc[:, pl.ds(n, 256)] = value + row(offset, n)

        return put

    def load_weight(c, slot):
        target = pool.at[slot].reshape(4, 256, D)
        return pltpu.make_async_copy(full_ref.at[c], target, load_sem.at[slot])

    def weight(c, slot):
        emit_all(planner.until(c))
        return load_weight(c, slot)

    def attend_loop(causal, step, valid, query, key, value, out, spent, rows, key_rows):
        ahead = [planner.tick(spent) for _ in range(8)]
        first_row, count = rows

        def body(i, carry):
            lanes = pl.ds(pl.multiple_of(i * 128, 128), 128)
            attend_pair(
                causal,
                step,
                valid,
                query.at[pl.ds(first_row, count), lanes],
                key.at[pl.ds(0, key_rows), lanes],
                value.at[pl.ds(0, key_rows), lanes],
                out.at[pl.ds(first_row, count), lanes],
                lse_held.at[pl.ds(i, 1)],
                o_t,
                first_row,
            )
            for n in range(8):
                if ahead[n]:

                    @pl.when(i == n)
                    def _(events=ahead[n]):
                        emit_all(events)

            return carry

        lax.fori_loop(0, 8, body, 0)

    TILE = 128

    def over_rows(sums, body):
        zero = jnp.zeros((8, D), jnp.float32)

        def step(i, carry):
            r = pl.multiple_of(i * TILE, TILE)
            place = half_lanes((TILE, 1), 0) + r
            usable = (place < length).astype(jnp.float32)
            terms = body(pl.ds(r, TILE), usable)
            return tuple(c + fold(t) for c, t in zip(carry, terms))

        totals = lax.fori_loop(0, D // TILE, step, (zero,) * sums)
        return [jnp.sum(t, axis=0, keepdims=True) for t in totals]

    lane = half_lanes((1, D), 1)

    def square_at(index, total):
        small_out[17:18, :] += jnp.where(lane == index, jnp.sum(total), 0.0)

    for copy in prepare:
        copy.start()
    barrier = pltpu.get_barrier_semaphore()

    def greet_one(offset):
        pl.semaphore_signal(barrier, inc=1, device_id=device(offset)[1], device_id_type=MESH)

    each_other(greet_one)
    pl.semaphore_wait(barrier, 31)
    own_spread().start()
    each_other(lambda offset: spread_copy(offset).start())
    make_pieces()
    planner.opened = 3
    tick(0.5)
    planner.spend(3.0, z=42.0, x=21.0, y=21.0)
    e_load = pltpu.make_async_copy(e_ref, states.at[2], state_sem.at[2])
    e_load.start()
    load(9, cot_ref).start()
    small_out[...] = jnp.zeros_like(small_out)
    for _ in range(4):
        tick(12.0)
    turn_back()
    planner.spend(58.0, z=42.0, x=21.0, y=21.0)
    for _ in range(3):
        tick(10.0)
    for i in range(3):
        weight(i, 1 + i).start()
    own_back().wait()
    each_other(lambda offset: back_copy(offset).wait())
    planner.spend(112.0)
    planner.opened = GATHERED
    tick(0.5)
    x_store = pltpu.make_async_copy(x_held, x_out, acc_sem.at[1])
    x_store.start()

    for i, (slot, offset, scale) in enumerate(((4, 0, 0.125), (5, None, None), (6, 1, None))):
        load_weight(i, 1 + i).wait()
        product_into(lambda: x_held[...].reshape(1024, D), 1 + i, put_low(slot, offset, scale))
        store(slot, (q_out, k_out, v_out)[i]).start()
        tick(2.5)
    refs_held = [pool.at[slot] for slot in (4, 5, 6, 7)]
    attend_loop(True, 256, length, *refs_held, 4.5, (0, 1024), 1024)
    store(7, o_out).start()
    lse_copy = pltpu.make_async_copy(lse_held, lse_out, state_sem.at[3])
    lse_copy.start()
    w_copy = weight(3, 1)
    w_copy.start()
    w_copy.wait()
    product_into(lambda: pool[7], 1, put_acc(2))
    tick(2.5)
    store(4, q_out).wait()

    def first_norm(rows, usable):
        held_rows = pl.ds(pl.multiple_of(rows.start // 32, TILE // 32), TILE // 32)
        x = x_held[held_rows].reshape(TILE, D).astype(jnp.float32)
        a = acc[rows, :]
        total = x + a
        acc[rows, :] = total
        h = norm_parts(total)[0] * par[11:12, :] + par[12:13, :]
        held[rows, :] = h
        pool[4, rows, :] = h.astype(jnp.bfloat16)
        return usable * x * x, usable * a * a, usable * h * h

    for index, total in enumerate(over_rows(3, first_norm)):
        square_at(index, total)
    store(4, h1_out).start()
    r1_copy = pltpu.make_async_copy(acc, r1_out, acc_sem.at[0])
    r1_copy.start()
    tick(4.0)

    for c, slot in ((4, 2), (5, 3), (6, 1)):
        weight(c, slot).start()
    store(5, k_out).wait()
    load_weight(4, 2).wait()
    product_into(lambda: pool[4], 2, put_low(5, 3, 0.125))
    store(5, cq_out).start()
    w_copy = weight(7, 2)
    w_copy.start()
    tick(2.5)
    e_load.wait()
    load_weight(5, 3).wait()
    load_weight(6, 1).wait()

    def put_keys(n, value):
        states[0, :, pl.ds(n, 256)] = value.astype(jnp.bfloat16)

    def put_values(n, value):
        states[1, :, pl.ds(n, 256)] = (value + row(4, n)).astype(jnp.bfloat16)

    product_into(lambda: states[2], 3, put_keys)
    product_into(lambda: states[2], 1, put_values)
    state_stores = [
        pltpu.make_async_copy(states.at[0], ck_out, state_sem.at[0]),
        pltpu.make_async_copy(states.at[1], cv_out, state_sem.at[1]),
    ]
    for copy in state_stores:
        copy.start()
    tick(1.0)
    store(6, v_out).wait()
    lse_copy.wait()
    attend_loop(
        False,
        512,
        state_lengths_ref[me],
        pool.at[5],
        states.at[0],
        states.at[1],
        pool.at[6],
        1.6,
        (0, 1024),
        128,
    )
    store(6, oc_out).start()
    lse_copy = pltpu.make_async_copy(lse_held, lse_cross_out, state_sem.at[3])
    lse_copy.start()
    w_copy.wait()
    r1_copy.wait()
    product_into(lambda: pool[6], 2, put_acc(5))
    tick(2.5)
    weight(EXPAND_AT[0], 0).start()
    weight(SHRINK_AT[0], 2).start()
    store(7, o_out).wait()

    def second_norm(rows, usable):
        c = acc[rows, :]
        total = held[rows, :] + c
        acc[rows, :] = total
        h = norm_parts(total)[0] * par[13:14, :] + par[14:15, :]
        held[rows, :] = h
        pool[7, rows, :] = h.astype(jnp.bfloat16)
        return usable * c * c, usable * h * h

    for index, total in enumerate(over_rows(2, second_norm)):
        square_at(3 + index, total)
    store(7, h2_out).start()
    r2_copy = pltpu.make_async_copy(acc, r2_out, acc_sem.at[0])
    r2_copy.start()
    tick(4.0)

    store(4, h1_out).wait()
    store(5, cq_out).wait()
    g_slots, slope_slots = (4, 6), (5, 8)
    r2_copy.wait()
    store(6, oc_out).wait()
    for j in range(5):
        if j > 1:
            store(g_slots[j % 2], g_out.at[j - 2]).wait()
            store(slope_slots[j % 2], gp_out.at[j - 2]).wait()
        if j < 4:
            load_weight(EXPAND_AT[j], j % 2).wait()
        if j > 0:
            load_weight(SHRINK_AT[j - 1], 2 + (j - 1) % 2).wait()

        def body(i, carry, j=j):
            n = pl.multiple_of(i * 256, 256)
            here = pl.ds(n, 256)
            if j < 4:
                offset = par[pl.ds(6 + i, 1), j * 256 : j * 256 + 256]
                u = product(pool[7], pool[j % 2, :, here]) + offset
            if j > 0:
                more = product(pool[g_slots[(j - 1) % 2]], pool[2 + (j - 1) % 2, :, here])
                if j == 1:
                    acc[:, here] = more + row(10, n)
                else:
                    acc[:, here] += more
            if j < 4:
                g, slope = gelu_parts(u)
                pool[g_slots[j % 2], :, here] = g.astype(jnp.bfloat16)
                pool[slope_slots[j % 2], :, here] = slope.astype(jnp.bfloat16)
            return carry

        lax.fori_loop(0, 4, body, 0)
        if j < 4:
            store(g_slots[j % 2], g_out.at[j]).start()
            store(slope_slots[j % 2], gp_out.at[j]).start()
        tick(9.0 if j < 4 else 2.5)
        if j < 3:
            weight(EXPAND_AT[j + 1], (j + 1) % 2).start()
            weight(SHRINK_AT[j + 1], 2 + (j + 1) % 2).start()

    load(9, cot_ref).wait()

    def third_norm(rows, usable):
        m = acc[rows, :]
        unit, scale = norm_parts(held[rows, :] + m)
        gain = par[15:16, :]
        pool[0, rows, :] = (unit * gain + par[16:17, :]).astype(jnp.bfloat16)
        grad = pool[9, rows, :].astype(jnp.float32) * usable
        inner = grad * gain
        first = jnp.mean(inner, axis=1, keepdims=True)
        second = jnp.mean(inner * unit, axis=1, keepdims=True)
        back = scale * (inner - first - unit * second)
        acc[rows, :] = back
        low = back.astype(jnp.bfloat16)
        pool[1, rows, :] = low
        return usable * m * m, grad * unit, grad, low.astype(jnp.float32)

    m_total, gain_sum, shift_sum, offset_sum = over_rows(4, third_norm)
    square_at(5, m_total)
    small_out[15:16, :] = gain_sum
    small_out[16:17, :] = shift_sum
    small_out[10:11, :] = offset_sum
    last = [
        store(0, y_out),
        store(1, dm_out),
        pltpu.make_async_copy(acc, d_third_out, acc_sem.at[0]),
    ]
    for copy in last:
        copy.start()
    for c in range(GATHERED):
        emit_all(planner.until(c))
    for copy in last + state_stores + [lse_copy, x_store]:
        copy.wait()
    store(7, h2_out).wait()
    store(6, g_out.at[3]).wait()
    store(8, gp_out.at[3]).wait()


def forward(scalars, tokens, weights, states, cotangent, params):
    any_space = pl.BlockSpec(memory_space=pl.ANY)
    vmem = pl.BlockSpec(memory_space=pltpu.VMEM)
    shape = jax.ShapeDtypeStruct
    dma = pltpu.SemaphoreType.DMA
    low = jnp.bfloat16
    wide = jnp.float32
    square = shape((1024, D), low)
    square_wide = shape((1024, D), wide)
    lse = shape((8, 8, 1024), wide)
    short = shape((128, D), low)
    blocks = shape((4, 1024, D), low)
    outs = (
        shape((32, 32, D), low),
        shape((GATHERED, 4, 256, D), low),
        square,
        square,
        square,
        square,
        lse,
        square,
        short,
        short,
        square,
        lse,
        square_wide,
        square_wide,
        square,
        square,
        blocks,
        blocks,
        square,
        square,
        square_wide,
        shape((24, D), wide),
    )
    return pl.pallas_call(
        forward_kernel,
        out_shape=outs,
        in_specs=[SCALARS] * 3 + [any_space] * 6 + [vmem],
        out_specs=(any_space,) * 21 + (vmem,),
        scratch_shapes=[
            pltpu.VMEM((10, 1024, D), low),
            pltpu.VMEM((1024, D), wide),
            pltpu.VMEM((1024, D), wide),
            pltpu.VMEM((128, 1024), wide),
            pltpu.VMEM((8, 8, 1024), wide),
            pltpu.VMEM((3, 128, D), low),
            pltpu.VMEM((32, 32, D), low),
            pltpu.VMEM((32, 32, D), low),
            pltpu.VMEM((32, 32, D), low),
            pltpu.VMEM((GATHERED, 32, D), low),
            pltpu.VMEM((2, 8, 256, 128), wide),
            pltpu.VMEM((2, 32, FF), wide),
            pltpu.VMEM((4, 32, D), wide),
            dma((22,)),
            dma((10,)),
            dma((10,)),
            dma((4,)),
            dma((2,)),
            dma((32,)),
            dma((32,)),
            dma((32,)),
            dma((32,)),
        ]
        + gather_sems(GATHERED),
        compiler_params=pltpu.CompilerParams(
            collective_id=3, has_side_effects=True, vmem_limit_bytes=62 * MIB
        ),
    )(*scalars, tokens.reshape(32, 32, D), *weights, states, cotangent, params)


def add_blocks(target, first, second, planes, rows, step):
    per_plane = rows // step

    def body(i, carry):
        s = i // per_plane
        r = pl.multiple_of((i % per_plane) * step, step)
        target(s, r, first(s, r) + second(s, r))
        return carry

    lax.fori_loop(0, planes * per_plane, body, 0)


POOL = 8
G_SLOTS = 3
R_SLOTS = 4
PLAN = {"core": 3.0, "load": 1.5, "a": 11.5, "b": 6.5, "z": 6.5, "bb": 2.5, "ba": 4.0, "bc": 2.0}


class Planner:
    def __init__(self):
        self.now = 0.0
        self.links = {"core": 0.0, "x": 0.0, "y": 0.0, "z": 0.0, "load": 0.0}
        self.stage = {}
        self.ready = {}

    def link_of(self, c, stage):
        first, second = ("x", "y") if c % 2 == 0 else ("y", "x")
        return {
            0: ("core", "core"),
            1: ("load", "load"),
            2: (first, "a"),
            3: (second, "b"),
            4: ("z", "z"),
            5: (second, "bb"),
            6: (first, "ba"),
            7: ("core", "bc"),
            8: (None, None),
        }[stage]

    def can(self, c):
        stage = self.stage[c]
        if stage > 8:
            return False
        if stage == 1 and c >= R_SLOTS and self.stage[c - R_SLOTS] <= 3:
            return False
        return True

    def emit(self, c):
        stage = self.stage[c]
        link, kind = self.link_of(c, stage)
        self.now = max(self.now, self.ready[c]) + {2: 0.8, 3: 0.5, 4: 0.3, 5: 0.2}.get(stage, 0.1)
        if link is not None:
            begin = max(self.now, self.links[link])
            span = PLAN[kind]
            self.links[link] = begin + span - 1.0
            self.ready[c] = begin + span
        self.stage[c] = stage + 1
        return (stage, c)

    def tick(self, spent):
        self.now += spent
        events = []
        progress = True
        while progress:
            progress = False
            for c in sorted(self.stage):
                if self.can(c) and self.ready[c] <= self.now:
                    events.append(self.emit(c))
                    progress = True
        return events

    def produce(self, c):
        self.stage[c] = 0
        self.ready[c] = self.now
        return [self.emit(c)]

    def until(self, done):
        events = []
        while not done():
            choices = [c for c in sorted(self.stage) if self.can(c)]
            c = min(choices, key=lambda i: (self.ready[i], i))
            events.append(self.emit(c))
        return events

    def free_slot(self, c):
        before = c - G_SLOTS
        if before < 0:
            return []
        return self.until(lambda: self.stage[before] > 2)

    def drain(self, tasks, spent):
        events = []
        waiting = list(tasks)
        while waiting or any(s <= 8 for s in self.stage.values()):
            choices = [c for c in sorted(self.stage) if self.can(c)]
            best = min(choices, key=lambda i: (self.ready[i], i)) if choices else None
            open_tasks = [t for t in waiting if all(self.stage[c] > 8 for c in t[0])]
            if open_tasks and (best is None or self.ready[best] > self.now):
                task = open_tasks[0]
                waiting.remove(task)
                self.now += spent
                events.append(("task", task[1]))
            else:
                events.append(self.emit(best))
        return events


def backward_kernel(
    lengths_ref,
    state_lengths_ref,
    dm_ref,
    d_third_ref,
    g_ref,
    gp_ref,
    full_ref,
    h2_ref,
    h1_ref,
    x_in_ref,
    e_ref,
    oc_ref,
    o_ref,
    r1_ref,
    r2_ref,
    q_ref,
    k_ref,
    v_ref,
    cq_ref,
    ck_ref,
    cv_ref,
    lse_ref,
    lse_cross_ref,
    gains_ref,
    small_ref,
    rows_ref,
    cols_ref,
    token_grad_ref,
    state_grad_ref,
    out_ref,
    totals_ref,
    rows_out,
    cols_out,
    scale_out,
    half,
    pool,
    acc,
    made,
    summed,
    quarter,
    eighth,
    pieces,
    stream,
    dq_t,
    dk_sum,
    dv_sum,
    lse_held,
    states,
    states_t,
    small,
    small_in,
    small_sum,
    small_z,
    part,
    whole,
    load_sem,
    stream_sem,
    state_sem,
    half_sem,
    scan_sem,
    line_send_sem,
    line_recv_sem,
    send_sem,
    recv_sem,
    z_send_sem,
    z_recv_sem,
    place_sem,
    small_send_sem,
    small_recv_sem,
):
    core, x, y, z, other_core, other_x, other_y, others_z = neighbours()
    me = lax.axis_index("rep") * 4 + z
    kept = pl.multiple_of(core * 128, 128)
    given = pl.multiple_of(128 - core * 128, 128)
    planner = Planner()
    place_of = (12, 8, 13, 9, 14, 10, 15, 11, 7, 4, 5, 6, 3, 0, 1, 2)

    def axes(c):
        if c % 2 == 0:
            return x, y, other_x, other_y
        return y, x, other_y, other_x

    def core_copy(c):
        source = made.at[c % G_SLOTS, :, pl.ds(given, 128), :]
        return remote(source, half.at[c], send_sem.at[0, c], recv_sem.at[0, c], other_core)

    def half_copy(c):
        return pltpu.make_async_copy(
            half.at[c], summed.at[c % R_SLOTS], half_sem.at[c % R_SLOTS]
        )

    def first_copy(c):
        a, b, first, second = axes(c)
        rows = pl.ds(pl.multiple_of(64 - a * 64, 64), 64)
        source = summed.at[c % R_SLOTS, :, rows, :]
        return remote(source, quarter.at[c], send_sem.at[1, c], recv_sem.at[1, c], first)

    def second_copy(c):
        a, b, first, second = axes(c)
        rows = pl.ds(pl.multiple_of(32 - b * 32, 32), 32)
        source = quarter.at[c, :, rows, :]
        return remote(source, eighth.at[c], send_sem.at[2, c], recv_sem.at[2, c], second)

    def z_copy(c, d):
        device = others_z[d]
        return remote(
            eighth.at[c, device[1]],
            pieces.at[c, d],
            z_send_sem.at[c, d],
            z_recv_sem.at[c, d],
            device,
        )

    def own_rows_of(c):
        a, b, first, second = axes(c)
        return pl.ds(pl.multiple_of(core * 128 + a * 64 + b * 32, 32), 32)

    def place_copy(c):
        return pltpu.make_async_copy(
            pieces.at[c, 0], out_ref.at[place_of[c], own_rows_of(c), :], place_sem.at[c]
        )

    def back_second(c):
        device = axes(c)[3]
        target = out_ref.at[place_of[c], own_rows_of(c), :]
        return remote(pieces.at[c, 0], target, send_sem.at[3, c], recv_sem.at[3, c], device)

    def back_first(c):
        a, b, first, second = axes(c)
        block = out_ref.at[place_of[c], pl.ds(pl.multiple_of(core * 128 + a * 64, 64), 64), :]
        return remote(block, block, send_sem.at[4, c], recv_sem.at[4, c], first)

    def back_core(c):
        block = out_ref.at[place_of[c], pl.ds(kept, 128), :]
        return remote(block, block, send_sem.at[5, c], recv_sem.at[5, c], other_core)

    def emit(stage, c):
        a, b, first, second = axes(c)
        slot = c % R_SLOTS
        if stage == 0:
            core_copy(c).start()
        if stage == 1:
            if c >= R_SLOTS:
                first_copy(c - R_SLOTS).wait_send()
            core_copy(c).wait_recv()
            half_copy(c).start()
        if stage == 2:
            half_copy(c).wait()

            def put(s, r, value):
                summed[slot, s, pl.ds(r, 32), :] = value

            add_blocks(
                put,
                lambda s, r: summed[slot, s, pl.ds(r, 32), :],
                lambda s, r: made[c % G_SLOTS, s, pl.ds(pl.multiple_of(kept + r, 32), 32), :],
                4,
                128,
                32,
            )
            first_copy(c).start()
            core_copy(c).wait_send()
        if stage == 3:
            first_copy(c).wait_recv()

            def put(s, r, value):
                quarter[c, s, pl.ds(r, 32), :] = value

            add_blocks(
                put,
                lambda s, r: quarter[c, s, pl.ds(r, 32), :],
                lambda s, r: summed[slot, s, pl.ds(pl.multiple_of(a * 64 + r, 32), 32), :],
                4,
                64,
                32,
            )
            second_copy(c).start()
        if stage == 4:
            second_copy(c).wait_recv()

            def put(s, r, value):
                eighth[c, s, pl.ds(r, 32), :] = value

            add_blocks(
                put,
                lambda s, r: eighth[c, s, pl.ds(r, 32), :],
                lambda s, r: quarter[c, s, pl.ds(pl.multiple_of(b * 32 + r, 32), 32), :],
                4,
                32,
                32,
            )
            for d in range(3):
                z_copy(c, d).start()
        if stage == 5:
            for d in range(3):
                z_copy(c, d).wait_recv()
            total = eighth[c, z].astype(jnp.float32)
            for d in range(3):
                total = total + pieces[c, d].astype(jnp.float32)
            pieces[c, 0] = total.astype(jnp.bfloat16)
            back_second(c).start()
            place_copy(c).start()
        if stage == 6:
            place_copy(c).wait()
            back_second(c).wait_recv()
            back_first(c).start()
        if stage == 7:
            back_first(c).wait_recv()
            back_core(c).start()
        if stage == 8:
            back_core(c).wait()
            back_first(c).wait_send()
            back_second(c).wait_send()
            for d in range(3):
                z_copy(c, d).wait_send()
            second_copy(c).wait_send()
            if c >= CHUNKS - R_SLOTS:
                first_copy(c).wait_send()

    def emit_all(events):
        for stage, c in events:
            emit(stage, c)

    def tick(spent):
        emit_all(planner.tick(spent))

    def produced(c, spent):
        planner.now += spent
        emit_all(planner.produce(c))
        emit_all(planner.tick(0.0))

    def load(slot, source):
        return pltpu.make_async_copy(source, pool.at[slot], load_sem.at[slot])

    def state_load(index, source):
        return pltpu.make_async_copy(source, states.at[index], state_sem.at[index])

    def turn_tile(target, source):
        def turn(n):
            pool[target, pl.ds(n, 256), :] = pool[source, :, pl.ds(n, 256)].T

        return turn

    def transpose_into(target, source):
        turn = turn_tile(target, source)

        def body(i, carry):
            turn(pl.multiple_of(i * 256, 256))
            return carry

        lax.fori_loop(0, 4, body, 0)

    def product_nn(left, right, put, beside=None):
        def body(i, carry):
            n = pl.multiple_of(i * 256, 256)
            if beside is not None:
                beside(n)
            put(n, product(left(), right(n)))
            return carry

        lax.fori_loop(0, 4, body, 0)

    def product_nt(left, right, put, beside=None):
        def body(i, carry):
            n = pl.multiple_of(i * 256, 256)
            if beside is not None:
                beside(n)
            put(
                n,
                lax.dot_general(
                    left(),
                    right(n),
                    (((1,), (1,)), ((), ())),
                    preferred_element_type=jnp.float32,
                ),
            )
            return carry

        lax.fori_loop(0, 4, body, 0)

    def columns_of(slot):
        return lambda n: pool[slot, :, pl.ds(n, 256)]

    def rows_of(slot):
        return lambda n: pool[slot, pl.ds(n, 256), :]

    def weight_grad(slot_in_made, left, right, beside=None):
        def put(n, value):
            low = value.astype(jnp.bfloat16).reshape(4, 256, 256)
            made[slot_in_made, :, :, pl.ds(n, 256)] = low

        product_nn(left, right, put, beside)

    def add_to_acc(n, value):
        acc[:, pl.ds(n, 256)] += value

    def put_in(slot):
        def put(n, value):
            pool[slot, :, pl.ds(n, 256)] = value.astype(jnp.bfloat16)

        return put

    def norm_back(source, gain_row, gain_at, shift_at, offset_at, target):
        tiles = 8
        rows = 1024 // tiles

        def fetch(i):
            place = pl.ds(pl.multiple_of(i * rows, rows), rows)
            return pltpu.make_async_copy(
                source.at[place, :], stream.at[i % 2], stream_sem.at[i % 2]
            )

        fetch(0).start()

        def body(i, carry):
            gain_sum, shift_sum, offset_sum = carry

            @pl.when(i + 1 < tiles)
            def _():
                fetch(i + 1).start()

            fetch(i).wait()
            r = pl.multiple_of(i * rows, rows)
            values = stream[i % 2]
            centred = values - jnp.mean(values, axis=1, keepdims=True)
            spread = jnp.mean(centred * centred, axis=1, keepdims=True)
            scale = lax.rsqrt(spread + NORM_EPS)
            unit = centred * scale
            grad = acc[pl.ds(r, rows), :]
            inner = grad * gains_ref[gain_row : gain_row + 1, :]
            first = jnp.mean(inner, axis=1, keepdims=True)
            second = jnp.mean(inner * unit, axis=1, keepdims=True)
            back = scale * (inner - first - unit * second)
            acc[pl.ds(r, rows), :] = back
            low = back.astype(jnp.bfloat16)
            pool[target, pl.ds(r, rows), :] = low
            return (
                gain_sum + fold(grad * unit),
                shift_sum + fold(grad),
                offset_sum + fold(low.astype(jnp.float32)),
            )

        zero = jnp.zeros((8, D), jnp.float32)
        sums = lax.fori_loop(0, tiles, body, (zero, zero, zero))
        for row, value in zip((gain_at, shift_at, offset_at), sums):
            small[row : row + 1, :] = jnp.sum(value, axis=0, keepdims=True)

    greet([other_core, other_x, other_y] + others_z)
    load(0, dm_ref).start()
    load(6, h2_ref).start()
    load(2, full_ref.at[SHRINK_AT[0]]).start()
    load(3, gp_ref.at[0]).start()
    load(4, g_ref.at[0]).start()
    load(5, full_ref.at[EXPAND_AT[0]]).start()
    acc_load = pltpu.make_async_copy(d_third_ref, acc, place_sem.at[0])
    acc_load.start()
    small[...] = small_ref[...]
    load(6, h2_ref).wait()
    transpose_into(1, 6)
    load(0, dm_ref).wait()
    acc_load.wait()

    planner.now = 4.0
    plan = []
    for j in range(4):
        entry = []
        planner.now += 3.5
        entry.append(planner.tick(0.0) + planner.free_slot(2 * j))
        planner.now += 2.5
        entry.append(planner.produce(2 * j) + planner.tick(0.0) + planner.free_slot(2 * j + 1))
        planner.now += 2.5
        entry.append(planner.produce(2 * j + 1) + planner.tick(0.0))
        entry.append(planner.tick(2.5))
        plan.append(entry)

    def emit_planned(j, place):
        for n in range(4):
            events = plan[n][place]
            if events:

                @pl.when(j == n)
                def _(events=events):
                    emit_all(events)

    def block(j, carry):
        last = j == 3
        load(2, full_ref.at[SHRINK_AT[0]]).wait()
        load(3, gp_ref.at[0]).wait()

        def put_pre(n, value):
            low = (value * pool[3, :, pl.ds(n, 256)].astype(jnp.float32)).astype(jnp.bfloat16)
            pool[7, :, pl.ds(n, 256)] = low
            small[pl.ds(6 + n // 256, 1), pl.ds(pl.multiple_of(j * 256, 256), 256)] = jnp.sum(
                low.astype(jnp.float32), axis=0, keepdims=True
            )

        load(4, g_ref.at[0]).wait()
        product_nt(lambda: pool[0], rows_of(2), put_pre, turn_tile(6, 4))

        @pl.when(jnp.logical_not(last))
        def _():
            load(2, full_ref.at[SHRINK_AT[0] + 2 * (j + 1) - (j + 1) // 3]).start()
            load(3, gp_ref.at[j + 1]).start()

        @pl.when(last)
        def _():
            load(2, full_ref.at[7]).start()
            load(3, cq_ref).start()

        emit_planned(j, 0)

        @pl.when(jnp.logical_not(last))
        def _():
            load(4, g_ref.at[j + 1]).start()

        @pl.when(last)
        def _():
            load(4, oc_ref).start()

        weight_grad((2 * j) % G_SLOTS, lambda: pool[6], columns_of(0))
        emit_planned(j, 1)
        weight_grad((2 * j + 1) % G_SLOTS, lambda: pool[1], columns_of(7))
        emit_planned(j, 2)
        load(5, full_ref.at[EXPAND_AT[0]]).wait()
        product_nt(lambda: pool[7], rows_of(5), add_to_acc)

        @pl.when(jnp.logical_not(last))
        def _():
            load(5, full_ref.at[EXPAND_AT[1] + 2 * j]).start()

        @pl.when(last)
        def _():
            load(5, full_ref.at[4]).start()

        emit_planned(j, 3)
        return carry

    lax.fori_loop(0, 4, block, 0)

    load(7, h1_ref).start()
    state_loads = [state_load(0, ck_ref), state_load(1, cv_ref), state_load(2, e_ref)]
    for copy in state_loads:
        copy.start()
    lse_load = pltpu.make_async_copy(lse_cross_ref, lse_held, state_sem.at[3])
    lse_load.start()
    norm_back(r2_ref, 13, 13, 14, 5, 0)
    tick(4.0)
    load(4, oc_ref).wait()
    load(2, full_ref.at[7]).wait()
    product_nt(lambda: pool[0], rows_of(2), put_in(4), turn_tile(6, 4))
    load(2, full_ref.at[3]).start()
    tick(2.5)
    emit_all(planner.free_slot(8))
    load(7, h1_ref).wait()
    weight_grad(8 % G_SLOTS, lambda: pool[6], columns_of(0), turn_tile(1, 7))
    load(6, o_ref).start()
    load(7, full_ref.at[5]).start()
    produced(8, 2.5)
    load(3, cq_ref).wait()
    for copy in state_loads:
        copy.wait()
    lse_load.wait()

    def attend_loop(causal, step, length, query, key, value, grad, rows, spent, span=(0, 8)):
        ahead = {n: planner.tick(spent) for n in range(*span)}

        def body(i, carry):
            lanes = pl.ds(pl.multiple_of(i * 128, 128), 128)

            def sums(dq, dv):
                small[rows[0] : rows[0] + 1, lanes] = dq
                small[rows[1] : rows[1] + 1, lanes] = dv

            attend_back_pair(
                causal,
                step,
                length,
                query.at[:, lanes],
                key.at[:, lanes],
                value.at[:, lanes],
                grad.at[:, lanes],
                lse_held.at[pl.ds(i, 1)],
                query.at[:, lanes],
                key.at[:, lanes],
                value.at[:, lanes],
                sums,
                dq_t,
                dk_sum,
                dv_sum,
            )
            for n in range(*span):
                if ahead[n]:

                    @pl.when(i == n)
                    def _(events=ahead[n]):
                        emit_all(events)

            return carry

        lax.fori_loop(*span, body, 0)

    attend_loop(
        False,
        512,
        state_lengths_ref[me],
        pool.at[3],
        states.at[0],
        states.at[1],
        pool.at[4],
        (3, 4),
        2.0,
    )
    lse_load = pltpu.make_async_copy(lse_ref, lse_held, state_sem.at[3])
    lse_load.start()
    emit_all(planner.free_slot(9))
    weight_grad(9 % G_SLOTS, lambda: pool[1], columns_of(3))
    produced(9, 2.5)
    load(5, full_ref.at[4]).wait()
    load(6, o_ref).wait()
    product_nt(lambda: pool[3], rows_of(5), add_to_acc, turn_tile(1, 6))
    load(6, x_in_ref).start()
    load(5, full_ref.at[6]).start()
    load(3, q_ref).start()
    tick(2.5)
    states_t[...] = states[2].T
    for c, index in ((10, 0), (11, 1)):
        emit_all(planner.free_slot(c))
        weight_grad(
            c % G_SLOTS, lambda: states_t[...], lambda n, i=index: states[i, :, pl.ds(n, 256)]
        )
        produced(c, 1.0)
    load(7, full_ref.at[5]).wait()
    load(5, full_ref.at[6]).wait()

    def state_part(n):
        dims = (((1,), (1,)), ((), ()))
        return lax.dot_general(
            states[0], pool[7, pl.ds(n, 256), :], dims, preferred_element_type=jnp.float32
        ) + lax.dot_general(
            states[1], pool[5, pl.ds(n, 256), :], dims, preferred_element_type=jnp.float32
        )

    def put_state(i, carry):
        n = pl.multiple_of(i * 256, 256)
        state_grad_ref[:, pl.ds(n, 256)] = state_part(n).astype(jnp.bfloat16)
        return carry

    lax.fori_loop(0, 4, put_state, 0)
    load(5, k_ref).start()
    load(7, v_ref).start()
    tick(1.0)

    norm_back(r1_ref, 11, 11, 12, 2, 0)
    tick(4.0)
    emit_all(planner.free_slot(12))
    weight_grad(12 % G_SLOTS, lambda: pool[1], columns_of(0))
    produced(12, 2.5)
    load(2, full_ref.at[3]).wait()
    load(6, x_in_ref).wait()
    product_nt(lambda: pool[0], rows_of(2), put_in(4), turn_tile(1, 6))
    load(0, full_ref.at[0]).start()
    load(2, full_ref.at[1]).start()
    load(6, full_ref.at[2]).start()
    tick(2.5)
    load(3, q_ref).wait()
    load(5, k_ref).wait()
    load(7, v_ref).wait()
    lse_load.wait()
    def self_heads(span):
        refs = [pool.at[slot] for slot in (3, 5, 7, 4)]
        attend_loop(True, 256, lengths_ref[me], *refs, (0, 1), 5.0, span)

    def query_key_grad(c, half_of):
        def put(i, carry):
            n = pl.multiple_of((i % 2) * 256 + 512 * half_of, 256)
            value = product(pool[1], pool[3 + 2 * (i // 2), :, pl.ds(n, 256)])
            low = value.astype(jnp.bfloat16).reshape(4, 256, 256)
            made[c % G_SLOTS, :, :, pl.ds(pl.multiple_of(i * 256, 256), 256)] = low
            return carry

        emit_all(planner.free_slot(c))
        lax.fori_loop(0, 4, put, 0)
        produced(c, 2.5)

    self_heads((0, 4))
    query_key_grad(13, 0)
    self_heads((4, 8))

    def small_copy(k):
        source = small if k == 0 else small_sum.at[k - 1]
        device = (other_core, other_x, other_y)[k]
        return remote(source, small_in.at[k], small_send_sem.at[k], small_recv_sem.at[k], device)

    def small_z_copy(d):
        return remote(
            small_sum.at[2],
            small_z.at[z],
            small_send_sem.at[3 + d],
            small_recv_sem.at[3 + d],
            others_z[d],
        )

    def small_step(k):
        small_copy(k).wait()
        before = small[...] if k == 0 else small_sum[k - 1]
        small_sum[k] = before + small_in[k]
        if k < 2:
            small_copy(k + 1).start()
        else:
            small_z[z] = small_sum[2]
            for d in range(3):
                small_z_copy(d).start()

    small_copy(0).start()
    emit_all(planner.free_slot(14))
    weight_grad(14 % G_SLOTS, lambda: pool[1], columns_of(7))
    produced(14, 2.5)
    small_step(0)
    query_key_grad(15, 1)
    small_step(1)
    load(0, full_ref.at[0]).wait()
    product_nt(lambda: pool[3], rows_of(0), add_to_acc)
    tick(2.5)
    small_step(2)
    load(2, full_ref.at[1]).wait()
    product_nt(lambda: pool[5], rows_of(2), add_to_acc)
    tick(2.5)
    for d in range(3):
        small_z_copy(d).wait()
    totals_ref[...] = (small_z[0] + small_z[1]) + (small_z[2] + small_z[3])
    load(6, full_ref.at[2]).wait()

    def put_input(n, value):
        total = acc[:, pl.ds(n, 256)] + value
        pool[4, :, pl.ds(n, 256)] = total.astype(jnp.bfloat16)

    product_nt(lambda: pool[7], rows_of(6), put_input)
    token_copy = pltpu.make_async_copy(pool.at[4], token_grad_ref, load_sem.at[4])
    token_copy.start()
    tick(2.5)

    part[...] = jnp.zeros_like(part)

    def spot(place):
        return (0, 1, 2, 6)[place // 4], (place % 4) * 256

    def scan_load(place):
        slot, row = spot(place)
        return pltpu.make_async_copy(
            out_ref.at[place], pool.at[slot, pl.ds(row, 256), :], scan_sem.at[place]
        )

    scans = {}
    for i in range(2):
        scans[i] = ([(0, 512 * i, 512, i, 0), (2, 512 * i, 512, i, 512)], i, (13, 128 * i))
    for i in range(2, 8):
        scans[i] = ([(1 if i == 2 else i, 0, D, i, 0)], i, (13, 128 * i))
    scans[8] = ([(8 + i, 0, D, 8 + i, 0) for i in range(4)], 8, (14, 0))
    for i in range(4):
        scans[9 + i] = ([(12 + i, 0, D, 12, 0)], 9 + i, (14, 128))

    def scan(name):
        sources, row_lane, (total_row, total_lane) = scans[name]
        width = float(sum(source[2] for source in sources))
        step = 64 if name == 8 else 256

        def body(i, carry):
            cols, weights, total = carry
            r = pl.multiple_of(i * step, step)
            squares = []
            for place, lane, lanes, _, _ in sources:
                slot, row = spot(place)
                tile = pool[slot, pl.ds(row + r, step), lane : lane + lanes]
                squares.append(jnp.square(tile.astype(jnp.float32)))
            row_sum = sum(jnp.sum(square, axis=1, keepdims=True) for square in squares)
            rows = DECAY_RATE * rows_ref[pl.ds(r, step), row_lane : row_lane + 1] + (
                1.0 - DECAY_RATE
            ) * (row_sum / width + FACTOR_EPS)
            rows_out[pl.ds(r, step), row_lane : row_lane + 1] = rows
            inverse = 1.0 / rows
            cols = [c + fold(s) for c, s in zip(cols, squares)]
            weights = [w + fold(s * inverse) for w, s in zip(weights, squares)]
            return cols, weights, total + fold(rows)

        zeros = [jnp.zeros((8, source[2]), jnp.float32) for source in sources]
        cols, weights, total = lax.fori_loop(
            0, 256 // step, body, (zeros, zeros, jnp.zeros((8, 1), jnp.float32))
        )
        for (_, _, lanes, slot, lane), col, weighted in zip(sources, cols, weights):
            here = slice(lane, lane + lanes)
            part[slot : slot + 1, here] += jnp.sum(col, axis=0, keepdims=True)
            part[16 + slot : 17 + slot, here] += jnp.sum(weighted, axis=0, keepdims=True)
        part[total_row : total_row + 1, total_lane : total_lane + 128] += jnp.broadcast_to(
            jnp.sum(total), (1, 128)
        )

    chunk_at = {place: c for c, place in enumerate(place_of)}
    tasks = [
        ([chunk_at[source[0]] for source in scans[name][0]], name)
        for name in (9, 10, 11, 12, 8, 7, 4, 5, 6, 3, 2, 0, 1)
    ]
    loaded = set()
    for c in range(CHUNKS):
        if planner.stage[c] > 8:
            scan_load(place_of[c]).start()
    for first, second in planner.drain(tasks, 1.5):
        if first != "task":
            emit(first, second)
            if first == 8:
                scan_load(place_of[second]).start()
            continue
        for source in scans[second][0]:
            if source[0] not in loaded:
                loaded.add(source[0])
                scan_load(source[0]).wait()
        scan(second)
    total = line_sum(part, whole, line_send_sem, line_recv_sem, z, others_z)
    row_counts = [D] * 12 + [FF]
    means = [total[13:14, 128 * i : 128 * i + 1] / D for i in range(8)]
    means = means + [total[14:15, 0:1] / D] * 4 + [total[14:15, 128:129] / FF]
    cols_new, quotients = [], []
    for slot in range(13):
        new = DECAY_RATE * cols_ref[slot : slot + 1, :] + (1.0 - DECAY_RATE) * (
            total[slot : slot + 1] / row_counts[slot] + FACTOR_EPS
        )
        cols_new.append(new)
        quotients.append(jnp.sum(total[16 + slot : 17 + slot] / new, axis=1, keepdims=True))
        cols_out[slot : slot + 1, :] = new
    expand_quotient = quotients[8] + quotients[9] + quotients[10] + quotients[11]
    for slot in range(13):
        if slot < 8:
            mean_square = means[slot] * quotients[slot] / (D * D)
            rate = STEP_RATE * (OUT_GAIN if slot % 4 == 3 else 1.0)
        else:
            quotient = expand_quotient if slot < 12 else quotients[12]
            mean_square = means[slot] * quotient / (D * FF)
            rate = STEP_RATE
        factor = rate / jnp.maximum(1.0, jnp.sqrt(mean_square) / CLIP_LEVEL)
        scale_out[slot : slot + 1, :] = lax.rsqrt(cols_new[slot] / means[slot]) * factor
    token_copy.wait()


def backward(scalars, held, gains, small, factor_rows, factor_cols):
    any_space = pl.BlockSpec(memory_space=pl.ANY)
    vmem = pl.BlockSpec(memory_space=pltpu.VMEM)
    shape = jax.ShapeDtypeStruct
    dma = pltpu.SemaphoreType.DMA
    low = jnp.bfloat16
    wide = jnp.float32
    rows = small.shape[0]
    return pl.pallas_call(
        backward_kernel,
        out_shape=(
            shape((1024, D), low),
            shape((128, D), low),
            shape((CHUNKS, 256, D), low),
            shape(small.shape, wide),
            shape((256, 128), wide),
            shape((16, D), wide),
            shape((16, D), wide),
            shape((CHUNKS, 4, 128, D), low),
        ),
        in_specs=[SCALARS] * 2 + [any_space] * len(held) + [vmem] * 4,
        out_specs=(any_space, vmem, any_space, vmem, vmem, vmem, vmem, any_space),
        scratch_shapes=[
            pltpu.VMEM((POOL, 1024, D), low),
            pltpu.VMEM((1024, D), wide),
            pltpu.VMEM((G_SLOTS, 4, 256, D), low),
            pltpu.VMEM((R_SLOTS, 4, 128, D), low),
            pltpu.VMEM((CHUNKS, 4, 64, D), low),
            pltpu.VMEM((CHUNKS, 4, 32, D), low),
            pltpu.VMEM((CHUNKS, 3, 32, D), low),
            pltpu.VMEM((2, 128, D), wide),
            pltpu.VMEM((128, 1024), wide),
            pltpu.VMEM((2, 1024, 128), wide),
            pltpu.VMEM((2, 1024, 128), wide),
            pltpu.VMEM((8, 8, 1024), wide),
            pltpu.VMEM((3, 128, D), low),
            pltpu.VMEM((D, 128), low),
            pltpu.VMEM((rows, D), wide),
            pltpu.VMEM((3, rows, D), wide),
            pltpu.VMEM((3, rows, D), wide),
            pltpu.VMEM((4, rows, D), wide),
            pltpu.VMEM((32, D), wide),
            pltpu.VMEM((4, 32, D), wide),
            dma((POOL,)),
            dma((2,)),
            dma((4,)),
            dma((R_SLOTS,)),
            dma((CHUNKS,)),
            dma((3,)),
            dma((3,)),
            dma((6, CHUNKS)),
            dma((6, CHUNKS)),
            dma((CHUNKS, 3)),
            dma((CHUNKS, 3)),
            dma((CHUNKS,)),
            dma((6,)),
            dma((6,)),
        ],
        compiler_params=pltpu.CompilerParams(
            collective_id=0, has_side_effects=True, vmem_limit_bytes=62 * MIB
        ),
    )(*scalars, *held, gains, small, factor_rows, factor_cols)[0:7]


def line_sum(part, whole, send_sem, recv_sem, z, others_z):
    copies = [
        remote(part, whole.at[z], send_sem.at[d], recv_sem.at[d], others_z[d]) for d in range(3)
    ]
    for copy in copies:
        copy.start()
    whole[z] = part[...]
    for copy in copies:
        copy.wait()
    return (whole[0] + whole[1]) + (whole[2] + whole[3])


def update_attention_kernel(
    grad_ref, weight_ref, rows_ref, scale_ref, grad_out, new_out, copy_out, grads, change
):
    block = grad_ref.shape[1]
    for i in range(8):
        rows = lax.rsqrt(rows_ref[:, i : i + 1])
        every = pl.ds(i, block, stride=8)
        for lane in range(8):
            columns = slice(lane * 128, lane * 128 + 128)
            if i < 2:
                start = 512 * i + 128 * (lane % 4)
                grad = grad_ref[2 * (lane // 4), :, start : start + 128]
            else:
                grad = grad_ref[1 if i == 2 else i, :, columns]
            grad = grad.astype(jnp.float32)
            grads[lane, every, :] = grad
            change[lane, every, :] = grad * rows * scale_ref[i : i + 1, columns]
    for lane in range(8):
        columns = slice(lane * 128, lane * 128 + 128)
        grad_out[:, columns] = grads[lane]
        new = weight_ref[:, columns] - change[lane]
        new_out[:, columns] = new
        copy_out[:, columns] = new.astype(jnp.bfloat16)


def update_attention(grads, weights, rows, scale):
    block = 32
    wide = pl.BlockSpec((block * 8, D), lambda i: (i, 0))
    shape = jax.ShapeDtypeStruct
    new = pl.pallas_call(
        update_attention_kernel,
        grid=(256 // block,),
        out_shape=(
            shape((2048, D), jnp.float32),
            shape((2048, D), jnp.float32),
            shape((2048, D), jnp.bfloat16),
        ),
        in_specs=[
            pl.BlockSpec((8, block, D), lambda i: (0, i, 0)),
            wide,
            pl.BlockSpec((block, 128), lambda i: (i, 0)),
            pl.BlockSpec((16, D), lambda i: (0, 0)),
        ],
        out_specs=(wide,) * 3,
        scratch_shapes=[pltpu.VMEM((8, block * 8, 128), jnp.float32)] * 2,
        compiler_params=pltpu.CompilerParams(vmem_limit_bytes=62 * MIB),
    )(grads, weights.reshape(2048, D), rows, scale)
    return [t.reshape(256, 8, D) for t in new]


def update_kernel(
    first, slots, grad_ref, weight_ref, rows_ref, scale_ref, grad_out, new_out, copy_out
):
    spans = 4 if slots == 4 else 1
    wide = D // spans
    for i in range(slots):
        grads = grad_ref[i].astype(jnp.float32)
        changes = grads * (lax.rsqrt(rows_ref[...]) * scale_ref[first + i : first + i + 1, :])
        for s in range(spans):
            start = s * D + i * wide
            columns = slice(start, start + wide)
            part = slice(s * wide, s * wide + wide)
            grad_out[:, columns] = grads[:, part]
            new = weight_ref[:, columns] - changes[:, part]
            new_out[:, columns] = new
            copy_out[:, columns] = new.astype(jnp.bfloat16)


def update_plain(grads, weights, rows, scale, first, slots, grad_map):
    count, width = weights.shape
    block = 128 // slots
    wide = pl.BlockSpec((block, width), lambda i: (i, 0))
    shape = jax.ShapeDtypeStruct
    return pl.pallas_call(
        lambda *refs: update_kernel(first, slots, *refs),
        grid=(count // block,),
        out_shape=(
            shape(weights.shape, jnp.float32),
            shape(weights.shape, jnp.float32),
            shape(weights.shape, jnp.bfloat16),
        ),
        in_specs=[
            pl.BlockSpec((slots, block, D), grad_map),
            wide,
            pl.BlockSpec((block, 1), lambda i: (i, 0)),
            pl.BlockSpec((16, D), lambda i: (0, 0)),
        ],
        out_specs=(wide,) * 3,
        compiler_params=pltpu.CompilerParams(vmem_limit_bytes=62 * MIB),
    )(grads, weights, rows, scale)


def update_direct(grads, rows, scale, attention_weights, expand_weight, shrink_weight):
    shr_rows = rows[:, 9:13].T.reshape(-1, 1)
    attention = update_attention(grads, attention_weights, rows, scale)
    expand = update_plain(grads, expand_weight, rows[:, 8:9], scale, 8, 4, lambda i: (2, i, 0))
    shrink = update_plain(
        grads, shrink_weight, shr_rows, scale, 12, 1, lambda i: (12 + i // 2, i % 2, 0)
    )
    return attention, expand, shrink, (rows[:, 0:8].T, rows[:, 8], shr_rows[:, 0])


def as_rows(vector):
    rows = -(-vector.shape[0] // 1024) * 8
    return jnp.pad(vector, (0, rows * 128 - vector.shape[0])).reshape(rows, 128)


def masked_scores(query_part, key_heads, first_row, valid_count, causal):
    scores = jnp.einsum("qhd,khd->hqk", query_part, key_heads, preferred_element_type=jnp.float32)
    key_places = jnp.arange(key_heads.shape[0], dtype=jnp.int32)[None, :]
    usable = key_places < valid_count
    if causal:
        query_places = first_row + jnp.arange(query_part.shape[0], dtype=jnp.int32)[:, None]
        usable = usable & (key_places <= query_places)
    return jnp.where(usable[None], scores, MASKED)


def attend_forward(queries, key_heads, values, valid_count, causal):
    query_rows = queries.shape[0]
    step_rows = min(512, query_rows)
    outputs, stored = ([], [])
    for b in range(query_rows // step_rows):
        first_row = b * step_rows
        key_end = first_row + step_rows if causal else key_heads.shape[0]
        scores = masked_scores(
            queries[first_row : first_row + step_rows],
            key_heads[:key_end],
            first_row,
            valid_count,
            causal,
        )
        row_max = jnp.max(scores, axis=-1, keepdims=True)
        raised = jnp.exp(scores - row_max)
        totals = jnp.sum(raised, axis=-1, keepdims=True)
        probs_low = (raised / totals).astype(jnp.bfloat16)
        outputs.append(
            jnp.einsum(
                "hqk,khd->qhd", probs_low, values[:key_end], preferred_element_type=jnp.float32
            )
        )
        stored.append(row_max + jnp.log(totals))
    return (jnp.concatenate(outputs, axis=0), stored)


def attend_backward(queries, key_heads, values, grad_out, stored, valid_count, causal):
    query_rows = queries.shape[0]
    key_rows = key_heads.shape[0]
    step_rows = min(512, query_rows)
    grad_queries = []
    grad_keys = jnp.zeros(key_heads.shape, jnp.float32)
    grad_values = jnp.zeros(values.shape, jnp.float32)
    for b in range(query_rows // step_rows):
        first_row = b * step_rows
        key_end = first_row + step_rows if causal else key_rows
        query_part = queries[first_row : first_row + step_rows]
        grad_part = grad_out[first_row : first_row + step_rows]
        scores = masked_scores(query_part, key_heads[:key_end], first_row, valid_count, causal)
        probs = jnp.exp(scores - stored[b])
        probs_low = probs.astype(jnp.bfloat16)
        grad_probs = jnp.einsum(
            "qhd,khd->hqk", grad_part, values[:key_end], preferred_element_type=jnp.float32
        )
        value_part = jnp.einsum(
            "hqk,qhd->khd", probs_low, grad_part, preferred_element_type=jnp.float32
        )
        grad_scores = probs * (grad_probs - jnp.sum(probs * grad_probs, axis=-1, keepdims=True))
        scores_low = grad_scores.astype(jnp.bfloat16)
        grad_queries.append(
            jnp.einsum(
                "hqk,khd->qhd", scores_low, key_heads[:key_end], preferred_element_type=jnp.float32
            )
        )
        key_part = jnp.einsum(
            "hqk,qhd->khd", scores_low, query_part, preferred_element_type=jnp.float32
        )
        padding = ((0, key_rows - key_end), (0, 0), (0, 0))
        grad_keys = grad_keys + jnp.pad(key_part, padding)
        grad_values = grad_values + jnp.pad(value_part, padding)
    return (jnp.concatenate(grad_queries, axis=0), grad_keys, grad_values)


def gather_rows(piece):
    return lax.all_gather(piece, ("shard", "rep"), axis=0, tiled=True)


def own_piece(block, replicas):
    rows = block.shape[0] // replicas
    return lax.dynamic_slice_in_dim(block, lax.axis_index("rep") * rows, rows, axis=0)


def scatter_rows(grad):
    piece = lax.psum_scatter(
        grad.astype(jnp.bfloat16), ("shard", "rep"), scatter_dimension=0, tiled=True
    )
    return lax.all_gather(piece, "rep", axis=0, tiled=True)


def local_factors(grad, rows):
    square = grad * grad
    rows_new = DECAY_RATE * rows + (1.0 - DECAY_RATE) * jnp.mean(square + FACTOR_EPS, axis=-1)
    col_part = jnp.sum(square + FACTOR_EPS, axis=0)
    weighted = jnp.sum(square / rows_new[..., None], axis=0)
    return rows_new, col_part, weighted, jnp.sum(rows_new, axis=0)


def finish_factors(grad, weight, rows_new, cols, col_sum, weighted, row_total, row_count, rate):
    cols_new = DECAY_RATE * cols + (1.0 - DECAY_RATE) * col_sum / row_count
    mean_rows = row_total / row_count
    mean_square = mean_rows * jnp.sum(weighted / cols_new, axis=-1) / (row_count * cols.shape[-1])
    factor = rate / jnp.maximum(1.0, jnp.sqrt(mean_square) / CLIP_LEVEL)
    scaled = lax.rsqrt(cols_new / mean_rows[..., None]) * factor[..., None]
    fresh = weight - grad * (lax.rsqrt(rows_new)[..., None] * scaled[None])
    return fresh, cols_new


def plain_device(
    tokens,
    encoder,
    cotangent,
    lengths,
    encoder_lengths,
    dealt_order,
    attention_weights,
    expand_weight,
    shrink_weight,
    small_params,
    attention_rows,
    attention_cols,
    expand_rows,
    expand_cols,
    shrink_rows,
    shrink_cols,
    small_moment,
):
    devices = lax.axis_size(("rep", "shard"))
    replicas = lax.axis_size("rep")
    shards = lax.axis_size("shard")
    slot_tokens = tokens.shape[0]
    slot_states = encoder.shape[0]
    position = lax.axis_index(("rep", "shard"))
    inverse = (
        jnp.zeros((devices,), jnp.int32).at[dealt_order].set(jnp.arange(devices, dtype=jnp.int32))
    )
    qkv_piece = own_piece(attention_weights[:, 0:3, :].reshape(-1, 3 * D), replicas)
    rest_piece = own_piece(attention_weights[:, 3:8, :].reshape(-1, 5 * D), replicas)
    qkv_full = gather_rows(qkv_piece.astype(jnp.bfloat16))
    rest_full = gather_rows(rest_piece.astype(jnp.bfloat16))
    expand_full = gather_rows(own_piece(expand_weight, replicas).astype(jnp.bfloat16))
    shrink_full = gather_rows(own_piece(shrink_weight, replicas).astype(jnp.bfloat16))
    spread = lax.all_to_all(
        tokens.reshape(devices, slot_tokens // devices, D),
        ("rep", "shard"),
        split_axis=0,
        concat_axis=0,
        tiled=True,
    )
    picked = jnp.take(spread, inverse, axis=0)
    tokens = lax.all_to_all(
        picked, ("rep", "shard"), split_axis=0, concat_axis=0, tiled=True
    ).reshape(slot_tokens, D)
    states = encoder
    incoming = cotangent
    valid_tokens = lengths[position]
    valid_states = encoder_lengths[position]
    matrices = [qkv_full[:, i * D : (i + 1) * D] for i in range(3)] + [
        rest_full[:, i * D : (i + 1) * D] for i in range(5)
    ]
    parts = unpack(small_params)
    token_heads = (slot_tokens, HEADS, HEAD_DIM)
    state_heads = (slot_states, HEADS, HEAD_DIM)
    q_self = ((forward_product(tokens, matrices[0]) + parts[0]) * 0.125).astype(
        jnp.bfloat16
    )
    k_self = forward_product(tokens, matrices[1]).astype(jnp.bfloat16)
    v_self = (forward_product(tokens, matrices[2]) + parts[1]).astype(jnp.bfloat16)
    o_self, lse_self = attend_forward(
        q_self.reshape(token_heads),
        k_self.reshape(token_heads),
        v_self.reshape(token_heads),
        valid_tokens,
        True,
    )
    o_self_low = o_self.reshape(slot_tokens, D).astype(jnp.bfloat16)
    branch_a = forward_product(o_self_low, matrices[3]) + parts[2]
    tokens_wide = tokens.astype(jnp.float32)
    hidden_one, norm_one_back = jax.vjp(layer_norm, tokens_wide + branch_a, parts[8], parts[9])
    hidden_one_low = hidden_one.astype(jnp.bfloat16)
    q_cross = (
        (forward_product(hidden_one_low, matrices[4]) + parts[3]) * 0.125
    ).astype(jnp.bfloat16)
    k_cross = forward_product(states, matrices[5]).astype(jnp.bfloat16)
    v_cross = (forward_product(states, matrices[6]) + parts[4]).astype(jnp.bfloat16)
    o_cross, lse_cross = attend_forward(
        q_cross.reshape(token_heads),
        k_cross.reshape(state_heads),
        v_cross.reshape(state_heads),
        valid_states,
        False,
    )
    o_cross_low = o_cross.reshape(slot_tokens, D).astype(jnp.bfloat16)
    branch_c = forward_product(o_cross_low, matrices[7]) + parts[5]
    hidden_two, norm_two_back = jax.vjp(layer_norm, hidden_one + branch_c, parts[10], parts[11])
    hidden_two_low = hidden_two.astype(jnp.bfloat16)
    pre_act = forward_product(hidden_two_low, expand_full) + parts[6]
    activated, gelu_back = jax.vjp(gelu_exact, pre_act)
    activated_low = activated.astype(jnp.bfloat16)
    branch_m = forward_product(activated_low, shrink_full) + parts[7]
    result, norm_three_back = jax.vjp(layer_norm, hidden_two + branch_m, parts[12], parts[13])
    usable_rows = (jnp.arange(slot_tokens, dtype=jnp.int32) < valid_tokens).astype(jnp.float32)[
        :, None
    ]
    squares = jnp.stack(
        [
            jnp.sum(usable_rows * t * t)
            for t in (tokens_wide, branch_a, hidden_one, branch_c, hidden_two, branch_m)
        ]
    )
    d_third, d_gain_three, d_shift_three = norm_three_back(
        incoming.astype(jnp.float32) * usable_rows
    )
    d_mlp = d_third.astype(jnp.bfloat16)
    grad_shrink = weight_product(activated_low, d_mlp)
    grad_shrink_offset = row_sum(d_mlp)
    d_activated = input_product(d_mlp, shrink_full)
    d_pre = gelu_back(d_activated)[0].astype(jnp.bfloat16)
    grad_expand = weight_product(hidden_two_low, d_pre)
    grad_expand_offset = row_sum(d_pre)
    d_hidden_two = d_third + input_product(d_pre, expand_full)
    d_second, d_gain_two, d_shift_two = norm_two_back(d_hidden_two)
    d_branch_c = d_second.astype(jnp.bfloat16)
    grad_cross_out = weight_product(o_cross_low, d_branch_c)
    grad_cross_out_offset = row_sum(d_branch_c)
    d_o_cross = input_product(d_branch_c, matrices[7]).astype(jnp.bfloat16)
    grad_cq, grad_ck, grad_cv = attend_backward(
        q_cross.reshape(token_heads),
        k_cross.reshape(state_heads),
        v_cross.reshape(state_heads),
        d_o_cross.reshape(token_heads),
        lse_cross,
        valid_states,
        False,
    )
    dq_cross = (grad_cq.reshape(slot_tokens, D) * 0.125).astype(jnp.bfloat16)
    dk_cross = grad_ck.reshape(slot_states, D).astype(jnp.bfloat16)
    dv_cross = grad_cv.reshape(slot_states, D).astype(jnp.bfloat16)
    grad_cross_query = weight_product(hidden_one_low, dq_cross)
    grad_cross_key = weight_product(states, dk_cross)
    grad_cross_value = weight_product(states, dv_cross)
    state_grad = input_product(dk_cross, matrices[5]) + input_product(
        dv_cross, matrices[6]
    )
    d_hidden_one = d_second + input_product(dq_cross, matrices[4])
    d_first, d_gain_one, d_shift_one = norm_one_back(d_hidden_one)
    d_branch_a = d_first.astype(jnp.bfloat16)
    grad_self_out = weight_product(o_self_low, d_branch_a)
    grad_self_out_offset = row_sum(d_branch_a)
    d_o_self = input_product(d_branch_a, matrices[3]).astype(jnp.bfloat16)
    grad_sq, grad_sk, grad_sv = attend_backward(
        q_self.reshape(token_heads),
        k_self.reshape(token_heads),
        v_self.reshape(token_heads),
        d_o_self.reshape(token_heads),
        lse_self,
        valid_tokens,
        True,
    )
    dq_self = (grad_sq.reshape(slot_tokens, D) * 0.125).astype(jnp.bfloat16)
    dk_self = grad_sk.reshape(slot_tokens, D).astype(jnp.bfloat16)
    dv_self = grad_sv.reshape(slot_tokens, D).astype(jnp.bfloat16)
    grad_self_query = weight_product(tokens, dq_self)
    grad_self_key = weight_product(tokens, dk_self)
    grad_self_value = weight_product(tokens, dv_self)
    token_grad = (
        d_first
        + input_product(dq_self, matrices[0])
        + input_product(dk_self, matrices[1])
        + input_product(dv_self, matrices[2])
    )
    small_partial = jnp.concatenate(
        [
            row_sum(dq_self),
            row_sum(dv_self),
            grad_self_out_offset,
            row_sum(dq_cross),
            row_sum(dv_cross),
            grad_cross_out_offset,
            grad_expand_offset,
            grad_shrink_offset,
            d_gain_one,
            d_shift_one,
            d_gain_two,
            d_shift_two,
            d_gain_three,
            d_shift_three,
        ]
    )
    totals = lax.psum(jnp.concatenate([small_partial, squares]), ("rep", "shard"))
    g_shrink = scatter_rows(grad_shrink)
    g_expand = scatter_rows(grad_expand)
    g_rest = scatter_rows(
        jnp.concatenate(
            [grad_self_out, grad_cross_query, grad_cross_key, grad_cross_value, grad_cross_out],
            axis=1,
        )
    )
    g_qkv = scatter_rows(
        jnp.concatenate([grad_self_query, grad_self_key, grad_self_value], axis=1)
    )
    g_attention = (
        jnp.concatenate([g_qkv, g_rest], axis=1).reshape(-1, 8, D).astype(jnp.float32)
    )
    g_expand = g_expand.astype(jnp.float32)
    g_shrink = g_shrink.astype(jnp.float32)
    attention_rows_new, *attention_parts = local_factors(g_attention, attention_rows.T)
    expand_rows_new, *expand_parts = local_factors(g_expand, expand_rows)
    shrink_rows_new, *shrink_parts = local_factors(g_shrink, shrink_rows)
    flat = attention_parts + expand_parts + shrink_parts
    summed = lax.psum(jnp.concatenate([t.reshape(-1) for t in flat]), "shard")
    sums = []
    offset = 0
    for t in flat:
        sums.append(summed[offset : offset + t.size].reshape(t.shape))
        offset = offset + t.size
    attention_rates = STEP_RATE * jnp.where(jnp.arange(8) % 4 == 3, OUT_GAIN, 1.0).astype(
        jnp.float32
    )
    attention_new, attention_cols_new = finish_factors(
        g_attention,
        attention_weights,
        attention_rows_new,
        attention_cols,
        *sums[0:3],
        D,
        attention_rates,
    )
    expand_new, expand_cols_new = finish_factors(
        g_expand, expand_weight, expand_rows_new, expand_cols, *sums[3:6], D, STEP_RATE
    )
    shrink_new, shrink_cols_new = finish_factors(
        g_shrink, shrink_weight, shrink_rows_new, shrink_cols, *sums[6:9], FF, STEP_RATE
    )
    small_grad = totals[: small_params.shape[0]]
    small_moment_new = DECAY_RATE * small_moment + (1.0 - DECAY_RATE) * (
        small_grad * small_grad + FACTOR_EPS
    )
    small_update = small_grad * lax.rsqrt(small_moment_new)
    small_scale = jnp.sqrt(jnp.mean(small_update * small_update))
    small_new = small_params - SMALL_RATE * small_update / jnp.maximum(
        1.0, small_scale / CLIP_LEVEL
    )
    norm_stats = jnp.sqrt(
        totals[small_params.shape[0] :] / (jnp.sum(lengths).astype(jnp.float32) * D)
    )
    return (
        result.astype(jnp.bfloat16),
        token_grad.astype(jnp.bfloat16),
        state_grad.astype(jnp.bfloat16),
        g_attention,
        g_expand,
        g_shrink,
        small_grad,
        attention_new,
        expand_new,
        shrink_new,
        small_new,
        attention_new.astype(jnp.bfloat16),
        expand_new.astype(jnp.bfloat16),
        shrink_new.astype(jnp.bfloat16),
        attention_rows_new.T,
        attention_cols_new,
        expand_rows_new,
        expand_cols_new,
        shrink_rows_new,
        shrink_cols_new,
        small_moment_new,
        norm_stats,
    )


def direct_device(
    tokens,
    encoder,
    cotangent,
    lengths,
    encoder_lengths,
    dealt_order,
    attention_weights,
    expand_weight,
    shrink_weight,
    small_params,
    attention_rows,
    attention_cols,
    expand_rows,
    expand_cols,
    shrink_rows,
    shrink_cols,
    small_moment,
):
    inverse = jnp.zeros((32,), jnp.int32).at[dealt_order].set(jnp.arange(32, dtype=jnp.int32))
    params = small_params.reshape(17, D)
    weights = (attention_weights.reshape(2048, D), expand_weight, shrink_weight)
    (
        tokens,
        full,
        q_self,
        k_self,
        v_self,
        o_self,
        lse_self,
        q_cross,
        k_cross,
        v_cross,
        o_cross,
        lse_cross,
        summed_one,
        summed_two,
        hidden_one,
        hidden_two,
        activated,
        slope,
        output,
        d_mlp,
        d_third,
        small_first,
    ) = forward(
        (inverse, lengths, encoder_lengths), tokens, weights, encoder, cotangent, params
    )
    factor_rows = jnp.concatenate(
        [attention_rows, expand_rows.reshape(1, 256), shrink_rows.reshape(4, 256)]
    )
    factor_rows = jnp.pad(factor_rows.T, ((0, 0), (0, 115)))
    factor_cols = jnp.concatenate(
        [attention_cols, hidden_blocks(expand_cols), shrink_cols.reshape(1, D), jnp.ones((3, D))]
    )
    token_grad, state_grad, reduced, totals, factor_rows, factor_cols, scale = backward(
        (lengths, encoder_lengths),
        (
            d_mlp,
            d_third,
            activated,
            slope,
            full.reshape(GATHERED, 1024, D),
            hidden_two,
            hidden_one,
            tokens.reshape(1024, D),
            encoder,
            o_cross,
            o_self,
            summed_one,
            summed_two,
            q_self,
            k_self,
            v_self,
            q_cross,
            k_cross,
            v_cross,
            lse_self,
            lse_cross,
        ),
        params,
        small_first,
        factor_rows,
        factor_cols,
    )
    attention, expand, shrink, rows_new = update_direct(
        reduced, factor_rows, scale, attention_weights, expand_weight, shrink_weight
    )
    cols_new = (factor_cols[0:8], hidden_flat(factor_cols[8:12]), factor_cols[12])
    small_grad = totals[0:17].reshape(-1)
    small_moment_new = DECAY_RATE * small_moment + (1.0 - DECAY_RATE) * (
        small_grad * small_grad + FACTOR_EPS
    )
    small_update = small_grad * lax.rsqrt(small_moment_new)
    small_scale = jnp.sqrt(jnp.mean(small_update * small_update))
    small_new = small_params - SMALL_RATE * small_update / jnp.maximum(
        1.0, small_scale / CLIP_LEVEL
    )
    norm_stats = jnp.sqrt(totals[17, 0:6] / (jnp.sum(lengths).astype(jnp.float32) * D))
    return (
        output,
        token_grad,
        state_grad,
        attention[0],
        expand[0],
        shrink[0],
        small_grad,
        attention[1],
        expand[1],
        shrink[1],
        small_new,
        attention[2],
        expand[2],
        shrink[2],
        rows_new[0],
        cols_new[0],
        rows_new[1],
        cols_new[1],
        rows_new[2],
        cols_new[2],
        small_moment_new,
        norm_stats,
    )


def on_device(*args):
    if lax.axis_size("rep") == 8 and lax.axis_size("shard") == 4:
        return direct_device(*args)
    return plain_device(*args)


def solution(mesh):
    in_specs = (
        P(("rep", "shard"), None),
        P(("rep", "shard"), None),
        P(("rep", "shard"), None),
        P(),
        P(),
        P(),
        P("shard", None, None),
        P("shard", None),
        P("shard", None),
        P(),
        P(None, "shard"),
        P(),
        P("shard"),
        P(),
        P("shard"),
        P(),
        P(),
    )
    out_specs = (
        P(("rep", "shard"), None),
        P(("rep", "shard"), None),
        P(("rep", "shard"), None),
        P("shard", None, None),
        P("shard", None),
        P("shard", None),
        P(),
        P("shard", None, None),
        P("shard", None),
        P("shard", None),
        P(),
        P("shard", None, None),
        P("shard", None),
        P("shard", None),
        P(None, "shard"),
        P(),
        P("shard"),
        P(),
        P("shard"),
        P(),
        P(),
        P(),
    )
    return jax.shard_map(
        on_device, mesh=mesh, in_specs=in_specs, out_specs=out_specs, check_vma=False
    )
```

```python
import math

import jax
import jax.numpy as jnp
from jax import lax
from jax.experimental import pallas as pl
from jax.experimental.pallas import tpu as pltpu
from jax.sharding import PartitionSpec as P

D = 1024
HEADS = 16
HEAD_DIM = 64
FF = 4096


DECAY_RATE = 0.5
CLIP_LEVEL = 0.25
STEP_RATE = 0.1
SMALL_RATE = 0.4
OUT_GAIN = 8.0
NORM_EPS = 1e-05
FACTOR_EPS = 1e-30
MASKED = -1e30
MESH = pl.DeviceIdType.MESH
CHUNKS = 16
GATHERED = 16
EXPAND_AT = (8, 9, 11, 13)
SHRINK_AT = (10, 12, 14, 15)
MIB = 1 << 20


def layer_norm(r, norm_gain, norm_shift):
    centred = r - jnp.mean(r, axis=-1, keepdims=True)
    spread = jnp.mean(centred * centred, axis=-1, keepdims=True)
    return centred * lax.rsqrt(spread + NORM_EPS) * norm_gain + norm_shift


def gelu_exact(values):
    return jax.nn.gelu(values, approximate=False)


def unpack(small):
    extents = [D] * 6 + [FF] + [D] * 7
    pieces = []
    offset = 0
    for extent in extents:
        pieces.append(small[offset : offset + extent])
        offset = offset + extent
    return pieces


def forward_product(source, matrix):
    return jnp.dot(source, matrix, preferred_element_type=jnp.float32)


def input_product(grad_low, matrix):
    return jnp.einsum("to,io->ti", grad_low, matrix, preferred_element_type=jnp.float32)


def weight_product(source, grad_low):
    return jnp.einsum("ti,to->io", source, grad_low, preferred_element_type=jnp.float32)


def row_sum(grad_low):
    return jnp.sum(grad_low.astype(jnp.float32), axis=0)


def transposed(block):
    return block.astype(jnp.float32).T.astype(jnp.bfloat16)


def half_lanes(shape, dim):
    return lax.broadcasted_iota(jnp.int32, shape, dim)


def masked_keys(keys, length, head):
    place = half_lanes(keys.shape, 0)
    lane = half_lanes(keys.shape, 1)
    blocked = jnp.where((lane == 64 - 64 * head) & (place >= length), MASKED, 0.0)
    own = (lane >= 64 * head) & (lane < 64 * head + 64)
    return jnp.where(own, keys.astype(jnp.float32), blocked).astype(jnp.bfloat16)


def own_head(rows_t, head, fill):
    place = half_lanes(rows_t.shape, 0)
    own = (place >= 64 * head) & (place < 64 * head + 64)
    other = jnp.where(place == 64 - 64 * head, fill, 0.0)
    return jnp.where(own, rows_t.astype(jnp.float32), other).astype(jnp.bfloat16)


def product(first, second):
    return jnp.dot(first, second, preferred_element_type=jnp.float32)


def causal_mask(scores, step):
    kept = scores.shape[0] - step
    last = scores[kept:]
    allowed = half_lanes(last.shape, 0) <= half_lanes(last.shape, 1)
    last = jnp.where(allowed, last, MASKED)
    return last if kept == 0 else jnp.concatenate([scores[:kept], last], axis=0)


def attend_pair(
    causal, step, length, q_ref, k_ref, v_ref, o_ref, lse_ref, o_t, first_row=0
):
    count = q_ref.shape[0]
    q_t = transposed(q_ref[...])
    v_t = transposed(v_ref[...])
    keys = [masked_keys(k_ref[...], length, head) for head in range(2)]
    queries = [own_head(q_t, head, 1.0) for head in range(2)]
    units = [(head, start) for start in range(0, count, step) for head in range(2)]

    def scores_of(head, start):
        end = first_row + start + step if causal else k_ref.shape[0]
        return product(keys[head][:end], queries[head][:, start : start + step])

    ahead = scores_of(*units[0])
    for index, (head, start) in enumerate(units):
        scores = ahead
        if index + 1 < len(units):
            ahead = scores_of(*units[index + 1])
        rows = slice(64 * head, 64 * head + 64)
        columns = slice(start, start + step)
        if causal:
            scores = causal_mask(scores, step)
        top = jnp.max(scores, axis=0, keepdims=True)
        raised = jnp.exp(scores - top)
        total = jnp.sum(raised, axis=0, keepdims=True)
        probs = (raised * (1.0 / total)).astype(jnp.bfloat16)
        o_t[rows, columns] = product(v_t[rows, : scores.shape[0]], probs)
        place = slice(first_row + start, first_row + start + step)
        lse_ref[0, head : head + 1, place] = top + jnp.log(total)
    o_ref[...] = o_t[:, :count].T.astype(jnp.bfloat16)


def attend_back_pair(
    causal,
    step,
    length,
    q_ref,
    k_ref,
    v_ref,
    do_ref,
    lse_ref,
    dq_ref,
    dk_ref,
    dv_ref,
    put_sums,
    dq_t,
    dk_sum,
    dv_sum,
):
    key_rows = k_ref.shape[0]
    q_t = transposed(q_ref[...])
    k_t = transposed(k_ref[...])
    do_t = transposed(do_ref[...])
    values = v_ref[...]
    keys = [masked_keys(k_ref[...], length, head) for head in range(2)]
    queries = [own_head(q_t, head, 1.0) for head in range(2)]
    grads = [own_head(do_t, head, 0.0) for head in range(2)]
    count = q_ref.shape[0] // step
    units = [(head, b) for b in reversed(range(count)) for head in range(2)]

    def products_of(head, b):
        columns = slice(b * step, b * step + step)
        end = b * step + step if causal else key_rows
        scores = product(keys[head][:end], queries[head][:, columns])
        return scores, product(values[:end], grads[head][:, columns])

    ahead = products_of(*units[0])
    for index, (head, b) in enumerate(units):
        scores, d_probs = ahead
        if index + 1 < len(units):
            ahead = products_of(*units[index + 1])
        rows = slice(64 * head, 64 * head + 64)
        columns = slice(b * step, b * step + step)
        end = scores.shape[0]
        if causal:
            scores = causal_mask(scores, step)
        probs = jnp.exp(scores - lse_ref[0, head : head + 1, columns])
        weighted = probs * d_probs
        delta = jnp.sum(weighted, axis=0, keepdims=True)
        d_scores = (weighted - probs * delta).astype(jnp.bfloat16)
        dv = product(probs.astype(jnp.bfloat16), do_ref[columns, :])
        dk = product(d_scores, q_ref[columns, :])
        if b == count - 1:
            dv_sum[head, :end] = dv
            dk_sum[head, :end] = dk
        else:
            dv_sum[head, :end] += dv
            dk_sum[head, :end] += dk
        dq_t[rows, columns] = product(k_t[rows, :end], d_scores)
    first = half_lanes((key_rows, 128), 1) < 64
    dk_ref[...] = jnp.where(first, dk_sum[0, :key_rows], dk_sum[1, :key_rows]).astype(jnp.bfloat16)
    dv = jnp.where(first, dv_sum[0, :key_rows], dv_sum[1, :key_rows]).astype(jnp.bfloat16)
    dv_ref[...] = dv
    dq = (dq_t[...] * 0.125).T.astype(jnp.bfloat16)
    dq_ref[...] = dq
    put_sums(
        jnp.sum(dq.astype(jnp.float32), axis=0, keepdims=True),
        jnp.sum(dv.astype(jnp.float32), axis=0, keepdims=True),
    )


SCALARS = pl.BlockSpec(memory_space=pltpu.SMEM)


def neighbours():
    rep = lax.axis_index("rep")
    z = lax.axis_index("shard")
    core = rep % 2
    x = (rep // 2) % 2
    y = rep // 4
    other_core = (rep + 1 - 2 * core, z)
    other_x = (rep + 2 - 4 * x, z)
    other_y = (rep + 4 - 8 * y, z)
    others_z = [(rep, (z + d) % 4) for d in (1, 2, 3)]
    return core, x, y, z, other_core, other_x, other_y, others_z


def greet(devices):
    barrier = pltpu.get_barrier_semaphore()
    for device in devices:
        pl.semaphore_signal(barrier, inc=1, device_id=device, device_id_type=MESH)
    pl.semaphore_wait(barrier, len(devices))


def remote(src, dst, send, recv, device):
    return pltpu.make_async_remote_copy(
        src_ref=src, dst_ref=dst, send_sem=send, recv_sem=recv, device_id=device, device_id_type=MESH
    )


def gather_copies(refs, c, parity, places):
    piece, full, place_sem, z_send, z_recv, send, recv = refs
    core, x, y, z, other_core, other_x, other_y, others_z = places
    a = x + parity * (y - x)
    b = y + parity * (x - y)
    first = (other_x[0] + parity * (other_y[0] - other_x[0]), z)
    second = (other_y[0] + parity * (other_x[0] - other_y[0]), z)
    own = pl.ds(pl.multiple_of(core * 128 + a * 64 + b * 32, 32), 32)
    steps = (
        (own, second),
        (pl.ds(pl.multiple_of(core * 128 + a * 64, 64), 64), first),
        (pl.ds(pl.multiple_of(core * 128, 128), 128), other_core),
    )

    def local():
        return pltpu.make_async_copy(piece.at[c], full.at[c, z, own, :], place_sem.at[c])

    def line(d):
        return remote(
            piece.at[c], full.at[c, z, own, :], z_send.at[c, d], z_recv.at[c, d], others_z[d]
        )

    def pair(k):
        block = full.at[c, :, steps[k][0], :]
        return remote(block, block, send.at[k, c], recv.at[k, c], steps[k][1])

    return local, line, pair


def gather_stage(k, refs, c, parity, places):
    local, line, pair = gather_copies(refs, c, parity, places)
    if k == 0:
        local().start()
        for d in range(3):
            line(d).start()
    if k == 1:
        local().wait()
        for d in range(3):
            line(d).wait_recv()
        pair(0).start()
    if k == 2 or k == 3:
        pair(k - 2).wait_recv()
        pair(k - 1).start()
    if k == 4:
        pair(2).wait()
        pair(1).wait_send()
        pair(0).wait_send()
        for d in range(3):
            line(d).wait_send()


def gather_sems(count):
    dma = pltpu.SemaphoreType.DMA
    return [dma((count,)), dma((count, 3)), dma((count, 3)), dma((3, count)), dma((3, count))]


def hidden_blocks(values):
    split = values.reshape(values.shape[:-1] + (4, 4, 256))
    split = jnp.swapaxes(split, -3, -2)
    return split.reshape(values.shape[:-1] + (4, 1024))


def hidden_flat(blocks):
    split = blocks.reshape(blocks.shape[:-2] + (4, 4, 256))
    split = jnp.swapaxes(split, -3, -2)
    return split.reshape(blocks.shape[:-2] + (FF,))


def fold(tile):
    return jnp.sum(tile.reshape(-1, 8, tile.shape[-1]), axis=0)


GATHER_PLAN = (("z", 7.5), ("second", 7.5), ("first", 13.0), ("core", 4.0), (None, 0.0))


class GatherPlanner:
    def __init__(self, count):
        self.now = 0.0
        self.links = {"core": 0.0, "x": 0.0, "y": 0.0, "z": 0.0}
        self.stage = {c: 0 for c in range(count)}
        self.ready = {c: 0.0 for c in range(count)}
        self.opened = count

    def can(self, c):
        if self.stage[c] == 0 and c >= 3 and self.stage[c - 3] < 2:
            return False
        return self.stage[c] < 5

    def spend(self, now, **busy):
        self.now = max(self.now, now)
        for link, span in busy.items():
            self.links[link] = max(self.links[link], self.now) + span

    def emit(self, c):
        stage = self.stage[c]
        link, span = GATHER_PLAN[stage]
        first, second = ("x", "y") if c % 2 == 0 else ("y", "x")
        link = {"first": first, "second": second}.get(link, link)
        self.now = max(self.now, self.ready[c]) + 0.1
        if link is not None:
            begin = max(self.now, self.links[link])
            self.links[link] = begin + span - 1.0
            self.ready[c] = begin + span
        self.stage[c] = stage + 1
        return (stage, c)

    def tick(self, spent):
        self.now += spent
        events = []
        progress = True
        while progress:
            progress = False
            for c in range(self.opened):
                if self.can(c) and self.ready[c] <= self.now:
                    events.append(self.emit(c))
                    progress = True
        return events

    def until(self, c):
        events = []
        while self.stage[c] < 5:
            choices = [i for i in range(self.opened) if self.can(i)]
            best = min(choices, key=lambda i: (self.ready[i], i))
            events.append(self.emit(best))
        return events


ERFC_SERIES = (
    0.08459648489952087,
    0.085321806371212,
    0.0743890032172203,
    0.10671534389257431,
    -0.04577348381280899,
    0.27184805274009705,
    -0.2545455992221832,
    0.24207571148872375,
    -0.06462734192609787,
)


def gelu_parts(u):
    bell = jnp.exp(-0.5 * u * u)
    t = 1.0 / (1.0 + (0.3 * math.sqrt(0.5)) * jnp.abs(u))
    series = ERFC_SERIES[8]
    for coefficient in ERFC_SERIES[7::-1]:
        series = series * t + coefficient
    tail = series * t * bell
    share = jnp.where(u < 0.0, tail, 1.0 - tail)
    return u * share, share + u * (bell * (1.0 / math.sqrt(2.0 * math.pi)))


def norm_parts(values):
    centred = values - jnp.mean(values, axis=1, keepdims=True)
    spread = jnp.mean(centred * centred, axis=1, keepdims=True)
    scale = lax.rsqrt(spread + NORM_EPS)
    return centred * scale, scale


def forward_kernel(
    order_ref,
    lengths_ref,
    state_lengths_ref,
    tokens_ref,
    att_ref,
    exp_ref,
    shr_ref,
    e_ref,
    cot_ref,
    par,
    x_out,
    full_ref,
    q_out,
    k_out,
    v_out,
    o_out,
    lse_out,
    cq_out,
    ck_out,
    cv_out,
    oc_out,
    lse_cross_out,
    r1_out,
    r2_out,
    h1_out,
    h2_out,
    g_out,
    gp_out,
    y_out,
    dm_out,
    d_third_out,
    small_out,
    pool,
    acc,
    held,
    o_t,
    lse_held,
    states,
    x_held,
    spread,
    picked,
    piece_ref,
    att_in,
    exp_in,
    shr_in,
    prepare_sem,
    load_sem,
    store_sem,
    state_sem,
    acc_sem,
    spread_send,
    spread_recv,
    back_send,
    back_recv,
    *gather_sem,
):
    places = neighbours()
    refs = (piece_ref, full_ref) + gather_sem
    planner = GatherPlanner(GATHERED)
    me = lax.axis_index("rep") * 4 + places[3]
    length = lengths_ref[me]

    core, x, y = places[0:3]

    def own_row(parity):
        a = x + parity * (y - x)
        b = y + parity * (x - y)
        return core * 128 + a * 64 + b * 32

    prepare = []
    for p in range(2):
        for lane in range(8):
            rows = pl.ds(pl.multiple_of(own_row(p) * 8, 256), 256)
            prepare.append((att_ref.at[rows, pl.ds(lane * 128, 128)], att_in.at[p, lane]))
        rows = pl.ds(pl.multiple_of(own_row(p), 32), 32)
        prepare.append((exp_ref.at[rows, :], exp_in.at[p]))
    for j in range(4):
        rows = pl.ds(pl.multiple_of(j * 256 + own_row(SHRINK_AT[j] % 2), 32), 32)
        prepare.append((shr_ref.at[rows, :], shr_in.at[j]))
    prepare = [
        pltpu.make_async_copy(source, target, prepare_sem.at[i])
        for i, (source, target) in enumerate(prepare)
    ]

    def make_pieces():
        for copy in prepare:
            copy.wait()
        for c in range(8):
            for lane in range(8):
                tile = att_in[c % 2, lane, pl.ds(c, 32, stride=8), :]
                piece_ref[c, :, lane * 128 : lane * 128 + 128] = tile.astype(jnp.bfloat16)
        for j in range(4):
            c = EXPAND_AT[j]
            for s in range(4):
                start = s * 1024 + j * 256
                tile = exp_in[c % 2, :, start : start + 256]
                piece_ref[c, :, s * 256 : s * 256 + 256] = tile.astype(jnp.bfloat16)
            piece_ref[SHRINK_AT[j]] = shr_in[j].astype(jnp.bfloat16)

    def device(offset):
        j = lax.rem(me + offset, 32)
        return j, (j // 4, j % 4)

    def spread_copy(offset):
        j, target = device(offset)
        return remote(
            tokens_ref.at[j],
            spread.at[me],
            spread_send.at[offset],
            spread_recv.at[offset],
            target,
        )

    def back_copy(offset):
        return remote(
            picked.at[offset],
            x_held.at[me],
            back_send.at[offset],
            back_recv.at[offset],
            device(offset)[1],
        )

    def own_spread():
        return pltpu.make_async_copy(tokens_ref.at[me], spread.at[me], spread_recv.at[0])

    def own_back():
        return pltpu.make_async_copy(picked.at[0], x_held.at[me], back_recv.at[0])

    def each_other(act):
        def body(offset, carry):
            act(offset)
            return carry

        lax.fori_loop(1, 32, body, 0)

    def turn_back():
        own_spread().wait()
        each_other(lambda offset: spread_copy(offset).wait())
        picked[0] = spread[order_ref[me]]
        own_back().start()

        def pick(offset):
            picked[offset] = spread[order_ref[device(offset)[0]]]
            back_copy(offset).start()

        each_other(pick)

    def emit_all(events):
        for stage, c in events:
            gather_stage(stage, refs, c, c % 2, places)

    def tick(spent):
        emit_all(planner.tick(spent))

    def load(slot, source):
        return pltpu.make_async_copy(source, pool.at[slot], load_sem.at[slot])

    def store(slot, target):
        return pltpu.make_async_copy(pool.at[slot], target, store_sem.at[slot])

    def product_into(left, right, put):
        def body(i, carry):
            n = pl.multiple_of(i * 256, 256)
            put(n, product(left(), pool[right, :, pl.ds(n, 256)]))
            return carry

        lax.fori_loop(0, 4, body, 0)

    def row(index, n):
        return par[index : index + 1, pl.ds(n, 256)]

    def put_low(slot, offset=None, scale=None):
        def put(n, value):
            if offset is not None:
                value = value + row(offset, n)
            if scale is not None:
                value = value * scale
            pool[slot, :, pl.ds(n, 256)] = value.astype(jnp.bfloat16)

        return put

    def put_acc(offset):
        def put(n, value):
            acc[:, pl.ds(n, 256)] = value + row(offset, n)

        return put

    def load_weight(c, slot):
        target = pool.at[slot].reshape(4, 256, D)
        return pltpu.make_async_copy(full_ref.at[c], target, load_sem.at[slot])

    def weight(c, slot):
        emit_all(planner.until(c))
        return load_weight(c, slot)

    def attend_loop(causal, step, valid, query, key, value, out, spent, rows, key_rows):
        ahead = [planner.tick(spent) for _ in range(8)]
        first_row, count = rows

        def body(i, carry):
            lanes = pl.ds(pl.multiple_of(i * 128, 128), 128)
            attend_pair(
                causal,
                step,
                valid,
                query.at[pl.ds(first_row, count), lanes],
                key.at[pl.ds(0, key_rows), lanes],
                value.at[pl.ds(0, key_rows), lanes],
                out.at[pl.ds(first_row, count), lanes],
                lse_held.at[pl.ds(i, 1)],
                o_t,
                first_row,
            )
            for n in range(8):
                if ahead[n]:

                    @pl.when(i == n)
                    def _(events=ahead[n]):
                        emit_all(events)

            return carry

        lax.fori_loop(0, 8, body, 0)

    TILE = 128

    def over_rows(sums, body):
        zero = jnp.zeros((8, D), jnp.float32)

        def step(i, carry):
            r = pl.multiple_of(i * TILE, TILE)
            place = half_lanes((TILE, 1), 0) + r
            usable = (place < length).astype(jnp.float32)
            terms = body(pl.ds(r, TILE), usable)
            return tuple(c + fold(t) for c, t in zip(carry, terms))

        totals = lax.fori_loop(0, D // TILE, step, (zero,) * sums)
        return [jnp.sum(t, axis=0, keepdims=True) for t in totals]

    lane = half_lanes((1, D), 1)

    def square_at(index, total):
        small_out[17:18, :] += jnp.where(lane == index, jnp.sum(total), 0.0)

    for copy in prepare:
        copy.start()
    barrier = pltpu.get_barrier_semaphore()

    def greet_one(offset):
        pl.semaphore_signal(barrier, inc=1, device_id=device(offset)[1], device_id_type=MESH)

    each_other(greet_one)
    pl.semaphore_wait(barrier, 31)
    own_spread().start()
    each_other(lambda offset: spread_copy(offset).start())
    make_pieces()
    planner.opened = 3
    tick(0.5)
    planner.spend(3.0, z=42.0, x=21.0, y=21.0)
    e_load = pltpu.make_async_copy(e_ref, states.at[2], state_sem.at[2])
    e_load.start()
    load(9, cot_ref).start()
    small_out[...] = jnp.zeros_like(small_out)
    turn_back()
    planner.spend(56.0, z=42.0, x=21.0, y=21.0)
    for i in range(3):
        weight(i, 1 + i).start()
    own_back().wait()
    each_other(lambda offset: back_copy(offset).wait())
    planner.spend(112.0)
    planner.opened = GATHERED
    tick(0.5)
    x_store = pltpu.make_async_copy(x_held, x_out, acc_sem.at[1])
    x_store.start()

    for i, (slot, offset, scale) in enumerate(((4, 0, 0.125), (5, None, None), (6, 1, None))):
        load_weight(i, 1 + i).wait()
        product_into(lambda: x_held[...].reshape(1024, D), 1 + i, put_low(slot, offset, scale))
        store(slot, (q_out, k_out, v_out)[i]).start()
        tick(2.5)
    refs_held = [pool.at[slot] for slot in (4, 5, 6, 7)]
    attend_loop(True, 256, length, *refs_held, 4.5, (0, 1024), 1024)
    store(7, o_out).start()
    lse_copy = pltpu.make_async_copy(lse_held, lse_out, state_sem.at[3])
    lse_copy.start()
    w_copy = weight(3, 1)
    w_copy.start()
    w_copy.wait()
    product_into(lambda: pool[7], 1, put_acc(2))
    tick(2.5)
    store(4, q_out).wait()

    def first_norm(rows, usable):
        held_rows = pl.ds(pl.multiple_of(rows.start // 32, TILE // 32), TILE // 32)
        x = x_held[held_rows].reshape(TILE, D).astype(jnp.float32)
        a = acc[rows, :]
        total = x + a
        acc[rows, :] = total
        h = norm_parts(total)[0] * par[11:12, :] + par[12:13, :]
        held[rows, :] = h
        pool[4, rows, :] = h.astype(jnp.bfloat16)
        return usable * x * x, usable * a * a, usable * h * h

    for index, total in enumerate(over_rows(3, first_norm)):
        square_at(index, total)
    store(4, h1_out).start()
    r1_copy = pltpu.make_async_copy(acc, r1_out, acc_sem.at[0])
    r1_copy.start()
    tick(4.0)

    for c, slot in ((4, 2), (5, 3), (6, 1)):
        weight(c, slot).start()
    store(5, k_out).wait()
    load_weight(4, 2).wait()
    product_into(lambda: pool[4], 2, put_low(5, 3, 0.125))
    store(5, cq_out).start()
    w_copy = weight(7, 2)
    w_copy.start()
    tick(2.5)
    e_load.wait()
    load_weight(5, 3).wait()
    load_weight(6, 1).wait()

    def put_keys(n, value):
        states[0, :, pl.ds(n, 256)] = value.astype(jnp.bfloat16)

    def put_values(n, value):
        states[1, :, pl.ds(n, 256)] = (value + row(4, n)).astype(jnp.bfloat16)

    product_into(lambda: states[2], 3, put_keys)
    product_into(lambda: states[2], 1, put_values)
    state_stores = [
        pltpu.make_async_copy(states.at[0], ck_out, state_sem.at[0]),
        pltpu.make_async_copy(states.at[1], cv_out, state_sem.at[1]),
    ]
    for copy in state_stores:
        copy.start()
    tick(1.0)
    store(6, v_out).wait()
    lse_copy.wait()
    attend_loop(
        False,
        512,
        state_lengths_ref[me],
        pool.at[5],
        states.at[0],
        states.at[1],
        pool.at[6],
        1.6,
        (0, 1024),
        128,
    )
    store(6, oc_out).start()
    lse_copy = pltpu.make_async_copy(lse_held, lse_cross_out, state_sem.at[3])
    lse_copy.start()
    w_copy.wait()
    r1_copy.wait()
    product_into(lambda: pool[6], 2, put_acc(5))
    tick(2.5)
    weight(EXPAND_AT[0], 0).start()
    weight(SHRINK_AT[0], 2).start()
    store(7, o_out).wait()

    def second_norm(rows, usable):
        c = acc[rows, :]
        total = held[rows, :] + c
        acc[rows, :] = total
        h = norm_parts(total)[0] * par[13:14, :] + par[14:15, :]
        held[rows, :] = h
        pool[7, rows, :] = h.astype(jnp.bfloat16)
        return usable * c * c, usable * h * h

    for index, total in enumerate(over_rows(2, second_norm)):
        square_at(3 + index, total)
    store(7, h2_out).start()
    r2_copy = pltpu.make_async_copy(acc, r2_out, acc_sem.at[0])
    r2_copy.start()
    tick(4.0)

    store(4, h1_out).wait()
    store(5, cq_out).wait()
    g_slots, slope_slots = (4, 6), (5, 8)
    r2_copy.wait()
    store(6, oc_out).wait()
    for j in range(5):
        if j > 1:
            store(g_slots[j % 2], g_out.at[j - 2]).wait()
            store(slope_slots[j % 2], gp_out.at[j - 2]).wait()
        if j < 4:
            load_weight(EXPAND_AT[j], j % 2).wait()
        if j > 0:
            load_weight(SHRINK_AT[j - 1], 2 + (j - 1) % 2).wait()

        def body(i, carry, j=j):
            n = pl.multiple_of(i * 256, 256)
            here = pl.ds(n, 256)
            if j < 4:
                offset = par[pl.ds(6 + i, 1), j * 256 : j * 256 + 256]
                u = product(pool[7], pool[j % 2, :, here]) + offset
            if j > 0:
                more = product(pool[g_slots[(j - 1) % 2]], pool[2 + (j - 1) % 2, :, here])
                if j == 1:
                    acc[:, here] = more + row(10, n)
                else:
                    acc[:, here] += more
            if j < 4:
                g, slope = gelu_parts(u)
                pool[g_slots[j % 2], :, here] = g.astype(jnp.bfloat16)
                pool[slope_slots[j % 2], :, here] = slope.astype(jnp.bfloat16)
            return carry

        lax.fori_loop(0, 4, body, 0)
        if j < 4:
            store(g_slots[j % 2], g_out.at[j]).start()
            store(slope_slots[j % 2], gp_out.at[j]).start()
        tick(9.0 if j < 4 else 2.5)
        if j < 3:
            weight(EXPAND_AT[j + 1], (j + 1) % 2).start()
            weight(SHRINK_AT[j + 1], 2 + (j + 1) % 2).start()

    load(9, cot_ref).wait()

    def third_norm(rows, usable):
        m = acc[rows, :]
        unit, scale = norm_parts(held[rows, :] + m)
        gain = par[15:16, :]
        pool[0, rows, :] = (unit * gain + par[16:17, :]).astype(jnp.bfloat16)
        grad = pool[9, rows, :].astype(jnp.float32) * usable
        inner = grad * gain
        first = jnp.mean(inner, axis=1, keepdims=True)
        second = jnp.mean(inner * unit, axis=1, keepdims=True)
        back = scale * (inner - first - unit * second)
        acc[rows, :] = back
        low = back.astype(jnp.bfloat16)
        pool[1, rows, :] = low
        return usable * m * m, grad * unit, grad, low.astype(jnp.float32)

    m_total, gain_sum, shift_sum, offset_sum = over_rows(4, third_norm)
    square_at(5, m_total)
    small_out[15:16, :] = gain_sum
    small_out[16:17, :] = shift_sum
    small_out[10:11, :] = offset_sum
    last = [
        store(0, y_out),
        store(1, dm_out),
        pltpu.make_async_copy(acc, d_third_out, acc_sem.at[0]),
    ]
    for copy in last:
        copy.start()
    for c in range(GATHERED):
        emit_all(planner.until(c))
    for copy in last + state_stores + [lse_copy, x_store]:
        copy.wait()
    store(7, h2_out).wait()
    store(6, g_out.at[3]).wait()
    store(8, gp_out.at[3]).wait()


def forward(scalars, tokens, weights, states, cotangent, params):
    any_space = pl.BlockSpec(memory_space=pl.ANY)
    vmem = pl.BlockSpec(memory_space=pltpu.VMEM)
    shape = jax.ShapeDtypeStruct
    dma = pltpu.SemaphoreType.DMA
    low = jnp.bfloat16
    wide = jnp.float32
    square = shape((1024, D), low)
    square_wide = shape((1024, D), wide)
    lse = shape((8, 8, 1024), wide)
    short = shape((128, D), low)
    blocks = shape((4, 1024, D), low)
    outs = (
        shape((32, 32, D), low),
        shape((GATHERED, 4, 256, D), low),
        square,
        square,
        square,
        square,
        lse,
        square,
        short,
        short,
        square,
        lse,
        square_wide,
        square_wide,
        square,
        square,
        blocks,
        blocks,
        square,
        square,
        square_wide,
        shape((24, D), wide),
    )
    return pl.pallas_call(
        forward_kernel,
        out_shape=outs,
        in_specs=[SCALARS] * 3 + [any_space] * 6 + [vmem],
        out_specs=(any_space,) * 21 + (vmem,),
        scratch_shapes=[
            pltpu.VMEM((10, 1024, D), low),
            pltpu.VMEM((1024, D), wide),
            pltpu.VMEM((1024, D), wide),
            pltpu.VMEM((128, 1024), wide),
            pltpu.VMEM((8, 8, 1024), wide),
            pltpu.VMEM((3, 128, D), low),
            pltpu.VMEM((32, 32, D), low),
            pltpu.VMEM((32, 32, D), low),
            pltpu.VMEM((32, 32, D), low),
            pltpu.VMEM((GATHERED, 32, D), low),
            pltpu.VMEM((2, 8, 256, 128), wide),
            pltpu.VMEM((2, 32, FF), wide),
            pltpu.VMEM((4, 32, D), wide),
            dma((22,)),
            dma((10,)),
            dma((10,)),
            dma((4,)),
            dma((2,)),
            dma((32,)),
            dma((32,)),
            dma((32,)),
            dma((32,)),
        ]
        + gather_sems(GATHERED),
        compiler_params=pltpu.CompilerParams(
            collective_id=3, has_side_effects=True, vmem_limit_bytes=62 * MIB
        ),
    )(*scalars, tokens.reshape(32, 32, D), *weights, states, cotangent, params)


def add_blocks(target, first, second, planes, rows, step):
    per_plane = rows // step

    def body(i, carry):
        s = i // per_plane
        r = pl.multiple_of((i % per_plane) * step, step)
        target(s, r, first(s, r) + second(s, r))
        return carry

    lax.fori_loop(0, planes * per_plane, body, 0)


POOL = 8
G_SLOTS = 3
R_SLOTS = 4
PLAN = {"core": 3.5, "load": 1.8, "a": 13.5, "b": 7.5, "z": 7.5, "bb": 3.0, "ba": 5.0, "bc": 2.5}


class Planner:
    def __init__(self):
        self.now = 0.0
        self.links = {"core": 0.0, "x": 0.0, "y": 0.0, "z": 0.0, "load": 0.0}
        self.stage = {}
        self.ready = {}

    def link_of(self, c, stage):
        first, second = ("x", "y") if c % 2 == 0 else ("y", "x")
        return {
            0: ("core", "core"),
            1: ("load", "load"),
            2: (first, "a"),
            3: (second, "b"),
            4: ("z", "z"),
            5: (second, "bb"),
            6: (first, "ba"),
            7: ("core", "bc"),
            8: (None, None),
        }[stage]

    def can(self, c):
        stage = self.stage[c]
        if stage > 8:
            return False
        if stage == 1 and c >= R_SLOTS and self.stage[c - R_SLOTS] <= 3:
            return False
        return True

    def emit(self, c):
        stage = self.stage[c]
        link, kind = self.link_of(c, stage)
        self.now = max(self.now, self.ready[c]) + {2: 0.8, 3: 0.5, 4: 0.3, 5: 0.2}.get(stage, 0.1)
        if link is not None:
            begin = max(self.now, self.links[link])
            span = PLAN[kind]
            self.links[link] = begin + span - 1.0
            self.ready[c] = begin + span
        self.stage[c] = stage + 1
        return (stage, c)

    def tick(self, spent):
        self.now += spent
        events = []
        progress = True
        while progress:
            progress = False
            for c in sorted(self.stage):
                if self.can(c) and self.ready[c] <= self.now:
                    events.append(self.emit(c))
                    progress = True
        return events

    def produce(self, c):
        self.stage[c] = 0
        self.ready[c] = self.now
        return [self.emit(c)]

    def until(self, done):
        events = []
        while not done():
            choices = [c for c in sorted(self.stage) if self.can(c)]
            c = min(choices, key=lambda i: (self.ready[i], i))
            events.append(self.emit(c))
        return events

    def free_slot(self, c):
        before = c - G_SLOTS
        if before < 0:
            return []
        return self.until(lambda: self.stage[before] > 2)

    def drain(self, tasks, spent):
        events = []
        waiting = list(tasks)
        while waiting or any(s <= 8 for s in self.stage.values()):
            choices = [c for c in sorted(self.stage) if self.can(c)]
            best = min(choices, key=lambda i: (self.ready[i], i)) if choices else None
            open_tasks = [t for t in waiting if all(self.stage[c] > 8 for c in t[0])]
            if open_tasks and (best is None or self.ready[best] > self.now):
                task = open_tasks[0]
                waiting.remove(task)
                self.now += spent
                events.append(("task", task[1]))
            else:
                events.append(self.emit(best))
        return events


def backward_kernel(
    lengths_ref,
    state_lengths_ref,
    dm_ref,
    d_third_ref,
    g_ref,
    gp_ref,
    full_ref,
    h2_ref,
    h1_ref,
    x_in_ref,
    e_ref,
    oc_ref,
    o_ref,
    r1_ref,
    r2_ref,
    q_ref,
    k_ref,
    v_ref,
    cq_ref,
    ck_ref,
    cv_ref,
    lse_ref,
    lse_cross_ref,
    gains_ref,
    small_ref,
    rows_ref,
    cols_ref,
    token_grad_ref,
    state_grad_ref,
    out_ref,
    totals_ref,
    rows_out,
    cols_out,
    scale_out,
    half,
    pool,
    acc,
    made,
    summed,
    quarter,
    eighth,
    pieces,
    stream,
    dq_t,
    dk_sum,
    dv_sum,
    lse_held,
    states,
    states_t,
    small,
    small_in,
    small_sum,
    small_z,
    part,
    whole,
    load_sem,
    stream_sem,
    state_sem,
    half_sem,
    scan_sem,
    line_send_sem,
    line_recv_sem,
    send_sem,
    recv_sem,
    z_send_sem,
    z_recv_sem,
    place_sem,
    small_send_sem,
    small_recv_sem,
):
    core, x, y, z, other_core, other_x, other_y, others_z = neighbours()
    me = lax.axis_index("rep") * 4 + z
    kept = pl.multiple_of(core * 128, 128)
    given = pl.multiple_of(128 - core * 128, 128)
    planner = Planner()
    place_of = (12, 8, 13, 9, 14, 10, 15, 11, 7, 4, 5, 6, 3, 0, 1, 2)

    def axes(c):
        if c % 2 == 0:
            return x, y, other_x, other_y
        return y, x, other_y, other_x

    def core_copy(c):
        source = made.at[c % G_SLOTS, :, pl.ds(given, 128), :]
        return remote(source, half.at[c], send_sem.at[0, c], recv_sem.at[0, c], other_core)

    def half_copy(c):
        return pltpu.make_async_copy(
            half.at[c], summed.at[c % R_SLOTS], half_sem.at[c % R_SLOTS]
        )

    def first_copy(c):
        a, b, first, second = axes(c)
        rows = pl.ds(pl.multiple_of(64 - a * 64, 64), 64)
        source = summed.at[c % R_SLOTS, :, rows, :]
        return remote(source, quarter.at[c], send_sem.at[1, c], recv_sem.at[1, c], first)

    def second_copy(c):
        a, b, first, second = axes(c)
        rows = pl.ds(pl.multiple_of(32 - b * 32, 32), 32)
        source = quarter.at[c, :, rows, :]
        return remote(source, eighth.at[c], send_sem.at[2, c], recv_sem.at[2, c], second)

    def z_copy(c, d):
        device = others_z[d]
        return remote(
            eighth.at[c, device[1]],
            pieces.at[c, d],
            z_send_sem.at[c, d],
            z_recv_sem.at[c, d],
            device,
        )

    def own_rows_of(c):
        a, b, first, second = axes(c)
        return pl.ds(pl.multiple_of(core * 128 + a * 64 + b * 32, 32), 32)

    def place_copy(c):
        return pltpu.make_async_copy(
            pieces.at[c, 0], out_ref.at[place_of[c], own_rows_of(c), :], place_sem.at[c]
        )

    def back_second(c):
        device = axes(c)[3]
        target = out_ref.at[place_of[c], own_rows_of(c), :]
        return remote(pieces.at[c, 0], target, send_sem.at[3, c], recv_sem.at[3, c], device)

    def back_first(c):
        a, b, first, second = axes(c)
        block = out_ref.at[place_of[c], pl.ds(pl.multiple_of(core * 128 + a * 64, 64), 64), :]
        return remote(block, block, send_sem.at[4, c], recv_sem.at[4, c], first)

    def back_core(c):
        block = out_ref.at[place_of[c], pl.ds(kept, 128), :]
        return remote(block, block, send_sem.at[5, c], recv_sem.at[5, c], other_core)

    def emit(stage, c):
        a, b, first, second = axes(c)
        slot = c % R_SLOTS
        if stage == 0:
            core_copy(c).start()
        if stage == 1:
            if c >= R_SLOTS:
                first_copy(c - R_SLOTS).wait_send()
            core_copy(c).wait_recv()
            half_copy(c).start()
        if stage == 2:
            half_copy(c).wait()

            def put(s, r, value):
                summed[slot, s, pl.ds(r, 32), :] = value

            add_blocks(
                put,
                lambda s, r: summed[slot, s, pl.ds(r, 32), :],
                lambda s, r: made[c % G_SLOTS, s, pl.ds(pl.multiple_of(kept + r, 32), 32), :],
                4,
                128,
                32,
            )
            first_copy(c).start()
            core_copy(c).wait_send()
        if stage == 3:
            first_copy(c).wait_recv()

            def put(s, r, value):
                quarter[c, s, pl.ds(r, 32), :] = value

            add_blocks(
                put,
                lambda s, r: quarter[c, s, pl.ds(r, 32), :],
                lambda s, r: summed[slot, s, pl.ds(pl.multiple_of(a * 64 + r, 32), 32), :],
                4,
                64,
                32,
            )
            second_copy(c).start()
        if stage == 4:
            second_copy(c).wait_recv()

            def put(s, r, value):
                eighth[c, s, pl.ds(r, 32), :] = value

            add_blocks(
                put,
                lambda s, r: eighth[c, s, pl.ds(r, 32), :],
                lambda s, r: quarter[c, s, pl.ds(pl.multiple_of(b * 32 + r, 32), 32), :],
                4,
                32,
                32,
            )
            for d in range(3):
                z_copy(c, d).start()
        if stage == 5:
            for d in range(3):
                z_copy(c, d).wait_recv()
            total = eighth[c, z].astype(jnp.float32)
            for d in range(3):
                total = total + pieces[c, d].astype(jnp.float32)
            pieces[c, 0] = total.astype(jnp.bfloat16)
            back_second(c).start()
            place_copy(c).start()
        if stage == 6:
            place_copy(c).wait()
            back_second(c).wait_recv()
            back_first(c).start()
        if stage == 7:
            back_first(c).wait_recv()
            back_core(c).start()
        if stage == 8:
            back_core(c).wait()
            back_first(c).wait_send()
            back_second(c).wait_send()
            for d in range(3):
                z_copy(c, d).wait_send()
            second_copy(c).wait_send()
            if c >= CHUNKS - R_SLOTS:
                first_copy(c).wait_send()

    def emit_all(events):
        for stage, c in events:
            emit(stage, c)

    def tick(spent):
        emit_all(planner.tick(spent))

    def produced(c, spent):
        planner.now += spent
        emit_all(planner.produce(c))
        emit_all(planner.tick(0.0))

    def load(slot, source):
        return pltpu.make_async_copy(source, pool.at[slot], load_sem.at[slot])

    def state_load(index, source):
        return pltpu.make_async_copy(source, states.at[index], state_sem.at[index])

    def turn_tile(target, source):
        def turn(n):
            pool[target, pl.ds(n, 256), :] = pool[source, :, pl.ds(n, 256)].T

        return turn

    def transpose_into(target, source):
        turn = turn_tile(target, source)

        def body(i, carry):
            turn(pl.multiple_of(i * 256, 256))
            return carry

        lax.fori_loop(0, 4, body, 0)

    def product_nn(left, right, put, beside=None):
        def body(i, carry):
            n = pl.multiple_of(i * 256, 256)
            if beside is not None:
                beside(n)
            put(n, product(left(), right(n)))
            return carry

        lax.fori_loop(0, 4, body, 0)

    def product_nt(left, right, put, beside=None):
        def body(i, carry):
            n = pl.multiple_of(i * 256, 256)
            if beside is not None:
                beside(n)
            put(
                n,
                lax.dot_general(
                    left(),
                    right(n),
                    (((1,), (1,)), ((), ())),
                    preferred_element_type=jnp.float32,
                ),
            )
            return carry

        lax.fori_loop(0, 4, body, 0)

    def columns_of(slot):
        return lambda n: pool[slot, :, pl.ds(n, 256)]

    def rows_of(slot):
        return lambda n: pool[slot, pl.ds(n, 256), :]

    def weight_grad(slot_in_made, left, right, beside=None):
        def put(n, value):
            low = value.astype(jnp.bfloat16).reshape(4, 256, 256)
            made[slot_in_made, :, :, pl.ds(n, 256)] = low

        product_nn(left, right, put, beside)

    def add_to_acc(n, value):
        acc[:, pl.ds(n, 256)] += value

    def put_in(slot):
        def put(n, value):
            pool[slot, :, pl.ds(n, 256)] = value.astype(jnp.bfloat16)

        return put

    def norm_back(source, gain_row, gain_at, shift_at, offset_at, target):
        tiles = 8
        rows = 1024 // tiles

        def fetch(i):
            place = pl.ds(pl.multiple_of(i * rows, rows), rows)
            return pltpu.make_async_copy(
                source.at[place, :], stream.at[i % 2], stream_sem.at[i % 2]
            )

        fetch(0).start()

        def body(i, carry):
            gain_sum, shift_sum, offset_sum = carry

            @pl.when(i + 1 < tiles)
            def _():
                fetch(i + 1).start()

            fetch(i).wait()
            r = pl.multiple_of(i * rows, rows)
            values = stream[i % 2]
            centred = values - jnp.mean(values, axis=1, keepdims=True)
            spread = jnp.mean(centred * centred, axis=1, keepdims=True)
            scale = lax.rsqrt(spread + NORM_EPS)
            unit = centred * scale
            grad = acc[pl.ds(r, rows), :]
            inner = grad * gains_ref[gain_row : gain_row + 1, :]
            first = jnp.mean(inner, axis=1, keepdims=True)
            second = jnp.mean(inner * unit, axis=1, keepdims=True)
            back = scale * (inner - first - unit * second)
            acc[pl.ds(r, rows), :] = back
            low = back.astype(jnp.bfloat16)
            pool[target, pl.ds(r, rows), :] = low
            return (
                gain_sum + fold(grad * unit),
                shift_sum + fold(grad),
                offset_sum + fold(low.astype(jnp.float32)),
            )

        zero = jnp.zeros((8, D), jnp.float32)
        sums = lax.fori_loop(0, tiles, body, (zero, zero, zero))
        for row, value in zip((gain_at, shift_at, offset_at), sums):
            small[row : row + 1, :] = jnp.sum(value, axis=0, keepdims=True)

    greet([other_core, other_x, other_y] + others_z)
    load(0, dm_ref).start()
    load(6, h2_ref).start()
    load(2, full_ref.at[SHRINK_AT[0]]).start()
    load(3, gp_ref.at[0]).start()
    load(4, g_ref.at[0]).start()
    load(5, full_ref.at[EXPAND_AT[0]]).start()
    acc_load = pltpu.make_async_copy(d_third_ref, acc, place_sem.at[0])
    acc_load.start()
    small[...] = small_ref[...]
    load(6, h2_ref).wait()
    transpose_into(1, 6)
    load(0, dm_ref).wait()
    acc_load.wait()

    planner.now = 4.0
    plan = []
    for j in range(4):
        entry = []
        planner.now += 3.5
        entry.append(planner.tick(0.0) + planner.free_slot(2 * j))
        planner.now += 2.5
        entry.append(planner.produce(2 * j) + planner.tick(0.0) + planner.free_slot(2 * j + 1))
        planner.now += 2.5
        entry.append(planner.produce(2 * j + 1) + planner.tick(0.0))
        entry.append(planner.tick(2.5))
        plan.append(entry)

    def emit_planned(j, place):
        for n in range(4):
            events = plan[n][place]
            if events:

                @pl.when(j == n)
                def _(events=events):
                    emit_all(events)

    def block(j, carry):
        last = j == 3
        load(2, full_ref.at[SHRINK_AT[0]]).wait()
        load(3, gp_ref.at[0]).wait()

        def put_pre(n, value):
            low = (value * pool[3, :, pl.ds(n, 256)].astype(jnp.float32)).astype(jnp.bfloat16)
            pool[7, :, pl.ds(n, 256)] = low
            small[pl.ds(6 + n // 256, 1), pl.ds(pl.multiple_of(j * 256, 256), 256)] = jnp.sum(
                low.astype(jnp.float32), axis=0, keepdims=True
            )

        load(4, g_ref.at[0]).wait()
        product_nt(lambda: pool[0], rows_of(2), put_pre, turn_tile(6, 4))

        @pl.when(jnp.logical_not(last))
        def _():
            load(2, full_ref.at[SHRINK_AT[0] + 2 * (j + 1) - (j + 1) // 3]).start()
            load(3, gp_ref.at[j + 1]).start()

        @pl.when(last)
        def _():
            load(2, full_ref.at[7]).start()
            load(3, cq_ref).start()

        emit_planned(j, 0)

        @pl.when(jnp.logical_not(last))
        def _():
            load(4, g_ref.at[j + 1]).start()

        @pl.when(last)
        def _():
            load(4, oc_ref).start()

        weight_grad((2 * j) % G_SLOTS, lambda: pool[6], columns_of(0))
        emit_planned(j, 1)
        weight_grad((2 * j + 1) % G_SLOTS, lambda: pool[1], columns_of(7))
        emit_planned(j, 2)
        load(5, full_ref.at[EXPAND_AT[0]]).wait()
        product_nt(lambda: pool[7], rows_of(5), add_to_acc)

        @pl.when(jnp.logical_not(last))
        def _():
            load(5, full_ref.at[EXPAND_AT[1] + 2 * j]).start()

        @pl.when(last)
        def _():
            load(5, full_ref.at[4]).start()

        emit_planned(j, 3)
        return carry

    lax.fori_loop(0, 4, block, 0)

    load(7, h1_ref).start()
    state_loads = [state_load(0, ck_ref), state_load(1, cv_ref), state_load(2, e_ref)]
    for copy in state_loads:
        copy.start()
    lse_load = pltpu.make_async_copy(lse_cross_ref, lse_held, state_sem.at[3])
    lse_load.start()
    norm_back(r2_ref, 13, 13, 14, 5, 0)
    tick(4.0)
    load(4, oc_ref).wait()
    load(2, full_ref.at[7]).wait()
    product_nt(lambda: pool[0], rows_of(2), put_in(4), turn_tile(6, 4))
    load(2, full_ref.at[3]).start()
    tick(2.5)
    emit_all(planner.free_slot(8))
    load(7, h1_ref).wait()
    weight_grad(8 % G_SLOTS, lambda: pool[6], columns_of(0), turn_tile(1, 7))
    load(6, o_ref).start()
    load(7, full_ref.at[5]).start()
    produced(8, 2.5)
    load(3, cq_ref).wait()
    for copy in state_loads:
        copy.wait()
    lse_load.wait()

    def attend_loop(causal, step, length, query, key, value, grad, rows, spent, span=(0, 8)):
        ahead = {n: planner.tick(spent) for n in range(*span)}

        def body(i, carry):
            lanes = pl.ds(pl.multiple_of(i * 128, 128), 128)

            def sums(dq, dv):
                small[rows[0] : rows[0] + 1, lanes] = dq
                small[rows[1] : rows[1] + 1, lanes] = dv

            attend_back_pair(
                causal,
                step,
                length,
                query.at[:, lanes],
                key.at[:, lanes],
                value.at[:, lanes],
                grad.at[:, lanes],
                lse_held.at[pl.ds(i, 1)],
                query.at[:, lanes],
                key.at[:, lanes],
                value.at[:, lanes],
                sums,
                dq_t,
                dk_sum,
                dv_sum,
            )
            for n in range(*span):
                if ahead[n]:

                    @pl.when(i == n)
                    def _(events=ahead[n]):
                        emit_all(events)

            return carry

        lax.fori_loop(*span, body, 0)

    attend_loop(
        False,
        512,
        state_lengths_ref[me],
        pool.at[3],
        states.at[0],
        states.at[1],
        pool.at[4],
        (3, 4),
        2.0,
    )
    lse_load = pltpu.make_async_copy(lse_ref, lse_held, state_sem.at[3])
    lse_load.start()
    emit_all(planner.free_slot(9))
    weight_grad(9 % G_SLOTS, lambda: pool[1], columns_of(3))
    produced(9, 2.5)
    load(5, full_ref.at[4]).wait()
    load(6, o_ref).wait()
    product_nt(lambda: pool[3], rows_of(5), add_to_acc, turn_tile(1, 6))
    load(6, x_in_ref).start()
    load(5, full_ref.at[6]).start()
    load(3, q_ref).start()
    tick(2.5)
    states_t[...] = states[2].T
    for c, index in ((10, 0), (11, 1)):
        emit_all(planner.free_slot(c))
        weight_grad(
            c % G_SLOTS, lambda: states_t[...], lambda n, i=index: states[i, :, pl.ds(n, 256)]
        )
        produced(c, 1.0)
    load(7, full_ref.at[5]).wait()
    load(5, full_ref.at[6]).wait()

    def state_part(n):
        dims = (((1,), (1,)), ((), ()))
        return lax.dot_general(
            states[0], pool[7, pl.ds(n, 256), :], dims, preferred_element_type=jnp.float32
        ) + lax.dot_general(
            states[1], pool[5, pl.ds(n, 256), :], dims, preferred_element_type=jnp.float32
        )

    def put_state(i, carry):
        n = pl.multiple_of(i * 256, 256)
        state_grad_ref[:, pl.ds(n, 256)] = state_part(n).astype(jnp.bfloat16)
        return carry

    lax.fori_loop(0, 4, put_state, 0)
    load(5, k_ref).start()
    load(7, v_ref).start()
    tick(1.0)

    norm_back(r1_ref, 11, 11, 12, 2, 0)
    tick(4.0)
    emit_all(planner.free_slot(12))
    weight_grad(12 % G_SLOTS, lambda: pool[1], columns_of(0))
    produced(12, 2.5)
    load(2, full_ref.at[3]).wait()
    load(6, x_in_ref).wait()
    product_nt(lambda: pool[0], rows_of(2), put_in(4), turn_tile(1, 6))
    load(0, full_ref.at[0]).start()
    load(2, full_ref.at[1]).start()
    load(6, full_ref.at[2]).start()
    tick(2.5)
    load(3, q_ref).wait()
    load(5, k_ref).wait()
    load(7, v_ref).wait()
    lse_load.wait()
    def self_heads(span):
        refs = [pool.at[slot] for slot in (3, 5, 7, 4)]
        attend_loop(True, 256, lengths_ref[me], *refs, (0, 1), 5.0, span)

    def query_key_grad(c, half_of):
        def put(i, carry):
            n = pl.multiple_of((i % 2) * 256 + 512 * half_of, 256)
            value = product(pool[1], pool[3 + 2 * (i // 2), :, pl.ds(n, 256)])
            low = value.astype(jnp.bfloat16).reshape(4, 256, 256)
            made[c % G_SLOTS, :, :, pl.ds(pl.multiple_of(i * 256, 256), 256)] = low
            return carry

        emit_all(planner.free_slot(c))
        lax.fori_loop(0, 4, put, 0)
        produced(c, 2.5)

    self_heads((0, 4))
    query_key_grad(13, 0)
    self_heads((4, 8))

    def small_copy(k):
        source = small if k == 0 else small_sum.at[k - 1]
        device = (other_core, other_x, other_y)[k]
        return remote(source, small_in.at[k], small_send_sem.at[k], small_recv_sem.at[k], device)

    def small_z_copy(d):
        return remote(
            small_sum.at[2],
            small_z.at[z],
            small_send_sem.at[3 + d],
            small_recv_sem.at[3 + d],
            others_z[d],
        )

    def small_step(k):
        small_copy(k).wait()
        before = small[...] if k == 0 else small_sum[k - 1]
        small_sum[k] = before + small_in[k]
        if k < 2:
            small_copy(k + 1).start()
        else:
            small_z[z] = small_sum[2]
            for d in range(3):
                small_z_copy(d).start()

    small_copy(0).start()
    emit_all(planner.free_slot(14))
    weight_grad(14 % G_SLOTS, lambda: pool[1], columns_of(7))
    produced(14, 2.5)
    small_step(0)
    query_key_grad(15, 1)
    small_step(1)
    load(0, full_ref.at[0]).wait()
    product_nt(lambda: pool[3], rows_of(0), add_to_acc)
    tick(2.5)
    small_step(2)
    load(2, full_ref.at[1]).wait()
    product_nt(lambda: pool[5], rows_of(2), add_to_acc)
    tick(2.5)
    for d in range(3):
        small_z_copy(d).wait()
    totals_ref[...] = (small_z[0] + small_z[1]) + (small_z[2] + small_z[3])
    load(6, full_ref.at[2]).wait()

    def put_input(n, value):
        total = acc[:, pl.ds(n, 256)] + value
        pool[4, :, pl.ds(n, 256)] = total.astype(jnp.bfloat16)

    product_nt(lambda: pool[7], rows_of(6), put_input)
    token_copy = pltpu.make_async_copy(pool.at[4], token_grad_ref, load_sem.at[4])
    token_copy.start()
    tick(2.5)

    part[...] = jnp.zeros_like(part)

    def spot(place):
        return (0, 1, 2, 6)[place // 4], (place % 4) * 256

    def scan_load(place):
        slot, row = spot(place)
        return pltpu.make_async_copy(
            out_ref.at[place], pool.at[slot, pl.ds(row, 256), :], scan_sem.at[place]
        )

    scans = {}
    for i in range(2):
        scans[i] = ([(0, 512 * i, 512, i, 0), (2, 512 * i, 512, i, 512)], i, (13, 128 * i))
    for i in range(2, 8):
        scans[i] = ([(1 if i == 2 else i, 0, D, i, 0)], i, (13, 128 * i))
    scans[8] = ([(8 + i, 0, D, 8 + i, 0) for i in range(4)], 8, (14, 0))
    for i in range(4):
        scans[9 + i] = ([(12 + i, 0, D, 12, 0)], 9 + i, (14, 128))

    def scan(name):
        sources, row_lane, (total_row, total_lane) = scans[name]
        width = float(sum(source[2] for source in sources))
        step = 64 if name == 8 else 256

        def body(i, carry):
            cols, weights, total = carry
            r = pl.multiple_of(i * step, step)
            squares = []
            for place, lane, lanes, _, _ in sources:
                slot, row = spot(place)
                tile = pool[slot, pl.ds(row + r, step), lane : lane + lanes]
                squares.append(jnp.square(tile.astype(jnp.float32)))
            row_sum = sum(jnp.sum(square, axis=1, keepdims=True) for square in squares)
            rows = DECAY_RATE * rows_ref[pl.ds(r, step), row_lane : row_lane + 1] + (
                1.0 - DECAY_RATE
            ) * (row_sum / width + FACTOR_EPS)
            rows_out[pl.ds(r, step), row_lane : row_lane + 1] = rows
            inverse = 1.0 / rows
            cols = [c + fold(s) for c, s in zip(cols, squares)]
            weights = [w + fold(s * inverse) for w, s in zip(weights, squares)]
            return cols, weights, total + fold(rows)

        zeros = [jnp.zeros((8, source[2]), jnp.float32) for source in sources]
        cols, weights, total = lax.fori_loop(
            0, 256 // step, body, (zeros, zeros, jnp.zeros((8, 1), jnp.float32))
        )
        for (_, _, lanes, slot, lane), col, weighted in zip(sources, cols, weights):
            here = slice(lane, lane + lanes)
            part[slot : slot + 1, here] += jnp.sum(col, axis=0, keepdims=True)
            part[16 + slot : 17 + slot, here] += jnp.sum(weighted, axis=0, keepdims=True)
        part[total_row : total_row + 1, total_lane : total_lane + 128] += jnp.broadcast_to(
            jnp.sum(total), (1, 128)
        )

    chunk_at = {place: c for c, place in enumerate(place_of)}
    tasks = [
        ([chunk_at[source[0]] for source in scans[name][0]], name)
        for name in (9, 10, 11, 12, 8, 7, 4, 5, 6, 3, 2, 0, 1)
    ]
    loaded = set()
    for c in range(CHUNKS):
        if planner.stage[c] > 8:
            scan_load(place_of[c]).start()
    for first, second in planner.drain(tasks, 1.5):
        if first != "task":
            emit(first, second)
            if first == 8:
                scan_load(place_of[second]).start()
            continue
        for source in scans[second][0]:
            if source[0] not in loaded:
                loaded.add(source[0])
                scan_load(source[0]).wait()
        scan(second)
    total = line_sum(part, whole, line_send_sem, line_recv_sem, z, others_z)
    row_counts = [D] * 12 + [FF]
    means = [total[13:14, 128 * i : 128 * i + 1] / D for i in range(8)]
    means = means + [total[14:15, 0:1] / D] * 4 + [total[14:15, 128:129] / FF]
    cols_new, quotients = [], []
    for slot in range(13):
        new = DECAY_RATE * cols_ref[slot : slot + 1, :] + (1.0 - DECAY_RATE) * (
            total[slot : slot + 1] / row_counts[slot] + FACTOR_EPS
        )
        cols_new.append(new)
        quotients.append(jnp.sum(total[16 + slot : 17 + slot] / new, axis=1, keepdims=True))
        cols_out[slot : slot + 1, :] = new
    expand_quotient = quotients[8] + quotients[9] + quotients[10] + quotients[11]
    for slot in range(13):
        if slot < 8:
            mean_square = means[slot] * quotients[slot] / (D * D)
            rate = STEP_RATE * (OUT_GAIN if slot % 4 == 3 else 1.0)
        else:
            quotient = expand_quotient if slot < 12 else quotients[12]
            mean_square = means[slot] * quotient / (D * FF)
            rate = STEP_RATE
        factor = rate / jnp.maximum(1.0, jnp.sqrt(mean_square) / CLIP_LEVEL)
        scale_out[slot : slot + 1, :] = lax.rsqrt(cols_new[slot] / means[slot]) * factor
    token_copy.wait()


def backward(scalars, held, gains, small, factor_rows, factor_cols):
    any_space = pl.BlockSpec(memory_space=pl.ANY)
    vmem = pl.BlockSpec(memory_space=pltpu.VMEM)
    shape = jax.ShapeDtypeStruct
    dma = pltpu.SemaphoreType.DMA
    low = jnp.bfloat16
    wide = jnp.float32
    rows = small.shape[0]
    return pl.pallas_call(
        backward_kernel,
        out_shape=(
            shape((1024, D), low),
            shape((128, D), low),
            shape((CHUNKS, 256, D), low),
            shape(small.shape, wide),
            shape((256, 128), wide),
            shape((16, D), wide),
            shape((16, D), wide),
            shape((CHUNKS, 4, 128, D), low),
        ),
        in_specs=[SCALARS] * 2 + [any_space] * len(held) + [vmem] * 4,
        out_specs=(any_space, vmem, any_space, vmem, vmem, vmem, vmem, any_space),
        scratch_shapes=[
            pltpu.VMEM((POOL, 1024, D), low),
            pltpu.VMEM((1024, D), wide),
            pltpu.VMEM((G_SLOTS, 4, 256, D), low),
            pltpu.VMEM((R_SLOTS, 4, 128, D), low),
            pltpu.VMEM((CHUNKS, 4, 64, D), low),
            pltpu.VMEM((CHUNKS, 4, 32, D), low),
            pltpu.VMEM((CHUNKS, 3, 32, D), low),
            pltpu.VMEM((2, 128, D), wide),
            pltpu.VMEM((128, 1024), wide),
            pltpu.VMEM((2, 1024, 128), wide),
            pltpu.VMEM((2, 1024, 128), wide),
            pltpu.VMEM((8, 8, 1024), wide),
            pltpu.VMEM((3, 128, D), low),
            pltpu.VMEM((D, 128), low),
            pltpu.VMEM((rows, D), wide),
            pltpu.VMEM((3, rows, D), wide),
            pltpu.VMEM((3, rows, D), wide),
            pltpu.VMEM((4, rows, D), wide),
            pltpu.VMEM((32, D), wide),
            pltpu.VMEM((4, 32, D), wide),
            dma((POOL,)),
            dma((2,)),
            dma((4,)),
            dma((R_SLOTS,)),
            dma((CHUNKS,)),
            dma((3,)),
            dma((3,)),
            dma((6, CHUNKS)),
            dma((6, CHUNKS)),
            dma((CHUNKS, 3)),
            dma((CHUNKS, 3)),
            dma((CHUNKS,)),
            dma((6,)),
            dma((6,)),
        ],
        compiler_params=pltpu.CompilerParams(
            collective_id=0, has_side_effects=True, vmem_limit_bytes=62 * MIB
        ),
    )(*scalars, *held, gains, small, factor_rows, factor_cols)[0:7]


def line_sum(part, whole, send_sem, recv_sem, z, others_z):
    copies = [
        remote(part, whole.at[z], send_sem.at[d], recv_sem.at[d], others_z[d]) for d in range(3)
    ]
    for copy in copies:
        copy.start()
    whole[z] = part[...]
    for copy in copies:
        copy.wait()
    return (whole[0] + whole[1]) + (whole[2] + whole[3])


def update_attention_kernel(
    grad_ref, weight_ref, rows_ref, scale_ref, grad_out, new_out, copy_out, grads, change
):
    block = grad_ref.shape[1]
    for i in range(8):
        rows = lax.rsqrt(rows_ref[:, i : i + 1])
        every = pl.ds(i, block, stride=8)
        for lane in range(8):
            columns = slice(lane * 128, lane * 128 + 128)
            if i < 2:
                start = 512 * i + 128 * (lane % 4)
                grad = grad_ref[2 * (lane // 4), :, start : start + 128]
            else:
                grad = grad_ref[1 if i == 2 else i, :, columns]
            grad = grad.astype(jnp.float32)
            grads[lane, every, :] = grad
            change[lane, every, :] = grad * rows * scale_ref[i : i + 1, columns]
    for lane in range(8):
        columns = slice(lane * 128, lane * 128 + 128)
        grad_out[:, columns] = grads[lane]
        new = weight_ref[:, columns] - change[lane]
        new_out[:, columns] = new
        copy_out[:, columns] = new.astype(jnp.bfloat16)


def update_attention(grads, weights, rows, scale):
    block = 32
    wide = pl.BlockSpec((block * 8, D), lambda i: (i, 0))
    shape = jax.ShapeDtypeStruct
    new = pl.pallas_call(
        update_attention_kernel,
        grid=(256 // block,),
        out_shape=(
            shape((2048, D), jnp.float32),
            shape((2048, D), jnp.float32),
            shape((2048, D), jnp.bfloat16),
        ),
        in_specs=[
            pl.BlockSpec((8, block, D), lambda i: (0, i, 0)),
            wide,
            pl.BlockSpec((block, 128), lambda i: (i, 0)),
            pl.BlockSpec((16, D), lambda i: (0, 0)),
        ],
        out_specs=(wide,) * 3,
        scratch_shapes=[pltpu.VMEM((8, block * 8, 128), jnp.float32)] * 2,
        compiler_params=pltpu.CompilerParams(vmem_limit_bytes=62 * MIB),
    )(grads, weights.reshape(2048, D), rows, scale)
    return [t.reshape(256, 8, D) for t in new]


def update_kernel(
    first, slots, grad_ref, weight_ref, rows_ref, scale_ref, grad_out, new_out, copy_out
):
    spans = 4 if slots == 4 else 1
    wide = D // spans
    for i in range(slots):
        grads = grad_ref[i].astype(jnp.float32)
        changes = grads * (lax.rsqrt(rows_ref[...]) * scale_ref[first + i : first + i + 1, :])
        for s in range(spans):
            start = s * D + i * wide
            columns = slice(start, start + wide)
            part = slice(s * wide, s * wide + wide)
            grad_out[:, columns] = grads[:, part]
            new = weight_ref[:, columns] - changes[:, part]
            new_out[:, columns] = new
            copy_out[:, columns] = new.astype(jnp.bfloat16)


def update_plain(grads, weights, rows, scale, first, slots, grad_map):
    count, width = weights.shape
    block = 128 // slots
    wide = pl.BlockSpec((block, width), lambda i: (i, 0))
    shape = jax.ShapeDtypeStruct
    return pl.pallas_call(
        lambda *refs: update_kernel(first, slots, *refs),
        grid=(count // block,),
        out_shape=(
            shape(weights.shape, jnp.float32),
            shape(weights.shape, jnp.float32),
            shape(weights.shape, jnp.bfloat16),
        ),
        in_specs=[
            pl.BlockSpec((slots, block, D), grad_map),
            wide,
            pl.BlockSpec((block, 1), lambda i: (i, 0)),
            pl.BlockSpec((16, D), lambda i: (0, 0)),
        ],
        out_specs=(wide,) * 3,
        compiler_params=pltpu.CompilerParams(vmem_limit_bytes=62 * MIB),
    )(grads, weights, rows, scale)


def update_direct(grads, rows, scale, attention_weights, expand_weight, shrink_weight):
    shr_rows = rows[:, 9:13].T.reshape(-1, 1)
    attention = update_attention(grads, attention_weights, rows, scale)
    expand = update_plain(grads, expand_weight, rows[:, 8:9], scale, 8, 4, lambda i: (2, i, 0))
    shrink = update_plain(
        grads, shrink_weight, shr_rows, scale, 12, 1, lambda i: (12 + i // 2, i % 2, 0)
    )
    return attention, expand, shrink, (rows[:, 0:8].T, rows[:, 8], shr_rows[:, 0])


def as_rows(vector):
    rows = -(-vector.shape[0] // 1024) * 8
    return jnp.pad(vector, (0, rows * 128 - vector.shape[0])).reshape(rows, 128)


def masked_scores(query_part, key_heads, first_row, valid_count, causal):
    scores = jnp.einsum("qhd,khd->hqk", query_part, key_heads, preferred_element_type=jnp.float32)
    key_places = jnp.arange(key_heads.shape[0], dtype=jnp.int32)[None, :]
    usable = key_places < valid_count
    if causal:
        query_places = first_row + jnp.arange(query_part.shape[0], dtype=jnp.int32)[:, None]
        usable = usable & (key_places <= query_places)
    return jnp.where(usable[None], scores, MASKED)


def attend_forward(queries, key_heads, values, valid_count, causal):
    query_rows = queries.shape[0]
    step_rows = min(512, query_rows)
    outputs, stored = ([], [])
    for b in range(query_rows // step_rows):
        first_row = b * step_rows
        key_end = first_row + step_rows if causal else key_heads.shape[0]
        scores = masked_scores(
            queries[first_row : first_row + step_rows],
            key_heads[:key_end],
            first_row,
            valid_count,
            causal,
        )
        row_max = jnp.max(scores, axis=-1, keepdims=True)
        raised = jnp.exp(scores - row_max)
        totals = jnp.sum(raised, axis=-1, keepdims=True)
        probs_low = (raised / totals).astype(jnp.bfloat16)
        outputs.append(
            jnp.einsum(
                "hqk,khd->qhd", probs_low, values[:key_end], preferred_element_type=jnp.float32
            )
        )
        stored.append(row_max + jnp.log(totals))
    return (jnp.concatenate(outputs, axis=0), stored)


def attend_backward(queries, key_heads, values, grad_out, stored, valid_count, causal):
    query_rows = queries.shape[0]
    key_rows = key_heads.shape[0]
    step_rows = min(512, query_rows)
    grad_queries = []
    grad_keys = jnp.zeros(key_heads.shape, jnp.float32)
    grad_values = jnp.zeros(values.shape, jnp.float32)
    for b in range(query_rows // step_rows):
        first_row = b * step_rows
        key_end = first_row + step_rows if causal else key_rows
        query_part = queries[first_row : first_row + step_rows]
        grad_part = grad_out[first_row : first_row + step_rows]
        scores = masked_scores(query_part, key_heads[:key_end], first_row, valid_count, causal)
        probs = jnp.exp(scores - stored[b])
        probs_low = probs.astype(jnp.bfloat16)
        grad_probs = jnp.einsum(
            "qhd,khd->hqk", grad_part, values[:key_end], preferred_element_type=jnp.float32
        )
        value_part = jnp.einsum(
            "hqk,qhd->khd", probs_low, grad_part, preferred_element_type=jnp.float32
        )
        grad_scores = probs * (grad_probs - jnp.sum(probs * grad_probs, axis=-1, keepdims=True))
        scores_low = grad_scores.astype(jnp.bfloat16)
        grad_queries.append(
            jnp.einsum(
                "hqk,khd->qhd", scores_low, key_heads[:key_end], preferred_element_type=jnp.float32
            )
        )
        key_part = jnp.einsum(
            "hqk,qhd->khd", scores_low, query_part, preferred_element_type=jnp.float32
        )
        padding = ((0, key_rows - key_end), (0, 0), (0, 0))
        grad_keys = grad_keys + jnp.pad(key_part, padding)
        grad_values = grad_values + jnp.pad(value_part, padding)
    return (jnp.concatenate(grad_queries, axis=0), grad_keys, grad_values)


def gather_rows(piece):
    return lax.all_gather(piece, ("shard", "rep"), axis=0, tiled=True)


def own_piece(block, replicas):
    rows = block.shape[0] // replicas
    return lax.dynamic_slice_in_dim(block, lax.axis_index("rep") * rows, rows, axis=0)


def scatter_rows(grad):
    piece = lax.psum_scatter(
        grad.astype(jnp.bfloat16), ("shard", "rep"), scatter_dimension=0, tiled=True
    )
    return lax.all_gather(piece, "rep", axis=0, tiled=True)


def local_factors(grad, rows):
    square = grad * grad
    rows_new = DECAY_RATE * rows + (1.0 - DECAY_RATE) * jnp.mean(square + FACTOR_EPS, axis=-1)
    col_part = jnp.sum(square + FACTOR_EPS, axis=0)
    weighted = jnp.sum(square / rows_new[..., None], axis=0)
    return rows_new, col_part, weighted, jnp.sum(rows_new, axis=0)


def finish_factors(grad, weight, rows_new, cols, col_sum, weighted, row_total, row_count, rate):
    cols_new = DECAY_RATE * cols + (1.0 - DECAY_RATE) * col_sum / row_count
    mean_rows = row_total / row_count
    mean_square = mean_rows * jnp.sum(weighted / cols_new, axis=-1) / (row_count * cols.shape[-1])
    factor = rate / jnp.maximum(1.0, jnp.sqrt(mean_square) / CLIP_LEVEL)
    scaled = lax.rsqrt(cols_new / mean_rows[..., None]) * factor[..., None]
    fresh = weight - grad * (lax.rsqrt(rows_new)[..., None] * scaled[None])
    return fresh, cols_new


def plain_device(
    tokens,
    encoder,
    cotangent,
    lengths,
    encoder_lengths,
    dealt_order,
    attention_weights,
    expand_weight,
    shrink_weight,
    small_params,
    attention_rows,
    attention_cols,
    expand_rows,
    expand_cols,
    shrink_rows,
    shrink_cols,
    small_moment,
):
    devices = lax.axis_size(("rep", "shard"))
    replicas = lax.axis_size("rep")
    shards = lax.axis_size("shard")
    slot_tokens = tokens.shape[0]
    slot_states = encoder.shape[0]
    position = lax.axis_index(("rep", "shard"))
    inverse = (
        jnp.zeros((devices,), jnp.int32).at[dealt_order].set(jnp.arange(devices, dtype=jnp.int32))
    )
    qkv_piece = own_piece(attention_weights[:, 0:3, :].reshape(-1, 3 * D), replicas)
    rest_piece = own_piece(attention_weights[:, 3:8, :].reshape(-1, 5 * D), replicas)
    qkv_full = gather_rows(qkv_piece.astype(jnp.bfloat16))
    rest_full = gather_rows(rest_piece.astype(jnp.bfloat16))
    expand_full = gather_rows(own_piece(expand_weight, replicas).astype(jnp.bfloat16))
    shrink_full = gather_rows(own_piece(shrink_weight, replicas).astype(jnp.bfloat16))
    spread = lax.all_to_all(
        tokens.reshape(devices, slot_tokens // devices, D),
        ("rep", "shard"),
        split_axis=0,
        concat_axis=0,
        tiled=True,
    )
    picked = jnp.take(spread, inverse, axis=0)
    tokens = lax.all_to_all(
        picked, ("rep", "shard"), split_axis=0, concat_axis=0, tiled=True
    ).reshape(slot_tokens, D)
    states = encoder
    incoming = cotangent
    valid_tokens = lengths[position]
    valid_states = encoder_lengths[position]
    matrices = [qkv_full[:, i * D : (i + 1) * D] for i in range(3)] + [
        rest_full[:, i * D : (i + 1) * D] for i in range(5)
    ]
    parts = unpack(small_params)
    token_heads = (slot_tokens, HEADS, HEAD_DIM)
    state_heads = (slot_states, HEADS, HEAD_DIM)
    q_self = ((forward_product(tokens, matrices[0]) + parts[0]) * 0.125).astype(
        jnp.bfloat16
    )
    k_self = forward_product(tokens, matrices[1]).astype(jnp.bfloat16)
    v_self = (forward_product(tokens, matrices[2]) + parts[1]).astype(jnp.bfloat16)
    o_self, lse_self = attend_forward(
        q_self.reshape(token_heads),
        k_self.reshape(token_heads),
        v_self.reshape(token_heads),
        valid_tokens,
        True,
    )
    o_self_low = o_self.reshape(slot_tokens, D).astype(jnp.bfloat16)
    branch_a = forward_product(o_self_low, matrices[3]) + parts[2]
    tokens_wide = tokens.astype(jnp.float32)
    hidden_one, norm_one_back = jax.vjp(layer_norm, tokens_wide + branch_a, parts[8], parts[9])
    hidden_one_low = hidden_one.astype(jnp.bfloat16)
    q_cross = (
        (forward_product(hidden_one_low, matrices[4]) + parts[3]) * 0.125
    ).astype(jnp.bfloat16)
    k_cross = forward_product(states, matrices[5]).astype(jnp.bfloat16)
    v_cross = (forward_product(states, matrices[6]) + parts[4]).astype(jnp.bfloat16)
    o_cross, lse_cross = attend_forward(
        q_cross.reshape(token_heads),
        k_cross.reshape(state_heads),
        v_cross.reshape(state_heads),
        valid_states,
        False,
    )
    o_cross_low = o_cross.reshape(slot_tokens, D).astype(jnp.bfloat16)
    branch_c = forward_product(o_cross_low, matrices[7]) + parts[5]
    hidden_two, norm_two_back = jax.vjp(layer_norm, hidden_one + branch_c, parts[10], parts[11])
    hidden_two_low = hidden_two.astype(jnp.bfloat16)
    pre_act = forward_product(hidden_two_low, expand_full) + parts[6]
    activated, gelu_back = jax.vjp(gelu_exact, pre_act)
    activated_low = activated.astype(jnp.bfloat16)
    branch_m = forward_product(activated_low, shrink_full) + parts[7]
    result, norm_three_back = jax.vjp(layer_norm, hidden_two + branch_m, parts[12], parts[13])
    usable_rows = (jnp.arange(slot_tokens, dtype=jnp.int32) < valid_tokens).astype(jnp.float32)[
        :, None
    ]
    squares = jnp.stack(
        [
            jnp.sum(usable_rows * t * t)
            for t in (tokens_wide, branch_a, hidden_one, branch_c, hidden_two, branch_m)
        ]
    )
    d_third, d_gain_three, d_shift_three = norm_three_back(
        incoming.astype(jnp.float32) * usable_rows
    )
    d_mlp = d_third.astype(jnp.bfloat16)
    grad_shrink = weight_product(activated_low, d_mlp)
    grad_shrink_offset = row_sum(d_mlp)
    d_activated = input_product(d_mlp, shrink_full)
    d_pre = gelu_back(d_activated)[0].astype(jnp.bfloat16)
    grad_expand = weight_product(hidden_two_low, d_pre)
    grad_expand_offset = row_sum(d_pre)
    d_hidden_two = d_third + input_product(d_pre, expand_full)
    d_second, d_gain_two, d_shift_two = norm_two_back(d_hidden_two)
    d_branch_c = d_second.astype(jnp.bfloat16)
    grad_cross_out = weight_product(o_cross_low, d_branch_c)
    grad_cross_out_offset = row_sum(d_branch_c)
    d_o_cross = input_product(d_branch_c, matrices[7]).astype(jnp.bfloat16)
    grad_cq, grad_ck, grad_cv = attend_backward(
        q_cross.reshape(token_heads),
        k_cross.reshape(state_heads),
        v_cross.reshape(state_heads),
        d_o_cross.reshape(token_heads),
        lse_cross,
        valid_states,
        False,
    )
    dq_cross = (grad_cq.reshape(slot_tokens, D) * 0.125).astype(jnp.bfloat16)
    dk_cross = grad_ck.reshape(slot_states, D).astype(jnp.bfloat16)
    dv_cross = grad_cv.reshape(slot_states, D).astype(jnp.bfloat16)
    grad_cross_query = weight_product(hidden_one_low, dq_cross)
    grad_cross_key = weight_product(states, dk_cross)
    grad_cross_value = weight_product(states, dv_cross)
    state_grad = input_product(dk_cross, matrices[5]) + input_product(
        dv_cross, matrices[6]
    )
    d_hidden_one = d_second + input_product(dq_cross, matrices[4])
    d_first, d_gain_one, d_shift_one = norm_one_back(d_hidden_one)
    d_branch_a = d_first.astype(jnp.bfloat16)
    grad_self_out = weight_product(o_self_low, d_branch_a)
    grad_self_out_offset = row_sum(d_branch_a)
    d_o_self = input_product(d_branch_a, matrices[3]).astype(jnp.bfloat16)
    grad_sq, grad_sk, grad_sv = attend_backward(
        q_self.reshape(token_heads),
        k_self.reshape(token_heads),
        v_self.reshape(token_heads),
        d_o_self.reshape(token_heads),
        lse_self,
        valid_tokens,
        True,
    )
    dq_self = (grad_sq.reshape(slot_tokens, D) * 0.125).astype(jnp.bfloat16)
    dk_self = grad_sk.reshape(slot_tokens, D).astype(jnp.bfloat16)
    dv_self = grad_sv.reshape(slot_tokens, D).astype(jnp.bfloat16)
    grad_self_query = weight_product(tokens, dq_self)
    grad_self_key = weight_product(tokens, dk_self)
    grad_self_value = weight_product(tokens, dv_self)
    token_grad = (
        d_first
        + input_product(dq_self, matrices[0])
        + input_product(dk_self, matrices[1])
        + input_product(dv_self, matrices[2])
    )
    small_partial = jnp.concatenate(
        [
            row_sum(dq_self),
            row_sum(dv_self),
            grad_self_out_offset,
            row_sum(dq_cross),
            row_sum(dv_cross),
            grad_cross_out_offset,
            grad_expand_offset,
            grad_shrink_offset,
            d_gain_one,
            d_shift_one,
            d_gain_two,
            d_shift_two,
            d_gain_three,
            d_shift_three,
        ]
    )
    totals = lax.psum(jnp.concatenate([small_partial, squares]), ("rep", "shard"))
    g_shrink = scatter_rows(grad_shrink)
    g_expand = scatter_rows(grad_expand)
    g_rest = scatter_rows(
        jnp.concatenate(
            [grad_self_out, grad_cross_query, grad_cross_key, grad_cross_value, grad_cross_out],
            axis=1,
        )
    )
    g_qkv = scatter_rows(
        jnp.concatenate([grad_self_query, grad_self_key, grad_self_value], axis=1)
    )
    g_attention = (
        jnp.concatenate([g_qkv, g_rest], axis=1).reshape(-1, 8, D).astype(jnp.float32)
    )
    g_expand = g_expand.astype(jnp.float32)
    g_shrink = g_shrink.astype(jnp.float32)
    attention_rows_new, *attention_parts = local_factors(g_attention, attention_rows.T)
    expand_rows_new, *expand_parts = local_factors(g_expand, expand_rows)
    shrink_rows_new, *shrink_parts = local_factors(g_shrink, shrink_rows)
    flat = attention_parts + expand_parts + shrink_parts
    summed = lax.psum(jnp.concatenate([t.reshape(-1) for t in flat]), "shard")
    sums = []
    offset = 0
    for t in flat:
        sums.append(summed[offset : offset + t.size].reshape(t.shape))
        offset = offset + t.size
    attention_rates = STEP_RATE * jnp.where(jnp.arange(8) % 4 == 3, OUT_GAIN, 1.0).astype(
        jnp.float32
    )
    attention_new, attention_cols_new = finish_factors(
        g_attention,
        attention_weights,
        attention_rows_new,
        attention_cols,
        *sums[0:3],
        D,
        attention_rates,
    )
    expand_new, expand_cols_new = finish_factors(
        g_expand, expand_weight, expand_rows_new, expand_cols, *sums[3:6], D, STEP_RATE
    )
    shrink_new, shrink_cols_new = finish_factors(
        g_shrink, shrink_weight, shrink_rows_new, shrink_cols, *sums[6:9], FF, STEP_RATE
    )
    small_grad = totals[: small_params.shape[0]]
    small_moment_new = DECAY_RATE * small_moment + (1.0 - DECAY_RATE) * (
        small_grad * small_grad + FACTOR_EPS
    )
    small_update = small_grad * lax.rsqrt(small_moment_new)
    small_scale = jnp.sqrt(jnp.mean(small_update * small_update))
    small_new = small_params - SMALL_RATE * small_update / jnp.maximum(
        1.0, small_scale / CLIP_LEVEL
    )
    norm_stats = jnp.sqrt(
        totals[small_params.shape[0] :] / (jnp.sum(lengths).astype(jnp.float32) * D)
    )
    return (
        result.astype(jnp.bfloat16),
        token_grad.astype(jnp.bfloat16),
        state_grad.astype(jnp.bfloat16),
        g_attention,
        g_expand,
        g_shrink,
        small_grad,
        attention_new,
        expand_new,
        shrink_new,
        small_new,
        attention_new.astype(jnp.bfloat16),
        expand_new.astype(jnp.bfloat16),
        shrink_new.astype(jnp.bfloat16),
        attention_rows_new.T,
        attention_cols_new,
        expand_rows_new,
        expand_cols_new,
        shrink_rows_new,
        shrink_cols_new,
        small_moment_new,
        norm_stats,
    )


def direct_device(
    tokens,
    encoder,
    cotangent,
    lengths,
    encoder_lengths,
    dealt_order,
    attention_weights,
    expand_weight,
    shrink_weight,
    small_params,
    attention_rows,
    attention_cols,
    expand_rows,
    expand_cols,
    shrink_rows,
    shrink_cols,
    small_moment,
):
    inverse = jnp.zeros((32,), jnp.int32).at[dealt_order].set(jnp.arange(32, dtype=jnp.int32))
    params = small_params.reshape(17, D)
    weights = (attention_weights.reshape(2048, D), expand_weight, shrink_weight)
    (
        tokens,
        full,
        q_self,
        k_self,
        v_self,
        o_self,
        lse_self,
        q_cross,
        k_cross,
        v_cross,
        o_cross,
        lse_cross,
        summed_one,
        summed_two,
        hidden_one,
        hidden_two,
        activated,
        slope,
        output,
        d_mlp,
        d_third,
        small_first,
    ) = forward(
        (inverse, lengths, encoder_lengths), tokens, weights, encoder, cotangent, params
    )
    factor_rows = jnp.concatenate(
        [attention_rows, expand_rows.reshape(1, 256), shrink_rows.reshape(4, 256)]
    )
    factor_rows = jnp.pad(factor_rows.T, ((0, 0), (0, 115)))
    factor_cols = jnp.concatenate(
        [attention_cols, hidden_blocks(expand_cols), shrink_cols.reshape(1, D), jnp.ones((3, D))]
    )
    token_grad, state_grad, reduced, totals, factor_rows, factor_cols, scale = backward(
        (lengths, encoder_lengths),
        (
            d_mlp,
            d_third,
            activated,
            slope,
            full.reshape(GATHERED, 1024, D),
            hidden_two,
            hidden_one,
            tokens.reshape(1024, D),
            encoder,
            o_cross,
            o_self,
            summed_one,
            summed_two,
            q_self,
            k_self,
            v_self,
            q_cross,
            k_cross,
            v_cross,
            lse_self,
            lse_cross,
        ),
        params,
        small_first,
        factor_rows,
        factor_cols,
    )
    attention, expand, shrink, rows_new = update_direct(
        reduced, factor_rows, scale, attention_weights, expand_weight, shrink_weight
    )
    cols_new = (factor_cols[0:8], hidden_flat(factor_cols[8:12]), factor_cols[12])
    small_grad = totals[0:17].reshape(-1)
    small_moment_new = DECAY_RATE * small_moment + (1.0 - DECAY_RATE) * (
        small_grad * small_grad + FACTOR_EPS
    )
    small_update = small_grad * lax.rsqrt(small_moment_new)
    small_scale = jnp.sqrt(jnp.mean(small_update * small_update))
    small_new = small_params - SMALL_RATE * small_update / jnp.maximum(
        1.0, small_scale / CLIP_LEVEL
    )
    norm_stats = jnp.sqrt(totals[17, 0:6] / (jnp.sum(lengths).astype(jnp.float32) * D))
    return (
        output,
        token_grad,
        state_grad,
        attention[0],
        expand[0],
        shrink[0],
        small_grad,
        attention[1],
        expand[1],
        shrink[1],
        small_new,
        attention[2],
        expand[2],
        shrink[2],
        rows_new[0],
        cols_new[0],
        rows_new[1],
        cols_new[1],
        rows_new[2],
        cols_new[2],
        small_moment_new,
        norm_stats,
    )


def on_device(*args):
    if lax.axis_size("rep") == 8 and lax.axis_size("shard") == 4:
        return direct_device(*args)
    return plain_device(*args)


def solution(mesh):
    in_specs = (
        P(("rep", "shard"), None),
        P(("rep", "shard"), None),
        P(("rep", "shard"), None),
        P(),
        P(),
        P(),
        P("shard", None, None),
        P("shard", None),
        P("shard", None),
        P(),
        P(None, "shard"),
        P(),
        P("shard"),
        P(),
        P("shard"),
        P(),
        P(),
    )
    out_specs = (
        P(("rep", "shard"), None),
        P(("rep", "shard"), None),
        P(("rep", "shard"), None),
        P("shard", None, None),
        P("shard", None),
        P("shard", None),
        P(),
        P("shard", None, None),
        P("shard", None),
        P("shard", None),
        P(),
        P("shard", None, None),
        P("shard", None),
        P("shard", None),
        P(None, "shard"),
        P(),
        P("shard"),
        P(),
        P("shard"),
        P(),
        P(),
        P(),
    )
    return jax.shard_map(
        on_device, mesh=mesh, in_specs=in_specs, out_specs=out_specs, check_vma=False
    )
```

```python
import math

import jax
import jax.numpy as jnp
from jax import lax
from jax.experimental import pallas as pl
from jax.experimental.pallas import tpu as pltpu
from jax.sharding import PartitionSpec as P

D = 1024
HEADS = 16
HEAD_DIM = 64
FF = 4096


DECAY_RATE = 0.5
CLIP_LEVEL = 0.25
STEP_RATE = 0.1
SMALL_RATE = 0.4
OUT_GAIN = 8.0
NORM_EPS = 1e-05
FACTOR_EPS = 1e-30
MASKED = -1e30
MESH = pl.DeviceIdType.MESH
CHUNKS = 16
GATHERED = 16
EXPAND_AT = (8, 9, 11, 13)
SHRINK_AT = (10, 12, 14, 15)
MIB = 1 << 20


def layer_norm(r, norm_gain, norm_shift):
    centred = r - jnp.mean(r, axis=-1, keepdims=True)
    spread = jnp.mean(centred * centred, axis=-1, keepdims=True)
    return centred * lax.rsqrt(spread + NORM_EPS) * norm_gain + norm_shift


def gelu_exact(values):
    return jax.nn.gelu(values, approximate=False)


def unpack(small):
    extents = [D] * 6 + [FF] + [D] * 7
    pieces = []
    offset = 0
    for extent in extents:
        pieces.append(small[offset : offset + extent])
        offset = offset + extent
    return pieces


def forward_product(source, matrix):
    return jnp.dot(source, matrix, preferred_element_type=jnp.float32)


def input_product(grad_low, matrix):
    return jnp.einsum("to,io->ti", grad_low, matrix, preferred_element_type=jnp.float32)


def weight_product(source, grad_low):
    return jnp.einsum("ti,to->io", source, grad_low, preferred_element_type=jnp.float32)


def row_sum(grad_low):
    return jnp.sum(grad_low.astype(jnp.float32), axis=0)


def transposed(block):
    return block.astype(jnp.float32).T.astype(jnp.bfloat16)


def half_lanes(shape, dim):
    return lax.broadcasted_iota(jnp.int32, shape, dim)


def masked_keys(keys, length, head):
    place = half_lanes(keys.shape, 0)
    lane = half_lanes(keys.shape, 1)
    blocked = jnp.where((lane == 64 - 64 * head) & (place >= length), MASKED, 0.0)
    own = (lane >= 64 * head) & (lane < 64 * head + 64)
    return jnp.where(own, keys.astype(jnp.float32), blocked).astype(jnp.bfloat16)


def own_head(rows_t, head, fill):
    place = half_lanes(rows_t.shape, 0)
    own = (place >= 64 * head) & (place < 64 * head + 64)
    other = jnp.where(place == 64 - 64 * head, fill, 0.0)
    return jnp.where(own, rows_t.astype(jnp.float32), other).astype(jnp.bfloat16)


def product(first, second):
    return jnp.dot(first, second, preferred_element_type=jnp.float32)


def causal_mask(scores, step):
    kept = scores.shape[0] - step
    last = scores[kept:]
    allowed = half_lanes(last.shape, 0) <= half_lanes(last.shape, 1)
    last = jnp.where(allowed, last, MASKED)
    return last if kept == 0 else jnp.concatenate([scores[:kept], last], axis=0)


def attend_pair(
    causal, step, length, q_ref, k_ref, v_ref, o_ref, lse_ref, o_t, first_row=0
):
    count = q_ref.shape[0]
    q_t = transposed(q_ref[...])
    v_t = transposed(v_ref[...])
    keys = [masked_keys(k_ref[...], length, head) for head in range(2)]
    queries = [own_head(q_t, head, 1.0) for head in range(2)]
    units = [(head, start) for start in range(0, count, step) for head in range(2)]

    def scores_of(head, start):
        end = first_row + start + step if causal else k_ref.shape[0]
        return product(keys[head][:end], queries[head][:, start : start + step])

    ahead = scores_of(*units[0])
    for index, (head, start) in enumerate(units):
        scores = ahead
        if index + 1 < len(units):
            ahead = scores_of(*units[index + 1])
        rows = slice(64 * head, 64 * head + 64)
        columns = slice(start, start + step)
        if causal:
            scores = causal_mask(scores, step)
        top = jnp.max(scores, axis=0, keepdims=True)
        raised = jnp.exp(scores - top)
        total = jnp.sum(raised, axis=0, keepdims=True)
        probs = (raised * (1.0 / total)).astype(jnp.bfloat16)
        o_t[rows, columns] = product(v_t[rows, : scores.shape[0]], probs)
        place = slice(first_row + start, first_row + start + step)
        lse_ref[0, head : head + 1, place] = top + jnp.log(total)
    o_ref[...] = o_t[:, :count].T.astype(jnp.bfloat16)


def attend_back_pair(
    causal,
    step,
    length,
    q_ref,
    k_ref,
    v_ref,
    do_ref,
    lse_ref,
    dq_ref,
    dk_ref,
    dv_ref,
    put_sums,
    dq_t,
    dk_sum,
    dv_sum,
):
    key_rows = k_ref.shape[0]
    q_t = transposed(q_ref[...])
    k_t = transposed(k_ref[...])
    do_t = transposed(do_ref[...])
    values = v_ref[...]
    keys = [masked_keys(k_ref[...], length, head) for head in range(2)]
    queries = [own_head(q_t, head, 1.0) for head in range(2)]
    grads = [own_head(do_t, head, 0.0) for head in range(2)]
    count = q_ref.shape[0] // step
    units = [(head, b) for b in reversed(range(count)) for head in range(2)]

    def products_of(head, b):
        columns = slice(b * step, b * step + step)
        end = b * step + step if causal else key_rows
        scores = product(keys[head][:end], queries[head][:, columns])
        return scores, product(values[:end], grads[head][:, columns])

    ahead = products_of(*units[0])
    for index, (head, b) in enumerate(units):
        scores, d_probs = ahead
        if index + 1 < len(units):
            ahead = products_of(*units[index + 1])
        rows = slice(64 * head, 64 * head + 64)
        columns = slice(b * step, b * step + step)
        end = scores.shape[0]
        if causal:
            scores = causal_mask(scores, step)
        probs = jnp.exp(scores - lse_ref[0, head : head + 1, columns])
        weighted = probs * d_probs
        delta = jnp.sum(weighted, axis=0, keepdims=True)
        d_scores = (weighted - probs * delta).astype(jnp.bfloat16)
        dv = product(probs.astype(jnp.bfloat16), do_ref[columns, :])
        dk = product(d_scores, q_ref[columns, :])
        if b == count - 1:
            dv_sum[head, :end] = dv
            dk_sum[head, :end] = dk
        else:
            dv_sum[head, :end] += dv
            dk_sum[head, :end] += dk
        dq_t[rows, columns] = product(k_t[rows, :end], d_scores)
    first = half_lanes((key_rows, 128), 1) < 64
    dk_ref[...] = jnp.where(first, dk_sum[0, :key_rows], dk_sum[1, :key_rows]).astype(jnp.bfloat16)
    dv = jnp.where(first, dv_sum[0, :key_rows], dv_sum[1, :key_rows]).astype(jnp.bfloat16)
    dv_ref[...] = dv
    dq = (dq_t[...] * 0.125).T.astype(jnp.bfloat16)
    dq_ref[...] = dq
    put_sums(
        jnp.sum(dq.astype(jnp.float32), axis=0, keepdims=True),
        jnp.sum(dv.astype(jnp.float32), axis=0, keepdims=True),
    )


SCALARS = pl.BlockSpec(memory_space=pltpu.SMEM)


def neighbours():
    rep = lax.axis_index("rep")
    z = lax.axis_index("shard")
    core = rep % 2
    x = (rep // 2) % 2
    y = rep // 4
    other_core = (rep + 1 - 2 * core, z)
    other_x = (rep + 2 - 4 * x, z)
    other_y = (rep + 4 - 8 * y, z)
    others_z = [(rep, (z + d) % 4) for d in (1, 2, 3)]
    return core, x, y, z, other_core, other_x, other_y, others_z


def greet(devices):
    barrier = pltpu.get_barrier_semaphore()
    for device in devices:
        pl.semaphore_signal(barrier, inc=1, device_id=device, device_id_type=MESH)
    pl.semaphore_wait(barrier, len(devices))


def remote(src, dst, send, recv, device):
    return pltpu.make_async_remote_copy(
        src_ref=src, dst_ref=dst, send_sem=send, recv_sem=recv, device_id=device, device_id_type=MESH
    )


def gather_copies(refs, c, parity, places):
    piece, full, place_sem, z_send, z_recv, send, recv = refs
    core, x, y, z, other_core, other_x, other_y, others_z = places
    a = x + parity * (y - x)
    b = y + parity * (x - y)
    first = (other_x[0] + parity * (other_y[0] - other_x[0]), z)
    second = (other_y[0] + parity * (other_x[0] - other_y[0]), z)
    own = pl.ds(pl.multiple_of(core * 128 + a * 64 + b * 32, 32), 32)
    steps = (
        (own, second),
        (pl.ds(pl.multiple_of(core * 128 + a * 64, 64), 64), first),
        (pl.ds(pl.multiple_of(core * 128, 128), 128), other_core),
    )

    def local():
        return pltpu.make_async_copy(piece.at[c], full.at[c, z, own, :], place_sem.at[c])

    def line(d):
        return remote(
            piece.at[c], full.at[c, z, own, :], z_send.at[c, d], z_recv.at[c, d], others_z[d]
        )

    def pair(k):
        block = full.at[c, :, steps[k][0], :]
        return remote(block, block, send.at[k, c], recv.at[k, c], steps[k][1])

    return local, line, pair


def gather_stage(k, refs, c, parity, places):
    local, line, pair = gather_copies(refs, c, parity, places)
    if k == 0:
        local().start()
        for d in range(3):
            line(d).start()
    if k == 1:
        local().wait()
        for d in range(3):
            line(d).wait_recv()
        pair(0).start()
    if k == 2 or k == 3:
        pair(k - 2).wait_recv()
        pair(k - 1).start()
    if k == 4:
        pair(2).wait()
        pair(1).wait_send()
        pair(0).wait_send()
        for d in range(3):
            line(d).wait_send()


def gather_sems(count):
    dma = pltpu.SemaphoreType.DMA
    return [dma((count,)), dma((count, 3)), dma((count, 3)), dma((3, count)), dma((3, count))]


def hidden_blocks(values):
    split = values.reshape(values.shape[:-1] + (4, 4, 256))
    split = jnp.swapaxes(split, -3, -2)
    return split.reshape(values.shape[:-1] + (4, 1024))


def hidden_flat(blocks):
    split = blocks.reshape(blocks.shape[:-2] + (4, 4, 256))
    split = jnp.swapaxes(split, -3, -2)
    return split.reshape(blocks.shape[:-2] + (FF,))


def fold(tile):
    return jnp.sum(tile.reshape(-1, 8, tile.shape[-1]), axis=0)


GATHER_PLAN = (("z", 7.5), ("second", 7.5), ("first", 13.0), ("core", 4.0), (None, 0.0))


class GatherPlanner:
    def __init__(self, count):
        self.now = 0.0
        self.links = {"core": 0.0, "x": 0.0, "y": 0.0, "z": 0.0}
        self.stage = {c: 0 for c in range(count)}
        self.ready = {c: 0.0 for c in range(count)}
        self.opened = count

    def can(self, c):
        if self.stage[c] == 0 and c >= 3 and self.stage[c - 3] < 2:
            return False
        return self.stage[c] < 5

    def spend(self, now, **busy):
        self.now = max(self.now, now)
        for link, span in busy.items():
            self.links[link] = max(self.links[link], self.now) + span

    def emit(self, c):
        stage = self.stage[c]
        link, span = GATHER_PLAN[stage]
        first, second = ("x", "y") if c % 2 == 0 else ("y", "x")
        link = {"first": first, "second": second}.get(link, link)
        self.now = max(self.now, self.ready[c]) + 0.1
        if link is not None:
            begin = max(self.now, self.links[link])
            self.links[link] = begin + span - 1.0
            self.ready[c] = begin + span
        self.stage[c] = stage + 1
        return (stage, c)

    def tick(self, spent):
        self.now += spent
        events = []
        progress = True
        while progress:
            progress = False
            for c in range(self.opened):
                if self.can(c) and self.ready[c] <= self.now:
                    events.append(self.emit(c))
                    progress = True
        return events

    def until(self, c):
        events = []
        while self.stage[c] < 5:
            choices = [i for i in range(self.opened) if self.can(i)]
            best = min(choices, key=lambda i: (self.ready[i], i))
            events.append(self.emit(best))
        return events


ERFC_SERIES = (
    0.08459648489952087,
    0.085321806371212,
    0.0743890032172203,
    0.10671534389257431,
    -0.04577348381280899,
    0.27184805274009705,
    -0.2545455992221832,
    0.24207571148872375,
    -0.06462734192609787,
)


def gelu_parts(u):
    bell = jnp.exp(-0.5 * u * u)
    t = 1.0 / (1.0 + (0.3 * math.sqrt(0.5)) * jnp.abs(u))
    series = ERFC_SERIES[8]
    for coefficient in ERFC_SERIES[7::-1]:
        series = series * t + coefficient
    tail = series * t * bell
    share = jnp.where(u < 0.0, tail, 1.0 - tail)
    return u * share, share + u * (bell * (1.0 / math.sqrt(2.0 * math.pi)))


def norm_parts(values):
    centred = values - jnp.mean(values, axis=1, keepdims=True)
    spread = jnp.mean(centred * centred, axis=1, keepdims=True)
    scale = lax.rsqrt(spread + NORM_EPS)
    return centred * scale, scale


def forward_kernel(
    order_ref,
    lengths_ref,
    state_lengths_ref,
    tokens_ref,
    att_ref,
    exp_ref,
    shr_ref,
    e_ref,
    cot_ref,
    par,
    x_out,
    full_ref,
    q_out,
    k_out,
    v_out,
    o_out,
    lse_out,
    cq_out,
    ck_out,
    cv_out,
    oc_out,
    lse_cross_out,
    r1_out,
    r2_out,
    h1_out,
    h2_out,
    g_out,
    gp_out,
    y_out,
    dm_out,
    d_third_out,
    small_out,
    pool,
    acc,
    held,
    o_t,
    lse_held,
    states,
    x_held,
    spread,
    picked,
    piece_ref,
    att_in,
    exp_in,
    shr_in,
    prepare_sem,
    load_sem,
    store_sem,
    state_sem,
    acc_sem,
    spread_send,
    spread_recv,
    back_send,
    back_recv,
    *gather_sem,
):
    places = neighbours()
    refs = (piece_ref, full_ref) + gather_sem
    planner = GatherPlanner(GATHERED)
    me = lax.axis_index("rep") * 4 + places[3]
    length = lengths_ref[me]

    core, x, y = places[0:3]

    def own_row(parity):
        a = x + parity * (y - x)
        b = y + parity * (x - y)
        return core * 128 + a * 64 + b * 32

    prepare = []
    for p in range(2):
        for lane in range(8):
            rows = pl.ds(pl.multiple_of(own_row(p) * 8, 256), 256)
            prepare.append((att_ref.at[rows, pl.ds(lane * 128, 128)], att_in.at[p, lane]))
        rows = pl.ds(pl.multiple_of(own_row(p), 32), 32)
        prepare.append((exp_ref.at[rows, :], exp_in.at[p]))
    for j in range(4):
        rows = pl.ds(pl.multiple_of(j * 256 + own_row(SHRINK_AT[j] % 2), 32), 32)
        prepare.append((shr_ref.at[rows, :], shr_in.at[j]))
    prepare = [
        pltpu.make_async_copy(source, target, prepare_sem.at[i])
        for i, (source, target) in enumerate(prepare)
    ]

    def make_pieces():
        for copy in prepare:
            copy.wait()
        for c in range(8):
            for lane in range(8):
                tile = att_in[c % 2, lane, pl.ds(c, 32, stride=8), :]
                piece_ref[c, :, lane * 128 : lane * 128 + 128] = tile.astype(jnp.bfloat16)
        for j in range(4):
            c = EXPAND_AT[j]
            for s in range(4):
                start = s * 1024 + j * 256
                tile = exp_in[c % 2, :, start : start + 256]
                piece_ref[c, :, s * 256 : s * 256 + 256] = tile.astype(jnp.bfloat16)
            piece_ref[SHRINK_AT[j]] = shr_in[j].astype(jnp.bfloat16)

    def device(offset):
        j = lax.rem(me + offset, 32)
        return j, (j // 4, j % 4)

    def spread_copy(offset):
        j, target = device(offset)
        return remote(
            tokens_ref.at[j],
            spread.at[me],
            spread_send.at[offset],
            spread_recv.at[offset],
            target,
        )

    def back_copy(offset):
        return remote(
            picked.at[offset],
            x_held.at[me],
            back_send.at[offset],
            back_recv.at[offset],
            device(offset)[1],
        )

    def own_spread():
        return pltpu.make_async_copy(tokens_ref.at[me], spread.at[me], spread_recv.at[0])

    def own_back():
        return pltpu.make_async_copy(picked.at[0], x_held.at[me], back_recv.at[0])

    def each_other(act):
        def body(offset, carry):
            act(offset)
            return carry

        lax.fori_loop(1, 32, body, 0)

    def turn_back():
        own_spread().wait()
        each_other(lambda offset: spread_copy(offset).wait())
        picked[0] = spread[order_ref[me]]
        own_back().start()

        def pick(offset):
            picked[offset] = spread[order_ref[device(offset)[0]]]
            back_copy(offset).start()

        each_other(pick)

    def emit_all(events):
        for stage, c in events:
            gather_stage(stage, refs, c, c % 2, places)

    def tick(spent):
        emit_all(planner.tick(spent))

    def load(slot, source):
        return pltpu.make_async_copy(source, pool.at[slot], load_sem.at[slot])

    def store(slot, target):
        return pltpu.make_async_copy(pool.at[slot], target, store_sem.at[slot])

    def product_into(left, right, put):
        def body(i, carry):
            n = pl.multiple_of(i * 256, 256)
            put(n, product(left(), pool[right, :, pl.ds(n, 256)]))
            return carry

        lax.fori_loop(0, 4, body, 0)

    def row(index, n):
        return par[index : index + 1, pl.ds(n, 256)]

    def put_low(slot, offset=None, scale=None):
        def put(n, value):
            if offset is not None:
                value = value + row(offset, n)
            if scale is not None:
                value = value * scale
            pool[slot, :, pl.ds(n, 256)] = value.astype(jnp.bfloat16)

        return put

    def put_acc(offset):
        def put(n, value):
            acc[:, pl.ds(n, 256)] = value + row(offset, n)

        return put

    def load_weight(c, slot):
        target = pool.at[slot].reshape(4, 256, D)
        return pltpu.make_async_copy(full_ref.at[c], target, load_sem.at[slot])

    def weight(c, slot):
        emit_all(planner.until(c))
        return load_weight(c, slot)

    def attend_loop(causal, step, valid, query, key, value, out, spent, rows, key_rows):
        ahead = [planner.tick(spent) for _ in range(8)]
        first_row, count = rows

        def body(i, carry):
            lanes = pl.ds(pl.multiple_of(i * 128, 128), 128)
            attend_pair(
                causal,
                step,
                valid,
                query.at[pl.ds(first_row, count), lanes],
                key.at[pl.ds(0, key_rows), lanes],
                value.at[pl.ds(0, key_rows), lanes],
                out.at[pl.ds(first_row, count), lanes],
                lse_held.at[pl.ds(i, 1)],
                o_t,
                first_row,
            )
            for n in range(8):
                if ahead[n]:

                    @pl.when(i == n)
                    def _(events=ahead[n]):
                        emit_all(events)

            return carry

        lax.fori_loop(0, 8, body, 0)

    TILE = 128

    def over_rows(sums, body):
        zero = jnp.zeros((8, D), jnp.float32)

        def step(i, carry):
            r = pl.multiple_of(i * TILE, TILE)
            place = half_lanes((TILE, 1), 0) + r
            usable = (place < length).astype(jnp.float32)
            terms = body(pl.ds(r, TILE), usable)
            return tuple(c + fold(t) for c, t in zip(carry, terms))

        totals = lax.fori_loop(0, D // TILE, step, (zero,) * sums)
        return [jnp.sum(t, axis=0, keepdims=True) for t in totals]

    lane = half_lanes((1, D), 1)

    def square_at(index, total):
        small_out[17:18, :] += jnp.where(lane == index, jnp.sum(total), 0.0)

    for copy in prepare:
        copy.start()
    barrier = pltpu.get_barrier_semaphore()

    def greet_one(offset):
        pl.semaphore_signal(barrier, inc=1, device_id=device(offset)[1], device_id_type=MESH)

    each_other(greet_one)
    pl.semaphore_wait(barrier, 31)
    own_spread().start()
    each_other(lambda offset: spread_copy(offset).start())
    make_pieces()
    planner.opened = 3
    tick(0.5)
    planner.spend(3.0, z=42.0, x=21.0, y=21.0)
    e_load = pltpu.make_async_copy(e_ref, states.at[2], state_sem.at[2])
    e_load.start()
    load(9, cot_ref).start()
    small_out[...] = jnp.zeros_like(small_out)
    turn_back()
    planner.spend(56.0, z=42.0, x=21.0, y=21.0)
    for i in range(3):
        weight(i, 1 + i).start()
    own_back().wait()
    each_other(lambda offset: back_copy(offset).wait())
    planner.spend(112.0)
    planner.opened = GATHERED
    tick(0.5)
    x_store = pltpu.make_async_copy(x_held, x_out, acc_sem.at[1])
    x_store.start()

    for i, (slot, offset, scale) in enumerate(((4, 0, 0.125), (5, None, None), (6, 1, None))):
        load_weight(i, 1 + i).wait()
        product_into(lambda: x_held[...].reshape(1024, D), 1 + i, put_low(slot, offset, scale))
        store(slot, (q_out, k_out, v_out)[i]).start()
        tick(2.5)
    refs_held = [pool.at[slot] for slot in (4, 5, 6, 7)]
    attend_loop(True, 256, length, *refs_held, 4.5, (0, 1024), 1024)
    store(7, o_out).start()
    lse_copy = pltpu.make_async_copy(lse_held, lse_out, state_sem.at[3])
    lse_copy.start()
    w_copy = weight(3, 1)
    w_copy.start()
    w_copy.wait()
    product_into(lambda: pool[7], 1, put_acc(2))
    tick(2.5)
    store(4, q_out).wait()

    def first_norm(rows, usable):
        held_rows = pl.ds(pl.multiple_of(rows.start // 32, TILE // 32), TILE // 32)
        x = x_held[held_rows].reshape(TILE, D).astype(jnp.float32)
        a = acc[rows, :]
        total = x + a
        acc[rows, :] = total
        h = norm_parts(total)[0] * par[11:12, :] + par[12:13, :]
        held[rows, :] = h
        pool[4, rows, :] = h.astype(jnp.bfloat16)
        return usable * x * x, usable * a * a, usable * h * h

    for index, total in enumerate(over_rows(3, first_norm)):
        square_at(index, total)
    store(4, h1_out).start()
    r1_copy = pltpu.make_async_copy(acc, r1_out, acc_sem.at[0])
    r1_copy.start()
    tick(4.0)

    for c, slot in ((4, 2), (5, 3), (6, 1)):
        weight(c, slot).start()
    store(5, k_out).wait()
    load_weight(4, 2).wait()
    product_into(lambda: pool[4], 2, put_low(5, 3, 0.125))
    store(5, cq_out).start()
    w_copy = weight(7, 2)
    w_copy.start()
    tick(2.5)
    e_load.wait()
    load_weight(5, 3).wait()
    load_weight(6, 1).wait()

    def put_keys(n, value):
        states[0, :, pl.ds(n, 256)] = value.astype(jnp.bfloat16)

    def put_values(n, value):
        states[1, :, pl.ds(n, 256)] = (value + row(4, n)).astype(jnp.bfloat16)

    product_into(lambda: states[2], 3, put_keys)
    product_into(lambda: states[2], 1, put_values)
    state_stores = [
        pltpu.make_async_copy(states.at[0], ck_out, state_sem.at[0]),
        pltpu.make_async_copy(states.at[1], cv_out, state_sem.at[1]),
    ]
    for copy in state_stores:
        copy.start()
    tick(1.0)
    store(6, v_out).wait()
    lse_copy.wait()
    attend_loop(
        False,
        512,
        state_lengths_ref[me],
        pool.at[5],
        states.at[0],
        states.at[1],
        pool.at[6],
        1.6,
        (0, 1024),
        128,
    )
    store(6, oc_out).start()
    lse_copy = pltpu.make_async_copy(lse_held, lse_cross_out, state_sem.at[3])
    lse_copy.start()
    w_copy.wait()
    r1_copy.wait()
    product_into(lambda: pool[6], 2, put_acc(5))
    tick(2.5)
    weight(EXPAND_AT[0], 0).start()
    store(7, o_out).wait()

    def second_norm(rows, usable):
        c = acc[rows, :]
        total = held[rows, :] + c
        acc[rows, :] = total
        h = norm_parts(total)[0] * par[13:14, :] + par[14:15, :]
        held[rows, :] = h
        pool[7, rows, :] = h.astype(jnp.bfloat16)
        return usable * c * c, usable * h * h

    for index, total in enumerate(over_rows(2, second_norm)):
        square_at(3 + index, total)
    store(7, h2_out).start()
    r2_copy = pltpu.make_async_copy(acc, r2_out, acc_sem.at[0])
    r2_copy.start()
    tick(4.0)

    store(4, h1_out).wait()
    store(5, cq_out).wait()
    g_slots, slope_slots = (4, 6), (5, 8)
    r2_copy.wait()
    store(6, oc_out).wait()
    for j in range(5):
        if j > 1:
            store(g_slots[j % 2], g_out.at[j - 2]).wait()
            store(slope_slots[j % 2], gp_out.at[j - 2]).wait()
        if j < 4:
            load_weight(EXPAND_AT[j], j % 2).wait()
        if j > 0:
            load_weight(SHRINK_AT[j - 1], 2 + (j - 1) % 2).wait()

        def body(i, carry, j=j):
            n = pl.multiple_of(i * 256, 256)
            here = pl.ds(n, 256)
            if j < 4:
                offset = par[pl.ds(6 + i, 1), j * 256 : j * 256 + 256]
                u = product(pool[7], pool[j % 2, :, here]) + offset
            if j > 0:
                more = product(pool[g_slots[(j - 1) % 2]], pool[2 + (j - 1) % 2, :, here])
                if j == 1:
                    acc[:, here] = more + row(10, n)
                else:
                    acc[:, here] += more
            if j < 4:
                g, slope = gelu_parts(u)
                pool[g_slots[j % 2], :, here] = g.astype(jnp.bfloat16)
                pool[slope_slots[j % 2], :, here] = slope.astype(jnp.bfloat16)
            return carry

        ahead = [planner.tick(2.2 if j < 4 else 0.6) for _ in range(4)]

        def body_and_stages(i, carry, body=body, ahead=ahead):
            body(i, carry)
            for n in range(4):
                if ahead[n]:

                    @pl.when(i == n)
                    def _(events=ahead[n]):
                        emit_all(events)

            return carry

        lax.fori_loop(0, 4, body_and_stages, 0)
        if j < 4:
            store(g_slots[j % 2], g_out.at[j]).start()
            store(slope_slots[j % 2], gp_out.at[j]).start()
        if j < 3:
            weight(EXPAND_AT[j + 1], (j + 1) % 2).start()
        if j < 4:
            weight(SHRINK_AT[j], 2 + j % 2).start()

    load(9, cot_ref).wait()

    def third_norm(rows, usable):
        m = acc[rows, :]
        unit, scale = norm_parts(held[rows, :] + m)
        gain = par[15:16, :]
        pool[0, rows, :] = (unit * gain + par[16:17, :]).astype(jnp.bfloat16)
        grad = pool[9, rows, :].astype(jnp.float32) * usable
        inner = grad * gain
        first = jnp.mean(inner, axis=1, keepdims=True)
        second = jnp.mean(inner * unit, axis=1, keepdims=True)
        back = scale * (inner - first - unit * second)
        acc[rows, :] = back
        low = back.astype(jnp.bfloat16)
        pool[1, rows, :] = low
        return usable * m * m, grad * unit, grad, low.astype(jnp.float32)

    m_total, gain_sum, shift_sum, offset_sum = over_rows(4, third_norm)
    square_at(5, m_total)
    small_out[15:16, :] = gain_sum
    small_out[16:17, :] = shift_sum
    small_out[10:11, :] = offset_sum
    last = [
        store(0, y_out),
        store(1, dm_out),
        pltpu.make_async_copy(acc, d_third_out, acc_sem.at[0]),
    ]
    for copy in last:
        copy.start()
    for c in range(GATHERED):
        emit_all(planner.until(c))
    for copy in last + state_stores + [lse_copy, x_store]:
        copy.wait()
    store(7, h2_out).wait()
    store(6, g_out.at[3]).wait()
    store(8, gp_out.at[3]).wait()


def forward(scalars, tokens, weights, states, cotangent, params):
    any_space = pl.BlockSpec(memory_space=pl.ANY)
    vmem = pl.BlockSpec(memory_space=pltpu.VMEM)
    shape = jax.ShapeDtypeStruct
    dma = pltpu.SemaphoreType.DMA
    low = jnp.bfloat16
    wide = jnp.float32
    square = shape((1024, D), low)
    square_wide = shape((1024, D), wide)
    lse = shape((8, 8, 1024), wide)
    short = shape((128, D), low)
    blocks = shape((4, 1024, D), low)
    outs = (
        shape((32, 32, D), low),
        shape((GATHERED, 4, 256, D), low),
        square,
        square,
        square,
        square,
        lse,
        square,
        short,
        short,
        square,
        lse,
        square_wide,
        square_wide,
        square,
        square,
        blocks,
        blocks,
        square,
        square,
        square_wide,
        shape((24, D), wide),
    )
    return pl.pallas_call(
        forward_kernel,
        out_shape=outs,
        in_specs=[SCALARS] * 3 + [any_space] * 6 + [vmem],
        out_specs=(any_space,) * 21 + (vmem,),
        scratch_shapes=[
            pltpu.VMEM((10, 1024, D), low),
            pltpu.VMEM((1024, D), wide),
            pltpu.VMEM((1024, D), wide),
            pltpu.VMEM((128, 1024), wide),
            pltpu.VMEM((8, 8, 1024), wide),
            pltpu.VMEM((3, 128, D), low),
            pltpu.VMEM((32, 32, D), low),
            pltpu.VMEM((32, 32, D), low),
            pltpu.VMEM((32, 32, D), low),
            pltpu.VMEM((GATHERED, 32, D), low),
            pltpu.VMEM((2, 8, 256, 128), wide),
            pltpu.VMEM((2, 32, FF), wide),
            pltpu.VMEM((4, 32, D), wide),
            dma((22,)),
            dma((10,)),
            dma((10,)),
            dma((4,)),
            dma((2,)),
            dma((32,)),
            dma((32,)),
            dma((32,)),
            dma((32,)),
        ]
        + gather_sems(GATHERED),
        compiler_params=pltpu.CompilerParams(
            collective_id=3, has_side_effects=True, vmem_limit_bytes=62 * MIB
        ),
    )(*scalars, tokens.reshape(32, 32, D), *weights, states, cotangent, params)


def add_blocks(target, first, second, planes, rows, step):
    per_plane = rows // step

    def body(i, carry):
        s = i // per_plane
        r = pl.multiple_of((i % per_plane) * step, step)
        target(s, r, first(s, r) + second(s, r))
        return carry

    lax.fori_loop(0, planes * per_plane, body, 0)


POOL = 8
G_SLOTS = 3
R_SLOTS = 4
PLAN = {"core": 4.5, "load": 2.2, "a": 16.5, "b": 9.5, "z": 9.5, "bb": 4.0, "ba": 6.5, "bc": 3.5}


class Planner:
    def __init__(self):
        self.now = 0.0
        self.links = {"core": 0.0, "x": 0.0, "y": 0.0, "z": 0.0, "load": 0.0}
        self.stage = {}
        self.ready = {}

    def link_of(self, c, stage):
        first, second = ("x", "y") if c % 2 == 0 else ("y", "x")
        return {
            0: ("core", "core"),
            1: ("load", "load"),
            2: (first, "a"),
            3: (second, "b"),
            4: ("z", "z"),
            5: (second, "bb"),
            6: (first, "ba"),
            7: ("core", "bc"),
            8: (None, None),
        }[stage]

    def can(self, c):
        stage = self.stage[c]
        if stage > 8:
            return False
        if stage == 1 and c >= R_SLOTS and self.stage[c - R_SLOTS] <= 3:
            return False
        return True

    def emit(self, c):
        stage = self.stage[c]
        link, kind = self.link_of(c, stage)
        self.now = max(self.now, self.ready[c]) + {2: 0.8, 3: 0.5, 4: 0.3, 5: 0.2}.get(stage, 0.1)
        if link is not None:
            begin = max(self.now, self.links[link])
            span = PLAN[kind]
            self.links[link] = begin + span - 1.0
            self.ready[c] = begin + span
        self.stage[c] = stage + 1
        return (stage, c)

    def tick(self, spent):
        self.now += spent
        events = []
        progress = True
        while progress:
            progress = False
            for c in sorted(self.stage):
                if self.can(c) and self.ready[c] <= self.now:
                    events.append(self.emit(c))
                    progress = True
        return events

    def produce(self, c):
        self.stage[c] = 0
        self.ready[c] = self.now
        return [self.emit(c)]

    def until(self, done):
        events = []
        while not done():
            choices = [c for c in sorted(self.stage) if self.can(c)]
            c = min(choices, key=lambda i: (self.ready[i], i))
            events.append(self.emit(c))
        return events

    def free_slot(self, c):
        before = c - G_SLOTS
        if before < 0:
            return []
        return self.until(lambda: self.stage[before] > 2)

    def drain(self, tasks, spent):
        events = []
        waiting = list(tasks)
        while waiting or any(s <= 8 for s in self.stage.values()):
            choices = [c for c in sorted(self.stage) if self.can(c)]
            best = min(choices, key=lambda i: (self.ready[i], i)) if choices else None
            open_tasks = [t for t in waiting if all(self.stage[c] > 8 for c in t[0])]
            if open_tasks and (best is None or self.ready[best] > self.now):
                task = open_tasks[0]
                waiting.remove(task)
                self.now += spent
                events.append(("task", task[1]))
            else:
                events.append(self.emit(best))
        return events


def backward_kernel(
    lengths_ref,
    state_lengths_ref,
    dm_ref,
    d_third_ref,
    g_ref,
    gp_ref,
    full_ref,
    h2_ref,
    h1_ref,
    x_in_ref,
    e_ref,
    oc_ref,
    o_ref,
    r1_ref,
    r2_ref,
    q_ref,
    k_ref,
    v_ref,
    cq_ref,
    ck_ref,
    cv_ref,
    lse_ref,
    lse_cross_ref,
    gains_ref,
    small_ref,
    rows_ref,
    cols_ref,
    token_grad_ref,
    state_grad_ref,
    out_ref,
    totals_ref,
    rows_out,
    cols_out,
    scale_out,
    half,
    pool,
    acc,
    made,
    summed,
    quarter,
    eighth,
    pieces,
    stream,
    dq_t,
    dk_sum,
    dv_sum,
    lse_held,
    states,
    states_t,
    small,
    small_in,
    small_sum,
    small_z,
    part,
    whole,
    load_sem,
    stream_sem,
    state_sem,
    half_sem,
    scan_sem,
    line_send_sem,
    line_recv_sem,
    send_sem,
    recv_sem,
    z_send_sem,
    z_recv_sem,
    place_sem,
    small_send_sem,
    small_recv_sem,
):
    core, x, y, z, other_core, other_x, other_y, others_z = neighbours()
    me = lax.axis_index("rep") * 4 + z
    kept = pl.multiple_of(core * 128, 128)
    given = pl.multiple_of(128 - core * 128, 128)
    planner = Planner()
    place_of = (12, 8, 13, 9, 14, 10, 15, 11, 7, 4, 5, 6, 3, 0, 1, 2)

    def axes(c):
        if c % 2 == 0:
            return x, y, other_x, other_y
        return y, x, other_y, other_x

    def core_copy(c):
        source = made.at[c % G_SLOTS, :, pl.ds(given, 128), :]
        return remote(source, half.at[c], send_sem.at[0, c], recv_sem.at[0, c], other_core)

    def half_copy(c):
        return pltpu.make_async_copy(
            half.at[c], summed.at[c % R_SLOTS], half_sem.at[c % R_SLOTS]
        )

    def first_copy(c):
        a, b, first, second = axes(c)
        rows = pl.ds(pl.multiple_of(64 - a * 64, 64), 64)
        source = summed.at[c % R_SLOTS, :, rows, :]
        return remote(source, quarter.at[c], send_sem.at[1, c], recv_sem.at[1, c], first)

    def second_copy(c):
        a, b, first, second = axes(c)
        rows = pl.ds(pl.multiple_of(32 - b * 32, 32), 32)
        source = quarter.at[c, :, rows, :]
        return remote(source, eighth.at[c], send_sem.at[2, c], recv_sem.at[2, c], second)

    def z_copy(c, d):
        device = others_z[d]
        return remote(
            eighth.at[c, device[1]],
            pieces.at[c, d],
            z_send_sem.at[c, d],
            z_recv_sem.at[c, d],
            device,
        )

    def own_rows_of(c):
        a, b, first, second = axes(c)
        return pl.ds(pl.multiple_of(core * 128 + a * 64 + b * 32, 32), 32)

    def place_copy(c):
        return pltpu.make_async_copy(
            pieces.at[c, 0], out_ref.at[place_of[c], own_rows_of(c), :], place_sem.at[c]
        )

    def back_second(c):
        device = axes(c)[3]
        target = out_ref.at[place_of[c], own_rows_of(c), :]
        return remote(pieces.at[c, 0], target, send_sem.at[3, c], recv_sem.at[3, c], device)

    def back_first(c):
        a, b, first, second = axes(c)
        block = out_ref.at[place_of[c], pl.ds(pl.multiple_of(core * 128 + a * 64, 64), 64), :]
        return remote(block, block, send_sem.at[4, c], recv_sem.at[4, c], first)

    def back_core(c):
        block = out_ref.at[place_of[c], pl.ds(kept, 128), :]
        return remote(block, block, send_sem.at[5, c], recv_sem.at[5, c], other_core)

    def emit(stage, c):
        a, b, first, second = axes(c)
        slot = c % R_SLOTS
        if stage == 0:
            core_copy(c).start()
        if stage == 1:
            if c >= R_SLOTS:
                first_copy(c - R_SLOTS).wait_send()
            core_copy(c).wait_recv()
            half_copy(c).start()
        if stage == 2:
            half_copy(c).wait()

            def put(s, r, value):
                summed[slot, s, pl.ds(r, 32), :] = value

            add_blocks(
                put,
                lambda s, r: summed[slot, s, pl.ds(r, 32), :],
                lambda s, r: made[c % G_SLOTS, s, pl.ds(pl.multiple_of(kept + r, 32), 32), :],
                4,
                128,
                32,
            )
            first_copy(c).start()
            core_copy(c).wait_send()
        if stage == 3:
            first_copy(c).wait_recv()

            def put(s, r, value):
                quarter[c, s, pl.ds(r, 32), :] = value

            add_blocks(
                put,
                lambda s, r: quarter[c, s, pl.ds(r, 32), :],
                lambda s, r: summed[slot, s, pl.ds(pl.multiple_of(a * 64 + r, 32), 32), :],
                4,
                64,
                32,
            )
            second_copy(c).start()
        if stage == 4:
            second_copy(c).wait_recv()

            def put(s, r, value):
                eighth[c, s, pl.ds(r, 32), :] = value

            add_blocks(
                put,
                lambda s, r: eighth[c, s, pl.ds(r, 32), :],
                lambda s, r: quarter[c, s, pl.ds(pl.multiple_of(b * 32 + r, 32), 32), :],
                4,
                32,
                32,
            )
            for d in range(3):
                z_copy(c, d).start()
        if stage == 5:
            for d in range(3):
                z_copy(c, d).wait_recv()
            total = eighth[c, z].astype(jnp.float32)
            for d in range(3):
                total = total + pieces[c, d].astype(jnp.float32)
            pieces[c, 0] = total.astype(jnp.bfloat16)
            back_second(c).start()
            place_copy(c).start()
        if stage == 6:
            place_copy(c).wait()
            back_second(c).wait_recv()
            back_first(c).start()
        if stage == 7:
            back_first(c).wait_recv()
            back_core(c).start()
        if stage == 8:
            back_core(c).wait()
            back_first(c).wait_send()
            back_second(c).wait_send()
            for d in range(3):
                z_copy(c, d).wait_send()
            second_copy(c).wait_send()
            if c >= CHUNKS - R_SLOTS:
                first_copy(c).wait_send()

    def emit_all(events):
        for stage, c in events:
            emit(stage, c)

    def tick(spent):
        emit_all(planner.tick(spent))

    def produced(c, spent):
        planner.now += spent
        emit_all(planner.produce(c))
        emit_all(planner.tick(0.0))

    def load(slot, source):
        return pltpu.make_async_copy(source, pool.at[slot], load_sem.at[slot])

    def state_load(index, source):
        return pltpu.make_async_copy(source, states.at[index], state_sem.at[index])

    def turn_tile(target, source):
        def turn(n):
            pool[target, pl.ds(n, 256), :] = pool[source, :, pl.ds(n, 256)].T

        return turn

    def transpose_into(target, source):
        turn = turn_tile(target, source)

        def body(i, carry):
            turn(pl.multiple_of(i * 256, 256))
            return carry

        lax.fori_loop(0, 4, body, 0)

    def product_nn(left, right, put, beside=None):
        def body(i, carry):
            n = pl.multiple_of(i * 256, 256)
            if beside is not None:
                beside(n)
            put(n, product(left(), right(n)))
            return carry

        lax.fori_loop(0, 4, body, 0)

    def product_nt(left, right, put, beside=None):
        def body(i, carry):
            n = pl.multiple_of(i * 256, 256)
            if beside is not None:
                beside(n)
            put(
                n,
                lax.dot_general(
                    left(),
                    right(n),
                    (((1,), (1,)), ((), ())),
                    preferred_element_type=jnp.float32,
                ),
            )
            return carry

        lax.fori_loop(0, 4, body, 0)

    def columns_of(slot):
        return lambda n: pool[slot, :, pl.ds(n, 256)]

    def rows_of(slot):
        return lambda n: pool[slot, pl.ds(n, 256), :]

    def weight_grad(slot_in_made, left, right, beside=None):
        def put(n, value):
            low = value.astype(jnp.bfloat16).reshape(4, 256, 256)
            made[slot_in_made, :, :, pl.ds(n, 256)] = low

        product_nn(left, right, put, beside)

    def add_to_acc(n, value):
        acc[:, pl.ds(n, 256)] += value

    def put_in(slot):
        def put(n, value):
            pool[slot, :, pl.ds(n, 256)] = value.astype(jnp.bfloat16)

        return put

    def norm_back(source, gain_row, gain_at, shift_at, offset_at, target):
        tiles = 8
        rows = 1024 // tiles

        def fetch(i):
            place = pl.ds(pl.multiple_of(i * rows, rows), rows)
            return pltpu.make_async_copy(
                source.at[place, :], stream.at[i % 2], stream_sem.at[i % 2]
            )

        fetch(0).start()

        def body(i, carry):
            gain_sum, shift_sum, offset_sum = carry

            @pl.when(i + 1 < tiles)
            def _():
                fetch(i + 1).start()

            fetch(i).wait()
            r = pl.multiple_of(i * rows, rows)
            values = stream[i % 2]
            centred = values - jnp.mean(values, axis=1, keepdims=True)
            spread = jnp.mean(centred * centred, axis=1, keepdims=True)
            scale = lax.rsqrt(spread + NORM_EPS)
            unit = centred * scale
            grad = acc[pl.ds(r, rows), :]
            inner = grad * gains_ref[gain_row : gain_row + 1, :]
            first = jnp.mean(inner, axis=1, keepdims=True)
            second = jnp.mean(inner * unit, axis=1, keepdims=True)
            back = scale * (inner - first - unit * second)
            acc[pl.ds(r, rows), :] = back
            low = back.astype(jnp.bfloat16)
            pool[target, pl.ds(r, rows), :] = low
            return (
                gain_sum + fold(grad * unit),
                shift_sum + fold(grad),
                offset_sum + fold(low.astype(jnp.float32)),
            )

        zero = jnp.zeros((8, D), jnp.float32)
        sums = lax.fori_loop(0, tiles, body, (zero, zero, zero))
        for row, value in zip((gain_at, shift_at, offset_at), sums):
            small[row : row + 1, :] = jnp.sum(value, axis=0, keepdims=True)

    greet([other_core, other_x, other_y] + others_z)
    load(0, dm_ref).start()
    load(6, h2_ref).start()
    load(2, full_ref.at[SHRINK_AT[0]]).start()
    load(3, gp_ref.at[0]).start()
    load(4, g_ref.at[0]).start()
    load(5, full_ref.at[EXPAND_AT[0]]).start()
    acc_load = pltpu.make_async_copy(d_third_ref, acc, place_sem.at[0])
    acc_load.start()
    small[...] = small_ref[...]
    load(6, h2_ref).wait()
    transpose_into(1, 6)
    load(0, dm_ref).wait()
    acc_load.wait()

    planner.now = 4.0
    plan = []
    for j in range(4):
        entry = []
        planner.now += 3.5
        entry.append(planner.tick(0.0) + planner.free_slot(2 * j))
        planner.now += 2.5
        entry.append(planner.produce(2 * j) + planner.tick(0.0) + planner.free_slot(2 * j + 1))
        planner.now += 2.5
        entry.append(planner.produce(2 * j + 1) + planner.tick(0.0))
        entry.append(planner.tick(2.5))
        plan.append(entry)

    def emit_planned(j, place):
        for n in range(4):
            events = plan[n][place]
            if events:

                @pl.when(j == n)
                def _(events=events):
                    emit_all(events)

    def block(j, carry):
        last = j == 3
        load(2, full_ref.at[SHRINK_AT[0]]).wait()
        load(3, gp_ref.at[0]).wait()

        def put_pre(n, value):
            low = (value * pool[3, :, pl.ds(n, 256)].astype(jnp.float32)).astype(jnp.bfloat16)
            pool[7, :, pl.ds(n, 256)] = low
            small[pl.ds(6 + n // 256, 1), pl.ds(pl.multiple_of(j * 256, 256), 256)] = jnp.sum(
                low.astype(jnp.float32), axis=0, keepdims=True
            )

        load(4, g_ref.at[0]).wait()
        product_nt(lambda: pool[0], rows_of(2), put_pre, turn_tile(6, 4))

        @pl.when(jnp.logical_not(last))
        def _():
            load(2, full_ref.at[SHRINK_AT[0] + 2 * (j + 1) - (j + 1) // 3]).start()
            load(3, gp_ref.at[j + 1]).start()

        @pl.when(last)
        def _():
            load(2, full_ref.at[7]).start()
            load(3, cq_ref).start()

        emit_planned(j, 0)

        @pl.when(jnp.logical_not(last))
        def _():
            load(4, g_ref.at[j + 1]).start()

        @pl.when(last)
        def _():
            load(4, oc_ref).start()

        weight_grad((2 * j) % G_SLOTS, lambda: pool[6], columns_of(0))
        emit_planned(j, 1)
        weight_grad((2 * j + 1) % G_SLOTS, lambda: pool[1], columns_of(7))
        emit_planned(j, 2)
        load(5, full_ref.at[EXPAND_AT[0]]).wait()
        product_nt(lambda: pool[7], rows_of(5), add_to_acc)

        @pl.when(jnp.logical_not(last))
        def _():
            load(5, full_ref.at[EXPAND_AT[1] + 2 * j]).start()

        @pl.when(last)
        def _():
            load(5, full_ref.at[4]).start()

        emit_planned(j, 3)
        return carry

    lax.fori_loop(0, 4, block, 0)

    load(7, h1_ref).start()
    state_loads = [state_load(0, ck_ref), state_load(1, cv_ref), state_load(2, e_ref)]
    for copy in state_loads:
        copy.start()
    lse_load = pltpu.make_async_copy(lse_cross_ref, lse_held, state_sem.at[3])
    lse_load.start()
    norm_back(r2_ref, 13, 13, 14, 5, 0)
    tick(4.0)
    load(4, oc_ref).wait()
    load(2, full_ref.at[7]).wait()
    product_nt(lambda: pool[0], rows_of(2), put_in(4), turn_tile(6, 4))
    load(2, full_ref.at[3]).start()
    tick(2.5)
    emit_all(planner.free_slot(8))
    load(7, h1_ref).wait()
    weight_grad(8 % G_SLOTS, lambda: pool[6], columns_of(0), turn_tile(1, 7))
    load(6, o_ref).start()
    load(7, full_ref.at[5]).start()
    produced(8, 2.5)
    load(3, cq_ref).wait()
    for copy in state_loads:
        copy.wait()
    lse_load.wait()

    def attend_loop(causal, step, length, query, key, value, grad, rows, spent, span=(0, 8)):
        ahead = {n: planner.tick(spent) for n in range(*span)}

        def body(i, carry):
            lanes = pl.ds(pl.multiple_of(i * 128, 128), 128)

            def sums(dq, dv):
                small[rows[0] : rows[0] + 1, lanes] = dq
                small[rows[1] : rows[1] + 1, lanes] = dv

            attend_back_pair(
                causal,
                step,
                length,
                query.at[:, lanes],
                key.at[:, lanes],
                value.at[:, lanes],
                grad.at[:, lanes],
                lse_held.at[pl.ds(i, 1)],
                query.at[:, lanes],
                key.at[:, lanes],
                value.at[:, lanes],
                sums,
                dq_t,
                dk_sum,
                dv_sum,
            )
            for n in range(*span):
                if ahead[n]:

                    @pl.when(i == n)
                    def _(events=ahead[n]):
                        emit_all(events)

            return carry

        lax.fori_loop(*span, body, 0)

    attend_loop(
        False,
        512,
        state_lengths_ref[me],
        pool.at[3],
        states.at[0],
        states.at[1],
        pool.at[4],
        (3, 4),
        2.0,
    )
    lse_load = pltpu.make_async_copy(lse_ref, lse_held, state_sem.at[3])
    lse_load.start()
    emit_all(planner.free_slot(9))
    weight_grad(9 % G_SLOTS, lambda: pool[1], columns_of(3))
    produced(9, 2.5)
    load(5, full_ref.at[4]).wait()
    load(6, o_ref).wait()
    product_nt(lambda: pool[3], rows_of(5), add_to_acc, turn_tile(1, 6))
    load(6, x_in_ref).start()
    load(5, full_ref.at[6]).start()
    load(3, q_ref).start()
    tick(2.5)
    states_t[...] = states[2].T
    for c, index in ((10, 0), (11, 1)):
        emit_all(planner.free_slot(c))
        weight_grad(
            c % G_SLOTS, lambda: states_t[...], lambda n, i=index: states[i, :, pl.ds(n, 256)]
        )
        produced(c, 1.0)
    load(7, full_ref.at[5]).wait()
    load(5, full_ref.at[6]).wait()

    def state_part(n):
        dims = (((1,), (1,)), ((), ()))
        return lax.dot_general(
            states[0], pool[7, pl.ds(n, 256), :], dims, preferred_element_type=jnp.float32
        ) + lax.dot_general(
            states[1], pool[5, pl.ds(n, 256), :], dims, preferred_element_type=jnp.float32
        )

    def put_state(i, carry):
        n = pl.multiple_of(i * 256, 256)
        state_grad_ref[:, pl.ds(n, 256)] = state_part(n).astype(jnp.bfloat16)
        return carry

    lax.fori_loop(0, 4, put_state, 0)
    load(5, k_ref).start()
    load(7, v_ref).start()
    tick(1.0)

    norm_back(r1_ref, 11, 11, 12, 2, 0)
    tick(4.0)
    emit_all(planner.free_slot(12))
    weight_grad(12 % G_SLOTS, lambda: pool[1], columns_of(0))
    produced(12, 2.5)
    load(2, full_ref.at[3]).wait()
    load(6, x_in_ref).wait()
    product_nt(lambda: pool[0], rows_of(2), put_in(4), turn_tile(1, 6))
    load(0, full_ref.at[0]).start()
    load(2, full_ref.at[1]).start()
    load(6, full_ref.at[2]).start()
    tick(2.5)
    load(3, q_ref).wait()
    load(5, k_ref).wait()
    load(7, v_ref).wait()
    lse_load.wait()
    def self_heads(span):
        refs = [pool.at[slot] for slot in (3, 5, 7, 4)]
        attend_loop(True, 256, lengths_ref[me], *refs, (0, 1), 5.0, span)

    def query_key_grad(c, half_of):
        def put(i, carry):
            n = pl.multiple_of((i % 2) * 256 + 512 * half_of, 256)
            value = product(pool[1], pool[3 + 2 * (i // 2), :, pl.ds(n, 256)])
            low = value.astype(jnp.bfloat16).reshape(4, 256, 256)
            made[c % G_SLOTS, :, :, pl.ds(pl.multiple_of(i * 256, 256), 256)] = low
            return carry

        emit_all(planner.free_slot(c))
        lax.fori_loop(0, 4, put, 0)
        produced(c, 2.5)

    self_heads((0, 4))
    query_key_grad(13, 0)
    self_heads((4, 8))

    def small_copy(k):
        source = small if k == 0 else small_sum.at[k - 1]
        device = (other_core, other_x, other_y)[k]
        return remote(source, small_in.at[k], small_send_sem.at[k], small_recv_sem.at[k], device)

    def small_z_copy(d):
        return remote(
            small_sum.at[2],
            small_z.at[z],
            small_send_sem.at[3 + d],
            small_recv_sem.at[3 + d],
            others_z[d],
        )

    def small_step(k):
        small_copy(k).wait()
        before = small[...] if k == 0 else small_sum[k - 1]
        small_sum[k] = before + small_in[k]
        if k < 2:
            small_copy(k + 1).start()
        else:
            small_z[z] = small_sum[2]
            for d in range(3):
                small_z_copy(d).start()

    small_copy(0).start()
    emit_all(planner.free_slot(14))
    weight_grad(14 % G_SLOTS, lambda: pool[1], columns_of(7))
    produced(14, 2.5)
    small_step(0)
    query_key_grad(15, 1)
    small_step(1)
    load(0, full_ref.at[0]).wait()
    product_nt(lambda: pool[3], rows_of(0), add_to_acc)
    tick(2.5)
    small_step(2)
    load(2, full_ref.at[1]).wait()
    product_nt(lambda: pool[5], rows_of(2), add_to_acc)
    tick(2.5)
    for d in range(3):
        small_z_copy(d).wait()
    totals_ref[...] = (small_z[0] + small_z[1]) + (small_z[2] + small_z[3])
    load(6, full_ref.at[2]).wait()

    def put_input(n, value):
        total = acc[:, pl.ds(n, 256)] + value
        pool[4, :, pl.ds(n, 256)] = total.astype(jnp.bfloat16)

    product_nt(lambda: pool[7], rows_of(6), put_input)
    token_copy = pltpu.make_async_copy(pool.at[4], token_grad_ref, load_sem.at[4])
    token_copy.start()
    tick(2.5)

    part[...] = jnp.zeros_like(part)

    def spot(place):
        return (0, 1, 2, 6)[place // 4], (place % 4) * 256

    def scan_load(place):
        slot, row = spot(place)
        return pltpu.make_async_copy(
            out_ref.at[place], pool.at[slot, pl.ds(row, 256), :], scan_sem.at[place]
        )

    scans = {}
    for i in range(2):
        scans[i] = ([(0, 512 * i, 512, i, 0), (2, 512 * i, 512, i, 512)], i, (13, 128 * i))
    for i in range(2, 8):
        scans[i] = ([(1 if i == 2 else i, 0, D, i, 0)], i, (13, 128 * i))
    scans[8] = ([(8 + i, 0, D, 8 + i, 0) for i in range(4)], 8, (14, 0))
    for i in range(4):
        scans[9 + i] = ([(12 + i, 0, D, 12, 0)], 9 + i, (14, 128))

    def scan(name):
        sources, row_lane, (total_row, total_lane) = scans[name]
        width = float(sum(source[2] for source in sources))
        step = 64 if name == 8 else 256

        def body(i, carry):
            cols, weights, total = carry
            r = pl.multiple_of(i * step, step)
            squares = []
            for place, lane, lanes, _, _ in sources:
                slot, row = spot(place)
                tile = pool[slot, pl.ds(row + r, step), lane : lane + lanes]
                squares.append(jnp.square(tile.astype(jnp.float32)))
            row_sum = sum(jnp.sum(square, axis=1, keepdims=True) for square in squares)
            rows = DECAY_RATE * rows_ref[pl.ds(r, step), row_lane : row_lane + 1] + (
                1.0 - DECAY_RATE
            ) * (row_sum / width + FACTOR_EPS)
            rows_out[pl.ds(r, step), row_lane : row_lane + 1] = rows
            inverse = 1.0 / rows
            cols = [c + fold(s) for c, s in zip(cols, squares)]
            weights = [w + fold(s * inverse) for w, s in zip(weights, squares)]
            return cols, weights, total + fold(rows)

        zeros = [jnp.zeros((8, source[2]), jnp.float32) for source in sources]
        cols, weights, total = lax.fori_loop(
            0, 256 // step, body, (zeros, zeros, jnp.zeros((8, 1), jnp.float32))
        )
        for (_, _, lanes, slot, lane), col, weighted in zip(sources, cols, weights):
            here = slice(lane, lane + lanes)
            part[slot : slot + 1, here] += jnp.sum(col, axis=0, keepdims=True)
            part[16 + slot : 17 + slot, here] += jnp.sum(weighted, axis=0, keepdims=True)
        part[total_row : total_row + 1, total_lane : total_lane + 128] += jnp.broadcast_to(
            jnp.sum(total), (1, 128)
        )

    chunk_at = {place: c for c, place in enumerate(place_of)}
    tasks = [
        ([chunk_at[source[0]] for source in scans[name][0]], name)
        for name in (9, 10, 11, 12, 8, 7, 4, 5, 6, 3, 2, 0, 1)
    ]
    loaded = set()
    for c in range(CHUNKS):
        if planner.stage[c] > 8:
            scan_load(place_of[c]).start()
    for first, second in planner.drain(tasks, 1.5):
        if first != "task":
            emit(first, second)
            if first == 8:
                scan_load(place_of[second]).start()
            continue
        for source in scans[second][0]:
            if source[0] not in loaded:
                loaded.add(source[0])
                scan_load(source[0]).wait()
        scan(second)
    total = line_sum(part, whole, line_send_sem, line_recv_sem, z, others_z)
    row_counts = [D] * 12 + [FF]
    means = [total[13:14, 128 * i : 128 * i + 1] / D for i in range(8)]
    means = means + [total[14:15, 0:1] / D] * 4 + [total[14:15, 128:129] / FF]
    cols_new, quotients = [], []
    for slot in range(13):
        new = DECAY_RATE * cols_ref[slot : slot + 1, :] + (1.0 - DECAY_RATE) * (
            total[slot : slot + 1] / row_counts[slot] + FACTOR_EPS
        )
        cols_new.append(new)
        quotients.append(jnp.sum(total[16 + slot : 17 + slot] / new, axis=1, keepdims=True))
        cols_out[slot : slot + 1, :] = new
    expand_quotient = quotients[8] + quotients[9] + quotients[10] + quotients[11]
    for slot in range(13):
        if slot < 8:
            mean_square = means[slot] * quotients[slot] / (D * D)
            rate = STEP_RATE * (OUT_GAIN if slot % 4 == 3 else 1.0)
        else:
            quotient = expand_quotient if slot < 12 else quotients[12]
            mean_square = means[slot] * quotient / (D * FF)
            rate = STEP_RATE
        factor = rate / jnp.maximum(1.0, jnp.sqrt(mean_square) / CLIP_LEVEL)
        scale_out[slot : slot + 1, :] = lax.rsqrt(cols_new[slot] / means[slot]) * factor
    token_copy.wait()


def backward(scalars, held, gains, small, factor_rows, factor_cols):
    any_space = pl.BlockSpec(memory_space=pl.ANY)
    vmem = pl.BlockSpec(memory_space=pltpu.VMEM)
    shape = jax.ShapeDtypeStruct
    dma = pltpu.SemaphoreType.DMA
    low = jnp.bfloat16
    wide = jnp.float32
    rows = small.shape[0]
    return pl.pallas_call(
        backward_kernel,
        out_shape=(
            shape((1024, D), low),
            shape((128, D), low),
            shape((CHUNKS, 256, D), low),
            shape(small.shape, wide),
            shape((256, 128), wide),
            shape((16, D), wide),
            shape((16, D), wide),
            shape((CHUNKS, 4, 128, D), low),
        ),
        in_specs=[SCALARS] * 2 + [any_space] * len(held) + [vmem] * 4,
        out_specs=(any_space, vmem, any_space, vmem, vmem, vmem, vmem, any_space),
        scratch_shapes=[
            pltpu.VMEM((POOL, 1024, D), low),
            pltpu.VMEM((1024, D), wide),
            pltpu.VMEM((G_SLOTS, 4, 256, D), low),
            pltpu.VMEM((R_SLOTS, 4, 128, D), low),
            pltpu.VMEM((CHUNKS, 4, 64, D), low),
            pltpu.VMEM((CHUNKS, 4, 32, D), low),
            pltpu.VMEM((CHUNKS, 3, 32, D), low),
            pltpu.VMEM((2, 128, D), wide),
            pltpu.VMEM((128, 1024), wide),
            pltpu.VMEM((2, 1024, 128), wide),
            pltpu.VMEM((2, 1024, 128), wide),
            pltpu.VMEM((8, 8, 1024), wide),
            pltpu.VMEM((3, 128, D), low),
            pltpu.VMEM((D, 128), low),
            pltpu.VMEM((rows, D), wide),
            pltpu.VMEM((3, rows, D), wide),
            pltpu.VMEM((3, rows, D), wide),
            pltpu.VMEM((4, rows, D), wide),
            pltpu.VMEM((32, D), wide),
            pltpu.VMEM((4, 32, D), wide),
            dma((POOL,)),
            dma((2,)),
            dma((4,)),
            dma((R_SLOTS,)),
            dma((CHUNKS,)),
            dma((3,)),
            dma((3,)),
            dma((6, CHUNKS)),
            dma((6, CHUNKS)),
            dma((CHUNKS, 3)),
            dma((CHUNKS, 3)),
            dma((CHUNKS,)),
            dma((6,)),
            dma((6,)),
        ],
        compiler_params=pltpu.CompilerParams(
            collective_id=0, has_side_effects=True, vmem_limit_bytes=62 * MIB
        ),
    )(*scalars, *held, gains, small, factor_rows, factor_cols)[0:7]


def line_sum(part, whole, send_sem, recv_sem, z, others_z):
    copies = [
        remote(part, whole.at[z], send_sem.at[d], recv_sem.at[d], others_z[d]) for d in range(3)
    ]
    for copy in copies:
        copy.start()
    whole[z] = part[...]
    for copy in copies:
        copy.wait()
    return (whole[0] + whole[1]) + (whole[2] + whole[3])


def update_attention_kernel(
    grad_ref, weight_ref, rows_ref, scale_ref, grad_out, new_out, copy_out, grads, change
):
    block = grad_ref.shape[1]
    for i in range(8):
        rows = lax.rsqrt(rows_ref[:, i : i + 1])
        every = pl.ds(i, block, stride=8)
        for lane in range(8):
            columns = slice(lane * 128, lane * 128 + 128)
            if i < 2:
                start = 512 * i + 128 * (lane % 4)
                grad = grad_ref[2 * (lane // 4), :, start : start + 128]
            else:
                grad = grad_ref[1 if i == 2 else i, :, columns]
            grad = grad.astype(jnp.float32)
            grads[lane, every, :] = grad
            change[lane, every, :] = grad * rows * scale_ref[i : i + 1, columns]
    for lane in range(8):
        columns = slice(lane * 128, lane * 128 + 128)
        grad_out[:, columns] = grads[lane]
        new = weight_ref[:, columns] - change[lane]
        new_out[:, columns] = new
        copy_out[:, columns] = new.astype(jnp.bfloat16)


def update_attention(grads, weights, rows, scale):
    block = 64
    wide = pl.BlockSpec((block * 8, D), lambda i: (i, 0))
    shape = jax.ShapeDtypeStruct
    new = pl.pallas_call(
        update_attention_kernel,
        grid=(256 // block,),
        out_shape=(
            shape((2048, D), jnp.float32),
            shape((2048, D), jnp.float32),
            shape((2048, D), jnp.bfloat16),
        ),
        in_specs=[
            pl.BlockSpec((8, block, D), lambda i: (0, i, 0)),
            wide,
            pl.BlockSpec((block, 128), lambda i: (i, 0)),
            pl.BlockSpec((16, D), lambda i: (0, 0)),
        ],
        out_specs=(wide,) * 3,
        scratch_shapes=[pltpu.VMEM((8, block * 8, 128), jnp.float32)] * 2,
        compiler_params=pltpu.CompilerParams(vmem_limit_bytes=62 * MIB),
    )(grads, weights.reshape(2048, D), rows, scale)
    return [t.reshape(256, 8, D) for t in new]


def update_kernel(
    first, slots, grad_ref, weight_ref, rows_ref, scale_ref, grad_out, new_out, copy_out
):
    spans = 4 if slots == 4 else 1
    wide = D // spans
    for i in range(slots):
        grads = grad_ref[i].astype(jnp.float32)
        changes = grads * (lax.rsqrt(rows_ref[...]) * scale_ref[first + i : first + i + 1, :])
        for s in range(spans):
            start = s * D + i * wide
            columns = slice(start, start + wide)
            part = slice(s * wide, s * wide + wide)
            grad_out[:, columns] = grads[:, part]
            new = weight_ref[:, columns] - changes[:, part]
            new_out[:, columns] = new
            copy_out[:, columns] = new.astype(jnp.bfloat16)


def update_plain(grads, weights, rows, scale, first, slots, grad_map):
    count, width = weights.shape
    block = 256 // slots
    wide = pl.BlockSpec((block, width), lambda i: (i, 0))
    shape = jax.ShapeDtypeStruct
    return pl.pallas_call(
        lambda *refs: update_kernel(first, slots, *refs),
        grid=(count // block,),
        out_shape=(
            shape(weights.shape, jnp.float32),
            shape(weights.shape, jnp.float32),
            shape(weights.shape, jnp.bfloat16),
        ),
        in_specs=[
            pl.BlockSpec((slots, block, D), grad_map),
            wide,
            pl.BlockSpec((block, 1), lambda i: (i, 0)),
            pl.BlockSpec((16, D), lambda i: (0, 0)),
        ],
        out_specs=(wide,) * 3,
        compiler_params=pltpu.CompilerParams(vmem_limit_bytes=62 * MIB),
    )(grads, weights, rows, scale)


def update_direct(grads, rows, scale, attention_weights, expand_weight, shrink_weight):
    shr_rows = rows[:, 9:13].T.reshape(-1, 1)
    attention = update_attention(grads, attention_weights, rows, scale)
    expand = update_plain(grads, expand_weight, rows[:, 8:9], scale, 8, 4, lambda i: (2, i, 0))
    shrink = update_plain(
        grads, shrink_weight, shr_rows, scale, 12, 1, lambda i: (12 + i, 0, 0)
    )
    return attention, expand, shrink, (rows[:, 0:8].T, rows[:, 8], shr_rows[:, 0])


def as_rows(vector):
    rows = -(-vector.shape[0] // 1024) * 8
    return jnp.pad(vector, (0, rows * 128 - vector.shape[0])).reshape(rows, 128)


def masked_scores(query_part, key_heads, first_row, valid_count, causal):
    scores = jnp.einsum("qhd,khd->hqk", query_part, key_heads, preferred_element_type=jnp.float32)
    key_places = jnp.arange(key_heads.shape[0], dtype=jnp.int32)[None, :]
    usable = key_places < valid_count
    if causal:
        query_places = first_row + jnp.arange(query_part.shape[0], dtype=jnp.int32)[:, None]
        usable = usable & (key_places <= query_places)
    return jnp.where(usable[None], scores, MASKED)


def attend_forward(queries, key_heads, values, valid_count, causal):
    query_rows = queries.shape[0]
    step_rows = min(512, query_rows)
    outputs, stored = ([], [])
    for b in range(query_rows // step_rows):
        first_row = b * step_rows
        key_end = first_row + step_rows if causal else key_heads.shape[0]
        scores = masked_scores(
            queries[first_row : first_row + step_rows],
            key_heads[:key_end],
            first_row,
            valid_count,
            causal,
        )
        row_max = jnp.max(scores, axis=-1, keepdims=True)
        raised = jnp.exp(scores - row_max)
        totals = jnp.sum(raised, axis=-1, keepdims=True)
        probs_low = (raised / totals).astype(jnp.bfloat16)
        outputs.append(
            jnp.einsum(
                "hqk,khd->qhd", probs_low, values[:key_end], preferred_element_type=jnp.float32
            )
        )
        stored.append(row_max + jnp.log(totals))
    return (jnp.concatenate(outputs, axis=0), stored)


def attend_backward(queries, key_heads, values, grad_out, stored, valid_count, causal):
    query_rows = queries.shape[0]
    key_rows = key_heads.shape[0]
    step_rows = min(512, query_rows)
    grad_queries = []
    grad_keys = jnp.zeros(key_heads.shape, jnp.float32)
    grad_values = jnp.zeros(values.shape, jnp.float32)
    for b in range(query_rows // step_rows):
        first_row = b * step_rows
        key_end = first_row + step_rows if causal else key_rows
        query_part = queries[first_row : first_row + step_rows]
        grad_part = grad_out[first_row : first_row + step_rows]
        scores = masked_scores(query_part, key_heads[:key_end], first_row, valid_count, causal)
        probs = jnp.exp(scores - stored[b])
        probs_low = probs.astype(jnp.bfloat16)
        grad_probs = jnp.einsum(
            "qhd,khd->hqk", grad_part, values[:key_end], preferred_element_type=jnp.float32
        )
        value_part = jnp.einsum(
            "hqk,qhd->khd", probs_low, grad_part, preferred_element_type=jnp.float32
        )
        grad_scores = probs * (grad_probs - jnp.sum(probs * grad_probs, axis=-1, keepdims=True))
        scores_low = grad_scores.astype(jnp.bfloat16)
        grad_queries.append(
            jnp.einsum(
                "hqk,khd->qhd", scores_low, key_heads[:key_end], preferred_element_type=jnp.float32
            )
        )
        key_part = jnp.einsum(
            "hqk,qhd->khd", scores_low, query_part, preferred_element_type=jnp.float32
        )
        padding = ((0, key_rows - key_end), (0, 0), (0, 0))
        grad_keys = grad_keys + jnp.pad(key_part, padding)
        grad_values = grad_values + jnp.pad(value_part, padding)
    return (jnp.concatenate(grad_queries, axis=0), grad_keys, grad_values)


def gather_rows(piece):
    return lax.all_gather(piece, ("shard", "rep"), axis=0, tiled=True)


def own_piece(block, replicas):
    rows = block.shape[0] // replicas
    return lax.dynamic_slice_in_dim(block, lax.axis_index("rep") * rows, rows, axis=0)


def scatter_rows(grad):
    piece = lax.psum_scatter(
        grad.astype(jnp.bfloat16), ("shard", "rep"), scatter_dimension=0, tiled=True
    )
    return lax.all_gather(piece, "rep", axis=0, tiled=True)


def local_factors(grad, rows):
    square = grad * grad
    rows_new = DECAY_RATE * rows + (1.0 - DECAY_RATE) * jnp.mean(square + FACTOR_EPS, axis=-1)
    col_part = jnp.sum(square + FACTOR_EPS, axis=0)
    weighted = jnp.sum(square / rows_new[..., None], axis=0)
    return rows_new, col_part, weighted, jnp.sum(rows_new, axis=0)


def finish_factors(grad, weight, rows_new, cols, col_sum, weighted, row_total, row_count, rate):
    cols_new = DECAY_RATE * cols + (1.0 - DECAY_RATE) * col_sum / row_count
    mean_rows = row_total / row_count
    mean_square = mean_rows * jnp.sum(weighted / cols_new, axis=-1) / (row_count * cols.shape[-1])
    factor = rate / jnp.maximum(1.0, jnp.sqrt(mean_square) / CLIP_LEVEL)
    scaled = lax.rsqrt(cols_new / mean_rows[..., None]) * factor[..., None]
    fresh = weight - grad * (lax.rsqrt(rows_new)[..., None] * scaled[None])
    return fresh, cols_new


def plain_device(
    tokens,
    encoder,
    cotangent,
    lengths,
    encoder_lengths,
    dealt_order,
    attention_weights,
    expand_weight,
    shrink_weight,
    small_params,
    attention_rows,
    attention_cols,
    expand_rows,
    expand_cols,
    shrink_rows,
    shrink_cols,
    small_moment,
):
    devices = lax.axis_size(("rep", "shard"))
    replicas = lax.axis_size("rep")
    shards = lax.axis_size("shard")
    slot_tokens = tokens.shape[0]
    slot_states = encoder.shape[0]
    position = lax.axis_index(("rep", "shard"))
    inverse = (
        jnp.zeros((devices,), jnp.int32).at[dealt_order].set(jnp.arange(devices, dtype=jnp.int32))
    )
    qkv_piece = own_piece(attention_weights[:, 0:3, :].reshape(-1, 3 * D), replicas)
    rest_piece = own_piece(attention_weights[:, 3:8, :].reshape(-1, 5 * D), replicas)
    qkv_full = gather_rows(qkv_piece.astype(jnp.bfloat16))
    rest_full = gather_rows(rest_piece.astype(jnp.bfloat16))
    expand_full = gather_rows(own_piece(expand_weight, replicas).astype(jnp.bfloat16))
    shrink_full = gather_rows(own_piece(shrink_weight, replicas).astype(jnp.bfloat16))
    spread = lax.all_to_all(
        tokens.reshape(devices, slot_tokens // devices, D),
        ("rep", "shard"),
        split_axis=0,
        concat_axis=0,
        tiled=True,
    )
    picked = jnp.take(spread, inverse, axis=0)
    tokens = lax.all_to_all(
        picked, ("rep", "shard"), split_axis=0, concat_axis=0, tiled=True
    ).reshape(slot_tokens, D)
    states = encoder
    incoming = cotangent
    valid_tokens = lengths[position]
    valid_states = encoder_lengths[position]
    matrices = [qkv_full[:, i * D : (i + 1) * D] for i in range(3)] + [
        rest_full[:, i * D : (i + 1) * D] for i in range(5)
    ]
    parts = unpack(small_params)
    token_heads = (slot_tokens, HEADS, HEAD_DIM)
    state_heads = (slot_states, HEADS, HEAD_DIM)
    q_self = ((forward_product(tokens, matrices[0]) + parts[0]) * 0.125).astype(
        jnp.bfloat16
    )
    k_self = forward_product(tokens, matrices[1]).astype(jnp.bfloat16)
    v_self = (forward_product(tokens, matrices[2]) + parts[1]).astype(jnp.bfloat16)
    o_self, lse_self = attend_forward(
        q_self.reshape(token_heads),
        k_self.reshape(token_heads),
        v_self.reshape(token_heads),
        valid_tokens,
        True,
    )
    o_self_low = o_self.reshape(slot_tokens, D).astype(jnp.bfloat16)
    branch_a = forward_product(o_self_low, matrices[3]) + parts[2]
    tokens_wide = tokens.astype(jnp.float32)
    hidden_one, norm_one_back = jax.vjp(layer_norm, tokens_wide + branch_a, parts[8], parts[9])
    hidden_one_low = hidden_one.astype(jnp.bfloat16)
    q_cross = (
        (forward_product(hidden_one_low, matrices[4]) + parts[3]) * 0.125
    ).astype(jnp.bfloat16)
    k_cross = forward_product(states, matrices[5]).astype(jnp.bfloat16)
    v_cross = (forward_product(states, matrices[6]) + parts[4]).astype(jnp.bfloat16)
    o_cross, lse_cross = attend_forward(
        q_cross.reshape(token_heads),
        k_cross.reshape(state_heads),
        v_cross.reshape(state_heads),
        valid_states,
        False,
    )
    o_cross_low = o_cross.reshape(slot_tokens, D).astype(jnp.bfloat16)
    branch_c = forward_product(o_cross_low, matrices[7]) + parts[5]
    hidden_two, norm_two_back = jax.vjp(layer_norm, hidden_one + branch_c, parts[10], parts[11])
    hidden_two_low = hidden_two.astype(jnp.bfloat16)
    pre_act = forward_product(hidden_two_low, expand_full) + parts[6]
    activated, gelu_back = jax.vjp(gelu_exact, pre_act)
    activated_low = activated.astype(jnp.bfloat16)
    branch_m = forward_product(activated_low, shrink_full) + parts[7]
    result, norm_three_back = jax.vjp(layer_norm, hidden_two + branch_m, parts[12], parts[13])
    usable_rows = (jnp.arange(slot_tokens, dtype=jnp.int32) < valid_tokens).astype(jnp.float32)[
        :, None
    ]
    squares = jnp.stack(
        [
            jnp.sum(usable_rows * t * t)
            for t in (tokens_wide, branch_a, hidden_one, branch_c, hidden_two, branch_m)
        ]
    )
    d_third, d_gain_three, d_shift_three = norm_three_back(
        incoming.astype(jnp.float32) * usable_rows
    )
    d_mlp = d_third.astype(jnp.bfloat16)
    grad_shrink = weight_product(activated_low, d_mlp)
    grad_shrink_offset = row_sum(d_mlp)
    d_activated = input_product(d_mlp, shrink_full)
    d_pre = gelu_back(d_activated)[0].astype(jnp.bfloat16)
    grad_expand = weight_product(hidden_two_low, d_pre)
    grad_expand_offset = row_sum(d_pre)
    d_hidden_two = d_third + input_product(d_pre, expand_full)
    d_second, d_gain_two, d_shift_two = norm_two_back(d_hidden_two)
    d_branch_c = d_second.astype(jnp.bfloat16)
    grad_cross_out = weight_product(o_cross_low, d_branch_c)
    grad_cross_out_offset = row_sum(d_branch_c)
    d_o_cross = input_product(d_branch_c, matrices[7]).astype(jnp.bfloat16)
    grad_cq, grad_ck, grad_cv = attend_backward(
        q_cross.reshape(token_heads),
        k_cross.reshape(state_heads),
        v_cross.reshape(state_heads),
        d_o_cross.reshape(token_heads),
        lse_cross,
        valid_states,
        False,
    )
    dq_cross = (grad_cq.reshape(slot_tokens, D) * 0.125).astype(jnp.bfloat16)
    dk_cross = grad_ck.reshape(slot_states, D).astype(jnp.bfloat16)
    dv_cross = grad_cv.reshape(slot_states, D).astype(jnp.bfloat16)
    grad_cross_query = weight_product(hidden_one_low, dq_cross)
    grad_cross_key = weight_product(states, dk_cross)
    grad_cross_value = weight_product(states, dv_cross)
    state_grad = input_product(dk_cross, matrices[5]) + input_product(
        dv_cross, matrices[6]
    )
    d_hidden_one = d_second + input_product(dq_cross, matrices[4])
    d_first, d_gain_one, d_shift_one = norm_one_back(d_hidden_one)
    d_branch_a = d_first.astype(jnp.bfloat16)
    grad_self_out = weight_product(o_self_low, d_branch_a)
    grad_self_out_offset = row_sum(d_branch_a)
    d_o_self = input_product(d_branch_a, matrices[3]).astype(jnp.bfloat16)
    grad_sq, grad_sk, grad_sv = attend_backward(
        q_self.reshape(token_heads),
        k_self.reshape(token_heads),
        v_self.reshape(token_heads),
        d_o_self.reshape(token_heads),
        lse_self,
        valid_tokens,
        True,
    )
    dq_self = (grad_sq.reshape(slot_tokens, D) * 0.125).astype(jnp.bfloat16)
    dk_self = grad_sk.reshape(slot_tokens, D).astype(jnp.bfloat16)
    dv_self = grad_sv.reshape(slot_tokens, D).astype(jnp.bfloat16)
    grad_self_query = weight_product(tokens, dq_self)
    grad_self_key = weight_product(tokens, dk_self)
    grad_self_value = weight_product(tokens, dv_self)
    token_grad = (
        d_first
        + input_product(dq_self, matrices[0])
        + input_product(dk_self, matrices[1])
        + input_product(dv_self, matrices[2])
    )
    small_partial = jnp.concatenate(
        [
            row_sum(dq_self),
            row_sum(dv_self),
            grad_self_out_offset,
            row_sum(dq_cross),
            row_sum(dv_cross),
            grad_cross_out_offset,
            grad_expand_offset,
            grad_shrink_offset,
            d_gain_one,
            d_shift_one,
            d_gain_two,
            d_shift_two,
            d_gain_three,
            d_shift_three,
        ]
    )
    totals = lax.psum(jnp.concatenate([small_partial, squares]), ("rep", "shard"))
    g_shrink = scatter_rows(grad_shrink)
    g_expand = scatter_rows(grad_expand)
    g_rest = scatter_rows(
        jnp.concatenate(
            [grad_self_out, grad_cross_query, grad_cross_key, grad_cross_value, grad_cross_out],
            axis=1,
        )
    )
    g_qkv = scatter_rows(
        jnp.concatenate([grad_self_query, grad_self_key, grad_self_value], axis=1)
    )
    g_attention = (
        jnp.concatenate([g_qkv, g_rest], axis=1).reshape(-1, 8, D).astype(jnp.float32)
    )
    g_expand = g_expand.astype(jnp.float32)
    g_shrink = g_shrink.astype(jnp.float32)
    attention_rows_new, *attention_parts = local_factors(g_attention, attention_rows.T)
    expand_rows_new, *expand_parts = local_factors(g_expand, expand_rows)
    shrink_rows_new, *shrink_parts = local_factors(g_shrink, shrink_rows)
    flat = attention_parts + expand_parts + shrink_parts
    summed = lax.psum(jnp.concatenate([t.reshape(-1) for t in flat]), "shard")
    sums = []
    offset = 0
    for t in flat:
        sums.append(summed[offset : offset + t.size].reshape(t.shape))
        offset = offset + t.size
    attention_rates = STEP_RATE * jnp.where(jnp.arange(8) % 4 == 3, OUT_GAIN, 1.0).astype(
        jnp.float32
    )
    attention_new, attention_cols_new = finish_factors(
        g_attention,
        attention_weights,
        attention_rows_new,
        attention_cols,
        *sums[0:3],
        D,
        attention_rates,
    )
    expand_new, expand_cols_new = finish_factors(
        g_expand, expand_weight, expand_rows_new, expand_cols, *sums[3:6], D, STEP_RATE
    )
    shrink_new, shrink_cols_new = finish_factors(
        g_shrink, shrink_weight, shrink_rows_new, shrink_cols, *sums[6:9], FF, STEP_RATE
    )
    small_grad = totals[: small_params.shape[0]]
    small_moment_new = DECAY_RATE * small_moment + (1.0 - DECAY_RATE) * (
        small_grad * small_grad + FACTOR_EPS
    )
    small_update = small_grad * lax.rsqrt(small_moment_new)
    small_scale = jnp.sqrt(jnp.mean(small_update * small_update))
    small_new = small_params - SMALL_RATE * small_update / jnp.maximum(
        1.0, small_scale / CLIP_LEVEL
    )
    norm_stats = jnp.sqrt(
        totals[small_params.shape[0] :] / (jnp.sum(lengths).astype(jnp.float32) * D)
    )
    return (
        result.astype(jnp.bfloat16),
        token_grad.astype(jnp.bfloat16),
        state_grad.astype(jnp.bfloat16),
        g_attention,
        g_expand,
        g_shrink,
        small_grad,
        attention_new,
        expand_new,
        shrink_new,
        small_new,
        attention_new.astype(jnp.bfloat16),
        expand_new.astype(jnp.bfloat16),
        shrink_new.astype(jnp.bfloat16),
        attention_rows_new.T,
        attention_cols_new,
        expand_rows_new,
        expand_cols_new,
        shrink_rows_new,
        shrink_cols_new,
        small_moment_new,
        norm_stats,
    )


def direct_device(
    tokens,
    encoder,
    cotangent,
    lengths,
    encoder_lengths,
    dealt_order,
    attention_weights,
    expand_weight,
    shrink_weight,
    small_params,
    attention_rows,
    attention_cols,
    expand_rows,
    expand_cols,
    shrink_rows,
    shrink_cols,
    small_moment,
):
    inverse = jnp.zeros((32,), jnp.int32).at[dealt_order].set(jnp.arange(32, dtype=jnp.int32))
    params = small_params.reshape(17, D)
    weights = (attention_weights.reshape(2048, D), expand_weight, shrink_weight)
    (
        tokens,
        full,
        q_self,
        k_self,
        v_self,
        o_self,
        lse_self,
        q_cross,
        k_cross,
        v_cross,
        o_cross,
        lse_cross,
        summed_one,
        summed_two,
        hidden_one,
        hidden_two,
        activated,
        slope,
        output,
        d_mlp,
        d_third,
        small_first,
    ) = forward(
        (inverse, lengths, encoder_lengths), tokens, weights, encoder, cotangent, params
    )
    factor_rows = jnp.concatenate(
        [attention_rows, expand_rows.reshape(1, 256), shrink_rows.reshape(4, 256)]
    )
    factor_rows = jnp.pad(factor_rows.T, ((0, 0), (0, 115)))
    factor_cols = jnp.concatenate(
        [attention_cols, hidden_blocks(expand_cols), shrink_cols.reshape(1, D), jnp.ones((3, D))]
    )
    token_grad, state_grad, reduced, totals, factor_rows, factor_cols, scale = backward(
        (lengths, encoder_lengths),
        (
            d_mlp,
            d_third,
            activated,
            slope,
            full.reshape(GATHERED, 1024, D),
            hidden_two,
            hidden_one,
            tokens.reshape(1024, D),
            encoder,
            o_cross,
            o_self,
            summed_one,
            summed_two,
            q_self,
            k_self,
            v_self,
            q_cross,
            k_cross,
            v_cross,
            lse_self,
            lse_cross,
        ),
        params,
        small_first,
        factor_rows,
        factor_cols,
    )
    attention, expand, shrink, rows_new = update_direct(
        reduced, factor_rows, scale, attention_weights, expand_weight, shrink_weight
    )
    cols_new = (factor_cols[0:8], hidden_flat(factor_cols[8:12]), factor_cols[12])
    small_grad = totals[0:17].reshape(-1)
    small_moment_new = DECAY_RATE * small_moment + (1.0 - DECAY_RATE) * (
        small_grad * small_grad + FACTOR_EPS
    )
    small_update = small_grad * lax.rsqrt(small_moment_new)
    small_scale = jnp.sqrt(jnp.mean(small_update * small_update))
    small_new = small_params - SMALL_RATE * small_update / jnp.maximum(
        1.0, small_scale / CLIP_LEVEL
    )
    norm_stats = jnp.sqrt(totals[17, 0:6] / (jnp.sum(lengths).astype(jnp.float32) * D))
    return (
        output,
        token_grad,
        state_grad,
        attention[0],
        expand[0],
        shrink[0],
        small_grad,
        attention[1],
        expand[1],
        shrink[1],
        small_new,
        attention[2],
        expand[2],
        shrink[2],
        rows_new[0],
        cols_new[0],
        rows_new[1],
        cols_new[1],
        rows_new[2],
        cols_new[2],
        small_moment_new,
        norm_stats,
    )


def on_device(*args):
    if lax.axis_size("rep") == 8 and lax.axis_size("shard") == 4:
        return direct_device(*args)
    return plain_device(*args)


def solution(mesh):
    in_specs = (
        P(("rep", "shard"), None),
        P(("rep", "shard"), None),
        P(("rep", "shard"), None),
        P(),
        P(),
        P(),
        P("shard", None, None),
        P("shard", None),
        P("shard", None),
        P(),
        P(None, "shard"),
        P(),
        P("shard"),
        P(),
        P("shard"),
        P(),
        P(),
    )
    out_specs = (
        P(("rep", "shard"), None),
        P(("rep", "shard"), None),
        P(("rep", "shard"), None),
        P("shard", None, None),
        P("shard", None),
        P("shard", None),
        P(),
        P("shard", None, None),
        P("shard", None),
        P("shard", None),
        P(),
        P("shard", None, None),
        P("shard", None),
        P("shard", None),
        P(None, "shard"),
        P(),
        P("shard"),
        P(),
        P("shard"),
        P(),
        P(),
        P(),
    )
    return jax.shard_map(
        on_device, mesh=mesh, in_specs=in_specs, out_specs=out_specs, check_vma=False
    )
```

```python
import math

import jax
import jax.numpy as jnp
from jax import lax
from jax.experimental import pallas as pl
from jax.experimental.pallas import tpu as pltpu
from jax.sharding import PartitionSpec as P

D = 1024
HEADS = 16
HEAD_DIM = 64
FF = 4096


DECAY_RATE = 0.5
CLIP_LEVEL = 0.25
STEP_RATE = 0.1
SMALL_RATE = 0.4
OUT_GAIN = 8.0
NORM_EPS = 1e-05
FACTOR_EPS = 1e-30
MASKED = -1e30
MESH = pl.DeviceIdType.MESH
CHUNKS = 16
GATHERED = 16
EXPAND_AT = (8, 9, 11, 13)
SHRINK_AT = (10, 12, 14, 15)
MIB = 1 << 20


def layer_norm(r, norm_gain, norm_shift):
    centred = r - jnp.mean(r, axis=-1, keepdims=True)
    spread = jnp.mean(centred * centred, axis=-1, keepdims=True)
    return centred * lax.rsqrt(spread + NORM_EPS) * norm_gain + norm_shift


def gelu_exact(values):
    return jax.nn.gelu(values, approximate=False)


def unpack(small):
    extents = [D] * 6 + [FF] + [D] * 7
    pieces = []
    offset = 0
    for extent in extents:
        pieces.append(small[offset : offset + extent])
        offset = offset + extent
    return pieces


def forward_product(source, matrix):
    return jnp.dot(source, matrix, preferred_element_type=jnp.float32)


def input_product(grad_low, matrix):
    return jnp.einsum("to,io->ti", grad_low, matrix, preferred_element_type=jnp.float32)


def weight_product(source, grad_low):
    return jnp.einsum("ti,to->io", source, grad_low, preferred_element_type=jnp.float32)


def row_sum(grad_low):
    return jnp.sum(grad_low.astype(jnp.float32), axis=0)


def transposed(block):
    return block.astype(jnp.float32).T.astype(jnp.bfloat16)


def half_lanes(shape, dim):
    return lax.broadcasted_iota(jnp.int32, shape, dim)


def masked_keys(keys, length, head):
    place = half_lanes(keys.shape, 0)
    lane = half_lanes(keys.shape, 1)
    blocked = jnp.where((lane == 64 - 64 * head) & (place >= length), MASKED, 0.0)
    own = (lane >= 64 * head) & (lane < 64 * head + 64)
    return jnp.where(own, keys.astype(jnp.float32), blocked).astype(jnp.bfloat16)


def own_head(rows_t, head, fill):
    place = half_lanes(rows_t.shape, 0)
    own = (place >= 64 * head) & (place < 64 * head + 64)
    other = jnp.where(place == 64 - 64 * head, fill, 0.0)
    return jnp.where(own, rows_t.astype(jnp.float32), other).astype(jnp.bfloat16)


def product(first, second):
    return jnp.dot(first, second, preferred_element_type=jnp.float32)


def causal_mask(scores, step):
    kept = scores.shape[0] - step
    last = scores[kept:]
    allowed = half_lanes(last.shape, 0) <= half_lanes(last.shape, 1)
    last = jnp.where(allowed, last, MASKED)
    return last if kept == 0 else jnp.concatenate([scores[:kept], last], axis=0)


def attend_pair(
    causal, step, length, q_ref, k_ref, v_ref, o_ref, lse_ref, o_t, first_row=0
):
    count = q_ref.shape[0]
    q_t = transposed(q_ref[...])
    v_t = transposed(v_ref[...])
    keys = [masked_keys(k_ref[...], length, head) for head in range(2)]
    queries = [own_head(q_t, head, 1.0) for head in range(2)]
    units = [(head, start) for start in range(0, count, step) for head in range(2)]

    def scores_of(head, start):
        end = first_row + start + step if causal else k_ref.shape[0]
        return product(keys[head][:end], queries[head][:, start : start + step])

    ahead = scores_of(*units[0])
    for index, (head, start) in enumerate(units):
        scores = ahead
        if index + 1 < len(units):
            ahead = scores_of(*units[index + 1])
        rows = slice(64 * head, 64 * head + 64)
        columns = slice(start, start + step)
        if causal:
            scores = causal_mask(scores, step)
        top = jnp.max(scores, axis=0, keepdims=True)
        raised = jnp.exp(scores - top)
        total = jnp.sum(raised, axis=0, keepdims=True)
        probs = (raised * (1.0 / total)).astype(jnp.bfloat16)
        o_t[rows, columns] = product(v_t[rows, : scores.shape[0]], probs)
        place = slice(first_row + start, first_row + start + step)
        lse_ref[0, head : head + 1, place] = top + jnp.log(total)
    o_ref[...] = o_t[:, :count].T.astype(jnp.bfloat16)


def attend_back_pair(
    causal,
    step,
    length,
    q_ref,
    k_ref,
    v_ref,
    do_ref,
    lse_ref,
    dq_ref,
    dk_ref,
    dv_ref,
    put_sums,
    dq_t,
    dk_sum,
    dv_sum,
):
    key_rows = k_ref.shape[0]
    q_t = transposed(q_ref[...])
    k_t = transposed(k_ref[...])
    do_t = transposed(do_ref[...])
    values = v_ref[...]
    keys = [masked_keys(k_ref[...], length, head) for head in range(2)]
    queries = [own_head(q_t, head, 1.0) for head in range(2)]
    grads = [own_head(do_t, head, 0.0) for head in range(2)]
    count = q_ref.shape[0] // step
    units = [(head, b) for b in reversed(range(count)) for head in range(2)]

    def products_of(head, b):
        columns = slice(b * step, b * step + step)
        end = b * step + step if causal else key_rows
        scores = product(keys[head][:end], queries[head][:, columns])
        return scores, product(values[:end], grads[head][:, columns])

    ahead = products_of(*units[0])
    for index, (head, b) in enumerate(units):
        scores, d_probs = ahead
        if index + 1 < len(units):
            ahead = products_of(*units[index + 1])
        rows = slice(64 * head, 64 * head + 64)
        columns = slice(b * step, b * step + step)
        end = scores.shape[0]
        if causal:
            scores = causal_mask(scores, step)
        probs = jnp.exp(scores - lse_ref[0, head : head + 1, columns])
        weighted = probs * d_probs
        delta = jnp.sum(weighted, axis=0, keepdims=True)
        d_scores = (weighted - probs * delta).astype(jnp.bfloat16)
        dv = product(probs.astype(jnp.bfloat16), do_ref[columns, :])
        dk = product(d_scores, q_ref[columns, :])
        if b == count - 1:
            dv_sum[head, :end] = dv
            dk_sum[head, :end] = dk
        else:
            dv_sum[head, :end] += dv
            dk_sum[head, :end] += dk
        dq_t[rows, columns] = product(k_t[rows, :end], d_scores)
    first = half_lanes((key_rows, 128), 1) < 64
    dk_ref[...] = jnp.where(first, dk_sum[0, :key_rows], dk_sum[1, :key_rows]).astype(jnp.bfloat16)
    dv = jnp.where(first, dv_sum[0, :key_rows], dv_sum[1, :key_rows]).astype(jnp.bfloat16)
    dv_ref[...] = dv
    dq = (dq_t[...] * 0.125).T.astype(jnp.bfloat16)
    dq_ref[...] = dq
    put_sums(
        jnp.sum(dq.astype(jnp.float32), axis=0, keepdims=True),
        jnp.sum(dv.astype(jnp.float32), axis=0, keepdims=True),
    )


SCALARS = pl.BlockSpec(memory_space=pltpu.SMEM)


def neighbours():
    rep = lax.axis_index("rep")
    z = lax.axis_index("shard")
    core = rep % 2
    x = (rep // 2) % 2
    y = rep // 4
    other_core = (rep + 1 - 2 * core, z)
    other_x = (rep + 2 - 4 * x, z)
    other_y = (rep + 4 - 8 * y, z)
    others_z = [(rep, (z + d) % 4) for d in (1, 2, 3)]
    return core, x, y, z, other_core, other_x, other_y, others_z


def greet(devices):
    barrier = pltpu.get_barrier_semaphore()
    for device in devices:
        pl.semaphore_signal(barrier, inc=1, device_id=device, device_id_type=MESH)
    pl.semaphore_wait(barrier, len(devices))


def remote(src, dst, send, recv, device):
    return pltpu.make_async_remote_copy(
        src_ref=src, dst_ref=dst, send_sem=send, recv_sem=recv, device_id=device, device_id_type=MESH
    )


def gather_copies(refs, c, parity, places):
    piece, full, place_sem, z_send, z_recv, send, recv = refs
    core, x, y, z, other_core, other_x, other_y, others_z = places
    a = x + parity * (y - x)
    b = y + parity * (x - y)
    first = (other_x[0] + parity * (other_y[0] - other_x[0]), z)
    second = (other_y[0] + parity * (other_x[0] - other_y[0]), z)
    own = pl.ds(pl.multiple_of(core * 128 + a * 64 + b * 32, 32), 32)
    steps = (
        (own, second),
        (pl.ds(pl.multiple_of(core * 128 + a * 64, 64), 64), first),
        (pl.ds(pl.multiple_of(core * 128, 128), 128), other_core),
    )

    def local():
        return pltpu.make_async_copy(piece.at[c], full.at[c, z, own, :], place_sem.at[c])

    def line(d):
        return remote(
            piece.at[c], full.at[c, z, own, :], z_send.at[c, d], z_recv.at[c, d], others_z[d]
        )

    def pair(k):
        block = full.at[c, :, steps[k][0], :]
        return remote(block, block, send.at[k, c], recv.at[k, c], steps[k][1])

    return local, line, pair


def gather_stage(k, refs, c, parity, places):
    local, line, pair = gather_copies(refs, c, parity, places)
    if k == 0:
        local().start()
        for d in range(3):
            line(d).start()
    if k == 1:
        local().wait()
        for d in range(3):
            line(d).wait_recv()
        pair(0).start()
    if k == 2 or k == 3:
        pair(k - 2).wait_recv()
        pair(k - 1).start()
    if k == 4:
        pair(2).wait()
        pair(1).wait_send()
        pair(0).wait_send()
        for d in range(3):
            line(d).wait_send()


def gather_sems(count):
    dma = pltpu.SemaphoreType.DMA
    return [dma((count,)), dma((count, 3)), dma((count, 3)), dma((3, count)), dma((3, count))]


def hidden_blocks(values):
    split = values.reshape(values.shape[:-1] + (4, 4, 256))
    split = jnp.swapaxes(split, -3, -2)
    return split.reshape(values.shape[:-1] + (4, 1024))


def hidden_flat(blocks):
    split = blocks.reshape(blocks.shape[:-2] + (4, 4, 256))
    split = jnp.swapaxes(split, -3, -2)
    return split.reshape(blocks.shape[:-2] + (FF,))


def fold(tile):
    return jnp.sum(tile.reshape(-1, 8, tile.shape[-1]), axis=0)


GATHER_PLAN = (("z", 7.5), ("second", 7.5), ("first", 13.0), ("core", 4.0), (None, 0.0))


class GatherPlanner:
    def __init__(self, count):
        self.now = 0.0
        self.links = {"core": 0.0, "x": 0.0, "y": 0.0, "z": 0.0}
        self.stage = {c: 0 for c in range(count)}
        self.ready = {c: 0.0 for c in range(count)}
        self.opened = count

    def can(self, c):
        if self.stage[c] == 0 and c >= 3 and self.stage[c - 3] < 2:
            return False
        return self.stage[c] < 5

    def spend(self, now, **busy):
        self.now = max(self.now, now)
        for link, span in busy.items():
            self.links[link] = max(self.links[link], self.now) + span

    def emit(self, c):
        stage = self.stage[c]
        link, span = GATHER_PLAN[stage]
        first, second = ("x", "y") if c % 2 == 0 else ("y", "x")
        link = {"first": first, "second": second}.get(link, link)
        self.now = max(self.now, self.ready[c]) + 0.1
        if link is not None:
            begin = max(self.now, self.links[link])
            self.links[link] = begin + span - 1.0
            self.ready[c] = begin + span
        self.stage[c] = stage + 1
        return (stage, c)

    def tick(self, spent):
        self.now += spent
        events = []
        progress = True
        while progress:
            progress = False
            for c in range(self.opened):
                if self.can(c) and self.ready[c] <= self.now:
                    events.append(self.emit(c))
                    progress = True
        return events

    def until(self, c):
        events = []
        while self.stage[c] < 5:
            choices = [i for i in range(self.opened) if self.can(i)]
            best = min(choices, key=lambda i: (self.ready[i], i))
            events.append(self.emit(best))
        return events


ERFC_SERIES = (
    0.08459648489952087,
    0.085321806371212,
    0.0743890032172203,
    0.10671534389257431,
    -0.04577348381280899,
    0.27184805274009705,
    -0.2545455992221832,
    0.24207571148872375,
    -0.06462734192609787,
)


def gelu_parts(u):
    bell = jnp.exp(-0.5 * u * u)
    t = 1.0 / (1.0 + (0.3 * math.sqrt(0.5)) * jnp.abs(u))
    series = ERFC_SERIES[8]
    for coefficient in ERFC_SERIES[7::-1]:
        series = series * t + coefficient
    tail = series * t * bell
    share = jnp.where(u < 0.0, tail, 1.0 - tail)
    return u * share, share + u * (bell * (1.0 / math.sqrt(2.0 * math.pi)))


def norm_parts(values):
    centred = values - jnp.mean(values, axis=1, keepdims=True)
    spread = jnp.mean(centred * centred, axis=1, keepdims=True)
    scale = lax.rsqrt(spread + NORM_EPS)
    return centred * scale, scale


def forward_kernel(
    order_ref,
    lengths_ref,
    state_lengths_ref,
    tokens_ref,
    att_ref,
    exp_ref,
    shr_ref,
    e_ref,
    cot_ref,
    par,
    x_out,
    full_ref,
    q_out,
    k_out,
    v_out,
    o_out,
    lse_out,
    cq_out,
    ck_out,
    cv_out,
    oc_out,
    lse_cross_out,
    r1_out,
    r2_out,
    h1_out,
    h2_out,
    g_out,
    gp_out,
    y_out,
    dm_out,
    d_third_out,
    small_out,
    pool,
    acc,
    held,
    o_t,
    lse_held,
    states,
    x_held,
    spread,
    picked,
    piece_ref,
    att_in,
    exp_in,
    shr_in,
    prepare_sem,
    load_sem,
    store_sem,
    state_sem,
    acc_sem,
    spread_send,
    spread_recv,
    back_send,
    back_recv,
    *gather_sem,
):
    places = neighbours()
    refs = (piece_ref, full_ref) + gather_sem
    planner = GatherPlanner(GATHERED)
    me = lax.axis_index("rep") * 4 + places[3]
    length = lengths_ref[me]

    core, x, y = places[0:3]

    def own_row(parity):
        a = x + parity * (y - x)
        b = y + parity * (x - y)
        return core * 128 + a * 64 + b * 32

    prepare = []
    for p in range(2):
        for lane in range(8):
            rows = pl.ds(pl.multiple_of(own_row(p) * 8, 256), 256)
            prepare.append((att_ref.at[rows, pl.ds(lane * 128, 128)], att_in.at[p, lane]))
        rows = pl.ds(pl.multiple_of(own_row(p), 32), 32)
        prepare.append((exp_ref.at[rows, :], exp_in.at[p]))
    for j in range(4):
        rows = pl.ds(pl.multiple_of(j * 256 + own_row(SHRINK_AT[j] % 2), 32), 32)
        prepare.append((shr_ref.at[rows, :], shr_in.at[j]))
    prepare = [
        pltpu.make_async_copy(source, target, prepare_sem.at[i])
        for i, (source, target) in enumerate(prepare)
    ]

    def make_pieces():
        for copy in prepare:
            copy.wait()
        for c in range(8):
            for lane in range(8):
                tile = att_in[c % 2, lane, pl.ds(c, 32, stride=8), :]
                piece_ref[c, :, lane * 128 : lane * 128 + 128] = tile.astype(jnp.bfloat16)
        for j in range(4):
            c = EXPAND_AT[j]
            for s in range(4):
                start = s * 1024 + j * 256
                tile = exp_in[c % 2, :, start : start + 256]
                piece_ref[c, :, s * 256 : s * 256 + 256] = tile.astype(jnp.bfloat16)
            piece_ref[SHRINK_AT[j]] = shr_in[j].astype(jnp.bfloat16)

    def device(offset):
        j = lax.rem(me + offset, 32)
        return j, (j // 4, j % 4)

    def spread_copy(offset):
        j, target = device(offset)
        return remote(
            tokens_ref.at[j],
            spread.at[me],
            spread_send.at[offset],
            spread_recv.at[offset],
            target,
        )

    def back_copy(offset):
        return remote(
            picked.at[offset],
            x_held.at[me],
            back_send.at[offset],
            back_recv.at[offset],
            device(offset)[1],
        )

    def own_spread():
        return pltpu.make_async_copy(tokens_ref.at[me], spread.at[me], spread_recv.at[0])

    def own_back():
        return pltpu.make_async_copy(picked.at[0], x_held.at[me], back_recv.at[0])

    def each_other(act):
        def body(offset, carry):
            act(offset)
            return carry

        lax.fori_loop(1, 32, body, 0)

    def turn_back():
        own_spread().wait()
        each_other(lambda offset: spread_copy(offset).wait())
        picked[0] = spread[order_ref[me]]
        own_back().start()

        def pick(offset):
            picked[offset] = spread[order_ref[device(offset)[0]]]
            back_copy(offset).start()

        each_other(pick)

    def emit_all(events):
        for stage, c in events:
            gather_stage(stage, refs, c, c % 2, places)

    def tick(spent):
        emit_all(planner.tick(spent))

    def load(slot, source):
        return pltpu.make_async_copy(source, pool.at[slot], load_sem.at[slot])

    def store(slot, target):
        return pltpu.make_async_copy(pool.at[slot], target, store_sem.at[slot])

    def product_into(left, right, put):
        def body(i, carry):
            n = pl.multiple_of(i * 256, 256)
            put(n, product(left(), pool[right, :, pl.ds(n, 256)]))
            return carry

        lax.fori_loop(0, 4, body, 0)

    def row(index, n):
        return par[index : index + 1, pl.ds(n, 256)]

    def put_low(slot, offset=None, scale=None):
        def put(n, value):
            if offset is not None:
                value = value + row(offset, n)
            if scale is not None:
                value = value * scale
            pool[slot, :, pl.ds(n, 256)] = value.astype(jnp.bfloat16)

        return put

    def put_acc(offset):
        def put(n, value):
            acc[:, pl.ds(n, 256)] = value + row(offset, n)

        return put

    def load_weight(c, slot):
        target = pool.at[slot].reshape(4, 256, D)
        return pltpu.make_async_copy(full_ref.at[c], target, load_sem.at[slot])

    def weight(c, slot):
        emit_all(planner.until(c))
        return load_weight(c, slot)

    def attend_loop(causal, step, valid, query, key, value, out, spent, rows, key_rows):
        ahead = [planner.tick(spent) for _ in range(8)]
        first_row, count = rows

        def body(i, carry):
            lanes = pl.ds(pl.multiple_of(i * 128, 128), 128)
            attend_pair(
                causal,
                step,
                valid,
                query.at[pl.ds(first_row, count), lanes],
                key.at[pl.ds(0, key_rows), lanes],
                value.at[pl.ds(0, key_rows), lanes],
                out.at[pl.ds(first_row, count), lanes],
                lse_held.at[pl.ds(i, 1)],
                o_t,
                first_row,
            )
            for n in range(8):
                if ahead[n]:

                    @pl.when(i == n)
                    def _(events=ahead[n]):
                        emit_all(events)

            return carry

        lax.fori_loop(0, 8, body, 0)

    TILE = 128

    def over_rows(sums, body):
        zero = jnp.zeros((8, D), jnp.float32)

        def step(i, carry):
            r = pl.multiple_of(i * TILE, TILE)
            place = half_lanes((TILE, 1), 0) + r
            usable = (place < length).astype(jnp.float32)
            terms = body(pl.ds(r, TILE), usable)
            return tuple(c + fold(t) for c, t in zip(carry, terms))

        totals = lax.fori_loop(0, D // TILE, step, (zero,) * sums)
        return [jnp.sum(t, axis=0, keepdims=True) for t in totals]

    lane = half_lanes((1, D), 1)

    def square_at(index, total):
        small_out[17:18, :] += jnp.where(lane == index, jnp.sum(total), 0.0)

    for copy in prepare:
        copy.start()
    barrier = pltpu.get_barrier_semaphore()

    def greet_one(offset):
        pl.semaphore_signal(barrier, inc=1, device_id=device(offset)[1], device_id_type=MESH)

    each_other(greet_one)
    pl.semaphore_wait(barrier, 31)
    own_spread().start()
    each_other(lambda offset: spread_copy(offset).start())
    make_pieces()
    planner.opened = 3
    tick(0.5)
    planner.spend(3.0, z=42.0, x=21.0, y=21.0)
    e_load = pltpu.make_async_copy(e_ref, states.at[2], state_sem.at[2])
    e_load.start()
    load(9, cot_ref).start()
    small_out[...] = jnp.zeros_like(small_out)
    turn_back()
    planner.spend(56.0, z=42.0, x=21.0, y=21.0)
    planner.opened = 5
    for i in range(3):
        weight(i, 1 + i).start()
    own_back().wait()
    each_other(lambda offset: back_copy(offset).wait())
    planner.spend(112.0)
    planner.opened = GATHERED
    tick(0.5)
    x_store = pltpu.make_async_copy(x_held, x_out, acc_sem.at[1])
    x_store.start()

    for i, (slot, offset, scale) in enumerate(((4, 0, 0.125), (5, None, None), (6, 1, None))):
        load_weight(i, 1 + i).wait()
        product_into(lambda: x_held[...].reshape(1024, D), 1 + i, put_low(slot, offset, scale))
        store(slot, (q_out, k_out, v_out)[i]).start()
        tick(2.5)
    refs_held = [pool.at[slot] for slot in (4, 5, 6, 7)]
    attend_loop(True, 256, length, *refs_held, 4.5, (0, 1024), 1024)
    store(7, o_out).start()
    lse_copy = pltpu.make_async_copy(lse_held, lse_out, state_sem.at[3])
    lse_copy.start()
    w_copy = weight(3, 1)
    w_copy.start()
    w_copy.wait()
    product_into(lambda: pool[7], 1, put_acc(2))
    tick(2.5)
    store(4, q_out).wait()

    def first_norm(rows, usable):
        held_rows = pl.ds(pl.multiple_of(rows.start // 32, TILE // 32), TILE // 32)
        x = x_held[held_rows].reshape(TILE, D).astype(jnp.float32)
        a = acc[rows, :]
        total = x + a
        acc[rows, :] = total
        h = norm_parts(total)[0] * par[11:12, :] + par[12:13, :]
        held[rows, :] = h
        pool[4, rows, :] = h.astype(jnp.bfloat16)
        return usable * x * x, usable * a * a, usable * h * h

    for index, total in enumerate(over_rows(3, first_norm)):
        square_at(index, total)
    store(4, h1_out).start()
    r1_copy = pltpu.make_async_copy(acc, r1_out, acc_sem.at[0])
    r1_copy.start()
    tick(4.0)

    for c, slot in ((4, 2), (5, 3), (6, 1)):
        weight(c, slot).start()
    store(5, k_out).wait()
    load_weight(4, 2).wait()
    product_into(lambda: pool[4], 2, put_low(5, 3, 0.125))
    store(5, cq_out).start()
    w_copy = weight(7, 2)
    w_copy.start()
    tick(2.5)
    e_load.wait()
    load_weight(5, 3).wait()
    load_weight(6, 1).wait()

    def put_keys(n, value):
        states[0, :, pl.ds(n, 256)] = value.astype(jnp.bfloat16)

    def put_values(n, value):
        states[1, :, pl.ds(n, 256)] = (value + row(4, n)).astype(jnp.bfloat16)

    product_into(lambda: states[2], 3, put_keys)
    product_into(lambda: states[2], 1, put_values)
    state_stores = [
        pltpu.make_async_copy(states.at[0], ck_out, state_sem.at[0]),
        pltpu.make_async_copy(states.at[1], cv_out, state_sem.at[1]),
    ]
    for copy in state_stores:
        copy.start()
    tick(1.0)
    store(6, v_out).wait()
    lse_copy.wait()
    attend_loop(
        False,
        512,
        state_lengths_ref[me],
        pool.at[5],
        states.at[0],
        states.at[1],
        pool.at[6],
        1.6,
        (0, 1024),
        128,
    )
    store(6, oc_out).start()
    lse_copy = pltpu.make_async_copy(lse_held, lse_cross_out, state_sem.at[3])
    lse_copy.start()
    w_copy.wait()
    r1_copy.wait()
    product_into(lambda: pool[6], 2, put_acc(5))
    tick(2.5)
    weight(EXPAND_AT[0], 0).start()
    store(7, o_out).wait()

    def second_norm(rows, usable):
        c = acc[rows, :]
        total = held[rows, :] + c
        acc[rows, :] = total
        h = norm_parts(total)[0] * par[13:14, :] + par[14:15, :]
        held[rows, :] = h
        pool[7, rows, :] = h.astype(jnp.bfloat16)
        return usable * c * c, usable * h * h

    for index, total in enumerate(over_rows(2, second_norm)):
        square_at(3 + index, total)
    store(7, h2_out).start()
    r2_copy = pltpu.make_async_copy(acc, r2_out, acc_sem.at[0])
    r2_copy.start()
    tick(4.0)

    store(4, h1_out).wait()
    store(5, cq_out).wait()
    g_slots, slope_slots = (4, 6), (5, 8)
    r2_copy.wait()
    store(6, oc_out).wait()
    for j in range(5):
        if j > 1:
            store(g_slots[j % 2], g_out.at[j - 2]).wait()
            store(slope_slots[j % 2], gp_out.at[j - 2]).wait()
        if j < 4:
            load_weight(EXPAND_AT[j], j % 2).wait()
        if j > 0:
            load_weight(SHRINK_AT[j - 1], 2 + (j - 1) % 2).wait()

        def body(i, carry, j=j):
            n = pl.multiple_of(i * 256, 256)
            here = pl.ds(n, 256)
            if j < 4:
                offset = par[pl.ds(6 + i, 1), j * 256 : j * 256 + 256]
                u = product(pool[7], pool[j % 2, :, here]) + offset
            if j > 0:
                more = product(pool[g_slots[(j - 1) % 2]], pool[2 + (j - 1) % 2, :, here])
                if j == 1:
                    acc[:, here] = more + row(10, n)
                else:
                    acc[:, here] += more
            if j < 4:
                g, slope = gelu_parts(u)
                pool[g_slots[j % 2], :, here] = g.astype(jnp.bfloat16)
                pool[slope_slots[j % 2], :, here] = slope.astype(jnp.bfloat16)
            return carry

        ahead = [planner.tick(2.2 if j < 4 else 0.6) for _ in range(4)]

        def body_and_stages(i, carry, body=body, ahead=ahead):
            body(i, carry)
            for n in range(4):
                if ahead[n]:

                    @pl.when(i == n)
                    def _(events=ahead[n]):
                        emit_all(events)

            return carry

        lax.fori_loop(0, 4, body_and_stages, 0)
        if j < 4:
            store(g_slots[j % 2], g_out.at[j]).start()
            store(slope_slots[j % 2], gp_out.at[j]).start()
        if j < 3:
            weight(EXPAND_AT[j + 1], (j + 1) % 2).start()
        if j < 4:
            weight(SHRINK_AT[j], 2 + j % 2).start()

    load(9, cot_ref).wait()

    def third_norm(rows, usable):
        m = acc[rows, :]
        unit, scale = norm_parts(held[rows, :] + m)
        gain = par[15:16, :]
        pool[0, rows, :] = (unit * gain + par[16:17, :]).astype(jnp.bfloat16)
        grad = pool[9, rows, :].astype(jnp.float32) * usable
        inner = grad * gain
        first = jnp.mean(inner, axis=1, keepdims=True)
        second = jnp.mean(inner * unit, axis=1, keepdims=True)
        back = scale * (inner - first - unit * second)
        acc[rows, :] = back
        low = back.astype(jnp.bfloat16)
        pool[1, rows, :] = low
        return usable * m * m, grad * unit, grad, low.astype(jnp.float32)

    m_total, gain_sum, shift_sum, offset_sum = over_rows(4, third_norm)
    square_at(5, m_total)
    small_out[15:16, :] = gain_sum
    small_out[16:17, :] = shift_sum
    small_out[10:11, :] = offset_sum
    last = [
        store(0, y_out),
        store(1, dm_out),
        pltpu.make_async_copy(acc, d_third_out, acc_sem.at[0]),
    ]
    for copy in last:
        copy.start()
    for c in range(GATHERED):
        emit_all(planner.until(c))
    for copy in last + state_stores + [lse_copy, x_store]:
        copy.wait()
    store(7, h2_out).wait()
    store(6, g_out.at[3]).wait()
    store(8, gp_out.at[3]).wait()


def forward(scalars, tokens, weights, states, cotangent, params):
    any_space = pl.BlockSpec(memory_space=pl.ANY)
    vmem = pl.BlockSpec(memory_space=pltpu.VMEM)
    shape = jax.ShapeDtypeStruct
    dma = pltpu.SemaphoreType.DMA
    low = jnp.bfloat16
    wide = jnp.float32
    square = shape((1024, D), low)
    square_wide = shape((1024, D), wide)
    lse = shape((8, 8, 1024), wide)
    short = shape((128, D), low)
    blocks = shape((4, 1024, D), low)
    outs = (
        shape((32, 32, D), low),
        shape((GATHERED, 4, 256, D), low),
        square,
        square,
        square,
        square,
        lse,
        square,
        short,
        short,
        square,
        lse,
        square_wide,
        square_wide,
        square,
        square,
        blocks,
        blocks,
        square,
        square,
        square_wide,
        shape((24, D), wide),
    )
    return pl.pallas_call(
        forward_kernel,
        out_shape=outs,
        in_specs=[SCALARS] * 3 + [any_space] * 6 + [vmem],
        out_specs=(any_space,) * 21 + (vmem,),
        scratch_shapes=[
            pltpu.VMEM((10, 1024, D), low),
            pltpu.VMEM((1024, D), wide),
            pltpu.VMEM((1024, D), wide),
            pltpu.VMEM((128, 1024), wide),
            pltpu.VMEM((8, 8, 1024), wide),
            pltpu.VMEM((3, 128, D), low),
            pltpu.VMEM((32, 32, D), low),
            pltpu.VMEM((32, 32, D), low),
            pltpu.VMEM((32, 32, D), low),
            pltpu.VMEM((GATHERED, 32, D), low),
            pltpu.VMEM((2, 8, 256, 128), wide),
            pltpu.VMEM((2, 32, FF), wide),
            pltpu.VMEM((4, 32, D), wide),
            dma((22,)),
            dma((10,)),
            dma((10,)),
            dma((4,)),
            dma((2,)),
            dma((32,)),
            dma((32,)),
            dma((32,)),
            dma((32,)),
        ]
        + gather_sems(GATHERED),
        compiler_params=pltpu.CompilerParams(
            collective_id=3, has_side_effects=True, vmem_limit_bytes=62 * MIB
        ),
    )(*scalars, tokens.reshape(32, 32, D), *weights, states, cotangent, params)


def add_blocks(target, first, second, planes, rows, step):
    per_plane = rows // step

    def body(i, carry):
        s = i // per_plane
        r = pl.multiple_of((i % per_plane) * step, step)
        target(s, r, first(s, r) + second(s, r))
        return carry

    lax.fori_loop(0, planes * per_plane, body, 0)


POOL = 8
G_SLOTS = 3
R_SLOTS = 4
PLAN = {"core": 3.5, "load": 1.8, "a": 13.5, "b": 7.5, "z": 7.5, "bb": 3.0, "ba": 5.0, "bc": 2.5}


class Planner:
    def __init__(self):
        self.now = 0.0
        self.links = {"core": 0.0, "x": 0.0, "y": 0.0, "z": 0.0, "load": 0.0}
        self.stage = {}
        self.ready = {}

    def link_of(self, c, stage):
        first, second = ("x", "y") if c % 2 == 0 else ("y", "x")
        return {
            0: ("core", "core"),
            1: ("load", "load"),
            2: (first, "a"),
            3: (second, "b"),
            4: ("z", "z"),
            5: (second, "bb"),
            6: (first, "ba"),
            7: ("core", "bc"),
            8: (None, None),
        }[stage]

    def can(self, c):
        stage = self.stage[c]
        if stage > 8:
            return False
        if stage == 1 and c >= R_SLOTS and self.stage[c - R_SLOTS] <= 3:
            return False
        return True

    def emit(self, c):
        stage = self.stage[c]
        link, kind = self.link_of(c, stage)
        self.now = max(self.now, self.ready[c]) + {2: 0.8, 3: 0.5, 4: 0.3, 5: 0.2}.get(stage, 0.1)
        if link is not None:
            begin = max(self.now, self.links[link])
            span = PLAN[kind]
            self.links[link] = begin + span - 1.0
            self.ready[c] = begin + span
        self.stage[c] = stage + 1
        return (stage, c)

    def tick(self, spent):
        self.now += spent
        events = []
        progress = True
        while progress:
            progress = False
            for c in sorted(self.stage):
                if self.can(c) and self.ready[c] <= self.now:
                    events.append(self.emit(c))
                    progress = True
        return events

    def produce(self, c):
        self.stage[c] = 0
        self.ready[c] = self.now
        return [self.emit(c)]

    def until(self, done):
        events = []
        while not done():
            choices = [c for c in sorted(self.stage) if self.can(c)]
            c = min(choices, key=lambda i: (self.ready[i], i))
            events.append(self.emit(c))
        return events

    def free_slot(self, c):
        before = c - G_SLOTS
        if before < 0:
            return []
        return self.until(lambda: self.stage[before] > 2)

    def drain(self, tasks, spent):
        events = []
        waiting = list(tasks)
        while waiting or any(s <= 8 for s in self.stage.values()):
            choices = [c for c in sorted(self.stage) if self.can(c)]
            best = min(choices, key=lambda i: (self.ready[i], i)) if choices else None
            open_tasks = [t for t in waiting if all(self.stage[c] > 8 for c in t[0])]
            if open_tasks and (best is None or self.ready[best] > self.now):
                task = open_tasks[0]
                waiting.remove(task)
                self.now += spent
                events.append(("task", task[1]))
            else:
                events.append(self.emit(best))
        return events


def backward_kernel(
    lengths_ref,
    state_lengths_ref,
    dm_ref,
    d_third_ref,
    g_ref,
    gp_ref,
    full_ref,
    h2_ref,
    h1_ref,
    x_in_ref,
    e_ref,
    oc_ref,
    o_ref,
    r1_ref,
    r2_ref,
    q_ref,
    k_ref,
    v_ref,
    cq_ref,
    ck_ref,
    cv_ref,
    lse_ref,
    lse_cross_ref,
    gains_ref,
    small_ref,
    rows_ref,
    cols_ref,
    token_grad_ref,
    state_grad_ref,
    out_ref,
    totals_ref,
    rows_out,
    cols_out,
    scale_out,
    half,
    pool,
    acc,
    made,
    summed,
    quarter,
    eighth,
    pieces,
    stream,
    dq_t,
    dk_sum,
    dv_sum,
    lse_held,
    states,
    states_t,
    small,
    small_in,
    small_sum,
    small_z,
    part,
    whole,
    load_sem,
    stream_sem,
    state_sem,
    half_sem,
    scan_sem,
    line_send_sem,
    line_recv_sem,
    send_sem,
    recv_sem,
    z_send_sem,
    z_recv_sem,
    place_sem,
    small_send_sem,
    small_recv_sem,
):
    core, x, y, z, other_core, other_x, other_y, others_z = neighbours()
    me = lax.axis_index("rep") * 4 + z
    kept = pl.multiple_of(core * 128, 128)
    given = pl.multiple_of(128 - core * 128, 128)
    planner = Planner()
    place_of = (12, 8, 13, 9, 14, 10, 15, 11, 7, 4, 5, 6, 3, 0, 1, 2)

    def axes(c):
        if c % 2 == 0:
            return x, y, other_x, other_y
        return y, x, other_y, other_x

    def core_copy(c):
        source = made.at[c % G_SLOTS, :, pl.ds(given, 128), :]
        return remote(source, half.at[c], send_sem.at[0, c], recv_sem.at[0, c], other_core)

    def half_copy(c):
        return pltpu.make_async_copy(
            half.at[c], summed.at[c % R_SLOTS], half_sem.at[c % R_SLOTS]
        )

    def first_copy(c):
        a, b, first, second = axes(c)
        rows = pl.ds(pl.multiple_of(64 - a * 64, 64), 64)
        source = summed.at[c % R_SLOTS, :, rows, :]
        return remote(source, quarter.at[c], send_sem.at[1, c], recv_sem.at[1, c], first)

    def second_copy(c):
        a, b, first, second = axes(c)
        rows = pl.ds(pl.multiple_of(32 - b * 32, 32), 32)
        source = quarter.at[c, :, rows, :]
        return remote(source, eighth.at[c], send_sem.at[2, c], recv_sem.at[2, c], second)

    def z_copy(c, d):
        device = others_z[d]
        return remote(
            eighth.at[c, device[1]],
            pieces.at[c, d],
            z_send_sem.at[c, d],
            z_recv_sem.at[c, d],
            device,
        )

    def own_rows_of(c):
        a, b, first, second = axes(c)
        return pl.ds(pl.multiple_of(core * 128 + a * 64 + b * 32, 32), 32)

    def place_copy(c):
        return pltpu.make_async_copy(
            pieces.at[c, 0], out_ref.at[place_of[c], own_rows_of(c), :], place_sem.at[c]
        )

    def back_second(c):
        device = axes(c)[3]
        target = out_ref.at[place_of[c], own_rows_of(c), :]
        return remote(pieces.at[c, 0], target, send_sem.at[3, c], recv_sem.at[3, c], device)

    def back_first(c):
        a, b, first, second = axes(c)
        block = out_ref.at[place_of[c], pl.ds(pl.multiple_of(core * 128 + a * 64, 64), 64), :]
        return remote(block, block, send_sem.at[4, c], recv_sem.at[4, c], first)

    def back_core(c):
        block = out_ref.at[place_of[c], pl.ds(kept, 128), :]
        return remote(block, block, send_sem.at[5, c], recv_sem.at[5, c], other_core)

    def emit(stage, c):
        a, b, first, second = axes(c)
        slot = c % R_SLOTS
        if stage == 0:
            core_copy(c).start()
        if stage == 1:
            if c >= R_SLOTS:
                first_copy(c - R_SLOTS).wait_send()
            core_copy(c).wait_recv()
            half_copy(c).start()
        if stage == 2:
            half_copy(c).wait()

            def put(s, r, value):
                summed[slot, s, pl.ds(r, 32), :] = value

            add_blocks(
                put,
                lambda s, r: summed[slot, s, pl.ds(r, 32), :],
                lambda s, r: made[c % G_SLOTS, s, pl.ds(pl.multiple_of(kept + r, 32), 32), :],
                4,
                128,
                32,
            )
            first_copy(c).start()
            core_copy(c).wait_send()
        if stage == 3:
            first_copy(c).wait_recv()

            def put(s, r, value):
                quarter[c, s, pl.ds(r, 32), :] = value

            add_blocks(
                put,
                lambda s, r: quarter[c, s, pl.ds(r, 32), :],
                lambda s, r: summed[slot, s, pl.ds(pl.multiple_of(a * 64 + r, 32), 32), :],
                4,
                64,
                32,
            )
            second_copy(c).start()
        if stage == 4:
            second_copy(c).wait_recv()

            def put(s, r, value):
                eighth[c, s, pl.ds(r, 32), :] = value

            add_blocks(
                put,
                lambda s, r: eighth[c, s, pl.ds(r, 32), :],
                lambda s, r: quarter[c, s, pl.ds(pl.multiple_of(b * 32 + r, 32), 32), :],
                4,
                32,
                32,
            )
            for d in range(3):
                z_copy(c, d).start()
        if stage == 5:
            for d in range(3):
                z_copy(c, d).wait_recv()
            total = eighth[c, z].astype(jnp.float32)
            for d in range(3):
                total = total + pieces[c, d].astype(jnp.float32)
            pieces[c, 0] = total.astype(jnp.bfloat16)
            back_second(c).start()
            place_copy(c).start()
        if stage == 6:
            place_copy(c).wait()
            back_second(c).wait_recv()
            back_first(c).start()
        if stage == 7:
            back_first(c).wait_recv()
            back_core(c).start()
        if stage == 8:
            back_core(c).wait()
            back_first(c).wait_send()
            back_second(c).wait_send()
            for d in range(3):
                z_copy(c, d).wait_send()
            second_copy(c).wait_send()
            if c >= CHUNKS - R_SLOTS:
                first_copy(c).wait_send()

    def emit_all(events):
        for stage, c in events:
            emit(stage, c)

    def tick(spent):
        emit_all(planner.tick(spent))

    def produced(c, spent):
        planner.now += spent
        emit_all(planner.produce(c))
        emit_all(planner.tick(0.0))

    def load(slot, source):
        return pltpu.make_async_copy(source, pool.at[slot], load_sem.at[slot])

    def state_load(index, source):
        return pltpu.make_async_copy(source, states.at[index], state_sem.at[index])

    def turn_tile(target, source):
        def turn(n):
            pool[target, pl.ds(n, 256), :] = pool[source, :, pl.ds(n, 256)].T

        return turn

    def transpose_into(target, source):
        turn = turn_tile(target, source)

        def body(i, carry):
            turn(pl.multiple_of(i * 256, 256))
            return carry

        lax.fori_loop(0, 4, body, 0)

    def product_nn(left, right, put, beside=None):
        def body(i, carry):
            n = pl.multiple_of(i * 256, 256)
            if beside is not None:
                beside(n)
            put(n, product(left(), right(n)))
            return carry

        lax.fori_loop(0, 4, body, 0)

    def product_nt(left, right, put, beside=None):
        def body(i, carry):
            n = pl.multiple_of(i * 256, 256)
            if beside is not None:
                beside(n)
            put(
                n,
                lax.dot_general(
                    left(),
                    right(n),
                    (((1,), (1,)), ((), ())),
                    preferred_element_type=jnp.float32,
                ),
            )
            return carry

        lax.fori_loop(0, 4, body, 0)

    def columns_of(slot):
        return lambda n: pool[slot, :, pl.ds(n, 256)]

    def rows_of(slot):
        return lambda n: pool[slot, pl.ds(n, 256), :]

    def weight_grad(slot_in_made, left, right, beside=None):
        def put(n, value):
            low = value.astype(jnp.bfloat16).reshape(4, 256, 256)
            made[slot_in_made, :, :, pl.ds(n, 256)] = low

        product_nn(left, right, put, beside)

    def add_to_acc(n, value):
        acc[:, pl.ds(n, 256)] += value

    def put_in(slot):
        def put(n, value):
            pool[slot, :, pl.ds(n, 256)] = value.astype(jnp.bfloat16)

        return put

    def norm_back(source, gain_row, gain_at, shift_at, offset_at, target):
        tiles = 8
        rows = 1024 // tiles

        def fetch(i):
            place = pl.ds(pl.multiple_of(i * rows, rows), rows)
            return pltpu.make_async_copy(
                source.at[place, :], stream.at[i % 2], stream_sem.at[i % 2]
            )

        fetch(0).start()

        def body(i, carry):
            gain_sum, shift_sum, offset_sum = carry

            @pl.when(i + 1 < tiles)
            def _():
                fetch(i + 1).start()

            fetch(i).wait()
            r = pl.multiple_of(i * rows, rows)
            values = stream[i % 2]
            centred = values - jnp.mean(values, axis=1, keepdims=True)
            spread = jnp.mean(centred * centred, axis=1, keepdims=True)
            scale = lax.rsqrt(spread + NORM_EPS)
            unit = centred * scale
            grad = acc[pl.ds(r, rows), :]
            inner = grad * gains_ref[gain_row : gain_row + 1, :]
            first = jnp.mean(inner, axis=1, keepdims=True)
            second = jnp.mean(inner * unit, axis=1, keepdims=True)
            back = scale * (inner - first - unit * second)
            acc[pl.ds(r, rows), :] = back
            low = back.astype(jnp.bfloat16)
            pool[target, pl.ds(r, rows), :] = low
            return (
                gain_sum + fold(grad * unit),
                shift_sum + fold(grad),
                offset_sum + fold(low.astype(jnp.float32)),
            )

        zero = jnp.zeros((8, D), jnp.float32)
        sums = lax.fori_loop(0, tiles, body, (zero, zero, zero))
        for row, value in zip((gain_at, shift_at, offset_at), sums):
            small[row : row + 1, :] = jnp.sum(value, axis=0, keepdims=True)

    greet([other_core, other_x, other_y] + others_z)
    load(0, dm_ref).start()
    load(6, h2_ref).start()
    load(2, full_ref.at[SHRINK_AT[0]]).start()
    load(3, gp_ref.at[0]).start()
    load(4, g_ref.at[0]).start()
    load(5, full_ref.at[EXPAND_AT[0]]).start()
    acc_load = pltpu.make_async_copy(d_third_ref, acc, place_sem.at[0])
    acc_load.start()
    small[...] = small_ref[...]
    load(6, h2_ref).wait()
    transpose_into(1, 6)
    load(0, dm_ref).wait()
    acc_load.wait()

    planner.now = 4.0
    plan = []
    for j in range(4):
        entry = []
        planner.now += 3.5
        entry.append(planner.tick(0.0) + planner.free_slot(2 * j))
        planner.now += 2.5
        entry.append(planner.produce(2 * j) + planner.tick(0.0) + planner.free_slot(2 * j + 1))
        planner.now += 2.5
        entry.append(planner.produce(2 * j + 1) + planner.tick(0.0))
        entry.append(planner.tick(2.5))
        plan.append(entry)

    def emit_planned(j, place):
        for n in range(4):
            events = plan[n][place]
            if events:

                @pl.when(j == n)
                def _(events=events):
                    emit_all(events)

    def block(j, carry):
        last = j == 3
        load(2, full_ref.at[SHRINK_AT[0]]).wait()
        load(3, gp_ref.at[0]).wait()

        def put_pre(n, value):
            low = (value * pool[3, :, pl.ds(n, 256)].astype(jnp.float32)).astype(jnp.bfloat16)
            pool[7, :, pl.ds(n, 256)] = low
            small[pl.ds(6 + n // 256, 1), pl.ds(pl.multiple_of(j * 256, 256), 256)] = jnp.sum(
                low.astype(jnp.float32), axis=0, keepdims=True
            )

        load(4, g_ref.at[0]).wait()
        product_nt(lambda: pool[0], rows_of(2), put_pre, turn_tile(6, 4))

        @pl.when(jnp.logical_not(last))
        def _():
            load(2, full_ref.at[SHRINK_AT[0] + 2 * (j + 1) - (j + 1) // 3]).start()
            load(3, gp_ref.at[j + 1]).start()

        @pl.when(last)
        def _():
            load(2, full_ref.at[7]).start()
            load(3, cq_ref).start()

        emit_planned(j, 0)

        @pl.when(jnp.logical_not(last))
        def _():
            load(4, g_ref.at[j + 1]).start()

        @pl.when(last)
        def _():
            load(4, oc_ref).start()

        weight_grad((2 * j) % G_SLOTS, lambda: pool[6], columns_of(0))
        emit_planned(j, 1)
        weight_grad((2 * j + 1) % G_SLOTS, lambda: pool[1], columns_of(7))
        emit_planned(j, 2)
        load(5, full_ref.at[EXPAND_AT[0]]).wait()
        product_nt(lambda: pool[7], rows_of(5), add_to_acc)

        @pl.when(jnp.logical_not(last))
        def _():
            load(5, full_ref.at[EXPAND_AT[1] + 2 * j]).start()

        @pl.when(last)
        def _():
            load(5, full_ref.at[4]).start()

        emit_planned(j, 3)
        return carry

    lax.fori_loop(0, 4, block, 0)

    load(7, h1_ref).start()
    state_loads = [state_load(0, ck_ref), state_load(1, cv_ref), state_load(2, e_ref)]
    for copy in state_loads:
        copy.start()
    lse_load = pltpu.make_async_copy(lse_cross_ref, lse_held, state_sem.at[3])
    lse_load.start()
    norm_back(r2_ref, 13, 13, 14, 5, 0)
    tick(4.0)
    load(4, oc_ref).wait()
    load(2, full_ref.at[7]).wait()
    product_nt(lambda: pool[0], rows_of(2), put_in(4), turn_tile(6, 4))
    load(2, full_ref.at[3]).start()
    tick(2.5)
    emit_all(planner.free_slot(8))
    load(7, h1_ref).wait()
    weight_grad(8 % G_SLOTS, lambda: pool[6], columns_of(0), turn_tile(1, 7))
    load(6, o_ref).start()
    load(7, full_ref.at[5]).start()
    produced(8, 2.5)
    load(3, cq_ref).wait()
    for copy in state_loads:
        copy.wait()
    lse_load.wait()

    def attend_loop(causal, step, length, query, key, value, grad, rows, spent, span=(0, 8)):
        ahead = {n: planner.tick(spent) for n in range(*span)}

        def body(i, carry):
            lanes = pl.ds(pl.multiple_of(i * 128, 128), 128)

            def sums(dq, dv):
                small[rows[0] : rows[0] + 1, lanes] = dq
                small[rows[1] : rows[1] + 1, lanes] = dv

            attend_back_pair(
                causal,
                step,
                length,
                query.at[:, lanes],
                key.at[:, lanes],
                value.at[:, lanes],
                grad.at[:, lanes],
                lse_held.at[pl.ds(i, 1)],
                query.at[:, lanes],
                key.at[:, lanes],
                value.at[:, lanes],
                sums,
                dq_t,
                dk_sum,
                dv_sum,
            )
            for n in range(*span):
                if ahead[n]:

                    @pl.when(i == n)
                    def _(events=ahead[n]):
                        emit_all(events)

            return carry

        lax.fori_loop(*span, body, 0)

    attend_loop(
        False,
        512,
        state_lengths_ref[me],
        pool.at[3],
        states.at[0],
        states.at[1],
        pool.at[4],
        (3, 4),
        2.0,
    )
    lse_load = pltpu.make_async_copy(lse_ref, lse_held, state_sem.at[3])
    lse_load.start()
    emit_all(planner.free_slot(9))
    weight_grad(9 % G_SLOTS, lambda: pool[1], columns_of(3))
    produced(9, 2.5)
    load(5, full_ref.at[4]).wait()
    load(6, o_ref).wait()
    product_nt(lambda: pool[3], rows_of(5), add_to_acc, turn_tile(1, 6))
    load(6, x_in_ref).start()
    load(5, full_ref.at[6]).start()
    load(3, q_ref).start()
    tick(2.5)
    states_t[...] = states[2].T
    for c, index in ((10, 0), (11, 1)):
        emit_all(planner.free_slot(c))
        weight_grad(
            c % G_SLOTS, lambda: states_t[...], lambda n, i=index: states[i, :, pl.ds(n, 256)]
        )
        produced(c, 1.0)
    load(7, full_ref.at[5]).wait()
    load(5, full_ref.at[6]).wait()

    def state_part(n):
        dims = (((1,), (1,)), ((), ()))
        return lax.dot_general(
            states[0], pool[7, pl.ds(n, 256), :], dims, preferred_element_type=jnp.float32
        ) + lax.dot_general(
            states[1], pool[5, pl.ds(n, 256), :], dims, preferred_element_type=jnp.float32
        )

    def put_state(i, carry):
        n = pl.multiple_of(i * 256, 256)
        state_grad_ref[:, pl.ds(n, 256)] = state_part(n).astype(jnp.bfloat16)
        return carry

    lax.fori_loop(0, 4, put_state, 0)
    load(5, k_ref).start()
    load(7, v_ref).start()
    tick(1.0)

    norm_back(r1_ref, 11, 11, 12, 2, 0)
    tick(4.0)
    emit_all(planner.free_slot(12))
    weight_grad(12 % G_SLOTS, lambda: pool[1], columns_of(0))
    produced(12, 2.5)
    load(2, full_ref.at[3]).wait()
    load(6, x_in_ref).wait()
    product_nt(lambda: pool[0], rows_of(2), put_in(4), turn_tile(1, 6))
    load(0, full_ref.at[0]).start()
    load(2, full_ref.at[1]).start()
    load(6, full_ref.at[2]).start()
    tick(2.5)
    load(3, q_ref).wait()
    load(5, k_ref).wait()
    load(7, v_ref).wait()
    lse_load.wait()
    def self_heads(span):
        refs = [pool.at[slot] for slot in (3, 5, 7, 4)]
        attend_loop(True, 256, lengths_ref[me], *refs, (0, 1), 5.0, span)

    def query_key_grad(c, half_of):
        def put(i, carry):
            n = pl.multiple_of((i % 2) * 256 + 512 * half_of, 256)
            value = product(pool[1], pool[3 + 2 * (i // 2), :, pl.ds(n, 256)])
            low = value.astype(jnp.bfloat16).reshape(4, 256, 256)
            made[c % G_SLOTS, :, :, pl.ds(pl.multiple_of(i * 256, 256), 256)] = low
            return carry

        emit_all(planner.free_slot(c))
        lax.fori_loop(0, 4, put, 0)
        produced(c, 2.5)

    self_heads((0, 4))
    query_key_grad(13, 0)
    self_heads((4, 8))

    def small_copy(k):
        source = small if k == 0 else small_sum.at[k - 1]
        device = (other_core, other_x, other_y)[k]
        return remote(source, small_in.at[k], small_send_sem.at[k], small_recv_sem.at[k], device)

    def small_z_copy(d):
        return remote(
            small_sum.at[2],
            small_z.at[z],
            small_send_sem.at[3 + d],
            small_recv_sem.at[3 + d],
            others_z[d],
        )

    def small_step(k):
        small_copy(k).wait()
        before = small[...] if k == 0 else small_sum[k - 1]
        small_sum[k] = before + small_in[k]
        if k < 2:
            small_copy(k + 1).start()
        else:
            small_z[z] = small_sum[2]
            for d in range(3):
                small_z_copy(d).start()

    small_copy(0).start()
    emit_all(planner.free_slot(14))
    weight_grad(14 % G_SLOTS, lambda: pool[1], columns_of(7))
    produced(14, 2.5)
    small_step(0)
    query_key_grad(15, 1)
    small_step(1)
    load(0, full_ref.at[0]).wait()
    product_nt(lambda: pool[3], rows_of(0), add_to_acc)
    tick(2.5)
    small_step(2)
    load(2, full_ref.at[1]).wait()
    product_nt(lambda: pool[5], rows_of(2), add_to_acc)
    tick(2.5)
    for d in range(3):
        small_z_copy(d).wait()
    totals_ref[...] = (small_z[0] + small_z[1]) + (small_z[2] + small_z[3])
    load(6, full_ref.at[2]).wait()

    def put_input(n, value):
        total = acc[:, pl.ds(n, 256)] + value
        pool[4, :, pl.ds(n, 256)] = total.astype(jnp.bfloat16)

    product_nt(lambda: pool[7], rows_of(6), put_input)
    token_copy = pltpu.make_async_copy(pool.at[4], token_grad_ref, load_sem.at[4])
    token_copy.start()
    tick(2.5)

    part[...] = jnp.zeros_like(part)

    def spot(place):
        return (0, 1, 2, 6)[place // 4], (place % 4) * 256

    def scan_load(place):
        slot, row = spot(place)
        return pltpu.make_async_copy(
            out_ref.at[place], pool.at[slot, pl.ds(row, 256), :], scan_sem.at[place]
        )

    scans = {}
    for i in range(2):
        scans[i] = ([(0, 512 * i, 512, i, 0), (2, 512 * i, 512, i, 512)], i, (13, 128 * i))
    for i in range(2, 8):
        scans[i] = ([(1 if i == 2 else i, 0, D, i, 0)], i, (13, 128 * i))
    scans[8] = ([(8 + i, 0, D, 8 + i, 0) for i in range(4)], 8, (14, 0))
    for i in range(4):
        scans[9 + i] = ([(12 + i, 0, D, 12, 0)], 9 + i, (14, 128))

    def scan(name):
        sources, row_lane, (total_row, total_lane) = scans[name]
        width = float(sum(source[2] for source in sources))
        step = 64 if name == 8 else 256

        def body(i, carry):
            cols, weights, total = carry
            r = pl.multiple_of(i * step, step)
            squares = []
            for place, lane, lanes, _, _ in sources:
                slot, row = spot(place)
                tile = pool[slot, pl.ds(row + r, step), lane : lane + lanes]
                squares.append(jnp.square(tile.astype(jnp.float32)))
            row_sum = sum(jnp.sum(square, axis=1, keepdims=True) for square in squares)
            rows = DECAY_RATE * rows_ref[pl.ds(r, step), row_lane : row_lane + 1] + (
                1.0 - DECAY_RATE
            ) * (row_sum / width + FACTOR_EPS)
            rows_out[pl.ds(r, step), row_lane : row_lane + 1] = rows
            inverse = 1.0 / rows
            cols = [c + fold(s) for c, s in zip(cols, squares)]
            weights = [w + fold(s * inverse) for w, s in zip(weights, squares)]
            return cols, weights, total + fold(rows)

        zeros = [jnp.zeros((8, source[2]), jnp.float32) for source in sources]
        cols, weights, total = lax.fori_loop(
            0, 256 // step, body, (zeros, zeros, jnp.zeros((8, 1), jnp.float32))
        )
        for (_, _, lanes, slot, lane), col, weighted in zip(sources, cols, weights):
            here = slice(lane, lane + lanes)
            part[slot : slot + 1, here] += jnp.sum(col, axis=0, keepdims=True)
            part[16 + slot : 17 + slot, here] += jnp.sum(weighted, axis=0, keepdims=True)
        part[total_row : total_row + 1, total_lane : total_lane + 128] += jnp.broadcast_to(
            jnp.sum(total), (1, 128)
        )

    chunk_at = {place: c for c, place in enumerate(place_of)}
    tasks = [
        ([chunk_at[source[0]] for source in scans[name][0]], name)
        for name in (9, 10, 11, 12, 8, 7, 4, 5, 6, 3, 2, 0, 1)
    ]
    loaded = set()
    for c in range(CHUNKS):
        if planner.stage[c] > 8:
            scan_load(place_of[c]).start()
    for first, second in planner.drain(tasks, 1.5):
        if first != "task":
            emit(first, second)
            if first == 8:
                scan_load(place_of[second]).start()
            continue
        for source in scans[second][0]:
            if source[0] not in loaded:
                loaded.add(source[0])
                scan_load(source[0]).wait()
        scan(second)
    total = line_sum(part, whole, line_send_sem, line_recv_sem, z, others_z)
    row_counts = [D] * 12 + [FF]
    means = [total[13:14, 128 * i : 128 * i + 1] / D for i in range(8)]
    means = means + [total[14:15, 0:1] / D] * 4 + [total[14:15, 128:129] / FF]
    cols_new, quotients = [], []
    for slot in range(13):
        new = DECAY_RATE * cols_ref[slot : slot + 1, :] + (1.0 - DECAY_RATE) * (
            total[slot : slot + 1] / row_counts[slot] + FACTOR_EPS
        )
        cols_new.append(new)
        quotients.append(jnp.sum(total[16 + slot : 17 + slot] / new, axis=1, keepdims=True))
        cols_out[slot : slot + 1, :] = new
    expand_quotient = quotients[8] + quotients[9] + quotients[10] + quotients[11]
    for slot in range(13):
        if slot < 8:
            mean_square = means[slot] * quotients[slot] / (D * D)
            rate = STEP_RATE * (OUT_GAIN if slot % 4 == 3 else 1.0)
        else:
            quotient = expand_quotient if slot < 12 else quotients[12]
            mean_square = means[slot] * quotient / (D * FF)
            rate = STEP_RATE
        factor = rate / jnp.maximum(1.0, jnp.sqrt(mean_square) / CLIP_LEVEL)
        scale_out[slot : slot + 1, :] = lax.rsqrt(cols_new[slot] / means[slot]) * factor
    token_copy.wait()


def backward(scalars, held, gains, small, factor_rows, factor_cols):
    any_space = pl.BlockSpec(memory_space=pl.ANY)
    vmem = pl.BlockSpec(memory_space=pltpu.VMEM)
    shape = jax.ShapeDtypeStruct
    dma = pltpu.SemaphoreType.DMA
    low = jnp.bfloat16
    wide = jnp.float32
    rows = small.shape[0]
    return pl.pallas_call(
        backward_kernel,
        out_shape=(
            shape((1024, D), low),
            shape((128, D), low),
            shape((CHUNKS, 256, D), low),
            shape(small.shape, wide),
            shape((256, 128), wide),
            shape((16, D), wide),
            shape((16, D), wide),
            shape((CHUNKS, 4, 128, D), low),
        ),
        in_specs=[SCALARS] * 2 + [any_space] * len(held) + [vmem] * 4,
        out_specs=(any_space, vmem, any_space, vmem, vmem, vmem, vmem, any_space),
        scratch_shapes=[
            pltpu.VMEM((POOL, 1024, D), low),
            pltpu.VMEM((1024, D), wide),
            pltpu.VMEM((G_SLOTS, 4, 256, D), low),
            pltpu.VMEM((R_SLOTS, 4, 128, D), low),
            pltpu.VMEM((CHUNKS, 4, 64, D), low),
            pltpu.VMEM((CHUNKS, 4, 32, D), low),
            pltpu.VMEM((CHUNKS, 3, 32, D), low),
            pltpu.VMEM((2, 128, D), wide),
            pltpu.VMEM((128, 1024), wide),
            pltpu.VMEM((2, 1024, 128), wide),
            pltpu.VMEM((2, 1024, 128), wide),
            pltpu.VMEM((8, 8, 1024), wide),
            pltpu.VMEM((3, 128, D), low),
            pltpu.VMEM((D, 128), low),
            pltpu.VMEM((rows, D), wide),
            pltpu.VMEM((3, rows, D), wide),
            pltpu.VMEM((3, rows, D), wide),
            pltpu.VMEM((4, rows, D), wide),
            pltpu.VMEM((32, D), wide),
            pltpu.VMEM((4, 32, D), wide),
            dma((POOL,)),
            dma((2,)),
            dma((4,)),
            dma((R_SLOTS,)),
            dma((CHUNKS,)),
            dma((3,)),
            dma((3,)),
            dma((6, CHUNKS)),
            dma((6, CHUNKS)),
            dma((CHUNKS, 3)),
            dma((CHUNKS, 3)),
            dma((CHUNKS,)),
            dma((6,)),
            dma((6,)),
        ],
        compiler_params=pltpu.CompilerParams(
            collective_id=0, has_side_effects=True, vmem_limit_bytes=62 * MIB
        ),
    )(*scalars, *held, gains, small, factor_rows, factor_cols)[0:7]


def line_sum(part, whole, send_sem, recv_sem, z, others_z):
    copies = [
        remote(part, whole.at[z], send_sem.at[d], recv_sem.at[d], others_z[d]) for d in range(3)
    ]
    for copy in copies:
        copy.start()
    whole[z] = part[...]
    for copy in copies:
        copy.wait()
    return (whole[0] + whole[1]) + (whole[2] + whole[3])


def update_attention_kernel(
    grad_ref, weight_ref, rows_ref, scale_ref, grad_out, new_out, copy_out, grads, change
):
    block = grad_ref.shape[1]
    for i in range(8):
        rows = lax.rsqrt(rows_ref[:, i : i + 1])
        every = pl.ds(i, block, stride=8)
        for lane in range(8):
            columns = slice(lane * 128, lane * 128 + 128)
            if i < 2:
                start = 512 * i + 128 * (lane % 4)
                grad = grad_ref[2 * (lane // 4), :, start : start + 128]
            else:
                grad = grad_ref[1 if i == 2 else i, :, columns]
            grad = grad.astype(jnp.float32)
            grads[lane, every, :] = grad
            change[lane, every, :] = grad * rows * scale_ref[i : i + 1, columns]
    for lane in range(8):
        columns = slice(lane * 128, lane * 128 + 128)
        grad_out[:, columns] = grads[lane]
        new = weight_ref[:, columns] - change[lane]
        new_out[:, columns] = new
        copy_out[:, columns] = new.astype(jnp.bfloat16)


def update_attention(grads, weights, rows, scale):
    block = 64
    wide = pl.BlockSpec((block * 8, D), lambda i: (i, 0))
    shape = jax.ShapeDtypeStruct
    new = pl.pallas_call(
        update_attention_kernel,
        grid=(256 // block,),
        out_shape=(
            shape((2048, D), jnp.float32),
            shape((2048, D), jnp.float32),
            shape((2048, D), jnp.bfloat16),
        ),
        in_specs=[
            pl.BlockSpec((8, block, D), lambda i: (0, i, 0)),
            wide,
            pl.BlockSpec((block, 128), lambda i: (i, 0)),
            pl.BlockSpec((16, D), lambda i: (0, 0)),
        ],
        out_specs=(wide,) * 3,
        scratch_shapes=[pltpu.VMEM((8, block * 8, 128), jnp.float32)] * 2,
        compiler_params=pltpu.CompilerParams(vmem_limit_bytes=62 * MIB),
    )(grads, weights.reshape(2048, D), rows, scale)
    return [t.reshape(256, 8, D) for t in new]


def update_kernel(
    first, slots, grad_ref, weight_ref, rows_ref, scale_ref, grad_out, new_out, copy_out
):
    spans = 4 if slots == 4 else 1
    wide = D // spans
    for i in range(slots):
        grads = grad_ref[i].astype(jnp.float32)
        changes = grads * (lax.rsqrt(rows_ref[...]) * scale_ref[first + i : first + i + 1, :])
        for s in range(spans):
            start = s * D + i * wide
            columns = slice(start, start + wide)
            part = slice(s * wide, s * wide + wide)
            grad_out[:, columns] = grads[:, part]
            new = weight_ref[:, columns] - changes[:, part]
            new_out[:, columns] = new
            copy_out[:, columns] = new.astype(jnp.bfloat16)


def update_plain(grads, weights, rows, scale, first, slots, grad_map):
    count, width = weights.shape
    block = 256 // slots
    wide = pl.BlockSpec((block, width), lambda i: (i, 0))
    shape = jax.ShapeDtypeStruct
    return pl.pallas_call(
        lambda *refs: update_kernel(first, slots, *refs),
        grid=(count // block,),
        out_shape=(
            shape(weights.shape, jnp.float32),
            shape(weights.shape, jnp.float32),
            shape(weights.shape, jnp.bfloat16),
        ),
        in_specs=[
            pl.BlockSpec((slots, block, D), grad_map),
            wide,
            pl.BlockSpec((block, 1), lambda i: (i, 0)),
            pl.BlockSpec((16, D), lambda i: (0, 0)),
        ],
        out_specs=(wide,) * 3,
        compiler_params=pltpu.CompilerParams(vmem_limit_bytes=62 * MIB),
    )(grads, weights, rows, scale)


def update_direct(grads, rows, scale, attention_weights, expand_weight, shrink_weight):
    shr_rows = rows[:, 9:13].T.reshape(-1, 1)
    attention = update_attention(grads, attention_weights, rows, scale)
    expand = update_plain(grads, expand_weight, rows[:, 8:9], scale, 8, 4, lambda i: (2, i, 0))
    shrink = update_plain(
        grads, shrink_weight, shr_rows, scale, 12, 1, lambda i: (12 + i, 0, 0)
    )
    return attention, expand, shrink, (rows[:, 0:8].T, rows[:, 8], shr_rows[:, 0])


def as_rows(vector):
    rows = -(-vector.shape[0] // 1024) * 8
    return jnp.pad(vector, (0, rows * 128 - vector.shape[0])).reshape(rows, 128)


def masked_scores(query_part, key_heads, first_row, valid_count, causal):
    scores = jnp.einsum("qhd,khd->hqk", query_part, key_heads, preferred_element_type=jnp.float32)
    key_places = jnp.arange(key_heads.shape[0], dtype=jnp.int32)[None, :]
    usable = key_places < valid_count
    if causal:
        query_places = first_row + jnp.arange(query_part.shape[0], dtype=jnp.int32)[:, None]
        usable = usable & (key_places <= query_places)
    return jnp.where(usable[None], scores, MASKED)


def attend_forward(queries, key_heads, values, valid_count, causal):
    query_rows = queries.shape[0]
    step_rows = min(512, query_rows)
    outputs, stored = ([], [])
    for b in range(query_rows // step_rows):
        first_row = b * step_rows
        key_end = first_row + step_rows if causal else key_heads.shape[0]
        scores = masked_scores(
            queries[first_row : first_row + step_rows],
            key_heads[:key_end],
            first_row,
            valid_count,
            causal,
        )
        row_max = jnp.max(scores, axis=-1, keepdims=True)
        raised = jnp.exp(scores - row_max)
        totals = jnp.sum(raised, axis=-1, keepdims=True)
        probs_low = (raised / totals).astype(jnp.bfloat16)
        outputs.append(
            jnp.einsum(
                "hqk,khd->qhd", probs_low, values[:key_end], preferred_element_type=jnp.float32
            )
        )
        stored.append(row_max + jnp.log(totals))
    return (jnp.concatenate(outputs, axis=0), stored)


def attend_backward(queries, key_heads, values, grad_out, stored, valid_count, causal):
    query_rows = queries.shape[0]
    key_rows = key_heads.shape[0]
    step_rows = min(512, query_rows)
    grad_queries = []
    grad_keys = jnp.zeros(key_heads.shape, jnp.float32)
    grad_values = jnp.zeros(values.shape, jnp.float32)
    for b in range(query_rows // step_rows):
        first_row = b * step_rows
        key_end = first_row + step_rows if causal else key_rows
        query_part = queries[first_row : first_row + step_rows]
        grad_part = grad_out[first_row : first_row + step_rows]
        scores = masked_scores(query_part, key_heads[:key_end], first_row, valid_count, causal)
        probs = jnp.exp(scores - stored[b])
        probs_low = probs.astype(jnp.bfloat16)
        grad_probs = jnp.einsum(
            "qhd,khd->hqk", grad_part, values[:key_end], preferred_element_type=jnp.float32
        )
        value_part = jnp.einsum(
            "hqk,qhd->khd", probs_low, grad_part, preferred_element_type=jnp.float32
        )
        grad_scores = probs * (grad_probs - jnp.sum(probs * grad_probs, axis=-1, keepdims=True))
        scores_low = grad_scores.astype(jnp.bfloat16)
        grad_queries.append(
            jnp.einsum(
                "hqk,khd->qhd", scores_low, key_heads[:key_end], preferred_element_type=jnp.float32
            )
        )
        key_part = jnp.einsum(
            "hqk,qhd->khd", scores_low, query_part, preferred_element_type=jnp.float32
        )
        padding = ((0, key_rows - key_end), (0, 0), (0, 0))
        grad_keys = grad_keys + jnp.pad(key_part, padding)
        grad_values = grad_values + jnp.pad(value_part, padding)
    return (jnp.concatenate(grad_queries, axis=0), grad_keys, grad_values)


def gather_rows(piece):
    return lax.all_gather(piece, ("shard", "rep"), axis=0, tiled=True)


def own_piece(block, replicas):
    rows = block.shape[0] // replicas
    return lax.dynamic_slice_in_dim(block, lax.axis_index("rep") * rows, rows, axis=0)


def scatter_rows(grad):
    piece = lax.psum_scatter(
        grad.astype(jnp.bfloat16), ("shard", "rep"), scatter_dimension=0, tiled=True
    )
    return lax.all_gather(piece, "rep", axis=0, tiled=True)


def local_factors(grad, rows):
    square = grad * grad
    rows_new = DECAY_RATE * rows + (1.0 - DECAY_RATE) * jnp.mean(square + FACTOR_EPS, axis=-1)
    col_part = jnp.sum(square + FACTOR_EPS, axis=0)
    weighted = jnp.sum(square / rows_new[..., None], axis=0)
    return rows_new, col_part, weighted, jnp.sum(rows_new, axis=0)


def finish_factors(grad, weight, rows_new, cols, col_sum, weighted, row_total, row_count, rate):
    cols_new = DECAY_RATE * cols + (1.0 - DECAY_RATE) * col_sum / row_count
    mean_rows = row_total / row_count
    mean_square = mean_rows * jnp.sum(weighted / cols_new, axis=-1) / (row_count * cols.shape[-1])
    factor = rate / jnp.maximum(1.0, jnp.sqrt(mean_square) / CLIP_LEVEL)
    scaled = lax.rsqrt(cols_new / mean_rows[..., None]) * factor[..., None]
    fresh = weight - grad * (lax.rsqrt(rows_new)[..., None] * scaled[None])
    return fresh, cols_new


def plain_device(
    tokens,
    encoder,
    cotangent,
    lengths,
    encoder_lengths,
    dealt_order,
    attention_weights,
    expand_weight,
    shrink_weight,
    small_params,
    attention_rows,
    attention_cols,
    expand_rows,
    expand_cols,
    shrink_rows,
    shrink_cols,
    small_moment,
):
    devices = lax.axis_size(("rep", "shard"))
    replicas = lax.axis_size("rep")
    shards = lax.axis_size("shard")
    slot_tokens = tokens.shape[0]
    slot_states = encoder.shape[0]
    position = lax.axis_index(("rep", "shard"))
    inverse = (
        jnp.zeros((devices,), jnp.int32).at[dealt_order].set(jnp.arange(devices, dtype=jnp.int32))
    )
    qkv_piece = own_piece(attention_weights[:, 0:3, :].reshape(-1, 3 * D), replicas)
    rest_piece = own_piece(attention_weights[:, 3:8, :].reshape(-1, 5 * D), replicas)
    qkv_full = gather_rows(qkv_piece.astype(jnp.bfloat16))
    rest_full = gather_rows(rest_piece.astype(jnp.bfloat16))
    expand_full = gather_rows(own_piece(expand_weight, replicas).astype(jnp.bfloat16))
    shrink_full = gather_rows(own_piece(shrink_weight, replicas).astype(jnp.bfloat16))
    spread = lax.all_to_all(
        tokens.reshape(devices, slot_tokens // devices, D),
        ("rep", "shard"),
        split_axis=0,
        concat_axis=0,
        tiled=True,
    )
    picked = jnp.take(spread, inverse, axis=0)
    tokens = lax.all_to_all(
        picked, ("rep", "shard"), split_axis=0, concat_axis=0, tiled=True
    ).reshape(slot_tokens, D)
    states = encoder
    incoming = cotangent
    valid_tokens = lengths[position]
    valid_states = encoder_lengths[position]
    matrices = [qkv_full[:, i * D : (i + 1) * D] for i in range(3)] + [
        rest_full[:, i * D : (i + 1) * D] for i in range(5)
    ]
    parts = unpack(small_params)
    token_heads = (slot_tokens, HEADS, HEAD_DIM)
    state_heads = (slot_states, HEADS, HEAD_DIM)
    q_self = ((forward_product(tokens, matrices[0]) + parts[0]) * 0.125).astype(
        jnp.bfloat16
    )
    k_self = forward_product(tokens, matrices[1]).astype(jnp.bfloat16)
    v_self = (forward_product(tokens, matrices[2]) + parts[1]).astype(jnp.bfloat16)
    o_self, lse_self = attend_forward(
        q_self.reshape(token_heads),
        k_self.reshape(token_heads),
        v_self.reshape(token_heads),
        valid_tokens,
        True,
    )
    o_self_low = o_self.reshape(slot_tokens, D).astype(jnp.bfloat16)
    branch_a = forward_product(o_self_low, matrices[3]) + parts[2]
    tokens_wide = tokens.astype(jnp.float32)
    hidden_one, norm_one_back = jax.vjp(layer_norm, tokens_wide + branch_a, parts[8], parts[9])
    hidden_one_low = hidden_one.astype(jnp.bfloat16)
    q_cross = (
        (forward_product(hidden_one_low, matrices[4]) + parts[3]) * 0.125
    ).astype(jnp.bfloat16)
    k_cross = forward_product(states, matrices[5]).astype(jnp.bfloat16)
    v_cross = (forward_product(states, matrices[6]) + parts[4]).astype(jnp.bfloat16)
    o_cross, lse_cross = attend_forward(
        q_cross.reshape(token_heads),
        k_cross.reshape(state_heads),
        v_cross.reshape(state_heads),
        valid_states,
        False,
    )
    o_cross_low = o_cross.reshape(slot_tokens, D).astype(jnp.bfloat16)
    branch_c = forward_product(o_cross_low, matrices[7]) + parts[5]
    hidden_two, norm_two_back = jax.vjp(layer_norm, hidden_one + branch_c, parts[10], parts[11])
    hidden_two_low = hidden_two.astype(jnp.bfloat16)
    pre_act = forward_product(hidden_two_low, expand_full) + parts[6]
    activated, gelu_back = jax.vjp(gelu_exact, pre_act)
    activated_low = activated.astype(jnp.bfloat16)
    branch_m = forward_product(activated_low, shrink_full) + parts[7]
    result, norm_three_back = jax.vjp(layer_norm, hidden_two + branch_m, parts[12], parts[13])
    usable_rows = (jnp.arange(slot_tokens, dtype=jnp.int32) < valid_tokens).astype(jnp.float32)[
        :, None
    ]
    squares = jnp.stack(
        [
            jnp.sum(usable_rows * t * t)
            for t in (tokens_wide, branch_a, hidden_one, branch_c, hidden_two, branch_m)
        ]
    )
    d_third, d_gain_three, d_shift_three = norm_three_back(
        incoming.astype(jnp.float32) * usable_rows
    )
    d_mlp = d_third.astype(jnp.bfloat16)
    grad_shrink = weight_product(activated_low, d_mlp)
    grad_shrink_offset = row_sum(d_mlp)
    d_activated = input_product(d_mlp, shrink_full)
    d_pre = gelu_back(d_activated)[0].astype(jnp.bfloat16)
    grad_expand = weight_product(hidden_two_low, d_pre)
    grad_expand_offset = row_sum(d_pre)
    d_hidden_two = d_third + input_product(d_pre, expand_full)
    d_second, d_gain_two, d_shift_two = norm_two_back(d_hidden_two)
    d_branch_c = d_second.astype(jnp.bfloat16)
    grad_cross_out = weight_product(o_cross_low, d_branch_c)
    grad_cross_out_offset = row_sum(d_branch_c)
    d_o_cross = input_product(d_branch_c, matrices[7]).astype(jnp.bfloat16)
    grad_cq, grad_ck, grad_cv = attend_backward(
        q_cross.reshape(token_heads),
        k_cross.reshape(state_heads),
        v_cross.reshape(state_heads),
        d_o_cross.reshape(token_heads),
        lse_cross,
        valid_states,
        False,
    )
    dq_cross = (grad_cq.reshape(slot_tokens, D) * 0.125).astype(jnp.bfloat16)
    dk_cross = grad_ck.reshape(slot_states, D).astype(jnp.bfloat16)
    dv_cross = grad_cv.reshape(slot_states, D).astype(jnp.bfloat16)
    grad_cross_query = weight_product(hidden_one_low, dq_cross)
    grad_cross_key = weight_product(states, dk_cross)
    grad_cross_value = weight_product(states, dv_cross)
    state_grad = input_product(dk_cross, matrices[5]) + input_product(
        dv_cross, matrices[6]
    )
    d_hidden_one = d_second + input_product(dq_cross, matrices[4])
    d_first, d_gain_one, d_shift_one = norm_one_back(d_hidden_one)
    d_branch_a = d_first.astype(jnp.bfloat16)
    grad_self_out = weight_product(o_self_low, d_branch_a)
    grad_self_out_offset = row_sum(d_branch_a)
    d_o_self = input_product(d_branch_a, matrices[3]).astype(jnp.bfloat16)
    grad_sq, grad_sk, grad_sv = attend_backward(
        q_self.reshape(token_heads),
        k_self.reshape(token_heads),
        v_self.reshape(token_heads),
        d_o_self.reshape(token_heads),
        lse_self,
        valid_tokens,
        True,
    )
    dq_self = (grad_sq.reshape(slot_tokens, D) * 0.125).astype(jnp.bfloat16)
    dk_self = grad_sk.reshape(slot_tokens, D).astype(jnp.bfloat16)
    dv_self = grad_sv.reshape(slot_tokens, D).astype(jnp.bfloat16)
    grad_self_query = weight_product(tokens, dq_self)
    grad_self_key = weight_product(tokens, dk_self)
    grad_self_value = weight_product(tokens, dv_self)
    token_grad = (
        d_first
        + input_product(dq_self, matrices[0])
        + input_product(dk_self, matrices[1])
        + input_product(dv_self, matrices[2])
    )
    small_partial = jnp.concatenate(
        [
            row_sum(dq_self),
            row_sum(dv_self),
            grad_self_out_offset,
            row_sum(dq_cross),
            row_sum(dv_cross),
            grad_cross_out_offset,
            grad_expand_offset,
            grad_shrink_offset,
            d_gain_one,
            d_shift_one,
            d_gain_two,
            d_shift_two,
            d_gain_three,
            d_shift_three,
        ]
    )
    totals = lax.psum(jnp.concatenate([small_partial, squares]), ("rep", "shard"))
    g_shrink = scatter_rows(grad_shrink)
    g_expand = scatter_rows(grad_expand)
    g_rest = scatter_rows(
        jnp.concatenate(
            [grad_self_out, grad_cross_query, grad_cross_key, grad_cross_value, grad_cross_out],
            axis=1,
        )
    )
    g_qkv = scatter_rows(
        jnp.concatenate([grad_self_query, grad_self_key, grad_self_value], axis=1)
    )
    g_attention = (
        jnp.concatenate([g_qkv, g_rest], axis=1).reshape(-1, 8, D).astype(jnp.float32)
    )
    g_expand = g_expand.astype(jnp.float32)
    g_shrink = g_shrink.astype(jnp.float32)
    attention_rows_new, *attention_parts = local_factors(g_attention, attention_rows.T)
    expand_rows_new, *expand_parts = local_factors(g_expand, expand_rows)
    shrink_rows_new, *shrink_parts = local_factors(g_shrink, shrink_rows)
    flat = attention_parts + expand_parts + shrink_parts
    summed = lax.psum(jnp.concatenate([t.reshape(-1) for t in flat]), "shard")
    sums = []
    offset = 0
    for t in flat:
        sums.append(summed[offset : offset + t.size].reshape(t.shape))
        offset = offset + t.size
    attention_rates = STEP_RATE * jnp.where(jnp.arange(8) % 4 == 3, OUT_GAIN, 1.0).astype(
        jnp.float32
    )
    attention_new, attention_cols_new = finish_factors(
        g_attention,
        attention_weights,
        attention_rows_new,
        attention_cols,
        *sums[0:3],
        D,
        attention_rates,
    )
    expand_new, expand_cols_new = finish_factors(
        g_expand, expand_weight, expand_rows_new, expand_cols, *sums[3:6], D, STEP_RATE
    )
    shrink_new, shrink_cols_new = finish_factors(
        g_shrink, shrink_weight, shrink_rows_new, shrink_cols, *sums[6:9], FF, STEP_RATE
    )
    small_grad = totals[: small_params.shape[0]]
    small_moment_new = DECAY_RATE * small_moment + (1.0 - DECAY_RATE) * (
        small_grad * small_grad + FACTOR_EPS
    )
    small_update = small_grad * lax.rsqrt(small_moment_new)
    small_scale = jnp.sqrt(jnp.mean(small_update * small_update))
    small_new = small_params - SMALL_RATE * small_update / jnp.maximum(
        1.0, small_scale / CLIP_LEVEL
    )
    norm_stats = jnp.sqrt(
        totals[small_params.shape[0] :] / (jnp.sum(lengths).astype(jnp.float32) * D)
    )
    return (
        result.astype(jnp.bfloat16),
        token_grad.astype(jnp.bfloat16),
        state_grad.astype(jnp.bfloat16),
        g_attention,
        g_expand,
        g_shrink,
        small_grad,
        attention_new,
        expand_new,
        shrink_new,
        small_new,
        attention_new.astype(jnp.bfloat16),
        expand_new.astype(jnp.bfloat16),
        shrink_new.astype(jnp.bfloat16),
        attention_rows_new.T,
        attention_cols_new,
        expand_rows_new,
        expand_cols_new,
        shrink_rows_new,
        shrink_cols_new,
        small_moment_new,
        norm_stats,
    )


def direct_device(
    tokens,
    encoder,
    cotangent,
    lengths,
    encoder_lengths,
    dealt_order,
    attention_weights,
    expand_weight,
    shrink_weight,
    small_params,
    attention_rows,
    attention_cols,
    expand_rows,
    expand_cols,
    shrink_rows,
    shrink_cols,
    small_moment,
):
    inverse = jnp.zeros((32,), jnp.int32).at[dealt_order].set(jnp.arange(32, dtype=jnp.int32))
    params = small_params.reshape(17, D)
    weights = (attention_weights.reshape(2048, D), expand_weight, shrink_weight)
    (
        tokens,
        full,
        q_self,
        k_self,
        v_self,
        o_self,
        lse_self,
        q_cross,
        k_cross,
        v_cross,
        o_cross,
        lse_cross,
        summed_one,
        summed_two,
        hidden_one,
        hidden_two,
        activated,
        slope,
        output,
        d_mlp,
        d_third,
        small_first,
    ) = forward(
        (inverse, lengths, encoder_lengths), tokens, weights, encoder, cotangent, params
    )
    factor_rows = jnp.concatenate(
        [attention_rows, expand_rows.reshape(1, 256), shrink_rows.reshape(4, 256)]
    )
    factor_rows = jnp.pad(factor_rows.T, ((0, 0), (0, 115)))
    factor_cols = jnp.concatenate(
        [attention_cols, hidden_blocks(expand_cols), shrink_cols.reshape(1, D), jnp.ones((3, D))]
    )
    token_grad, state_grad, reduced, totals, factor_rows, factor_cols, scale = backward(
        (lengths, encoder_lengths),
        (
            d_mlp,
            d_third,
            activated,
            slope,
            full.reshape(GATHERED, 1024, D),
            hidden_two,
            hidden_one,
            tokens.reshape(1024, D),
            encoder,
            o_cross,
            o_self,
            summed_one,
            summed_two,
            q_self,
            k_self,
            v_self,
            q_cross,
            k_cross,
            v_cross,
            lse_self,
            lse_cross,
        ),
        params,
        small_first,
        factor_rows,
        factor_cols,
    )
    attention, expand, shrink, rows_new = update_direct(
        reduced, factor_rows, scale, attention_weights, expand_weight, shrink_weight
    )
    cols_new = (factor_cols[0:8], hidden_flat(factor_cols[8:12]), factor_cols[12])
    small_grad = totals[0:17].reshape(-1)
    small_moment_new = DECAY_RATE * small_moment + (1.0 - DECAY_RATE) * (
        small_grad * small_grad + FACTOR_EPS
    )
    small_update = small_grad * lax.rsqrt(small_moment_new)
    small_scale = jnp.sqrt(jnp.mean(small_update * small_update))
    small_new = small_params - SMALL_RATE * small_update / jnp.maximum(
        1.0, small_scale / CLIP_LEVEL
    )
    norm_stats = jnp.sqrt(totals[17, 0:6] / (jnp.sum(lengths).astype(jnp.float32) * D))
    return (
        output,
        token_grad,
        state_grad,
        attention[0],
        expand[0],
        shrink[0],
        small_grad,
        attention[1],
        expand[1],
        shrink[1],
        small_new,
        attention[2],
        expand[2],
        shrink[2],
        rows_new[0],
        cols_new[0],
        rows_new[1],
        cols_new[1],
        rows_new[2],
        cols_new[2],
        small_moment_new,
        norm_stats,
    )


def on_device(*args):
    if lax.axis_size("rep") == 8 and lax.axis_size("shard") == 4:
        return direct_device(*args)
    return plain_device(*args)


def solution(mesh):
    in_specs = (
        P(("rep", "shard"), None),
        P(("rep", "shard"), None),
        P(("rep", "shard"), None),
        P(),
        P(),
        P(),
        P("shard", None, None),
        P("shard", None),
        P("shard", None),
        P(),
        P(None, "shard"),
        P(),
        P("shard"),
        P(),
        P("shard"),
        P(),
        P(),
    )
    out_specs = (
        P(("rep", "shard"), None),
        P(("rep", "shard"), None),
        P(("rep", "shard"), None),
        P("shard", None, None),
        P("shard", None),
        P("shard", None),
        P(),
        P("shard", None, None),
        P("shard", None),
        P("shard", None),
        P(),
        P("shard", None, None),
        P("shard", None),
        P("shard", None),
        P(None, "shard"),
        P(),
        P("shard"),
        P(),
        P("shard"),
        P(),
        P(),
        P(),
    )
    return jax.shard_map(
        on_device, mesh=mesh, in_specs=in_specs, out_specs=out_specs, check_vma=False
    )
```

```python
import math

import jax
import jax.numpy as jnp
from jax import lax
from jax.experimental import pallas as pl
from jax.experimental.pallas import tpu as pltpu
from jax.sharding import PartitionSpec as P

D = 1024
HEADS = 16
HEAD_DIM = 64
FF = 4096


DECAY_RATE = 0.5
CLIP_LEVEL = 0.25
STEP_RATE = 0.1
SMALL_RATE = 0.4
OUT_GAIN = 8.0
NORM_EPS = 1e-05
FACTOR_EPS = 1e-30
MASKED = -1e30
MESH = pl.DeviceIdType.MESH
CHUNKS = 16
GATHERED = 16
EXPAND_AT = (8, 9, 11, 13)
SHRINK_AT = (10, 12, 14, 15)
MIB = 1 << 20


def layer_norm(r, norm_gain, norm_shift):
    centred = r - jnp.mean(r, axis=-1, keepdims=True)
    spread = jnp.mean(centred * centred, axis=-1, keepdims=True)
    return centred * lax.rsqrt(spread + NORM_EPS) * norm_gain + norm_shift


def gelu_exact(values):
    return jax.nn.gelu(values, approximate=False)


def unpack(small):
    extents = [D] * 6 + [FF] + [D] * 7
    pieces = []
    offset = 0
    for extent in extents:
        pieces.append(small[offset : offset + extent])
        offset = offset + extent
    return pieces


def forward_product(source, matrix):
    return jnp.dot(source, matrix, preferred_element_type=jnp.float32)


def input_product(grad_low, matrix):
    return jnp.einsum("to,io->ti", grad_low, matrix, preferred_element_type=jnp.float32)


def weight_product(source, grad_low):
    return jnp.einsum("ti,to->io", source, grad_low, preferred_element_type=jnp.float32)


def row_sum(grad_low):
    return jnp.sum(grad_low.astype(jnp.float32), axis=0)


def transposed(block):
    return block.astype(jnp.float32).T.astype(jnp.bfloat16)


def half_lanes(shape, dim):
    return lax.broadcasted_iota(jnp.int32, shape, dim)


def masked_keys(keys, length, head):
    place = half_lanes(keys.shape, 0)
    lane = half_lanes(keys.shape, 1)
    blocked = jnp.where((lane == 64 - 64 * head) & (place >= length), MASKED, 0.0)
    own = (lane >= 64 * head) & (lane < 64 * head + 64)
    return jnp.where(own, keys.astype(jnp.float32), blocked).astype(jnp.bfloat16)


def own_head(rows_t, head, fill):
    place = half_lanes(rows_t.shape, 0)
    own = (place >= 64 * head) & (place < 64 * head + 64)
    other = jnp.where(place == 64 - 64 * head, fill, 0.0)
    return jnp.where(own, rows_t.astype(jnp.float32), other).astype(jnp.bfloat16)


def product(first, second):
    return jnp.dot(first, second, preferred_element_type=jnp.float32)


def causal_mask(scores, step):
    kept = scores.shape[0] - step
    last = scores[kept:]
    allowed = half_lanes(last.shape, 0) <= half_lanes(last.shape, 1)
    last = jnp.where(allowed, last, MASKED)
    return last if kept == 0 else jnp.concatenate([scores[:kept], last], axis=0)


def attend_pair(
    causal, step, length, q_ref, k_ref, v_ref, o_ref, lse_ref, o_t, first_row=0
):
    count = q_ref.shape[0]
    q_t = transposed(q_ref[...])
    v_t = transposed(v_ref[...])
    keys = [masked_keys(k_ref[...], length, head) for head in range(2)]
    queries = [own_head(q_t, head, 1.0) for head in range(2)]
    units = [(head, start) for start in range(0, count, step) for head in range(2)]

    def scores_of(head, start):
        end = first_row + start + step if causal else k_ref.shape[0]
        return product(keys[head][:end], queries[head][:, start : start + step])

    ahead = scores_of(*units[0])
    for index, (head, start) in enumerate(units):
        scores = ahead
        if index + 1 < len(units):
            ahead = scores_of(*units[index + 1])
        rows = slice(64 * head, 64 * head + 64)
        columns = slice(start, start + step)
        if causal:
            scores = causal_mask(scores, step)
        top = jnp.max(scores, axis=0, keepdims=True)
        raised = jnp.exp(scores - top)
        total = jnp.sum(raised, axis=0, keepdims=True)
        probs = (raised * (1.0 / total)).astype(jnp.bfloat16)
        o_t[rows, columns] = product(v_t[rows, : scores.shape[0]], probs)
        place = slice(first_row + start, first_row + start + step)
        lse_ref[0, head : head + 1, place] = top + jnp.log(total)
    o_ref[...] = o_t[:, :count].T.astype(jnp.bfloat16)


def attend_back_pair(
    causal,
    step,
    length,
    q_ref,
    k_ref,
    v_ref,
    do_ref,
    lse_ref,
    dq_ref,
    dk_ref,
    dv_ref,
    put_sums,
    dq_t,
    dk_sum,
    dv_sum,
):
    key_rows = k_ref.shape[0]
    q_t = transposed(q_ref[...])
    k_t = transposed(k_ref[...])
    do_t = transposed(do_ref[...])
    values = v_ref[...]
    keys = [masked_keys(k_ref[...], length, head) for head in range(2)]
    queries = [own_head(q_t, head, 1.0) for head in range(2)]
    grads = [own_head(do_t, head, 0.0) for head in range(2)]
    count = q_ref.shape[0] // step
    units = [(head, b) for b in reversed(range(count)) for head in range(2)]

    def products_of(head, b):
        columns = slice(b * step, b * step + step)
        end = b * step + step if causal else key_rows
        scores = product(keys[head][:end], queries[head][:, columns])
        return scores, product(values[:end], grads[head][:, columns])

    ahead = products_of(*units[0])
    for index, (head, b) in enumerate(units):
        scores, d_probs = ahead
        if index + 1 < len(units):
            ahead = products_of(*units[index + 1])
        rows = slice(64 * head, 64 * head + 64)
        columns = slice(b * step, b * step + step)
        end = scores.shape[0]
        if causal:
            scores = causal_mask(scores, step)
        probs = jnp.exp(scores - lse_ref[0, head : head + 1, columns])
        weighted = probs * d_probs
        delta = jnp.sum(weighted, axis=0, keepdims=True)
        d_scores = (weighted - probs * delta).astype(jnp.bfloat16)
        dv = product(probs.astype(jnp.bfloat16), do_ref[columns, :])
        dk = product(d_scores, q_ref[columns, :])
        if b == count - 1:
            dv_sum[head, :end] = dv
            dk_sum[head, :end] = dk
        else:
            dv_sum[head, :end] += dv
            dk_sum[head, :end] += dk
        dq_t[rows, columns] = product(k_t[rows, :end], d_scores)
    first = half_lanes((key_rows, 128), 1) < 64
    dk_ref[...] = jnp.where(first, dk_sum[0, :key_rows], dk_sum[1, :key_rows]).astype(jnp.bfloat16)
    dv = jnp.where(first, dv_sum[0, :key_rows], dv_sum[1, :key_rows]).astype(jnp.bfloat16)
    dv_ref[...] = dv
    dq = (dq_t[...] * 0.125).T.astype(jnp.bfloat16)
    dq_ref[...] = dq
    put_sums(
        jnp.sum(dq.astype(jnp.float32), axis=0, keepdims=True),
        jnp.sum(dv.astype(jnp.float32), axis=0, keepdims=True),
    )


SCALARS = pl.BlockSpec(memory_space=pltpu.SMEM)


def neighbours():
    rep = lax.axis_index("rep")
    z = lax.axis_index("shard")
    core = rep % 2
    x = (rep // 2) % 2
    y = rep // 4
    other_core = (rep + 1 - 2 * core, z)
    other_x = (rep + 2 - 4 * x, z)
    other_y = (rep + 4 - 8 * y, z)
    others_z = [(rep, (z + d) % 4) for d in (1, 2, 3)]
    return core, x, y, z, other_core, other_x, other_y, others_z


def greet(devices):
    barrier = pltpu.get_barrier_semaphore()
    for device in devices:
        pl.semaphore_signal(barrier, inc=1, device_id=device, device_id_type=MESH)
    pl.semaphore_wait(barrier, len(devices))


def remote(src, dst, send, recv, device):
    return pltpu.make_async_remote_copy(
        src_ref=src, dst_ref=dst, send_sem=send, recv_sem=recv, device_id=device, device_id_type=MESH
    )


def gather_copies(refs, c, parity, places):
    piece, full, place_sem, z_send, z_recv, send, recv = refs
    core, x, y, z, other_core, other_x, other_y, others_z = places
    a = x + parity * (y - x)
    b = y + parity * (x - y)
    first = (other_x[0] + parity * (other_y[0] - other_x[0]), z)
    second = (other_y[0] + parity * (other_x[0] - other_y[0]), z)
    own = pl.ds(pl.multiple_of(core * 128 + a * 64 + b * 32, 32), 32)
    steps = (
        (own, second),
        (pl.ds(pl.multiple_of(core * 128 + a * 64, 64), 64), first),
        (pl.ds(pl.multiple_of(core * 128, 128), 128), other_core),
    )

    def local():
        return pltpu.make_async_copy(piece.at[c], full.at[c, z, own, :], place_sem.at[c])

    def line(d):
        return remote(
            piece.at[c], full.at[c, z, own, :], z_send.at[c, d], z_recv.at[c, d], others_z[d]
        )

    def pair(k):
        block = full.at[c, :, steps[k][0], :]
        return remote(block, block, send.at[k, c], recv.at[k, c], steps[k][1])

    return local, line, pair


def gather_stage(k, refs, c, parity, places):
    local, line, pair = gather_copies(refs, c, parity, places)
    if k == 0:
        local().start()
        for d in range(3):
            line(d).start()
    if k == 1:
        local().wait()
        for d in range(3):
            line(d).wait_recv()
        pair(0).start()
    if k == 2 or k == 3:
        pair(k - 2).wait_recv()
        pair(k - 1).start()
    if k == 4:
        pair(2).wait()
        pair(1).wait_send()
        pair(0).wait_send()
        for d in range(3):
            line(d).wait_send()


def gather_sems(count):
    dma = pltpu.SemaphoreType.DMA
    return [dma((count,)), dma((count, 3)), dma((count, 3)), dma((3, count)), dma((3, count))]


def hidden_blocks(values):
    split = values.reshape(values.shape[:-1] + (4, 4, 256))
    split = jnp.swapaxes(split, -3, -2)
    return split.reshape(values.shape[:-1] + (4, 1024))


def hidden_flat(blocks):
    split = blocks.reshape(blocks.shape[:-2] + (4, 4, 256))
    split = jnp.swapaxes(split, -3, -2)
    return split.reshape(blocks.shape[:-2] + (FF,))


def fold(tile):
    return jnp.sum(tile.reshape(-1, 8, tile.shape[-1]), axis=0)


GATHER_PLAN = (("z", 7.5), ("second", 7.5), ("first", 13.0), ("core", 4.0), (None, 0.0))


class GatherPlanner:
    def __init__(self, count):
        self.now = 0.0
        self.links = {"core": 0.0, "x": 0.0, "y": 0.0, "z": 0.0}
        self.stage = {c: 0 for c in range(count)}
        self.ready = {c: 0.0 for c in range(count)}
        self.opened = count

    def can(self, c):
        if self.stage[c] == 0 and c >= 3 and self.stage[c - 3] < 2:
            return False
        return self.stage[c] < 5

    def spend(self, now, **busy):
        self.now = max(self.now, now)
        for link, span in busy.items():
            self.links[link] = max(self.links[link], self.now) + span

    def emit(self, c):
        stage = self.stage[c]
        link, span = GATHER_PLAN[stage]
        first, second = ("x", "y") if c % 2 == 0 else ("y", "x")
        link = {"first": first, "second": second}.get(link, link)
        self.now = max(self.now, self.ready[c]) + 0.1
        if link is not None:
            begin = max(self.now, self.links[link])
            self.links[link] = begin + span - 1.0
            self.ready[c] = begin + span
        self.stage[c] = stage + 1
        return (stage, c)

    def tick(self, spent):
        self.now += spent
        events = []
        progress = True
        while progress:
            progress = False
            for c in range(self.opened):
                if self.can(c) and self.ready[c] <= self.now:
                    events.append(self.emit(c))
                    progress = True
        return events

    def until(self, c):
        events = []
        while self.stage[c] < 5:
            choices = [i for i in range(self.opened) if self.can(i)]
            best = min(choices, key=lambda i: (self.ready[i], i))
            events.append(self.emit(best))
        return events


ERFC_SERIES = (
    0.08459648489952087,
    0.085321806371212,
    0.0743890032172203,
    0.10671534389257431,
    -0.04577348381280899,
    0.27184805274009705,
    -0.2545455992221832,
    0.24207571148872375,
    -0.06462734192609787,
)


def gelu_parts(u):
    bell = jnp.exp(-0.5 * u * u)
    t = 1.0 / (1.0 + (0.3 * math.sqrt(0.5)) * jnp.abs(u))
    series = ERFC_SERIES[8]
    for coefficient in ERFC_SERIES[7::-1]:
        series = series * t + coefficient
    tail = series * t * bell
    share = jnp.where(u < 0.0, tail, 1.0 - tail)
    return u * share, share + u * (bell * (1.0 / math.sqrt(2.0 * math.pi)))


def norm_parts(values):
    centred = values - jnp.mean(values, axis=1, keepdims=True)
    spread = jnp.mean(centred * centred, axis=1, keepdims=True)
    scale = lax.rsqrt(spread + NORM_EPS)
    return centred * scale, scale


def forward_kernel(
    order_ref,
    lengths_ref,
    state_lengths_ref,
    tokens_ref,
    att_ref,
    exp_ref,
    shr_ref,
    e_ref,
    cot_ref,
    par,
    x_out,
    full_ref,
    q_out,
    k_out,
    v_out,
    o_out,
    lse_out,
    cq_out,
    ck_out,
    cv_out,
    oc_out,
    lse_cross_out,
    r1_out,
    r2_out,
    h1_out,
    h2_out,
    g_out,
    gp_out,
    y_out,
    dm_out,
    d_third_out,
    small_out,
    pool,
    acc,
    held,
    o_t,
    lse_held,
    states,
    x_held,
    spread,
    picked,
    piece_ref,
    att_in,
    exp_in,
    shr_in,
    prepare_sem,
    load_sem,
    store_sem,
    state_sem,
    acc_sem,
    spread_send,
    spread_recv,
    back_send,
    back_recv,
    *gather_sem,
):
    places = neighbours()
    refs = (piece_ref, full_ref) + gather_sem
    planner = GatherPlanner(GATHERED)
    me = lax.axis_index("rep") * 4 + places[3]
    length = lengths_ref[me]

    core, x, y = places[0:3]

    def own_row(parity):
        a = x + parity * (y - x)
        b = y + parity * (x - y)
        return core * 128 + a * 64 + b * 32

    prepare = []
    for p in range(2):
        for lane in range(8):
            rows = pl.ds(pl.multiple_of(own_row(p) * 8, 256), 256)
            prepare.append((att_ref.at[rows, pl.ds(lane * 128, 128)], att_in.at[p, lane]))
        rows = pl.ds(pl.multiple_of(own_row(p), 32), 32)
        prepare.append((exp_ref.at[rows, :], exp_in.at[p]))
    for j in range(4):
        rows = pl.ds(pl.multiple_of(j * 256 + own_row(SHRINK_AT[j] % 2), 32), 32)
        prepare.append((shr_ref.at[rows, :], shr_in.at[j]))
    prepare = [
        pltpu.make_async_copy(source, target, prepare_sem.at[i])
        for i, (source, target) in enumerate(prepare)
    ]

    def make_pieces():
        for copy in prepare:
            copy.wait()
        for c in range(8):
            for lane in range(8):
                tile = att_in[c % 2, lane, pl.ds(c, 32, stride=8), :]
                piece_ref[c, :, lane * 128 : lane * 128 + 128] = tile.astype(jnp.bfloat16)
        for j in range(4):
            c = EXPAND_AT[j]
            for s in range(4):
                start = s * 1024 + j * 256
                tile = exp_in[c % 2, :, start : start + 256]
                piece_ref[c, :, s * 256 : s * 256 + 256] = tile.astype(jnp.bfloat16)
            piece_ref[SHRINK_AT[j]] = shr_in[j].astype(jnp.bfloat16)

    def device(offset):
        j = lax.rem(me + offset, 32)
        return j, (j // 4, j % 4)

    def spread_copy(offset):
        j, target = device(offset)
        return remote(
            tokens_ref.at[j],
            spread.at[me],
            spread_send.at[offset],
            spread_recv.at[offset],
            target,
        )

    def back_copy(offset):
        return remote(
            picked.at[offset],
            x_held.at[me],
            back_send.at[offset],
            back_recv.at[offset],
            device(offset)[1],
        )

    def own_spread():
        return pltpu.make_async_copy(tokens_ref.at[me], spread.at[me], spread_recv.at[0])

    def own_back():
        return pltpu.make_async_copy(picked.at[0], x_held.at[me], back_recv.at[0])

    def each_other(act):
        def body(offset, carry):
            act(offset)
            return carry

        lax.fori_loop(1, 32, body, 0)

    def turn_back():
        own_spread().wait()
        each_other(lambda offset: spread_copy(offset).wait())
        picked[0] = spread[order_ref[me]]
        own_back().start()

        def pick(offset):
            picked[offset] = spread[order_ref[device(offset)[0]]]
            back_copy(offset).start()

        each_other(pick)

    def emit_all(events):
        for stage, c in events:
            gather_stage(stage, refs, c, c % 2, places)

    def tick(spent):
        emit_all(planner.tick(spent))

    def load(slot, source):
        return pltpu.make_async_copy(source, pool.at[slot], load_sem.at[slot])

    def store(slot, target):
        return pltpu.make_async_copy(pool.at[slot], target, store_sem.at[slot])

    def product_into(left, right, put):
        def body(i, carry):
            n = pl.multiple_of(i * 256, 256)
            put(n, product(left(), pool[right, :, pl.ds(n, 256)]))
            return carry

        lax.fori_loop(0, 4, body, 0)

    def row(index, n):
        return par[index : index + 1, pl.ds(n, 256)]

    def put_low(slot, offset=None, scale=None):
        def put(n, value):
            if offset is not None:
                value = value + row(offset, n)
            if scale is not None:
                value = value * scale
            pool[slot, :, pl.ds(n, 256)] = value.astype(jnp.bfloat16)

        return put

    def put_acc(offset):
        def put(n, value):
            acc[:, pl.ds(n, 256)] = value + row(offset, n)

        return put

    def load_weight(c, slot):
        target = pool.at[slot].reshape(4, 256, D)
        return pltpu.make_async_copy(full_ref.at[c], target, load_sem.at[slot])

    def weight(c, slot):
        emit_all(planner.until(c))
        return load_weight(c, slot)

    def attend_loop(causal, step, valid, query, key, value, out, spent, rows, key_rows):
        ahead = [planner.tick(spent) for _ in range(8)]
        first_row, count = rows

        def body(i, carry):
            lanes = pl.ds(pl.multiple_of(i * 128, 128), 128)
            attend_pair(
                causal,
                step,
                valid,
                query.at[pl.ds(first_row, count), lanes],
                key.at[pl.ds(0, key_rows), lanes],
                value.at[pl.ds(0, key_rows), lanes],
                out.at[pl.ds(first_row, count), lanes],
                lse_held.at[pl.ds(i, 1)],
                o_t,
                first_row,
            )
            for n in range(8):
                if ahead[n]:

                    @pl.when(i == n)
                    def _(events=ahead[n]):
                        emit_all(events)

            return carry

        lax.fori_loop(0, 8, body, 0)

    TILE = 128

    def over_rows(sums, body):
        zero = jnp.zeros((8, D), jnp.float32)

        def step(i, carry):
            r = pl.multiple_of(i * TILE, TILE)
            place = half_lanes((TILE, 1), 0) + r
            usable = (place < length).astype(jnp.float32)
            terms = body(pl.ds(r, TILE), usable)
            return tuple(c + fold(t) for c, t in zip(carry, terms))

        totals = lax.fori_loop(0, D // TILE, step, (zero,) * sums)
        return [jnp.sum(t, axis=0, keepdims=True) for t in totals]

    lane = half_lanes((1, D), 1)

    def square_at(index, total):
        small_out[17:18, :] += jnp.where(lane == index, jnp.sum(total), 0.0)

    for copy in prepare:
        copy.start()
    barrier = pltpu.get_barrier_semaphore()

    def greet_one(offset):
        pl.semaphore_signal(barrier, inc=1, device_id=device(offset)[1], device_id_type=MESH)

    each_other(greet_one)
    pl.semaphore_wait(barrier, 31)
    own_spread().start()
    each_other(lambda offset: spread_copy(offset).start())
    make_pieces()
    planner.opened = 3
    tick(0.5)
    planner.spend(3.0, z=42.0, x=21.0, y=21.0)
    e_load = pltpu.make_async_copy(e_ref, states.at[2], state_sem.at[2])
    e_load.start()
    load(9, cot_ref).start()
    small_out[...] = jnp.zeros_like(small_out)
    turn_back()
    planner.spend(56.0, z=42.0, x=21.0, y=21.0)
    planner.opened = 6
    for i in range(3):
        weight(i, 1 + i).start()
    tick(20.0)
    tick(8.0)
    own_back().wait()
    each_other(lambda offset: back_copy(offset).wait())
    planner.spend(112.0)
    planner.opened = GATHERED
    tick(0.5)
    x_store = pltpu.make_async_copy(x_held, x_out, acc_sem.at[1])
    x_store.start()

    for i, (slot, offset, scale) in enumerate(((4, 0, 0.125), (5, None, None), (6, 1, None))):
        load_weight(i, 1 + i).wait()
        product_into(lambda: x_held[...].reshape(1024, D), 1 + i, put_low(slot, offset, scale))
        store(slot, (q_out, k_out, v_out)[i]).start()
        tick(2.5)
    refs_held = [pool.at[slot] for slot in (4, 5, 6, 7)]
    attend_loop(True, 256, length, *refs_held, 4.5, (0, 1024), 1024)
    store(7, o_out).start()
    lse_copy = pltpu.make_async_copy(lse_held, lse_out, state_sem.at[3])
    lse_copy.start()
    w_copy = weight(3, 1)
    w_copy.start()
    w_copy.wait()
    product_into(lambda: pool[7], 1, put_acc(2))
    tick(2.5)
    store(4, q_out).wait()

    def first_norm(rows, usable):
        held_rows = pl.ds(pl.multiple_of(rows.start // 32, TILE // 32), TILE // 32)
        x = x_held[held_rows].reshape(TILE, D).astype(jnp.float32)
        a = acc[rows, :]
        total = x + a
        acc[rows, :] = total
        h = norm_parts(total)[0] * par[11:12, :] + par[12:13, :]
        held[rows, :] = h
        pool[4, rows, :] = h.astype(jnp.bfloat16)
        return usable * x * x, usable * a * a, usable * h * h

    for index, total in enumerate(over_rows(3, first_norm)):
        square_at(index, total)
    store(4, h1_out).start()
    r1_copy = pltpu.make_async_copy(acc, r1_out, acc_sem.at[0])
    r1_copy.start()
    tick(4.0)

    for c, slot in ((4, 2), (5, 3), (6, 1)):
        weight(c, slot).start()
    store(5, k_out).wait()
    load_weight(4, 2).wait()
    product_into(lambda: pool[4], 2, put_low(5, 3, 0.125))
    store(5, cq_out).start()
    w_copy = weight(7, 2)
    w_copy.start()
    tick(2.5)
    e_load.wait()
    load_weight(5, 3).wait()
    load_weight(6, 1).wait()

    def put_keys(n, value):
        states[0, :, pl.ds(n, 256)] = value.astype(jnp.bfloat16)

    def put_values(n, value):
        states[1, :, pl.ds(n, 256)] = (value + row(4, n)).astype(jnp.bfloat16)

    product_into(lambda: states[2], 3, put_keys)
    product_into(lambda: states[2], 1, put_values)
    state_stores = [
        pltpu.make_async_copy(states.at[0], ck_out, state_sem.at[0]),
        pltpu.make_async_copy(states.at[1], cv_out, state_sem.at[1]),
    ]
    for copy in state_stores:
        copy.start()
    tick(1.0)
    store(6, v_out).wait()
    lse_copy.wait()
    attend_loop(
        False,
        512,
        state_lengths_ref[me],
        pool.at[5],
        states.at[0],
        states.at[1],
        pool.at[6],
        1.6,
        (0, 1024),
        128,
    )
    store(6, oc_out).start()
    lse_copy = pltpu.make_async_copy(lse_held, lse_cross_out, state_sem.at[3])
    lse_copy.start()
    w_copy.wait()
    r1_copy.wait()
    product_into(lambda: pool[6], 2, put_acc(5))
    tick(2.5)
    weight(EXPAND_AT[0], 0).start()
    store(7, o_out).wait()

    def second_norm(rows, usable):
        c = acc[rows, :]
        total = held[rows, :] + c
        acc[rows, :] = total
        h = norm_parts(total)[0] * par[13:14, :] + par[14:15, :]
        held[rows, :] = h
        pool[7, rows, :] = h.astype(jnp.bfloat16)
        return usable * c * c, usable * h * h

    for index, total in enumerate(over_rows(2, second_norm)):
        square_at(3 + index, total)
    store(7, h2_out).start()
    r2_copy = pltpu.make_async_copy(acc, r2_out, acc_sem.at[0])
    r2_copy.start()
    tick(4.0)

    store(4, h1_out).wait()
    store(5, cq_out).wait()
    g_slots, slope_slots = (4, 6), (5, 8)
    r2_copy.wait()
    store(6, oc_out).wait()
    for j in range(5):
        if j > 1:
            store(g_slots[j % 2], g_out.at[j - 2]).wait()
            store(slope_slots[j % 2], gp_out.at[j - 2]).wait()
        if j < 4:
            load_weight(EXPAND_AT[j], j % 2).wait()
        if j > 0:
            load_weight(SHRINK_AT[j - 1], 2 + (j - 1) % 2).wait()

        def body(i, carry, j=j):
            n = pl.multiple_of(i * 256, 256)
            here = pl.ds(n, 256)
            if j < 4:
                offset = par[pl.ds(6 + i, 1), j * 256 : j * 256 + 256]
                u = product(pool[7], pool[j % 2, :, here]) + offset
            if j > 0:
                more = product(pool[g_slots[(j - 1) % 2]], pool[2 + (j - 1) % 2, :, here])
                if j == 1:
                    acc[:, here] = more + row(10, n)
                else:
                    acc[:, here] += more
            if j < 4:
                g, slope = gelu_parts(u)
                pool[g_slots[j % 2], :, here] = g.astype(jnp.bfloat16)
                pool[slope_slots[j % 2], :, here] = slope.astype(jnp.bfloat16)
            return carry

        ahead = [planner.tick(2.2 if j < 4 else 0.6) for _ in range(4)]

        def body_and_stages(i, carry, body=body, ahead=ahead):
            body(i, carry)
            for n in range(4):
                if ahead[n]:

                    @pl.when(i == n)
                    def _(events=ahead[n]):
                        emit_all(events)

            return carry

        lax.fori_loop(0, 4, body_and_stages, 0)
        if j < 4:
            store(g_slots[j % 2], g_out.at[j]).start()
            store(slope_slots[j % 2], gp_out.at[j]).start()
        if j < 3:
            weight(EXPAND_AT[j + 1], (j + 1) % 2).start()
        if j < 4:
            weight(SHRINK_AT[j], 2 + j % 2).start()

    load(9, cot_ref).wait()

    def third_norm(rows, usable):
        m = acc[rows, :]
        unit, scale = norm_parts(held[rows, :] + m)
        gain = par[15:16, :]
        pool[0, rows, :] = (unit * gain + par[16:17, :]).astype(jnp.bfloat16)
        grad = pool[9, rows, :].astype(jnp.float32) * usable
        inner = grad * gain
        first = jnp.mean(inner, axis=1, keepdims=True)
        second = jnp.mean(inner * unit, axis=1, keepdims=True)
        back = scale * (inner - first - unit * second)
        acc[rows, :] = back
        low = back.astype(jnp.bfloat16)
        pool[1, rows, :] = low
        return usable * m * m, grad * unit, grad, low.astype(jnp.float32)

    m_total, gain_sum, shift_sum, offset_sum = over_rows(4, third_norm)
    square_at(5, m_total)
    small_out[15:16, :] = gain_sum
    small_out[16:17, :] = shift_sum
    small_out[10:11, :] = offset_sum
    last = [
        store(0, y_out),
        store(1, dm_out),
        pltpu.make_async_copy(acc, d_third_out, acc_sem.at[0]),
    ]
    for copy in last:
        copy.start()
    for c in range(GATHERED):
        emit_all(planner.until(c))
    for copy in last + state_stores + [lse_copy, x_store]:
        copy.wait()
    store(7, h2_out).wait()
    store(6, g_out.at[3]).wait()
    store(8, gp_out.at[3]).wait()


def forward(scalars, tokens, weights, states, cotangent, params):
    any_space = pl.BlockSpec(memory_space=pl.ANY)
    vmem = pl.BlockSpec(memory_space=pltpu.VMEM)
    shape = jax.ShapeDtypeStruct
    dma = pltpu.SemaphoreType.DMA
    low = jnp.bfloat16
    wide = jnp.float32
    square = shape((1024, D), low)
    square_wide = shape((1024, D), wide)
    lse = shape((8, 8, 1024), wide)
    short = shape((128, D), low)
    blocks = shape((4, 1024, D), low)
    outs = (
        shape((32, 32, D), low),
        shape((GATHERED, 4, 256, D), low),
        square,
        square,
        square,
        square,
        lse,
        square,
        short,
        short,
        square,
        lse,
        square_wide,
        square_wide,
        square,
        square,
        blocks,
        blocks,
        square,
        square,
        square_wide,
        shape((24, D), wide),
    )
    return pl.pallas_call(
        forward_kernel,
        out_shape=outs,
        in_specs=[SCALARS] * 3 + [any_space] * 6 + [vmem],
        out_specs=(any_space,) * 21 + (vmem,),
        scratch_shapes=[
            pltpu.VMEM((10, 1024, D), low),
            pltpu.VMEM((1024, D), wide),
            pltpu.VMEM((1024, D), wide),
            pltpu.VMEM((128, 1024), wide),
            pltpu.VMEM((8, 8, 1024), wide),
            pltpu.VMEM((3, 128, D), low),
            pltpu.VMEM((32, 32, D), low),
            pltpu.VMEM((32, 32, D), low),
            pltpu.VMEM((32, 32, D), low),
            pltpu.VMEM((GATHERED, 32, D), low),
            pltpu.VMEM((2, 8, 256, 128), wide),
            pltpu.VMEM((2, 32, FF), wide),
            pltpu.VMEM((4, 32, D), wide),
            dma((22,)),
            dma((10,)),
            dma((10,)),
            dma((4,)),
            dma((2,)),
            dma((32,)),
            dma((32,)),
            dma((32,)),
            dma((32,)),
        ]
        + gather_sems(GATHERED),
        compiler_params=pltpu.CompilerParams(
            collective_id=3, has_side_effects=True, vmem_limit_bytes=62 * MIB
        ),
    )(*scalars, tokens.reshape(32, 32, D), *weights, states, cotangent, params)


def add_blocks(target, first, second, planes, rows, step):
    per_plane = rows // step

    def body(i, carry):
        s = i // per_plane
        r = pl.multiple_of((i % per_plane) * step, step)
        target(s, r, first(s, r) + second(s, r))
        return carry

    lax.fori_loop(0, planes * per_plane, body, 0)


POOL = 8
G_SLOTS = 3
R_SLOTS = 4
PLAN = {"core": 3.5, "load": 1.8, "a": 13.5, "b": 7.5, "z": 7.5, "bb": 3.0, "ba": 5.0, "bc": 2.5}


class Planner:
    def __init__(self):
        self.now = 0.0
        self.links = {"core": 0.0, "x": 0.0, "y": 0.0, "z": 0.0, "load": 0.0}
        self.stage = {}
        self.ready = {}

    def link_of(self, c, stage):
        first, second = ("x", "y") if c % 2 == 0 else ("y", "x")
        return {
            0: ("core", "core"),
            1: ("load", "load"),
            2: (first, "a"),
            3: (second, "b"),
            4: ("z", "z"),
            5: (second, "bb"),
            6: (first, "ba"),
            7: ("core", "bc"),
            8: (None, None),
        }[stage]

    def can(self, c):
        stage = self.stage[c]
        if stage > 8:
            return False
        if stage == 1 and c >= R_SLOTS and self.stage[c - R_SLOTS] <= 3:
            return False
        return True

    def emit(self, c):
        stage = self.stage[c]
        link, kind = self.link_of(c, stage)
        self.now = max(self.now, self.ready[c]) + {2: 0.8, 3: 0.5, 4: 0.3, 5: 0.2}.get(stage, 0.1)
        if link is not None:
            begin = max(self.now, self.links[link])
            span = PLAN[kind]
            self.links[link] = begin + span - 1.0
            self.ready[c] = begin + span
        self.stage[c] = stage + 1
        return (stage, c)

    def tick(self, spent):
        self.now += spent
        events = []
        progress = True
        while progress:
            progress = False
            for c in sorted(self.stage):
                if self.can(c) and self.ready[c] <= self.now:
                    events.append(self.emit(c))
                    progress = True
        return events

    def produce(self, c):
        self.stage[c] = 0
        self.ready[c] = self.now
        return [self.emit(c)]

    def until(self, done):
        events = []
        while not done():
            choices = [c for c in sorted(self.stage) if self.can(c)]
            c = min(choices, key=lambda i: (self.ready[i], i))
            events.append(self.emit(c))
        return events

    def free_slot(self, c):
        before = c - G_SLOTS
        if before < 0:
            return []
        return self.until(lambda: self.stage[before] > 2)

    def drain(self, tasks, spent):
        events = []
        waiting = list(tasks)
        while waiting or any(s <= 8 for s in self.stage.values()):
            choices = [c for c in sorted(self.stage) if self.can(c)]
            best = min(choices, key=lambda i: (self.ready[i], i)) if choices else None
            open_tasks = [t for t in waiting if all(self.stage[c] > 8 for c in t[0])]
            if open_tasks and (best is None or self.ready[best] > self.now):
                task = open_tasks[0]
                waiting.remove(task)
                self.now += spent
                events.append(("task", task[1]))
            else:
                events.append(self.emit(best))
        return events


def backward_kernel(
    lengths_ref,
    state_lengths_ref,
    dm_ref,
    d_third_ref,
    g_ref,
    gp_ref,
    full_ref,
    h2_ref,
    h1_ref,
    x_in_ref,
    e_ref,
    oc_ref,
    o_ref,
    r1_ref,
    r2_ref,
    q_ref,
    k_ref,
    v_ref,
    cq_ref,
    ck_ref,
    cv_ref,
    lse_ref,
    lse_cross_ref,
    gains_ref,
    small_ref,
    rows_ref,
    cols_ref,
    token_grad_ref,
    state_grad_ref,
    out_ref,
    totals_ref,
    rows_out,
    cols_out,
    scale_out,
    half,
    pool,
    acc,
    made,
    summed,
    quarter,
    eighth,
    pieces,
    stream,
    dq_t,
    dk_sum,
    dv_sum,
    lse_held,
    states,
    states_t,
    small,
    small_in,
    small_sum,
    small_z,
    part,
    whole,
    load_sem,
    stream_sem,
    state_sem,
    half_sem,
    scan_sem,
    line_send_sem,
    line_recv_sem,
    send_sem,
    recv_sem,
    z_send_sem,
    z_recv_sem,
    place_sem,
    small_send_sem,
    small_recv_sem,
):
    core, x, y, z, other_core, other_x, other_y, others_z = neighbours()
    me = lax.axis_index("rep") * 4 + z
    kept = pl.multiple_of(core * 128, 128)
    given = pl.multiple_of(128 - core * 128, 128)
    planner = Planner()
    place_of = (12, 8, 13, 9, 14, 10, 15, 11, 7, 4, 5, 6, 3, 0, 1, 2)

    def axes(c):
        if c % 2 == 0:
            return x, y, other_x, other_y
        return y, x, other_y, other_x

    def core_copy(c):
        source = made.at[c % G_SLOTS, :, pl.ds(given, 128), :]
        return remote(source, half.at[c], send_sem.at[0, c], recv_sem.at[0, c], other_core)

    def half_copy(c):
        return pltpu.make_async_copy(
            half.at[c], summed.at[c % R_SLOTS], half_sem.at[c % R_SLOTS]
        )

    def first_copy(c):
        a, b, first, second = axes(c)
        rows = pl.ds(pl.multiple_of(64 - a * 64, 64), 64)
        source = summed.at[c % R_SLOTS, :, rows, :]
        return remote(source, quarter.at[c], send_sem.at[1, c], recv_sem.at[1, c], first)

    def second_copy(c):
        a, b, first, second = axes(c)
        rows = pl.ds(pl.multiple_of(32 - b * 32, 32), 32)
        source = quarter.at[c, :, rows, :]
        return remote(source, eighth.at[c], send_sem.at[2, c], recv_sem.at[2, c], second)

    def z_copy(c, d):
        device = others_z[d]
        return remote(
            eighth.at[c, device[1]],
            pieces.at[c, d],
            z_send_sem.at[c, d],
            z_recv_sem.at[c, d],
            device,
        )

    def own_rows_of(c):
        a, b, first, second = axes(c)
        return pl.ds(pl.multiple_of(core * 128 + a * 64 + b * 32, 32), 32)

    def place_copy(c):
        return pltpu.make_async_copy(
            pieces.at[c, 0], out_ref.at[place_of[c], own_rows_of(c), :], place_sem.at[c]
        )

    def back_second(c):
        device = axes(c)[3]
        target = out_ref.at[place_of[c], own_rows_of(c), :]
        return remote(pieces.at[c, 0], target, send_sem.at[3, c], recv_sem.at[3, c], device)

    def back_first(c):
        a, b, first, second = axes(c)
        block = out_ref.at[place_of[c], pl.ds(pl.multiple_of(core * 128 + a * 64, 64), 64), :]
        return remote(block, block, send_sem.at[4, c], recv_sem.at[4, c], first)

    def back_core(c):
        block = out_ref.at[place_of[c], pl.ds(kept, 128), :]
        return remote(block, block, send_sem.at[5, c], recv_sem.at[5, c], other_core)

    def emit(stage, c):
        a, b, first, second = axes(c)
        slot = c % R_SLOTS
        if stage == 0:
            core_copy(c).start()
        if stage == 1:
            if c >= R_SLOTS:
                first_copy(c - R_SLOTS).wait_send()
            core_copy(c).wait_recv()
            half_copy(c).start()
        if stage == 2:
            half_copy(c).wait()

            def put(s, r, value):
                summed[slot, s, pl.ds(r, 32), :] = value

            add_blocks(
                put,
                lambda s, r: summed[slot, s, pl.ds(r, 32), :],
                lambda s, r: made[c % G_SLOTS, s, pl.ds(pl.multiple_of(kept + r, 32), 32), :],
                4,
                128,
                32,
            )
            first_copy(c).start()
            core_copy(c).wait_send()
        if stage == 3:
            first_copy(c).wait_recv()

            def put(s, r, value):
                quarter[c, s, pl.ds(r, 32), :] = value

            add_blocks(
                put,
                lambda s, r: quarter[c, s, pl.ds(r, 32), :],
                lambda s, r: summed[slot, s, pl.ds(pl.multiple_of(a * 64 + r, 32), 32), :],
                4,
                64,
                32,
            )
            second_copy(c).start()
        if stage == 4:
            second_copy(c).wait_recv()

            def put(s, r, value):
                eighth[c, s, pl.ds(r, 32), :] = value

            add_blocks(
                put,
                lambda s, r: eighth[c, s, pl.ds(r, 32), :],
                lambda s, r: quarter[c, s, pl.ds(pl.multiple_of(b * 32 + r, 32), 32), :],
                4,
                32,
                32,
            )
            for d in range(3):
                z_copy(c, d).start()
        if stage == 5:
            for d in range(3):
                z_copy(c, d).wait_recv()
            total = eighth[c, z].astype(jnp.float32)
            for d in range(3):
                total = total + pieces[c, d].astype(jnp.float32)
            pieces[c, 0] = total.astype(jnp.bfloat16)
            back_second(c).start()
            place_copy(c).start()
        if stage == 6:
            place_copy(c).wait()
            back_second(c).wait_recv()
            back_first(c).start()
        if stage == 7:
            back_first(c).wait_recv()
            back_core(c).start()
        if stage == 8:
            back_core(c).wait()
            back_first(c).wait_send()
            back_second(c).wait_send()
            for d in range(3):
                z_copy(c, d).wait_send()
            second_copy(c).wait_send()
            if c >= CHUNKS - R_SLOTS:
                first_copy(c).wait_send()

    def emit_all(events):
        for stage, c in events:
            emit(stage, c)

    def tick(spent):
        emit_all(planner.tick(spent))

    def produced(c, spent):
        planner.now += spent
        emit_all(planner.produce(c))
        emit_all(planner.tick(0.0))

    def load(slot, source):
        return pltpu.make_async_copy(source, pool.at[slot], load_sem.at[slot])

    def state_load(index, source):
        return pltpu.make_async_copy(source, states.at[index], state_sem.at[index])

    def turn_tile(target, source):
        def turn(n):
            pool[target, pl.ds(n, 256), :] = pool[source, :, pl.ds(n, 256)].T

        return turn

    def transpose_into(target, source):
        turn = turn_tile(target, source)

        def body(i, carry):
            turn(pl.multiple_of(i * 256, 256))
            return carry

        lax.fori_loop(0, 4, body, 0)

    def product_nn(left, right, put, beside=None):
        def body(i, carry):
            n = pl.multiple_of(i * 256, 256)
            if beside is not None:
                beside(n)
            put(n, product(left(), right(n)))
            return carry

        lax.fori_loop(0, 4, body, 0)

    def product_nt(left, right, put, beside=None):
        def body(i, carry):
            n = pl.multiple_of(i * 256, 256)
            if beside is not None:
                beside(n)
            put(
                n,
                lax.dot_general(
                    left(),
                    right(n),
                    (((1,), (1,)), ((), ())),
                    preferred_element_type=jnp.float32,
                ),
            )
            return carry

        lax.fori_loop(0, 4, body, 0)

    def columns_of(slot):
        return lambda n: pool[slot, :, pl.ds(n, 256)]

    def rows_of(slot):
        return lambda n: pool[slot, pl.ds(n, 256), :]

    def weight_grad(slot_in_made, left, right, beside=None):
        def put(n, value):
            low = value.astype(jnp.bfloat16).reshape(4, 256, 256)
            made[slot_in_made, :, :, pl.ds(n, 256)] = low

        product_nn(left, right, put, beside)

    def add_to_acc(n, value):
        acc[:, pl.ds(n, 256)] += value

    def put_in(slot):
        def put(n, value):
            pool[slot, :, pl.ds(n, 256)] = value.astype(jnp.bfloat16)

        return put

    def norm_back(source, gain_row, gain_at, shift_at, offset_at, target):
        tiles = 8
        rows = 1024 // tiles

        def fetch(i):
            place = pl.ds(pl.multiple_of(i * rows, rows), rows)
            return pltpu.make_async_copy(
                source.at[place, :], stream.at[i % 2], stream_sem.at[i % 2]
            )

        fetch(0).start()

        def body(i, carry):
            gain_sum, shift_sum, offset_sum = carry

            @pl.when(i + 1 < tiles)
            def _():
                fetch(i + 1).start()

            fetch(i).wait()
            r = pl.multiple_of(i * rows, rows)
            values = stream[i % 2]
            centred = values - jnp.mean(values, axis=1, keepdims=True)
            spread = jnp.mean(centred * centred, axis=1, keepdims=True)
            scale = lax.rsqrt(spread + NORM_EPS)
            unit = centred * scale
            grad = acc[pl.ds(r, rows), :]
            inner = grad * gains_ref[gain_row : gain_row + 1, :]
            first = jnp.mean(inner, axis=1, keepdims=True)
            second = jnp.mean(inner * unit, axis=1, keepdims=True)
            back = scale * (inner - first - unit * second)
            acc[pl.ds(r, rows), :] = back
            low = back.astype(jnp.bfloat16)
            pool[target, pl.ds(r, rows), :] = low
            return (
                gain_sum + fold(grad * unit),
                shift_sum + fold(grad),
                offset_sum + fold(low.astype(jnp.float32)),
            )

        zero = jnp.zeros((8, D), jnp.float32)
        sums = lax.fori_loop(0, tiles, body, (zero, zero, zero))
        for row, value in zip((gain_at, shift_at, offset_at), sums):
            small[row : row + 1, :] = jnp.sum(value, axis=0, keepdims=True)

    greet([other_core, other_x, other_y] + others_z)
    load(0, dm_ref).start()
    load(6, h2_ref).start()
    load(2, full_ref.at[SHRINK_AT[0]]).start()
    load(3, gp_ref.at[0]).start()
    load(4, g_ref.at[0]).start()
    load(5, full_ref.at[EXPAND_AT[0]]).start()
    acc_load = pltpu.make_async_copy(d_third_ref, acc, place_sem.at[0])
    acc_load.start()
    small[...] = small_ref[...]
    load(6, h2_ref).wait()
    transpose_into(1, 6)
    load(0, dm_ref).wait()
    acc_load.wait()

    planner.now = 4.0
    plan = []
    for j in range(4):
        entry = []
        planner.now += 3.5
        entry.append(planner.tick(0.0) + planner.free_slot(2 * j))
        planner.now += 2.5
        entry.append(planner.produce(2 * j) + planner.tick(0.0) + planner.free_slot(2 * j + 1))
        planner.now += 2.5
        entry.append(planner.produce(2 * j + 1) + planner.tick(0.0))
        entry.append(planner.tick(2.5))
        plan.append(entry)

    def emit_planned(j, place):
        for n in range(4):
            events = plan[n][place]
            if events:

                @pl.when(j == n)
                def _(events=events):
                    emit_all(events)

    def block(j, carry):
        last = j == 3
        load(2, full_ref.at[SHRINK_AT[0]]).wait()
        load(3, gp_ref.at[0]).wait()

        def put_pre(n, value):
            low = (value * pool[3, :, pl.ds(n, 256)].astype(jnp.float32)).astype(jnp.bfloat16)
            pool[7, :, pl.ds(n, 256)] = low
            small[pl.ds(6 + n // 256, 1), pl.ds(pl.multiple_of(j * 256, 256), 256)] = jnp.sum(
                low.astype(jnp.float32), axis=0, keepdims=True
            )

        load(4, g_ref.at[0]).wait()
        product_nt(lambda: pool[0], rows_of(2), put_pre, turn_tile(6, 4))

        @pl.when(jnp.logical_not(last))
        def _():
            load(2, full_ref.at[SHRINK_AT[0] + 2 * (j + 1) - (j + 1) // 3]).start()
            load(3, gp_ref.at[j + 1]).start()

        @pl.when(last)
        def _():
            load(2, full_ref.at[7]).start()
            load(3, cq_ref).start()

        emit_planned(j, 0)

        @pl.when(jnp.logical_not(last))
        def _():
            load(4, g_ref.at[j + 1]).start()

        @pl.when(last)
        def _():
            load(4, oc_ref).start()

        weight_grad((2 * j) % G_SLOTS, lambda: pool[6], columns_of(0))
        emit_planned(j, 1)
        weight_grad((2 * j + 1) % G_SLOTS, lambda: pool[1], columns_of(7))
        emit_planned(j, 2)
        load(5, full_ref.at[EXPAND_AT[0]]).wait()
        product_nt(lambda: pool[7], rows_of(5), add_to_acc)

        @pl.when(jnp.logical_not(last))
        def _():
            load(5, full_ref.at[EXPAND_AT[1] + 2 * j]).start()

        @pl.when(last)
        def _():
            load(5, full_ref.at[4]).start()

        emit_planned(j, 3)
        return carry

    lax.fori_loop(0, 4, block, 0)

    load(7, h1_ref).start()
    state_loads = [state_load(0, ck_ref), state_load(1, cv_ref), state_load(2, e_ref)]
    for copy in state_loads:
        copy.start()
    lse_load = pltpu.make_async_copy(lse_cross_ref, lse_held, state_sem.at[3])
    lse_load.start()
    norm_back(r2_ref, 13, 13, 14, 5, 0)
    tick(4.0)
    load(4, oc_ref).wait()
    load(2, full_ref.at[7]).wait()
    product_nt(lambda: pool[0], rows_of(2), put_in(4), turn_tile(6, 4))
    load(2, full_ref.at[3]).start()
    tick(2.5)
    emit_all(planner.free_slot(8))
    load(7, h1_ref).wait()
    weight_grad(8 % G_SLOTS, lambda: pool[6], columns_of(0), turn_tile(1, 7))
    load(6, o_ref).start()
    load(7, full_ref.at[5]).start()
    produced(8, 2.5)
    load(3, cq_ref).wait()
    for copy in state_loads:
        copy.wait()
    lse_load.wait()

    def attend_loop(causal, step, length, query, key, value, grad, rows, spent, span=(0, 8)):
        ahead = {n: planner.tick(spent) for n in range(*span)}

        def body(i, carry):
            lanes = pl.ds(pl.multiple_of(i * 128, 128), 128)

            def sums(dq, dv):
                small[rows[0] : rows[0] + 1, lanes] = dq
                small[rows[1] : rows[1] + 1, lanes] = dv

            attend_back_pair(
                causal,
                step,
                length,
                query.at[:, lanes],
                key.at[:, lanes],
                value.at[:, lanes],
                grad.at[:, lanes],
                lse_held.at[pl.ds(i, 1)],
                query.at[:, lanes],
                key.at[:, lanes],
                value.at[:, lanes],
                sums,
                dq_t,
                dk_sum,
                dv_sum,
            )
            for n in range(*span):
                if ahead[n]:

                    @pl.when(i == n)
                    def _(events=ahead[n]):
                        emit_all(events)

            return carry

        lax.fori_loop(*span, body, 0)

    attend_loop(
        False,
        512,
        state_lengths_ref[me],
        pool.at[3],
        states.at[0],
        states.at[1],
        pool.at[4],
        (3, 4),
        2.0,
    )
    lse_load = pltpu.make_async_copy(lse_ref, lse_held, state_sem.at[3])
    lse_load.start()
    emit_all(planner.free_slot(9))
    weight_grad(9 % G_SLOTS, lambda: pool[1], columns_of(3))
    produced(9, 2.5)
    load(5, full_ref.at[4]).wait()
    load(6, o_ref).wait()
    product_nt(lambda: pool[3], rows_of(5), add_to_acc, turn_tile(1, 6))
    load(6, x_in_ref).start()
    load(5, full_ref.at[6]).start()
    load(3, q_ref).start()
    tick(2.5)
    states_t[...] = states[2].T
    for c, index in ((10, 0), (11, 1)):
        emit_all(planner.free_slot(c))
        weight_grad(
            c % G_SLOTS, lambda: states_t[...], lambda n, i=index: states[i, :, pl.ds(n, 256)]
        )
        produced(c, 1.0)
    load(7, full_ref.at[5]).wait()
    load(5, full_ref.at[6]).wait()

    def state_part(n):
        dims = (((1,), (1,)), ((), ()))
        return lax.dot_general(
            states[0], pool[7, pl.ds(n, 256), :], dims, preferred_element_type=jnp.float32
        ) + lax.dot_general(
            states[1], pool[5, pl.ds(n, 256), :], dims, preferred_element_type=jnp.float32
        )

    def put_state(i, carry):
        n = pl.multiple_of(i * 256, 256)
        state_grad_ref[:, pl.ds(n, 256)] = state_part(n).astype(jnp.bfloat16)
        return carry

    lax.fori_loop(0, 4, put_state, 0)
    load(5, k_ref).start()
    load(7, v_ref).start()
    tick(1.0)

    norm_back(r1_ref, 11, 11, 12, 2, 0)
    tick(4.0)
    emit_all(planner.free_slot(12))
    weight_grad(12 % G_SLOTS, lambda: pool[1], columns_of(0))
    produced(12, 2.5)
    load(2, full_ref.at[3]).wait()
    load(6, x_in_ref).wait()
    product_nt(lambda: pool[0], rows_of(2), put_in(4), turn_tile(1, 6))
    load(0, full_ref.at[0]).start()
    load(2, full_ref.at[1]).start()
    load(6, full_ref.at[2]).start()
    tick(2.5)
    load(3, q_ref).wait()
    load(5, k_ref).wait()
    load(7, v_ref).wait()
    lse_load.wait()
    def self_heads(span):
        refs = [pool.at[slot] for slot in (3, 5, 7, 4)]
        attend_loop(True, 256, lengths_ref[me], *refs, (0, 1), 5.0, span)

    def query_key_grad(c, half_of):
        def put(i, carry):
            n = pl.multiple_of((i % 2) * 256 + 512 * half_of, 256)
            value = product(pool[1], pool[3 + 2 * (i // 2), :, pl.ds(n, 256)])
            low = value.astype(jnp.bfloat16).reshape(4, 256, 256)
            made[c % G_SLOTS, :, :, pl.ds(pl.multiple_of(i * 256, 256), 256)] = low
            return carry

        emit_all(planner.free_slot(c))
        lax.fori_loop(0, 4, put, 0)
        produced(c, 2.5)

    self_heads((0, 4))
    query_key_grad(13, 0)
    self_heads((4, 8))

    def small_copy(k):
        source = small if k == 0 else small_sum.at[k - 1]
        device = (other_core, other_x, other_y)[k]
        return remote(source, small_in.at[k], small_send_sem.at[k], small_recv_sem.at[k], device)

    def small_z_copy(d):
        return remote(
            small_sum.at[2],
            small_z.at[z],
            small_send_sem.at[3 + d],
            small_recv_sem.at[3 + d],
            others_z[d],
        )

    def small_step(k):
        small_copy(k).wait()
        before = small[...] if k == 0 else small_sum[k - 1]
        small_sum[k] = before + small_in[k]
        if k < 2:
            small_copy(k + 1).start()
        else:
            small_z[z] = small_sum[2]
            for d in range(3):
                small_z_copy(d).start()

    small_copy(0).start()
    emit_all(planner.free_slot(14))
    weight_grad(14 % G_SLOTS, lambda: pool[1], columns_of(7))
    produced(14, 2.5)
    small_step(0)
    query_key_grad(15, 1)
    small_step(1)
    load(0, full_ref.at[0]).wait()
    product_nt(lambda: pool[3], rows_of(0), add_to_acc)
    tick(2.5)
    small_step(2)
    load(2, full_ref.at[1]).wait()
    product_nt(lambda: pool[5], rows_of(2), add_to_acc)
    tick(2.5)
    for d in range(3):
        small_z_copy(d).wait()
    totals_ref[...] = (small_z[0] + small_z[1]) + (small_z[2] + small_z[3])
    load(6, full_ref.at[2]).wait()

    def put_input(n, value):
        total = acc[:, pl.ds(n, 256)] + value
        pool[4, :, pl.ds(n, 256)] = total.astype(jnp.bfloat16)

    product_nt(lambda: pool[7], rows_of(6), put_input)
    token_copy = pltpu.make_async_copy(pool.at[4], token_grad_ref, load_sem.at[4])
    token_copy.start()
    tick(2.5)

    part[...] = jnp.zeros_like(part)

    def spot(place):
        return (0, 1, 2, 6)[place // 4], (place % 4) * 256

    def scan_load(place):
        slot, row = spot(place)
        return pltpu.make_async_copy(
            out_ref.at[place], pool.at[slot, pl.ds(row, 256), :], scan_sem.at[place]
        )

    scans = {}
    for i in range(2):
        scans[i] = ([(0, 512 * i, 512, i, 0), (2, 512 * i, 512, i, 512)], i, (13, 128 * i))
    for i in range(2, 8):
        scans[i] = ([(1 if i == 2 else i, 0, D, i, 0)], i, (13, 128 * i))
    scans[8] = ([(8 + i, 0, D, 8 + i, 0) for i in range(4)], 8, (14, 0))
    for i in range(4):
        scans[9 + i] = ([(12 + i, 0, D, 12, 0)], 9 + i, (14, 128))

    def scan(name):
        sources, row_lane, (total_row, total_lane) = scans[name]
        width = float(sum(source[2] for source in sources))
        step = 64 if name == 8 else 256

        def body(i, carry):
            cols, weights, total = carry
            r = pl.multiple_of(i * step, step)
            squares = []
            for place, lane, lanes, _, _ in sources:
                slot, row = spot(place)
                tile = pool[slot, pl.ds(row + r, step), lane : lane + lanes]
                squares.append(jnp.square(tile.astype(jnp.float32)))
            row_sum = sum(jnp.sum(square, axis=1, keepdims=True) for square in squares)
            rows = DECAY_RATE * rows_ref[pl.ds(r, step), row_lane : row_lane + 1] + (
                1.0 - DECAY_RATE
            ) * (row_sum / width + FACTOR_EPS)
            rows_out[pl.ds(r, step), row_lane : row_lane + 1] = rows
            inverse = 1.0 / rows
            cols = [c + fold(s) for c, s in zip(cols, squares)]
            weights = [w + fold(s * inverse) for w, s in zip(weights, squares)]
            return cols, weights, total + fold(rows)

        zeros = [jnp.zeros((8, source[2]), jnp.float32) for source in sources]
        cols, weights, total = lax.fori_loop(
            0, 256 // step, body, (zeros, zeros, jnp.zeros((8, 1), jnp.float32))
        )
        for (_, _, lanes, slot, lane), col, weighted in zip(sources, cols, weights):
            here = slice(lane, lane + lanes)
            part[slot : slot + 1, here] += jnp.sum(col, axis=0, keepdims=True)
            part[16 + slot : 17 + slot, here] += jnp.sum(weighted, axis=0, keepdims=True)
        part[total_row : total_row + 1, total_lane : total_lane + 128] += jnp.broadcast_to(
            jnp.sum(total), (1, 128)
        )

    chunk_at = {place: c for c, place in enumerate(place_of)}
    tasks = [
        ([chunk_at[source[0]] for source in scans[name][0]], name)
        for name in (9, 10, 11, 12, 8, 7, 4, 5, 6, 3, 2, 0, 1)
    ]
    loaded = set()
    for c in range(CHUNKS):
        if planner.stage[c] > 8:
            scan_load(place_of[c]).start()
    for first, second in planner.drain(tasks, 1.5):
        if first != "task":
            emit(first, second)
            if first == 8:
                scan_load(place_of[second]).start()
            continue
        for source in scans[second][0]:
            if source[0] not in loaded:
                loaded.add(source[0])
                scan_load(source[0]).wait()
        scan(second)
    total = line_sum(part, whole, line_send_sem, line_recv_sem, z, others_z)
    row_counts = [D] * 12 + [FF]
    means = [total[13:14, 128 * i : 128 * i + 1] / D for i in range(8)]
    means = means + [total[14:15, 0:1] / D] * 4 + [total[14:15, 128:129] / FF]
    cols_new, quotients = [], []
    for slot in range(13):
        new = DECAY_RATE * cols_ref[slot : slot + 1, :] + (1.0 - DECAY_RATE) * (
            total[slot : slot + 1] / row_counts[slot] + FACTOR_EPS
        )
        cols_new.append(new)
        quotients.append(jnp.sum(total[16 + slot : 17 + slot] / new, axis=1, keepdims=True))
        cols_out[slot : slot + 1, :] = new
    expand_quotient = quotients[8] + quotients[9] + quotients[10] + quotients[11]
    for slot in range(13):
        if slot < 8:
            mean_square = means[slot] * quotients[slot] / (D * D)
            rate = STEP_RATE * (OUT_GAIN if slot % 4 == 3 else 1.0)
        else:
            quotient = expand_quotient if slot < 12 else quotients[12]
            mean_square = means[slot] * quotient / (D * FF)
            rate = STEP_RATE
        factor = rate / jnp.maximum(1.0, jnp.sqrt(mean_square) / CLIP_LEVEL)
        scale_out[slot : slot + 1, :] = lax.rsqrt(cols_new[slot] / means[slot]) * factor
    token_copy.wait()


def backward(scalars, held, gains, small, factor_rows, factor_cols):
    any_space = pl.BlockSpec(memory_space=pl.ANY)
    vmem = pl.BlockSpec(memory_space=pltpu.VMEM)
    shape = jax.ShapeDtypeStruct
    dma = pltpu.SemaphoreType.DMA
    low = jnp.bfloat16
    wide = jnp.float32
    rows = small.shape[0]
    return pl.pallas_call(
        backward_kernel,
        out_shape=(
            shape((1024, D), low),
            shape((128, D), low),
            shape((CHUNKS, 256, D), low),
            shape(small.shape, wide),
            shape((256, 128), wide),
            shape((16, D), wide),
            shape((16, D), wide),
            shape((CHUNKS, 4, 128, D), low),
        ),
        in_specs=[SCALARS] * 2 + [any_space] * len(held) + [vmem] * 4,
        out_specs=(any_space, vmem, any_space, vmem, vmem, vmem, vmem, any_space),
        scratch_shapes=[
            pltpu.VMEM((POOL, 1024, D), low),
            pltpu.VMEM((1024, D), wide),
            pltpu.VMEM((G_SLOTS, 4, 256, D), low),
            pltpu.VMEM((R_SLOTS, 4, 128, D), low),
            pltpu.VMEM((CHUNKS, 4, 64, D), low),
            pltpu.VMEM((CHUNKS, 4, 32, D), low),
            pltpu.VMEM((CHUNKS, 3, 32, D), low),
            pltpu.VMEM((2, 128, D), wide),
            pltpu.VMEM((128, 1024), wide),
            pltpu.VMEM((2, 1024, 128), wide),
            pltpu.VMEM((2, 1024, 128), wide),
            pltpu.VMEM((8, 8, 1024), wide),
            pltpu.VMEM((3, 128, D), low),
            pltpu.VMEM((D, 128), low),
            pltpu.VMEM((rows, D), wide),
            pltpu.VMEM((3, rows, D), wide),
            pltpu.VMEM((3, rows, D), wide),
            pltpu.VMEM((4, rows, D), wide),
            pltpu.VMEM((32, D), wide),
            pltpu.VMEM((4, 32, D), wide),
            dma((POOL,)),
            dma((2,)),
            dma((4,)),
            dma((R_SLOTS,)),
            dma((CHUNKS,)),
            dma((3,)),
            dma((3,)),
            dma((6, CHUNKS)),
            dma((6, CHUNKS)),
            dma((CHUNKS, 3)),
            dma((CHUNKS, 3)),
            dma((CHUNKS,)),
            dma((6,)),
            dma((6,)),
        ],
        compiler_params=pltpu.CompilerParams(
            collective_id=0, has_side_effects=True, vmem_limit_bytes=62 * MIB
        ),
    )(*scalars, *held, gains, small, factor_rows, factor_cols)[0:7]


def line_sum(part, whole, send_sem, recv_sem, z, others_z):
    copies = [
        remote(part, whole.at[z], send_sem.at[d], recv_sem.at[d], others_z[d]) for d in range(3)
    ]
    for copy in copies:
        copy.start()
    whole[z] = part[...]
    for copy in copies:
        copy.wait()
    return (whole[0] + whole[1]) + (whole[2] + whole[3])


def update_attention_kernel(
    grad_ref, weight_ref, rows_ref, scale_ref, grad_out, new_out, copy_out, grads, change
):
    block = grad_ref.shape[1]
    for i in range(8):
        rows = lax.rsqrt(rows_ref[:, i : i + 1])
        every = pl.ds(i, block, stride=8)
        for lane in range(8):
            columns = slice(lane * 128, lane * 128 + 128)
            if i < 2:
                start = 512 * i + 128 * (lane % 4)
                grad = grad_ref[2 * (lane // 4), :, start : start + 128]
            else:
                grad = grad_ref[1 if i == 2 else i, :, columns]
            grad = grad.astype(jnp.float32)
            grads[lane, every, :] = grad
            change[lane, every, :] = grad * rows * scale_ref[i : i + 1, columns]
    for lane in range(8):
        columns = slice(lane * 128, lane * 128 + 128)
        grad_out[:, columns] = grads[lane]
        new = weight_ref[:, columns] - change[lane]
        new_out[:, columns] = new
        copy_out[:, columns] = new.astype(jnp.bfloat16)


def update_attention(grads, weights, rows, scale):
    block = 64
    wide = pl.BlockSpec((block * 8, D), lambda i: (i, 0))
    shape = jax.ShapeDtypeStruct
    new = pl.pallas_call(
        update_attention_kernel,
        grid=(256 // block,),
        out_shape=(
            shape((2048, D), jnp.float32),
            shape((2048, D), jnp.float32),
            shape((2048, D), jnp.bfloat16),
        ),
        in_specs=[
            pl.BlockSpec((8, block, D), lambda i: (0, i, 0)),
            wide,
            pl.BlockSpec((block, 128), lambda i: (i, 0)),
            pl.BlockSpec((16, D), lambda i: (0, 0)),
        ],
        out_specs=(wide,) * 3,
        scratch_shapes=[pltpu.VMEM((8, block * 8, 128), jnp.float32)] * 2,
        compiler_params=pltpu.CompilerParams(vmem_limit_bytes=62 * MIB),
    )(grads, weights.reshape(2048, D), rows, scale)
    return [t.reshape(256, 8, D) for t in new]


def update_kernel(
    first, slots, grad_ref, weight_ref, rows_ref, scale_ref, grad_out, new_out, copy_out
):
    spans = 4 if slots == 4 else 1
    wide = D // spans
    for i in range(slots):
        grads = grad_ref[i].astype(jnp.float32)
        changes = grads * (lax.rsqrt(rows_ref[...]) * scale_ref[first + i : first + i + 1, :])
        for s in range(spans):
            start = s * D + i * wide
            columns = slice(start, start + wide)
            part = slice(s * wide, s * wide + wide)
            grad_out[:, columns] = grads[:, part]
            new = weight_ref[:, columns] - changes[:, part]
            new_out[:, columns] = new
            copy_out[:, columns] = new.astype(jnp.bfloat16)


def update_plain(grads, weights, rows, scale, first, slots, grad_map):
    count, width = weights.shape
    block = 256 // slots
    wide = pl.BlockSpec((block, width), lambda i: (i, 0))
    shape = jax.ShapeDtypeStruct
    return pl.pallas_call(
        lambda *refs: update_kernel(first, slots, *refs),
        grid=(count // block,),
        out_shape=(
            shape(weights.shape, jnp.float32),
            shape(weights.shape, jnp.float32),
            shape(weights.shape, jnp.bfloat16),
        ),
        in_specs=[
            pl.BlockSpec((slots, block, D), grad_map),
            wide,
            pl.BlockSpec((block, 1), lambda i: (i, 0)),
            pl.BlockSpec((16, D), lambda i: (0, 0)),
        ],
        out_specs=(wide,) * 3,
        compiler_params=pltpu.CompilerParams(vmem_limit_bytes=62 * MIB),
    )(grads, weights, rows, scale)


def update_direct(grads, rows, scale, attention_weights, expand_weight, shrink_weight):
    shr_rows = rows[:, 9:13].T.reshape(-1, 1)
    attention = update_attention(grads, attention_weights, rows, scale)
    expand = update_plain(grads, expand_weight, rows[:, 8:9], scale, 8, 4, lambda i: (2, i, 0))
    shrink = update_plain(
        grads, shrink_weight, shr_rows, scale, 12, 1, lambda i: (12 + i, 0, 0)
    )
    return attention, expand, shrink, (rows[:, 0:8].T, rows[:, 8], shr_rows[:, 0])


def as_rows(vector):
    rows = -(-vector.shape[0] // 1024) * 8
    return jnp.pad(vector, (0, rows * 128 - vector.shape[0])).reshape(rows, 128)


def masked_scores(query_part, key_heads, first_row, valid_count, causal):
    scores = jnp.einsum("qhd,khd->hqk", query_part, key_heads, preferred_element_type=jnp.float32)
    key_places = jnp.arange(key_heads.shape[0], dtype=jnp.int32)[None, :]
    usable = key_places < valid_count
    if causal:
        query_places = first_row + jnp.arange(query_part.shape[0], dtype=jnp.int32)[:, None]
        usable = usable & (key_places <= query_places)
    return jnp.where(usable[None], scores, MASKED)


def attend_forward(queries, key_heads, values, valid_count, causal):
    query_rows = queries.shape[0]
    step_rows = min(512, query_rows)
    outputs, stored = ([], [])
    for b in range(query_rows // step_rows):
        first_row = b * step_rows
        key_end = first_row + step_rows if causal else key_heads.shape[0]
        scores = masked_scores(
            queries[first_row : first_row + step_rows],
            key_heads[:key_end],
            first_row,
            valid_count,
            causal,
        )
        row_max = jnp.max(scores, axis=-1, keepdims=True)
        raised = jnp.exp(scores - row_max)
        totals = jnp.sum(raised, axis=-1, keepdims=True)
        probs_low = (raised / totals).astype(jnp.bfloat16)
        outputs.append(
            jnp.einsum(
                "hqk,khd->qhd", probs_low, values[:key_end], preferred_element_type=jnp.float32
            )
        )
        stored.append(row_max + jnp.log(totals))
    return (jnp.concatenate(outputs, axis=0), stored)


def attend_backward(queries, key_heads, values, grad_out, stored, valid_count, causal):
    query_rows = queries.shape[0]
    key_rows = key_heads.shape[0]
    step_rows = min(512, query_rows)
    grad_queries = []
    grad_keys = jnp.zeros(key_heads.shape, jnp.float32)
    grad_values = jnp.zeros(values.shape, jnp.float32)
    for b in range(query_rows // step_rows):
        first_row = b * step_rows
        key_end = first_row + step_rows if causal else key_rows
        query_part = queries[first_row : first_row + step_rows]
        grad_part = grad_out[first_row : first_row + step_rows]
        scores = masked_scores(query_part, key_heads[:key_end], first_row, valid_count, causal)
        probs = jnp.exp(scores - stored[b])
        probs_low = probs.astype(jnp.bfloat16)
        grad_probs = jnp.einsum(
            "qhd,khd->hqk", grad_part, values[:key_end], preferred_element_type=jnp.float32
        )
        value_part = jnp.einsum(
            "hqk,qhd->khd", probs_low, grad_part, preferred_element_type=jnp.float32
        )
        grad_scores = probs * (grad_probs - jnp.sum(probs * grad_probs, axis=-1, keepdims=True))
        scores_low = grad_scores.astype(jnp.bfloat16)
        grad_queries.append(
            jnp.einsum(
                "hqk,khd->qhd", scores_low, key_heads[:key_end], preferred_element_type=jnp.float32
            )
        )
        key_part = jnp.einsum(
            "hqk,qhd->khd", scores_low, query_part, preferred_element_type=jnp.float32
        )
        padding = ((0, key_rows - key_end), (0, 0), (0, 0))
        grad_keys = grad_keys + jnp.pad(key_part, padding)
        grad_values = grad_values + jnp.pad(value_part, padding)
    return (jnp.concatenate(grad_queries, axis=0), grad_keys, grad_values)


def gather_rows(piece):
    return lax.all_gather(piece, ("shard", "rep"), axis=0, tiled=True)


def own_piece(block, replicas):
    rows = block.shape[0] // replicas
    return lax.dynamic_slice_in_dim(block, lax.axis_index("rep") * rows, rows, axis=0)


def scatter_rows(grad):
    piece = lax.psum_scatter(
        grad.astype(jnp.bfloat16), ("shard", "rep"), scatter_dimension=0, tiled=True
    )
    return lax.all_gather(piece, "rep", axis=0, tiled=True)


def local_factors(grad, rows):
    square = grad * grad
    rows_new = DECAY_RATE * rows + (1.0 - DECAY_RATE) * jnp.mean(square + FACTOR_EPS, axis=-1)
    col_part = jnp.sum(square + FACTOR_EPS, axis=0)
    weighted = jnp.sum(square / rows_new[..., None], axis=0)
    return rows_new, col_part, weighted, jnp.sum(rows_new, axis=0)


def finish_factors(grad, weight, rows_new, cols, col_sum, weighted, row_total, row_count, rate):
    cols_new = DECAY_RATE * cols + (1.0 - DECAY_RATE) * col_sum / row_count
    mean_rows = row_total / row_count
    mean_square = mean_rows * jnp.sum(weighted / cols_new, axis=-1) / (row_count * cols.shape[-1])
    factor = rate / jnp.maximum(1.0, jnp.sqrt(mean_square) / CLIP_LEVEL)
    scaled = lax.rsqrt(cols_new / mean_rows[..., None]) * factor[..., None]
    fresh = weight - grad * (lax.rsqrt(rows_new)[..., None] * scaled[None])
    return fresh, cols_new


def plain_device(
    tokens,
    encoder,
    cotangent,
    lengths,
    encoder_lengths,
    dealt_order,
    attention_weights,
    expand_weight,
    shrink_weight,
    small_params,
    attention_rows,
    attention_cols,
    expand_rows,
    expand_cols,
    shrink_rows,
    shrink_cols,
    small_moment,
):
    devices = lax.axis_size(("rep", "shard"))
    replicas = lax.axis_size("rep")
    shards = lax.axis_size("shard")
    slot_tokens = tokens.shape[0]
    slot_states = encoder.shape[0]
    position = lax.axis_index(("rep", "shard"))
    inverse = (
        jnp.zeros((devices,), jnp.int32).at[dealt_order].set(jnp.arange(devices, dtype=jnp.int32))
    )
    qkv_piece = own_piece(attention_weights[:, 0:3, :].reshape(-1, 3 * D), replicas)
    rest_piece = own_piece(attention_weights[:, 3:8, :].reshape(-1, 5 * D), replicas)
    qkv_full = gather_rows(qkv_piece.astype(jnp.bfloat16))
    rest_full = gather_rows(rest_piece.astype(jnp.bfloat16))
    expand_full = gather_rows(own_piece(expand_weight, replicas).astype(jnp.bfloat16))
    shrink_full = gather_rows(own_piece(shrink_weight, replicas).astype(jnp.bfloat16))
    spread = lax.all_to_all(
        tokens.reshape(devices, slot_tokens // devices, D),
        ("rep", "shard"),
        split_axis=0,
        concat_axis=0,
        tiled=True,
    )
    picked = jnp.take(spread, inverse, axis=0)
    tokens = lax.all_to_all(
        picked, ("rep", "shard"), split_axis=0, concat_axis=0, tiled=True
    ).reshape(slot_tokens, D)
    states = encoder
    incoming = cotangent
    valid_tokens = lengths[position]
    valid_states = encoder_lengths[position]
    matrices = [qkv_full[:, i * D : (i + 1) * D] for i in range(3)] + [
        rest_full[:, i * D : (i + 1) * D] for i in range(5)
    ]
    parts = unpack(small_params)
    token_heads = (slot_tokens, HEADS, HEAD_DIM)
    state_heads = (slot_states, HEADS, HEAD_DIM)
    q_self = ((forward_product(tokens, matrices[0]) + parts[0]) * 0.125).astype(
        jnp.bfloat16
    )
    k_self = forward_product(tokens, matrices[1]).astype(jnp.bfloat16)
    v_self = (forward_product(tokens, matrices[2]) + parts[1]).astype(jnp.bfloat16)
    o_self, lse_self = attend_forward(
        q_self.reshape(token_heads),
        k_self.reshape(token_heads),
        v_self.reshape(token_heads),
        valid_tokens,
        True,
    )
    o_self_low = o_self.reshape(slot_tokens, D).astype(jnp.bfloat16)
    branch_a = forward_product(o_self_low, matrices[3]) + parts[2]
    tokens_wide = tokens.astype(jnp.float32)
    hidden_one, norm_one_back = jax.vjp(layer_norm, tokens_wide + branch_a, parts[8], parts[9])
    hidden_one_low = hidden_one.astype(jnp.bfloat16)
    q_cross = (
        (forward_product(hidden_one_low, matrices[4]) + parts[3]) * 0.125
    ).astype(jnp.bfloat16)
    k_cross = forward_product(states, matrices[5]).astype(jnp.bfloat16)
    v_cross = (forward_product(states, matrices[6]) + parts[4]).astype(jnp.bfloat16)
    o_cross, lse_cross = attend_forward(
        q_cross.reshape(token_heads),
        k_cross.reshape(state_heads),
        v_cross.reshape(state_heads),
        valid_states,
        False,
    )
    o_cross_low = o_cross.reshape(slot_tokens, D).astype(jnp.bfloat16)
    branch_c = forward_product(o_cross_low, matrices[7]) + parts[5]
    hidden_two, norm_two_back = jax.vjp(layer_norm, hidden_one + branch_c, parts[10], parts[11])
    hidden_two_low = hidden_two.astype(jnp.bfloat16)
    pre_act = forward_product(hidden_two_low, expand_full) + parts[6]
    activated, gelu_back = jax.vjp(gelu_exact, pre_act)
    activated_low = activated.astype(jnp.bfloat16)
    branch_m = forward_product(activated_low, shrink_full) + parts[7]
    result, norm_three_back = jax.vjp(layer_norm, hidden_two + branch_m, parts[12], parts[13])
    usable_rows = (jnp.arange(slot_tokens, dtype=jnp.int32) < valid_tokens).astype(jnp.float32)[
        :, None
    ]
    squares = jnp.stack(
        [
            jnp.sum(usable_rows * t * t)
            for t in (tokens_wide, branch_a, hidden_one, branch_c, hidden_two, branch_m)
        ]
    )
    d_third, d_gain_three, d_shift_three = norm_three_back(
        incoming.astype(jnp.float32) * usable_rows
    )
    d_mlp = d_third.astype(jnp.bfloat16)
    grad_shrink = weight_product(activated_low, d_mlp)
    grad_shrink_offset = row_sum(d_mlp)
    d_activated = input_product(d_mlp, shrink_full)
    d_pre = gelu_back(d_activated)[0].astype(jnp.bfloat16)
    grad_expand = weight_product(hidden_two_low, d_pre)
    grad_expand_offset = row_sum(d_pre)
    d_hidden_two = d_third + input_product(d_pre, expand_full)
    d_second, d_gain_two, d_shift_two = norm_two_back(d_hidden_two)
    d_branch_c = d_second.astype(jnp.bfloat16)
    grad_cross_out = weight_product(o_cross_low, d_branch_c)
    grad_cross_out_offset = row_sum(d_branch_c)
    d_o_cross = input_product(d_branch_c, matrices[7]).astype(jnp.bfloat16)
    grad_cq, grad_ck, grad_cv = attend_backward(
        q_cross.reshape(token_heads),
        k_cross.reshape(state_heads),
        v_cross.reshape(state_heads),
        d_o_cross.reshape(token_heads),
        lse_cross,
        valid_states,
        False,
    )
    dq_cross = (grad_cq.reshape(slot_tokens, D) * 0.125).astype(jnp.bfloat16)
    dk_cross = grad_ck.reshape(slot_states, D).astype(jnp.bfloat16)
    dv_cross = grad_cv.reshape(slot_states, D).astype(jnp.bfloat16)
    grad_cross_query = weight_product(hidden_one_low, dq_cross)
    grad_cross_key = weight_product(states, dk_cross)
    grad_cross_value = weight_product(states, dv_cross)
    state_grad = input_product(dk_cross, matrices[5]) + input_product(
        dv_cross, matrices[6]
    )
    d_hidden_one = d_second + input_product(dq_cross, matrices[4])
    d_first, d_gain_one, d_shift_one = norm_one_back(d_hidden_one)
    d_branch_a = d_first.astype(jnp.bfloat16)
    grad_self_out = weight_product(o_self_low, d_branch_a)
    grad_self_out_offset = row_sum(d_branch_a)
    d_o_self = input_product(d_branch_a, matrices[3]).astype(jnp.bfloat16)
    grad_sq, grad_sk, grad_sv = attend_backward(
        q_self.reshape(token_heads),
        k_self.reshape(token_heads),
        v_self.reshape(token_heads),
        d_o_self.reshape(token_heads),
        lse_self,
        valid_tokens,
        True,
    )
    dq_self = (grad_sq.reshape(slot_tokens, D) * 0.125).astype(jnp.bfloat16)
    dk_self = grad_sk.reshape(slot_tokens, D).astype(jnp.bfloat16)
    dv_self = grad_sv.reshape(slot_tokens, D).astype(jnp.bfloat16)
    grad_self_query = weight_product(tokens, dq_self)
    grad_self_key = weight_product(tokens, dk_self)
    grad_self_value = weight_product(tokens, dv_self)
    token_grad = (
        d_first
        + input_product(dq_self, matrices[0])
        + input_product(dk_self, matrices[1])
        + input_product(dv_self, matrices[2])
    )
    small_partial = jnp.concatenate(
        [
            row_sum(dq_self),
            row_sum(dv_self),
            grad_self_out_offset,
            row_sum(dq_cross),
            row_sum(dv_cross),
            grad_cross_out_offset,
            grad_expand_offset,
            grad_shrink_offset,
            d_gain_one,
            d_shift_one,
            d_gain_two,
            d_shift_two,
            d_gain_three,
            d_shift_three,
        ]
    )
    totals = lax.psum(jnp.concatenate([small_partial, squares]), ("rep", "shard"))
    g_shrink = scatter_rows(grad_shrink)
    g_expand = scatter_rows(grad_expand)
    g_rest = scatter_rows(
        jnp.concatenate(
            [grad_self_out, grad_cross_query, grad_cross_key, grad_cross_value, grad_cross_out],
            axis=1,
        )
    )
    g_qkv = scatter_rows(
        jnp.concatenate([grad_self_query, grad_self_key, grad_self_value], axis=1)
    )
    g_attention = (
        jnp.concatenate([g_qkv, g_rest], axis=1).reshape(-1, 8, D).astype(jnp.float32)
    )
    g_expand = g_expand.astype(jnp.float32)
    g_shrink = g_shrink.astype(jnp.float32)
    attention_rows_new, *attention_parts = local_factors(g_attention, attention_rows.T)
    expand_rows_new, *expand_parts = local_factors(g_expand, expand_rows)
    shrink_rows_new, *shrink_parts = local_factors(g_shrink, shrink_rows)
    flat = attention_parts + expand_parts + shrink_parts
    summed = lax.psum(jnp.concatenate([t.reshape(-1) for t in flat]), "shard")
    sums = []
    offset = 0
    for t in flat:
        sums.append(summed[offset : offset + t.size].reshape(t.shape))
        offset = offset + t.size
    attention_rates = STEP_RATE * jnp.where(jnp.arange(8) % 4 == 3, OUT_GAIN, 1.0).astype(
        jnp.float32
    )
    attention_new, attention_cols_new = finish_factors(
        g_attention,
        attention_weights,
        attention_rows_new,
        attention_cols,
        *sums[0:3],
        D,
        attention_rates,
    )
    expand_new, expand_cols_new = finish_factors(
        g_expand, expand_weight, expand_rows_new, expand_cols, *sums[3:6], D, STEP_RATE
    )
    shrink_new, shrink_cols_new = finish_factors(
        g_shrink, shrink_weight, shrink_rows_new, shrink_cols, *sums[6:9], FF, STEP_RATE
    )
    small_grad = totals[: small_params.shape[0]]
    small_moment_new = DECAY_RATE * small_moment + (1.0 - DECAY_RATE) * (
        small_grad * small_grad + FACTOR_EPS
    )
    small_update = small_grad * lax.rsqrt(small_moment_new)
    small_scale = jnp.sqrt(jnp.mean(small_update * small_update))
    small_new = small_params - SMALL_RATE * small_update / jnp.maximum(
        1.0, small_scale / CLIP_LEVEL
    )
    norm_stats = jnp.sqrt(
        totals[small_params.shape[0] :] / (jnp.sum(lengths).astype(jnp.float32) * D)
    )
    return (
        result.astype(jnp.bfloat16),
        token_grad.astype(jnp.bfloat16),
        state_grad.astype(jnp.bfloat16),
        g_attention,
        g_expand,
        g_shrink,
        small_grad,
        attention_new,
        expand_new,
        shrink_new,
        small_new,
        attention_new.astype(jnp.bfloat16),
        expand_new.astype(jnp.bfloat16),
        shrink_new.astype(jnp.bfloat16),
        attention_rows_new.T,
        attention_cols_new,
        expand_rows_new,
        expand_cols_new,
        shrink_rows_new,
        shrink_cols_new,
        small_moment_new,
        norm_stats,
    )


def direct_device(
    tokens,
    encoder,
    cotangent,
    lengths,
    encoder_lengths,
    dealt_order,
    attention_weights,
    expand_weight,
    shrink_weight,
    small_params,
    attention_rows,
    attention_cols,
    expand_rows,
    expand_cols,
    shrink_rows,
    shrink_cols,
    small_moment,
):
    inverse = jnp.zeros((32,), jnp.int32).at[dealt_order].set(jnp.arange(32, dtype=jnp.int32))
    params = small_params.reshape(17, D)
    weights = (attention_weights.reshape(2048, D), expand_weight, shrink_weight)
    (
        tokens,
        full,
        q_self,
        k_self,
        v_self,
        o_self,
        lse_self,
        q_cross,
        k_cross,
        v_cross,
        o_cross,
        lse_cross,
        summed_one,
        summed_two,
        hidden_one,
        hidden_two,
        activated,
        slope,
        output,
        d_mlp,
        d_third,
        small_first,
    ) = forward(
        (inverse, lengths, encoder_lengths), tokens, weights, encoder, cotangent, params
    )
    factor_rows = jnp.concatenate(
        [attention_rows, expand_rows.reshape(1, 256), shrink_rows.reshape(4, 256)]
    )
    factor_rows = jnp.pad(factor_rows.T, ((0, 0), (0, 115)))
    factor_cols = jnp.concatenate(
        [attention_cols, hidden_blocks(expand_cols), shrink_cols.reshape(1, D), jnp.ones((3, D))]
    )
    token_grad, state_grad, reduced, totals, factor_rows, factor_cols, scale = backward(
        (lengths, encoder_lengths),
        (
            d_mlp,
            d_third,
            activated,
            slope,
            full.reshape(GATHERED, 1024, D),
            hidden_two,
            hidden_one,
            tokens.reshape(1024, D),
            encoder,
            o_cross,
            o_self,
            summed_one,
            summed_two,
            q_self,
            k_self,
            v_self,
            q_cross,
            k_cross,
            v_cross,
            lse_self,
            lse_cross,
        ),
        params,
        small_first,
        factor_rows,
        factor_cols,
    )
    attention, expand, shrink, rows_new = update_direct(
        reduced, factor_rows, scale, attention_weights, expand_weight, shrink_weight
    )
    cols_new = (factor_cols[0:8], hidden_flat(factor_cols[8:12]), factor_cols[12])
    small_grad = totals[0:17].reshape(-1)
    small_moment_new = DECAY_RATE * small_moment + (1.0 - DECAY_RATE) * (
        small_grad * small_grad + FACTOR_EPS
    )
    small_update = small_grad * lax.rsqrt(small_moment_new)
    small_scale = jnp.sqrt(jnp.mean(small_update * small_update))
    small_new = small_params - SMALL_RATE * small_update / jnp.maximum(
        1.0, small_scale / CLIP_LEVEL
    )
    norm_stats = jnp.sqrt(totals[17, 0:6] / (jnp.sum(lengths).astype(jnp.float32) * D))
    return (
        output,
        token_grad,
        state_grad,
        attention[0],
        expand[0],
        shrink[0],
        small_grad,
        attention[1],
        expand[1],
        shrink[1],
        small_new,
        attention[2],
        expand[2],
        shrink[2],
        rows_new[0],
        cols_new[0],
        rows_new[1],
        cols_new[1],
        rows_new[2],
        cols_new[2],
        small_moment_new,
        norm_stats,
    )


def on_device(*args):
    if lax.axis_size("rep") == 8 and lax.axis_size("shard") == 4:
        return direct_device(*args)
    return plain_device(*args)


def solution(mesh):
    in_specs = (
        P(("rep", "shard"), None),
        P(("rep", "shard"), None),
        P(("rep", "shard"), None),
        P(),
        P(),
        P(),
        P("shard", None, None),
        P("shard", None),
        P("shard", None),
        P(),
        P(None, "shard"),
        P(),
        P("shard"),
        P(),
        P("shard"),
        P(),
        P(),
    )
    out_specs = (
        P(("rep", "shard"), None),
        P(("rep", "shard"), None),
        P(("rep", "shard"), None),
        P("shard", None, None),
        P("shard", None),
        P("shard", None),
        P(),
        P("shard", None, None),
        P("shard", None),
        P("shard", None),
        P(),
        P("shard", None, None),
        P("shard", None),
        P("shard", None),
        P(None, "shard"),
        P(),
        P("shard"),
        P(),
        P("shard"),
        P(),
        P(),
        P(),
    )
    return jax.shard_map(
        on_device, mesh=mesh, in_specs=in_specs, out_specs=out_specs, check_vma=False
    )
```
